32 devices in a mesh: dp: 2 (over x), context: 8 (over z, y), tensor: 2 (over core).
Axes of the slice: x: 2, y: 2, z: 4, core: 2. Of those that a mesh axis runs over, the one named last changes fastest.
Arguments:
- tokens: bfloat16 [4096, 2, 1536], P('context', 'dp'), may hold values from -6 to 6
- positions: int32 [4096, 2], P('context', 'dp'), may hold values from 0 to 4095, as said below
- gain_one: bfloat16 [1536], P(('dp', 'context')), may hold values from 0.099609375 to 1.8984375
- gain_two: bfloat16 [1536], P(('dp', 'context')), may hold values from 0.099609375 to 1.8984375
- w_query: bfloat16 [1536, 1536], P(('dp', 'context'), 'tensor'), may hold values from -0.15625 to 0.15625
- w_key: bfloat16 [1536, 768], P(('dp', 'context'), 'tensor'), may hold values from -0.15625 to 0.15625
- w_value: bfloat16 [1536, 768], P(('dp', 'context'), 'tensor'), may hold values from -0.15625 to 0.15625
- w_out: bfloat16 [1536, 1536], P('tensor', ('dp', 'context')), may hold values from -0.875 to 0.875
- w_gate: bfloat16 [1536, 4096], P(('dp', 'context'), 'tensor'), may hold values from -0.15625 to 0.15625
- w_up: bfloat16 [1536, 4096], P(('dp', 'context'), 'tensor'), may hold values from -0.15625 to 0.15625
- w_down: bfloat16 [4096, 1536], P('tensor', ('dp', 'context')), may hold values from -0.09375 to 0.09375
- cotangent: bfloat16 [4096, 2, 1536], P('context', 'dp'), may hold values from -6 to 6
Outputs:
- layer_out: bfloat16 [4096, 2, 1536], P('context', 'dp')
- input_grad: float32 [4096, 2, 1536], P('context', 'dp')
- grad_gain_one: float32 [1536], P(('dp', 'context'))
- grad_gain_two: float32 [1536], P(('dp', 'context'))
- grad_query: float32 [1536, 1536], P(('dp', 'context'), 'tensor')
- grad_key: float32 [1536, 768], P(('dp', 'context'), 'tensor')
- grad_value: float32 [1536, 768], P(('dp', 'context'), 'tensor')
- grad_out: float32 [1536, 1536], P('tensor', ('dp', 'context'))
- grad_gate: float32 [1536, 4096], P(('dp', 'context'), 'tensor')
- grad_up: float32 [1536, 4096], P(('dp', 'context'), 'tensor')
- grad_down: float32 [4096, 1536], P('tensor', ('dp', 'context'))
The draws below stay inside these ranges and needn't reach their ends.
Inputs may be any that keep to these rules, and one draw needn't show every extreme that they name: In every sequence the positions are each of 0 to 4095 once; the 512 slots of one index of context hold two runs of 256 consecutive positions, block c in the first half and block 15 - c in the second, with c different for each index of context.
All inputs are finite; a program needn't handle non-finite values.
Results may differ from the reference program's by a relative error of at most 0.02.
Values may be sent and summed in bfloat16 or wider, within the bound.
A program may use at most 256 MiB of HBM per device.

```python
import jax
import jax.numpy as jnp
from jax import lax

D = 1536
HEADS = 16
KV_HEADS = 8
HEAD = 96
FF = 4096
LENGTH = 4096
SEQS = 2
QD = 1536
KVD = 768
N_CONTEXT = 8


def draw_positions(key, part):
    key = jax.random.fold_in(key, 7)
    piece_len = LENGTH // (2 * N_CONTEXT)
    local_len = LENGTH // N_CONTEXT
    seq_keys = jax.random.split(key, SEQS)
    orders = jax.vmap(lambda one_key: jax.random.permutation(one_key, N_CONTEXT))(seq_keys).astype(jnp.int32)
    slot_ids = jnp.arange(LENGTH, dtype=jnp.int32)
    device = slot_ids // local_len
    within = slot_ids % local_len
    upper_half = within // piece_len
    offset = within % piece_len
    owned_block = orders[:, device]
    block_id = jnp.where(upper_half[None, :] == 0, owned_block, 2 * N_CONTEXT - 1 - owned_block)
    return (block_id * piece_len + offset[None, :]).T.astype(jnp.int32)


def spiked(result, key, source, target, parts, factor):
    def block_of(position):
        return (jnp.arange(result.shape[position]) // (result.shape[position] // parts)).reshape((-1,) + (1,) * (result.ndim - 1 - position))

    one_side = jax.random.permutation(key, parts)[block_of(target)]
    second = (block_of(target) + parts // 2) % parts
    return jnp.where((block_of(source) == one_side) | (block_of(source) == second), factor * result, result)


def shard_levels(key, extent, cuts, smallest, largest):
    def one(dim, parts):
        draws = jax.random.uniform(jax.random.fold_in(jax.random.fold_in(key, 6), dim), (parts,), jnp.float32, smallest / len(cuts), largest / len(cuts))
        return jnp.repeat(jnp.exp(draws), extent[dim] // parts).reshape((-1,) + (1,) * (len(extent) - dim - 1))

    gain = one(*cuts[0])
    for cut in cuts[1:]:
        gain = gain * one(*cut)
    return gain


def normal_values(key, dims, width, bound, pieces=(), kind=jnp.bfloat16):
    values = width * jax.random.normal(key, dims, jnp.float32)
    if pieces:
        values = values * shard_levels(key, dims, pieces, -0.22, 0.18)
    return jnp.clip(values, -bound, bound).astype(kind)


def noise_with(rng, extent, width, bound, cuts, heavy, kind=jnp.bfloat16):
    values = width * jax.random.normal(rng, extent, jnp.float32)
    if cuts:
        values = values * shard_levels(rng, extent, cuts, -0.22, 0.18)
    return jnp.clip(spiked(values, jax.random.fold_in(rng, 3), *heavy), -bound, bound).astype(kind)


def setup_inputs(seed: int = 0) -> dict:
    arg_keys = jax.random.split(jax.random.key(seed), 13)
    return {
        "tokens": noise_with(arg_keys[0], (LENGTH, SEQS, D), 1.0, 6.0, ((0, 8), (1, 2)), (0, 2, 8, 2.0)),
        "positions": draw_positions(jax.random.fold_in(arg_keys[12], 71), 0),
        "gain_one": jnp.clip(1.0 + 0.18 * jax.random.normal(arg_keys[2], (D,), jnp.float32), 0.099609375, 1.8984375).astype(jnp.bfloat16),
        "gain_two": jnp.clip(1.0 + 0.18 * jax.random.normal(arg_keys[3], (D,), jnp.float32), 0.099609375, 1.8984375).astype(jnp.bfloat16),
        "w_query": normal_values(arg_keys[4], (D, QD), D ** -0.5, 0.15625, ((0, 16), (1, 2))),
        "w_key": normal_values(arg_keys[5], (D, KVD), D ** -0.5, 0.15625, ((0, 16), (1, 2))),
        "w_value": normal_values(arg_keys[6], (D, KVD), D ** -0.5, 0.15625, ((0, 16), (1, 2))),
        "w_out": normal_values(arg_keys[7], (QD, D), (QD // 32) ** -0.5, 0.875, ((0, 2), (1, 16))),
        "w_gate": normal_values(arg_keys[8], (D, FF), D ** -0.5, 0.15625, ((0, 16), (1, 2))),
        "w_up": normal_values(arg_keys[9], (D, FF), D ** -0.5, 0.15625, ((0, 16), (1, 2))),
        "w_down": normal_values(arg_keys[10], (FF, D), FF ** -0.5, 0.09375, ((0, 2), (1, 16))),
        "cotangent": noise_with(arg_keys[11], (LENGTH, SEQS, D), 1.0, 6.0, ((0, 8), (1, 2)), (0, 2, 8, 2.0)),
    }


@jax.custom_vjp
def low(v):
    return lax.optimization_barrier(v.astype(jnp.bfloat16)).astype(jnp.float32)

@jax.custom_vjp
def low_back(v):
    return v

def low_keep(v):
    return (low(v), None)

def low_pass(kept, grad):
    return (grad,)

def back_keep(v):
    return (v, None)

def back_low(kept, grad):
    return (low(grad),)
low.defvjp(low_keep, low_pass)
low_back.defvjp(back_keep, back_low)
highest = lax.Precision.HIGHEST
epsilon = 1e-05
theta_base = 100000.0
masked_value = -1e+30

def rms_scale(values_in, gain_vec):
    return values_in * lax.rsqrt(lax.optimization_barrier(jnp.mean(values_in * values_in, axis=-1, keepdims=True)) + epsilon) * gain_vec

def rotate(values_in, cos_part, sin_part):
    half_size = values_in.shape[-1] // 2
    front_half = values_in[..., :half_size]
    back_half = values_in[..., half_size:]
    return jnp.concatenate([front_half * cos_part - back_half * sin_part, back_half * cos_part + front_half * sin_part], axis=-1)

def attend(queries, keys_in, values_in, seq_pos):
    group_size = HEADS // KV_HEADS
    keys_all = jnp.repeat(keys_in, group_size, axis=1)
    values_all = jnp.repeat(values_in, group_size, axis=1)
    block_len = min(512, LENGTH)
    block_count = LENGTH // block_len
    score_scale = HEAD ** (-0.5)

    def one_block(block_items):
        query_blk, pos_blk = block_items
        raw_scores = jnp.einsum('qhd,khd->hqk', query_blk, keys_all, precision=highest) * score_scale
        scores = low_back(raw_scores)
        allowed = seq_pos[None, None, :] <= pos_blk[None, :, None]
        masked = jnp.where(allowed, scores, masked_value)
        peak_val = lax.optimization_barrier(jnp.max(masked, axis=-1, keepdims=True))
        weights = jnp.where(allowed, jnp.exp(masked - peak_val), 0.0)
        prob_vals = low(weights / lax.optimization_barrier(jnp.sum(weights, axis=-1, keepdims=True)))
        return jnp.einsum('hqk,khd->qhd', prob_vals, values_all, precision=highest)
    mixed = lax.map(jax.checkpoint(one_block), (queries.reshape(block_count, block_len, HEADS, HEAD), seq_pos.reshape(block_count, block_len)))
    return mixed.reshape(LENGTH, HEADS * HEAD)

def layer_forward(seq_tokens, seq_pos, weights_f32):
    gain_one, gain_two, w_query, w_key, w_value, w_out, w_gate, w_up, w_down = weights_f32
    half_size = HEAD // 2
    inv_freqs = theta_base ** (-2.0 * jnp.arange(half_size, dtype=jnp.float32) / HEAD)
    angles = seq_pos.astype(jnp.float32)[:, None] * inv_freqs[None, :]
    cos_part = jnp.cos(angles)[:, None, :]
    sin_part = jnp.sin(angles)[:, None, :]
    normed = low(rms_scale(seq_tokens, gain_one))
    query_proj = low_back(jnp.dot(normed, w_query, precision=highest)).reshape(LENGTH, HEADS, HEAD)
    key_proj = low_back(jnp.dot(normed, w_key, precision=highest)).reshape(LENGTH, KV_HEADS, HEAD)
    values = low(low_back(jnp.dot(normed, w_value, precision=highest))).reshape(LENGTH, KV_HEADS, HEAD)
    queries = low(rotate(query_proj, cos_part, sin_part))
    keys_rot = low(rotate(key_proj, cos_part, sin_part))
    mixed = attend(queries, keys_rot, values, seq_pos)
    branch = low_back(jnp.dot(low(low_back(mixed)), w_out, precision=highest))
    middle = seq_tokens + branch
    second = low(rms_scale(middle, gain_two))
    gate_vals = low_back(jnp.dot(second, w_gate, precision=highest))
    up_vals = low_back(jnp.dot(second, w_up, precision=highest))
    hidden = low(jax.nn.silu(gate_vals) * up_vals)
    return middle + low_back(jnp.dot(hidden, w_down, precision=highest))

def reference(tokens, positions, gain_one, gain_two, w_query, w_key, w_value, w_out, w_gate, w_up, w_down, cotangent):
    weights_f32 = tuple((weight.astype(jnp.float32) for weight in (gain_one, gain_two, w_query, w_key, w_value, w_out, w_gate, w_up, w_down)))
    all_tokens = jnp.moveaxis(tokens.astype(jnp.float32), 1, 0)
    all_cot = jnp.moveaxis(cotangent.astype(jnp.float32), 1, 0)
    all_pos = jnp.moveaxis(positions, 1, 0)
    zero_grads = tuple((jnp.zeros_like(weight) for weight in weights_f32))

    def seq_step(grad_total, seq_items):
        seq_tokens, seq_pos, seq_cot = seq_items

        def forward_one(tokens_in, weights_in):
            return layer_forward(tokens_in, seq_pos, weights_in)
        seq_out, pullback = jax.vjp(forward_one, seq_tokens, weights_f32)
        grad_tokens, grad_weights = pullback(seq_cot)
        return (tuple((left_sum + right_sum for left_sum, right_sum in zip(grad_total, grad_weights))), (seq_out, grad_tokens))
    grad_total, (out_rows, grad_rows) = lax.scan(seq_step, zero_grads, (all_tokens, all_pos, all_cot))
    layer_out = jnp.moveaxis(out_rows, 0, 1).astype(jnp.bfloat16)
    input_grad = jnp.moveaxis(grad_rows, 0, 1)
    return (layer_out, input_grad, grad_total[0], grad_total[1], grad_total[2], grad_total[3], grad_total[4], grad_total[5], grad_total[6], grad_total[7], grad_total[8])
```

```python
import functools

import jax
import jax.numpy as jnp
from jax import lax
from jax.experimental import pallas as pl
from jax.experimental.pallas import tpu as pltpu
from jax.sharding import PartitionSpec as P

HEAD = 96


epsilon = 1e-05
theta_base = 100000.0
masked_value = -1e30


def norm_forward(values_in, gain_vec):
    inverse = lax.rsqrt(jnp.mean(values_in * values_in, axis=-1, keepdims=True) + epsilon)
    unit_vals = values_in * inverse
    return (unit_vals, inverse, (unit_vals * gain_vec.astype(jnp.float32)).astype(jnp.bfloat16))


def norm_backward(grad_in, unit_vals, inverse, gain_vec):
    scaled = grad_in * gain_vec.astype(jnp.float32)
    grad_vals = inverse * (
        scaled - unit_vals * jnp.mean(scaled * unit_vals, axis=-1, keepdims=True)
    )
    return (grad_vals, jnp.sum(grad_in * unit_vals, axis=0))


def rotate(values_in, cos_part, sin_part):
    half_size = values_in.shape[-1] // 2
    front_half = values_in[..., :half_size]
    back_half = values_in[..., half_size:]
    return jnp.concatenate(
        [
            front_half * cos_part - back_half * sin_part,
            back_half * cos_part + front_half * sin_part,
        ],
        axis=-1,
    )


def contract_rows(left_mat, right_mat):
    return lax.dot_general(
        left_mat, right_mat, (((0,), (0,)), ((), ())), preferred_element_type=jnp.float32
    )


def contract_cols(left_mat, right_mat):
    return lax.dot_general(
        left_mat, right_mat, (((1,), (1,)), ((), ())), preferred_element_type=jnp.float32
    )


def on_device(
    tokens,
    positions,
    gain_one,
    gain_two,
    w_query,
    w_key,
    w_value,
    w_out,
    w_gate,
    w_up,
    w_down,
    cotangent,
):
    slot_count, seq_count, model_width = tokens.shape
    row_count = slot_count * seq_count
    gathered = (
        lax.all_gather(gain_one, ("dp", "context"), axis=0, tiled=True),
        lax.all_gather(gain_two, ("dp", "context"), axis=0, tiled=True),
        lax.all_gather(w_query, ("dp", "context"), axis=0, tiled=True),
        lax.all_gather(w_key, ("dp", "context"), axis=0, tiled=True),
        lax.all_gather(w_value, ("dp", "context"), axis=0, tiled=True),
        lax.all_gather(w_out, ("dp", "context"), axis=1, tiled=True),
        lax.all_gather(w_gate, ("dp", "context"), axis=0, tiled=True),
        lax.all_gather(w_up, ("dp", "context"), axis=0, tiled=True),
        lax.all_gather(w_down, ("dp", "context"), axis=1, tiled=True),
    )
    full_one, full_two, query_mat, key_mat, value_mat, out_mat, gate_mat, up_mat, down_mat = (
        gathered
    )
    heads_kv = key_mat.shape[1] // HEAD
    heads_q = query_mat.shape[1] // HEAD
    group_size = heads_q // heads_kv
    score_scale = HEAD ** (-0.5)
    half_size = HEAD // 2
    inv_freqs = theta_base ** (-2.0 * jnp.arange(half_size, dtype=jnp.float32) / HEAD)
    angles = positions.astype(jnp.float32)[:, :, None] * inv_freqs
    cos_part = jnp.cos(angles)[:, :, None, :]
    sin_part = jnp.sin(angles)[:, :, None, :]
    flat_in = tokens.astype(jnp.float32).reshape(row_count, model_width)
    unit_one, inverse_one, normed = norm_forward(flat_in, full_one)
    query_proj = jnp.dot(normed, query_mat, preferred_element_type=jnp.float32).reshape(
        slot_count, seq_count, heads_q, HEAD
    )
    key_proj = jnp.dot(normed, key_mat, preferred_element_type=jnp.float32).reshape(
        slot_count, seq_count, heads_kv, HEAD
    )
    value_low = (
        jnp.dot(normed, value_mat, preferred_element_type=jnp.float32)
        .astype(jnp.bfloat16)
        .reshape(slot_count, seq_count, heads_kv * HEAD)
    )
    queries = rotate(query_proj, cos_part, sin_part).astype(jnp.bfloat16)
    keys_low = (
        rotate(key_proj, cos_part, sin_part)
        .astype(jnp.bfloat16)
        .reshape(slot_count, seq_count, heads_kv * HEAD)
    )
    query_seq = jnp.transpose(
        queries.reshape(slot_count, seq_count, heads_kv, group_size, HEAD), (1, 2, 3, 0, 4)
    )
    query_pos = positions.T
    stat_shape = (seq_count, heads_kv, group_size, slot_count)
    initial = (
        jnp.full(stat_shape, masked_value, jnp.float32),
        jnp.zeros(stat_shape, jnp.float32),
        jnp.zeros(stat_shape + (HEAD,), jnp.float32),
    )
    key_piece = lax.all_gather(keys_low, "context", axis=0, tiled=True)
    value_piece = lax.all_gather(value_low, "context", axis=0, tiled=True)
    pos_piece = lax.all_gather(positions, "context", axis=0, tiled=True)
    piece_len = key_piece.shape[0]
    key_seq = jnp.transpose(key_piece.reshape(piece_len, seq_count, heads_kv, HEAD), (1, 2, 0, 3))
    value_seq = jnp.transpose(
        value_piece.reshape(piece_len, seq_count, heads_kv, HEAD), (1, 2, 0, 3)
    )
    pos_seq = pos_piece.T

    def per_sequence(seq_items):
        peak_val, totals, accum_vals, query_one, qpos_one, key_one, value_one, kpos_one = seq_items
        raw_scores = (
            jnp.einsum("hgqd,hkd->hgqk", query_one, key_one, preferred_element_type=jnp.float32)
            * score_scale
        )
        allowed = kpos_one[None, None, None, :] <= qpos_one[None, None, :, None]
        masked = jnp.where(allowed, raw_scores, masked_value)
        new_peak = jnp.maximum(peak_val, jnp.max(masked, axis=-1))
        decay_vals = jnp.exp(peak_val - new_peak)
        weights = jnp.where(allowed, jnp.exp(masked - new_peak[..., None]), 0.0)
        totals = totals * decay_vals + jnp.sum(weights, axis=-1)
        accum_vals = accum_vals * decay_vals[..., None] + jnp.einsum(
            "hgqk,hkd->hgqd",
            weights.astype(jnp.bfloat16),
            value_one,
            preferred_element_type=jnp.float32,
        )
        return (new_peak, totals, accum_vals)

    peak_val, totals, accum_vals = lax.map(
        per_sequence,
        (initial[0], initial[1], initial[2], query_seq, query_pos, key_seq, value_seq, pos_seq),
    )
    log_total = peak_val + jnp.log(totals)
    mixed_seq = accum_vals / totals[..., None]
    mixed_low = (
        jnp.transpose(mixed_seq, (3, 0, 1, 2, 4))
        .reshape(row_count, heads_q * HEAD)
        .astype(jnp.bfloat16)
    )
    branch = lax.psum(
        jnp.dot(mixed_low, out_mat, preferred_element_type=jnp.float32).astype(jnp.bfloat16),
        "tensor",
    ).astype(jnp.float32)
    middle = flat_in + branch
    unit_two, inverse_two, second = norm_forward(middle, full_two)
    gate_vals = jnp.dot(second, gate_mat, preferred_element_type=jnp.float32)
    up_vals = jnp.dot(second, up_mat, preferred_element_type=jnp.float32)
    sigmoid_vals = jax.nn.sigmoid(gate_vals)
    silu_vals = gate_vals * sigmoid_vals
    hidden = (silu_vals * up_vals).astype(jnp.bfloat16)
    mlp_part = lax.psum(
        jnp.dot(hidden, down_mat, preferred_element_type=jnp.float32).astype(jnp.bfloat16), "tensor"
    ).astype(jnp.float32)
    layer_out = (middle + mlp_part).astype(jnp.bfloat16).reshape(slot_count, seq_count, model_width)
    regathered = (
        lax.all_gather(gain_one, ("dp", "context"), axis=0, tiled=True),
        lax.all_gather(gain_two, ("dp", "context"), axis=0, tiled=True),
        lax.all_gather(w_query, ("dp", "context"), axis=0, tiled=True),
        lax.all_gather(w_key, ("dp", "context"), axis=0, tiled=True),
        lax.all_gather(w_value, ("dp", "context"), axis=0, tiled=True),
        lax.all_gather(w_out, ("dp", "context"), axis=1, tiled=True),
        lax.all_gather(w_gate, ("dp", "context"), axis=0, tiled=True),
        lax.all_gather(w_up, ("dp", "context"), axis=0, tiled=True),
        lax.all_gather(w_down, ("dp", "context"), axis=1, tiled=True),
    )
    full_one, full_two, query_mat, key_mat, value_mat, out_mat, gate_mat, up_mat, down_mat = (
        regathered
    )
    grad_low = cotangent.reshape(row_count, model_width)
    grad_down = contract_rows(hidden, grad_low)
    grad_hidden = contract_cols(grad_low, down_mat)
    grad_gate_low = (
        grad_hidden * up_vals * sigmoid_vals * (1.0 + gate_vals * (1.0 - sigmoid_vals))
    ).astype(jnp.bfloat16)
    grad_up_low = (grad_hidden * silu_vals).astype(jnp.bfloat16)
    grad_gate = contract_rows(second, grad_gate_low)
    grad_up = contract_rows(second, grad_up_low)
    grad_second = lax.psum(
        (contract_cols(grad_gate_low, gate_mat) + contract_cols(grad_up_low, up_mat)).astype(
            jnp.bfloat16
        ),
        "tensor",
    ).astype(jnp.float32)
    grad_mid_norm, grad_gain_two = norm_backward(grad_second, unit_two, inverse_two, full_two)
    grad_middle = grad_low.astype(jnp.float32) + grad_mid_norm
    grad_mid_low = grad_middle.astype(jnp.bfloat16)
    grad_out = contract_rows(mixed_low, grad_mid_low)
    grad_mixed = contract_cols(grad_mid_low, out_mat).astype(jnp.bfloat16)
    grad_mixed_seq = jnp.transpose(
        grad_mixed.reshape(slot_count, seq_count, heads_kv, group_size, HEAD), (1, 2, 3, 0, 4)
    )
    delta_rows = jnp.sum(grad_mixed_seq.astype(jnp.float32) * mixed_seq, axis=-1)
    kv_width = heads_kv * HEAD

    def block_grads(grad_query_acc, key_blk, value_blk, pos_blk):
        block_len = key_blk.shape[0]
        key_seq = jnp.transpose(key_blk.reshape(block_len, seq_count, heads_kv, HEAD), (1, 2, 0, 3))
        value_seq = jnp.transpose(
            value_blk.reshape(block_len, seq_count, heads_kv, HEAD), (1, 2, 0, 3)
        )
        raw_scores = (
            jnp.einsum("shgqd,shkd->shgqk", query_seq, key_seq, preferred_element_type=jnp.float32)
            * score_scale
        )
        allowed = pos_blk.T[:, None, None, None, :] <= query_pos[:, None, None, :, None]
        prob_vals = jnp.where(
            allowed,
            jnp.exp(jnp.where(allowed, raw_scores - log_total[..., None], masked_value)),
            0.0,
        )
        grad_value_blk = jnp.einsum(
            "shgqk,shgqd->kshd",
            prob_vals.astype(jnp.bfloat16),
            grad_mixed_seq,
            preferred_element_type=jnp.float32,
        )
        grad_probs = jnp.einsum(
            "shgqd,shkd->shgqk", grad_mixed_seq, value_seq, preferred_element_type=jnp.float32
        )
        grad_scores = (prob_vals * (grad_probs - delta_rows[..., None])).astype(jnp.bfloat16)
        grad_query_acc = grad_query_acc + jnp.einsum(
            "shgqk,shkd->shgqd", grad_scores, key_seq, preferred_element_type=jnp.float32
        )
        grad_key_blk = jnp.einsum(
            "shgqk,shgqd->kshd", grad_scores, query_seq, preferred_element_type=jnp.float32
        )
        return (
            grad_query_acc,
            grad_key_blk.reshape(block_len, seq_count, kv_width),
            grad_value_blk.reshape(block_len, seq_count, kv_width),
        )

    zero_query = jnp.zeros(stat_shape + (HEAD,), jnp.float32)
    key_all, value_all, pos_all = (
        lax.all_gather(keys_low, "context", axis=0, tiled=True),
        lax.all_gather(value_low, "context", axis=0, tiled=True),
        lax.all_gather(positions, "context", axis=0, tiled=True),
    )
    total_len = key_all.shape[0]
    block_size = min(512, total_len)
    block_count = total_len // block_size

    def key_block(grad_query_acc, block_items):
        key_blk, value_blk, pos_blk = block_items
        grad_query_acc, grad_key_blk, grad_value_blk = block_grads(
            grad_query_acc, key_blk, value_blk, pos_blk
        )
        return (grad_query_acc, (grad_key_blk, grad_value_blk))

    grad_query_acc, (grad_keys_all, grad_values_all) = lax.scan(
        key_block,
        zero_query,
        (
            key_all.reshape(block_count, block_size, seq_count, kv_width),
            value_all.reshape(block_count, block_size, seq_count, kv_width),
            pos_all.reshape(block_count, block_size, seq_count),
        ),
    )
    grad_key_own, grad_value_own = (
        lax.psum_scatter(
            grad_keys_all.reshape(total_len, seq_count, kv_width).astype(jnp.bfloat16),
            "context",
            scatter_dimension=0,
            tiled=True,
        ).astype(jnp.float32),
        lax.psum_scatter(
            grad_values_all.reshape(total_len, seq_count, kv_width).astype(jnp.bfloat16),
            "context",
            scatter_dimension=0,
            tiled=True,
        ).astype(jnp.float32),
    )
    grad_rot_q = jnp.transpose(grad_query_acc * score_scale, (3, 0, 1, 2, 4)).reshape(
        slot_count, seq_count, heads_q, HEAD
    )
    grad_q_low = (
        rotate(grad_rot_q, cos_part, -sin_part)
        .reshape(row_count, heads_q * HEAD)
        .astype(jnp.bfloat16)
    )
    grad_rot_k = (grad_key_own * score_scale).reshape(slot_count, seq_count, heads_kv, HEAD)
    grad_k_low = (
        rotate(grad_rot_k, cos_part, -sin_part).reshape(row_count, kv_width).astype(jnp.bfloat16)
    )
    grad_v_low = grad_value_own.reshape(row_count, kv_width).astype(jnp.bfloat16)
    grad_query = contract_rows(normed, grad_q_low)
    grad_key = contract_rows(normed, grad_k_low)
    grad_value = contract_rows(normed, grad_v_low)
    grad_normed = lax.psum(
        (
            contract_cols(grad_q_low, query_mat)
            + contract_cols(grad_k_low, key_mat)
            + contract_cols(grad_v_low, value_mat)
        ).astype(jnp.bfloat16),
        "tensor",
    ).astype(jnp.float32)
    grad_in_norm, grad_gain_one = norm_backward(grad_normed, unit_one, inverse_one, full_one)
    input_grad = (grad_middle + grad_in_norm).reshape(slot_count, seq_count, model_width)
    reduced = (
        lax.psum_scatter(grad_gain_one, ("dp", "context"), scatter_dimension=0, tiled=True),
        lax.psum_scatter(grad_gain_two, ("dp", "context"), scatter_dimension=0, tiled=True),
        lax.psum_scatter(grad_query, ("dp", "context"), scatter_dimension=0, tiled=True),
        lax.psum_scatter(grad_key, ("dp", "context"), scatter_dimension=0, tiled=True),
        lax.psum_scatter(grad_value, ("dp", "context"), scatter_dimension=0, tiled=True),
        lax.psum_scatter(grad_out, ("dp", "context"), scatter_dimension=1, tiled=True),
        lax.psum_scatter(grad_gate, ("dp", "context"), scatter_dimension=0, tiled=True),
        lax.psum_scatter(grad_up, ("dp", "context"), scatter_dimension=0, tiled=True),
        lax.psum_scatter(grad_down, ("dp", "context"), scatter_dimension=1, tiled=True),
    )
    return (
        layer_out,
        input_grad,
        reduced[0],
        reduced[1],
        reduced[2],
        reduced[3],
        reduced[4],
        reduced[5],
        reduced[6],
        reduced[7],
        reduced[8],
    )


WIDE = 128
RUN = 256
TILE = 512
LOG2_E = 1.4426950408889634
MESH = pl.DeviceIdType.MESH
VMEM_LIMIT = 56 * 1024 * 1024


def any_spec():
    return pl.BlockSpec(memory_space=pl.ANY)


def vmem_spec():
    return pl.BlockSpec(memory_space=pltpu.VMEM)


def place():
    return lax.axis_index("dp"), lax.axis_index("context"), lax.axis_index("tensor")


def greet(devices):
    barrier = pltpu.get_barrier_semaphore()
    for device in devices:
        pl.semaphore_signal(barrier, inc=1, device_id=device, device_id_type=MESH)
    pl.semaphore_wait(barrier, len(devices))


def greet_sequence():
    row, spot, core = place()
    greet(
        [
            (row, lax.rem(spot + shift, 8), lax.rem(core + flip, 2))
            for shift in range(8)
            for flip in range(2)
            if shift or flip
        ]
    )


def remote(source, target, send, recv, device):
    return pltpu.make_async_remote_copy(
        src_ref=source,
        dst_ref=target,
        send_sem=send,
        recv_sem=recv,
        device_id=device,
        device_id_type=MESH,
    )


def move(source, target, send, recv, device, is_self):
    @pl.when(is_self)
    def _():
        pltpu.make_async_copy(source, target, recv).start()

    @pl.when(jnp.logical_not(is_self))
    def _():
        remote(source, target, send, recv, device).start()


def spread_matrix(heads):
    shape = (heads * HEAD, heads * WIDE)
    rows = lax.broadcasted_iota(jnp.int32, shape, 0)
    cols = lax.broadcasted_iota(jnp.int32, shape, 1)
    dims = rows % HEAD
    target = (rows // HEAD) * WIDE + dims + jnp.where(dims >= HEAD // 2, (WIDE - HEAD) // 2, 0)
    return (cols == target).astype(jnp.bfloat16)


def lane_tables(positions):
    half = HEAD // 2
    inv_freqs = theta_base ** (-2.0 * jnp.arange(half, dtype=jnp.float32) / HEAD)
    gap = jnp.zeros((WIDE // 2 - half,), jnp.float32)
    freqs = jnp.concatenate([inv_freqs, gap, inv_freqs, gap])
    sign = jnp.where(jnp.arange(WIDE) < WIDE // 2, -1.0, 1.0)
    angles = positions.astype(jnp.float32)[:, None] * freqs
    return jnp.cos(angles), jnp.sin(angles) * sign


def project_kernel(normed, weight, spread, cos_tab, sin_tab, q_out, kv_out):
    step = pl.program_id(0)
    wide = jnp.dot(weight[...], spread[...], preferred_element_type=jnp.float32)
    proj = jnp.dot(normed[...], wide.astype(jnp.bfloat16), preferred_element_type=jnp.float32)
    for head in range(4):
        part = proj[:, head * WIDE : (head + 1) * WIDE]
        turned = part * cos_tab[0] + pltpu.roll(part, WIDE // 2, 1) * sin_tab[0]
        low = turned.astype(jnp.bfloat16)

        @pl.when(step < 2)
        def _():
            q_out[head] = low

        @pl.when(step >= 2)
        def _():
            kv_out[head, 0] = low


def project(normed, weights, spread, cos_tab, sin_tab):
    rows, width = normed.shape
    return pl.pallas_call(
        project_kernel,
        grid=(4,),
        in_specs=[
            pl.BlockSpec((rows, width), lambda s: (0, 0)),
            pl.BlockSpec((width, 4 * HEAD), lambda s: (0, s)),
            pl.BlockSpec((4 * HEAD, 4 * WIDE), lambda s: (0, 0)),
            pl.BlockSpec((1, rows, WIDE), lambda s: (s // 3, 0, 0)),
            pl.BlockSpec((1, rows, WIDE), lambda s: (s // 3, 0, 0)),
        ],
        out_specs=[
            pl.BlockSpec((4, rows, WIDE), lambda s: (jnp.minimum(s, 1), 0, 0)),
            pl.BlockSpec((4, 1, rows, WIDE), lambda s: (0, jnp.maximum(s - 2, 0), 0, 0)),
        ],
        out_shape=[
            jax.ShapeDtypeStruct((8, rows, WIDE), jnp.bfloat16),
            jax.ShapeDtypeStruct((4, 2, rows, WIDE), jnp.bfloat16),
        ],
        compiler_params=pltpu.CompilerParams(vmem_limit_bytes=VMEM_LIMIT),
        name="project",
    )(normed, weights, spread, cos_tab, sin_tab)


def to_heads_kernel(q_ref, kv_ref, q_all, kv_all, send_q, recv_q, send_kv, recv_kv, send_x, recv_x):
    row, spot, core = place()
    greet_sequence()
    for step in range(4):
        slot = lax.rem(spot + step, 4)
        chip = 4 * core + slot
        for other in range(2):
            is_self = jnp.logical_and(chip == spot, core == other)
            device = (row, chip, other)
            rows = pl.ds(other * RUN, RUN)
            move(
                kv_ref.at[slot, :, rows],
                kv_all.at[spot, :, rows],
                send_kv.at[step, other],
                recv_kv.at[spot],
                device,
                is_self,
            )
            move(
                q_ref.at[2 * slot + other],
                q_all.at[spot],
                send_q.at[step, other],
                recv_q.at[spot],
                device,
                is_self,
            )
    own_rows = pl.ds(pl.multiple_of(core * RUN, RUN), RUN)
    sibling = (row, spot, 1 - core)

    def hand_on(source):
        block = kv_all.at[source, :, own_rows]
        return remote(block, block, send_x.at[source], recv_x.at[source], sibling)

    for step in range(8):
        source = lax.rem(spot + step, 8)
        block = kv_all.at[source, :, own_rows]
        remote(block, block, send_x.at[source], recv_kv.at[source], sibling).wait_recv()
        hand_on(source).start()
    for step in range(8):
        remote(
            q_all.at[step], q_all.at[step], send_x.at[step], recv_q.at[step], sibling
        ).wait_recv()
        hand_on(step).wait()
    for step in range(4):
        slot = lax.rem(spot + step, 4)
        chip = 4 * core + slot
        for other in range(2):

            @pl.when(jnp.logical_not(jnp.logical_and(chip == spot, core == other)))
            def _():
                rows = pl.ds(other * RUN, RUN)
                device = (row, chip, other)
                remote(
                    kv_ref.at[slot, :, rows],
                    kv_all.at[spot, :, rows],
                    send_kv.at[step, other],
                    recv_kv.at[spot],
                    device,
                ).wait_send()
                remote(
                    q_ref.at[2 * slot + other],
                    q_all.at[spot],
                    send_q.at[step, other],
                    recv_q.at[spot],
                    device,
                ).wait_send()


def to_heads(q_heads, kv_heads):
    dma = pltpu.SemaphoreType.DMA
    rows = q_heads.shape[1]
    return pl.pallas_call(
        to_heads_kernel,
        in_specs=[any_spec(), any_spec()],
        out_specs=[any_spec(), any_spec()],
        out_shape=[
            jax.ShapeDtypeStruct((8, rows, WIDE), jnp.bfloat16),
            jax.ShapeDtypeStruct((8, 2, rows, WIDE), jnp.bfloat16),
        ],
        scratch_shapes=[dma((4, 2)), dma((8,)), dma((4, 2)), dma((8,)), dma((8,)), dma((8,))],
        compiler_params=pltpu.CompilerParams(collective_id=1, has_side_effects=True),
        name="to_heads",
    )(q_heads, kv_heads)


def grads_to_heads_kernel(d_ref, d_all, send, recv):
    row, spot, core = place()
    greet_sequence()
    copies = []
    for step in range(4):
        slot = lax.rem(spot + step, 4)
        chip = 4 * core + slot
        for other in range(2):
            is_self = jnp.logical_and(chip == spot, core == other)
            copies.append(
                (
                    (
                        d_ref.at[2 * slot + other],
                        d_all.at[spot],
                        send.at[step, other],
                        recv.at[spot],
                        (row, chip, other),
                    ),
                    is_self,
                )
            )
    for parts, is_self in copies:
        move(*parts, is_self)
    for step in range(8):
        remote(
            d_all.at[step], d_all.at[step], send.at[0, 0], recv.at[step], (row, spot, 1 - core)
        ).wait_recv()
    for parts, is_self in copies:

        @pl.when(jnp.logical_not(is_self))
        def _():
            remote(*parts).wait_send()


def grads_to_heads(grad_heads):
    dma = pltpu.SemaphoreType.DMA
    return pl.pallas_call(
        grads_to_heads_kernel,
        in_specs=[any_spec()],
        out_specs=any_spec(),
        out_shape=jax.ShapeDtypeStruct(grad_heads.shape, jnp.bfloat16),
        scratch_shapes=[dma((4, 2)), dma((8,))],
        compiler_params=pltpu.CompilerParams(collective_id=2, has_side_effects=True),
        name="grads_to_heads",
    )(grad_heads)


def return_copies(ref, out, send, recv):
    row, spot, core = place()
    head = 2 * lax.rem(spot, 4) + core
    owner = spot // 4
    copies = []
    for step in range(8):
        chip = lax.rem(spot + step, 8)
        is_self = (owner == core) if step == 0 else False
        parts = (ref.at[chip], out.at[head], send.at[step], recv.at[head], (row, chip, owner))
        copies.append((parts, is_self))
    return copies


def start_return(copies):
    for parts, is_self in copies:
        if is_self is False:
            remote(*parts).start()
        else:
            move(*parts, is_self)


def finish_return(copies, out, send, recv):
    row, spot, core = place()
    for head in range(8):
        remote(
            out.at[head], out.at[head], send.at[0], recv.at[head], (row, spot, 1 - core)
        ).wait_recv()
    for parts, is_self in copies:
        if is_self is False:
            remote(*parts).wait_send()
        else:

            @pl.when(jnp.logical_not(is_self))
            def _():
                remote(*parts).wait_send()


def to_tokens_kernel(ref, out, send, recv):
    greet_sequence()
    copies = return_copies(ref, out, send, recv)
    start_return(copies)
    finish_return(copies, out, send, recv)


def to_tokens(mixed):
    dma = pltpu.SemaphoreType.DMA
    return pl.pallas_call(
        to_tokens_kernel,
        in_specs=[any_spec()],
        out_specs=any_spec(),
        out_shape=jax.ShapeDtypeStruct(mixed.shape, jnp.bfloat16),
        scratch_shapes=[dma((8,)), dma((8,))],
        compiler_params=pltpu.CompilerParams(collective_id=3, has_side_effects=True),
        name="to_tokens",
    )(mixed)


def grads_to_tokens_kernel(
    dq_ref, dkv_ref, dq_out, dkv_out, own, other, send, recv, send_x, recv_x, local, send_k, recv_k
):
    row, spot, core = place()
    greet_sequence()
    own_rows = pl.ds(pl.multiple_of(core * RUN, RUN), RUN)
    other_rows = pl.ds(pl.multiple_of((1 - core) * RUN, RUN), RUN)
    swap = remote(
        dkv_ref.at[:, :, other_rows], other, send_x, recv_x, (row, spot, 1 - core)
    )
    swap.start()
    load = pltpu.make_async_copy(dkv_ref.at[:, :, own_rows], own, local)
    load.start()
    copies = return_copies(dq_ref, dq_out, send, recv)
    start_return(copies)
    load.wait()
    swap.wait()
    slot = lax.rem(spot, 4)
    owner = spot // 4
    backs = []
    for step in range(8):
        chip = lax.rem(spot + step, 8)
        total = own[:, chip].astype(jnp.float32) + other[:, chip].astype(jnp.float32)
        own[:, chip] = total.astype(jnp.bfloat16)
        parts = (
            own.at[:, chip],
            dkv_out.at[slot, :, own_rows],
            send_k.at[step],
            recv_k.at[slot, core],
            (row, chip, owner),
        )
        is_self = (owner == core) if step == 0 else False
        backs.append((parts, is_self))
        start_return(backs[-1:])
    for slot_in in range(4):
        for core_in in range(2):
            target = dkv_out.at[slot_in, :, pl.ds(core_in * RUN, RUN)]
            remote(
                target, target, send_k.at[0], recv_k.at[slot_in, core_in], (row, spot, 1 - core)
            ).wait_recv()
    for parts, is_self in backs:
        if is_self is False:
            remote(*parts).wait_send()
        else:

            @pl.when(jnp.logical_not(is_self))
            def _():
                remote(*parts).wait_send()

    finish_return(copies, dq_out, send, recv)


def grads_to_tokens(dq, dkv):
    dma = pltpu.SemaphoreType.DMA
    rows = dq.shape[1]
    return pl.pallas_call(
        grads_to_tokens_kernel,
        in_specs=[any_spec(), any_spec()],
        out_specs=[any_spec(), any_spec()],
        out_shape=[
            jax.ShapeDtypeStruct((8, rows, WIDE), jnp.bfloat16),
            jax.ShapeDtypeStruct((4, 2, rows, WIDE), jnp.bfloat16),
        ],
        scratch_shapes=[
            pltpu.VMEM((2, 8, RUN, WIDE), jnp.bfloat16),
            pltpu.VMEM((2, 8, RUN, WIDE), jnp.bfloat16),
            dma((8,)),
            dma((8,)),
            dma(()),
            dma(()),
            dma(()),
            dma((8,)),
            dma((4, 2)),
        ],
        compiler_params=pltpu.CompilerParams(
            collective_id=4, has_side_effects=True, vmem_limit_bytes=VMEM_LIMIT
        ),
        name="grads_to_tokens",
    )(dq, dkv)


def pair_sum_kernel(part, total, other, send, recv):
    row, spot, core = place()
    sibling = (row, spot, 1 - core)
    greet([sibling])
    pieces = send.shape[0]
    rows = part.shape[0] // pieces

    def piece(index):
        cut = pl.ds(index * rows, rows)
        return remote(part.at[cut], other.at[cut], send.at[index], recv.at[index], sibling)

    for index in range(pieces):
        piece(index).start()
    for index in range(pieces):
        cut = pl.ds(index * rows, rows)
        piece(index).wait()
        total[cut] = part[cut].astype(jnp.float32) + other[cut].astype(jnp.float32)


def pair_sum(part, collective_id):
    dma = pltpu.SemaphoreType.DMA
    return pl.pallas_call(
        pair_sum_kernel,
        in_specs=[vmem_spec()],
        out_specs=vmem_spec(),
        out_shape=jax.ShapeDtypeStruct(part.shape, jnp.float32),
        scratch_shapes=[pltpu.VMEM(part.shape, part.dtype), dma((4,)), dma((4,))],
        compiler_params=pltpu.CompilerParams(
            collective_id=collective_id, has_side_effects=True, vmem_limit_bytes=VMEM_LIMIT
        ),
        name="pair_sum",
    )(part)


def tile_at(index, size):
    return pl.ds(pl.multiple_of(index * size, size), size)


def causal(scores):
    keys = lax.broadcasted_iota(jnp.int32, scores.shape, 0)
    queries = lax.broadcasted_iota(jnp.int32, scores.shape, 1)
    return jnp.where(keys <= queries, scores, masked_value)


def attend_kernel(order, q_in, kv_in, mixed, mixed_t, lse, q_t, keys, v_t):
    runs = q_in.shape[0] // RUN

    def sort_run(index, carry):
        run = order[index]
        cols = tile_at(index, RUN)
        q_t[:, cols] = q_in[tile_at(run, RUN)].T
        keys[cols] = kv_in[run // 2, 0, tile_at(run % 2, RUN)]
        v_t[:, cols] = kv_in[run // 2, 1, tile_at(run % 2, RUN)].T
        return carry

    lax.fori_loop(0, runs, sort_run, 0)
    scale = HEAD ** (-0.5) * LOG2_E

    def query_tile(index, carry):
        cols = tile_at(index, TILE)
        queries = q_t[:, cols]

        def step(scores, block, peak, total, mix):
            high = jnp.maximum(peak, jnp.max(scores, axis=0, keepdims=True))
            decay = jnp.exp2(peak - high)
            weights = jnp.exp2(scores - high)
            total = total * decay + jnp.sum(weights, axis=0, keepdims=True)
            mix = mix * decay + jnp.dot(
                v_t[:, tile_at(block, TILE)],
                weights.astype(jnp.bfloat16),
                preferred_element_type=jnp.float32,
            )
            return high, total, mix

        def scores_of(block):
            return (
                jnp.dot(keys[tile_at(block, TILE)], queries, preferred_element_type=jnp.float32)
                * scale
            )

        state = (
            jnp.full((1, TILE), masked_value, jnp.float32),
            jnp.zeros((1, TILE), jnp.float32),
            jnp.zeros((WIDE, TILE), jnp.float32),
        )
        state = step(causal(scores_of(index)), index, *state)
        peak, total, mix = lax.fori_loop(
            0, index, lambda block, now: step(scores_of(block), block, *now), state
        )
        mix = mix / total
        mixed_t[:, cols] = mix
        lse[:, cols] = peak + jnp.log2(total)
        for half in range(TILE // RUN):
            run = order[index * (TILE // RUN) + half]
            mixed[tile_at(run, RUN)] = mix[:, half * RUN : (half + 1) * RUN].T.astype(jnp.bfloat16)
        return carry

    lax.fori_loop(0, q_in.shape[0] // TILE, query_tile, 0)


def attend(order, q_all, kv_all):
    length = q_all.shape[0]
    low = jnp.bfloat16
    return pl.pallas_call(
        attend_kernel,
        in_specs=[pl.BlockSpec(memory_space=pltpu.SMEM), vmem_spec(), vmem_spec()],
        out_specs=[vmem_spec()] * 3,
        out_shape=[
            jax.ShapeDtypeStruct((length, WIDE), low),
            jax.ShapeDtypeStruct((WIDE, length), jnp.float32),
            jax.ShapeDtypeStruct((1, length), jnp.float32),
        ],
        scratch_shapes=[
            pltpu.VMEM((WIDE, length), low),
            pltpu.VMEM((length, WIDE), low),
            pltpu.VMEM((WIDE, length), low),
        ],
        compiler_params=pltpu.CompilerParams(vmem_limit_bytes=VMEM_LIMIT),
        cost_estimate=pl.CostEstimate(
            flops=2 * length * length * WIDE, bytes_accessed=8 * length * WIDE, transcendentals=0
        ),
        name="attend",
    )(order, q_all, kv_all)


def attend_back_kernel(
    order, q_in, kv_in, d_in, mixed_t, lse, dq, dkv, q, q_t, k, k_t, v, d, d_t, delta, dq_t, dk, dv
):
    runs = q_in.shape[0] // RUN
    tiles = q_in.shape[0] // TILE

    def sort_run(index, carry):
        run = order[index]
        cols = tile_at(index, RUN)
        q_run = q_in[tile_at(run, RUN)]
        k_run = kv_in[run // 2, 0, tile_at(run % 2, RUN)]
        d_run = d_in[tile_at(run, RUN)]
        d_turned = d_run.T
        q[cols] = q_run
        q_t[:, cols] = q_run.T
        k[cols] = k_run
        k_t[:, cols] = k_run.T
        v[cols] = kv_in[run // 2, 1, tile_at(run % 2, RUN)]
        d[cols] = d_run
        d_t[:, cols] = d_turned
        delta[:, cols] = jnp.sum(
            d_turned.astype(jnp.float32) * mixed_t[:, cols], axis=0, keepdims=True
        )
        return carry

    lax.fori_loop(0, runs, sort_run, 0)
    scale = HEAD ** (-0.5)
    dq_t[...] = jnp.zeros_like(dq_t)

    def key_tile(block, carry):
        rows = tile_at(block, TILE)
        keys, keys_t, values = k[rows], k_t[:, rows], v[rows]
        dk[...] = jnp.zeros_like(dk)
        dv[...] = jnp.zeros_like(dv)

        def query_tile(index, diagonal):
            cols = tile_at(index, TILE)
            scores = jnp.dot(keys, q_t[:, cols], preferred_element_type=jnp.float32) * (
                scale * LOG2_E
            )
            if diagonal:
                scores = causal(scores)
            probs = jnp.exp2(scores - lse[:, cols])
            dv[...] += jnp.dot(
                probs.astype(jnp.bfloat16), d[cols], preferred_element_type=jnp.float32
            )
            grad_probs = jnp.dot(values, d_t[:, cols], preferred_element_type=jnp.float32)
            grad_scores = (probs * (grad_probs - delta[:, cols])).astype(jnp.bfloat16)
            dk[...] += jnp.dot(grad_scores, q[cols], preferred_element_type=jnp.float32)
            dq_t[:, cols] += jnp.dot(keys_t, grad_scores, preferred_element_type=jnp.float32)

        query_tile(block, True)

        def later(index, inner):
            query_tile(index, False)
            return inner

        lax.fori_loop(block + 1, tiles, later, 0)
        for half in range(TILE // RUN):
            run = order[block * (TILE // RUN) + half]
            cut = pl.ds(half * RUN, RUN)
            dkv[0, tile_at(run, RUN)] = (dk[cut] * scale).astype(jnp.bfloat16)
            dkv[1, tile_at(run, RUN)] = dv[cut].astype(jnp.bfloat16)
        return carry

    lax.fori_loop(0, tiles, key_tile, 0)

    def unsort_run(index, carry):
        run = order[index]
        dq[tile_at(run, RUN)] = (dq_t[:, tile_at(index, RUN)] * scale).T.astype(jnp.bfloat16)
        return carry

    lax.fori_loop(0, runs, unsort_run, 0)


def attend_back(order, q_all, kv_all, d_all, mixed_t, lse):
    length = q_all.shape[0]
    low = jnp.bfloat16
    tall = pltpu.VMEM((length, WIDE), low)
    flat = pltpu.VMEM((WIDE, length), low)
    return pl.pallas_call(
        attend_back_kernel,
        in_specs=[pl.BlockSpec(memory_space=pltpu.SMEM)] + [vmem_spec()] * 5,
        out_specs=[vmem_spec()] * 2,
        out_shape=[
            jax.ShapeDtypeStruct((length, WIDE), low),
            jax.ShapeDtypeStruct((2, length, WIDE), low),
        ],
        scratch_shapes=[
            tall,
            flat,
            tall,
            flat,
            tall,
            tall,
            flat,
            pltpu.VMEM((1, length), jnp.float32),
            pltpu.VMEM((WIDE, length), jnp.float32),
            pltpu.VMEM((TILE, WIDE), jnp.float32),
            pltpu.VMEM((TILE, WIDE), jnp.float32),
        ],
        compiler_params=pltpu.CompilerParams(vmem_limit_bytes=VMEM_LIMIT),
        cost_estimate=pl.CostEstimate(
            flops=5 * length * length * WIDE, bytes_accessed=20 * length * WIDE, transcendentals=0
        ),
        name="attend_back",
    )(order, q_all, kv_all, d_all, mixed_t, lse)


def dot_f32(left, right):
    return jnp.dot(left, right, preferred_element_type=jnp.float32)


def by_heads(
    tokens,
    positions,
    gain_one,
    gain_two,
    w_query,
    w_key,
    w_value,
    w_out,
    w_gate,
    w_up,
    w_down,
    cotangent,
):
    low = jnp.bfloat16
    rows, _, width = tokens.shape
    both = ("dp", "context")
    share = gain_one.shape[0]
    hidden_width = w_gate.shape[1]
    length = rows * 8

    run_ids = (positions[::RUN, 0] // RUN).astype(low)
    extra = jnp.zeros((share, WIDE), low)
    extra = extra.at[:, 0].set(gain_one).at[:, 1].set(gain_two).at[: rows // RUN, 2].set(run_ids)
    near = lax.all_gather(
        jnp.concatenate([w_query, w_key, w_value, w_out.T, extra], axis=1), both, axis=0, tiled=True
    )
    far = lax.all_gather(
        jnp.concatenate([w_gate, w_up, w_down.T], axis=1), both, axis=0, tiled=True
    )
    qkv_width = w_query.shape[1] + w_key.shape[1] + w_value.shape[1]
    out_width = w_out.shape[0]
    qkv_mat = near[:, :qkv_width]
    out_mat_t = near[:, qkv_width : qkv_width + out_width]
    extras = near[:, qkv_width + out_width :]
    full_one, full_two = extras[:, 0], extras[:, 1]
    row = lax.axis_index("dp")
    ids = lax.dynamic_slice_in_dim(extras[:, 2].reshape(2, 8, share), row, 1, 0)[0, :, : rows // RUN]
    ids = ids.reshape(-1).astype(jnp.int32)
    count = ids.shape[0]
    order = jnp.sum(
        jnp.where(ids[None, :] == jnp.arange(count)[:, None], jnp.arange(count)[None, :], 0), axis=1
    ).astype(jnp.int32)
    gate_mat = far[:, :hidden_width]
    up_mat = far[:, hidden_width : 2 * hidden_width]
    down_mat_t = far[:, 2 * hidden_width :]

    spread = spread_matrix(8)
    cos_tab, sin_tab = lane_tables(positions[:, 0])
    flat_in = tokens.astype(jnp.float32).reshape(rows, width)
    unit_one, inverse_one, normed = norm_forward(flat_in, full_one)
    q_heads, kv_heads = project(
        normed,
        qkv_mat,
        spread[: 4 * HEAD, : 4 * WIDE],
        jnp.stack([cos_tab, jnp.ones_like(cos_tab)]),
        jnp.stack([sin_tab, jnp.zeros_like(sin_tab)]),
    )
    q_all, kv_all = to_heads(q_heads, kv_heads)
    q_all = q_all.reshape(length, WIDE)
    mixed, mixed_t, lse = attend(order, q_all, kv_all)
    mixed_heads = to_tokens(mixed.reshape(8, rows, WIDE))

    def narrow(heads):
        count = heads.shape[0]
        side = jnp.transpose(heads, (1, 0, 2)).reshape(rows, count * WIDE)
        return contract_cols(side, spread[: count * HEAD, : count * WIDE]).astype(low)

    mixed_low = narrow(mixed_heads)
    middle = flat_in + pair_sum(contract_cols(mixed_low, out_mat_t).astype(low), 5)
    unit_two, inverse_two, second = norm_forward(middle, full_two)
    gate_vals = dot_f32(second, gate_mat)
    up_vals = dot_f32(second, up_mat)
    sigmoid_vals = jax.nn.sigmoid(gate_vals)
    silu_vals = gate_vals * sigmoid_vals
    hidden = (silu_vals * up_vals).astype(low)
    mlp_part = pair_sum(contract_cols(hidden, down_mat_t).astype(low), 6)
    layer_out = (middle + mlp_part).astype(low).reshape(rows, 1, width)

    grad_low = cotangent.reshape(rows, width)
    grad_down_t = contract_rows(grad_low, hidden)
    grad_hidden = dot_f32(grad_low, down_mat_t)
    grad_gate_low = (
        grad_hidden * up_vals * sigmoid_vals * (1.0 + gate_vals * (1.0 - sigmoid_vals))
    ).astype(low)
    grad_up_low = (grad_hidden * silu_vals).astype(low)
    grad_gate = contract_rows(second, grad_gate_low)
    grad_up = contract_rows(second, grad_up_low)
    far_grads = jnp.concatenate(
        [grad_gate.astype(low), grad_up.astype(low), grad_down_t.astype(low)], axis=1
    )
    far_own = lax.psum_scatter(far_grads, both, scatter_dimension=0, tiled=True)
    grad_second = pair_sum(
        (contract_cols(grad_gate_low, gate_mat) + contract_cols(grad_up_low, up_mat)).astype(low), 7
    )
    grad_mid_norm, grad_gain_two = norm_backward(grad_second, unit_two, inverse_two, full_two)
    grad_middle = grad_low.astype(jnp.float32) + grad_mid_norm
    grad_mid_low = grad_middle.astype(low)
    grad_out_t = contract_rows(grad_mid_low, mixed_low)
    grad_mixed = dot_f32(grad_mid_low, out_mat_t).astype(low)
    grad_heads = jnp.transpose(
        dot_f32(grad_mixed, spread).astype(low).reshape(rows, 8, WIDE), (1, 0, 2)
    )
    d_all = grads_to_heads(grad_heads).reshape(length, WIDE)
    dq, dkv = attend_back(order, q_all, kv_all, d_all, mixed_t, lse)
    dq_own, dkv_own = grads_to_tokens(
        dq.reshape(8, rows, WIDE), dkv.reshape(2, 8, rows, WIDE)
    )

    def unturn(heads):
        part = heads.astype(jnp.float32)
        return (part * cos_tab - jnp.roll(part, WIDE // 2, axis=-1) * sin_tab).astype(low)

    grad_qkv_low = jnp.concatenate(
        [narrow(unturn(dq_own)), narrow(unturn(dkv_own[:, 0])), narrow(dkv_own[:, 1])], axis=1
    )
    grad_qkv = contract_rows(normed, grad_qkv_low)
    grad_normed = pair_sum(contract_cols(grad_qkv_low, qkv_mat).astype(low), 8)
    grad_in_norm, grad_gain_one = norm_backward(grad_normed, unit_one, inverse_one, full_one)
    input_grad = (grad_middle + grad_in_norm).reshape(rows, 1, width)
    gains = jnp.zeros((width, WIDE), jnp.float32)
    gains = gains.at[:, 0].set(grad_gain_one).at[:, 1].set(grad_gain_two)
    near_grads = jnp.concatenate(
        [grad_qkv.astype(low), grad_out_t.astype(low), gains.astype(low)], axis=1
    )
    near_own = lax.psum_scatter(near_grads, both, scatter_dimension=0, tiled=True).astype(
        jnp.float32
    )
    far_own = far_own.astype(jnp.float32)
    q_width, k_width = w_query.shape[1], w_key.shape[1]
    return (
        layer_out,
        input_grad,
        near_own[:, qkv_width + out_width],
        near_own[:, qkv_width + out_width + 1],
        near_own[:, :q_width],
        near_own[:, q_width : q_width + k_width],
        near_own[:, q_width + k_width : qkv_width],
        near_own[:, qkv_width : qkv_width + out_width].T,
        far_own[:, :hidden_width],
        far_own[:, hidden_width : 2 * hidden_width],
        far_own[:, 2 * hidden_width :].T,
    )


def solution(mesh):
    sizes = (mesh.shape["dp"], mesh.shape["context"], mesh.shape["tensor"])
    return jax.shard_map(
        by_heads if sizes == (2, 8, 2) else on_device,
        mesh=mesh,
        in_specs=(
            P("context", "dp", None),
            P("context", "dp"),
            P(("dp", "context")),
            P(("dp", "context")),
            P(("dp", "context"), "tensor"),
            P(("dp", "context"), "tensor"),
            P(("dp", "context"), "tensor"),
            P("tensor", ("dp", "context")),
            P(("dp", "context"), "tensor"),
            P(("dp", "context"), "tensor"),
            P("tensor", ("dp", "context")),
            P("context", "dp", None),
        ),
        out_specs=(
            P("context", "dp", None),
            P("context", "dp", None),
            P(("dp", "context")),
            P(("dp", "context")),
            P(("dp", "context"), "tensor"),
            P(("dp", "context"), "tensor"),
            P(("dp", "context"), "tensor"),
            P("tensor", ("dp", "context")),
            P(("dp", "context"), "tensor"),
            P(("dp", "context"), "tensor"),
            P("tensor", ("dp", "context")),
        ),
        check_vma=False,
    )
```

```python
import functools

import jax
import jax.numpy as jnp
from jax import lax
from jax.experimental import pallas as pl
from jax.experimental.pallas import tpu as pltpu
from jax.sharding import PartitionSpec as P

HEAD = 96


epsilon = 1e-05
theta_base = 100000.0
masked_value = -1e30


def norm_forward(values_in, gain_vec):
    inverse = lax.rsqrt(jnp.mean(values_in * values_in, axis=-1, keepdims=True) + epsilon)
    unit_vals = values_in * inverse
    return (unit_vals, inverse, (unit_vals * gain_vec.astype(jnp.float32)).astype(jnp.bfloat16))


def norm_backward(grad_in, unit_vals, inverse, gain_vec):
    scaled = grad_in * gain_vec.astype(jnp.float32)
    grad_vals = inverse * (
        scaled - unit_vals * jnp.mean(scaled * unit_vals, axis=-1, keepdims=True)
    )
    return (grad_vals, jnp.sum(grad_in * unit_vals, axis=0))


def rotate(values_in, cos_part, sin_part):
    half_size = values_in.shape[-1] // 2
    front_half = values_in[..., :half_size]
    back_half = values_in[..., half_size:]
    return jnp.concatenate(
        [
            front_half * cos_part - back_half * sin_part,
            back_half * cos_part + front_half * sin_part,
        ],
        axis=-1,
    )


def contract_rows(left_mat, right_mat):
    return lax.dot_general(
        left_mat, right_mat, (((0,), (0,)), ((), ())), preferred_element_type=jnp.float32
    )


def contract_cols(left_mat, right_mat):
    return lax.dot_general(
        left_mat, right_mat, (((1,), (1,)), ((), ())), preferred_element_type=jnp.float32
    )


def on_device(
    tokens,
    positions,
    gain_one,
    gain_two,
    w_query,
    w_key,
    w_value,
    w_out,
    w_gate,
    w_up,
    w_down,
    cotangent,
):
    slot_count, seq_count, model_width = tokens.shape
    row_count = slot_count * seq_count
    gathered = (
        lax.all_gather(gain_one, ("dp", "context"), axis=0, tiled=True),
        lax.all_gather(gain_two, ("dp", "context"), axis=0, tiled=True),
        lax.all_gather(w_query, ("dp", "context"), axis=0, tiled=True),
        lax.all_gather(w_key, ("dp", "context"), axis=0, tiled=True),
        lax.all_gather(w_value, ("dp", "context"), axis=0, tiled=True),
        lax.all_gather(w_out, ("dp", "context"), axis=1, tiled=True),
        lax.all_gather(w_gate, ("dp", "context"), axis=0, tiled=True),
        lax.all_gather(w_up, ("dp", "context"), axis=0, tiled=True),
        lax.all_gather(w_down, ("dp", "context"), axis=1, tiled=True),
    )
    full_one, full_two, query_mat, key_mat, value_mat, out_mat, gate_mat, up_mat, down_mat = (
        gathered
    )
    heads_kv = key_mat.shape[1] // HEAD
    heads_q = query_mat.shape[1] // HEAD
    group_size = heads_q // heads_kv
    score_scale = HEAD ** (-0.5)
    half_size = HEAD // 2
    inv_freqs = theta_base ** (-2.0 * jnp.arange(half_size, dtype=jnp.float32) / HEAD)
    angles = positions.astype(jnp.float32)[:, :, None] * inv_freqs
    cos_part = jnp.cos(angles)[:, :, None, :]
    sin_part = jnp.sin(angles)[:, :, None, :]
    flat_in = tokens.astype(jnp.float32).reshape(row_count, model_width)
    unit_one, inverse_one, normed = norm_forward(flat_in, full_one)
    query_proj = jnp.dot(normed, query_mat, preferred_element_type=jnp.float32).reshape(
        slot_count, seq_count, heads_q, HEAD
    )
    key_proj = jnp.dot(normed, key_mat, preferred_element_type=jnp.float32).reshape(
        slot_count, seq_count, heads_kv, HEAD
    )
    value_low = (
        jnp.dot(normed, value_mat, preferred_element_type=jnp.float32)
        .astype(jnp.bfloat16)
        .reshape(slot_count, seq_count, heads_kv * HEAD)
    )
    queries = rotate(query_proj, cos_part, sin_part).astype(jnp.bfloat16)
    keys_low = (
        rotate(key_proj, cos_part, sin_part)
        .astype(jnp.bfloat16)
        .reshape(slot_count, seq_count, heads_kv * HEAD)
    )
    query_seq = jnp.transpose(
        queries.reshape(slot_count, seq_count, heads_kv, group_size, HEAD), (1, 2, 3, 0, 4)
    )
    query_pos = positions.T
    stat_shape = (seq_count, heads_kv, group_size, slot_count)
    initial = (
        jnp.full(stat_shape, masked_value, jnp.float32),
        jnp.zeros(stat_shape, jnp.float32),
        jnp.zeros(stat_shape + (HEAD,), jnp.float32),
    )
    key_piece = lax.all_gather(keys_low, "context", axis=0, tiled=True)
    value_piece = lax.all_gather(value_low, "context", axis=0, tiled=True)
    pos_piece = lax.all_gather(positions, "context", axis=0, tiled=True)
    piece_len = key_piece.shape[0]
    key_seq = jnp.transpose(key_piece.reshape(piece_len, seq_count, heads_kv, HEAD), (1, 2, 0, 3))
    value_seq = jnp.transpose(
        value_piece.reshape(piece_len, seq_count, heads_kv, HEAD), (1, 2, 0, 3)
    )
    pos_seq = pos_piece.T

    def per_sequence(seq_items):
        peak_val, totals, accum_vals, query_one, qpos_one, key_one, value_one, kpos_one = seq_items
        raw_scores = (
            jnp.einsum("hgqd,hkd->hgqk", query_one, key_one, preferred_element_type=jnp.float32)
            * score_scale
        )
        allowed = kpos_one[None, None, None, :] <= qpos_one[None, None, :, None]
        masked = jnp.where(allowed, raw_scores, masked_value)
        new_peak = jnp.maximum(peak_val, jnp.max(masked, axis=-1))
        decay_vals = jnp.exp(peak_val - new_peak)
        weights = jnp.where(allowed, jnp.exp(masked - new_peak[..., None]), 0.0)
        totals = totals * decay_vals + jnp.sum(weights, axis=-1)
        accum_vals = accum_vals * decay_vals[..., None] + jnp.einsum(
            "hgqk,hkd->hgqd",
            weights.astype(jnp.bfloat16),
            value_one,
            preferred_element_type=jnp.float32,
        )
        return (new_peak, totals, accum_vals)

    peak_val, totals, accum_vals = lax.map(
        per_sequence,
        (initial[0], initial[1], initial[2], query_seq, query_pos, key_seq, value_seq, pos_seq),
    )
    log_total = peak_val + jnp.log(totals)
    mixed_seq = accum_vals / totals[..., None]
    mixed_low = (
        jnp.transpose(mixed_seq, (3, 0, 1, 2, 4))
        .reshape(row_count, heads_q * HEAD)
        .astype(jnp.bfloat16)
    )
    branch = lax.psum(
        jnp.dot(mixed_low, out_mat, preferred_element_type=jnp.float32).astype(jnp.bfloat16),
        "tensor",
    ).astype(jnp.float32)
    middle = flat_in + branch
    unit_two, inverse_two, second = norm_forward(middle, full_two)
    gate_vals = jnp.dot(second, gate_mat, preferred_element_type=jnp.float32)
    up_vals = jnp.dot(second, up_mat, preferred_element_type=jnp.float32)
    sigmoid_vals = jax.nn.sigmoid(gate_vals)
    silu_vals = gate_vals * sigmoid_vals
    hidden = (silu_vals * up_vals).astype(jnp.bfloat16)
    mlp_part = lax.psum(
        jnp.dot(hidden, down_mat, preferred_element_type=jnp.float32).astype(jnp.bfloat16), "tensor"
    ).astype(jnp.float32)
    layer_out = (middle + mlp_part).astype(jnp.bfloat16).reshape(slot_count, seq_count, model_width)
    regathered = (
        lax.all_gather(gain_one, ("dp", "context"), axis=0, tiled=True),
        lax.all_gather(gain_two, ("dp", "context"), axis=0, tiled=True),
        lax.all_gather(w_query, ("dp", "context"), axis=0, tiled=True),
        lax.all_gather(w_key, ("dp", "context"), axis=0, tiled=True),
        lax.all_gather(w_value, ("dp", "context"), axis=0, tiled=True),
        lax.all_gather(w_out, ("dp", "context"), axis=1, tiled=True),
        lax.all_gather(w_gate, ("dp", "context"), axis=0, tiled=True),
        lax.all_gather(w_up, ("dp", "context"), axis=0, tiled=True),
        lax.all_gather(w_down, ("dp", "context"), axis=1, tiled=True),
    )
    full_one, full_two, query_mat, key_mat, value_mat, out_mat, gate_mat, up_mat, down_mat = (
        regathered
    )
    grad_low = cotangent.reshape(row_count, model_width)
    grad_down = contract_rows(hidden, grad_low)
    grad_hidden = contract_cols(grad_low, down_mat)
    grad_gate_low = (
        grad_hidden * up_vals * sigmoid_vals * (1.0 + gate_vals * (1.0 - sigmoid_vals))
    ).astype(jnp.bfloat16)
    grad_up_low = (grad_hidden * silu_vals).astype(jnp.bfloat16)
    grad_gate = contract_rows(second, grad_gate_low)
    grad_up = contract_rows(second, grad_up_low)
    grad_second = lax.psum(
        (contract_cols(grad_gate_low, gate_mat) + contract_cols(grad_up_low, up_mat)).astype(
            jnp.bfloat16
        ),
        "tensor",
    ).astype(jnp.float32)
    grad_mid_norm, grad_gain_two = norm_backward(grad_second, unit_two, inverse_two, full_two)
    grad_middle = grad_low.astype(jnp.float32) + grad_mid_norm
    grad_mid_low = grad_middle.astype(jnp.bfloat16)
    grad_out = contract_rows(mixed_low, grad_mid_low)
    grad_mixed = contract_cols(grad_mid_low, out_mat).astype(jnp.bfloat16)
    grad_mixed_seq = jnp.transpose(
        grad_mixed.reshape(slot_count, seq_count, heads_kv, group_size, HEAD), (1, 2, 3, 0, 4)
    )
    delta_rows = jnp.sum(grad_mixed_seq.astype(jnp.float32) * mixed_seq, axis=-1)
    kv_width = heads_kv * HEAD

    def block_grads(grad_query_acc, key_blk, value_blk, pos_blk):
        block_len = key_blk.shape[0]
        key_seq = jnp.transpose(key_blk.reshape(block_len, seq_count, heads_kv, HEAD), (1, 2, 0, 3))
        value_seq = jnp.transpose(
            value_blk.reshape(block_len, seq_count, heads_kv, HEAD), (1, 2, 0, 3)
        )
        raw_scores = (
            jnp.einsum("shgqd,shkd->shgqk", query_seq, key_seq, preferred_element_type=jnp.float32)
            * score_scale
        )
        allowed = pos_blk.T[:, None, None, None, :] <= query_pos[:, None, None, :, None]
        prob_vals = jnp.where(
            allowed,
            jnp.exp(jnp.where(allowed, raw_scores - log_total[..., None], masked_value)),
            0.0,
        )
        grad_value_blk = jnp.einsum(
            "shgqk,shgqd->kshd",
            prob_vals.astype(jnp.bfloat16),
            grad_mixed_seq,
            preferred_element_type=jnp.float32,
        )
        grad_probs = jnp.einsum(
            "shgqd,shkd->shgqk", grad_mixed_seq, value_seq, preferred_element_type=jnp.float32
        )
        grad_scores = (prob_vals * (grad_probs - delta_rows[..., None])).astype(jnp.bfloat16)
        grad_query_acc = grad_query_acc + jnp.einsum(
            "shgqk,shkd->shgqd", grad_scores, key_seq, preferred_element_type=jnp.float32
        )
        grad_key_blk = jnp.einsum(
            "shgqk,shgqd->kshd", grad_scores, query_seq, preferred_element_type=jnp.float32
        )
        return (
            grad_query_acc,
            grad_key_blk.reshape(block_len, seq_count, kv_width),
            grad_value_blk.reshape(block_len, seq_count, kv_width),
        )

    zero_query = jnp.zeros(stat_shape + (HEAD,), jnp.float32)
    key_all, value_all, pos_all = (
        lax.all_gather(keys_low, "context", axis=0, tiled=True),
        lax.all_gather(value_low, "context", axis=0, tiled=True),
        lax.all_gather(positions, "context", axis=0, tiled=True),
    )
    total_len = key_all.shape[0]
    block_size = min(512, total_len)
    block_count = total_len // block_size

    def key_block(grad_query_acc, block_items):
        key_blk, value_blk, pos_blk = block_items
        grad_query_acc, grad_key_blk, grad_value_blk = block_grads(
            grad_query_acc, key_blk, value_blk, pos_blk
        )
        return (grad_query_acc, (grad_key_blk, grad_value_blk))

    grad_query_acc, (grad_keys_all, grad_values_all) = lax.scan(
        key_block,
        zero_query,
        (
            key_all.reshape(block_count, block_size, seq_count, kv_width),
            value_all.reshape(block_count, block_size, seq_count, kv_width),
            pos_all.reshape(block_count, block_size, seq_count),
        ),
    )
    grad_key_own, grad_value_own = (
        lax.psum_scatter(
            grad_keys_all.reshape(total_len, seq_count, kv_width).astype(jnp.bfloat16),
            "context",
            scatter_dimension=0,
            tiled=True,
        ).astype(jnp.float32),
        lax.psum_scatter(
            grad_values_all.reshape(total_len, seq_count, kv_width).astype(jnp.bfloat16),
            "context",
            scatter_dimension=0,
            tiled=True,
        ).astype(jnp.float32),
    )
    grad_rot_q = jnp.transpose(grad_query_acc * score_scale, (3, 0, 1, 2, 4)).reshape(
        slot_count, seq_count, heads_q, HEAD
    )
    grad_q_low = (
        rotate(grad_rot_q, cos_part, -sin_part)
        .reshape(row_count, heads_q * HEAD)
        .astype(jnp.bfloat16)
    )
    grad_rot_k = (grad_key_own * score_scale).reshape(slot_count, seq_count, heads_kv, HEAD)
    grad_k_low = (
        rotate(grad_rot_k, cos_part, -sin_part).reshape(row_count, kv_width).astype(jnp.bfloat16)
    )
    grad_v_low = grad_value_own.reshape(row_count, kv_width).astype(jnp.bfloat16)
    grad_query = contract_rows(normed, grad_q_low)
    grad_key = contract_rows(normed, grad_k_low)
    grad_value = contract_rows(normed, grad_v_low)
    grad_normed = lax.psum(
        (
            contract_cols(grad_q_low, query_mat)
            + contract_cols(grad_k_low, key_mat)
            + contract_cols(grad_v_low, value_mat)
        ).astype(jnp.bfloat16),
        "tensor",
    ).astype(jnp.float32)
    grad_in_norm, grad_gain_one = norm_backward(grad_normed, unit_one, inverse_one, full_one)
    input_grad = (grad_middle + grad_in_norm).reshape(slot_count, seq_count, model_width)
    reduced = (
        lax.psum_scatter(grad_gain_one, ("dp", "context"), scatter_dimension=0, tiled=True),
        lax.psum_scatter(grad_gain_two, ("dp", "context"), scatter_dimension=0, tiled=True),
        lax.psum_scatter(grad_query, ("dp", "context"), scatter_dimension=0, tiled=True),
        lax.psum_scatter(grad_key, ("dp", "context"), scatter_dimension=0, tiled=True),
        lax.psum_scatter(grad_value, ("dp", "context"), scatter_dimension=0, tiled=True),
        lax.psum_scatter(grad_out, ("dp", "context"), scatter_dimension=1, tiled=True),
        lax.psum_scatter(grad_gate, ("dp", "context"), scatter_dimension=0, tiled=True),
        lax.psum_scatter(grad_up, ("dp", "context"), scatter_dimension=0, tiled=True),
        lax.psum_scatter(grad_down, ("dp", "context"), scatter_dimension=1, tiled=True),
    )
    return (
        layer_out,
        input_grad,
        reduced[0],
        reduced[1],
        reduced[2],
        reduced[3],
        reduced[4],
        reduced[5],
        reduced[6],
        reduced[7],
        reduced[8],
    )


WIDE = 128
RUN = 256
TILE = 512
LOG2_E = 1.4426950408889634
MESH = pl.DeviceIdType.MESH
VMEM_LIMIT = 56 * 1024 * 1024


def any_spec():
    return pl.BlockSpec(memory_space=pl.ANY)


def vmem_spec():
    return pl.BlockSpec(memory_space=pltpu.VMEM)


def place():
    return lax.axis_index("dp"), lax.axis_index("context"), lax.axis_index("tensor")


def greet(devices):
    barrier = pltpu.get_barrier_semaphore()
    for device in devices:
        pl.semaphore_signal(barrier, inc=1, device_id=device, device_id_type=MESH)
    pl.semaphore_wait(barrier, len(devices))


def greet_sequence():
    row, spot, core = place()
    greet(
        [
            (row, lax.rem(spot + shift, 8), lax.rem(core + flip, 2))
            for shift in range(8)
            for flip in range(2)
            if shift or flip
        ]
    )


def remote(source, target, send, recv, device):
    return pltpu.make_async_remote_copy(
        src_ref=source,
        dst_ref=target,
        send_sem=send,
        recv_sem=recv,
        device_id=device,
        device_id_type=MESH,
    )


def move(source, target, send, recv, device, is_self):
    @pl.when(is_self)
    def _():
        pltpu.make_async_copy(source, target, recv).start()

    @pl.when(jnp.logical_not(is_self))
    def _():
        remote(source, target, send, recv, device).start()


def spread_matrix(heads):
    shape = (heads * HEAD, heads * WIDE)
    rows = lax.broadcasted_iota(jnp.int32, shape, 0)
    cols = lax.broadcasted_iota(jnp.int32, shape, 1)
    dims = rows % HEAD
    target = (rows // HEAD) * WIDE + dims + jnp.where(dims >= HEAD // 2, (WIDE - HEAD) // 2, 0)
    return (cols == target).astype(jnp.bfloat16)


def lane_tables(positions):
    half = HEAD // 2
    inv_freqs = theta_base ** (-2.0 * jnp.arange(half, dtype=jnp.float32) / HEAD)
    gap = jnp.zeros((WIDE // 2 - half,), jnp.float32)
    freqs = jnp.concatenate([inv_freqs, gap, inv_freqs, gap])
    sign = jnp.where(jnp.arange(WIDE) < WIDE // 2, -1.0, 1.0)
    angles = positions.astype(jnp.float32)[:, None] * freqs
    return jnp.cos(angles), jnp.sin(angles) * sign


def project_kernel(normed, weight, spread, cos_tab, sin_tab, q_out, kv_out):
    step = pl.program_id(0)
    wide = jnp.dot(weight[...], spread[...], preferred_element_type=jnp.float32)
    proj = jnp.dot(normed[...], wide.astype(jnp.bfloat16), preferred_element_type=jnp.float32)
    for head in range(4):
        part = proj[:, head * WIDE : (head + 1) * WIDE]
        turned = part * cos_tab[0] + pltpu.roll(part, WIDE // 2, 1) * sin_tab[0]
        low = turned.astype(jnp.bfloat16)

        @pl.when(step < 2)
        def _():
            q_out[head] = low

        @pl.when(step >= 2)
        def _():
            kv_out[head, 0] = low


def project(normed, weights, spread, cos_tab, sin_tab):
    rows, width = normed.shape
    return pl.pallas_call(
        project_kernel,
        grid=(4,),
        in_specs=[
            pl.BlockSpec((rows, width), lambda s: (0, 0)),
            pl.BlockSpec((width, 4 * HEAD), lambda s: (0, s)),
            pl.BlockSpec((4 * HEAD, 4 * WIDE), lambda s: (0, 0)),
            pl.BlockSpec((1, rows, WIDE), lambda s: (s // 3, 0, 0)),
            pl.BlockSpec((1, rows, WIDE), lambda s: (s // 3, 0, 0)),
        ],
        out_specs=[
            pl.BlockSpec((4, rows, WIDE), lambda s: (jnp.minimum(s, 1), 0, 0)),
            pl.BlockSpec((4, 1, rows, WIDE), lambda s: (0, jnp.maximum(s - 2, 0), 0, 0)),
        ],
        out_shape=[
            jax.ShapeDtypeStruct((8, rows, WIDE), jnp.bfloat16),
            jax.ShapeDtypeStruct((4, 2, rows, WIDE), jnp.bfloat16),
        ],
        compiler_params=pltpu.CompilerParams(vmem_limit_bytes=VMEM_LIMIT),
        name="project",
    )(normed, weights, spread, cos_tab, sin_tab)


def to_heads_kernel(q_ref, kv_ref, q_all, kv_all, send_q, recv_q, send_kv, recv_kv, send_x, recv_x):
    row, spot, core = place()
    greet_sequence()
    for step in range(4):
        slot = lax.rem(spot + step, 4)
        chip = 4 * core + slot
        for other in range(2):
            is_self = jnp.logical_and(chip == spot, core == other)
            device = (row, chip, other)
            rows = pl.ds(other * RUN, RUN)
            move(
                kv_ref.at[slot, :, rows],
                kv_all.at[spot, :, rows],
                send_kv.at[step, other],
                recv_kv.at[spot],
                device,
                is_self,
            )
            move(
                q_ref.at[2 * slot + other],
                q_all.at[spot],
                send_q.at[step, other],
                recv_q.at[spot],
                device,
                is_self,
            )
    own_rows = pl.ds(pl.multiple_of(core * RUN, RUN), RUN)
    sibling = (row, spot, 1 - core)

    def hand_on(source):
        block = kv_all.at[source, :, own_rows]
        return remote(block, block, send_x.at[source], recv_x.at[source], sibling)

    for step in range(8):
        source = lax.rem(spot + step, 8)
        block = kv_all.at[source, :, own_rows]
        remote(block, block, send_x.at[source], recv_kv.at[source], sibling).wait_recv()
        hand_on(source).start()
    for step in range(8):
        remote(
            q_all.at[step], q_all.at[step], send_x.at[step], recv_q.at[step], sibling
        ).wait_recv()
        hand_on(step).wait()
    for step in range(4):
        slot = lax.rem(spot + step, 4)
        chip = 4 * core + slot
        for other in range(2):

            @pl.when(jnp.logical_not(jnp.logical_and(chip == spot, core == other)))
            def _():
                rows = pl.ds(other * RUN, RUN)
                device = (row, chip, other)
                remote(
                    kv_ref.at[slot, :, rows],
                    kv_all.at[spot, :, rows],
                    send_kv.at[step, other],
                    recv_kv.at[spot],
                    device,
                ).wait_send()
                remote(
                    q_ref.at[2 * slot + other],
                    q_all.at[spot],
                    send_q.at[step, other],
                    recv_q.at[spot],
                    device,
                ).wait_send()


def to_heads(q_heads, kv_heads):
    dma = pltpu.SemaphoreType.DMA
    rows = q_heads.shape[1]
    return pl.pallas_call(
        to_heads_kernel,
        in_specs=[any_spec(), any_spec()],
        out_specs=[any_spec(), any_spec()],
        out_shape=[
            jax.ShapeDtypeStruct((8, rows, WIDE), jnp.bfloat16),
            jax.ShapeDtypeStruct((8, 2, rows, WIDE), jnp.bfloat16),
        ],
        scratch_shapes=[dma((4, 2)), dma((8,)), dma((4, 2)), dma((8,)), dma((8,)), dma((8,))],
        compiler_params=pltpu.CompilerParams(collective_id=1, has_side_effects=True),
        name="to_heads",
    )(q_heads, kv_heads)


def grads_to_heads_kernel(d_ref, d_all, send, recv):
    row, spot, core = place()
    greet_sequence()
    copies = []
    for step in range(4):
        slot = lax.rem(spot + step, 4)
        chip = 4 * core + slot
        for other in range(2):
            is_self = jnp.logical_and(chip == spot, core == other)
            copies.append(
                (
                    (
                        d_ref.at[2 * slot + other],
                        d_all.at[spot],
                        send.at[step, other],
                        recv.at[spot],
                        (row, chip, other),
                    ),
                    is_self,
                )
            )
    for parts, is_self in copies:
        move(*parts, is_self)
    for step in range(8):
        remote(
            d_all.at[step], d_all.at[step], send.at[0, 0], recv.at[step], (row, spot, 1 - core)
        ).wait_recv()
    for parts, is_self in copies:

        @pl.when(jnp.logical_not(is_self))
        def _():
            remote(*parts).wait_send()


def grads_to_heads(grad_heads):
    dma = pltpu.SemaphoreType.DMA
    return pl.pallas_call(
        grads_to_heads_kernel,
        in_specs=[any_spec()],
        out_specs=any_spec(),
        out_shape=jax.ShapeDtypeStruct(grad_heads.shape, jnp.bfloat16),
        scratch_shapes=[dma((4, 2)), dma((8,))],
        compiler_params=pltpu.CompilerParams(collective_id=2, has_side_effects=True),
        name="grads_to_heads",
    )(grad_heads)


def return_copies(ref, out, send, recv):
    row, spot, core = place()
    head = 2 * lax.rem(spot, 4) + core
    owner = spot // 4
    copies = []
    for step in range(8):
        chip = lax.rem(spot + step, 8)
        is_self = (owner == core) if step == 0 else False
        parts = (ref.at[chip], out.at[head], send.at[step], recv.at[head], (row, chip, owner))
        copies.append((parts, is_self))
    return copies


def start_return(copies):
    for parts, is_self in copies:
        if is_self is False:
            remote(*parts).start()
        else:
            move(*parts, is_self)


def finish_return(copies, out, send, recv):
    row, spot, core = place()
    for head in range(8):
        remote(
            out.at[head], out.at[head], send.at[0], recv.at[head], (row, spot, 1 - core)
        ).wait_recv()
    for parts, is_self in copies:
        if is_self is False:
            remote(*parts).wait_send()
        else:

            @pl.when(jnp.logical_not(is_self))
            def _():
                remote(*parts).wait_send()


def to_tokens_kernel(ref, out, send, recv):
    greet_sequence()
    copies = return_copies(ref, out, send, recv)
    start_return(copies)
    finish_return(copies, out, send, recv)


def to_tokens(mixed):
    dma = pltpu.SemaphoreType.DMA
    return pl.pallas_call(
        to_tokens_kernel,
        in_specs=[any_spec()],
        out_specs=any_spec(),
        out_shape=jax.ShapeDtypeStruct(mixed.shape, jnp.bfloat16),
        scratch_shapes=[dma((8,)), dma((8,))],
        compiler_params=pltpu.CompilerParams(collective_id=3, has_side_effects=True),
        name="to_tokens",
    )(mixed)


def grads_to_tokens_kernel(
    dq_ref, dkv_ref, dq_out, dkv_out, own, other, send, recv, send_x, recv_x, local, send_k, recv_k
):
    row, spot, core = place()
    greet_sequence()
    own_rows = pl.ds(pl.multiple_of(core * RUN, RUN), RUN)
    other_rows = pl.ds(pl.multiple_of((1 - core) * RUN, RUN), RUN)
    swap = remote(
        dkv_ref.at[:, :, other_rows], other, send_x, recv_x, (row, spot, 1 - core)
    )
    swap.start()
    load = pltpu.make_async_copy(dkv_ref.at[:, :, own_rows], own, local)
    load.start()
    copies = return_copies(dq_ref, dq_out, send, recv)
    start_return(copies)
    load.wait()
    swap.wait()
    slot = lax.rem(spot, 4)
    owner = spot // 4
    backs = []
    for step in range(8):
        chip = lax.rem(spot + step, 8)
        total = own[:, chip].astype(jnp.float32) + other[:, chip].astype(jnp.float32)
        own[:, chip] = total.astype(jnp.bfloat16)
        parts = (
            own.at[:, chip],
            dkv_out.at[slot, :, own_rows],
            send_k.at[step],
            recv_k.at[slot, core],
            (row, chip, owner),
        )
        is_self = (owner == core) if step == 0 else False
        backs.append((parts, is_self))
        start_return(backs[-1:])
    for slot_in in range(4):
        for core_in in range(2):
            target = dkv_out.at[slot_in, :, pl.ds(core_in * RUN, RUN)]
            remote(
                target, target, send_k.at[0], recv_k.at[slot_in, core_in], (row, spot, 1 - core)
            ).wait_recv()
    for parts, is_self in backs:
        if is_self is False:
            remote(*parts).wait_send()
        else:

            @pl.when(jnp.logical_not(is_self))
            def _():
                remote(*parts).wait_send()

    finish_return(copies, dq_out, send, recv)


def grads_to_tokens(dq, dkv):
    dma = pltpu.SemaphoreType.DMA
    rows = dq.shape[1]
    return pl.pallas_call(
        grads_to_tokens_kernel,
        in_specs=[any_spec(), any_spec()],
        out_specs=[any_spec(), any_spec()],
        out_shape=[
            jax.ShapeDtypeStruct((8, rows, WIDE), jnp.bfloat16),
            jax.ShapeDtypeStruct((4, 2, rows, WIDE), jnp.bfloat16),
        ],
        scratch_shapes=[
            pltpu.VMEM((2, 8, RUN, WIDE), jnp.bfloat16),
            pltpu.VMEM((2, 8, RUN, WIDE), jnp.bfloat16),
            dma((8,)),
            dma((8,)),
            dma(()),
            dma(()),
            dma(()),
            dma((8,)),
            dma((4, 2)),
        ],
        compiler_params=pltpu.CompilerParams(
            collective_id=4, has_side_effects=True, vmem_limit_bytes=VMEM_LIMIT
        ),
        name="grads_to_tokens",
    )(dq, dkv)


def pair_sum_kernel(part, total, other, send, recv):
    row, spot, core = place()
    sibling = (row, spot, 1 - core)
    greet([sibling])
    pieces = send.shape[0]
    rows = part.shape[0] // pieces

    def piece(index):
        cut = pl.ds(index * rows, rows)
        return remote(part.at[cut], other.at[cut], send.at[index], recv.at[index], sibling)

    for index in range(pieces):
        piece(index).start()
    for index in range(pieces):
        cut = pl.ds(index * rows, rows)
        piece(index).wait()
        total[cut] = part[cut].astype(jnp.float32) + other[cut].astype(jnp.float32)


def pair_sum(part, collective_id):
    dma = pltpu.SemaphoreType.DMA
    return pl.pallas_call(
        pair_sum_kernel,
        in_specs=[vmem_spec()],
        out_specs=vmem_spec(),
        out_shape=jax.ShapeDtypeStruct(part.shape, jnp.float32),
        scratch_shapes=[pltpu.VMEM(part.shape, part.dtype), dma((4,)), dma((4,))],
        compiler_params=pltpu.CompilerParams(
            collective_id=collective_id, has_side_effects=True, vmem_limit_bytes=VMEM_LIMIT
        ),
        name="pair_sum",
    )(part)


def tile_at(index, size):
    return pl.ds(pl.multiple_of(index * size, size), size)


def causal(scores):
    keys = lax.broadcasted_iota(jnp.int32, scores.shape, 0)
    queries = lax.broadcasted_iota(jnp.int32, scores.shape, 1)
    return jnp.where(keys <= queries, scores, masked_value)


def attend_kernel(order, q_in, kv_in, mixed, mixed_t, lse, q_t, keys, v_t):
    runs = q_in.shape[0] // RUN

    def sort_run(index, carry):
        run = order[index]
        cols = tile_at(index, RUN)
        q_t[:, cols] = q_in[tile_at(run, RUN)].T
        keys[cols] = kv_in[run // 2, 0, tile_at(run % 2, RUN)]
        v_t[:, cols] = kv_in[run // 2, 1, tile_at(run % 2, RUN)].T
        return carry

    lax.fori_loop(0, runs, sort_run, 0)
    scale = HEAD ** (-0.5) * LOG2_E

    def query_tile(index, carry):
        cols = tile_at(index, TILE)
        queries = q_t[:, cols]

        def step(scores, block, peak, total, mix):
            high = jnp.maximum(peak, jnp.max(scores, axis=0, keepdims=True))
            decay = jnp.exp2(peak - high)
            weights = jnp.exp2(scores - high)
            total = total * decay + jnp.sum(weights, axis=0, keepdims=True)
            mix = mix * decay + jnp.dot(
                v_t[:, tile_at(block, TILE)],
                weights.astype(jnp.bfloat16),
                preferred_element_type=jnp.float32,
            )
            return high, total, mix

        def scores_of(block):
            return (
                jnp.dot(keys[tile_at(block, TILE)], queries, preferred_element_type=jnp.float32)
                * scale
            )

        state = (
            jnp.full((1, TILE), masked_value, jnp.float32),
            jnp.zeros((1, TILE), jnp.float32),
            jnp.zeros((WIDE, TILE), jnp.float32),
        )
        state = step(causal(scores_of(index)), index, *state)
        peak, total, mix = lax.fori_loop(
            0, index, lambda block, now: step(scores_of(block), block, *now), state
        )
        mix = mix / total
        mixed_t[:, cols] = mix
        lse[:, cols] = peak + jnp.log2(total)
        for half in range(TILE // RUN):
            run = order[index * (TILE // RUN) + half]
            mixed[tile_at(run, RUN)] = mix[:, half * RUN : (half + 1) * RUN].T.astype(jnp.bfloat16)
        return carry

    lax.fori_loop(0, q_in.shape[0] // TILE, query_tile, 0)


def attend(order, q_all, kv_all):
    length = q_all.shape[0]
    low = jnp.bfloat16
    return pl.pallas_call(
        attend_kernel,
        in_specs=[pl.BlockSpec(memory_space=pltpu.SMEM), vmem_spec(), vmem_spec()],
        out_specs=[vmem_spec()] * 3,
        out_shape=[
            jax.ShapeDtypeStruct((length, WIDE), low),
            jax.ShapeDtypeStruct((WIDE, length), jnp.float32),
            jax.ShapeDtypeStruct((1, length), jnp.float32),
        ],
        scratch_shapes=[
            pltpu.VMEM((WIDE, length), low),
            pltpu.VMEM((length, WIDE), low),
            pltpu.VMEM((WIDE, length), low),
        ],
        compiler_params=pltpu.CompilerParams(vmem_limit_bytes=VMEM_LIMIT),
        cost_estimate=pl.CostEstimate(
            flops=2 * length * length * WIDE, bytes_accessed=8 * length * WIDE, transcendentals=0
        ),
        name="attend",
    )(order, q_all, kv_all)


def attend_back_kernel(
    order, q_in, kv_in, d_in, mixed_t, lse, dq, dkv, q, q_t, k, k_t, v, d, d_t, delta, dq_t, dk, dv
):
    runs = q_in.shape[0] // RUN
    tiles = q_in.shape[0] // TILE

    def sort_run(index, carry):
        run = order[index]
        cols = tile_at(index, RUN)
        q_run = q_in[tile_at(run, RUN)]
        k_run = kv_in[run // 2, 0, tile_at(run % 2, RUN)]
        d_run = d_in[tile_at(run, RUN)]
        d_turned = d_run.T
        q[cols] = q_run
        q_t[:, cols] = q_run.T
        k[cols] = k_run
        k_t[:, cols] = k_run.T
        v[cols] = kv_in[run // 2, 1, tile_at(run % 2, RUN)]
        d[cols] = d_run
        d_t[:, cols] = d_turned
        delta[:, cols] = jnp.sum(
            d_turned.astype(jnp.float32) * mixed_t[:, cols], axis=0, keepdims=True
        )
        return carry

    lax.fori_loop(0, runs, sort_run, 0)
    scale = HEAD ** (-0.5)
    dq_t[...] = jnp.zeros_like(dq_t)

    def key_tile(block, carry):
        rows = tile_at(block, TILE)
        keys, keys_t, values = k[rows], k_t[:, rows], v[rows]
        dk[...] = jnp.zeros_like(dk)
        dv[...] = jnp.zeros_like(dv)

        def query_tile(index, diagonal):
            cols = tile_at(index, TILE)
            scores = jnp.dot(keys, q_t[:, cols], preferred_element_type=jnp.float32) * (
                scale * LOG2_E
            )
            if diagonal:
                scores = causal(scores)
            probs = jnp.exp2(scores - lse[:, cols])
            dv[...] += jnp.dot(
                probs.astype(jnp.bfloat16), d[cols], preferred_element_type=jnp.float32
            )
            grad_probs = jnp.dot(values, d_t[:, cols], preferred_element_type=jnp.float32)
            grad_scores = (probs * (grad_probs - delta[:, cols])).astype(jnp.bfloat16)
            dk[...] += jnp.dot(grad_scores, q[cols], preferred_element_type=jnp.float32)
            dq_t[:, cols] += jnp.dot(keys_t, grad_scores, preferred_element_type=jnp.float32)

        query_tile(block, True)

        def later(index, inner):
            query_tile(index, False)
            return inner

        lax.fori_loop(block + 1, tiles, later, 0)
        for half in range(TILE // RUN):
            run = order[block * (TILE // RUN) + half]
            cut = pl.ds(half * RUN, RUN)
            dkv[0, tile_at(run, RUN)] = (dk[cut] * scale).astype(jnp.bfloat16)
            dkv[1, tile_at(run, RUN)] = dv[cut].astype(jnp.bfloat16)
        return carry

    lax.fori_loop(0, tiles, key_tile, 0)

    def unsort_run(index, carry):
        run = order[index]
        dq[tile_at(run, RUN)] = (dq_t[:, tile_at(index, RUN)] * scale).T.astype(jnp.bfloat16)
        return carry

    lax.fori_loop(0, runs, unsort_run, 0)


def attend_back(order, q_all, kv_all, d_all, mixed_t, lse):
    length = q_all.shape[0]
    low = jnp.bfloat16
    tall = pltpu.VMEM((length, WIDE), low)
    flat = pltpu.VMEM((WIDE, length), low)
    return pl.pallas_call(
        attend_back_kernel,
        in_specs=[pl.BlockSpec(memory_space=pltpu.SMEM)] + [vmem_spec()] * 5,
        out_specs=[vmem_spec()] * 2,
        out_shape=[
            jax.ShapeDtypeStruct((length, WIDE), low),
            jax.ShapeDtypeStruct((2, length, WIDE), low),
        ],
        scratch_shapes=[
            tall,
            flat,
            tall,
            flat,
            tall,
            tall,
            flat,
            pltpu.VMEM((1, length), jnp.float32),
            pltpu.VMEM((WIDE, length), jnp.float32),
            pltpu.VMEM((TILE, WIDE), jnp.float32),
            pltpu.VMEM((TILE, WIDE), jnp.float32),
        ],
        compiler_params=pltpu.CompilerParams(vmem_limit_bytes=VMEM_LIMIT),
        cost_estimate=pl.CostEstimate(
            flops=5 * length * length * WIDE, bytes_accessed=20 * length * WIDE, transcendentals=0
        ),
        name="attend_back",
    )(order, q_all, kv_all, d_all, mixed_t, lse)


def neighbours():
    row, spot, core = place()
    level, column = spot // 2, lax.rem(spot, 2)
    beside_x = (1 - row, spot, core)
    beside_y = (row, 2 * level + 1 - column, core)
    along_z = [(row, 2 * lax.rem(level + k, 4) + column, core) for k in (1, 2, 3)]
    return row, level, column, beside_x, beside_y, along_z


def gather_kernel(own, whole, cut, local, send_z, recv_z, send_x, recv_x, send_y, recv_y, send_d, recv_d):
    row, level, column, beside_x, beside_y, along_z = neighbours()
    greet([beside_x, beside_y] + along_z)
    width = own.shape[1]
    halves = (pl.ds(0, cut), pl.ds(cut, width - cut))

    def block(x, z, y):
        return whole.at[x, z, y]

    keep = pltpu.make_async_copy(own, block(row, level, column), local)
    keep.start()
    started = []

    def send(source, target, send_sem, recv_sem, device):
        copy = remote(source, target, send_sem, recv_sem, device)
        copy.start()
        started.append(copy)

    def arrived(target, recv_sem):
        remote(target, target, send_z.at[0], recv_sem, beside_x).wait_recv()

    mine = block(row, level, column)
    send(own, mine, send_x.at[0], recv_x.at[0], beside_x)
    send(own, mine, send_y.at[0], recv_y.at[0], beside_y)
    for k in range(3):
        send(own, mine, send_z.at[k], recv_z.at[k], along_z[k])

    def diagonal(k):
        z = lax.rem(level + 4 - k, 4)
        from_x, from_y = block(1 - row, z, column), block(row, z, 1 - column)
        arrived(from_x, recv_x.at[k])
        part = from_x.at[:, halves[1]]
        send(part, part, send_d.at[0, k], recv_d.at[0, k], beside_y)
        arrived(from_y, recv_y.at[k])
        part = from_y.at[:, halves[0]]
        send(part, part, send_d.at[1, k], recv_d.at[1, k], beside_x)

    for k in range(1, 4):
        z = lax.rem(level + 4 - k, 4)
        column_block = block(row, z, column)
        arrived(column_block, recv_z.at[k - 1])
        send(column_block, column_block, send_x.at[k], recv_x.at[k], beside_x)
        send(column_block, column_block, send_y.at[k], recv_y.at[k], beside_y)
        diagonal(k - 1)
    diagonal(3)
    for k in range(4):
        z = lax.rem(level + 4 - k, 4)
        far_block = block(1 - row, z, 1 - column)
        arrived(far_block.at[:, halves[1]], recv_d.at[0, k])
        arrived(far_block.at[:, halves[0]], recv_d.at[1, k])
    for copy in started:
        copy.wait_send()
    keep.wait()


def gather_rows(own, collective_id):
    dma = pltpu.SemaphoreType.DMA
    rows, width = own.shape
    cut = width // 2 // WIDE * WIDE
    whole = pl.pallas_call(
        lambda own, whole, *sems: gather_kernel(own, whole, cut, *sems),
        in_specs=[any_spec()],
        out_specs=any_spec(),
        out_shape=jax.ShapeDtypeStruct((2, 4, 2, rows, width), own.dtype),
        scratch_shapes=[
            dma(()),
            dma((3,)),
            dma((3,)),
            dma((4,)),
            dma((4,)),
            dma((4,)),
            dma((4,)),
            dma((2, 4)),
            dma((2, 4)),
        ],
        compiler_params=pltpu.CompilerParams(collective_id=collective_id, has_side_effects=True),
        name="gather_rows",
    )(own)
    return whole.reshape(16 * rows, width)


PIECE = 256


def reduce_kernel(
    n,
    tail,
    lefts,
    groups,
    right,
    gains,
    own,
    left_t,
    staged,
    send_one,
    recv_one,
    send_two,
    recv_two,
    kept,
    recv_three,
    load,
    ss_one,
    rs_one,
    ss_two,
    rs_two,
    ss_three,
    rs_three,
):
    row, level, column, beside_x, beside_y, along_z = neighbours()
    share = own.shape[0]
    quarter = 4 * share

    def load_left(index):
        copy = pltpu.make_async_copy(lefts[index], staged, load)
        copy.start()
        copy.wait()
        for part in range(4):
            turned = staged[:, part * quarter : (part + 1) * quarter].T
            for inner in range(4):
                x, z, y = part // 2, 2 * (part % 2) + inner // 2, inner % 2
                left_t[index, x, y, z * share : (z + 1) * share] = turned[
                    inner * share : (inner + 1) * share
                ]

    load_left(0)
    greet([beside_x, beside_y] + along_z)

    def group_of(step):
        found = 0
        for start in groups[1:]:
            found = found + jnp.where(step >= start, 1, 0)
        return found

    def columns(step, kind):
        return pl.ds(pl.multiple_of(step * 2 * PIECE + kind * PIECE, PIECE), PIECE)

    def product(step, kind, x, y):
        term = jnp.dot(
            left_t[group_of(step), x, y],
            right[:, columns(step, kind)],
            preferred_element_type=jnp.float32,
        )
        if kind == 1:
            at_gains = jnp.where(step == n - 1, 1.0, 0.0)
            term = term * (1.0 - at_gains) + gains[x, y].astype(jnp.float32) * at_gains
        return term

    def first_copy(step, kind):
        slot = lax.rem(step, 2)
        return remote(
            send_one.at[slot, kind],
            recv_one.at[step, kind],
            ss_one.at[slot, kind],
            rs_one.at[step, kind],
            beside_x if kind == 0 else beside_y,
        )

    def second_copy(step, kind):
        slot = lax.rem(step, 2)
        return remote(
            send_two.at[slot, kind],
            recv_two.at[step, kind],
            ss_two.at[slot, kind],
            rs_two.at[step, kind],
            beside_y if kind == 0 else beside_x,
        )

    def third_copy(step, kind, k):
        target = lax.rem(level + k + 1, 4)
        slot = lax.rem(step, 3)
        return remote(
            kept.at[slot, kind, pl.ds(pl.multiple_of(target * share, share), share)],
            recv_three.at[step, kind, k],
            ss_three.at[slot, kind, k],
            rs_three.at[step, kind, k],
            along_z[k],
        )

    def first(step):
        slot = lax.rem(step, 2)
        for half in range(2):
            send_one[slot, 0, half] = product(step, 0, 1 - row, half).astype(jnp.bfloat16)
        first_copy(step, 0).start()
        for half in range(2):
            send_one[slot, 1, half] = product(step, 1, half, 1 - column).astype(jnp.bfloat16)
        first_copy(step, 1).start()

    def second(step):
        slot = lax.rem(step, 2)
        keep = lax.rem(step, 3)
        first_copy(step, 0).wait()
        away = product(step, 0, row, 1 - column) + recv_one[step, 0, 1 - column].astype(jnp.float32)
        send_two[slot, 0] = away.astype(jnp.bfloat16)
        second_copy(step, 0).start()
        here = product(step, 0, row, column) + recv_one[step, 0, column].astype(jnp.float32)
        kept[keep, 0] = here.astype(jnp.bfloat16)
        first_copy(step, 1).wait()
        away = product(step, 1, 1 - row, column) + recv_one[step, 1, 1 - row].astype(jnp.float32)
        send_two[slot, 1] = away.astype(jnp.bfloat16)
        second_copy(step, 1).start()
        here = product(step, 1, row, column) + recv_one[step, 1, row].astype(jnp.float32)
        kept[keep, 1] = here.astype(jnp.bfloat16)

    def third(step):
        keep = lax.rem(step, 3)
        for kind in range(2):
            second_copy(step, kind).wait()
            here = kept[keep, kind].astype(jnp.float32) + recv_two[step, kind].astype(jnp.float32)
            kept[keep, kind] = here.astype(jnp.bfloat16)
            for k in range(3):
                third_copy(step, kind, k).start()

    def last(step):
        keep = lax.rem(step, 3)
        for kind in range(2):
            total = kept[keep, kind, pl.ds(pl.multiple_of(level * share, share), share)].astype(
                jnp.float32
            )
            for k in range(3):
                third_copy(step, kind, k).wait()
                total = total + recv_three[step, kind, k].astype(jnp.float32)
            own[:, columns(step, kind)] = total

    def turn(step, carry):
        @pl.when(step < n)
        def _():
            first(step)

        for index in range(1, len(lefts)):

            @pl.when(step == index - 1)
            def _():
                load_left(index)

        @pl.when(jnp.logical_and(step >= 1, step < n + 1))
        def _():
            second(step - 1)

        @pl.when(jnp.logical_and(step >= 2, step < n + 2))
        def _():
            third(step - 2)

        @pl.when(step >= 3)
        def _():
            last(step - 3)

        return carry

    lax.fori_loop(0, n + 3, turn, 0)


def reduce_products(lefts, groups, right, gains, collective_id):
    dma = pltpu.SemaphoreType.DMA
    low = jnp.bfloat16
    rows, width = lefts[0].shape
    n = right.shape[1] // (2 * PIECE)
    share = width // 16
    count = len(lefts)

    def kernel(*refs):
        reduce_kernel(n, None, refs[:count], groups, *refs[count:])

    return pl.pallas_call(
        kernel,
        in_specs=[any_spec()] * count + [vmem_spec()] * 2,
        out_specs=vmem_spec(),
        out_shape=jax.ShapeDtypeStruct((share, right.shape[1]), jnp.float32),
        scratch_shapes=[
            pltpu.VMEM((count, 2, 2, 4 * share, rows), low),
            pltpu.VMEM((rows, width), low),
            pltpu.VMEM((2, 2, 2, 4 * share, PIECE), low),
            pltpu.VMEM((n, 2, 2, 4 * share, PIECE), low),
            pltpu.VMEM((2, 2, 4 * share, PIECE), low),
            pltpu.VMEM((n, 2, 4 * share, PIECE), low),
            pltpu.VMEM((3, 2, 4 * share, PIECE), low),
            pltpu.VMEM((n, 2, 3, share, PIECE), low),
            dma(()),
            dma((2, 2)),
            dma((n, 2)),
            dma((2, 2)),
            dma((n, 2)),
            dma((3, 2, 3)),
            dma((n, 2, 3)),
        ],
        compiler_params=pltpu.CompilerParams(
            collective_id=collective_id, has_side_effects=True, vmem_limit_bytes=61 * 1024 * 1024
        ),
        name="reduce_products",
    )(*lefts, right, gains)


def dot_f32(left, right):
    return jnp.dot(left, right, preferred_element_type=jnp.float32)


def by_heads(
    tokens,
    positions,
    gain_one,
    gain_two,
    w_query,
    w_key,
    w_value,
    w_out,
    w_gate,
    w_up,
    w_down,
    cotangent,
):
    low = jnp.bfloat16
    rows, _, width = tokens.shape
    both = ("dp", "context")
    share = gain_one.shape[0]
    hidden_width = w_gate.shape[1]
    length = rows * 8

    run_ids = (positions[::RUN, 0] // RUN).astype(low)
    extra = jnp.zeros((share, WIDE), low)
    extra = extra.at[:, 0].set(gain_one).at[:, 1].set(gain_two).at[: rows // RUN, 2].set(run_ids)
    near = gather_rows(jnp.concatenate([w_query, w_key, w_value, w_out.T, extra], axis=1), 9)
    far = lax.all_gather(
        jnp.concatenate([w_gate, w_up, w_down.T], axis=1), both, axis=0, tiled=True
    )
    qkv_width = w_query.shape[1] + w_key.shape[1] + w_value.shape[1]
    out_width = w_out.shape[0]
    qkv_mat = near[:, :qkv_width]
    out_mat_t = near[:, qkv_width : qkv_width + out_width]
    extras = near[:, qkv_width + out_width :]
    full_one, full_two = extras[:, 0], extras[:, 1]
    row = lax.axis_index("dp")
    ids = lax.dynamic_slice_in_dim(extras[:, 2].reshape(2, 8, share), row, 1, 0)[0, :, : rows // RUN]
    ids = ids.reshape(-1).astype(jnp.int32)
    count = ids.shape[0]
    order = jnp.sum(
        jnp.where(ids[None, :] == jnp.arange(count)[:, None], jnp.arange(count)[None, :], 0), axis=1
    ).astype(jnp.int32)
    gate_mat = far[:, :hidden_width]
    up_mat = far[:, hidden_width : 2 * hidden_width]
    down_mat_t = far[:, 2 * hidden_width :]

    spread = spread_matrix(8)
    cos_tab, sin_tab = lane_tables(positions[:, 0])
    flat_in = tokens.astype(jnp.float32).reshape(rows, width)
    unit_one, inverse_one, normed = norm_forward(flat_in, full_one)
    q_heads, kv_heads = project(
        normed,
        qkv_mat,
        spread[: 4 * HEAD, : 4 * WIDE],
        jnp.stack([cos_tab, jnp.ones_like(cos_tab)]),
        jnp.stack([sin_tab, jnp.zeros_like(sin_tab)]),
    )
    q_all, kv_all = to_heads(q_heads, kv_heads)
    q_all = q_all.reshape(length, WIDE)
    mixed, mixed_t, lse = attend(order, q_all, kv_all)
    mixed_heads = to_tokens(mixed.reshape(8, rows, WIDE))

    def narrow(heads):
        count = heads.shape[0]
        side = jnp.transpose(heads, (1, 0, 2)).reshape(rows, count * WIDE)
        return contract_cols(side, spread[: count * HEAD, : count * WIDE]).astype(low)

    mixed_low = narrow(mixed_heads)
    middle = flat_in + pair_sum(contract_cols(mixed_low, out_mat_t).astype(low), 5)
    unit_two, inverse_two, second = norm_forward(middle, full_two)
    gate_vals = dot_f32(second, gate_mat)
    up_vals = dot_f32(second, up_mat)
    sigmoid_vals = jax.nn.sigmoid(gate_vals)
    silu_vals = gate_vals * sigmoid_vals
    hidden = (silu_vals * up_vals).astype(low)
    mlp_part = pair_sum(contract_cols(hidden, down_mat_t).astype(low), 6)
    layer_out = (middle + mlp_part).astype(low).reshape(rows, 1, width)

    grad_low = cotangent.reshape(rows, width)
    grad_hidden = dot_f32(grad_low, down_mat_t)
    grad_gate_low = (
        grad_hidden * up_vals * sigmoid_vals * (1.0 + gate_vals * (1.0 - sigmoid_vals))
    ).astype(low)
    grad_up_low = (grad_hidden * silu_vals).astype(low)
    grad_second = pair_sum(
        (contract_cols(grad_gate_low, gate_mat) + contract_cols(grad_up_low, up_mat)).astype(low), 7
    )
    grad_mid_norm, grad_gain_two = norm_backward(grad_second, unit_two, inverse_two, full_two)
    grad_middle = grad_low.astype(jnp.float32) + grad_mid_norm
    grad_mid_low = grad_middle.astype(low)
    grad_mixed = dot_f32(grad_mid_low, out_mat_t).astype(low)
    grad_heads = jnp.transpose(
        dot_f32(grad_mixed, spread).astype(low).reshape(rows, 8, WIDE), (1, 0, 2)
    )
    d_all = grads_to_heads(grad_heads).reshape(length, WIDE)
    dq, dkv = attend_back(order, q_all, kv_all, d_all, mixed_t, lse)
    dq_own, dkv_own = grads_to_tokens(
        dq.reshape(8, rows, WIDE), dkv.reshape(2, 8, rows, WIDE)
    )

    def unturn(heads):
        part = heads.astype(jnp.float32)
        return (part * cos_tab - jnp.roll(part, WIDE // 2, axis=-1) * sin_tab).astype(low)

    grad_qkv_low = jnp.concatenate(
        [narrow(unturn(dq_own)), narrow(unturn(dkv_own[:, 0])), narrow(dkv_own[:, 1])], axis=1
    )
    grad_normed = pair_sum(contract_cols(grad_qkv_low, qkv_mat).astype(low), 8)
    grad_in_norm, grad_gain_one = norm_backward(grad_normed, unit_one, inverse_one, full_one)
    input_grad = (grad_middle + grad_in_norm).reshape(rows, 1, width)
    gains = jnp.stack([grad_gain_one, grad_gain_two], axis=1)
    gains_high = gains.astype(low)
    gains_low = (gains - gains_high.astype(jnp.float32)).astype(low)
    gains = jnp.concatenate([gains_high, gains_low], axis=1)
    gains = jnp.pad(gains, ((0, 0), (0, PIECE - gains.shape[1])))
    gains = jnp.transpose(gains.reshape(2, 4, 2, share, PIECE), (0, 2, 1, 3, 4))
    right = jnp.concatenate(
        [
            grad_gate_low,
            grad_up_low,
            hidden,
            grad_qkv_low,
            mixed_low,
            jnp.zeros((rows, PIECE), low),
        ],
        axis=1,
    )
    steps = hidden_width // (2 * PIECE)
    near_steps = qkv_width // (2 * PIECE)
    grads = reduce_products(
        (second, grad_low, normed, grad_mid_low),
        (0, 2 * steps, 3 * steps, 3 * steps + near_steps),
        right,
        gains.reshape(2, 2, 4 * share, PIECE),
        10,
    )
    far_own = grads[:, : 3 * hidden_width]
    near_own = grads[:, 3 * hidden_width :]
    gain_own = near_own[:, qkv_width + out_width :]
    q_width, k_width = w_query.shape[1], w_key.shape[1]
    return (
        layer_out,
        input_grad,
        gain_own[:, 0] + gain_own[:, 2],
        gain_own[:, 1] + gain_own[:, 3],
        near_own[:, :q_width],
        near_own[:, q_width : q_width + k_width],
        near_own[:, q_width + k_width : qkv_width],
        near_own[:, qkv_width : qkv_width + out_width].T,
        far_own[:, :hidden_width],
        far_own[:, hidden_width : 2 * hidden_width],
        far_own[:, 2 * hidden_width :].T,
    )


def solution(mesh):
    sizes = (mesh.shape["dp"], mesh.shape["context"], mesh.shape["tensor"])
    return jax.shard_map(
        by_heads if sizes == (2, 8, 2) else on_device,
        mesh=mesh,
        in_specs=(
            P("context", "dp", None),
            P("context", "dp"),
            P(("dp", "context")),
            P(("dp", "context")),
            P(("dp", "context"), "tensor"),
            P(("dp", "context"), "tensor"),
            P(("dp", "context"), "tensor"),
            P("tensor", ("dp", "context")),
            P(("dp", "context"), "tensor"),
            P(("dp", "context"), "tensor"),
            P("tensor", ("dp", "context")),
            P("context", "dp", None),
        ),
        out_specs=(
            P("context", "dp", None),
            P("context", "dp", None),
            P(("dp", "context")),
            P(("dp", "context")),
            P(("dp", "context"), "tensor"),
            P(("dp", "context"), "tensor"),
            P(("dp", "context"), "tensor"),
            P("tensor", ("dp", "context")),
            P(("dp", "context"), "tensor"),
            P(("dp", "context"), "tensor"),
            P("tensor", ("dp", "context")),
        ),
        check_vma=False,
    )
```

```python
import functools

import jax
import jax.numpy as jnp
from jax import lax
from jax.experimental import pallas as pl
from jax.experimental.pallas import tpu as pltpu
from jax.sharding import PartitionSpec as P

HEAD = 96


epsilon = 1e-05
theta_base = 100000.0
masked_value = -1e30


def norm_forward(values_in, gain_vec):
    inverse = lax.rsqrt(jnp.mean(values_in * values_in, axis=-1, keepdims=True) + epsilon)
    unit_vals = values_in * inverse
    return (unit_vals, inverse, (unit_vals * gain_vec.astype(jnp.float32)).astype(jnp.bfloat16))


def norm_backward(grad_in, unit_vals, inverse, gain_vec):
    scaled = grad_in * gain_vec.astype(jnp.float32)
    grad_vals = inverse * (
        scaled - unit_vals * jnp.mean(scaled * unit_vals, axis=-1, keepdims=True)
    )
    return (grad_vals, jnp.sum(grad_in * unit_vals, axis=0))


def rotate(values_in, cos_part, sin_part):
    half_size = values_in.shape[-1] // 2
    front_half = values_in[..., :half_size]
    back_half = values_in[..., half_size:]
    return jnp.concatenate(
        [
            front_half * cos_part - back_half * sin_part,
            back_half * cos_part + front_half * sin_part,
        ],
        axis=-1,
    )


def contract_rows(left_mat, right_mat):
    return lax.dot_general(
        left_mat, right_mat, (((0,), (0,)), ((), ())), preferred_element_type=jnp.float32
    )


def contract_cols(left_mat, right_mat):
    return lax.dot_general(
        left_mat, right_mat, (((1,), (1,)), ((), ())), preferred_element_type=jnp.float32
    )


def on_device(
    tokens,
    positions,
    gain_one,
    gain_two,
    w_query,
    w_key,
    w_value,
    w_out,
    w_gate,
    w_up,
    w_down,
    cotangent,
):
    slot_count, seq_count, model_width = tokens.shape
    row_count = slot_count * seq_count
    gathered = (
        lax.all_gather(gain_one, ("dp", "context"), axis=0, tiled=True),
        lax.all_gather(gain_two, ("dp", "context"), axis=0, tiled=True),
        lax.all_gather(w_query, ("dp", "context"), axis=0, tiled=True),
        lax.all_gather(w_key, ("dp", "context"), axis=0, tiled=True),
        lax.all_gather(w_value, ("dp", "context"), axis=0, tiled=True),
        lax.all_gather(w_out, ("dp", "context"), axis=1, tiled=True),
        lax.all_gather(w_gate, ("dp", "context"), axis=0, tiled=True),
        lax.all_gather(w_up, ("dp", "context"), axis=0, tiled=True),
        lax.all_gather(w_down, ("dp", "context"), axis=1, tiled=True),
    )
    full_one, full_two, query_mat, key_mat, value_mat, out_mat, gate_mat, up_mat, down_mat = (
        gathered
    )
    heads_kv = key_mat.shape[1] // HEAD
    heads_q = query_mat.shape[1] // HEAD
    group_size = heads_q // heads_kv
    score_scale = HEAD ** (-0.5)
    half_size = HEAD // 2
    inv_freqs = theta_base ** (-2.0 * jnp.arange(half_size, dtype=jnp.float32) / HEAD)
    angles = positions.astype(jnp.float32)[:, :, None] * inv_freqs
    cos_part = jnp.cos(angles)[:, :, None, :]
    sin_part = jnp.sin(angles)[:, :, None, :]
    flat_in = tokens.astype(jnp.float32).reshape(row_count, model_width)
    unit_one, inverse_one, normed = norm_forward(flat_in, full_one)
    query_proj = jnp.dot(normed, query_mat, preferred_element_type=jnp.float32).reshape(
        slot_count, seq_count, heads_q, HEAD
    )
    key_proj = jnp.dot(normed, key_mat, preferred_element_type=jnp.float32).reshape(
        slot_count, seq_count, heads_kv, HEAD
    )
    value_low = (
        jnp.dot(normed, value_mat, preferred_element_type=jnp.float32)
        .astype(jnp.bfloat16)
        .reshape(slot_count, seq_count, heads_kv * HEAD)
    )
    queries = rotate(query_proj, cos_part, sin_part).astype(jnp.bfloat16)
    keys_low = (
        rotate(key_proj, cos_part, sin_part)
        .astype(jnp.bfloat16)
        .reshape(slot_count, seq_count, heads_kv * HEAD)
    )
    query_seq = jnp.transpose(
        queries.reshape(slot_count, seq_count, heads_kv, group_size, HEAD), (1, 2, 3, 0, 4)
    )
    query_pos = positions.T
    stat_shape = (seq_count, heads_kv, group_size, slot_count)
    initial = (
        jnp.full(stat_shape, masked_value, jnp.float32),
        jnp.zeros(stat_shape, jnp.float32),
        jnp.zeros(stat_shape + (HEAD,), jnp.float32),
    )
    key_piece = lax.all_gather(keys_low, "context", axis=0, tiled=True)
    value_piece = lax.all_gather(value_low, "context", axis=0, tiled=True)
    pos_piece = lax.all_gather(positions, "context", axis=0, tiled=True)
    piece_len = key_piece.shape[0]
    key_seq = jnp.transpose(key_piece.reshape(piece_len, seq_count, heads_kv, HEAD), (1, 2, 0, 3))
    value_seq = jnp.transpose(
        value_piece.reshape(piece_len, seq_count, heads_kv, HEAD), (1, 2, 0, 3)
    )
    pos_seq = pos_piece.T

    def per_sequence(seq_items):
        peak_val, totals, accum_vals, query_one, qpos_one, key_one, value_one, kpos_one = seq_items
        raw_scores = (
            jnp.einsum("hgqd,hkd->hgqk", query_one, key_one, preferred_element_type=jnp.float32)
            * score_scale
        )
        allowed = kpos_one[None, None, None, :] <= qpos_one[None, None, :, None]
        masked = jnp.where(allowed, raw_scores, masked_value)
        new_peak = jnp.maximum(peak_val, jnp.max(masked, axis=-1))
        decay_vals = jnp.exp(peak_val - new_peak)
        weights = jnp.where(allowed, jnp.exp(masked - new_peak[..., None]), 0.0)
        totals = totals * decay_vals + jnp.sum(weights, axis=-1)
        accum_vals = accum_vals * decay_vals[..., None] + jnp.einsum(
            "hgqk,hkd->hgqd",
            weights.astype(jnp.bfloat16),
            value_one,
            preferred_element_type=jnp.float32,
        )
        return (new_peak, totals, accum_vals)

    peak_val, totals, accum_vals = lax.map(
        per_sequence,
        (initial[0], initial[1], initial[2], query_seq, query_pos, key_seq, value_seq, pos_seq),
    )
    log_total = peak_val + jnp.log(totals)
    mixed_seq = accum_vals / totals[..., None]
    mixed_low = (
        jnp.transpose(mixed_seq, (3, 0, 1, 2, 4))
        .reshape(row_count, heads_q * HEAD)
        .astype(jnp.bfloat16)
    )
    branch = lax.psum(
        jnp.dot(mixed_low, out_mat, preferred_element_type=jnp.float32).astype(jnp.bfloat16),
        "tensor",
    ).astype(jnp.float32)
    middle = flat_in + branch
    unit_two, inverse_two, second = norm_forward(middle, full_two)
    gate_vals = jnp.dot(second, gate_mat, preferred_element_type=jnp.float32)
    up_vals = jnp.dot(second, up_mat, preferred_element_type=jnp.float32)
    sigmoid_vals = jax.nn.sigmoid(gate_vals)
    silu_vals = gate_vals * sigmoid_vals
    hidden = (silu_vals * up_vals).astype(jnp.bfloat16)
    mlp_part = lax.psum(
        jnp.dot(hidden, down_mat, preferred_element_type=jnp.float32).astype(jnp.bfloat16), "tensor"
    ).astype(jnp.float32)
    layer_out = (middle + mlp_part).astype(jnp.bfloat16).reshape(slot_count, seq_count, model_width)
    regathered = (
        lax.all_gather(gain_one, ("dp", "context"), axis=0, tiled=True),
        lax.all_gather(gain_two, ("dp", "context"), axis=0, tiled=True),
        lax.all_gather(w_query, ("dp", "context"), axis=0, tiled=True),
        lax.all_gather(w_key, ("dp", "context"), axis=0, tiled=True),
        lax.all_gather(w_value, ("dp", "context"), axis=0, tiled=True),
        lax.all_gather(w_out, ("dp", "context"), axis=1, tiled=True),
        lax.all_gather(w_gate, ("dp", "context"), axis=0, tiled=True),
        lax.all_gather(w_up, ("dp", "context"), axis=0, tiled=True),
        lax.all_gather(w_down, ("dp", "context"), axis=1, tiled=True),
    )
    full_one, full_two, query_mat, key_mat, value_mat, out_mat, gate_mat, up_mat, down_mat = (
        regathered
    )
    grad_low = cotangent.reshape(row_count, model_width)
    grad_down = contract_rows(hidden, grad_low)
    grad_hidden = contract_cols(grad_low, down_mat)
    grad_gate_low = (
        grad_hidden * up_vals * sigmoid_vals * (1.0 + gate_vals * (1.0 - sigmoid_vals))
    ).astype(jnp.bfloat16)
    grad_up_low = (grad_hidden * silu_vals).astype(jnp.bfloat16)
    grad_gate = contract_rows(second, grad_gate_low)
    grad_up = contract_rows(second, grad_up_low)
    grad_second = lax.psum(
        (contract_cols(grad_gate_low, gate_mat) + contract_cols(grad_up_low, up_mat)).astype(
            jnp.bfloat16
        ),
        "tensor",
    ).astype(jnp.float32)
    grad_mid_norm, grad_gain_two = norm_backward(grad_second, unit_two, inverse_two, full_two)
    grad_middle = grad_low.astype(jnp.float32) + grad_mid_norm
    grad_mid_low = grad_middle.astype(jnp.bfloat16)
    grad_out = contract_rows(mixed_low, grad_mid_low)
    grad_mixed = contract_cols(grad_mid_low, out_mat).astype(jnp.bfloat16)
    grad_mixed_seq = jnp.transpose(
        grad_mixed.reshape(slot_count, seq_count, heads_kv, group_size, HEAD), (1, 2, 3, 0, 4)
    )
    delta_rows = jnp.sum(grad_mixed_seq.astype(jnp.float32) * mixed_seq, axis=-1)
    kv_width = heads_kv * HEAD

    def block_grads(grad_query_acc, key_blk, value_blk, pos_blk):
        block_len = key_blk.shape[0]
        key_seq = jnp.transpose(key_blk.reshape(block_len, seq_count, heads_kv, HEAD), (1, 2, 0, 3))
        value_seq = jnp.transpose(
            value_blk.reshape(block_len, seq_count, heads_kv, HEAD), (1, 2, 0, 3)
        )
        raw_scores = (
            jnp.einsum("shgqd,shkd->shgqk", query_seq, key_seq, preferred_element_type=jnp.float32)
            * score_scale
        )
        allowed = pos_blk.T[:, None, None, None, :] <= query_pos[:, None, None, :, None]
        prob_vals = jnp.where(
            allowed,
            jnp.exp(jnp.where(allowed, raw_scores - log_total[..., None], masked_value)),
            0.0,
        )
        grad_value_blk = jnp.einsum(
            "shgqk,shgqd->kshd",
            prob_vals.astype(jnp.bfloat16),
            grad_mixed_seq,
            preferred_element_type=jnp.float32,
        )
        grad_probs = jnp.einsum(
            "shgqd,shkd->shgqk", grad_mixed_seq, value_seq, preferred_element_type=jnp.float32
        )
        grad_scores = (prob_vals * (grad_probs - delta_rows[..., None])).astype(jnp.bfloat16)
        grad_query_acc = grad_query_acc + jnp.einsum(
            "shgqk,shkd->shgqd", grad_scores, key_seq, preferred_element_type=jnp.float32
        )
        grad_key_blk = jnp.einsum(
            "shgqk,shgqd->kshd", grad_scores, query_seq, preferred_element_type=jnp.float32
        )
        return (
            grad_query_acc,
            grad_key_blk.reshape(block_len, seq_count, kv_width),
            grad_value_blk.reshape(block_len, seq_count, kv_width),
        )

    zero_query = jnp.zeros(stat_shape + (HEAD,), jnp.float32)
    key_all, value_all, pos_all = (
        lax.all_gather(keys_low, "context", axis=0, tiled=True),
        lax.all_gather(value_low, "context", axis=0, tiled=True),
        lax.all_gather(positions, "context", axis=0, tiled=True),
    )
    total_len = key_all.shape[0]
    block_size = min(512, total_len)
    block_count = total_len // block_size

    def key_block(grad_query_acc, block_items):
        key_blk, value_blk, pos_blk = block_items
        grad_query_acc, grad_key_blk, grad_value_blk = block_grads(
            grad_query_acc, key_blk, value_blk, pos_blk
        )
        return (grad_query_acc, (grad_key_blk, grad_value_blk))

    grad_query_acc, (grad_keys_all, grad_values_all) = lax.scan(
        key_block,
        zero_query,
        (
            key_all.reshape(block_count, block_size, seq_count, kv_width),
            value_all.reshape(block_count, block_size, seq_count, kv_width),
            pos_all.reshape(block_count, block_size, seq_count),
        ),
    )
    grad_key_own, grad_value_own = (
        lax.psum_scatter(
            grad_keys_all.reshape(total_len, seq_count, kv_width).astype(jnp.bfloat16),
            "context",
            scatter_dimension=0,
            tiled=True,
        ).astype(jnp.float32),
        lax.psum_scatter(
            grad_values_all.reshape(total_len, seq_count, kv_width).astype(jnp.bfloat16),
            "context",
            scatter_dimension=0,
            tiled=True,
        ).astype(jnp.float32),
    )
    grad_rot_q = jnp.transpose(grad_query_acc * score_scale, (3, 0, 1, 2, 4)).reshape(
        slot_count, seq_count, heads_q, HEAD
    )
    grad_q_low = (
        rotate(grad_rot_q, cos_part, -sin_part)
        .reshape(row_count, heads_q * HEAD)
        .astype(jnp.bfloat16)
    )
    grad_rot_k = (grad_key_own * score_scale).reshape(slot_count, seq_count, heads_kv, HEAD)
    grad_k_low = (
        rotate(grad_rot_k, cos_part, -sin_part).reshape(row_count, kv_width).astype(jnp.bfloat16)
    )
    grad_v_low = grad_value_own.reshape(row_count, kv_width).astype(jnp.bfloat16)
    grad_query = contract_rows(normed, grad_q_low)
    grad_key = contract_rows(normed, grad_k_low)
    grad_value = contract_rows(normed, grad_v_low)
    grad_normed = lax.psum(
        (
            contract_cols(grad_q_low, query_mat)
            + contract_cols(grad_k_low, key_mat)
            + contract_cols(grad_v_low, value_mat)
        ).astype(jnp.bfloat16),
        "tensor",
    ).astype(jnp.float32)
    grad_in_norm, grad_gain_one = norm_backward(grad_normed, unit_one, inverse_one, full_one)
    input_grad = (grad_middle + grad_in_norm).reshape(slot_count, seq_count, model_width)
    reduced = (
        lax.psum_scatter(grad_gain_one, ("dp", "context"), scatter_dimension=0, tiled=True),
        lax.psum_scatter(grad_gain_two, ("dp", "context"), scatter_dimension=0, tiled=True),
        lax.psum_scatter(grad_query, ("dp", "context"), scatter_dimension=0, tiled=True),
        lax.psum_scatter(grad_key, ("dp", "context"), scatter_dimension=0, tiled=True),
        lax.psum_scatter(grad_value, ("dp", "context"), scatter_dimension=0, tiled=True),
        lax.psum_scatter(grad_out, ("dp", "context"), scatter_dimension=1, tiled=True),
        lax.psum_scatter(grad_gate, ("dp", "context"), scatter_dimension=0, tiled=True),
        lax.psum_scatter(grad_up, ("dp", "context"), scatter_dimension=0, tiled=True),
        lax.psum_scatter(grad_down, ("dp", "context"), scatter_dimension=1, tiled=True),
    )
    return (
        layer_out,
        input_grad,
        reduced[0],
        reduced[1],
        reduced[2],
        reduced[3],
        reduced[4],
        reduced[5],
        reduced[6],
        reduced[7],
        reduced[8],
    )


WIDE = 128
RUN = 256
TILE = 512
LOG2_E = 1.4426950408889634
MESH = pl.DeviceIdType.MESH
VMEM_LIMIT = 56 * 1024 * 1024


def any_spec():
    return pl.BlockSpec(memory_space=pl.ANY)


def vmem_spec():
    return pl.BlockSpec(memory_space=pltpu.VMEM)


def place():
    return lax.axis_index("dp"), lax.axis_index("context"), lax.axis_index("tensor")


def greet(devices):
    barrier = pltpu.get_barrier_semaphore()
    for device in devices:
        pl.semaphore_signal(barrier, inc=1, device_id=device, device_id_type=MESH)
    pl.semaphore_wait(barrier, len(devices))


def sequence_others():
    row, spot, core = place()
    return [
        (row, lax.rem(spot + shift, 8), lax.rem(core + flip, 2))
        for shift in range(8)
        for flip in range(2)
        if shift or flip
    ]


def greet_sequence():
    greet(sequence_others())


def remote(source, target, send, recv, device):
    return pltpu.make_async_remote_copy(
        src_ref=source,
        dst_ref=target,
        send_sem=send,
        recv_sem=recv,
        device_id=device,
        device_id_type=MESH,
    )


def move(source, target, send, recv, device, is_self):
    @pl.when(is_self)
    def _():
        pltpu.make_async_copy(source, target, recv).start()

    @pl.when(jnp.logical_not(is_self))
    def _():
        remote(source, target, send, recv, device).start()


def spread_matrix(heads):
    shape = (heads * HEAD, heads * WIDE)
    rows = lax.broadcasted_iota(jnp.int32, shape, 0)
    cols = lax.broadcasted_iota(jnp.int32, shape, 1)
    dims = rows % HEAD
    target = (rows // HEAD) * WIDE + dims + jnp.where(dims >= HEAD // 2, (WIDE - HEAD) // 2, 0)
    return (cols == target).astype(jnp.bfloat16)


def lane_tables(positions):
    half = HEAD // 2
    inv_freqs = theta_base ** (-2.0 * jnp.arange(half, dtype=jnp.float32) / HEAD)
    gap = jnp.zeros((WIDE // 2 - half,), jnp.float32)
    freqs = jnp.concatenate([inv_freqs, gap, inv_freqs, gap])
    sign = jnp.where(jnp.arange(WIDE) < WIDE // 2, -1.0, 1.0)
    angles = positions.astype(jnp.float32)[:, None] * freqs
    return jnp.cos(angles), jnp.sin(angles) * sign


def grads_to_heads_kernel(d_ref, d_all, send, recv):
    row, spot, core = place()
    greet_sequence()
    copies = []
    for step in range(4):
        slot = lax.rem(spot + step, 4)
        chip = 4 * core + slot
        for other in range(2):
            is_self = jnp.logical_and(chip == spot, core == other)
            copies.append(
                (
                    (
                        d_ref.at[2 * slot + other],
                        d_all.at[spot],
                        send.at[step, other],
                        recv.at[spot],
                        (row, chip, other),
                    ),
                    is_self,
                )
            )
    for parts, is_self in copies:
        move(*parts, is_self)
    for step in range(8):
        remote(
            d_all.at[step], d_all.at[step], send.at[0, 0], recv.at[step], (row, spot, 1 - core)
        ).wait_recv()
    for parts, is_self in copies:

        @pl.when(jnp.logical_not(is_self))
        def _():
            remote(*parts).wait_send()


def grads_to_heads(grad_heads):
    dma = pltpu.SemaphoreType.DMA
    return pl.pallas_call(
        grads_to_heads_kernel,
        in_specs=[any_spec()],
        out_specs=any_spec(),
        out_shape=jax.ShapeDtypeStruct(grad_heads.shape, jnp.bfloat16),
        scratch_shapes=[dma((4, 2)), dma((8,))],
        compiler_params=pltpu.CompilerParams(collective_id=2, has_side_effects=True),
        name="grads_to_heads",
    )(grad_heads)


def return_copies(ref, out, send, recv):
    row, spot, core = place()
    head = 2 * lax.rem(spot, 4) + core
    owner = spot // 4
    copies = []
    for step in range(8):
        chip = lax.rem(spot + step, 8)
        is_self = (owner == core) if step == 0 else False
        parts = (ref.at[chip], out.at[head], send.at[step], recv.at[head], (row, chip, owner))
        copies.append((parts, is_self))
    return copies


def start_return(copies):
    for parts, is_self in copies:
        if is_self is False:
            remote(*parts).start()
        else:
            move(*parts, is_self)


def finish_return(copies, out, send, recv):
    row, spot, core = place()
    for head in range(8):
        remote(
            out.at[head], out.at[head], send.at[0], recv.at[head], (row, spot, 1 - core)
        ).wait_recv()
    for parts, is_self in copies:
        if is_self is False:
            remote(*parts).wait_send()
        else:

            @pl.when(jnp.logical_not(is_self))
            def _():
                remote(*parts).wait_send()


def grads_to_tokens_kernel(
    dq_ref, dkv_ref, dq_out, dkv_out, own, other, send, recv, send_x, recv_x, local, send_k, recv_k
):
    row, spot, core = place()
    greet_sequence()
    own_rows = pl.ds(pl.multiple_of(core * RUN, RUN), RUN)
    other_rows = pl.ds(pl.multiple_of((1 - core) * RUN, RUN), RUN)
    swap = remote(
        dkv_ref.at[:, :, other_rows], other, send_x, recv_x, (row, spot, 1 - core)
    )
    swap.start()
    load = pltpu.make_async_copy(dkv_ref.at[:, :, own_rows], own, local)
    load.start()
    copies = return_copies(dq_ref, dq_out, send, recv)
    start_return(copies)
    load.wait()
    swap.wait()
    slot = lax.rem(spot, 4)
    owner = spot // 4
    backs = []
    for step in range(8):
        chip = lax.rem(spot + step, 8)
        total = own[:, chip].astype(jnp.float32) + other[:, chip].astype(jnp.float32)
        own[:, chip] = total.astype(jnp.bfloat16)
        parts = (
            own.at[:, chip],
            dkv_out.at[slot, :, own_rows],
            send_k.at[step],
            recv_k.at[slot, core],
            (row, chip, owner),
        )
        is_self = (owner == core) if step == 0 else False
        backs.append((parts, is_self))
        start_return(backs[-1:])
    for slot_in in range(4):
        for core_in in range(2):
            target = dkv_out.at[slot_in, :, pl.ds(core_in * RUN, RUN)]
            remote(
                target, target, send_k.at[0], recv_k.at[slot_in, core_in], (row, spot, 1 - core)
            ).wait_recv()
    for parts, is_self in backs:
        if is_self is False:
            remote(*parts).wait_send()
        else:

            @pl.when(jnp.logical_not(is_self))
            def _():
                remote(*parts).wait_send()

    finish_return(copies, dq_out, send, recv)


def grads_to_tokens(dq, dkv):
    dma = pltpu.SemaphoreType.DMA
    rows = dq.shape[1]
    return pl.pallas_call(
        grads_to_tokens_kernel,
        in_specs=[any_spec(), any_spec()],
        out_specs=[any_spec(), any_spec()],
        out_shape=[
            jax.ShapeDtypeStruct((8, rows, WIDE), jnp.bfloat16),
            jax.ShapeDtypeStruct((4, 2, rows, WIDE), jnp.bfloat16),
        ],
        scratch_shapes=[
            pltpu.VMEM((2, 8, RUN, WIDE), jnp.bfloat16),
            pltpu.VMEM((2, 8, RUN, WIDE), jnp.bfloat16),
            dma((8,)),
            dma((8,)),
            dma(()),
            dma(()),
            dma(()),
            dma((8,)),
            dma((4, 2)),
        ],
        compiler_params=pltpu.CompilerParams(
            collective_id=4, has_side_effects=True, vmem_limit_bytes=VMEM_LIMIT
        ),
        name="grads_to_tokens",
    )(dq, dkv)


def pair_sum_kernel(part, total, other, send, recv):
    row, spot, core = place()
    sibling = (row, spot, 1 - core)
    greet([sibling])
    pieces = send.shape[0]
    rows = part.shape[0] // pieces

    def piece(index):
        cut = pl.ds(index * rows, rows)
        return remote(part.at[cut], other.at[cut], send.at[index], recv.at[index], sibling)

    for index in range(pieces):
        piece(index).start()
    for index in range(pieces):
        cut = pl.ds(index * rows, rows)
        piece(index).wait()
        total[cut] = part[cut].astype(jnp.float32) + other[cut].astype(jnp.float32)


def pair_sum(part, collective_id):
    dma = pltpu.SemaphoreType.DMA
    return pl.pallas_call(
        pair_sum_kernel,
        in_specs=[vmem_spec()],
        out_specs=vmem_spec(),
        out_shape=jax.ShapeDtypeStruct(part.shape, jnp.float32),
        scratch_shapes=[pltpu.VMEM(part.shape, part.dtype), dma((4,)), dma((4,))],
        compiler_params=pltpu.CompilerParams(
            collective_id=collective_id, has_side_effects=True, vmem_limit_bytes=VMEM_LIMIT
        ),
        name="pair_sum",
    )(part)


def tile_at(index, size):
    return pl.ds(pl.multiple_of(index * size, size), size)


def causal(scores):
    keys = lax.broadcasted_iota(jnp.int32, scores.shape, 0)
    queries = lax.broadcasted_iota(jnp.int32, scores.shape, 1)
    return jnp.where(keys <= queries, scores, masked_value)


def neighbours():
    row, spot, core = place()
    level, column = spot // 2, lax.rem(spot, 2)
    beside_x = (1 - row, spot, core)
    beside_y = (row, 2 * level + 1 - column, core)
    along_z = [(row, 2 * lax.rem(level + k, 4) + column, core) for k in (1, 2, 3)]
    return row, level, column, beside_x, beside_y, along_z


class Gather:
    def __init__(self, own, whole, start, width, piece, sems):
        self.own, self.whole = own.at[:, pl.ds(start, width)], whole
        self.start, self.width = start, width
        self.sems = [sem.at[piece] for sem in sems]

    def block(self, x, z, y, half=None):
        cut = self.width // 2 // WIDE * WIDE
        start, width = self.start, self.width
        if half == 0:
            width = cut
        elif half == 1:
            start, width = start + cut, width - cut
        return self.whole.at[x, z, y, :, pl.ds(start, width)]

    def arrived(self, target, recv_sem):
        device = neighbours()[3]
        remote(target, target, self.sems[0].at[0], recv_sem, device).wait_recv()

    def copies_z(self):
        send_z, recv_z = self.sems[:2]
        row, level, column, beside_x, beside_y, along_z = neighbours()
        mine = self.block(row, level, column)
        return [
            remote(self.own, mine, send_z.at[k], recv_z.at[k], along_z[k]) for k in range(3)
        ]

    def copies_xy(self, k):
        send_x, recv_x, send_y, recv_y = self.sems[2:6]
        row, level, column, beside_x, beside_y, along_z = neighbours()
        block = self.block(row, lax.rem(level + 4 - k, 4), column)
        source = self.own if k == 0 else block
        return [
            remote(source, block, send_x.at[k], recv_x.at[k], beside_x),
            remote(source, block, send_y.at[k], recv_y.at[k], beside_y),
        ]

    def copies_diagonal(self, k):
        send_d, recv_d = self.sems[6:8]
        row, level, column, beside_x, beside_y, along_z = neighbours()
        z = lax.rem(level + 4 - k, 4)
        by_y = self.block(1 - row, z, column, 1)
        by_x = self.block(row, z, 1 - column, 0)
        return [
            remote(by_y, by_y, send_d.at[0, k], recv_d.at[0, k], beside_y),
            remote(by_x, by_x, send_d.at[1, k], recv_d.at[1, k], beside_x),
        ]

    def open_z(self):
        for copy in self.copies_z():
            copy.start()

    def open_xy(self):
        row, level, column, beside_x, beside_y, along_z = neighbours()
        for copy in self.copies_xy(0):
            copy.start()
        pltpu.make_async_copy(self.own, self.block(row, level, column), self.sems[8]).start()

    def pass_on(self, k):
        row, level, column, beside_x, beside_y, along_z = neighbours()
        self.arrived(self.block(row, lax.rem(level + 4 - k, 4), column), self.sems[1].at[k - 1])
        for copy in self.copies_xy(k):
            copy.start()

    def diagonal(self, k):
        recv_x, recv_y = self.sems[3], self.sems[5]
        row, level, column, beside_x, beside_y, along_z = neighbours()
        z = lax.rem(level + 4 - k, 4)
        by_y, by_x = self.copies_diagonal(k)
        self.arrived(self.block(1 - row, z, column), recv_x.at[k])
        by_y.start()
        self.arrived(self.block(row, z, 1 - column), recv_y.at[k])
        by_x.start()

    def finish(self):
        recv_d, local = self.sems[7:]
        row, level, column, beside_x, beside_y, along_z = neighbours()
        for k in range(4):
            z = lax.rem(level + 4 - k, 4)
            self.arrived(self.block(1 - row, z, 1 - column, 1), recv_d.at[0, k])
            self.arrived(self.block(1 - row, z, 1 - column, 0), recv_d.at[1, k])
        mine = self.block(row, level, column)
        pltpu.make_async_copy(self.own, mine, local).wait()

    def close(self):
        for copy in self.copies_z():
            copy.wait_send()
        for k in range(4):
            for copy in self.copies_xy(k) + self.copies_diagonal(k):
                copy.wait_send()


def gather_sems(pieces):
    dma = pltpu.SemaphoreType.DMA
    shapes = [(3,), (3,), (4,), (4,), (4,), (4,), (2, 4), (2, 4), ()]
    return [dma((pieces,) + shape) for shape in shapes]


def forward_kernel(
    tokens,
    ids_in,
    near_own,
    far_own,
    spread,
    cos_tab,
    sin_tab,
    near,
    far,
    normed_out,
    q_out,
    kv_out,
    mixed_heads,
    mixed_t_out,
    lse_out,
    unit,
    normed,
    weight,
    extras,
    q_heads,
    kv_heads,
    q_slots,
    kv_slots,
    q_t,
    keys,
    v_t,
    mixed_t,
    lse,
    mixed,
    mixed_slots,
    ids_all,
    ids,
    order,
    send_ids,
    recv_ids,
    load_ids,
    load_w,
    load_extra,
    saves,
    send_q,
    recv_q,
    send_kv,
    recv_kv,
    send_x,
    recv_x,
    send_m,
    recv_m,
    *sems,
):
    row, spot, core = place()
    level, column = spot // 2, lax.rem(spot, 2)
    rows = tokens.shape[0]
    low = jnp.bfloat16
    length = 8 * rows
    near_gather = Gather(near_own, near, 0, near_own.shape[1], 0, sems)
    third = far_own.shape[1] // 3
    far_gathers = [Gather(far_own, far, part * third, third, part + 1, sems) for part in range(3)]

    greet(sequence_others() + [neighbours()[3]])
    near_gather.open_z()
    near_gather.open_xy()

    ids_copies = []
    for shift in range(1, 8):
        copy = remote(
            ids_in,
            ids_all.at[spot],
            send_ids.at[shift],
            recv_ids.at[shift],
            (row, lax.rem(spot + shift, 8), core),
        )
        copy.start()
        ids_copies.append(copy)
    ids_all[spot] = ids_in[...]

    values = tokens[...].astype(jnp.float32)
    unit[...] = values * lax.rsqrt(jnp.mean(values * values, axis=-1, keepdims=True) + epsilon)

    for k in range(1, 4):
        near_gather.pass_on(k)
        near_gather.diagonal(k - 1)
        if k == 2:
            far_gathers[0].open_z()
    far_gathers[0].open_xy()
    near_gather.diagonal(3)
    for shift in range(1, 8):
        remote(
            ids_in,
            ids_all.at[lax.rem(spot + 8 - shift, 8)],
            send_ids.at[shift],
            recv_ids.at[shift],
            (row, lax.rem(spot + shift, 8), core),
        ).wait_recv()
    pltpu.make_async_copy(ids_all, ids, load_ids).start()
    far_gathers[0].pass_on(1)
    near_gather.finish()

    width = near.shape[3] * 16
    qkv_width = 16 * HEAD

    def load_group(group):
        lanes = pl.ds(group * 4 * HEAD, 4 * HEAD)
        return pltpu.make_async_copy(
            near.at[:, :, :, :, lanes], weight.at[group % 2], load_w.at[group % 2]
        )

    load_extras = pltpu.make_async_copy(
        near.at[:, :, :, :, pl.ds(near_own.shape[1] - WIDE, WIDE)], extras, load_extra
    )
    load_extras.start()
    load_group(0).start()
    load_group(1).start()
    load_extras.wait()
    gain = extras[...].reshape(width, WIDE).T[0:1].astype(jnp.float32)
    normed[...] = (unit[...] * gain).astype(low)
    save_normed = pltpu.make_async_copy(normed, normed_out, saves.at[0])
    save_normed.start()
    for group in range(4):
        load_group(group).wait()
        wide = jnp.dot(
            weight[group % 2].reshape(width, 4 * HEAD),
            spread[...],
            preferred_element_type=jnp.float32,
        ).astype(low)
        if group < 2:
            load_group(group + 2).start()
        proj = jnp.dot(normed[...], wide, preferred_element_type=jnp.float32)
        for head in range(4):
            part = proj[:, head * WIDE : (head + 1) * WIDE]
            if group < 3:
                part = part * cos_tab[...] + pltpu.roll(part, WIDE // 2, 1) * sin_tab[...]
            part = part.astype(low).reshape(rows // RUN, RUN, WIDE)
            if group < 2:
                q_heads[4 * group + head] = part
            else:
                kv_heads[head, group - 2] = part

    sibling = (row, spot, 1 - core)
    outgoing = []
    for step in range(4):
        slot = lax.rem(spot + step, 4)
        chip = 4 * core + slot
        for other in range(2):
            is_self = jnp.logical_and(chip == spot, core == other)
            device = (row, chip, other)
            outgoing.append(
                (
                    (
                        kv_heads.at[slot, :, other],
                        kv_slots.at[spot, :, other],
                        send_kv.at[step, other],
                        recv_kv.at[spot],
                        device,
                    ),
                    is_self,
                )
            )
            outgoing.append(
                (
                    (
                        q_heads.at[2 * slot + other],
                        q_slots.at[spot],
                        send_q.at[step, other],
                        recv_q.at[spot],
                        device,
                    ),
                    is_self,
                )
            )
    for parts, is_self in outgoing:
        move(*parts, is_self)
    far_gathers[0].pass_on(2)
    far_gathers[0].pass_on(3)
    for k in range(4):
        far_gathers[0].diagonal(k)

    def hand_on(source):
        block = kv_slots.at[source, :, core]
        return remote(block, block, send_x.at[source], recv_x.at[source], sibling)

    for step in range(8):
        source = lax.rem(spot + step, 8)
        block = kv_slots.at[source, :, core]
        remote(block, block, send_x.at[source], recv_kv.at[source], sibling).wait_recv()
        hand_on(source).start()
    far_gathers[1].open_z()
    far_gathers[1].open_xy()
    for step in range(8):
        remote(
            q_slots.at[step], q_slots.at[step], send_x.at[step], recv_q.at[step], sibling
        ).wait_recv()
        hand_on(step).wait()
    save_q = pltpu.make_async_copy(q_slots, q_out, saves.at[1])
    save_q.start()
    save_kv = pltpu.make_async_copy(kv_slots, kv_out, saves.at[2])
    save_kv.start()

    pltpu.make_async_copy(ids_all, ids, load_ids).wait()
    runs = length // RUN
    per_device = rows // RUN

    def find_run(index, carry):
        device, part = 0, 0
        for run in range(runs):
            here = ids[run // per_device, 0, run % per_device] == index
            device = jnp.where(here, run // per_device, device)
            part = jnp.where(here, run % per_device, part)
        order[index, 0] = device
        order[index, 1] = part
        return carry

    lax.fori_loop(0, runs, find_run, 0)

    def sort_run(index, carry):
        device, part = order[index, 0], order[index, 1]
        cols = tile_at(index, RUN)
        q_t[:, cols] = q_slots[device, part].T
        keys[cols] = kv_slots[device, 0, part]
        v_t[:, cols] = kv_slots[device, 1, part].T
        return carry

    lax.fori_loop(0, runs, sort_run, 0)
    scale = HEAD ** (-0.5) * LOG2_E
    tiles = length // TILE

    def query_tile(index, carry):
        cols = tile_at(index, TILE)
        queries = q_t[:, cols]

        def step(scores, block, peak, total, mix):
            high = jnp.maximum(peak, jnp.max(scores, axis=0, keepdims=True))
            decay = jnp.exp2(peak - high)
            weights = jnp.exp2(scores - high)
            total = total * decay + jnp.sum(weights, axis=0, keepdims=True)
            mix = mix * decay + jnp.dot(
                v_t[:, tile_at(block, TILE)],
                weights.astype(low),
                preferred_element_type=jnp.float32,
            )
            return high, total, mix

        def scores_of(block):
            return (
                jnp.dot(keys[tile_at(block, TILE)], queries, preferred_element_type=jnp.float32)
                * scale
            )

        state = (
            jnp.full((1, TILE), masked_value, jnp.float32),
            jnp.zeros((1, TILE), jnp.float32),
            jnp.zeros((WIDE, TILE), jnp.float32),
        )
        state = step(causal(scores_of(index)), index, *state)
        peak, total, mix = lax.fori_loop(
            0, index, lambda block, now: step(scores_of(block), block, *now), state
        )
        mix = mix / total
        mixed_t[:, cols] = mix
        lse[:, cols] = peak + jnp.log2(total)
        for half in range(TILE // RUN):
            mixed[index * (TILE // RUN) + half] = mix[:, half * RUN : (half + 1) * RUN].T.astype(low)

        for k in range(1, 4):

            @pl.when(index == k + 3)
            def _():
                far_gathers[1].pass_on(k)

        return carry

    lax.fori_loop(0, tiles, query_tile, 0)
    save_mixed = pltpu.make_async_copy(mixed_t, mixed_t_out, saves.at[3])
    save_mixed.start()
    save_lse = pltpu.make_async_copy(lse, lse_out, saves.at[4])
    save_lse.start()

    def unsort_run(run, carry):
        index = ids[run // per_device, 0, run % per_device]
        mixed_slots[run // per_device, run % per_device] = mixed[index]
        return carry

    lax.fori_loop(0, runs, unsort_run, 0)
    copies = return_copies(mixed_slots, mixed_heads, send_m, recv_m)
    start_return(copies)
    far_gathers[2].open_z()
    far_gathers[2].open_xy()
    for k in range(4):
        far_gathers[1].diagonal(k)
    for k in range(1, 4):
        far_gathers[2].pass_on(k)
        far_gathers[2].diagonal(k - 1)
    far_gathers[2].diagonal(3)
    finish_return(copies, mixed_heads, send_m, recv_m)
    for gather in far_gathers:
        gather.finish()
    for gather in [near_gather] + far_gathers:
        gather.close()
    for parts, is_self in outgoing:

        @pl.when(jnp.logical_not(is_self))
        def _():
            remote(*parts).wait_send()

    for copy in ids_copies:
        copy.wait_send()
    for copy in (save_normed, save_q, save_kv, save_mixed, save_lse):
        copy.wait()


def forward(tokens, ids, near_own, far_own, spread, cos_tab, sin_tab):
    dma = pltpu.SemaphoreType.DMA
    vmem = pltpu.VMEM
    low, full = jnp.bfloat16, jnp.float32
    rows, width = tokens.shape
    share = near_own.shape[0]
    length = 8 * rows
    heads = (8, rows // RUN, RUN, WIDE)
    both = (2, rows // RUN, RUN, WIDE)
    return pl.pallas_call(
        forward_kernel,
        in_specs=[vmem_spec(), vmem_spec(), any_spec(), any_spec()] + [vmem_spec()] * 3,
        out_specs=[any_spec()] * 8,
        out_shape=[
            jax.ShapeDtypeStruct((2, 4, 2, share, near_own.shape[1]), low),
            jax.ShapeDtypeStruct((2, 4, 2, share, far_own.shape[1]), low),
            jax.ShapeDtypeStruct((rows, width), low),
            jax.ShapeDtypeStruct(heads, low),
            jax.ShapeDtypeStruct((8,) + both, low),
            jax.ShapeDtypeStruct(heads, low),
            jax.ShapeDtypeStruct((WIDE, length), full),
            jax.ShapeDtypeStruct((1, length), full),
        ],
        scratch_shapes=[
            vmem((rows, width), full),
            vmem((rows, width), low),
            vmem((2, 2, 4, 2, share, 4 * HEAD), low),
            vmem((2, 4, 2, share, WIDE), low),
            vmem(heads, low),
            vmem((4,) + both, low),
            vmem(heads, low),
            vmem((8,) + both, low),
            vmem((WIDE, length), low),
            vmem((length, WIDE), low),
            vmem((WIDE, length), low),
            vmem((WIDE, length), full),
            vmem((1, length), full),
            vmem((length // RUN, RUN, WIDE), low),
            vmem(heads, low),
            vmem((8, 8, WIDE), jnp.int32),
            pltpu.SMEM((8, 8, WIDE), jnp.int32),
            pltpu.SMEM((length // RUN, 2), jnp.int32),
            dma((8,)),
            dma((8,)),
            dma(()),
            dma((2,)),
            dma(()),
            dma((5,)),
            dma((4, 2)),
            dma((8,)),
            dma((4, 2)),
            dma((8,)),
            dma((8,)),
            dma((8,)),
            dma((8,)),
            dma((8,)),
        ]
        + gather_sems(4),
        compiler_params=pltpu.CompilerParams(
            collective_id=1, has_side_effects=True, vmem_limit_bytes=VMEM_LIMIT
        ),
        name="forward",
    )(tokens, ids, near_own, far_own, spread, cos_tab, sin_tab)


def attend_back_kernel(
    order, q_in, kv_in, d_in, mixed_t, lse, dq, dkv, q, q_t, k, k_t, v, d, d_t, delta, dq_t, dk, dv
):
    runs = q_in.shape[0] // RUN
    tiles = q_in.shape[0] // TILE

    def sort_run(index, carry):
        run = order[index]
        cols = tile_at(index, RUN)
        q_run = q_in[tile_at(run, RUN)]
        k_run = kv_in[run // 2, 0, tile_at(run % 2, RUN)]
        d_run = d_in[tile_at(run, RUN)]
        d_turned = d_run.T
        q[cols] = q_run
        q_t[:, cols] = q_run.T
        k[cols] = k_run
        k_t[:, cols] = k_run.T
        v[cols] = kv_in[run // 2, 1, tile_at(run % 2, RUN)]
        d[cols] = d_run
        d_t[:, cols] = d_turned
        delta[:, cols] = jnp.sum(
            d_turned.astype(jnp.float32) * mixed_t[:, cols], axis=0, keepdims=True
        )
        return carry

    lax.fori_loop(0, runs, sort_run, 0)
    scale = HEAD ** (-0.5)
    dq_t[...] = jnp.zeros_like(dq_t)

    def key_tile(block, carry):
        rows = tile_at(block, TILE)
        keys, keys_t, values = k[rows], k_t[:, rows], v[rows]
        dk[...] = jnp.zeros_like(dk)
        dv[...] = jnp.zeros_like(dv)

        def query_tile(index, diagonal):
            cols = tile_at(index, TILE)
            scores = jnp.dot(keys, q_t[:, cols], preferred_element_type=jnp.float32) * (
                scale * LOG2_E
            )
            if diagonal:
                scores = causal(scores)
            probs = jnp.exp2(scores - lse[:, cols])
            dv[...] += jnp.dot(
                probs.astype(jnp.bfloat16), d[cols], preferred_element_type=jnp.float32
            )
            grad_probs = jnp.dot(values, d_t[:, cols], preferred_element_type=jnp.float32)
            grad_scores = (probs * (grad_probs - delta[:, cols])).astype(jnp.bfloat16)
            dk[...] += jnp.dot(grad_scores, q[cols], preferred_element_type=jnp.float32)
            dq_t[:, cols] += jnp.dot(keys_t, grad_scores, preferred_element_type=jnp.float32)

        query_tile(block, True)

        def later(index, inner):
            query_tile(index, False)
            return inner

        lax.fori_loop(block + 1, tiles, later, 0)
        for half in range(TILE // RUN):
            run = order[block * (TILE // RUN) + half]
            cut = pl.ds(half * RUN, RUN)
            dkv[0, tile_at(run, RUN)] = (dk[cut] * scale).astype(jnp.bfloat16)
            dkv[1, tile_at(run, RUN)] = dv[cut].astype(jnp.bfloat16)
        return carry

    lax.fori_loop(0, tiles, key_tile, 0)

    def unsort_run(index, carry):
        run = order[index]
        dq[tile_at(run, RUN)] = (dq_t[:, tile_at(index, RUN)] * scale).T.astype(jnp.bfloat16)
        return carry

    lax.fori_loop(0, runs, unsort_run, 0)


def attend_back(order, q_all, kv_all, d_all, mixed_t, lse):
    length = q_all.shape[0]
    low = jnp.bfloat16
    tall = pltpu.VMEM((length, WIDE), low)
    flat = pltpu.VMEM((WIDE, length), low)
    return pl.pallas_call(
        attend_back_kernel,
        in_specs=[pl.BlockSpec(memory_space=pltpu.SMEM)] + [vmem_spec()] * 5,
        out_specs=[vmem_spec()] * 2,
        out_shape=[
            jax.ShapeDtypeStruct((length, WIDE), low),
            jax.ShapeDtypeStruct((2, length, WIDE), low),
        ],
        scratch_shapes=[
            tall,
            flat,
            tall,
            flat,
            tall,
            tall,
            flat,
            pltpu.VMEM((1, length), jnp.float32),
            pltpu.VMEM((WIDE, length), jnp.float32),
            pltpu.VMEM((TILE, WIDE), jnp.float32),
            pltpu.VMEM((TILE, WIDE), jnp.float32),
        ],
        compiler_params=pltpu.CompilerParams(vmem_limit_bytes=VMEM_LIMIT),
        cost_estimate=pl.CostEstimate(
            flops=5 * length * length * WIDE, bytes_accessed=20 * length * WIDE, transcendentals=0
        ),
        name="attend_back",
    )(order, q_all, kv_all, d_all, mixed_t, lse)


PIECE = 256


def reduce_kernel(
    n,
    tail,
    lefts,
    groups,
    right,
    gains,
    own,
    left_t,
    staged,
    send_one,
    recv_one,
    send_two,
    recv_two,
    kept,
    recv_three,
    load,
    ss_one,
    rs_one,
    ss_two,
    rs_two,
    ss_three,
    rs_three,
):
    row, level, column, beside_x, beside_y, along_z = neighbours()
    share = own.shape[0]
    quarter = 4 * share

    def load_left(index):
        copy = pltpu.make_async_copy(lefts[index], staged, load)
        copy.start()
        copy.wait()
        for part in range(4):
            turned = staged[:, part * quarter : (part + 1) * quarter].T
            for inner in range(4):
                x, z, y = part // 2, 2 * (part % 2) + inner // 2, inner % 2
                left_t[index, x, y, z * share : (z + 1) * share] = turned[
                    inner * share : (inner + 1) * share
                ]

    load_left(0)
    greet([beside_x, beside_y] + along_z)

    def group_of(step):
        found = 0
        for start in groups[1:]:
            found = found + jnp.where(step >= start, 1, 0)
        return found

    def columns(step, kind):
        return pl.ds(pl.multiple_of(step * 2 * PIECE + kind * PIECE, PIECE), PIECE)

    def product(step, kind, x, y):
        term = jnp.dot(
            left_t[group_of(step), x, y],
            right[:, columns(step, kind)],
            preferred_element_type=jnp.float32,
        )
        if kind == 1:
            at_gains = jnp.where(step == n - 1, 1.0, 0.0)
            term = term * (1.0 - at_gains) + gains[x, y].astype(jnp.float32) * at_gains
        return term

    def first_copy(step, kind):
        slot = lax.rem(step, 2)
        return remote(
            send_one.at[slot, kind],
            recv_one.at[step, kind],
            ss_one.at[slot, kind],
            rs_one.at[step, kind],
            beside_x if kind == 0 else beside_y,
        )

    def second_copy(step, kind):
        slot = lax.rem(step, 2)
        return remote(
            send_two.at[slot, kind],
            recv_two.at[step, kind],
            ss_two.at[slot, kind],
            rs_two.at[step, kind],
            beside_y if kind == 0 else beside_x,
        )

    def third_copy(step, kind, k):
        target = lax.rem(level + k + 1, 4)
        slot = lax.rem(step, 3)
        return remote(
            kept.at[slot, kind, pl.ds(pl.multiple_of(target * share, share), share)],
            recv_three.at[step, kind, k],
            ss_three.at[slot, kind, k],
            rs_three.at[step, kind, k],
            along_z[k],
        )

    def first(step):
        slot = lax.rem(step, 2)
        for half in range(2):
            send_one[slot, 0, half] = product(step, 0, 1 - row, half).astype(jnp.bfloat16)
        first_copy(step, 0).start()
        for half in range(2):
            send_one[slot, 1, half] = product(step, 1, half, 1 - column).astype(jnp.bfloat16)
        first_copy(step, 1).start()

    def second(step):
        slot = lax.rem(step, 2)
        keep = lax.rem(step, 3)
        first_copy(step, 0).wait()
        away = product(step, 0, row, 1 - column) + recv_one[step, 0, 1 - column].astype(jnp.float32)
        send_two[slot, 0] = away.astype(jnp.bfloat16)
        second_copy(step, 0).start()
        here = product(step, 0, row, column) + recv_one[step, 0, column].astype(jnp.float32)
        kept[keep, 0] = here.astype(jnp.bfloat16)
        first_copy(step, 1).wait()
        away = product(step, 1, 1 - row, column) + recv_one[step, 1, 1 - row].astype(jnp.float32)
        send_two[slot, 1] = away.astype(jnp.bfloat16)
        second_copy(step, 1).start()
        here = product(step, 1, row, column) + recv_one[step, 1, row].astype(jnp.float32)
        kept[keep, 1] = here.astype(jnp.bfloat16)

    def third(step):
        keep = lax.rem(step, 3)
        for kind in range(2):
            second_copy(step, kind).wait()
            here = kept[keep, kind].astype(jnp.float32) + recv_two[step, kind].astype(jnp.float32)
            kept[keep, kind] = here.astype(jnp.bfloat16)
            for k in range(3):
                third_copy(step, kind, k).start()

    def last(step):
        keep = lax.rem(step, 3)
        for kind in range(2):
            total = kept[keep, kind, pl.ds(pl.multiple_of(level * share, share), share)].astype(
                jnp.float32
            )
            for k in range(3):
                third_copy(step, kind, k).wait()
                total = total + recv_three[step, kind, k].astype(jnp.float32)
            own[:, columns(step, kind)] = total

    def turn(step, carry):
        @pl.when(step < n)
        def _():
            first(step)

        for index in range(1, len(lefts)):

            @pl.when(step == index - 1)
            def _():
                load_left(index)

        @pl.when(jnp.logical_and(step >= 1, step < n + 1))
        def _():
            second(step - 1)

        @pl.when(jnp.logical_and(step >= 2, step < n + 2))
        def _():
            third(step - 2)

        @pl.when(step >= 3)
        def _():
            last(step - 3)

        return carry

    lax.fori_loop(0, n + 3, turn, 0)


def reduce_products(lefts, groups, right, gains, collective_id):
    dma = pltpu.SemaphoreType.DMA
    low = jnp.bfloat16
    rows, width = lefts[0].shape
    n = right.shape[1] // (2 * PIECE)
    share = width // 16
    count = len(lefts)

    def kernel(*refs):
        reduce_kernel(n, None, refs[:count], groups, *refs[count:])

    return pl.pallas_call(
        kernel,
        in_specs=[any_spec()] * count + [vmem_spec()] * 2,
        out_specs=vmem_spec(),
        out_shape=jax.ShapeDtypeStruct((share, right.shape[1]), jnp.float32),
        scratch_shapes=[
            pltpu.VMEM((count, 2, 2, 4 * share, rows), low),
            pltpu.VMEM((rows, width), low),
            pltpu.VMEM((2, 2, 2, 4 * share, PIECE), low),
            pltpu.VMEM((n, 2, 2, 4 * share, PIECE), low),
            pltpu.VMEM((2, 2, 4 * share, PIECE), low),
            pltpu.VMEM((n, 2, 4 * share, PIECE), low),
            pltpu.VMEM((3, 2, 4 * share, PIECE), low),
            pltpu.VMEM((n, 2, 3, share, PIECE), low),
            dma(()),
            dma((2, 2)),
            dma((n, 2)),
            dma((2, 2)),
            dma((n, 2)),
            dma((3, 2, 3)),
            dma((n, 2, 3)),
        ],
        compiler_params=pltpu.CompilerParams(
            collective_id=collective_id, has_side_effects=True, vmem_limit_bytes=61 * 1024 * 1024
        ),
        name="reduce_products",
    )(*lefts, right, gains)


def dot_f32(left, right):
    return jnp.dot(left, right, preferred_element_type=jnp.float32)


def by_heads(
    tokens,
    positions,
    gain_one,
    gain_two,
    w_query,
    w_key,
    w_value,
    w_out,
    w_gate,
    w_up,
    w_down,
    cotangent,
):
    low = jnp.bfloat16
    rows, _, width = tokens.shape
    share = gain_one.shape[0]
    hidden_width = w_gate.shape[1]
    length = rows * 8

    run_ids = positions[::RUN, 0] // RUN
    extra = jnp.zeros((share, WIDE), low)
    extra = extra.at[:, 0].set(gain_one).at[:, 1].set(gain_two)
    extra = extra.at[: rows // RUN, 2].set(run_ids.astype(low))
    spread = spread_matrix(8)
    cos_tab, sin_tab = lane_tables(positions[:, 0])
    near, far, normed, q_all, kv_all, mixed_heads, mixed_t, lse = forward(
        tokens.reshape(rows, width),
        jnp.broadcast_to(jnp.pad(run_ids, (0, WIDE - rows // RUN)), (8, WIDE)),
        jnp.concatenate([w_query, w_key, w_value, w_out.T, extra], axis=1),
        jnp.concatenate([w_gate, w_up, w_down.T], axis=1),
        spread[: 4 * HEAD, : 4 * WIDE],
        cos_tab,
        sin_tab,
    )
    near = near.reshape(width, near.shape[-1])
    far = far.reshape(width, far.shape[-1])
    qkv_width = w_query.shape[1] + w_key.shape[1] + w_value.shape[1]
    out_width = w_out.shape[0]
    qkv_mat = near[:, :qkv_width]
    out_mat_t = near[:, qkv_width : qkv_width + out_width]
    extras = near[:, qkv_width + out_width :]
    full_one, full_two = extras[:, 0], extras[:, 1]
    row = lax.axis_index("dp")
    ids = lax.dynamic_slice_in_dim(extras[:, 2].reshape(2, 8, share), row, 1, 0)[0, :, : rows // RUN]
    ids = ids.reshape(-1).astype(jnp.int32)
    count = ids.shape[0]
    order = jnp.sum(
        jnp.where(ids[None, :] == jnp.arange(count)[:, None], jnp.arange(count)[None, :], 0), axis=1
    ).astype(jnp.int32)
    gate_mat = far[:, :hidden_width]
    up_mat = far[:, hidden_width : 2 * hidden_width]
    down_mat_t = far[:, 2 * hidden_width :]

    flat_in = tokens.astype(jnp.float32).reshape(rows, width)
    unit_one, inverse_one, _ = norm_forward(flat_in, full_one)
    q_all = q_all.reshape(length, WIDE)
    kv_all = kv_all.reshape(8, 2, rows, WIDE)
    mixed_heads = mixed_heads.reshape(8, rows, WIDE)

    def narrow(heads):
        count = heads.shape[0]
        side = jnp.transpose(heads, (1, 0, 2)).reshape(rows, count * WIDE)
        return contract_cols(side, spread[: count * HEAD, : count * WIDE]).astype(low)

    mixed_low = narrow(mixed_heads)
    middle = flat_in + pair_sum(contract_cols(mixed_low, out_mat_t).astype(low), 5)
    unit_two, inverse_two, second = norm_forward(middle, full_two)
    gate_vals = dot_f32(second, gate_mat)
    up_vals = dot_f32(second, up_mat)
    sigmoid_vals = jax.nn.sigmoid(gate_vals)
    silu_vals = gate_vals * sigmoid_vals
    hidden = (silu_vals * up_vals).astype(low)
    mlp_part = pair_sum(contract_cols(hidden, down_mat_t).astype(low), 6)
    layer_out = (middle + mlp_part).astype(low).reshape(rows, 1, width)

    grad_low = cotangent.reshape(rows, width)
    grad_hidden = dot_f32(grad_low, down_mat_t)
    grad_gate_low = (
        grad_hidden * up_vals * sigmoid_vals * (1.0 + gate_vals * (1.0 - sigmoid_vals))
    ).astype(low)
    grad_up_low = (grad_hidden * silu_vals).astype(low)
    grad_second = pair_sum(
        (contract_cols(grad_gate_low, gate_mat) + contract_cols(grad_up_low, up_mat)).astype(low), 7
    )
    grad_mid_norm, grad_gain_two = norm_backward(grad_second, unit_two, inverse_two, full_two)
    grad_middle = grad_low.astype(jnp.float32) + grad_mid_norm
    grad_mid_low = grad_middle.astype(low)
    grad_mixed = dot_f32(grad_mid_low, out_mat_t).astype(low)
    grad_heads = jnp.transpose(
        dot_f32(grad_mixed, spread).astype(low).reshape(rows, 8, WIDE), (1, 0, 2)
    )
    d_all = grads_to_heads(grad_heads).reshape(length, WIDE)
    dq, dkv = attend_back(order, q_all, kv_all, d_all, mixed_t, lse)
    dq_own, dkv_own = grads_to_tokens(
        dq.reshape(8, rows, WIDE), dkv.reshape(2, 8, rows, WIDE)
    )

    def unturn(heads):
        part = heads.astype(jnp.float32)
        return (part * cos_tab - jnp.roll(part, WIDE // 2, axis=-1) * sin_tab).astype(low)

    grad_qkv_low = jnp.concatenate(
        [narrow(unturn(dq_own)), narrow(unturn(dkv_own[:, 0])), narrow(dkv_own[:, 1])], axis=1
    )
    grad_normed = pair_sum(contract_cols(grad_qkv_low, qkv_mat).astype(low), 8)
    grad_in_norm, grad_gain_one = norm_backward(grad_normed, unit_one, inverse_one, full_one)
    input_grad = (grad_middle + grad_in_norm).reshape(rows, 1, width)
    gains = jnp.stack([grad_gain_one, grad_gain_two], axis=1)
    gains_high = gains.astype(low)
    gains_low = (gains - gains_high.astype(jnp.float32)).astype(low)
    gains = jnp.concatenate([gains_high, gains_low], axis=1)
    gains = jnp.pad(gains, ((0, 0), (0, PIECE - gains.shape[1])))
    gains = jnp.transpose(gains.reshape(2, 4, 2, share, PIECE), (0, 2, 1, 3, 4))
    right = jnp.concatenate(
        [
            grad_gate_low,
            grad_up_low,
            hidden,
            grad_qkv_low,
            mixed_low,
            jnp.zeros((rows, PIECE), low),
        ],
        axis=1,
    )
    steps = hidden_width // (2 * PIECE)
    near_steps = qkv_width // (2 * PIECE)
    grads = reduce_products(
        (second, grad_low, normed, grad_mid_low),
        (0, 2 * steps, 3 * steps, 3 * steps + near_steps),
        right,
        gains.reshape(2, 2, 4 * share, PIECE),
        10,
    )
    far_own = grads[:, : 3 * hidden_width]
    near_own = grads[:, 3 * hidden_width :]
    gain_own = near_own[:, qkv_width + out_width :]
    q_width, k_width = w_query.shape[1], w_key.shape[1]
    return (
        layer_out,
        input_grad,
        gain_own[:, 0] + gain_own[:, 2],
        gain_own[:, 1] + gain_own[:, 3],
        near_own[:, :q_width],
        near_own[:, q_width : q_width + k_width],
        near_own[:, q_width + k_width : qkv_width],
        near_own[:, qkv_width : qkv_width + out_width].T,
        far_own[:, :hidden_width],
        far_own[:, hidden_width : 2 * hidden_width],
        far_own[:, 2 * hidden_width :].T,
    )


def solution(mesh):
    sizes = (mesh.shape["dp"], mesh.shape["context"], mesh.shape["tensor"])
    return jax.shard_map(
        by_heads if sizes == (2, 8, 2) else on_device,
        mesh=mesh,
        in_specs=(
            P("context", "dp", None),
            P("context", "dp"),
            P(("dp", "context")),
            P(("dp", "context")),
            P(("dp", "context"), "tensor"),
            P(("dp", "context"), "tensor"),
            P(("dp", "context"), "tensor"),
            P("tensor", ("dp", "context")),
            P(("dp", "context"), "tensor"),
            P(("dp", "context"), "tensor"),
            P("tensor", ("dp", "context")),
            P("context", "dp", None),
        ),
        out_specs=(
            P("context", "dp", None),
            P("context", "dp", None),
            P(("dp", "context")),
            P(("dp", "context")),
            P(("dp", "context"), "tensor"),
            P(("dp", "context"), "tensor"),
            P(("dp", "context"), "tensor"),
            P("tensor", ("dp", "context")),
            P(("dp", "context"), "tensor"),
            P(("dp", "context"), "tensor"),
            P("tensor", ("dp", "context")),
        ),
        check_vma=False,
    )
```

```python
import functools

import jax
import jax.numpy as jnp
from jax import lax
from jax.experimental import pallas as pl
from jax.experimental.pallas import tpu as pltpu
from jax.sharding import PartitionSpec as P

HEAD = 96


epsilon = 1e-05
theta_base = 100000.0
masked_value = -1e30


def norm_forward(values_in, gain_vec):
    inverse = lax.rsqrt(jnp.mean(values_in * values_in, axis=-1, keepdims=True) + epsilon)
    unit_vals = values_in * inverse
    return (unit_vals, inverse, (unit_vals * gain_vec.astype(jnp.float32)).astype(jnp.bfloat16))


def norm_backward(grad_in, unit_vals, inverse, gain_vec):
    scaled = grad_in * gain_vec.astype(jnp.float32)
    grad_vals = inverse * (
        scaled - unit_vals * jnp.mean(scaled * unit_vals, axis=-1, keepdims=True)
    )
    return (grad_vals, jnp.sum(grad_in * unit_vals, axis=0))


def rotate(values_in, cos_part, sin_part):
    half_size = values_in.shape[-1] // 2
    front_half = values_in[..., :half_size]
    back_half = values_in[..., half_size:]
    return jnp.concatenate(
        [
            front_half * cos_part - back_half * sin_part,
            back_half * cos_part + front_half * sin_part,
        ],
        axis=-1,
    )


def contract_rows(left_mat, right_mat):
    return lax.dot_general(
        left_mat, right_mat, (((0,), (0,)), ((), ())), preferred_element_type=jnp.float32
    )


def contract_cols(left_mat, right_mat):
    return lax.dot_general(
        left_mat, right_mat, (((1,), (1,)), ((), ())), preferred_element_type=jnp.float32
    )


def on_device(
    tokens,
    positions,
    gain_one,
    gain_two,
    w_query,
    w_key,
    w_value,
    w_out,
    w_gate,
    w_up,
    w_down,
    cotangent,
):
    slot_count, seq_count, model_width = tokens.shape
    row_count = slot_count * seq_count
    gathered = (
        lax.all_gather(gain_one, ("dp", "context"), axis=0, tiled=True),
        lax.all_gather(gain_two, ("dp", "context"), axis=0, tiled=True),
        lax.all_gather(w_query, ("dp", "context"), axis=0, tiled=True),
        lax.all_gather(w_key, ("dp", "context"), axis=0, tiled=True),
        lax.all_gather(w_value, ("dp", "context"), axis=0, tiled=True),
        lax.all_gather(w_out, ("dp", "context"), axis=1, tiled=True),
        lax.all_gather(w_gate, ("dp", "context"), axis=0, tiled=True),
        lax.all_gather(w_up, ("dp", "context"), axis=0, tiled=True),
        lax.all_gather(w_down, ("dp", "context"), axis=1, tiled=True),
    )
    full_one, full_two, query_mat, key_mat, value_mat, out_mat, gate_mat, up_mat, down_mat = (
        gathered
    )
    heads_kv = key_mat.shape[1] // HEAD
    heads_q = query_mat.shape[1] // HEAD
    group_size = heads_q // heads_kv
    score_scale = HEAD ** (-0.5)
    half_size = HEAD // 2
    inv_freqs = theta_base ** (-2.0 * jnp.arange(half_size, dtype=jnp.float32) / HEAD)
    angles = positions.astype(jnp.float32)[:, :, None] * inv_freqs
    cos_part = jnp.cos(angles)[:, :, None, :]
    sin_part = jnp.sin(angles)[:, :, None, :]
    flat_in = tokens.astype(jnp.float32).reshape(row_count, model_width)
    unit_one, inverse_one, normed = norm_forward(flat_in, full_one)
    query_proj = jnp.dot(normed, query_mat, preferred_element_type=jnp.float32).reshape(
        slot_count, seq_count, heads_q, HEAD
    )
    key_proj = jnp.dot(normed, key_mat, preferred_element_type=jnp.float32).reshape(
        slot_count, seq_count, heads_kv, HEAD
    )
    value_low = (
        jnp.dot(normed, value_mat, preferred_element_type=jnp.float32)
        .astype(jnp.bfloat16)
        .reshape(slot_count, seq_count, heads_kv * HEAD)
    )
    queries = rotate(query_proj, cos_part, sin_part).astype(jnp.bfloat16)
    keys_low = (
        rotate(key_proj, cos_part, sin_part)
        .astype(jnp.bfloat16)
        .reshape(slot_count, seq_count, heads_kv * HEAD)
    )
    query_seq = jnp.transpose(
        queries.reshape(slot_count, seq_count, heads_kv, group_size, HEAD), (1, 2, 3, 0, 4)
    )
    query_pos = positions.T
    stat_shape = (seq_count, heads_kv, group_size, slot_count)
    initial = (
        jnp.full(stat_shape, masked_value, jnp.float32),
        jnp.zeros(stat_shape, jnp.float32),
        jnp.zeros(stat_shape + (HEAD,), jnp.float32),
    )
    key_piece = lax.all_gather(keys_low, "context", axis=0, tiled=True)
    value_piece = lax.all_gather(value_low, "context", axis=0, tiled=True)
    pos_piece = lax.all_gather(positions, "context", axis=0, tiled=True)
    piece_len = key_piece.shape[0]
    key_seq = jnp.transpose(key_piece.reshape(piece_len, seq_count, heads_kv, HEAD), (1, 2, 0, 3))
    value_seq = jnp.transpose(
        value_piece.reshape(piece_len, seq_count, heads_kv, HEAD), (1, 2, 0, 3)
    )
    pos_seq = pos_piece.T

    def per_sequence(seq_items):
        peak_val, totals, accum_vals, query_one, qpos_one, key_one, value_one, kpos_one = seq_items
        raw_scores = (
            jnp.einsum("hgqd,hkd->hgqk", query_one, key_one, preferred_element_type=jnp.float32)
            * score_scale
        )
        allowed = kpos_one[None, None, None, :] <= qpos_one[None, None, :, None]
        masked = jnp.where(allowed, raw_scores, masked_value)
        new_peak = jnp.maximum(peak_val, jnp.max(masked, axis=-1))
        decay_vals = jnp.exp(peak_val - new_peak)
        weights = jnp.where(allowed, jnp.exp(masked - new_peak[..., None]), 0.0)
        totals = totals * decay_vals + jnp.sum(weights, axis=-1)
        accum_vals = accum_vals * decay_vals[..., None] + jnp.einsum(
            "hgqk,hkd->hgqd",
            weights.astype(jnp.bfloat16),
            value_one,
            preferred_element_type=jnp.float32,
        )
        return (new_peak, totals, accum_vals)

    peak_val, totals, accum_vals = lax.map(
        per_sequence,
        (initial[0], initial[1], initial[2], query_seq, query_pos, key_seq, value_seq, pos_seq),
    )
    log_total = peak_val + jnp.log(totals)
    mixed_seq = accum_vals / totals[..., None]
    mixed_low = (
        jnp.transpose(mixed_seq, (3, 0, 1, 2, 4))
        .reshape(row_count, heads_q * HEAD)
        .astype(jnp.bfloat16)
    )
    branch = lax.psum(
        jnp.dot(mixed_low, out_mat, preferred_element_type=jnp.float32).astype(jnp.bfloat16),
        "tensor",
    ).astype(jnp.float32)
    middle = flat_in + branch
    unit_two, inverse_two, second = norm_forward(middle, full_two)
    gate_vals = jnp.dot(second, gate_mat, preferred_element_type=jnp.float32)
    up_vals = jnp.dot(second, up_mat, preferred_element_type=jnp.float32)
    sigmoid_vals = jax.nn.sigmoid(gate_vals)
    silu_vals = gate_vals * sigmoid_vals
    hidden = (silu_vals * up_vals).astype(jnp.bfloat16)
    mlp_part = lax.psum(
        jnp.dot(hidden, down_mat, preferred_element_type=jnp.float32).astype(jnp.bfloat16), "tensor"
    ).astype(jnp.float32)
    layer_out = (middle + mlp_part).astype(jnp.bfloat16).reshape(slot_count, seq_count, model_width)
    regathered = (
        lax.all_gather(gain_one, ("dp", "context"), axis=0, tiled=True),
        lax.all_gather(gain_two, ("dp", "context"), axis=0, tiled=True),
        lax.all_gather(w_query, ("dp", "context"), axis=0, tiled=True),
        lax.all_gather(w_key, ("dp", "context"), axis=0, tiled=True),
        lax.all_gather(w_value, ("dp", "context"), axis=0, tiled=True),
        lax.all_gather(w_out, ("dp", "context"), axis=1, tiled=True),
        lax.all_gather(w_gate, ("dp", "context"), axis=0, tiled=True),
        lax.all_gather(w_up, ("dp", "context"), axis=0, tiled=True),
        lax.all_gather(w_down, ("dp", "context"), axis=1, tiled=True),
    )
    full_one, full_two, query_mat, key_mat, value_mat, out_mat, gate_mat, up_mat, down_mat = (
        regathered
    )
    grad_low = cotangent.reshape(row_count, model_width)
    grad_down = contract_rows(hidden, grad_low)
    grad_hidden = contract_cols(grad_low, down_mat)
    grad_gate_low = (
        grad_hidden * up_vals * sigmoid_vals * (1.0 + gate_vals * (1.0 - sigmoid_vals))
    ).astype(jnp.bfloat16)
    grad_up_low = (grad_hidden * silu_vals).astype(jnp.bfloat16)
    grad_gate = contract_rows(second, grad_gate_low)
    grad_up = contract_rows(second, grad_up_low)
    grad_second = lax.psum(
        (contract_cols(grad_gate_low, gate_mat) + contract_cols(grad_up_low, up_mat)).astype(
            jnp.bfloat16
        ),
        "tensor",
    ).astype(jnp.float32)
    grad_mid_norm, grad_gain_two = norm_backward(grad_second, unit_two, inverse_two, full_two)
    grad_middle = grad_low.astype(jnp.float32) + grad_mid_norm
    grad_mid_low = grad_middle.astype(jnp.bfloat16)
    grad_out = contract_rows(mixed_low, grad_mid_low)
    grad_mixed = contract_cols(grad_mid_low, out_mat).astype(jnp.bfloat16)
    grad_mixed_seq = jnp.transpose(
        grad_mixed.reshape(slot_count, seq_count, heads_kv, group_size, HEAD), (1, 2, 3, 0, 4)
    )
    delta_rows = jnp.sum(grad_mixed_seq.astype(jnp.float32) * mixed_seq, axis=-1)
    kv_width = heads_kv * HEAD

    def block_grads(grad_query_acc, key_blk, value_blk, pos_blk):
        block_len = key_blk.shape[0]
        key_seq = jnp.transpose(key_blk.reshape(block_len, seq_count, heads_kv, HEAD), (1, 2, 0, 3))
        value_seq = jnp.transpose(
            value_blk.reshape(block_len, seq_count, heads_kv, HEAD), (1, 2, 0, 3)
        )
        raw_scores = (
            jnp.einsum("shgqd,shkd->shgqk", query_seq, key_seq, preferred_element_type=jnp.float32)
            * score_scale
        )
        allowed = pos_blk.T[:, None, None, None, :] <= query_pos[:, None, None, :, None]
        prob_vals = jnp.where(
            allowed,
            jnp.exp(jnp.where(allowed, raw_scores - log_total[..., None], masked_value)),
            0.0,
        )
        grad_value_blk = jnp.einsum(
            "shgqk,shgqd->kshd",
            prob_vals.astype(jnp.bfloat16),
            grad_mixed_seq,
            preferred_element_type=jnp.float32,
        )
        grad_probs = jnp.einsum(
            "shgqd,shkd->shgqk", grad_mixed_seq, value_seq, preferred_element_type=jnp.float32
        )
        grad_scores = (prob_vals * (grad_probs - delta_rows[..., None])).astype(jnp.bfloat16)
        grad_query_acc = grad_query_acc + jnp.einsum(
            "shgqk,shkd->shgqd", grad_scores, key_seq, preferred_element_type=jnp.float32
        )
        grad_key_blk = jnp.einsum(
            "shgqk,shgqd->kshd", grad_scores, query_seq, preferred_element_type=jnp.float32
        )
        return (
            grad_query_acc,
            grad_key_blk.reshape(block_len, seq_count, kv_width),
            grad_value_blk.reshape(block_len, seq_count, kv_width),
        )

    zero_query = jnp.zeros(stat_shape + (HEAD,), jnp.float32)
    key_all, value_all, pos_all = (
        lax.all_gather(keys_low, "context", axis=0, tiled=True),
        lax.all_gather(value_low, "context", axis=0, tiled=True),
        lax.all_gather(positions, "context", axis=0, tiled=True),
    )
    total_len = key_all.shape[0]
    block_size = min(512, total_len)
    block_count = total_len // block_size

    def key_block(grad_query_acc, block_items):
        key_blk, value_blk, pos_blk = block_items
        grad_query_acc, grad_key_blk, grad_value_blk = block_grads(
            grad_query_acc, key_blk, value_blk, pos_blk
        )
        return (grad_query_acc, (grad_key_blk, grad_value_blk))

    grad_query_acc, (grad_keys_all, grad_values_all) = lax.scan(
        key_block,
        zero_query,
        (
            key_all.reshape(block_count, block_size, seq_count, kv_width),
            value_all.reshape(block_count, block_size, seq_count, kv_width),
            pos_all.reshape(block_count, block_size, seq_count),
        ),
    )
    grad_key_own, grad_value_own = (
        lax.psum_scatter(
            grad_keys_all.reshape(total_len, seq_count, kv_width).astype(jnp.bfloat16),
            "context",
            scatter_dimension=0,
            tiled=True,
        ).astype(jnp.float32),
        lax.psum_scatter(
            grad_values_all.reshape(total_len, seq_count, kv_width).astype(jnp.bfloat16),
            "context",
            scatter_dimension=0,
            tiled=True,
        ).astype(jnp.float32),
    )
    grad_rot_q = jnp.transpose(grad_query_acc * score_scale, (3, 0, 1, 2, 4)).reshape(
        slot_count, seq_count, heads_q, HEAD
    )
    grad_q_low = (
        rotate(grad_rot_q, cos_part, -sin_part)
        .reshape(row_count, heads_q * HEAD)
        .astype(jnp.bfloat16)
    )
    grad_rot_k = (grad_key_own * score_scale).reshape(slot_count, seq_count, heads_kv, HEAD)
    grad_k_low = (
        rotate(grad_rot_k, cos_part, -sin_part).reshape(row_count, kv_width).astype(jnp.bfloat16)
    )
    grad_v_low = grad_value_own.reshape(row_count, kv_width).astype(jnp.bfloat16)
    grad_query = contract_rows(normed, grad_q_low)
    grad_key = contract_rows(normed, grad_k_low)
    grad_value = contract_rows(normed, grad_v_low)
    grad_normed = lax.psum(
        (
            contract_cols(grad_q_low, query_mat)
            + contract_cols(grad_k_low, key_mat)
            + contract_cols(grad_v_low, value_mat)
        ).astype(jnp.bfloat16),
        "tensor",
    ).astype(jnp.float32)
    grad_in_norm, grad_gain_one = norm_backward(grad_normed, unit_one, inverse_one, full_one)
    input_grad = (grad_middle + grad_in_norm).reshape(slot_count, seq_count, model_width)
    reduced = (
        lax.psum_scatter(grad_gain_one, ("dp", "context"), scatter_dimension=0, tiled=True),
        lax.psum_scatter(grad_gain_two, ("dp", "context"), scatter_dimension=0, tiled=True),
        lax.psum_scatter(grad_query, ("dp", "context"), scatter_dimension=0, tiled=True),
        lax.psum_scatter(grad_key, ("dp", "context"), scatter_dimension=0, tiled=True),
        lax.psum_scatter(grad_value, ("dp", "context"), scatter_dimension=0, tiled=True),
        lax.psum_scatter(grad_out, ("dp", "context"), scatter_dimension=1, tiled=True),
        lax.psum_scatter(grad_gate, ("dp", "context"), scatter_dimension=0, tiled=True),
        lax.psum_scatter(grad_up, ("dp", "context"), scatter_dimension=0, tiled=True),
        lax.psum_scatter(grad_down, ("dp", "context"), scatter_dimension=1, tiled=True),
    )
    return (
        layer_out,
        input_grad,
        reduced[0],
        reduced[1],
        reduced[2],
        reduced[3],
        reduced[4],
        reduced[5],
        reduced[6],
        reduced[7],
        reduced[8],
    )


WIDE = 128
RUN = 256
TILE = 512
LOG2_E = 1.4426950408889634
MESH = pl.DeviceIdType.MESH
VMEM_LIMIT = 56 * 1024 * 1024


def any_spec():
    return pl.BlockSpec(memory_space=pl.ANY)


def vmem_spec():
    return pl.BlockSpec(memory_space=pltpu.VMEM)


def place():
    return lax.axis_index("dp"), lax.axis_index("context"), lax.axis_index("tensor")


def greet(devices):
    barrier = pltpu.get_barrier_semaphore()
    for device in devices:
        pl.semaphore_signal(barrier, inc=1, device_id=device, device_id_type=MESH)
    pl.semaphore_wait(barrier, len(devices))


def sequence_others():
    row, spot, core = place()
    return [
        (row, lax.rem(spot + shift, 8), lax.rem(core + flip, 2))
        for shift in range(8)
        for flip in range(2)
        if shift or flip
    ]


def remote(source, target, send, recv, device):
    return pltpu.make_async_remote_copy(
        src_ref=source,
        dst_ref=target,
        send_sem=send,
        recv_sem=recv,
        device_id=device,
        device_id_type=MESH,
    )


def move(source, target, send, recv, device, is_self):
    @pl.when(is_self)
    def _():
        pltpu.make_async_copy(source, target, recv).start()

    @pl.when(jnp.logical_not(is_self))
    def _():
        remote(source, target, send, recv, device).start()


def spread_matrix(heads):
    shape = (heads * HEAD, heads * WIDE)
    rows = lax.broadcasted_iota(jnp.int32, shape, 0)
    cols = lax.broadcasted_iota(jnp.int32, shape, 1)
    dims = rows % HEAD
    target = (rows // HEAD) * WIDE + dims + jnp.where(dims >= HEAD // 2, (WIDE - HEAD) // 2, 0)
    return (cols == target).astype(jnp.bfloat16)


def lane_tables(positions):
    half = HEAD // 2
    inv_freqs = theta_base ** (-2.0 * jnp.arange(half, dtype=jnp.float32) / HEAD)
    gap = jnp.zeros((WIDE // 2 - half,), jnp.float32)
    freqs = jnp.concatenate([inv_freqs, gap, inv_freqs, gap])
    sign = jnp.where(jnp.arange(WIDE) < WIDE // 2, -1.0, 1.0)
    angles = positions.astype(jnp.float32)[:, None] * freqs
    return jnp.cos(angles), jnp.sin(angles) * sign


def return_copies(ref, out, send, recv):
    row, spot, core = place()
    head = 2 * lax.rem(spot, 4) + core
    owner = spot // 4
    copies = []
    for step in range(8):
        chip = lax.rem(spot + step, 8)
        is_self = (owner == core) if step == 0 else False
        parts = (ref.at[chip], out.at[head], send.at[step], recv.at[head], (row, chip, owner))
        copies.append((parts, is_self))
    return copies


def start_return(copies):
    for parts, is_self in copies:
        if is_self is False:
            remote(*parts).start()
        else:
            move(*parts, is_self)


def finish_return(copies, out, send, recv):
    row, spot, core = place()
    for head in range(8):
        remote(
            out.at[head], out.at[head], send.at[0], recv.at[head], (row, spot, 1 - core)
        ).wait_recv()
    for parts, is_self in copies:
        if is_self is False:
            remote(*parts).wait_send()
        else:

            @pl.when(jnp.logical_not(is_self))
            def _():
                remote(*parts).wait_send()


def pair_sum_kernel(part, total, other, send, recv):
    row, spot, core = place()
    sibling = (row, spot, 1 - core)
    greet([sibling])
    pieces = send.shape[0]
    rows = part.shape[0] // pieces

    def piece(index):
        cut = pl.ds(index * rows, rows)
        return remote(part.at[cut], other.at[cut], send.at[index], recv.at[index], sibling)

    for index in range(pieces):
        piece(index).start()
    for index in range(pieces):
        cut = pl.ds(index * rows, rows)
        piece(index).wait()
        total[cut] = part[cut].astype(jnp.float32) + other[cut].astype(jnp.float32)


def pair_sum(part, collective_id):
    dma = pltpu.SemaphoreType.DMA
    return pl.pallas_call(
        pair_sum_kernel,
        in_specs=[vmem_spec()],
        out_specs=vmem_spec(),
        out_shape=jax.ShapeDtypeStruct(part.shape, jnp.float32),
        scratch_shapes=[pltpu.VMEM(part.shape, part.dtype), dma((4,)), dma((4,))],
        compiler_params=pltpu.CompilerParams(
            collective_id=collective_id, has_side_effects=True, vmem_limit_bytes=VMEM_LIMIT
        ),
        name="pair_sum",
    )(part)


def tile_at(index, size):
    return pl.ds(pl.multiple_of(index * size, size), size)


def causal(scores):
    keys = lax.broadcasted_iota(jnp.int32, scores.shape, 0)
    queries = lax.broadcasted_iota(jnp.int32, scores.shape, 1)
    return jnp.where(keys <= queries, scores, masked_value)


def neighbours():
    row, spot, core = place()
    level, column = spot // 2, lax.rem(spot, 2)
    beside_x = (1 - row, spot, core)
    beside_y = (row, 2 * level + 1 - column, core)
    along_z = [(row, 2 * lax.rem(level + k, 4) + column, core) for k in (1, 2, 3)]
    return row, level, column, beside_x, beside_y, along_z


class Gather:
    def __init__(self, own, whole, start, width, piece, sems):
        self.own, self.whole = own.at[:, pl.ds(start, width)], whole
        self.start, self.width = start, width
        self.sems = [sem.at[piece] for sem in sems]

    def block(self, x, z, y, half=None):
        cut = self.width // 2 // WIDE * WIDE
        start, width = self.start, self.width
        if half == 0:
            width = cut
        elif half == 1:
            start, width = start + cut, width - cut
        return self.whole.at[x, z, y, :, pl.ds(start, width)]

    def arrived(self, target, recv_sem):
        device = neighbours()[3]
        remote(target, target, self.sems[0].at[0], recv_sem, device).wait_recv()

    def copies_z(self):
        send_z, recv_z = self.sems[:2]
        row, level, column, beside_x, beside_y, along_z = neighbours()
        mine = self.block(row, level, column)
        return [
            remote(self.own, mine, send_z.at[k], recv_z.at[k], along_z[k]) for k in range(3)
        ]

    def copies_xy(self, k):
        send_x, recv_x, send_y, recv_y = self.sems[2:6]
        row, level, column, beside_x, beside_y, along_z = neighbours()
        block = self.block(row, lax.rem(level + 4 - k, 4), column)
        source = self.own if k == 0 else block
        return [
            remote(source, block, send_x.at[k], recv_x.at[k], beside_x),
            remote(source, block, send_y.at[k], recv_y.at[k], beside_y),
        ]

    def copies_diagonal(self, k):
        send_d, recv_d = self.sems[6:8]
        row, level, column, beside_x, beside_y, along_z = neighbours()
        z = lax.rem(level + 4 - k, 4)
        by_y = self.block(1 - row, z, column, 1)
        by_x = self.block(row, z, 1 - column, 0)
        return [
            remote(by_y, by_y, send_d.at[0, k], recv_d.at[0, k], beside_y),
            remote(by_x, by_x, send_d.at[1, k], recv_d.at[1, k], beside_x),
        ]

    def open_z(self):
        for copy in self.copies_z():
            copy.start()

    def open_xy(self):
        row, level, column, beside_x, beside_y, along_z = neighbours()
        for copy in self.copies_xy(0):
            copy.start()
        pltpu.make_async_copy(self.own, self.block(row, level, column), self.sems[8]).start()

    def pass_on(self, k):
        row, level, column, beside_x, beside_y, along_z = neighbours()
        self.arrived(self.block(row, lax.rem(level + 4 - k, 4), column), self.sems[1].at[k - 1])
        for copy in self.copies_xy(k):
            copy.start()

    def diagonal(self, k):
        recv_x, recv_y = self.sems[3], self.sems[5]
        row, level, column, beside_x, beside_y, along_z = neighbours()
        z = lax.rem(level + 4 - k, 4)
        by_y, by_x = self.copies_diagonal(k)
        self.arrived(self.block(1 - row, z, column), recv_x.at[k])
        by_y.start()
        self.arrived(self.block(row, z, 1 - column), recv_y.at[k])
        by_x.start()

    def finish(self):
        recv_d, local = self.sems[7:]
        row, level, column, beside_x, beside_y, along_z = neighbours()
        for k in range(4):
            z = lax.rem(level + 4 - k, 4)
            self.arrived(self.block(1 - row, z, 1 - column, 1), recv_d.at[0, k])
            self.arrived(self.block(1 - row, z, 1 - column, 0), recv_d.at[1, k])
        mine = self.block(row, level, column)
        pltpu.make_async_copy(self.own, mine, local).wait()

    def close(self):
        for copy in self.copies_z():
            copy.wait_send()
        for k in range(4):
            for copy in self.copies_xy(k) + self.copies_diagonal(k):
                copy.wait_send()


def gather_sems(pieces):
    dma = pltpu.SemaphoreType.DMA
    shapes = [(3,), (3,), (4,), (4,), (4,), (4,), (2, 4), (2, 4), ()]
    return [dma((pieces,) + shape) for shape in shapes]


def forward_kernel(
    tokens,
    ids_in,
    near_own,
    far_own,
    spread,
    cos_tab,
    sin_tab,
    near,
    far,
    normed_out,
    q_out,
    k_out,
    v_out,
    mixed_heads,
    mixed_t_out,
    lse_out,
    unit,
    normed,
    weight,
    extras,
    q_heads,
    kv_heads,
    q_slots,
    kv_slots,
    q,
    q_t,
    keys,
    v,
    v_t,
    mixed_t,
    lse,
    mixed,
    mixed_slots,
    ids_all,
    ids,
    order,
    send_ids,
    recv_ids,
    load_ids,
    load_w,
    load_extra,
    saves,
    send_q,
    recv_q,
    send_kv,
    recv_kv,
    send_x,
    recv_x,
    send_m,
    recv_m,
    *sems,
):
    row, spot, core = place()
    level, column = spot // 2, lax.rem(spot, 2)
    rows = tokens.shape[0]
    low = jnp.bfloat16
    length = 8 * rows
    near_gather = Gather(near_own, near, 0, near_own.shape[1], 0, sems)
    third = far_own.shape[1] // 3
    far_gathers = [Gather(far_own, far, part * third, third, part + 1, sems) for part in range(3)]

    greet(sequence_others() + [neighbours()[3]])
    near_gather.open_z()
    near_gather.open_xy()

    ids_copies = []
    for shift in range(1, 8):
        copy = remote(
            ids_in,
            ids_all.at[spot],
            send_ids.at[shift],
            recv_ids.at[shift],
            (row, lax.rem(spot + shift, 8), core),
        )
        copy.start()
        ids_copies.append(copy)
    ids_all[spot] = ids_in[...]

    values = tokens[...].astype(jnp.float32)
    unit[...] = values * lax.rsqrt(jnp.mean(values * values, axis=-1, keepdims=True) + epsilon)

    for k in range(1, 4):
        near_gather.pass_on(k)
        near_gather.diagonal(k - 1)
        if k == 2:
            far_gathers[0].open_z()
    far_gathers[0].open_xy()
    near_gather.diagonal(3)
    for shift in range(1, 8):
        remote(
            ids_in,
            ids_all.at[lax.rem(spot + 8 - shift, 8)],
            send_ids.at[shift],
            recv_ids.at[shift],
            (row, lax.rem(spot + shift, 8), core),
        ).wait_recv()
    pltpu.make_async_copy(ids_all, ids, load_ids).start()
    far_gathers[0].pass_on(1)
    near_gather.finish()

    width = near.shape[3] * 16
    qkv_width = 16 * HEAD

    def load_group(group):
        lanes = pl.ds(group * 4 * HEAD, 4 * HEAD)
        return pltpu.make_async_copy(
            near.at[:, :, :, :, lanes], weight.at[group % 2], load_w.at[group % 2]
        )

    load_extras = pltpu.make_async_copy(
        near.at[:, :, :, :, pl.ds(near_own.shape[1] - WIDE, WIDE)], extras, load_extra
    )
    load_extras.start()
    load_group(0).start()
    load_group(1).start()
    load_extras.wait()
    gain = extras[...].reshape(width, WIDE).T[0:1].astype(jnp.float32)
    normed[...] = (unit[...] * gain).astype(low)
    save_normed = pltpu.make_async_copy(normed, normed_out, saves.at[0])
    save_normed.start()
    for group in range(4):
        load_group(group).wait()
        wide = jnp.dot(
            weight[group % 2].reshape(width, 4 * HEAD),
            spread[...],
            preferred_element_type=jnp.float32,
        ).astype(low)
        if group < 2:
            load_group(group + 2).start()
        proj = jnp.dot(normed[...], wide, preferred_element_type=jnp.float32)
        for head in range(4):
            part = proj[:, head * WIDE : (head + 1) * WIDE]
            if group < 3:
                part = part * cos_tab[...] + pltpu.roll(part, WIDE // 2, 1) * sin_tab[...]
            part = part.astype(low).reshape(rows // RUN, RUN, WIDE)
            if group < 2:
                q_heads[4 * group + head] = part
            else:
                kv_heads[head, group - 2] = part

    sibling = (row, spot, 1 - core)
    outgoing = []
    for step in range(4):
        slot = lax.rem(spot + step, 4)
        chip = 4 * core + slot
        for other in range(2):
            is_self = jnp.logical_and(chip == spot, core == other)
            device = (row, chip, other)
            outgoing.append(
                (
                    (
                        kv_heads.at[slot, :, other],
                        kv_slots.at[spot, :, other],
                        send_kv.at[step, other],
                        recv_kv.at[spot],
                        device,
                    ),
                    is_self,
                )
            )
            outgoing.append(
                (
                    (
                        q_heads.at[2 * slot + other],
                        q_slots.at[spot],
                        send_q.at[step, other],
                        recv_q.at[spot],
                        device,
                    ),
                    is_self,
                )
            )
    for parts, is_self in outgoing:
        move(*parts, is_self)
    far_gathers[0].pass_on(2)
    far_gathers[0].pass_on(3)
    for k in range(4):
        far_gathers[0].diagonal(k)

    def hand_on(source):
        block = kv_slots.at[source, :, core]
        return remote(block, block, send_x.at[source], recv_x.at[source], sibling)

    for step in range(8):
        source = lax.rem(spot + step, 8)
        block = kv_slots.at[source, :, core]
        remote(block, block, send_x.at[source], recv_kv.at[source], sibling).wait_recv()
        hand_on(source).start()
    far_gathers[1].open_z()
    far_gathers[1].open_xy()
    for step in range(8):
        remote(
            q_slots.at[step], q_slots.at[step], send_x.at[step], recv_q.at[step], sibling
        ).wait_recv()
        hand_on(step).wait()

    pltpu.make_async_copy(ids_all, ids, load_ids).wait()
    runs = length // RUN
    per_device = rows // RUN

    def find_run(index, carry):
        device, part = 0, 0
        for run in range(runs):
            here = ids[run // per_device, 0, run % per_device] == index
            device = jnp.where(here, run // per_device, device)
            part = jnp.where(here, run % per_device, part)
        order[index, 0] = device
        order[index, 1] = part
        return carry

    lax.fori_loop(0, runs, find_run, 0)

    def sort_run(index, carry):
        device, part = order[index, 0], order[index, 1]
        cols = tile_at(index, RUN)
        queries, values = q_slots[device, part], kv_slots[device, 1, part]
        q[cols] = queries
        q_t[:, cols] = queries.T
        keys[cols] = kv_slots[device, 0, part]
        v[cols] = values
        v_t[:, cols] = values.T
        return carry

    lax.fori_loop(0, runs, sort_run, 0)
    sorted_saves = [
        pltpu.make_async_copy(source, target, saves.at[index])
        for index, (source, target) in enumerate([(q, q_out), (keys, k_out), (v, v_out)], 1)
    ]
    for copy in sorted_saves:
        copy.start()
    scale = HEAD ** (-0.5) * LOG2_E
    tiles = length // TILE

    def query_tile(index, carry):
        cols = tile_at(index, TILE)
        queries = q_t[:, cols]

        def step(scores, block, peak, total, mix):
            high = jnp.maximum(peak, jnp.max(scores, axis=0, keepdims=True))
            decay = jnp.exp2(peak - high)
            weights = jnp.exp2(scores - high)
            total = total * decay + jnp.sum(weights, axis=0, keepdims=True)
            mix = mix * decay + jnp.dot(
                v_t[:, tile_at(block, TILE)],
                weights.astype(low),
                preferred_element_type=jnp.float32,
            )
            return high, total, mix

        def scores_of(block):
            return (
                jnp.dot(keys[tile_at(block, TILE)], queries, preferred_element_type=jnp.float32)
                * scale
            )

        state = (
            jnp.full((1, TILE), masked_value, jnp.float32),
            jnp.zeros((1, TILE), jnp.float32),
            jnp.zeros((WIDE, TILE), jnp.float32),
        )
        state = step(causal(scores_of(index)), index, *state)
        peak, total, mix = lax.fori_loop(
            0, index, lambda block, now: step(scores_of(block), block, *now), state
        )
        mix = mix / total
        mixed_t[:, cols] = mix
        lse[:, cols] = peak + jnp.log2(total)
        for half in range(TILE // RUN):
            mixed[index * (TILE // RUN) + half] = mix[:, half * RUN : (half + 1) * RUN].T.astype(low)

        for k in range(1, 4):

            @pl.when(index == k + 3)
            def _():
                far_gathers[1].pass_on(k)

        return carry

    lax.fori_loop(0, tiles, query_tile, 0)
    save_mixed = pltpu.make_async_copy(mixed_t, mixed_t_out, saves.at[4])
    save_mixed.start()
    save_lse = pltpu.make_async_copy(lse, lse_out, saves.at[5])
    save_lse.start()

    def unsort_run(run, carry):
        index = ids[run // per_device, 0, run % per_device]
        mixed_slots[run // per_device, run % per_device] = mixed[index]
        return carry

    lax.fori_loop(0, runs, unsort_run, 0)
    copies = return_copies(mixed_slots, mixed_heads, send_m, recv_m)
    start_return(copies)
    far_gathers[2].open_z()
    far_gathers[2].open_xy()
    for k in range(4):
        far_gathers[1].diagonal(k)
    for k in range(1, 4):
        far_gathers[2].pass_on(k)
        far_gathers[2].diagonal(k - 1)
    far_gathers[2].diagonal(3)
    finish_return(copies, mixed_heads, send_m, recv_m)
    for gather in far_gathers:
        gather.finish()
    for gather in [near_gather] + far_gathers:
        gather.close()
    for parts, is_self in outgoing:

        @pl.when(jnp.logical_not(is_self))
        def _():
            remote(*parts).wait_send()

    for copy in ids_copies:
        copy.wait_send()
    for copy in [save_normed, save_mixed, save_lse] + sorted_saves:
        copy.wait()


def forward(tokens, ids, near_own, far_own, spread, cos_tab, sin_tab):
    dma = pltpu.SemaphoreType.DMA
    vmem = pltpu.VMEM
    low, full = jnp.bfloat16, jnp.float32
    rows, width = tokens.shape
    share = near_own.shape[0]
    length = 8 * rows
    heads = (8, rows // RUN, RUN, WIDE)
    both = (2, rows // RUN, RUN, WIDE)
    return pl.pallas_call(
        forward_kernel,
        in_specs=[vmem_spec(), vmem_spec(), any_spec(), any_spec()] + [vmem_spec()] * 3,
        out_specs=[any_spec()] * 9,
        out_shape=[
            jax.ShapeDtypeStruct((2, 4, 2, share, near_own.shape[1]), low),
            jax.ShapeDtypeStruct((2, 4, 2, share, far_own.shape[1]), low),
            jax.ShapeDtypeStruct((rows, width), low),
            jax.ShapeDtypeStruct((length, WIDE), low),
            jax.ShapeDtypeStruct((length, WIDE), low),
            jax.ShapeDtypeStruct((length, WIDE), low),
            jax.ShapeDtypeStruct(heads, low),
            jax.ShapeDtypeStruct((WIDE, length), full),
            jax.ShapeDtypeStruct((1, length), full),
        ],
        scratch_shapes=[
            vmem((rows, width), full),
            vmem((rows, width), low),
            vmem((2, 2, 4, 2, share, 4 * HEAD), low),
            vmem((2, 4, 2, share, WIDE), low),
            vmem(heads, low),
            vmem((4,) + both, low),
            vmem(heads, low),
            vmem((8,) + both, low),
            vmem((length, WIDE), low),
            vmem((WIDE, length), low),
            vmem((length, WIDE), low),
            vmem((length, WIDE), low),
            vmem((WIDE, length), low),
            vmem((WIDE, length), full),
            vmem((1, length), full),
            vmem((length // RUN, RUN, WIDE), low),
            vmem(heads, low),
            vmem((8, 8, WIDE), jnp.int32),
            pltpu.SMEM((8, 8, WIDE), jnp.int32),
            pltpu.SMEM((length // RUN, 2), jnp.int32),
            dma((8,)),
            dma((8,)),
            dma(()),
            dma((2,)),
            dma(()),
            dma((6,)),
            dma((4, 2)),
            dma((8,)),
            dma((4, 2)),
            dma((8,)),
            dma((8,)),
            dma((8,)),
            dma((8,)),
            dma((8,)),
        ]
        + gather_sems(4),
        compiler_params=pltpu.CompilerParams(
            collective_id=1, has_side_effects=True, vmem_limit_bytes=VMEM_LIMIT
        ),
        name="forward",
    )(tokens, ids, near_own, far_own, spread, cos_tab, sin_tab)


PIECE = 256
SECOND, THIRD, LAST = 2, 3, 4


class Reduce:
    def __init__(self, n, changes, refs):
        (
            self.left_t,
            self.right,
            self.gains,
            self.own,
            self.send_one,
            self.recv_one,
            self.send_two,
            self.recv_two,
            self.kept,
            self.recv_three,
            self.ss_one,
            self.rs_one,
            self.ss_two,
            self.rs_two,
            self.ss_three,
            self.rs_three,
        ) = refs
        self.n, self.changes = n, changes
        self.share = self.own.shape[0]

    def columns(self, step, kind):
        return pl.ds(pl.multiple_of(step * 2 * PIECE + kind * PIECE, PIECE), PIECE)

    def product(self, step, kind, x, y):
        left = 0
        for start in self.changes:
            left = left + jnp.where(step >= start, 1, 0)
        term = jnp.dot(
            self.left_t[lax.rem(left, 2), x, y],
            self.right[:, self.columns(step, kind)],
            preferred_element_type=jnp.float32,
        )
        if kind == 1:
            at_gains = jnp.where(step == self.n - 1, 1.0, 0.0)
            term = term * (1.0 - at_gains) + self.gains[x, y].astype(jnp.float32) * at_gains
        return term

    def first_copy(self, step, kind):
        beside_x, beside_y = neighbours()[3:5]
        out, into = lax.rem(step, 3), lax.rem(step, 4)
        return remote(
            self.send_one.at[out, kind],
            self.recv_one.at[into, kind],
            self.ss_one.at[out, kind],
            self.rs_one.at[into, kind],
            beside_x if kind == 0 else beside_y,
        )

    def second_copy(self, step, kind):
        beside_x, beside_y = neighbours()[3:5]
        out, into = lax.rem(step, 2), lax.rem(step, 4)
        return remote(
            self.send_two.at[out, kind],
            self.recv_two.at[into, kind],
            self.ss_two.at[out, kind],
            self.rs_two.at[into, kind],
            beside_y if kind == 0 else beside_x,
        )

    def third_copy(self, step, kind, k):
        row, level, column, beside_x, beside_y, along_z = neighbours()
        target = lax.rem(level + k + 1, 4)
        out, into = lax.rem(step, 3), lax.rem(step, 4)
        return remote(
            self.kept.at[out, kind, pl.ds(pl.multiple_of(target * self.share, 16), self.share)],
            self.recv_three.at[into, kind, k],
            self.ss_three.at[out, kind, k],
            self.rs_three.at[into, kind, k],
            along_z[k],
        )

    def first(self, step):
        row, level, column = neighbours()[:3]
        slot = lax.rem(step, 3)
        for half in range(2):
            self.send_one[slot, 0, half] = self.product(step, 0, 1 - row, half).astype(jnp.bfloat16)
        self.first_copy(step, 0).start()
        for half in range(2):
            self.send_one[slot, 1, half] = self.product(step, 1, half, 1 - column).astype(
                jnp.bfloat16
            )
        self.first_copy(step, 1).start()

    def second(self, step):
        row, level, column = neighbours()[:3]
        slot, came, keep = lax.rem(step, 2), lax.rem(step, 4), lax.rem(step, 3)
        for kind in range(2):
            self.first_copy(step, kind).wait()
        for kind in range(2):
            away_at = (row, 1 - column) if kind == 0 else (1 - row, column)
            arrived = self.recv_one.at[came, kind]
            away = self.product(step, kind, *away_at) + arrived[away_at[1 - kind]].astype(
                jnp.float32
            )
            self.send_two[slot, kind] = away.astype(jnp.bfloat16)
            here = self.product(step, kind, row, column) + arrived[
                column if kind == 0 else row
            ].astype(jnp.float32)
            self.kept[keep, kind] = here.astype(jnp.bfloat16)
        for kind in range(2):
            self.second_copy(step, kind).start()

    def third(self, step):
        came, keep = lax.rem(step, 4), lax.rem(step, 3)
        for kind in range(2):
            self.second_copy(step, kind).wait()
            here = self.kept[keep, kind].astype(jnp.float32) + self.recv_two[came, kind].astype(
                jnp.float32
            )
            self.kept[keep, kind] = here.astype(jnp.bfloat16)
            for k in range(3):
                self.third_copy(step, kind, k).start()

    def last(self, step):
        level = neighbours()[1]
        came, keep = lax.rem(step, 4), lax.rem(step, 3)
        mine = pl.ds(pl.multiple_of(level * self.share, 16), self.share)
        for kind in range(2):
            total = self.kept[keep, kind, mine].astype(jnp.float32)
            for k in range(3):
                self.third_copy(step, kind, k).wait()
                total = total + self.recv_three[came, kind, k].astype(jnp.float32)
            self.own[:, self.columns(step, kind)] = total

    def turn(self, step):
        for stage, lag in (
            (self.first, 0),
            (self.second, SECOND),
            (self.third, THIRD),
            (self.last, LAST),
        ):

            @pl.when(jnp.logical_and(step >= lag, step < self.n + lag))
            def _():
                stage(step - lag)


def backward_kernel(
    order,
    ids,
    d_heads,
    q_in,
    k_in,
    v_in,
    mixed_t_in,
    lse_in,
    left_0,
    left_1,
    left_2,
    left_3,
    right_0,
    right_1,
    right_2,
    right_3,
    near,
    spread,
    cos_tab,
    sin_tab,
    tokens,
    gain_one,
    grad_middle,
    grad_gain_two,
    input_grad,
    own,
    q,
    q_t,
    k,
    k_t,
    v,
    d_slots,
    d,
    d_t,
    dq_t,
    lse,
    delta,
    dk,
    dv,
    dkv_sorted,
    dkv_slots,
    dkv_other,
    dq_own,
    dkv_own,
    weight,
    part,
    part_other,
    total,
    staged,
    left_t,
    right,
    gains,
    send_one,
    recv_one,
    send_two,
    recv_two,
    kept,
    recv_three,
    loads,
    load_left_sem,
    load_right,
    load_w,
    send_d,
    recv_d,
    send_q,
    recv_q,
    send_x,
    recv_x,
    send_k,
    recv_k,
    send_p,
    recv_p,
    *sems,
):
    row, spot, core = place()
    low = jnp.bfloat16
    rows, width = tokens.shape
    length = 8 * rows
    runs, tiles = length // RUN, length // TILE
    per_device = rows // RUN
    share = own.shape[0]
    sibling = (row, spot, 1 - core)
    qkv_width = 16 * HEAD
    far_width = right_0.shape[1]
    n = own.shape[1] // (2 * PIECE)
    far_steps = 3 * far_width // (2 * PIECE)
    near_start = 3 * far_width
    changes = (2 * far_steps // 3, far_steps, far_steps + qkv_width // (2 * PIECE))
    sums = Reduce(
        n,
        changes,
        (left_t, right, gains, own, send_one, recv_one, send_two, recv_two, kept, recv_three)
        + sems,
    )
    lefts = (left_0, left_1, left_2, left_3)

    def load_left(index):
        quarter = 4 * share
        copy = pltpu.make_async_copy(lefts[index], staged, load_left_sem)
        copy.start()
        copy.wait()
        for piece in range(4):
            turned = staged[:, piece * quarter : (piece + 1) * quarter].T
            for inner in range(4):
                x, z, y = piece // 2, 2 * (piece % 2) + inner // 2, inner % 2
                left_t[index % 2, x, y, z * share : (z + 1) * share] = turned[
                    inner * share : (inner + 1) * share
                ]

    right_parts = [(right_0, 0), (right_1, far_width), (right_2, 2 * far_width)]
    right_parts.append((right_3, near_start + qkv_width))
    right_loads = [
        pltpu.make_async_copy(ref, right.at[:, pl.ds(start, ref.shape[1])], load_right.at[index])
        for index, (ref, start) in enumerate(right_parts)
    ]
    sorted_loads = [
        pltpu.make_async_copy(source, target, loads.at[index])
        for index, (source, target) in enumerate(
            [(q_in, q), (k_in, k), (v_in, v), (mixed_t_in, dq_t), (lse_in, lse)]
        )
    ]

    d_copies = []
    for step in range(4):
        slot = lax.rem(spot + step, 4)
        chip = 4 * core + slot
        for other in range(2):
            is_self = jnp.logical_and(chip == spot, core == other)
            parts = (
                d_heads.at[2 * slot + other],
                d_slots.at[spot],
                send_d.at[step, other],
                recv_d.at[spot],
                (row, chip, other),
            )
            d_copies.append((parts, is_self))

    right_loads[0].start()
    greet(sequence_others() + [neighbours()[3]])
    for parts, is_self in d_copies:
        move(*parts, is_self)
    for copy in right_loads[1:] + sorted_loads:
        copy.start()
    load_left(0)
    for copy in right_loads:
        copy.wait()
    right[:, right.shape[1] - PIECE :] = jnp.zeros((rows, PIECE), low)

    def load_group(group):
        lanes = pl.ds(group * 4 * HEAD, 4 * HEAD)
        return pltpu.make_async_copy(
            near.at[:, :, :, :, lanes], weight.at[group], load_w.at[group]
        )

    load_tokens = pltpu.make_async_copy(tokens, staged, load_left_sem)
    load_middle = pltpu.make_async_copy(grad_middle, total, load_w.at[4])


    def prepare():
        load_left(1)
        for copy in sorted_loads:
            copy.wait()
        for index in range(tiles):
            cut = pl.ds(index * TILE, TILE)
            q_t[:, cut] = q[cut].T
            k_t[:, cut] = k[cut].T

    def take_cotangents():
        for index in range(8):
            remote(
                d_slots.at[index], d_slots.at[index], send_d.at[0, 0], recv_d.at[index], sibling
            ).wait_recv()

        def sort_run(index, carry):
            cols = tile_at(index, RUN)
            run = d_slots[order[index, 0], order[index, 1]]
            turned = run.T
            d[index // per_device, index % per_device] = run
            d_t[:, cols] = turned
            delta[:, cols] = jnp.sum(
                turned.astype(jnp.float32) * dq_t[:, cols], axis=0, keepdims=True
            )
            return carry

        lax.fori_loop(0, runs, sort_run, 0)
        dq_t[...] = jnp.zeros_like(dq_t)

    scale = HEAD ** (-0.5)
    halves = TILE // RUN

    def key_tile(block):
        cut = tile_at(block, TILE)
        keys, keys_t, values = k[cut], k_t[:, cut], v[cut]
        dk[...] = jnp.zeros_like(dk)
        dv[...] = jnp.zeros_like(dv)

        def query_tile(index, diagonal):
            cols = tile_at(index, TILE)
            scores = jnp.dot(keys, q_t[:, cols], preferred_element_type=jnp.float32) * (
                scale * LOG2_E
            )
            if diagonal:
                scores = causal(scores)
            probs = jnp.exp2(scores - lse[:, cols])
            cotangents = d[index].reshape(TILE, WIDE)
            dv[...] += jnp.dot(probs.astype(low), cotangents, preferred_element_type=jnp.float32)
            grad_probs = jnp.dot(values, d_t[:, cols], preferred_element_type=jnp.float32)
            grad_scores = (probs * (grad_probs - delta[:, cols])).astype(low)
            dk[...] += jnp.dot(grad_scores, q[cols], preferred_element_type=jnp.float32)
            dq_t[:, cols] += jnp.dot(keys_t, grad_scores, preferred_element_type=jnp.float32)

        query_tile(block, True)

        def later(index, inner):
            query_tile(index, False)
            return inner

        lax.fori_loop(block + 1, tiles, later, 0)
        for half in range(halves):
            cut = pl.ds(half * RUN, RUN)
            dkv_sorted[0, block * halves + half] = (dk[cut] * scale).astype(low)
            dkv_sorted[1, block * halves + half] = dv[cut].astype(low)

    def key_tiles(start, stop):
        def one(block, carry):
            key_tile(block)
            return carry

        lax.fori_loop(start, stop, one, 0)

    swap = remote(
        dkv_slots.at[:, :, 1 - core], dkv_other, send_x, recv_x, sibling
    )
    dq_copies = return_copies(d, dq_own, send_q, recv_q)
    slot, owner = lax.rem(spot, 4), spot // 4
    dkv_copies = []
    for step in range(8):
        chip = lax.rem(spot + step, 8)
        parts = (
            dkv_slots.at[:, chip, core],
            dkv_own.at[slot, :, core],
            send_k.at[step],
            recv_k.at[slot, core],
            (row, chip, owner),
        )
        dkv_copies.append((parts, (owner == core) if step == 0 else False))

    def send_back():
        def unturn_run(index, carry):
            d_slots[index // per_device, index % per_device] = (
                (dq_t[:, tile_at(index, RUN)] * scale).T.astype(low)
            )
            return carry

        lax.fori_loop(0, runs, unturn_run, 0)

        def unsort_run(run, carry):
            index = ids[run]
            for kind in range(2):
                dkv_slots[kind, run // per_device, run % per_device] = dkv_sorted[kind, index]
            return carry

        lax.fori_loop(0, runs, unsort_run, 0)
        swap.start()

        def unsort_queries(run, carry):
            index = order[runs + run, 0], order[runs + run, 1]
            d[run // per_device, run % per_device] = d_slots[index]
            return carry

        lax.fori_loop(0, runs, unsort_queries, 0)
        start_return(dq_copies)

    def add_pairs():
        swap.wait()
        for chip in range(8):
            both = dkv_slots[:, chip, core].astype(jnp.float32) + dkv_other[:, chip].astype(
                jnp.float32
            )
            dkv_slots[:, chip, core] = both.astype(low)
        start_return(dkv_copies)

    def project_back():
        for group in range(4):
            load_group(group).start()
        for head in range(8):
            remote(
                dq_own.at[head], dq_own.at[head], send_q.at[0], recv_q.at[head], sibling
            ).wait_recv()
        for slot_in in range(4):
            for core_in in range(2):
                target = dkv_own.at[slot_in, :, core_in]
                remote(
                    target, target, send_k.at[0], recv_k.at[slot_in, core_in], sibling
                ).wait_recv()
        for group in range(4):
            turned = []
            for head in range(4):
                if group < 2:
                    value = dq_own[4 * group + head]
                else:
                    value = dkv_own[head, group - 2]
                value = value.reshape(rows, WIDE)
                if group < 3:
                    value = value.astype(jnp.float32)
                    value = value * cos_tab[...] - pltpu.roll(value, WIDE // 2, 1) * sin_tab[...]
                    value = value.astype(low)
                turned.append(value)
            narrow = lax.dot_general(
                jnp.concatenate(turned, axis=1),
                spread[...],
                (((1,), (1,)), ((), ())),
                preferred_element_type=jnp.float32,
            )
            start = near_start + group * 4 * HEAD
            right[:, start : start + 4 * HEAD] = narrow.astype(low)

    pair_copy = remote(part, part_other, send_p, recv_p, sibling)

    def project_normed():
        for group in range(4):
            load_group(group).wait()
        chunk = rows // 4

        def block(index, carry):
            cut = tile_at(index, chunk)
            grad = jnp.zeros((chunk, width), jnp.float32)
            for group in range(4):
                start = near_start + group * 4 * HEAD
                grad = grad + lax.dot_general(
                    right[cut, start : start + 4 * HEAD],
                    weight[group].reshape(width, 4 * HEAD),
                    (((1,), (1,)), ((), ())),
                    preferred_element_type=jnp.float32,
                )
            part[cut] = grad.astype(low)
            return carry

        lax.fori_loop(0, 4, block, 0)
        pair_copy.start()

    def norm_back():
        load_tokens.start()
        load_middle.start()
        load_tokens.wait()
        load_middle.wait()
        pair_copy.wait()
        chunk = rows // 8

        def block(index, gain_grad):
            cut = tile_at(index, chunk)
            grad = part[cut].astype(jnp.float32) + part_other[cut].astype(jnp.float32)
            values = staged[cut].astype(jnp.float32)
            inverse = lax.rsqrt(jnp.mean(values * values, axis=-1, keepdims=True) + epsilon)
            unit = values * inverse
            scaled = grad * gain_one[...]
            mean = jnp.mean(scaled * unit, axis=-1, keepdims=True)
            total[cut] = total[cut] + inverse * (scaled - unit * mean)
            return gain_grad + jnp.sum(grad * unit, axis=0, keepdims=True)

        gain_grad = lax.fori_loop(0, 8, block, jnp.zeros((1, width), jnp.float32))
        pltpu.make_async_copy(total, input_grad, load_w.at[4]).start()
        lines = []
        for value in (gain_grad, grad_gain_two[...]):
            high = value.astype(low).astype(jnp.float32)
            lines.append((high, value - high))
        which = lax.broadcasted_iota(jnp.int32, (WIDE, width), 0)
        table = jnp.zeros((WIDE, width), jnp.float32)
        for index, line in enumerate((lines[0][0], lines[1][0], lines[0][1], lines[1][1])):
            table = jnp.where(which == index, line, table)
        columns = table.T.astype(low)
        gains[...] = jnp.zeros_like(gains)
        for x in range(2):
            for z in range(4):
                for y in range(2):
                    start = ((x * 4 + z) * 2 + y) * share
                    gains[x, y, z * share : (z + 1) * share, :WIDE] = columns[start : start + share]

    plan = {
        0: [prepare],
        1: [take_cotangents],
        2: [lambda: key_tiles(0, 2)],
        3: [lambda: key_tiles(2, 4)],
        4: [lambda: key_tiles(4, 8), send_back],
        5: [add_pairs],
        7: [project_back],
        8: [project_normed],
        changes[0] + 2: [lambda: load_left(2)],
        far_steps + 2: [lambda: load_left(3)],
        far_steps + 3: [norm_back],
    }

    def run(step, carry):
        sums.turn(step)
        for when, tasks in plan.items():

            @pl.when(step == when)
            def _():
                for task in tasks:
                    task()

        return carry

    lax.fori_loop(0, n + LAST, run, 0)
    pltpu.make_async_copy(total, input_grad, load_w.at[4]).wait()
    for copies in (d_copies, dq_copies, dkv_copies):
        for parts, is_self in copies:
            if is_self is False:
                remote(*parts).wait_send()
            else:

                @pl.when(jnp.logical_not(is_self))
                def _():
                    remote(*parts).wait_send()


def backward(
    order,
    ids,
    d_heads,
    q_sorted,
    k_sorted,
    v_sorted,
    mixed_t,
    lse,
    lefts,
    rights,
    mixed_low,
    near,
    spread,
    cos_tab,
    sin_tab,
    tokens,
    gain_one,
    grad_middle,
    grad_gain_two,
):
    dma = pltpu.SemaphoreType.DMA
    vmem = pltpu.VMEM
    smem_spec = pl.BlockSpec(memory_space=pltpu.SMEM)
    low, full = jnp.bfloat16, jnp.float32
    rows, width = tokens.shape
    length = 8 * rows
    share = width // 16
    wide = sum(ref.shape[1] for ref in rights) + 16 * HEAD + mixed_low.shape[1] + PIECE
    n = wide // (2 * PIECE)
    quarter = 4 * share
    heads = (8, rows // RUN, RUN, WIDE)
    return pl.pallas_call(
        backward_kernel,
        in_specs=[smem_spec] * 2
        + [any_spec()] * 15
        + [vmem_spec()] * 3
        + [any_spec(), vmem_spec(), any_spec(), vmem_spec()],
        out_specs=[any_spec(), vmem_spec()],
        out_shape=[
            jax.ShapeDtypeStruct((rows, width), full),
            jax.ShapeDtypeStruct((share, wide), full),
        ],
        scratch_shapes=[
            vmem((length, WIDE), low),
            vmem((WIDE, length), low),
            vmem((length, WIDE), low),
            vmem((WIDE, length), low),
            vmem((length, WIDE), low),
            vmem(heads, low),
            vmem(heads, low),
            vmem((WIDE, length), low),
            vmem((WIDE, length), full),
            vmem((1, length), full),
            vmem((1, length), full),
            vmem((TILE, WIDE), full),
            vmem((TILE, WIDE), full),
            vmem((2, length // RUN, RUN, WIDE), low),
            vmem((2,) + heads, low),
            vmem((2, 8, RUN, WIDE), low),
            vmem(heads, low),
            vmem((4, 2, rows // RUN, RUN, WIDE), low),
            vmem((4, 2, 4, 2, share, 4 * HEAD), low),
            vmem((rows, width), low),
            vmem((rows, width), low),
            vmem((rows, width), full),
            vmem((rows, width), low),
            vmem((2, 2, 2, quarter, rows), low),
            vmem((rows, wide), low),
            vmem((2, 2, quarter, PIECE), low),
            vmem((3, 2, 2, quarter, PIECE), low),
            vmem((4, 2, 2, quarter, PIECE), low),
            vmem((2, 2, quarter, PIECE), low),
            vmem((4, 2, quarter, PIECE), low),
            vmem((3, 2, quarter, PIECE), low),
            vmem((4, 2, 3, share, PIECE), low),
            dma((5,)),
            dma(()),
            dma((4,)),
            dma((5,)),
            dma((4, 2)),
            dma((8,)),
            dma((8,)),
            dma((8,)),
            dma(()),
            dma(()),
            dma((8,)),
            dma((4, 2)),
            dma(()),
            dma(()),
            dma((3, 2)),
            dma((4, 2)),
            dma((2, 2)),
            dma((4, 2)),
            dma((3, 2, 3)),
            dma((4, 2, 3)),
        ],
        compiler_params=pltpu.CompilerParams(
            collective_id=2, has_side_effects=True, vmem_limit_bytes=62 * 1024 * 1024
        ),
        name="backward",
    )(
        order,
        ids,
        d_heads,
        q_sorted,
        k_sorted,
        v_sorted,
        mixed_t,
        lse,
        *lefts,
        *rights,
        mixed_low,
        near,
        spread,
        cos_tab,
        sin_tab,
        tokens,
        gain_one,
        grad_middle,
        grad_gain_two,
    )


def dot_f32(left, right):
    return jnp.dot(left, right, preferred_element_type=jnp.float32)


def by_heads(
    tokens,
    positions,
    gain_one,
    gain_two,
    w_query,
    w_key,
    w_value,
    w_out,
    w_gate,
    w_up,
    w_down,
    cotangent,
):
    low = jnp.bfloat16
    rows, _, width = tokens.shape
    share = gain_one.shape[0]
    hidden_width = w_gate.shape[1]
    length = rows * 8

    run_ids = positions[::RUN, 0] // RUN
    extra = jnp.zeros((share, WIDE), low)
    extra = extra.at[:, 0].set(gain_one).at[:, 1].set(gain_two)
    extra = extra.at[: rows // RUN, 2].set(run_ids.astype(low))
    spread = spread_matrix(8)
    cos_tab, sin_tab = lane_tables(positions[:, 0])
    near, far, normed, q_sorted, k_sorted, v_sorted, mixed_heads, mixed_t, lse = forward(
        tokens.reshape(rows, width),
        jnp.broadcast_to(jnp.pad(run_ids, (0, WIDE - rows // RUN)), (8, WIDE)),
        jnp.concatenate([w_query, w_key, w_value, w_out.T, extra], axis=1),
        jnp.concatenate([w_gate, w_up, w_down.T], axis=1),
        spread[: 4 * HEAD, : 4 * WIDE],
        cos_tab,
        sin_tab,
    )
    near_blocks = near
    near = near.reshape(width, near.shape[-1])
    far = far.reshape(width, far.shape[-1])
    qkv_width = w_query.shape[1] + w_key.shape[1] + w_value.shape[1]
    out_width = w_out.shape[0]
    qkv_mat = near[:, :qkv_width]
    out_mat_t = near[:, qkv_width : qkv_width + out_width]
    extras = near[:, qkv_width + out_width :]
    full_one, full_two = extras[:, 0], extras[:, 1]
    row = lax.axis_index("dp")
    ids = lax.dynamic_slice_in_dim(extras[:, 2].reshape(2, 8, share), row, 1, 0)[0, :, : rows // RUN]
    ids = ids.reshape(-1).astype(jnp.int32)
    count = ids.shape[0]
    order = jnp.sum(
        jnp.where(ids[None, :] == jnp.arange(count)[:, None], jnp.arange(count)[None, :], 0), axis=1
    ).astype(jnp.int32)
    gate_mat = far[:, :hidden_width]
    up_mat = far[:, hidden_width : 2 * hidden_width]
    down_mat_t = far[:, 2 * hidden_width :]

    flat_in = tokens.astype(jnp.float32).reshape(rows, width)
    mixed_heads = mixed_heads.reshape(8, rows, WIDE)

    def narrow(heads):
        count = heads.shape[0]
        side = jnp.transpose(heads, (1, 0, 2)).reshape(rows, count * WIDE)
        return contract_cols(side, spread[: count * HEAD, : count * WIDE]).astype(low)

    mixed_low = narrow(mixed_heads)
    middle = flat_in + pair_sum(contract_cols(mixed_low, out_mat_t).astype(low), 5)
    unit_two, inverse_two, second = norm_forward(middle, full_two)
    gate_vals = dot_f32(second, gate_mat)
    up_vals = dot_f32(second, up_mat)
    sigmoid_vals = jax.nn.sigmoid(gate_vals)
    silu_vals = gate_vals * sigmoid_vals
    hidden = (silu_vals * up_vals).astype(low)
    mlp_part = pair_sum(contract_cols(hidden, down_mat_t).astype(low), 6)
    layer_out = (middle + mlp_part).astype(low).reshape(rows, 1, width)

    grad_low = cotangent.reshape(rows, width)
    grad_hidden = dot_f32(grad_low, down_mat_t)
    grad_gate_low = (
        grad_hidden * up_vals * sigmoid_vals * (1.0 + gate_vals * (1.0 - sigmoid_vals))
    ).astype(low)
    grad_up_low = (grad_hidden * silu_vals).astype(low)
    grad_second = pair_sum(
        (contract_cols(grad_gate_low, gate_mat) + contract_cols(grad_up_low, up_mat)).astype(low), 7
    )
    grad_mid_norm, grad_gain_two = norm_backward(grad_second, unit_two, inverse_two, full_two)
    grad_middle = grad_low.astype(jnp.float32) + grad_mid_norm
    grad_mid_low = grad_middle.astype(low)
    grad_mixed = dot_f32(grad_mid_low, out_mat_t).astype(low)
    grad_heads = jnp.transpose(
        dot_f32(grad_mixed, spread).astype(low).reshape(rows, 8, WIDE), (1, 0, 2)
    )
    input_grad, grads = backward(
        jnp.concatenate(
            [jnp.stack([at // (rows // RUN), at % (rows // RUN)], axis=1) for at in (order, ids)]
        ),
        ids,
        grad_heads.reshape(8, rows // RUN, RUN, WIDE),
        q_sorted,
        k_sorted,
        v_sorted,
        mixed_t,
        lse,
        (second, grad_low, normed, grad_mid_low),
        (grad_gate_low, grad_up_low, hidden),
        mixed_low,
        near_blocks,
        spread[: 4 * HEAD, : 4 * WIDE],
        cos_tab,
        sin_tab,
        tokens.reshape(rows, width),
        full_one.astype(jnp.float32).reshape(1, width),
        grad_middle,
        grad_gain_two.reshape(1, width),
    )
    input_grad = input_grad.reshape(rows, 1, width)
    far_own = grads[:, : 3 * hidden_width]
    near_own = grads[:, 3 * hidden_width :]
    gain_own = near_own[:, qkv_width + out_width :]
    q_width, k_width = w_query.shape[1], w_key.shape[1]
    return (
        layer_out,
        input_grad,
        gain_own[:, 0] + gain_own[:, 2],
        gain_own[:, 1] + gain_own[:, 3],
        near_own[:, :q_width],
        near_own[:, q_width : q_width + k_width],
        near_own[:, q_width + k_width : qkv_width],
        near_own[:, qkv_width : qkv_width + out_width].T,
        far_own[:, :hidden_width],
        far_own[:, hidden_width : 2 * hidden_width],
        far_own[:, 2 * hidden_width :].T,
    )


def solution(mesh):
    sizes = (mesh.shape["dp"], mesh.shape["context"], mesh.shape["tensor"])
    return jax.shard_map(
        by_heads if sizes == (2, 8, 2) else on_device,
        mesh=mesh,
        in_specs=(
            P("context", "dp", None),
            P("context", "dp"),
            P(("dp", "context")),
            P(("dp", "context")),
            P(("dp", "context"), "tensor"),
            P(("dp", "context"), "tensor"),
            P(("dp", "context"), "tensor"),
            P("tensor", ("dp", "context")),
            P(("dp", "context"), "tensor"),
            P(("dp", "context"), "tensor"),
            P("tensor", ("dp", "context")),
            P("context", "dp", None),
        ),
        out_specs=(
            P("context", "dp", None),
            P("context", "dp", None),
            P(("dp", "context")),
            P(("dp", "context")),
            P(("dp", "context"), "tensor"),
            P(("dp", "context"), "tensor"),
            P(("dp", "context"), "tensor"),
            P("tensor", ("dp", "context")),
            P(("dp", "context"), "tensor"),
            P(("dp", "context"), "tensor"),
            P("tensor", ("dp", "context")),
        ),
        check_vma=False,
    )
```

```python
import functools

import jax
import jax.numpy as jnp
from jax import lax
from jax.experimental import pallas as pl
from jax.experimental.pallas import tpu as pltpu
from jax.sharding import PartitionSpec as P

HEAD = 96


epsilon = 1e-05
theta_base = 100000.0
masked_value = -1e30


def norm_forward(values_in, gain_vec):
    inverse = lax.rsqrt(jnp.mean(values_in * values_in, axis=-1, keepdims=True) + epsilon)
    unit_vals = values_in * inverse
    return (unit_vals, inverse, (unit_vals * gain_vec.astype(jnp.float32)).astype(jnp.bfloat16))


def norm_backward(grad_in, unit_vals, inverse, gain_vec):
    scaled = grad_in * gain_vec.astype(jnp.float32)
    grad_vals = inverse * (
        scaled - unit_vals * jnp.mean(scaled * unit_vals, axis=-1, keepdims=True)
    )
    return (grad_vals, jnp.sum(grad_in * unit_vals, axis=0))


def rotate(values_in, cos_part, sin_part):
    half_size = values_in.shape[-1] // 2
    front_half = values_in[..., :half_size]
    back_half = values_in[..., half_size:]
    return jnp.concatenate(
        [
            front_half * cos_part - back_half * sin_part,
            back_half * cos_part + front_half * sin_part,
        ],
        axis=-1,
    )


def contract_rows(left_mat, right_mat):
    return lax.dot_general(
        left_mat, right_mat, (((0,), (0,)), ((), ())), preferred_element_type=jnp.float32
    )


def contract_cols(left_mat, right_mat):
    return lax.dot_general(
        left_mat, right_mat, (((1,), (1,)), ((), ())), preferred_element_type=jnp.float32
    )


def on_device(
    tokens,
    positions,
    gain_one,
    gain_two,
    w_query,
    w_key,
    w_value,
    w_out,
    w_gate,
    w_up,
    w_down,
    cotangent,
):
    slot_count, seq_count, model_width = tokens.shape
    row_count = slot_count * seq_count
    gathered = (
        lax.all_gather(gain_one, ("dp", "context"), axis=0, tiled=True),
        lax.all_gather(gain_two, ("dp", "context"), axis=0, tiled=True),
        lax.all_gather(w_query, ("dp", "context"), axis=0, tiled=True),
        lax.all_gather(w_key, ("dp", "context"), axis=0, tiled=True),
        lax.all_gather(w_value, ("dp", "context"), axis=0, tiled=True),
        lax.all_gather(w_out, ("dp", "context"), axis=1, tiled=True),
        lax.all_gather(w_gate, ("dp", "context"), axis=0, tiled=True),
        lax.all_gather(w_up, ("dp", "context"), axis=0, tiled=True),
        lax.all_gather(w_down, ("dp", "context"), axis=1, tiled=True),
    )
    full_one, full_two, query_mat, key_mat, value_mat, out_mat, gate_mat, up_mat, down_mat = (
        gathered
    )
    heads_kv = key_mat.shape[1] // HEAD
    heads_q = query_mat.shape[1] // HEAD
    group_size = heads_q // heads_kv
    score_scale = HEAD ** (-0.5)
    half_size = HEAD // 2
    inv_freqs = theta_base ** (-2.0 * jnp.arange(half_size, dtype=jnp.float32) / HEAD)
    angles = positions.astype(jnp.float32)[:, :, None] * inv_freqs
    cos_part = jnp.cos(angles)[:, :, None, :]
    sin_part = jnp.sin(angles)[:, :, None, :]
    flat_in = tokens.astype(jnp.float32).reshape(row_count, model_width)
    unit_one, inverse_one, normed = norm_forward(flat_in, full_one)
    query_proj = jnp.dot(normed, query_mat, preferred_element_type=jnp.float32).reshape(
        slot_count, seq_count, heads_q, HEAD
    )
    key_proj = jnp.dot(normed, key_mat, preferred_element_type=jnp.float32).reshape(
        slot_count, seq_count, heads_kv, HEAD
    )
    value_low = (
        jnp.dot(normed, value_mat, preferred_element_type=jnp.float32)
        .astype(jnp.bfloat16)
        .reshape(slot_count, seq_count, heads_kv * HEAD)
    )
    queries = rotate(query_proj, cos_part, sin_part).astype(jnp.bfloat16)
    keys_low = (
        rotate(key_proj, cos_part, sin_part)
        .astype(jnp.bfloat16)
        .reshape(slot_count, seq_count, heads_kv * HEAD)
    )
    query_seq = jnp.transpose(
        queries.reshape(slot_count, seq_count, heads_kv, group_size, HEAD), (1, 2, 3, 0, 4)
    )
    query_pos = positions.T
    stat_shape = (seq_count, heads_kv, group_size, slot_count)
    initial = (
        jnp.full(stat_shape, masked_value, jnp.float32),
        jnp.zeros(stat_shape, jnp.float32),
        jnp.zeros(stat_shape + (HEAD,), jnp.float32),
    )
    key_piece = lax.all_gather(keys_low, "context", axis=0, tiled=True)
    value_piece = lax.all_gather(value_low, "context", axis=0, tiled=True)
    pos_piece = lax.all_gather(positions, "context", axis=0, tiled=True)
    piece_len = key_piece.shape[0]
    key_seq = jnp.transpose(key_piece.reshape(piece_len, seq_count, heads_kv, HEAD), (1, 2, 0, 3))
    value_seq = jnp.transpose(
        value_piece.reshape(piece_len, seq_count, heads_kv, HEAD), (1, 2, 0, 3)
    )
    pos_seq = pos_piece.T

    def per_sequence(seq_items):
        peak_val, totals, accum_vals, query_one, qpos_one, key_one, value_one, kpos_one = seq_items
        raw_scores = (
            jnp.einsum("hgqd,hkd->hgqk", query_one, key_one, preferred_element_type=jnp.float32)
            * score_scale
        )
        allowed = kpos_one[None, None, None, :] <= qpos_one[None, None, :, None]
        masked = jnp.where(allowed, raw_scores, masked_value)
        new_peak = jnp.maximum(peak_val, jnp.max(masked, axis=-1))
        decay_vals = jnp.exp(peak_val - new_peak)
        weights = jnp.where(allowed, jnp.exp(masked - new_peak[..., None]), 0.0)
        totals = totals * decay_vals + jnp.sum(weights, axis=-1)
        accum_vals = accum_vals * decay_vals[..., None] + jnp.einsum(
            "hgqk,hkd->hgqd",
            weights.astype(jnp.bfloat16),
            value_one,
            preferred_element_type=jnp.float32,
        )
        return (new_peak, totals, accum_vals)

    peak_val, totals, accum_vals = lax.map(
        per_sequence,
        (initial[0], initial[1], initial[2], query_seq, query_pos, key_seq, value_seq, pos_seq),
    )
    log_total = peak_val + jnp.log(totals)
    mixed_seq = accum_vals / totals[..., None]
    mixed_low = (
        jnp.transpose(mixed_seq, (3, 0, 1, 2, 4))
        .reshape(row_count, heads_q * HEAD)
        .astype(jnp.bfloat16)
    )
    branch = lax.psum(
        jnp.dot(mixed_low, out_mat, preferred_element_type=jnp.float32).astype(jnp.bfloat16),
        "tensor",
    ).astype(jnp.float32)
    middle = flat_in + branch
    unit_two, inverse_two, second = norm_forward(middle, full_two)
    gate_vals = jnp.dot(second, gate_mat, preferred_element_type=jnp.float32)
    up_vals = jnp.dot(second, up_mat, preferred_element_type=jnp.float32)
    sigmoid_vals = jax.nn.sigmoid(gate_vals)
    silu_vals = gate_vals * sigmoid_vals
    hidden = (silu_vals * up_vals).astype(jnp.bfloat16)
    mlp_part = lax.psum(
        jnp.dot(hidden, down_mat, preferred_element_type=jnp.float32).astype(jnp.bfloat16), "tensor"
    ).astype(jnp.float32)
    layer_out = (middle + mlp_part).astype(jnp.bfloat16).reshape(slot_count, seq_count, model_width)
    regathered = (
        lax.all_gather(gain_one, ("dp", "context"), axis=0, tiled=True),
        lax.all_gather(gain_two, ("dp", "context"), axis=0, tiled=True),
        lax.all_gather(w_query, ("dp", "context"), axis=0, tiled=True),
        lax.all_gather(w_key, ("dp", "context"), axis=0, tiled=True),
        lax.all_gather(w_value, ("dp", "context"), axis=0, tiled=True),
        lax.all_gather(w_out, ("dp", "context"), axis=1, tiled=True),
        lax.all_gather(w_gate, ("dp", "context"), axis=0, tiled=True),
        lax.all_gather(w_up, ("dp", "context"), axis=0, tiled=True),
        lax.all_gather(w_down, ("dp", "context"), axis=1, tiled=True),
    )
    full_one, full_two, query_mat, key_mat, value_mat, out_mat, gate_mat, up_mat, down_mat = (
        regathered
    )
    grad_low = cotangent.reshape(row_count, model_width)
    grad_down = contract_rows(hidden, grad_low)
    grad_hidden = contract_cols(grad_low, down_mat)
    grad_gate_low = (
        grad_hidden * up_vals * sigmoid_vals * (1.0 + gate_vals * (1.0 - sigmoid_vals))
    ).astype(jnp.bfloat16)
    grad_up_low = (grad_hidden * silu_vals).astype(jnp.bfloat16)
    grad_gate = contract_rows(second, grad_gate_low)
    grad_up = contract_rows(second, grad_up_low)
    grad_second = lax.psum(
        (contract_cols(grad_gate_low, gate_mat) + contract_cols(grad_up_low, up_mat)).astype(
            jnp.bfloat16
        ),
        "tensor",
    ).astype(jnp.float32)
    grad_mid_norm, grad_gain_two = norm_backward(grad_second, unit_two, inverse_two, full_two)
    grad_middle = grad_low.astype(jnp.float32) + grad_mid_norm
    grad_mid_low = grad_middle.astype(jnp.bfloat16)
    grad_out = contract_rows(mixed_low, grad_mid_low)
    grad_mixed = contract_cols(grad_mid_low, out_mat).astype(jnp.bfloat16)
    grad_mixed_seq = jnp.transpose(
        grad_mixed.reshape(slot_count, seq_count, heads_kv, group_size, HEAD), (1, 2, 3, 0, 4)
    )
    delta_rows = jnp.sum(grad_mixed_seq.astype(jnp.float32) * mixed_seq, axis=-1)
    kv_width = heads_kv * HEAD

    def block_grads(grad_query_acc, key_blk, value_blk, pos_blk):
        block_len = key_blk.shape[0]
        key_seq = jnp.transpose(key_blk.reshape(block_len, seq_count, heads_kv, HEAD), (1, 2, 0, 3))
        value_seq = jnp.transpose(
            value_blk.reshape(block_len, seq_count, heads_kv, HEAD), (1, 2, 0, 3)
        )
        raw_scores = (
            jnp.einsum("shgqd,shkd->shgqk", query_seq, key_seq, preferred_element_type=jnp.float32)
            * score_scale
        )
        allowed = pos_blk.T[:, None, None, None, :] <= query_pos[:, None, None, :, None]
        prob_vals = jnp.where(
            allowed,
            jnp.exp(jnp.where(allowed, raw_scores - log_total[..., None], masked_value)),
            0.0,
        )
        grad_value_blk = jnp.einsum(
            "shgqk,shgqd->kshd",
            prob_vals.astype(jnp.bfloat16),
            grad_mixed_seq,
            preferred_element_type=jnp.float32,
        )
        grad_probs = jnp.einsum(
            "shgqd,shkd->shgqk", grad_mixed_seq, value_seq, preferred_element_type=jnp.float32
        )
        grad_scores = (prob_vals * (grad_probs - delta_rows[..., None])).astype(jnp.bfloat16)
        grad_query_acc = grad_query_acc + jnp.einsum(
            "shgqk,shkd->shgqd", grad_scores, key_seq, preferred_element_type=jnp.float32
        )
        grad_key_blk = jnp.einsum(
            "shgqk,shgqd->kshd", grad_scores, query_seq, preferred_element_type=jnp.float32
        )
        return (
            grad_query_acc,
            grad_key_blk.reshape(block_len, seq_count, kv_width),
            grad_value_blk.reshape(block_len, seq_count, kv_width),
        )

    zero_query = jnp.zeros(stat_shape + (HEAD,), jnp.float32)
    key_all, value_all, pos_all = (
        lax.all_gather(keys_low, "context", axis=0, tiled=True),
        lax.all_gather(value_low, "context", axis=0, tiled=True),
        lax.all_gather(positions, "context", axis=0, tiled=True),
    )
    total_len = key_all.shape[0]
    block_size = min(512, total_len)
    block_count = total_len // block_size

    def key_block(grad_query_acc, block_items):
        key_blk, value_blk, pos_blk = block_items
        grad_query_acc, grad_key_blk, grad_value_blk = block_grads(
            grad_query_acc, key_blk, value_blk, pos_blk
        )
        return (grad_query_acc, (grad_key_blk, grad_value_blk))

    grad_query_acc, (grad_keys_all, grad_values_all) = lax.scan(
        key_block,
        zero_query,
        (
            key_all.reshape(block_count, block_size, seq_count, kv_width),
            value_all.reshape(block_count, block_size, seq_count, kv_width),
            pos_all.reshape(block_count, block_size, seq_count),
        ),
    )
    grad_key_own, grad_value_own = (
        lax.psum_scatter(
            grad_keys_all.reshape(total_len, seq_count, kv_width).astype(jnp.bfloat16),
            "context",
            scatter_dimension=0,
            tiled=True,
        ).astype(jnp.float32),
        lax.psum_scatter(
            grad_values_all.reshape(total_len, seq_count, kv_width).astype(jnp.bfloat16),
            "context",
            scatter_dimension=0,
            tiled=True,
        ).astype(jnp.float32),
    )
    grad_rot_q = jnp.transpose(grad_query_acc * score_scale, (3, 0, 1, 2, 4)).reshape(
        slot_count, seq_count, heads_q, HEAD
    )
    grad_q_low = (
        rotate(grad_rot_q, cos_part, -sin_part)
        .reshape(row_count, heads_q * HEAD)
        .astype(jnp.bfloat16)
    )
    grad_rot_k = (grad_key_own * score_scale).reshape(slot_count, seq_count, heads_kv, HEAD)
    grad_k_low = (
        rotate(grad_rot_k, cos_part, -sin_part).reshape(row_count, kv_width).astype(jnp.bfloat16)
    )
    grad_v_low = grad_value_own.reshape(row_count, kv_width).astype(jnp.bfloat16)
    grad_query = contract_rows(normed, grad_q_low)
    grad_key = contract_rows(normed, grad_k_low)
    grad_value = contract_rows(normed, grad_v_low)
    grad_normed = lax.psum(
        (
            contract_cols(grad_q_low, query_mat)
            + contract_cols(grad_k_low, key_mat)
            + contract_cols(grad_v_low, value_mat)
        ).astype(jnp.bfloat16),
        "tensor",
    ).astype(jnp.float32)
    grad_in_norm, grad_gain_one = norm_backward(grad_normed, unit_one, inverse_one, full_one)
    input_grad = (grad_middle + grad_in_norm).reshape(slot_count, seq_count, model_width)
    reduced = (
        lax.psum_scatter(grad_gain_one, ("dp", "context"), scatter_dimension=0, tiled=True),
        lax.psum_scatter(grad_gain_two, ("dp", "context"), scatter_dimension=0, tiled=True),
        lax.psum_scatter(grad_query, ("dp", "context"), scatter_dimension=0, tiled=True),
        lax.psum_scatter(grad_key, ("dp", "context"), scatter_dimension=0, tiled=True),
        lax.psum_scatter(grad_value, ("dp", "context"), scatter_dimension=0, tiled=True),
        lax.psum_scatter(grad_out, ("dp", "context"), scatter_dimension=1, tiled=True),
        lax.psum_scatter(grad_gate, ("dp", "context"), scatter_dimension=0, tiled=True),
        lax.psum_scatter(grad_up, ("dp", "context"), scatter_dimension=0, tiled=True),
        lax.psum_scatter(grad_down, ("dp", "context"), scatter_dimension=1, tiled=True),
    )
    return (
        layer_out,
        input_grad,
        reduced[0],
        reduced[1],
        reduced[2],
        reduced[3],
        reduced[4],
        reduced[5],
        reduced[6],
        reduced[7],
        reduced[8],
    )


WIDE = 128
RUN = 256
TILE = 512
LOG2_E = 1.4426950408889634
MESH = pl.DeviceIdType.MESH
VMEM_LIMIT = 56 * 1024 * 1024


def any_spec():
    return pl.BlockSpec(memory_space=pl.ANY)


def vmem_spec():
    return pl.BlockSpec(memory_space=pltpu.VMEM)


def place():
    return lax.axis_index("dp"), lax.axis_index("context"), lax.axis_index("tensor")


def greet(devices):
    barrier = pltpu.get_barrier_semaphore()
    for device in devices:
        pl.semaphore_signal(barrier, inc=1, device_id=device, device_id_type=MESH)
    pl.semaphore_wait(barrier, len(devices))


def sequence_others():
    row, spot, core = place()
    return [
        (row, lax.rem(spot + shift, 8), lax.rem(core + flip, 2))
        for shift in range(8)
        for flip in range(2)
        if shift or flip
    ]


def spread_matrix():
    shape = (4 * HEAD, 4 * WIDE)
    rows = lax.broadcasted_iota(jnp.int32, shape, 0)
    cols = lax.broadcasted_iota(jnp.int32, shape, 1)
    head = 0
    for start in (1, 2, 3):
        head = head + jnp.where(rows >= start * HEAD, 1, 0)
    dims = rows - head * HEAD
    target = head * WIDE + dims + jnp.where(dims >= HEAD // 2, (WIDE - HEAD) // 2, 0)
    return jnp.where(cols == target, 1.0, 0.0).astype(jnp.bfloat16)


def lane_freqs():
    half = HEAD // 2
    inv_freqs = theta_base ** (-2.0 * jnp.arange(half, dtype=jnp.float32) / HEAD)
    gap = jnp.zeros((WIDE // 2 - half,), jnp.float32)
    return jnp.concatenate([inv_freqs, gap, inv_freqs, gap]).reshape(1, WIDE)


def dot_f32(left, right):
    return jnp.dot(left, right, preferred_element_type=jnp.float32)


def remote(source, target, send, recv, device):
    return pltpu.make_async_remote_copy(
        src_ref=source,
        dst_ref=target,
        send_sem=send,
        recv_sem=recv,
        device_id=device,
        device_id_type=MESH,
    )


def move(source, target, send, recv, device, is_self):
    @pl.when(is_self)
    def _():
        pltpu.make_async_copy(source, target, recv).start()

    @pl.when(jnp.logical_not(is_self))
    def _():
        remote(source, target, send, recv, device).start()


def return_copies(ref, out, send, recv):
    row, spot, core = place()
    head = 2 * lax.rem(spot, 4) + core
    owner = spot // 4
    copies = []
    for step in range(8):
        chip = lax.rem(spot + step, 8)
        is_self = (owner == core) if step == 0 else False
        parts = (ref.at[chip], out.at[head], send.at[step], recv.at[head], (row, chip, owner))
        copies.append((parts, is_self))
    return copies


def start_return(copies):
    for parts, is_self in copies:
        if is_self is False:
            remote(*parts).start()
        else:
            move(*parts, is_self)


def finish_return(copies, out, send, recv):
    row, spot, core = place()
    for head in range(8):
        remote(
            out.at[head], out.at[head], send.at[0], recv.at[head], (row, spot, 1 - core)
        ).wait_recv()
    for parts, is_self in copies:
        if is_self is False:
            remote(*parts).wait_send()
        else:

            @pl.when(jnp.logical_not(is_self))
            def _():
                remote(*parts).wait_send()


def tile_at(index, size):
    return pl.ds(pl.multiple_of(index * size, size), size)


def causal(scores):
    keys = lax.broadcasted_iota(jnp.int32, scores.shape, 0)
    queries = lax.broadcasted_iota(jnp.int32, scores.shape, 1)
    return jnp.where(keys <= queries, scores, masked_value)


def neighbours():
    row, spot, core = place()
    level, column = spot // 2, lax.rem(spot, 2)
    beside_x = (1 - row, spot, core)
    beside_y = (row, 2 * level + 1 - column, core)
    along_z = [(row, 2 * lax.rem(level + k, 4) + column, core) for k in (1, 2, 3)]
    return row, level, column, beside_x, beside_y, along_z


class Gather:
    def __init__(self, own, whole, start, width, piece, sems):
        self.own, self.whole = own.at[:, pl.ds(start, width)], whole
        self.start, self.width = start, width
        self.sems = [sem.at[piece] for sem in sems]

    def block(self, x, z, y, half=None):
        cut = self.width // 2 // WIDE * WIDE
        start, width = self.start, self.width
        if half == 0:
            width = cut
        elif half == 1:
            start, width = start + cut, width - cut
        return self.whole.at[x, z, y, :, pl.ds(start, width)]

    def arrived(self, target, recv_sem):
        device = neighbours()[3]
        remote(target, target, self.sems[0].at[0], recv_sem, device).wait_recv()

    def copies_z(self):
        send_z, recv_z = self.sems[:2]
        row, level, column, beside_x, beside_y, along_z = neighbours()
        mine = self.block(row, level, column)
        return [
            remote(self.own, mine, send_z.at[k], recv_z.at[k], along_z[k]) for k in range(3)
        ]

    def copies_xy(self, k):
        send_x, recv_x, send_y, recv_y = self.sems[2:6]
        row, level, column, beside_x, beside_y, along_z = neighbours()
        block = self.block(row, lax.rem(level + 4 - k, 4), column)
        source = self.own if k == 0 else block
        return [
            remote(source, block, send_x.at[k], recv_x.at[k], beside_x),
            remote(source, block, send_y.at[k], recv_y.at[k], beside_y),
        ]

    def copies_diagonal(self, k):
        send_d, recv_d = self.sems[6:8]
        row, level, column, beside_x, beside_y, along_z = neighbours()
        z = lax.rem(level + 4 - k, 4)
        by_y = self.block(1 - row, z, column, 1)
        by_x = self.block(row, z, 1 - column, 0)
        return [
            remote(by_y, by_y, send_d.at[0, k], recv_d.at[0, k], beside_y),
            remote(by_x, by_x, send_d.at[1, k], recv_d.at[1, k], beside_x),
        ]

    def open_z(self):
        for copy in self.copies_z():
            copy.start()

    def open_xy(self):
        row, level, column, beside_x, beside_y, along_z = neighbours()
        for copy in self.copies_xy(0):
            copy.start()
        pltpu.make_async_copy(self.own, self.block(row, level, column), self.sems[8]).start()

    def pass_on(self, k):
        row, level, column, beside_x, beside_y, along_z = neighbours()
        self.arrived(self.block(row, lax.rem(level + 4 - k, 4), column), self.sems[1].at[k - 1])
        for copy in self.copies_xy(k):
            copy.start()

    def diagonal(self, k):
        recv_x, recv_y = self.sems[3], self.sems[5]
        row, level, column, beside_x, beside_y, along_z = neighbours()
        z = lax.rem(level + 4 - k, 4)
        by_y, by_x = self.copies_diagonal(k)
        self.arrived(self.block(1 - row, z, column), recv_x.at[k])
        by_y.start()
        self.arrived(self.block(row, z, 1 - column), recv_y.at[k])
        by_x.start()

    def finish(self):
        recv_d, local = self.sems[7:]
        row, level, column, beside_x, beside_y, along_z = neighbours()
        for k in range(4):
            z = lax.rem(level + 4 - k, 4)
            self.arrived(self.block(1 - row, z, 1 - column, 1), recv_d.at[0, k])
            self.arrived(self.block(1 - row, z, 1 - column, 0), recv_d.at[1, k])
        mine = self.block(row, level, column)
        pltpu.make_async_copy(self.own, mine, local).wait()

    def close(self):
        for copy in self.copies_z():
            copy.wait_send()
        for k in range(4):
            for copy in self.copies_xy(k) + self.copies_diagonal(k):
                copy.wait_send()


def gather_sems(pieces):
    dma = pltpu.SemaphoreType.DMA
    shapes = [(3,), (3,), (4,), (4,), (4,), (4,), (2, 4), (2, 4), ()]
    return [dma((pieces,) + shape) for shape in shapes]


def forward_kernel(
    tokens,
    positions,
    freqs,
    ids_in,
    gain_one,
    gain_two,
    w_query,
    w_key,
    w_value,
    w_out_t,
    w_gate,
    w_up,
    w_down_t,
    near,
    far,
    normed_out,
    q_out,
    k_out,
    v_out,
    mixed_t_out,
    lse_out,
    mixed_low_out,
    middle_out,
    second_out,
    hidden_out,
    gate_out,
    up_out,
    gains_out,
    tables_out,
    order,
    ids_flat,
    near_own,
    far_own,
    unit,
    normed,
    spread,
    tables,
    weight,
    extras,
    gain_rows,
    q_heads,
    kv_heads,
    q_slots,
    kv_slots,
    q,
    q_t,
    keys,
    v,
    v_t,
    mixed_t,
    lse,
    mixed,
    mixed_slots,
    mixed_heads,
    mixed_low,
    out_weight,
    part,
    part_other,
    second,
    hidden,
    pair_weight,
    pair_values,
    ids_all,
    ids,
    load_own,
    send_ids,
    recv_ids,
    load_ids,
    load_w,
    load_extra,
    load_out,
    load_pair,
    save_pair,
    saves,
    send_q,
    recv_q,
    send_kv,
    recv_kv,
    send_x,
    recv_x,
    send_m,
    recv_m,
    send_p,
    recv_p,
    *sems,
):
    row, spot, core = place()
    low, full = jnp.bfloat16, jnp.float32
    rows, width = tokens.shape
    share = near_own.shape[0]
    length = 8 * rows
    runs, tiles = length // RUN, length // TILE
    per_device = rows // RUN
    halves = TILE // RUN
    quarter = 4 * share
    sibling = (row, spot, 1 - core)
    hidden_width = w_gate.shape[1]
    out_width = w_out_t.shape[1]
    qkv_width = 16 * HEAD

    near_loads, far_loads, start = [], [], 0
    for ref in (w_query, w_key, w_value, w_out_t):
        target = near_own.at[:, pl.ds(start, ref.shape[1])]
        near_loads.append(pltpu.make_async_copy(ref, target, load_own.at[len(near_loads)]))
        start += ref.shape[1]
    for index, ref in enumerate((w_gate, w_up, w_down_t)):
        target = far_own.at[:, pl.ds(index * hidden_width, hidden_width)]
        far_loads.append(pltpu.make_async_copy(ref, target, load_own.at[4 + index]))
    for copy in near_loads + far_loads:
        copy.start()
    line = lax.broadcasted_iota(jnp.int32, (WIDE, share), 0)
    gains = jnp.where(line == 0, gain_one[...].astype(full), 0.0)
    gains = jnp.where(line == 1, gain_two[...].astype(full), gains)
    near_own[:, qkv_width + out_width :] = gains.T.astype(low)

    near_gather = Gather(near_own, near, 0, near_own.shape[1], 0, sems)
    far_gathers = [
        Gather(far_own, far, index * hidden_width, hidden_width, index + 1, sems)
        for index in range(3)
    ]
    greet(sequence_others() + [neighbours()[3]])
    for copy in near_loads:
        copy.wait()
    near_gather.open_z()
    near_gather.open_xy()

    for shift in range(1, 8):
        remote(
            ids_in,
            ids_all.at[spot],
            send_ids.at[shift],
            recv_ids.at[shift],
            (row, lax.rem(spot + shift, 8), core),
        ).start()
    ids_all[spot] = ids_in[...]

    values = tokens[...].astype(full)
    unit[...] = values * lax.rsqrt(jnp.mean(values * values, axis=-1, keepdims=True) + epsilon)
    spread[...] = spread_matrix()
    angles = positions[...].astype(full) * freqs[...]
    sign = jnp.where(lax.broadcasted_iota(jnp.int32, (1, WIDE), 1) < WIDE // 2, -1.0, 1.0)
    tables[0] = jnp.cos(angles)
    tables[1] = jnp.sin(angles) * sign
    for copy in far_loads:
        copy.wait()

    for k in range(1, 4):
        near_gather.pass_on(k)
        near_gather.diagonal(k - 1)
        if k == 1:
            far_gathers[0].open_z()
        if k == 3:
            far_gathers[1].open_z()
    far_gathers[0].open_xy()
    near_gather.diagonal(3)
    for shift in range(1, 8):
        remote(
            ids_in,
            ids_all.at[lax.rem(spot + 8 - shift, 8)],
            send_ids.at[shift],
            recv_ids.at[shift],
            (row, lax.rem(spot + shift, 8), core),
        ).wait_recv()
    pltpu.make_async_copy(ids_all, ids, load_ids).start()
    far_gathers[0].pass_on(1)
    near_gather.finish()

    def load_group(group):
        lanes = pl.ds(group * 4 * HEAD, 4 * HEAD)
        return pltpu.make_async_copy(
            near.at[:, :, :, :, lanes], weight.at[group % 2], load_w.at[group % 2]
        )

    load_extras = pltpu.make_async_copy(
        near.at[:, :, :, :, pl.ds(qkv_width + out_width, WIDE)], extras, load_extra
    )
    load_out_weight = pltpu.make_async_copy(
        near.at[:, :, :, :, pl.ds(qkv_width, out_width)], out_weight, load_out
    )
    load_extras.start()
    load_group(0).start()
    load_group(1).start()
    load_out_weight.start()
    load_extras.wait()
    gain_rows[...] = extras[...].reshape(width, WIDE).T[0:8].astype(full)
    normed[...] = (unit[...] * gain_rows[0:1]).astype(low)
    for group in range(4):
        load_group(group).wait()
        wide = dot_f32(weight[group % 2].reshape(width, 4 * HEAD), spread[...]).astype(low)
        if group < 2:
            load_group(group + 2).start()
        proj = dot_f32(normed[...], wide)
        for head in range(4):
            value = proj[:, head * WIDE : (head + 1) * WIDE]
            if group < 3:
                value = value * tables[0] + pltpu.roll(value, WIDE // 2, 1) * tables[1]
            value = value.astype(low).reshape(per_device, RUN, WIDE)
            if group < 2:
                q_heads[4 * group + head] = value
            else:
                kv_heads[head, group - 2] = value

    outgoing = []
    for step in range(4):
        slot = lax.rem(spot + step, 4)
        chip = 4 * core + slot
        for other in range(2):
            is_self = jnp.logical_and(chip == spot, core == other)
            device = (row, chip, other)
            kv_parts = (
                kv_heads.at[slot, :, other],
                kv_slots.at[spot, :, other],
                send_kv.at[step, other],
                recv_kv.at[spot],
                device,
            )
            q_parts = (
                q_heads.at[2 * slot + other],
                q_slots.at[spot],
                send_q.at[step, other],
                recv_q.at[spot],
                device,
            )
            outgoing.append((kv_parts, is_self))
            outgoing.append((q_parts, is_self))
    for parts, is_self in outgoing:
        move(*parts, is_self)
    far_gathers[0].pass_on(2)
    far_gathers[0].pass_on(3)
    far_gathers[1].open_xy()
    for k in range(4):
        far_gathers[0].diagonal(k)

    def hand_on(source):
        block = kv_slots.at[source, :, core]
        return remote(block, block, send_x.at[source], recv_x.at[source], sibling)

    for step in range(8):
        source = lax.rem(spot + step, 8)
        block = kv_slots.at[source, :, core]
        remote(block, block, send_x.at[source], recv_kv.at[source], sibling).wait_recv()
        hand_on(source).start()
    for step in range(8):
        remote(
            q_slots.at[step], q_slots.at[step], send_x.at[step], recv_q.at[step], sibling
        ).wait_recv()
        hand_on(step).wait()
    far_gathers[2].open_z()
    far_gathers[1].pass_on(1)

    pltpu.make_async_copy(ids_all, ids, load_ids).wait()

    def find_run(index, carry):
        device, piece = 0, 0
        for run in range(runs):
            here = ids[run // per_device, 0, run % per_device] == index
            device = jnp.where(here, run // per_device, device)
            piece = jnp.where(here, run % per_device, piece)
        order[index, 0] = device
        order[index, 1] = piece
        found = ids[index // per_device, 0, index % per_device]
        order[runs + index, 0] = lax.div(found, per_device)
        order[runs + index, 1] = lax.rem(found, per_device)
        ids_flat[index] = found
        return carry

    lax.fori_loop(0, runs, find_run, 0)

    def sort_run(index, carry):
        device, piece = order[index, 0], order[index, 1]
        cols = tile_at(index, RUN)
        queries, values = q_slots[device, piece], kv_slots[device, 1, piece]
        q[cols] = queries
        q_t[:, cols] = queries.T
        keys[cols] = kv_slots[device, 0, piece]
        v[cols] = values
        v_t[:, cols] = values.T
        return carry

    lax.fori_loop(0, runs, sort_run, 0)
    scale = HEAD ** (-0.5) * LOG2_E

    def query_tile(index, carry):
        cols = tile_at(index, TILE)
        queries = q_t[:, cols]

        def step(scores, block, peak, total, mix):
            high = jnp.maximum(peak, jnp.max(scores, axis=0, keepdims=True))
            decay = jnp.exp2(peak - high)
            weights = jnp.exp2(scores - high)
            total = total * decay + jnp.sum(weights, axis=0, keepdims=True)
            mix = mix * decay + dot_f32(v_t[:, tile_at(block, TILE)], weights.astype(low))
            return high, total, mix

        def scores_of(block):
            return dot_f32(keys[tile_at(block, TILE)], queries) * scale

        state = (
            jnp.full((1, TILE), masked_value, full),
            jnp.zeros((1, TILE), full),
            jnp.zeros((WIDE, TILE), full),
        )
        state = step(causal(scores_of(index)), index, *state)
        peak, total, mix = lax.fori_loop(
            0, index, lambda block, now: step(scores_of(block), block, *now), state
        )
        mix = mix / total
        mixed_t[:, cols] = mix
        lse[:, cols] = peak + jnp.log2(total)
        for half in range(halves):
            mixed[index * halves + half] = mix[:, half * RUN : (half + 1) * RUN].T.astype(low)

        @pl.when(index == 2)
        def _():
            far_gathers[1].pass_on(2)

        @pl.when(index == 4)
        def _():
            far_gathers[1].pass_on(3)
            far_gathers[2].open_xy()

        for k in range(2):

            @pl.when(index == 5 + k)
            def _():
                far_gathers[1].diagonal(k)

        return carry

    lax.fori_loop(0, tiles, query_tile, 0)

    def unsort_run(run, carry):
        index = ids[run // per_device, 0, run % per_device]
        mixed_slots[run // per_device, run % per_device] = mixed[index]
        return carry

    lax.fori_loop(0, runs, unsort_run, 0)
    copies = return_copies(mixed_slots, mixed_heads, send_m, recv_m)
    start_return(copies)
    early_saves = [
        pltpu.make_async_copy(source, target, saves.at[index])
        for index, (source, target) in enumerate(
            [
                (normed, normed_out),
                (q, q_out),
                (keys, k_out),
                (v, v_out),
                (mixed_t, mixed_t_out),
                (lse, lse_out),
                (gain_rows, gains_out),
                (tables, tables_out),
            ]
        )
    ]
    for copy in early_saves:
        copy.start()
    far_gathers[1].diagonal(2)
    far_gathers[1].diagonal(3)
    for k in range(1, 4):
        far_gathers[2].pass_on(k)
    far_gathers[2].diagonal(0)
    finish_return(copies, mixed_heads, send_m, recv_m)

    load_out_weight.wait()
    for group in range(2):
        side = [mixed_heads[4 * group + head].reshape(rows, WIDE) for head in range(4)]
        narrow = contract_cols(jnp.concatenate(side, axis=1), spread[...])
        mixed_low[:, group * 4 * HEAD : (group + 1) * 4 * HEAD] = narrow.astype(low)

    def pair_copy(index):
        cut = pl.ds(index * quarter, quarter)
        return remote(
            part.at[:, cut], part_other.at[:, cut], send_p.at[index], recv_p.at[index], sibling
        )

    for index in range(4):
        block = out_weight[index // 2, 2 * (index % 2) : 2 * (index % 2) + 2]
        term = contract_cols(mixed_low[...], block.reshape(quarter, out_width))
        part[:, index * quarter : (index + 1) * quarter] = term.astype(low)
        pair_copy(index).start()
    far_gathers[0].finish()
    far_gathers[1].finish()

    def load_pair_weight(index, kind):
        lanes = pl.ds(pl.multiple_of(kind * hidden_width + index * PIECE, PIECE), PIECE)
        slot = lax.rem(index, 2)
        return pltpu.make_async_copy(
            far.at[:, :, :, :, lanes], pair_weight.at[slot, kind], load_pair.at[slot, kind]
        )

    for index in range(2):
        for kind in range(2):
            load_pair_weight(index, kind).start()
    for index in range(4):
        pair_copy(index).wait()
    chunk = rows // 8

    def norm_block(index, carry):
        cut = tile_at(index, chunk)
        sums = part[cut].astype(full) + part_other[cut].astype(full)
        values = tokens[cut].astype(full) + sums
        unit[cut] = values
        inverse = lax.rsqrt(jnp.mean(values * values, axis=-1, keepdims=True) + epsilon)
        second[cut] = (values * inverse * gain_rows[1:2]).astype(low)
        return carry

    lax.fori_loop(0, 8, norm_block, 0)
    late_saves = [
        pltpu.make_async_copy(source, target, saves.at[8 + index])
        for index, (source, target) in enumerate(
            [(mixed_low, mixed_low_out), (unit, middle_out), (second, second_out)]
        )
    ]
    for copy in late_saves:
        copy.start()

    count = hidden_width // PIECE

    def save_values(index, kind):
        lanes = pl.ds(pl.multiple_of(index * PIECE, PIECE), PIECE)
        slot = lax.rem(index, 2)
        target = (gate_out, up_out)[kind]
        return pltpu.make_async_copy(
            pair_values.at[slot, kind], target.at[:, lanes], save_pair.at[slot, kind]
        )

    def hidden_block(index, carry):
        slot = lax.rem(index, 2)

        @pl.when(index >= 2)
        def _():
            for kind in range(2):
                save_values(index - 2, kind).wait()

        for kind in range(2):
            load_pair_weight(index, kind).wait()
            pair_values[slot, kind] = dot_f32(
                second[...], pair_weight[slot, kind].reshape(width, PIECE)
            )

            @pl.when(index + 2 < count)
            def _():
                load_pair_weight(index + 2, kind).start()

        for kind in range(2):
            save_values(index, kind).start()
        gate, up = pair_values[slot, 0], pair_values[slot, 1]
        hidden[:, tile_at(index, PIECE)] = (gate * jax.nn.sigmoid(gate) * up).astype(low)

        for k in range(1, 4):

            @pl.when(index == 2 * k - 1)
            def _():
                far_gathers[2].diagonal(k)

        return carry

    lax.fori_loop(0, count, hidden_block, 0)
    save_hidden = pltpu.make_async_copy(hidden, hidden_out, saves.at[11])
    save_hidden.start()
    far_gathers[2].finish()
    for gather in [near_gather] + far_gathers:
        gather.close()
    for parts, is_self in outgoing:

        @pl.when(jnp.logical_not(is_self))
        def _():
            remote(*parts).wait_send()

    for shift in range(1, 8):
        remote(
            ids_in,
            ids_all.at[spot],
            send_ids.at[shift],
            recv_ids.at[shift],
            (row, lax.rem(spot + shift, 8), core),
        ).wait_send()
    for index in range(count - 2, count):
        for kind in range(2):
            save_values(index, kind).wait()
    for copy in early_saves + late_saves + [save_hidden]:
        copy.wait()


def forward(
    tokens,
    positions,
    ids,
    gain_one,
    gain_two,
    w_query,
    w_key,
    w_value,
    w_out_t,
    w_gate,
    w_up,
    w_down_t,
):
    dma = pltpu.SemaphoreType.DMA
    vmem = pltpu.VMEM
    low, full = jnp.bfloat16, jnp.float32
    rows, width = tokens.shape
    share, hidden_width = w_gate.shape
    out_width = w_out_t.shape[1]
    near_width = 16 * HEAD + out_width + WIDE
    length = 8 * rows
    per_device = rows // RUN
    heads = (8, per_device, RUN, WIDE)
    both = (2, per_device, RUN, WIDE)
    smem_spec = pl.BlockSpec(memory_space=pltpu.SMEM)
    shape = jax.ShapeDtypeStruct
    tall, flat = (length, WIDE), (WIDE, length)
    return pl.pallas_call(
        forward_kernel,
        in_specs=[vmem_spec()] * 6 + [any_spec()] * 7,
        out_specs=[any_spec()] * 16 + [smem_spec] * 2,
        out_shape=[
            shape((2, 4, 2, share, near_width), low),
            shape((2, 4, 2, share, 3 * hidden_width), low),
            shape((rows, width), low),
            shape(tall, low),
            shape(tall, low),
            shape(tall, low),
            shape(flat, full),
            shape((1, length), full),
            shape((rows, out_width), low),
            shape((rows, width), full),
            shape((rows, width), low),
            shape((rows, hidden_width), low),
            shape((rows, hidden_width), full),
            shape((rows, hidden_width), full),
            shape((8, width), full),
            shape((2, rows, WIDE), full),
            shape((2 * length // RUN, 2), jnp.int32),
            shape((length // RUN,), jnp.int32),
        ],
        scratch_shapes=[
            vmem((share, near_width), low),
            vmem((share, 3 * hidden_width), low),
            vmem((rows, width), full),
            vmem((rows, width), low),
            vmem((4 * HEAD, 4 * WIDE), low),
            vmem((2, rows, WIDE), full),
            vmem((2, 2, 4, 2, share, 4 * HEAD), low),
            vmem((2, 4, 2, share, WIDE), low),
            vmem((8, width), full),
            vmem(heads, low),
            vmem((4,) + both, low),
            vmem(heads, low),
            vmem((8,) + both, low),
            vmem(tall, low),
            vmem(flat, low),
            vmem(tall, low),
            vmem(tall, low),
            vmem(flat, low),
            vmem(flat, full),
            vmem((1, length), full),
            vmem((length // RUN, RUN, WIDE), low),
            vmem(heads, low),
            vmem(heads, low),
            vmem((rows, out_width), low),
            vmem((2, 4, 2, share, out_width), low),
            vmem((rows, width), low),
            vmem((rows, width), low),
            vmem((rows, width), low),
            vmem((rows, hidden_width), low),
            vmem((2, 2, 2, 4, 2, share, PIECE), low),
            vmem((2, 2, rows, PIECE), full),
            vmem((8, 8, WIDE), jnp.int32),
            pltpu.SMEM((8, 8, WIDE), jnp.int32),
            dma((7,)),
            dma((8,)),
            dma((8,)),
            dma(()),
            dma((2,)),
            dma(()),
            dma(()),
            dma((2, 2)),
            dma((2, 2)),
            dma((12,)),
            dma((4, 2)),
            dma((8,)),
            dma((4, 2)),
            dma((8,)),
            dma((8,)),
            dma((8,)),
            dma((8,)),
            dma((8,)),
            dma((4,)),
            dma((4,)),
        ]
        + gather_sems(4),
        compiler_params=pltpu.CompilerParams(
            collective_id=1, has_side_effects=True, vmem_limit_bytes=VMEM_LIMIT
        ),
        name="forward",
    )(
        tokens,
        positions,
        lane_freqs(),
        ids,
        gain_one,
        gain_two,
        w_query,
        w_key,
        w_value,
        w_out_t,
        w_gate,
        w_up,
        w_down_t,
    )


PIECE = 256
SECOND, THIRD, LAST = 2, 3, 4


class Reduce:
    def __init__(self, n, changes, refs):
        (
            self.left_t,
            self.right,
            self.gains,
            self.own,
            self.out,
            self.save,
            self.send_one,
            self.recv_one,
            self.send_two,
            self.recv_two,
            self.kept,
            self.recv_three,
            self.ss_one,
            self.rs_one,
            self.ss_two,
            self.rs_two,
            self.ss_three,
            self.rs_three,
        ) = refs
        self.n, self.changes = n, changes
        self.share = self.own.shape[1]

    def columns(self, step, kind):
        held = self.right.shape[1] // (2 * PIECE)
        start = lax.rem(step, held) * 2 * PIECE + kind * PIECE
        return pl.ds(pl.multiple_of(start, PIECE), PIECE)

    def saving(self, step):
        slot = lax.rem(step, 2)
        cut = pl.ds(pl.multiple_of(step * 2 * PIECE, 2 * PIECE), 2 * PIECE)
        return pltpu.make_async_copy(self.own.at[slot], self.out.at[:, cut], self.save.at[slot])

    def product(self, step, kind, x, y):
        left = 0
        for start in self.changes:
            left = left + jnp.where(step >= start, 1, 0)
        term = jnp.dot(
            self.left_t[lax.rem(left, 2), x, y],
            self.right[:, self.columns(step, kind)],
            preferred_element_type=jnp.float32,
        )
        if kind == 1:
            term = jnp.where(step == self.n - 1, self.gains[x, y].astype(jnp.float32), term)
        return term

    def first_copy(self, step, kind):
        beside_x, beside_y = neighbours()[3:5]
        out, into = lax.rem(step, 3), lax.rem(step, 4)
        return remote(
            self.send_one.at[out, kind],
            self.recv_one.at[into, kind],
            self.ss_one.at[out, kind],
            self.rs_one.at[into, kind],
            beside_x if kind == 0 else beside_y,
        )

    def second_copy(self, step, kind):
        beside_x, beside_y = neighbours()[3:5]
        out, into = lax.rem(step, 2), lax.rem(step, 4)
        return remote(
            self.send_two.at[out, kind],
            self.recv_two.at[into, kind],
            self.ss_two.at[out, kind],
            self.rs_two.at[into, kind],
            beside_y if kind == 0 else beside_x,
        )

    def third_copy(self, step, kind, k):
        row, level, column, beside_x, beside_y, along_z = neighbours()
        target = lax.rem(level + k + 1, 4)
        out, into = lax.rem(step, 3), lax.rem(step, 4)
        return remote(
            self.kept.at[out, kind, pl.ds(pl.multiple_of(target * self.share, 16), self.share)],
            self.recv_three.at[into, kind, k],
            self.ss_three.at[out, kind, k],
            self.rs_three.at[into, kind, k],
            along_z[k],
        )

    def first(self, step):
        row, level, column = neighbours()[:3]
        slot = lax.rem(step, 3)
        for half in range(2):
            self.send_one[slot, 0, half] = self.product(step, 0, 1 - row, half).astype(jnp.bfloat16)
        self.first_copy(step, 0).start()
        for half in range(2):
            self.send_one[slot, 1, half] = self.product(step, 1, half, 1 - column).astype(
                jnp.bfloat16
            )
        self.first_copy(step, 1).start()

    def second(self, step):
        row, level, column = neighbours()[:3]
        slot, came, keep = lax.rem(step, 2), lax.rem(step, 4), lax.rem(step, 3)
        for kind in range(2):
            self.first_copy(step, kind).wait()
        for kind in range(2):
            away_at = (row, 1 - column) if kind == 0 else (1 - row, column)
            arrived = self.recv_one.at[came, kind]
            away = self.product(step, kind, *away_at) + arrived[away_at[1 - kind]].astype(
                jnp.float32
            )
            self.send_two[slot, kind] = away.astype(jnp.bfloat16)
            here = self.product(step, kind, row, column) + arrived[
                column if kind == 0 else row
            ].astype(jnp.float32)
            self.kept[keep, kind] = here.astype(jnp.bfloat16)
        for kind in range(2):
            self.second_copy(step, kind).start()

    def third(self, step):
        came, keep = lax.rem(step, 4), lax.rem(step, 3)
        for kind in range(2):
            self.second_copy(step, kind).wait()
            here = self.kept[keep, kind].astype(jnp.float32) + self.recv_two[came, kind].astype(
                jnp.float32
            )
            self.kept[keep, kind] = here.astype(jnp.bfloat16)
            for k in range(3):
                self.third_copy(step, kind, k).start()

    def last(self, step):
        level = neighbours()[1]
        came, keep = lax.rem(step, 4), lax.rem(step, 3)
        mine = pl.ds(pl.multiple_of(level * self.share, 16), self.share)

        @pl.when(step >= 2)
        def _():
            self.saving(step - 2).wait()

        for kind in range(2):
            total = self.kept[keep, kind, mine].astype(jnp.float32)
            for k in range(3):
                self.third_copy(step, kind, k).wait()
                total = total + self.recv_three[came, kind, k].astype(jnp.float32)
            self.own[lax.rem(step, 2), :, kind * PIECE : (kind + 1) * PIECE] = total
        self.saving(step).start()

    def turn(self, step):
        for stage, lag in (
            (self.first, 0),
            (self.second, SECOND),
            (self.third, THIRD),
            (self.last, LAST),
        ):

            @pl.when(jnp.logical_and(step >= lag, step < self.n + lag))
            def _():
                stage(step - lag)


def backward_kernel(
    order,
    ids,
    q_in,
    k_in,
    v_in,
    mixed_t_in,
    lse_in,
    cotangent,
    second_in,
    normed_in,
    hidden_in,
    gate_in,
    up_in,
    mixed_low,
    middle,
    near,
    far,
    tokens,
    gains_in,
    tables,
    input_grad,
    layer_out,
    grads,
    q,
    q_t,
    k,
    k_t,
    v,
    d_own,
    d_slots,
    d,
    d_t,
    dq_t,
    lse,
    delta,
    dk,
    dv,
    dkv_slots,
    dkv_other,
    dq_own,
    dkv_own,
    spread,
    weight,
    row_weight,
    values_ring,
    part,
    part_other,
    total,
    staged,
    grad_mid,
    gain_two_grad,
    left_t,
    right,
    gains,
    own,
    send_one,
    recv_one,
    send_two,
    recv_two,
    kept,
    recv_three,
    loads,
    load_left_sem,
    load_w,
    load_rows,
    load_values,
    save_sem,
    send_d,
    recv_d,
    send_q,
    recv_q,
    send_x,
    recv_x,
    send_k,
    recv_k,
    send_p,
    recv_p,
    save,
    *sems,
):
    row, spot, core = place()
    low, full = jnp.bfloat16, jnp.float32
    rows, width = staged.shape
    length = 8 * rows
    runs, tiles = length // RUN, length // TILE
    per_device = rows // RUN
    halves = TILE // RUN
    share = width // 16
    quarter = 4 * share
    sibling = (row, spot, 1 - core)
    qkv_width = 16 * HEAD
    hidden_width = hidden_in.shape[1]
    out_width = mixed_low.shape[1]
    n = grads.shape[1] // (2 * PIECE)
    quarter_steps = hidden_width // (2 * PIECE)
    near_at = 3 * quarter_steps
    changes = (quarter_steps, near_at, near_at + qkv_width // (2 * PIECE))
    sums = Reduce(
        n,
        changes,
        (left_t, right, gains, own, grads, save)
        + (send_one, recv_one, send_two, recv_two, kept, recv_three)
        + sems,
    )

    def stage(source):
        return pltpu.make_async_copy(source, staged, load_left_sem)

    def turn_left(index, source):
        for piece in range(4):
            turned = source[:, piece * quarter : (piece + 1) * quarter].T
            for inner in range(4):
                x, z, y = piece // 2, 2 * (piece % 2) + inner // 2, inner % 2
                left_t[index % 2, x, y, z * share : (z + 1) * share] = turned[
                    inner * share : (inner + 1) * share
                ]

    early_loads = [
        pltpu.make_async_copy(source, target, loads.at[index])
        for index, (source, target) in enumerate(
            [
                (hidden_in, right.at[:, pl.ds(0, hidden_width)]),
                (q_in, q),
                (k_in, k),
                (v_in, v),
                (mixed_t_in, dq_t),
                (lse_in, lse),
                (middle, total),
            ]
        )
    ]


    count = hidden_width // PIECE

    def load_down(index):
        lanes = pl.ds(pl.multiple_of(2 * hidden_width + index * PIECE, PIECE), PIECE)
        slot = lax.rem(index, 4)
        return pltpu.make_async_copy(
            far.at[:, :, :, :, lanes],
            weight.at[slot, :, :, :, :, pl.ds(0, PIECE)],
            load_w.at[slot],
        )

    def load_value(index, kind):
        lanes = pl.ds(pl.multiple_of(index * PIECE, PIECE), PIECE)
        slot = lax.rem(index, 2)
        return pltpu.make_async_copy(
            (gate_in, up_in)[kind].at[:, lanes],
            values_ring.at[slot, kind],
            load_values.at[slot, kind],
        )


    def load_block(index, which):
        lanes = pl.ds(which * hidden_width, hidden_width)
        levels = pl.ds(2 * lax.rem(index, 2), 2)
        slot = which % 2
        return pltpu.make_async_copy(
            far.at[index // 2, levels, :, :, lanes], row_weight.at[slot], load_rows.at[slot]
        )

    def pair_copy(index, landing):
        cut = pl.ds(pl.multiple_of(index * quarter, quarter), quarter)
        return remote(
            part.at[:, cut],
            part_other.at[landing, :, cut],
            send_p.at[index],
            recv_p.at[landing, index],
            sibling,
        )

    def feed_back():
        spread[...] = spread_matrix()

        def block(index, carry):
            slot = lax.rem(index, 2)
            load_down(index).wait()
            grad_hidden = dot_f32(
                staged[...],
                weight[lax.rem(index, 4), :, :, :, :, :PIECE].reshape(width, PIECE),
            )

            @pl.when(index + 4 < count)
            def _():
                load_down(index + 4).start()

            for kind in range(2):
                load_value(index, kind).wait()
            gate, up = values_ring[slot, 0], values_ring[slot, 1]
            sigmoid = jax.nn.sigmoid(gate)
            grad_gate = grad_hidden * up * sigmoid * (1.0 + gate * (1.0 - sigmoid))
            grad_up = grad_hidden * (gate * sigmoid)
            cut = pl.ds(pl.multiple_of(hidden_width + index * PIECE, PIECE), PIECE)
            right[:, cut] = grad_gate.astype(low)
            cut = pl.ds(pl.multiple_of(2 * hidden_width + index * PIECE, PIECE), PIECE)
            right[:, cut] = grad_up.astype(low)

            @pl.when(index + 2 < count)
            def _():
                for kind in range(2):
                    load_value(index + 2, kind).start()

            return carry

        lax.fori_loop(0, count, block, 0)
        stage(second_in).start()

    def second_back():
        for which in range(2):
            load_block(0, which).start()
        stage(second_in).wait()
        turn_left(1, staged)
        stage(cotangent).start()

        def block(index, carry):
            term = jnp.zeros((rows, quarter), full)
            for which in range(2):
                load_block(index, which).wait()
                term = term + contract_cols(
                    right[:, (1 + which) * hidden_width : (2 + which) * hidden_width],
                    row_weight[which].reshape(quarter, hidden_width),
                )

                @pl.when(index + 1 < 4)
                def _():
                    load_block(index + 1, which).start()

            part[:, tile_at(index, quarter)] = term.astype(low)
            pair_copy(index, 0).start()
            return carry

        lax.fori_loop(0, 4, block, 0)
        for index in range(2):
            load_out_weight(index).start()

    def load_out_weight(index):
        lanes = pl.ds(qkv_width + index * 4 * HEAD, 4 * HEAD)
        return pltpu.make_async_copy(
            near.at[:, :, :, :, lanes], weight.at[index], load_w.at[index]
        )

    d_copies = []
    for step in range(4):
        slot = lax.rem(spot + step, 4)
        chip = 4 * core + slot
        for other in range(2):
            parts = (
                d_own.at[2 * slot + other],
                d_slots.at[spot],
                send_d.at[step, other],
                recv_d.at[spot],
                (row, chip, other),
            )
            d_copies.append((parts, jnp.logical_and(chip == spot, core == other)))

    def middle_back():
        for index in range(4):
            pair_copy(index, 0).wait()
        stage(cotangent).wait()
        early_loads[6].wait()
        chunk = rows // 8

        def block(index, gain_grad):
            cut = tile_at(index, chunk)
            grad = part[cut].astype(full) + part_other[0, cut].astype(full)
            values = total[cut]
            inverse = lax.rsqrt(jnp.mean(values * values, axis=-1, keepdims=True) + epsilon)
            unit = values * inverse
            scaled = grad * gains_in[1:2]
            mean = jnp.mean(scaled * unit, axis=-1, keepdims=True)
            result = staged[cut].astype(full) + inverse * (scaled - unit * mean)
            total[cut] = result
            grad_mid[cut] = result.astype(low)
            return gain_grad + jnp.sum(grad * unit, axis=0, keepdims=True)

        gain_two_grad[...] = lax.fori_loop(0, 8, block, jnp.zeros((1, width), full))
        for index in range(2):
            load_out_weight(index).wait()
            grad = dot_f32(grad_mid[...], weight[index].reshape(width, 4 * HEAD)).astype(low)
            wide = dot_f32(grad, spread[...]).astype(low)
            for head in range(4):
                value = wide[:, head * WIDE : (head + 1) * WIDE]
                d_own[4 * index + head] = value.reshape(per_device, RUN, WIDE)
        for parts, is_self in d_copies:
            move(*parts, is_self)


    def prepare():
        for copy in early_loads[1:6]:
            copy.wait()
        for index in range(tiles):
            cut = pl.ds(index * TILE, TILE)
            q_t[:, cut] = q[cut].T
            k_t[:, cut] = k[halves * index : halves * (index + 1)].reshape(TILE, WIDE).T

    def take_cotangents():
        for index in range(8):
            remote(
                d_slots.at[index], d_slots.at[index], send_d.at[0, 0], recv_d.at[index], sibling
            ).wait_recv()

        def sort_run(index, carry):
            cols = tile_at(index, RUN)
            run = d_slots[order[index, 0], order[index, 1]]
            turned = run.T
            d[index // per_device, index % per_device] = run
            d_t[:, cols] = turned
            delta[:, cols] = jnp.sum(turned.astype(full) * dq_t[:, cols], axis=0, keepdims=True)
            return carry

        lax.fori_loop(0, runs, sort_run, 0)
        dq_t[...] = jnp.zeros_like(dq_t)

    scale = HEAD ** (-0.5)

    def key_tile(block):
        cut = tile_at(block, TILE)
        both = pl.ds(block * halves, halves)
        keys, values = k[both].reshape(TILE, WIDE), v[both].reshape(TILE, WIDE)
        keys_t = k_t[:, cut]
        dk[...] = jnp.zeros_like(dk)
        dv[...] = jnp.zeros_like(dv)

        def query_tile(index, diagonal):
            cols = tile_at(index, TILE)
            scores = dot_f32(keys, q_t[:, cols]) * (scale * LOG2_E)
            if diagonal:
                scores = causal(scores)
            probs = jnp.exp2(scores - lse[:, cols])
            dv[...] += dot_f32(probs.astype(low), d[index].reshape(TILE, WIDE))
            grad_probs = dot_f32(values, d_t[:, cols])
            grad_scores = (probs * (grad_probs - delta[:, cols])).astype(low)
            dk[...] += dot_f32(grad_scores, q[cols])
            dq_t[:, cols] += dot_f32(keys_t, grad_scores)

        query_tile(block, True)

        def later(index, inner):
            query_tile(index, False)
            return inner

        lax.fori_loop(block + 1, tiles, later, 0)
        k[both] = (dk[...] * scale).astype(low).reshape(halves, RUN, WIDE)
        v[both] = dv[...].astype(low).reshape(halves, RUN, WIDE)

    def key_tiles(start, stop):
        def one(block, carry):
            key_tile(block)
            return carry

        lax.fori_loop(start, stop, one, 0)

    swap = remote(dkv_slots.at[:, :, 1 - core], dkv_other, send_x, recv_x, sibling)
    dq_copies = return_copies(d, dq_own, send_q, recv_q)
    slot, owner = lax.rem(spot, 4), spot // 4
    dkv_copies = []
    for step in range(8):
        chip = lax.rem(spot + step, 8)
        parts = (
            dkv_slots.at[:, chip, core],
            dkv_own.at[slot, :, core],
            send_k.at[step],
            recv_k.at[slot, core],
            (row, chip, owner),
        )
        dkv_copies.append((parts, (owner == core) if step == 0 else False))

    def send_back():
        def unsort_run(run, carry):
            index = ids[run]
            dkv_slots[0, run // per_device, run % per_device] = k[index]
            dkv_slots[1, run // per_device, run % per_device] = v[index]
            return carry

        lax.fori_loop(0, runs, unsort_run, 0)
        swap.start()

        def turn_run(index, carry):
            value = (dq_t[:, tile_at(index, RUN)] * scale).T
            d_slots[index // per_device, index % per_device] = value.astype(low)
            return carry

        lax.fori_loop(0, runs, turn_run, 0)

        def unsort_queries(run, carry):
            value = d_slots[order[runs + run, 0], order[runs + run, 1]]
            d[run // per_device, run % per_device] = value
            return carry

        lax.fori_loop(0, runs, unsort_queries, 0)
        start_return(dq_copies)

    def add_pairs():
        swap.wait()
        for chip in range(8):
            both = dkv_slots[:, chip, core].astype(full) + dkv_other[:, chip].astype(full)
            dkv_slots[:, chip, core] = both.astype(low)
        start_return(dkv_copies)


    def feed_forward():
        load_block(0, 2).start()

        def block(index, carry):
            load_block(index, 2).wait()
            term = contract_cols(
                right[:, :hidden_width], row_weight[0].reshape(quarter, hidden_width)
            )

            @pl.when(index + 1 < 4)
            def _():
                load_block(index + 1, 2).start()

            part[:, tile_at(index, quarter)] = term.astype(low)
            pair_copy(index, 1).start()
            return carry

        lax.fori_loop(0, 4, block, 0)
        for group in range(4):
            load_group(group).start()

    save_layer = pltpu.make_async_copy(part, layer_out, save_sem)

    def finish_layer():
        for index in range(4):
            pair_copy(index, 1).wait()
        pieces = width // PIECE

        def load_piece(index):
            lanes = pl.ds(index * PIECE, PIECE)
            return pltpu.make_async_copy(
                middle.at[:, lanes], values_ring.at[index % 2, 0], load_values.at[index % 2, 0]
            )

        load_piece(0).start()
        for index in range(pieces):
            if index + 1 < pieces:
                load_piece(index + 1).start()
            load_piece(index).wait()
            cut = pl.ds(index * PIECE, PIECE)
            value = part[:, cut].astype(full) + part_other[1, :, cut].astype(full)
            part[:, cut] = (value + values_ring[index % 2, 0]).astype(low)
        save_layer.start()


    def load_group(group):
        lanes = pl.ds(group * 4 * HEAD, 4 * HEAD)
        return pltpu.make_async_copy(
            near.at[:, :, :, :, lanes], weight.at[group], load_w.at[group]
        )

    load_mixed = pltpu.make_async_copy(
        mixed_low, right.at[:, pl.ds(qkv_width, out_width)], loads.at[0]
    )

    def project_back():
        load_mixed.start()
        for head in range(8):
            remote(
                dq_own.at[head], dq_own.at[head], send_q.at[0], recv_q.at[head], sibling
            ).wait_recv()
        for slot_in in range(4):
            for core_in in range(2):
                target = dkv_own.at[slot_in, :, core_in]
                remote(
                    target, target, send_k.at[0], recv_k.at[slot_in, core_in], sibling
                ).wait_recv()
        for group in range(4):
            turned = []
            for head in range(4):
                if group < 2:
                    value = dq_own[4 * group + head]
                else:
                    value = dkv_own[head, group - 2]
                value = value.reshape(rows, WIDE)
                if group < 3:
                    value = value.astype(full)
                    value = value * tables[0] - pltpu.roll(value, WIDE // 2, 1) * tables[1]
                    value = value.astype(low)
                turned.append(value)
            narrow = contract_cols(jnp.concatenate(turned, axis=1), spread[...])
            right[:, group * 4 * HEAD : (group + 1) * 4 * HEAD] = narrow.astype(low)
        start = qkv_width + out_width
        right[:, start : start + PIECE] = jnp.zeros((rows, PIECE), low)
        load_mixed.wait()

    def project_normed():
        save_layer.wait()
        for group in range(4):
            load_group(group).wait()
        stage(tokens).start()

        def block(index, carry):
            term = jnp.zeros((rows, quarter), full)
            for group in range(4):
                held = weight[group, index // 2, pl.ds(2 * lax.rem(index, 2), 2)]
                term = term + contract_cols(
                    right[:, group * 4 * HEAD : (group + 1) * 4 * HEAD],
                    held.reshape(quarter, 4 * HEAD),
                )
            part[:, tile_at(index, quarter)] = term.astype(low)
            pair_copy(index, 0).start()
            return carry

        lax.fori_loop(0, 4, block, 0)

    save_input = pltpu.make_async_copy(total, input_grad, save_sem)

    def norm_back():
        stage(tokens).wait()
        for index in range(4):
            pair_copy(index, 0).wait()
        chunk = rows // 8

        def block(index, gain_grad):
            cut = tile_at(index, chunk)
            grad = part[cut].astype(full) + part_other[0, cut].astype(full)
            values = staged[cut].astype(full)
            inverse = lax.rsqrt(jnp.mean(values * values, axis=-1, keepdims=True) + epsilon)
            unit = values * inverse
            scaled = grad * gains_in[0:1]
            mean = jnp.mean(scaled * unit, axis=-1, keepdims=True)
            total[cut] = total[cut] + inverse * (scaled - unit * mean)
            return gain_grad + jnp.sum(grad * unit, axis=0, keepdims=True)

        gain_one_grad = lax.fori_loop(0, 8, block, jnp.zeros((1, width), full))
        save_input.start()
        lines = []
        for value in (gain_one_grad, gain_two_grad[...]):
            high = value.astype(low).astype(full)
            lines.append((high, value - high))
        which = lax.broadcasted_iota(jnp.int32, (WIDE, width), 0)
        table = jnp.zeros((WIDE, width), full)
        for index, line in enumerate((lines[0][0], lines[1][0], lines[0][1], lines[1][1])):
            table = jnp.where(which == index, line, table)
        columns = table.T.astype(low)
        gains[...] = jnp.zeros_like(gains)
        for x in range(2):
            for z in range(4):
                for y in range(2):
                    start = ((x * 4 + z) * 2 + y) * share
                    gains[x, y, z * share : (z + 1) * share, :WIDE] = columns[start : start + share]

    def take_normed():
        stage(normed_in).start()
        stage(normed_in).wait()
        turn_left(2, staged)

    stage(cotangent).start()
    for copy in early_loads:
        copy.start()
    for index in range(4):
        load_down(index).start()
    for index in range(2):
        for kind in range(2):
            load_value(index, kind).start()
    greet(sequence_others() + [neighbours()[3]])
    stage(cotangent).wait()
    turn_left(0, staged)
    early_loads[0].wait()

    plan = {
        0: [feed_back],
        1: [second_back],
        2: [middle_back],
        3: [prepare],
        4: [take_cotangents],
        5: [lambda: key_tiles(0, 2)],
        6: [lambda: key_tiles(2, 4)],
        7: [lambda: key_tiles(4, 8), send_back],
        8: [add_pairs, feed_forward],
        9: [finish_layer, take_normed],
        10: [project_back],
        11: [project_normed],
        13: [norm_back],
        14: [lambda: turn_left(3, grad_mid)],
    }

    def run(step, carry):
        sums.turn(step)
        for when, tasks in plan.items():

            @pl.when(step == when)
            def _():
                for task in tasks:
                    task()

        return carry

    lax.fori_loop(0, n + LAST, run, 0)
    save_input.wait()
    for step in (n - 2, n - 1):
        sums.saving(step).wait()
    for copies in (d_copies, dq_copies, dkv_copies):
        for parts, is_self in copies:
            if is_self is False:
                remote(*parts).wait_send()
            else:

                @pl.when(jnp.logical_not(is_self))
                def _():
                    remote(*parts).wait_send()


def backward(order, ids, *arrays):
    dma = pltpu.SemaphoreType.DMA
    vmem = pltpu.VMEM
    low, full = jnp.bfloat16, jnp.float32
    q_sorted, k_sorted, v_sorted, mixed_t, lse, cotangent, second, normed, hidden = arrays[:9]
    gate, up, mixed_low, middle, near, far, tokens, gains, tables = arrays[9:]
    rows, width = cotangent.shape
    length = 8 * rows
    share = width // 16
    hidden_width = hidden.shape[1]
    wide = 3 * hidden_width + 16 * HEAD + mixed_low.shape[1] + PIECE
    quarter = 4 * share
    per_device = rows // RUN
    heads = (8, per_device, RUN, WIDE)
    tall, flat = (length, WIDE), (WIDE, length)
    by_run = (length // RUN, RUN, WIDE)
    block = (rows, width)
    smem_spec = pl.BlockSpec(memory_space=pltpu.SMEM)
    shape = jax.ShapeDtypeStruct
    return pl.pallas_call(
        backward_kernel,
        in_specs=[smem_spec] * 2 + [any_spec()] * 16 + [vmem_spec()] * 2,
        out_specs=[any_spec()] * 3,
        out_shape=[shape(block, full), shape(block, low), shape((share, wide), full)],
        scratch_shapes=[
            vmem(tall, low),
            vmem(flat, low),
            vmem(by_run, low),
            vmem(flat, low),
            vmem(by_run, low),
            vmem(heads, low),
            vmem(heads, low),
            vmem(heads, low),
            vmem(flat, low),
            vmem(flat, full),
            vmem((1, length), full),
            vmem((1, length), full),
            vmem((TILE, WIDE), full),
            vmem((TILE, WIDE), full),
            vmem((2,) + heads, low),
            vmem((2, 8, RUN, WIDE), low),
            vmem(heads, low),
            vmem((4, 2, per_device, RUN, WIDE), low),
            vmem((4 * HEAD, 4 * WIDE), low),
            vmem((4, 2, 4, 2, share, 4 * HEAD), low),
            vmem((2, 2, 2, share, hidden_width), low),
            vmem((2, 2, rows, PIECE), full),
            vmem(block, low),
            vmem((2,) + block, low),
            vmem(block, full),
            vmem(block, low),
            vmem(block, low),
            vmem((1, width), full),
            vmem((2, 2, 2, quarter, rows), low),
            vmem((rows, 3 * hidden_width), low),
            vmem((2, 2, quarter, PIECE), low),
            vmem((2, share, 2 * PIECE), full),
            vmem((3, 2, 2, quarter, PIECE), low),
            vmem((4, 2, 2, quarter, PIECE), low),
            vmem((2, 2, quarter, PIECE), low),
            vmem((4, 2, quarter, PIECE), low),
            vmem((3, 2, quarter, PIECE), low),
            vmem((4, 2, 3, share, PIECE), low),
            dma((7,)),
            dma(()),
            dma((4,)),
            dma((2,)),
            dma((2, 2)),
            dma(()),
            dma((4, 2)),
            dma((8,)),
            dma((8,)),
            dma((8,)),
            dma(()),
            dma(()),
            dma((8,)),
            dma((4, 2)),
            dma((4,)),
            dma((2, 4)),
            dma((2,)),
            dma((3, 2)),
            dma((4, 2)),
            dma((2, 2)),
            dma((4, 2)),
            dma((3, 2, 3)),
            dma((4, 2, 3)),
        ],
        compiler_params=pltpu.CompilerParams(
            collective_id=2, has_side_effects=True, vmem_limit_bytes=62 * 1024 * 1024
        ),
        name="backward",
    )(
        order,
        ids,
        q_sorted,
        k_sorted.reshape(by_run),
        v_sorted.reshape(by_run),
        *arrays[3:],
    )


def by_heads(
    tokens,
    positions,
    gain_one,
    gain_two,
    w_query,
    w_key,
    w_value,
    w_out,
    w_gate,
    w_up,
    w_down,
    cotangent,
):
    rows, _, width = tokens.shape
    share = gain_one.shape[0]
    run_ids = positions[::RUN, 0] // RUN
    flat_in = tokens.reshape(rows, width)
    (
        near,
        far,
        normed,
        q_sorted,
        k_sorted,
        v_sorted,
        mixed_t,
        lse,
        mixed_low,
        middle,
        second,
        hidden,
        gate_vals,
        up_vals,
        gains,
        tables,
        order,
        ids,
    ) = forward(
        flat_in,
        positions,
        jnp.broadcast_to(jnp.pad(run_ids, (0, WIDE - rows // RUN)), (8, WIDE)),
        gain_one.reshape(1, share),
        gain_two.reshape(1, share),
        w_query,
        w_key,
        w_value,
        w_out.T,
        w_gate,
        w_up,
        w_down.T,
    )
    input_grad, layer_out, grads = backward(
        order,
        ids,
        q_sorted,
        k_sorted,
        v_sorted,
        mixed_t,
        lse,
        cotangent.reshape(rows, width),
        second,
        normed,
        hidden,
        gate_vals,
        up_vals,
        mixed_low,
        middle,
        near,
        far,
        flat_in,
        gains,
        tables,
    )
    splits, start = [], 0
    for wide in (
        w_down.shape[0],
        w_gate.shape[1],
        w_up.shape[1],
        w_query.shape[1],
        w_key.shape[1],
        w_value.shape[1],
        w_out.shape[0],
        4,
    ):
        splits.append(grads[:, start : start + wide])
        start += wide
    grad_down, grad_gate, grad_up, grad_query, grad_key, grad_value, grad_out, grad_gains = splits
    return (
        layer_out.reshape(rows, 1, width),
        input_grad.reshape(rows, 1, width),
        grad_gains[:, 0] + grad_gains[:, 2],
        grad_gains[:, 1] + grad_gains[:, 3],
        grad_query,
        grad_key,
        grad_value,
        grad_out.T,
        grad_gate,
        grad_up,
        grad_down.T,
    )


def solution(mesh):
    sizes = (mesh.shape["dp"], mesh.shape["context"], mesh.shape["tensor"])
    return jax.shard_map(
        by_heads if sizes == (2, 8, 2) else on_device,
        mesh=mesh,
        in_specs=(
            P("context", "dp", None),
            P("context", "dp"),
            P(("dp", "context")),
            P(("dp", "context")),
            P(("dp", "context"), "tensor"),
            P(("dp", "context"), "tensor"),
            P(("dp", "context"), "tensor"),
            P("tensor", ("dp", "context")),
            P(("dp", "context"), "tensor"),
            P(("dp", "context"), "tensor"),
            P("tensor", ("dp", "context")),
            P("context", "dp", None),
        ),
        out_specs=(
            P("context", "dp", None),
            P("context", "dp", None),
            P(("dp", "context")),
            P(("dp", "context")),
            P(("dp", "context"), "tensor"),
            P(("dp", "context"), "tensor"),
            P(("dp", "context"), "tensor"),
            P("tensor", ("dp", "context")),
            P(("dp", "context"), "tensor"),
            P(("dp", "context"), "tensor"),
            P("tensor", ("dp", "context")),
        ),
        check_vma=False,
    )
```

```python
import functools

import jax
import jax.numpy as jnp
from jax import lax
from jax.experimental import pallas as pl
from jax.experimental.pallas import tpu as pltpu
from jax.sharding import PartitionSpec as P

HEAD = 96


epsilon = 1e-05
theta_base = 100000.0
masked_value = -1e30


def norm_forward(values_in, gain_vec):
    inverse = lax.rsqrt(jnp.mean(values_in * values_in, axis=-1, keepdims=True) + epsilon)
    unit_vals = values_in * inverse
    return (unit_vals, inverse, (unit_vals * gain_vec.astype(jnp.float32)).astype(jnp.bfloat16))


def norm_backward(grad_in, unit_vals, inverse, gain_vec):
    scaled = grad_in * gain_vec.astype(jnp.float32)
    grad_vals = inverse * (
        scaled - unit_vals * jnp.mean(scaled * unit_vals, axis=-1, keepdims=True)
    )
    return (grad_vals, jnp.sum(grad_in * unit_vals, axis=0))


def rotate(values_in, cos_part, sin_part):
    half_size = values_in.shape[-1] // 2
    front_half = values_in[..., :half_size]
    back_half = values_in[..., half_size:]
    return jnp.concatenate(
        [
            front_half * cos_part - back_half * sin_part,
            back_half * cos_part + front_half * sin_part,
        ],
        axis=-1,
    )


def contract_rows(left_mat, right_mat):
    return lax.dot_general(
        left_mat, right_mat, (((0,), (0,)), ((), ())), preferred_element_type=jnp.float32
    )


def contract_cols(left_mat, right_mat):
    return lax.dot_general(
        left_mat, right_mat, (((1,), (1,)), ((), ())), preferred_element_type=jnp.float32
    )


def on_device(
    tokens,
    positions,
    gain_one,
    gain_two,
    w_query,
    w_key,
    w_value,
    w_out,
    w_gate,
    w_up,
    w_down,
    cotangent,
):
    slot_count, seq_count, model_width = tokens.shape
    row_count = slot_count * seq_count
    gathered = (
        lax.all_gather(gain_one, ("dp", "context"), axis=0, tiled=True),
        lax.all_gather(gain_two, ("dp", "context"), axis=0, tiled=True),
        lax.all_gather(w_query, ("dp", "context"), axis=0, tiled=True),
        lax.all_gather(w_key, ("dp", "context"), axis=0, tiled=True),
        lax.all_gather(w_value, ("dp", "context"), axis=0, tiled=True),
        lax.all_gather(w_out, ("dp", "context"), axis=1, tiled=True),
        lax.all_gather(w_gate, ("dp", "context"), axis=0, tiled=True),
        lax.all_gather(w_up, ("dp", "context"), axis=0, tiled=True),
        lax.all_gather(w_down, ("dp", "context"), axis=1, tiled=True),
    )
    full_one, full_two, query_mat, key_mat, value_mat, out_mat, gate_mat, up_mat, down_mat = (
        gathered
    )
    heads_kv = key_mat.shape[1] // HEAD
    heads_q = query_mat.shape[1] // HEAD
    group_size = heads_q // heads_kv
    score_scale = HEAD ** (-0.5)
    half_size = HEAD // 2
    inv_freqs = theta_base ** (-2.0 * jnp.arange(half_size, dtype=jnp.float32) / HEAD)
    angles = positions.astype(jnp.float32)[:, :, None] * inv_freqs
    cos_part = jnp.cos(angles)[:, :, None, :]
    sin_part = jnp.sin(angles)[:, :, None, :]
    flat_in = tokens.astype(jnp.float32).reshape(row_count, model_width)
    unit_one, inverse_one, normed = norm_forward(flat_in, full_one)
    query_proj = jnp.dot(normed, query_mat, preferred_element_type=jnp.float32).reshape(
        slot_count, seq_count, heads_q, HEAD
    )
    key_proj = jnp.dot(normed, key_mat, preferred_element_type=jnp.float32).reshape(
        slot_count, seq_count, heads_kv, HEAD
    )
    value_low = (
        jnp.dot(normed, value_mat, preferred_element_type=jnp.float32)
        .astype(jnp.bfloat16)
        .reshape(slot_count, seq_count, heads_kv * HEAD)
    )
    queries = rotate(query_proj, cos_part, sin_part).astype(jnp.bfloat16)
    keys_low = (
        rotate(key_proj, cos_part, sin_part)
        .astype(jnp.bfloat16)
        .reshape(slot_count, seq_count, heads_kv * HEAD)
    )
    query_seq = jnp.transpose(
        queries.reshape(slot_count, seq_count, heads_kv, group_size, HEAD), (1, 2, 3, 0, 4)
    )
    query_pos = positions.T
    stat_shape = (seq_count, heads_kv, group_size, slot_count)
    initial = (
        jnp.full(stat_shape, masked_value, jnp.float32),
        jnp.zeros(stat_shape, jnp.float32),
        jnp.zeros(stat_shape + (HEAD,), jnp.float32),
    )
    key_piece = lax.all_gather(keys_low, "context", axis=0, tiled=True)
    value_piece = lax.all_gather(value_low, "context", axis=0, tiled=True)
    pos_piece = lax.all_gather(positions, "context", axis=0, tiled=True)
    piece_len = key_piece.shape[0]
    key_seq = jnp.transpose(key_piece.reshape(piece_len, seq_count, heads_kv, HEAD), (1, 2, 0, 3))
    value_seq = jnp.transpose(
        value_piece.reshape(piece_len, seq_count, heads_kv, HEAD), (1, 2, 0, 3)
    )
    pos_seq = pos_piece.T

    def per_sequence(seq_items):
        peak_val, totals, accum_vals, query_one, qpos_one, key_one, value_one, kpos_one = seq_items
        raw_scores = (
            jnp.einsum("hgqd,hkd->hgqk", query_one, key_one, preferred_element_type=jnp.float32)
            * score_scale
        )
        allowed = kpos_one[None, None, None, :] <= qpos_one[None, None, :, None]
        masked = jnp.where(allowed, raw_scores, masked_value)
        new_peak = jnp.maximum(peak_val, jnp.max(masked, axis=-1))
        decay_vals = jnp.exp(peak_val - new_peak)
        weights = jnp.where(allowed, jnp.exp(masked - new_peak[..., None]), 0.0)
        totals = totals * decay_vals + jnp.sum(weights, axis=-1)
        accum_vals = accum_vals * decay_vals[..., None] + jnp.einsum(
            "hgqk,hkd->hgqd",
            weights.astype(jnp.bfloat16),
            value_one,
            preferred_element_type=jnp.float32,
        )
        return (new_peak, totals, accum_vals)

    peak_val, totals, accum_vals = lax.map(
        per_sequence,
        (initial[0], initial[1], initial[2], query_seq, query_pos, key_seq, value_seq, pos_seq),
    )
    log_total = peak_val + jnp.log(totals)
    mixed_seq = accum_vals / totals[..., None]
    mixed_low = (
        jnp.transpose(mixed_seq, (3, 0, 1, 2, 4))
        .reshape(row_count, heads_q * HEAD)
        .astype(jnp.bfloat16)
    )
    branch = lax.psum(
        jnp.dot(mixed_low, out_mat, preferred_element_type=jnp.float32).astype(jnp.bfloat16),
        "tensor",
    ).astype(jnp.float32)
    middle = flat_in + branch
    unit_two, inverse_two, second = norm_forward(middle, full_two)
    gate_vals = jnp.dot(second, gate_mat, preferred_element_type=jnp.float32)
    up_vals = jnp.dot(second, up_mat, preferred_element_type=jnp.float32)
    sigmoid_vals = jax.nn.sigmoid(gate_vals)
    silu_vals = gate_vals * sigmoid_vals
    hidden = (silu_vals * up_vals).astype(jnp.bfloat16)
    mlp_part = lax.psum(
        jnp.dot(hidden, down_mat, preferred_element_type=jnp.float32).astype(jnp.bfloat16), "tensor"
    ).astype(jnp.float32)
    layer_out = (middle + mlp_part).astype(jnp.bfloat16).reshape(slot_count, seq_count, model_width)
    regathered = (
        lax.all_gather(gain_one, ("dp", "context"), axis=0, tiled=True),
        lax.all_gather(gain_two, ("dp", "context"), axis=0, tiled=True),
        lax.all_gather(w_query, ("dp", "context"), axis=0, tiled=True),
        lax.all_gather(w_key, ("dp", "context"), axis=0, tiled=True),
        lax.all_gather(w_value, ("dp", "context"), axis=0, tiled=True),
        lax.all_gather(w_out, ("dp", "context"), axis=1, tiled=True),
        lax.all_gather(w_gate, ("dp", "context"), axis=0, tiled=True),
        lax.all_gather(w_up, ("dp", "context"), axis=0, tiled=True),
        lax.all_gather(w_down, ("dp", "context"), axis=1, tiled=True),
    )
    full_one, full_two, query_mat, key_mat, value_mat, out_mat, gate_mat, up_mat, down_mat = (
        regathered
    )
    grad_low = cotangent.reshape(row_count, model_width)
    grad_down = contract_rows(hidden, grad_low)
    grad_hidden = contract_cols(grad_low, down_mat)
    grad_gate_low = (
        grad_hidden * up_vals * sigmoid_vals * (1.0 + gate_vals * (1.0 - sigmoid_vals))
    ).astype(jnp.bfloat16)
    grad_up_low = (grad_hidden * silu_vals).astype(jnp.bfloat16)
    grad_gate = contract_rows(second, grad_gate_low)
    grad_up = contract_rows(second, grad_up_low)
    grad_second = lax.psum(
        (contract_cols(grad_gate_low, gate_mat) + contract_cols(grad_up_low, up_mat)).astype(
            jnp.bfloat16
        ),
        "tensor",
    ).astype(jnp.float32)
    grad_mid_norm, grad_gain_two = norm_backward(grad_second, unit_two, inverse_two, full_two)
    grad_middle = grad_low.astype(jnp.float32) + grad_mid_norm
    grad_mid_low = grad_middle.astype(jnp.bfloat16)
    grad_out = contract_rows(mixed_low, grad_mid_low)
    grad_mixed = contract_cols(grad_mid_low, out_mat).astype(jnp.bfloat16)
    grad_mixed_seq = jnp.transpose(
        grad_mixed.reshape(slot_count, seq_count, heads_kv, group_size, HEAD), (1, 2, 3, 0, 4)
    )
    delta_rows = jnp.sum(grad_mixed_seq.astype(jnp.float32) * mixed_seq, axis=-1)
    kv_width = heads_kv * HEAD

    def block_grads(grad_query_acc, key_blk, value_blk, pos_blk):
        block_len = key_blk.shape[0]
        key_seq = jnp.transpose(key_blk.reshape(block_len, seq_count, heads_kv, HEAD), (1, 2, 0, 3))
        value_seq = jnp.transpose(
            value_blk.reshape(block_len, seq_count, heads_kv, HEAD), (1, 2, 0, 3)
        )
        raw_scores = (
            jnp.einsum("shgqd,shkd->shgqk", query_seq, key_seq, preferred_element_type=jnp.float32)
            * score_scale
        )
        allowed = pos_blk.T[:, None, None, None, :] <= query_pos[:, None, None, :, None]
        prob_vals = jnp.where(
            allowed,
            jnp.exp(jnp.where(allowed, raw_scores - log_total[..., None], masked_value)),
            0.0,
        )
        grad_value_blk = jnp.einsum(
            "shgqk,shgqd->kshd",
            prob_vals.astype(jnp.bfloat16),
            grad_mixed_seq,
            preferred_element_type=jnp.float32,
        )
        grad_probs = jnp.einsum(
            "shgqd,shkd->shgqk", grad_mixed_seq, value_seq, preferred_element_type=jnp.float32
        )
        grad_scores = (prob_vals * (grad_probs - delta_rows[..., None])).astype(jnp.bfloat16)
        grad_query_acc = grad_query_acc + jnp.einsum(
            "shgqk,shkd->shgqd", grad_scores, key_seq, preferred_element_type=jnp.float32
        )
        grad_key_blk = jnp.einsum(
            "shgqk,shgqd->kshd", grad_scores, query_seq, preferred_element_type=jnp.float32
        )
        return (
            grad_query_acc,
            grad_key_blk.reshape(block_len, seq_count, kv_width),
            grad_value_blk.reshape(block_len, seq_count, kv_width),
        )

    zero_query = jnp.zeros(stat_shape + (HEAD,), jnp.float32)
    key_all, value_all, pos_all = (
        lax.all_gather(keys_low, "context", axis=0, tiled=True),
        lax.all_gather(value_low, "context", axis=0, tiled=True),
        lax.all_gather(positions, "context", axis=0, tiled=True),
    )
    total_len = key_all.shape[0]
    block_size = min(512, total_len)
    block_count = total_len // block_size

    def key_block(grad_query_acc, block_items):
        key_blk, value_blk, pos_blk = block_items
        grad_query_acc, grad_key_blk, grad_value_blk = block_grads(
            grad_query_acc, key_blk, value_blk, pos_blk
        )
        return (grad_query_acc, (grad_key_blk, grad_value_blk))

    grad_query_acc, (grad_keys_all, grad_values_all) = lax.scan(
        key_block,
        zero_query,
        (
            key_all.reshape(block_count, block_size, seq_count, kv_width),
            value_all.reshape(block_count, block_size, seq_count, kv_width),
            pos_all.reshape(block_count, block_size, seq_count),
        ),
    )
    grad_key_own, grad_value_own = (
        lax.psum_scatter(
            grad_keys_all.reshape(total_len, seq_count, kv_width).astype(jnp.bfloat16),
            "context",
            scatter_dimension=0,
            tiled=True,
        ).astype(jnp.float32),
        lax.psum_scatter(
            grad_values_all.reshape(total_len, seq_count, kv_width).astype(jnp.bfloat16),
            "context",
            scatter_dimension=0,
            tiled=True,
        ).astype(jnp.float32),
    )
    grad_rot_q = jnp.transpose(grad_query_acc * score_scale, (3, 0, 1, 2, 4)).reshape(
        slot_count, seq_count, heads_q, HEAD
    )
    grad_q_low = (
        rotate(grad_rot_q, cos_part, -sin_part)
        .reshape(row_count, heads_q * HEAD)
        .astype(jnp.bfloat16)
    )
    grad_rot_k = (grad_key_own * score_scale).reshape(slot_count, seq_count, heads_kv, HEAD)
    grad_k_low = (
        rotate(grad_rot_k, cos_part, -sin_part).reshape(row_count, kv_width).astype(jnp.bfloat16)
    )
    grad_v_low = grad_value_own.reshape(row_count, kv_width).astype(jnp.bfloat16)
    grad_query = contract_rows(normed, grad_q_low)
    grad_key = contract_rows(normed, grad_k_low)
    grad_value = contract_rows(normed, grad_v_low)
    grad_normed = lax.psum(
        (
            contract_cols(grad_q_low, query_mat)
            + contract_cols(grad_k_low, key_mat)
            + contract_cols(grad_v_low, value_mat)
        ).astype(jnp.bfloat16),
        "tensor",
    ).astype(jnp.float32)
    grad_in_norm, grad_gain_one = norm_backward(grad_normed, unit_one, inverse_one, full_one)
    input_grad = (grad_middle + grad_in_norm).reshape(slot_count, seq_count, model_width)
    reduced = (
        lax.psum_scatter(grad_gain_one, ("dp", "context"), scatter_dimension=0, tiled=True),
        lax.psum_scatter(grad_gain_two, ("dp", "context"), scatter_dimension=0, tiled=True),
        lax.psum_scatter(grad_query, ("dp", "context"), scatter_dimension=0, tiled=True),
        lax.psum_scatter(grad_key, ("dp", "context"), scatter_dimension=0, tiled=True),
        lax.psum_scatter(grad_value, ("dp", "context"), scatter_dimension=0, tiled=True),
        lax.psum_scatter(grad_out, ("dp", "context"), scatter_dimension=1, tiled=True),
        lax.psum_scatter(grad_gate, ("dp", "context"), scatter_dimension=0, tiled=True),
        lax.psum_scatter(grad_up, ("dp", "context"), scatter_dimension=0, tiled=True),
        lax.psum_scatter(grad_down, ("dp", "context"), scatter_dimension=1, tiled=True),
    )
    return (
        layer_out,
        input_grad,
        reduced[0],
        reduced[1],
        reduced[2],
        reduced[3],
        reduced[4],
        reduced[5],
        reduced[6],
        reduced[7],
        reduced[8],
    )


WIDE = 128
RUN = 256
TILE = 512
LOG2_E = 1.4426950408889634
MESH = pl.DeviceIdType.MESH
PIECE = 256
FEED = 512
VMEM_LIMIT = 56 * 1024 * 1024


def any_spec():
    return pl.BlockSpec(memory_space=pl.ANY)


def vmem_spec():
    return pl.BlockSpec(memory_space=pltpu.VMEM)


def place():
    return lax.axis_index("dp"), lax.axis_index("context"), lax.axis_index("tensor")


def greet(devices):
    barrier = pltpu.get_barrier_semaphore()
    for device in devices:
        pl.semaphore_signal(barrier, inc=1, device_id=device, device_id_type=MESH)
    pl.semaphore_wait(barrier, len(devices))


def sequence_others():
    row, spot, core = place()
    return [
        (row, lax.rem(spot + shift, 8), lax.rem(core + flip, 2))
        for shift in range(8)
        for flip in range(2)
        if shift or flip
    ]


def spread_matrix():
    shape = (4 * HEAD, 4 * WIDE)
    rows = lax.broadcasted_iota(jnp.int32, shape, 0)
    cols = lax.broadcasted_iota(jnp.int32, shape, 1)
    head = 0
    for start in (1, 2, 3):
        head = head + jnp.where(rows >= start * HEAD, 1, 0)
    dims = rows - head * HEAD
    target = head * WIDE + dims + jnp.where(dims >= HEAD // 2, (WIDE - HEAD) // 2, 0)
    return jnp.where(cols == target, 1.0, 0.0).astype(jnp.bfloat16)


def lane_freqs():
    half = HEAD // 2
    inv_freqs = theta_base ** (-2.0 * jnp.arange(half, dtype=jnp.float32) / HEAD)
    gap = jnp.zeros((WIDE // 2 - half,), jnp.float32)
    return jnp.concatenate([inv_freqs, gap, inv_freqs, gap]).reshape(1, WIDE)


def dot_f32(left, right):
    return jnp.dot(left, right, preferred_element_type=jnp.float32)


def remote(source, target, send, recv, device):
    return pltpu.make_async_remote_copy(
        src_ref=source,
        dst_ref=target,
        send_sem=send,
        recv_sem=recv,
        device_id=device,
        device_id_type=MESH,
    )


def move(source, target, send, recv, device, is_self):
    @pl.when(is_self)
    def _():
        pltpu.make_async_copy(source, target, recv).start()

    @pl.when(jnp.logical_not(is_self))
    def _():
        remote(source, target, send, recv, device).start()


def return_copies(ref, out, send, recv):
    row, spot, core = place()
    head = 2 * lax.rem(spot, 4) + core
    owner = spot // 4
    copies = []
    for step in range(8):
        chip = lax.rem(spot + step, 8)
        is_self = (owner == core) if step == 0 else False
        parts = (ref.at[chip], out.at[head], send.at[step], recv.at[head], (row, chip, owner))
        copies.append((parts, is_self))
    return copies


def start_return(copies):
    for parts, is_self in copies:
        if is_self is False:
            remote(*parts).start()
        else:
            move(*parts, is_self)


def finish_return(copies, out, send, recv):
    row, spot, core = place()
    for head in range(8):
        remote(
            out.at[head], out.at[head], send.at[0], recv.at[head], (row, spot, 1 - core)
        ).wait_recv()
    for parts, is_self in copies:
        if is_self is False:
            remote(*parts).wait_send()
        else:

            @pl.when(jnp.logical_not(is_self))
            def _():
                remote(*parts).wait_send()


def tile_at(index, size):
    return pl.ds(pl.multiple_of(index * size, size), size)


def causal(scores):
    keys = lax.broadcasted_iota(jnp.int32, scores.shape, 0)
    queries = lax.broadcasted_iota(jnp.int32, scores.shape, 1)
    return jnp.where(keys <= queries, scores, masked_value)


def neighbours():
    row, spot, core = place()
    level, column = spot // 2, lax.rem(spot, 2)
    beside_x = (1 - row, spot, core)
    beside_y = (row, 2 * level + 1 - column, core)
    along_z = [(row, 2 * lax.rem(level + k, 4) + column, core) for k in (1, 2, 3)]
    return row, level, column, beside_x, beside_y, along_z


class Gather:
    def __init__(self, own, whole, start, width, piece, sems):
        self.own, self.whole = own.at[:, pl.ds(start, width)], whole
        self.start, self.width = start, width
        names = ("send_z", "recv_z", "send_x", "recv_x", "send_y", "recv_y", "send_d", "recv_d")
        for name, sem in zip(names + ("local",), sems):
            setattr(self, name, sem.at[piece])

    def block(self, x, z, y, half=None):
        cut = self.width * 7 // 12 // WIDE * WIDE
        start, width = self.start, self.width
        if half == 0:
            width = cut
        elif half == 1:
            start, width = start + cut, width - cut
        return self.whole.at[x, z, y, :, pl.ds(start, width)]

    def arrived(self, target, recv_sem):
        device = neighbours()[3]
        remote(target, target, self.send_x.at[0], recv_sem, device).wait_recv()

    def copy_z(self, z, up):
        row, level, column, beside_x, beside_y = neighbours()[:5]
        core = place()[2]
        target = level + 1 if up else level - 1
        block = self.block(row, z, column)
        return remote(
            block,
            block,
            self.send_z.at[int(up), z],
            self.recv_z.at[z],
            (row, 2 * target + column, core),
        )

    def copies_xy(self, z):
        row, level, column, beside_x, beside_y = neighbours()[:5]
        block = self.block(row, z, column)
        return [
            remote(block, block, self.send_x.at[z], self.recv_x.at[z], beside_x),
            remote(block, block, self.send_y.at[z], self.recv_y.at[z], beside_y),
        ]

    def copies_diagonal(self, z):
        row, level, column, beside_x, beside_y = neighbours()[:5]
        by_y = self.block(1 - row, z, column, 1)
        by_x = self.block(row, z, 1 - column, 0)
        return [
            remote(by_y, by_y, self.send_d.at[0, z], self.recv_d.at[0, z], beside_y),
            remote(by_x, by_x, self.send_d.at[1, z], self.recv_d.at[1, z], beside_x),
        ]

    def own_copy(self):
        row, level, column = neighbours()[:3]
        return pltpu.make_async_copy(self.own, self.block(row, level, column), self.local)

    def each_at(self, hop, act):
        level = neighbours()[1]

        @pl.when(level >= hop)
        def _():
            act(level - hop, True)

        @pl.when(level + hop <= 3)
        def _():
            act(level + hop, False)

    def start_z(self, z, up):
        level = neighbours()[1]

        @pl.when(level < 3 if up else level > 0)
        def _():
            self.copy_z(z, up).start()

    def place_own(self):
        self.own_copy().start()

    def open(self):
        level = neighbours()[1]
        self.own_copy().wait()
        self.start_z(level, True)
        self.start_z(level, False)
        for copy in self.copies_xy(level):
            copy.start()

    def hop(self, hop):
        def act(z, up):
            row, level, column = neighbours()[:3]
            self.arrived(self.block(row, z, column), self.recv_z.at[z])
            self.start_z(z, up)
            for copy in self.copies_xy(z):
                copy.start()

        self.each_at(hop, act)

    def turn_diagonal(self, z):
        row, level, column = neighbours()[:3]
        by_y, by_x = self.copies_diagonal(z)
        self.arrived(self.block(1 - row, z, column), self.recv_x.at[z])
        by_y.start()
        self.arrived(self.block(row, z, 1 - column), self.recv_y.at[z])
        by_x.start()

    def diagonal(self, hop):
        if hop == 0:
            self.turn_diagonal(neighbours()[1])
        else:
            self.each_at(hop, lambda z, up: self.turn_diagonal(z))

    def finish(self):
        row, level, column = neighbours()[:3]
        for z in range(4):
            self.arrived(self.block(1 - row, z, 1 - column, 1), self.recv_d.at[0, z])
            self.arrived(self.block(1 - row, z, 1 - column, 0), self.recv_d.at[1, z])

    def close(self):
        level = neighbours()[1]

        def sent(z, up):
            @pl.when(level < 3 if up else level > 0)
            def _():
                self.copy_z(z, up).wait_send()

        sent(level, True)
        sent(level, False)
        for hop in range(1, 4):
            self.each_at(hop, sent)
        for z in range(4):
            for copy in self.copies_xy(z) + self.copies_diagonal(z):
                copy.wait_send()


def gather_sems(pieces):
    dma = pltpu.SemaphoreType.DMA
    shapes = [(2, 4), (4,), (4,), (4,), (4,), (4,), (2, 4), (2, 4), ()]
    return [dma((pieces,) + shape) for shape in shapes]


def forward_kernel(
    tokens,
    positions,
    freqs,
    ids_in,
    gain_one,
    gain_two,
    w_query,
    w_key,
    w_value,
    w_out_t,
    w_gate,
    w_up,
    w_down_t,
    cotangent,
    near,
    far,
    normed_out,
    q_out,
    k_out,
    v_out,
    mixed_t_out,
    lse_out,
    mixed_low_out,
    middle_out,
    second_out,
    right_out,
    gains_out,
    tables_out,
    order,
    ids_flat,
    near_own,
    far_own,
    unit,
    normed,
    spread,
    tables,
    weight,
    extras,
    gain_rows,
    q_heads,
    kv_heads,
    q_slots,
    kv_slots,
    q,
    q_t,
    keys,
    v,
    v_t,
    mixed_t,
    lse,
    mixed,
    mixed_slots,
    mixed_heads,
    mixed_low,
    out_weight,
    part,
    part_other,
    second,
    cot,
    right,
    feed_weight,
    ids_all,
    ids,
    load_own,
    send_ids,
    recv_ids,
    load_ids,
    load_w,
    load_extra,
    load_out,
    load_feed,
    load_cot,
    save_right,
    saves,
    send_q,
    recv_q,
    send_kv,
    recv_kv,
    send_x,
    recv_x,
    send_m,
    recv_m,
    send_p,
    recv_p,
    *sems,
):
    row, spot, core = place()
    low, full = jnp.bfloat16, jnp.float32
    rows, width = tokens.shape
    share = near_own.shape[0]
    length = 8 * rows
    runs, tiles = length // RUN, length // TILE
    per_device = rows // RUN
    halves = TILE // RUN
    quarter = 4 * share
    sibling = (row, spot, 1 - core)
    out_width = w_out_t.shape[1]
    qkv_width = 16 * HEAD

    near_loads, far_loads, start = [], [], 0
    for ref in (w_query, w_key, w_value, w_out_t):
        if ref is w_out_t:
            start += WIDE
        target = near_own.at[:, pl.ds(start, ref.shape[1])]
        near_loads.append(pltpu.make_async_copy(ref, target, load_own.at[len(near_loads)]))
        start += ref.shape[1]
    for index, ref in enumerate((w_gate, w_up, w_down_t)):
        for piece in range(4):
            source = ref.at[:, pl.ds(piece * FEED, FEED)]
            target = far_own.at[:, pl.ds((3 * piece + index) * FEED, FEED)]
            far_loads.append(
                pltpu.make_async_copy(source, target, load_own.at[4 + 4 * index + piece])
            )
    for copy in near_loads + far_loads:
        copy.start()
    load_cotangent = pltpu.make_async_copy(cotangent, cot, load_cot)
    load_cotangent.start()
    line = lax.broadcasted_iota(jnp.int32, (WIDE, share), 0)
    gains = jnp.where(line == 0, gain_one[...].astype(full), 0.0)
    gains = jnp.where(line == 1, gain_two[...].astype(full), gains)
    near_own[:, qkv_width : qkv_width + WIDE] = gains.T.astype(low)

    first = Gather(near_own, near, 0, qkv_width + WIDE, 0, sems)
    outer = Gather(near_own, near, qkv_width + WIDE, out_width, 1, sems)
    feeds = [Gather(far_own, far, 3 * FEED * p, 3 * FEED, 2 + p, sems) for p in range(4)]
    gathers = [first, outer] + feeds
    for copy in near_loads:
        copy.wait()
    first.place_own()
    outer.place_own()
    for copy in far_loads:
        copy.wait()
    for gather in feeds:
        gather.place_own()
    greet(sequence_others() + [neighbours()[3]])
    first.open()

    for shift in range(1, 8):
        remote(
            ids_in,
            ids_all.at[spot],
            send_ids.at[shift],
            recv_ids.at[shift],
            (row, lax.rem(spot + shift, 8), core),
        ).start()
    ids_all[spot] = ids_in[...]

    values = tokens[...].astype(full)
    unit[...] = values * lax.rsqrt(jnp.mean(values * values, axis=-1, keepdims=True) + epsilon)
    spread[...] = spread_matrix()
    angles = positions[...].astype(full) * freqs[...]
    sign = jnp.where(lax.broadcasted_iota(jnp.int32, (1, WIDE), 1) < WIDE // 2, -1.0, 1.0)
    tables[0] = jnp.cos(angles)
    tables[1] = jnp.sin(angles) * sign

    first.hop(1)
    first.diagonal(0)
    first.hop(2)
    first.diagonal(1)
    first.hop(3)
    outer.open()
    first.diagonal(2)
    first.diagonal(3)
    outer.hop(1)
    feeds[0].open()
    for shift in range(1, 8):
        remote(
            ids_in,
            ids_all.at[lax.rem(spot + 8 - shift, 8)],
            send_ids.at[shift],
            recv_ids.at[shift],
            (row, lax.rem(spot + shift, 8), core),
        ).wait_recv()
    pltpu.make_async_copy(ids_all, ids, load_ids).start()
    first.finish()

    def load_group(group):
        lanes = pl.ds(group * 4 * HEAD, 4 * HEAD)
        return pltpu.make_async_copy(
            near.at[:, :, :, :, lanes], weight.at[group % 2], load_w.at[group % 2]
        )

    load_extras = pltpu.make_async_copy(
        near.at[:, :, :, :, pl.ds(qkv_width, WIDE)], extras, load_extra
    )
    load_out_weight = pltpu.make_async_copy(
        near.at[:, :, :, :, pl.ds(qkv_width + WIDE, out_width)], out_weight, load_out
    )
    load_extras.start()
    load_group(0).start()
    load_group(1).start()
    load_extras.wait()
    gain_rows[...] = extras[...].reshape(width, WIDE).T[0:8].astype(full)
    normed[...] = (unit[...] * gain_rows[0:1]).astype(low)
    for group in range(4):
        load_group(group).wait()
        wide = dot_f32(weight[group % 2].reshape(width, 4 * HEAD), spread[...]).astype(low)
        if group < 2:
            load_group(group + 2).start()
        proj = dot_f32(normed[...], wide)
        for head in range(4):
            value = proj[:, head * WIDE : (head + 1) * WIDE]
            if group < 3:
                value = value * tables[0] + pltpu.roll(value, WIDE // 2, 1) * tables[1]
            value = value.astype(low).reshape(per_device, RUN, WIDE)
            if group < 2:
                q_heads[4 * group + head] = value
            else:
                kv_heads[head, group - 2] = value
        if group == 0:
            outer.hop(2)
            outer.diagonal(0)
        elif group == 1:
            outer.hop(3)
            outer.diagonal(1)
        elif group == 2:
            feeds[0].hop(1)
            outer.diagonal(2)

    outgoing = []
    for step in range(4):
        slot = lax.rem(spot + step, 4)
        chip = 4 * core + slot
        for other in range(2):
            is_self = jnp.logical_and(chip == spot, core == other)
            device = (row, chip, other)
            kv_parts = (
                kv_heads.at[slot, :, other],
                kv_slots.at[spot, :, other],
                send_kv.at[step, other],
                recv_kv.at[spot],
                device,
            )
            q_parts = (
                q_heads.at[2 * slot + other],
                q_slots.at[spot],
                send_q.at[step, other],
                recv_q.at[spot],
                device,
            )
            outgoing.append((kv_parts, is_self))
            outgoing.append((q_parts, is_self))
    for parts, is_self in outgoing:
        move(*parts, is_self)
    outer.diagonal(3)
    feeds[0].hop(2)
    feeds[0].diagonal(0)
    feeds[0].hop(3)
    outer.finish()
    load_out_weight.start()
    feeds[1].open()
    feeds[0].diagonal(1)
    feeds[0].diagonal(2)

    def hand_on(source):
        block = kv_slots.at[source, :, core]
        return remote(block, block, send_x.at[source], recv_x.at[source], sibling)

    for step in range(8):
        source = lax.rem(spot + step, 8)
        block = kv_slots.at[source, :, core]
        remote(block, block, send_x.at[source], recv_kv.at[source], sibling).wait_recv()
        hand_on(source).start()
    for step in range(8):
        remote(
            q_slots.at[step], q_slots.at[step], send_x.at[step], recv_q.at[step], sibling
        ).wait_recv()
        hand_on(step).wait()
    feeds[0].diagonal(3)
    feeds[1].hop(1)

    pltpu.make_async_copy(ids_all, ids, load_ids).wait()

    def find_run(index, carry):
        device, piece = 0, 0
        for run in range(runs):
            here = ids[run // per_device, 0, run % per_device] == index
            device = jnp.where(here, run // per_device, device)
            piece = jnp.where(here, run % per_device, piece)
        order[index, 0] = device
        order[index, 1] = piece
        found = ids[index // per_device, 0, index % per_device]
        order[runs + index, 0] = lax.div(found, per_device)
        order[runs + index, 1] = lax.rem(found, per_device)
        ids_flat[index] = found
        return carry

    lax.fori_loop(0, runs, find_run, 0)

    def sort_run(index, carry):
        device, piece = order[index, 0], order[index, 1]
        cols = tile_at(index, RUN)
        queries, values = q_slots[device, piece], kv_slots[device, 1, piece]
        q[cols] = queries
        q_t[:, cols] = queries.T
        keys[cols] = kv_slots[device, 0, piece]
        v[cols] = values
        v_t[:, cols] = values.T
        return carry

    lax.fori_loop(0, runs, sort_run, 0)
    scale = HEAD ** (-0.5) * LOG2_E

    def query_tile(index, carry):
        cols = tile_at(index, TILE)
        queries = q_t[:, cols]

        def step(scores, block, peak, total, mix):
            high = jnp.maximum(peak, jnp.max(scores, axis=0, keepdims=True))
            decay = jnp.exp2(peak - high)
            weights = jnp.exp2(scores - high)
            total = total * decay + jnp.sum(weights, axis=0, keepdims=True)
            mix = mix * decay + dot_f32(v_t[:, tile_at(block, TILE)], weights.astype(low))
            return high, total, mix

        def scores_of(block):
            return dot_f32(keys[tile_at(block, TILE)], queries) * scale

        state = (
            jnp.full((1, TILE), masked_value, full),
            jnp.zeros((1, TILE), full),
            jnp.zeros((WIDE, TILE), full),
        )
        state = step(causal(scores_of(index)), index, *state)
        peak, total, mix = lax.fori_loop(
            0, index, lambda block, now: step(scores_of(block), block, *now), state
        )
        mix = mix / total
        mixed_t[:, cols] = mix
        lse[:, cols] = peak + jnp.log2(total)
        for half in range(halves):
            mixed[index * halves + half] = mix[:, half * RUN : (half + 1) * RUN].T.astype(low)

        hooks = {
            1: [(feeds[1].hop, 2)],
            2: [(feeds[1].hop, 3), (feeds[1].diagonal, 0)],
            4: [(feeds[1].diagonal, 1)],
            5: [(feeds[1].diagonal, 2)],
            6: [(feeds[1].diagonal, 3)],
        }
        for when, acts in hooks.items():

            @pl.when(index == when)
            def _():
                for act, hop in acts:
                    act(hop)
                if when == 2:
                    feeds[2].open()

        return carry

    lax.fori_loop(0, tiles, query_tile, 0)

    def unsort_run(run, carry):
        index = ids[run // per_device, 0, run % per_device]
        mixed_slots[run // per_device, run % per_device] = mixed[index]
        return carry

    lax.fori_loop(0, runs, unsort_run, 0)
    copies = return_copies(mixed_slots, mixed_heads, send_m, recv_m)
    start_return(copies)
    early_saves = [
        pltpu.make_async_copy(source, target, saves.at[index])
        for index, (source, target) in enumerate(
            [
                (normed, normed_out),
                (q, q_out),
                (keys, k_out),
                (v, v_out),
                (mixed_t, mixed_t_out),
                (lse, lse_out),
                (gain_rows, gains_out),
                (tables, tables_out),
            ]
        )
    ]
    for copy in early_saves:
        copy.start()
    feeds[2].hop(1)
    feeds[2].diagonal(0)
    feeds[2].hop(2)
    feeds[2].hop(3)
    feeds[3].open()
    feeds[2].diagonal(1)
    finish_return(copies, mixed_heads, send_m, recv_m)

    load_out_weight.wait()
    for group in range(2):
        side = [mixed_heads[4 * group + head].reshape(rows, WIDE) for head in range(4)]
        narrow = contract_cols(jnp.concatenate(side, axis=1), spread[...])
        mixed_low[:, group * 4 * HEAD : (group + 1) * 4 * HEAD] = narrow.astype(low)

    def pair_copy(index):
        cut = pl.ds(index * quarter, quarter)
        return remote(
            part.at[:, cut], part_other.at[:, cut], send_p.at[index], recv_p.at[index], sibling
        )

    for index in range(4):
        block = out_weight[index // 2, 2 * (index % 2) : 2 * (index % 2) + 2]
        term = contract_cols(mixed_low[...], block.reshape(quarter, out_width))
        part[:, index * quarter : (index + 1) * quarter] = term.astype(low)
        pair_copy(index).start()
    feeds[2].diagonal(2)
    feeds[3].hop(1)
    load_cotangent.wait()
    for index in range(4):
        pair_copy(index).wait()
    chunk = rows // 8

    def norm_block(index, carry):
        cut = tile_at(index, chunk)
        sums = part[cut].astype(full) + part_other[cut].astype(full)
        values = tokens[cut].astype(full) + sums
        unit[cut] = values
        inverse = lax.rsqrt(jnp.mean(values * values, axis=-1, keepdims=True) + epsilon)
        second[cut] = (values * inverse * gain_rows[1:2]).astype(low)
        return carry

    lax.fori_loop(0, 8, norm_block, 0)
    late_saves = [
        pltpu.make_async_copy(source, target, saves.at[8 + index])
        for index, (source, target) in enumerate(
            [(mixed_low, mixed_low_out), (unit, middle_out), (second, second_out)]
        )
    ]
    for copy in late_saves:
        copy.start()

    def load_feed_weight(index, kind):
        piece, half = index // 2, lax.rem(index, 2)
        start = (3 * piece + kind) * FEED + half * PIECE
        lanes = pl.ds(pl.multiple_of(start, PIECE), PIECE)
        return pltpu.make_async_copy(
            far.at[:, :, :, :, lanes], feed_weight.at[half, kind], load_feed.at[half, kind]
        )

    def save_piece(piece):
        lanes = pl.ds(piece * 3 * FEED, 3 * FEED)
        return pltpu.make_async_copy(
            right.at[:, lanes], right_out.at[:, lanes], save_right.at[piece]
        )

    def feed_block(index, carry):
        piece, half = index // 2, lax.rem(index, 2)
        for when in range(4):

            @pl.when(index == 2 * when)
            def _():
                feeds[when].finish()

        @pl.when(half == 0)
        def _():
            for offset in range(2):
                for kind in range(3):
                    load_feed_weight(index + offset, kind).start()

        values = []
        for kind, left in enumerate((second, second, cot)):
            load_feed_weight(index, kind).wait()
            values.append(dot_f32(left[...], feed_weight[half, kind].reshape(width, PIECE)))
        gate, up, grad_hidden = values
        sigmoid = jax.nn.sigmoid(gate)
        silu = gate * sigmoid
        grad_gate = grad_hidden * up * sigmoid * (1.0 + gate * (1.0 - sigmoid))
        for kind, value in enumerate((grad_gate, grad_hidden * silu, silu * up)):
            start = (3 * piece + kind) * FEED + half * PIECE
            right[:, pl.ds(pl.multiple_of(start, PIECE), PIECE)] = value.astype(low)

        hooks = {
            1: [(feeds[2].diagonal, 3), (feeds[3].hop, 2), (feeds[3].diagonal, 0)],
            2: [(feeds[3].hop, 3)],
            3: [(feeds[3].diagonal, 1)],
            4: [(feeds[3].diagonal, 2)],
            5: [(feeds[3].diagonal, 3)],
        }
        for when, acts in hooks.items():

            @pl.when(index == when)
            def _():
                for act, hop in acts:
                    act(hop)

        for when in range(4):

            @pl.when(index == 2 * when + 1)
            def _():
                save_piece(when).start()

        return carry

    lax.fori_loop(0, 8, feed_block, 0)
    for gather in gathers:
        gather.close()
    for parts, is_self in outgoing:

        @pl.when(jnp.logical_not(is_self))
        def _():
            remote(*parts).wait_send()

    for shift in range(1, 8):
        remote(
            ids_in,
            ids_all.at[spot],
            send_ids.at[shift],
            recv_ids.at[shift],
            (row, lax.rem(spot + shift, 8), core),
        ).wait_send()
    for copy in early_saves + late_saves + [save_piece(piece) for piece in range(4)]:
        copy.wait()


def forward(
    tokens,
    positions,
    ids,
    gain_one,
    gain_two,
    w_query,
    w_key,
    w_value,
    w_out_t,
    w_gate,
    w_up,
    w_down_t,
    cotangent,
):
    dma = pltpu.SemaphoreType.DMA
    vmem = pltpu.VMEM
    low, full = jnp.bfloat16, jnp.float32
    rows, width = tokens.shape
    share, hidden_width = w_gate.shape
    out_width = w_out_t.shape[1]
    near_width = 16 * HEAD + out_width + WIDE
    length = 8 * rows
    per_device = rows // RUN
    heads = (8, per_device, RUN, WIDE)
    both = (2, per_device, RUN, WIDE)
    smem_spec = pl.BlockSpec(memory_space=pltpu.SMEM)
    shape = jax.ShapeDtypeStruct
    tall, flat = (length, WIDE), (WIDE, length)
    return pl.pallas_call(
        forward_kernel,
        in_specs=[vmem_spec()] * 6 + [any_spec()] * 8,
        out_specs=[any_spec()] * 14 + [smem_spec] * 2,
        out_shape=[
            shape((2, 4, 2, share, near_width), low),
            shape((2, 4, 2, share, 3 * hidden_width), low),
            shape((rows, width), low),
            shape(tall, low),
            shape(tall, low),
            shape(tall, low),
            shape(flat, full),
            shape((1, length), full),
            shape((rows, out_width), low),
            shape((rows, width), full),
            shape((rows, width), low),
            shape((rows, 3 * hidden_width), low),
            shape((8, width), full),
            shape((2, rows, WIDE), full),
            shape((2 * length // RUN, 2), jnp.int32),
            shape((length // RUN,), jnp.int32),
        ],
        scratch_shapes=[
            vmem((share, near_width), low),
            vmem((share, 3 * hidden_width), low),
            vmem((rows, width), full),
            vmem((rows, width), low),
            vmem((4 * HEAD, 4 * WIDE), low),
            vmem((2, rows, WIDE), full),
            vmem((2, 2, 4, 2, share, 4 * HEAD), low),
            vmem((2, 4, 2, share, WIDE), low),
            vmem((8, width), full),
            vmem(heads, low),
            vmem((4,) + both, low),
            vmem(heads, low),
            vmem((8,) + both, low),
            vmem(tall, low),
            vmem(flat, low),
            vmem(tall, low),
            vmem(tall, low),
            vmem(flat, low),
            vmem(flat, full),
            vmem((1, length), full),
            vmem((length // RUN, RUN, WIDE), low),
            vmem(heads, low),
            vmem(heads, low),
            vmem((rows, out_width), low),
            vmem((2, 4, 2, share, out_width), low),
            vmem((rows, width), low),
            vmem((rows, width), low),
            vmem((rows, width), low),
            vmem((rows, width), low),
            vmem((rows, 3 * hidden_width), low),
            vmem((2, 3, 2, 4, 2, share, PIECE), low),
            vmem((8, 8, WIDE), jnp.int32),
            pltpu.SMEM((8, 8, WIDE), jnp.int32),
            dma((16,)),
            dma((8,)),
            dma((8,)),
            dma(()),
            dma((2,)),
            dma(()),
            dma(()),
            dma((2, 3)),
            dma(()),
            dma((4,)),
            dma((12,)),
            dma((4, 2)),
            dma((8,)),
            dma((4, 2)),
            dma((8,)),
            dma((8,)),
            dma((8,)),
            dma((8,)),
            dma((8,)),
            dma((4,)),
            dma((4,)),
        ]
        + gather_sems(6),
        compiler_params=pltpu.CompilerParams(
            collective_id=1, has_side_effects=True, vmem_limit_bytes=VMEM_LIMIT
        ),
        name="forward",
    )(
        tokens,
        positions,
        lane_freqs(),
        ids,
        gain_one,
        gain_two,
        w_query,
        w_key,
        w_value,
        w_out_t,
        w_gate,
        w_up,
        w_down_t,
        cotangent,
    )


SECOND, THIRD, LAST = 2, 3, 4


class Reduce:
    def __init__(self, n, changes, refs):
        (
            self.left_t,
            self.right,
            self.gains,
            self.own,
            self.out,
            self.save,
            self.send_one,
            self.recv_one,
            self.send_two,
            self.recv_two,
            self.kept,
            self.recv_three,
            self.ss_one,
            self.rs_one,
            self.ss_two,
            self.rs_two,
            self.ss_three,
            self.rs_three,
        ) = refs
        self.n, self.changes = n, changes
        self.share = self.own.shape[1]

    def columns(self, step, kind):
        held = self.right.shape[1] // (2 * PIECE)
        start = lax.rem(step, held) * 2 * PIECE + kind * PIECE
        return pl.ds(pl.multiple_of(start, PIECE), PIECE)

    def saving(self, step):
        slot = lax.rem(step, 2)
        pieces = self.changes[0] // 3
        place = jnp.where(step < self.changes[0], lax.rem(step, 3) * pieces + step // 3, step)
        cut = pl.ds(pl.multiple_of(place * 2 * PIECE, 2 * PIECE), 2 * PIECE)
        return pltpu.make_async_copy(self.own.at[slot], self.out.at[:, cut], self.save.at[slot])

    def product(self, step, kind, x, y):
        left = jnp.where(lax.rem(step, 3) == 2, 0, 1)
        left = jnp.where(step >= self.changes[0], 2, left)
        left = jnp.where(step >= self.changes[1], 0, left)
        term = jnp.dot(
            self.left_t[left, x, y],
            self.right[:, self.columns(step, kind)],
            preferred_element_type=jnp.float32,
        )
        if kind == 1:
            term = jnp.where(step == self.n - 1, self.gains[x, y].astype(jnp.float32), term)
        return term

    def first_copy(self, step, kind):
        beside_x, beside_y = neighbours()[3:5]
        out, into = lax.rem(step, 3), lax.rem(step, 4)
        return remote(
            self.send_one.at[out, kind],
            self.recv_one.at[into, kind],
            self.ss_one.at[out, kind],
            self.rs_one.at[into, kind],
            beside_x if kind == 0 else beside_y,
        )

    def second_copy(self, step, kind):
        beside_x, beside_y = neighbours()[3:5]
        out, into = lax.rem(step, 2), lax.rem(step, 4)
        return remote(
            self.send_two.at[out, kind],
            self.recv_two.at[into, kind],
            self.ss_two.at[out, kind],
            self.rs_two.at[into, kind],
            beside_y if kind == 0 else beside_x,
        )

    def third_copy(self, step, kind, k):
        row, level, column, beside_x, beside_y, along_z = neighbours()
        target = lax.rem(level + k + 1, 4)
        out, into = lax.rem(step, 3), lax.rem(step, 4)
        return remote(
            self.kept.at[out, kind, pl.ds(pl.multiple_of(target * self.share, 16), self.share)],
            self.recv_three.at[into, kind, k],
            self.ss_three.at[out, kind, k],
            self.rs_three.at[into, kind, k],
            along_z[k],
        )

    def first(self, step):
        row, level, column = neighbours()[:3]
        slot = lax.rem(step, 3)
        for half in range(2):
            self.send_one[slot, 0, half] = self.product(step, 0, 1 - row, half).astype(jnp.bfloat16)
        self.first_copy(step, 0).start()
        for half in range(2):
            self.send_one[slot, 1, half] = self.product(step, 1, half, 1 - column).astype(
                jnp.bfloat16
            )
        self.first_copy(step, 1).start()

    def second(self, step):
        row, level, column = neighbours()[:3]
        slot, came, keep = lax.rem(step, 2), lax.rem(step, 4), lax.rem(step, 3)
        for kind in range(2):
            self.first_copy(step, kind).wait()
        for kind in range(2):
            away_at = (row, 1 - column) if kind == 0 else (1 - row, column)
            arrived = self.recv_one.at[came, kind]
            away = self.product(step, kind, *away_at) + arrived[away_at[1 - kind]].astype(
                jnp.float32
            )
            self.send_two[slot, kind] = away.astype(jnp.bfloat16)
            here = self.product(step, kind, row, column) + arrived[
                column if kind == 0 else row
            ].astype(jnp.float32)
            self.kept[keep, kind] = here.astype(jnp.bfloat16)
        for kind in range(2):
            self.second_copy(step, kind).start()

    def third(self, step):
        came, keep = lax.rem(step, 4), lax.rem(step, 3)
        for kind in range(2):
            self.second_copy(step, kind).wait()
            here = self.kept[keep, kind].astype(jnp.float32) + self.recv_two[came, kind].astype(
                jnp.float32
            )
            self.kept[keep, kind] = here.astype(jnp.bfloat16)
            for k in range(3):
                self.third_copy(step, kind, k).start()

    def last(self, step):
        level = neighbours()[1]
        came, keep = lax.rem(step, 4), lax.rem(step, 3)
        mine = pl.ds(pl.multiple_of(level * self.share, 16), self.share)

        @pl.when(step >= 2)
        def _():
            self.saving(step - 2).wait()

        for kind in range(2):
            total = self.kept[keep, kind, mine].astype(jnp.float32)
            for k in range(3):
                self.third_copy(step, kind, k).wait()
                total = total + self.recv_three[came, kind, k].astype(jnp.float32)
            self.own[lax.rem(step, 2), :, kind * PIECE : (kind + 1) * PIECE] = total
        self.saving(step).start()

    def turn(self, step):
        for stage, lag in (
            (self.first, 0),
            (self.second, SECOND),
            (self.third, THIRD),
            (self.last, LAST),
        ):

            @pl.when(jnp.logical_and(step >= lag, step < self.n + lag))
            def _():
                stage(step - lag)


def backward_kernel(
    order,
    ids,
    q_in,
    k_in,
    v_in,
    mixed_t_in,
    lse_in,
    cotangent,
    second_in,
    normed_in,
    right_in,
    mixed_low,
    middle,
    near,
    far,
    tokens,
    gains_in,
    tables,
    input_grad,
    layer_out,
    grads,
    q,
    q_t,
    k,
    k_t,
    v,
    d_own,
    d_slots,
    d,
    d_t,
    dq_t,
    lse,
    delta,
    dk,
    dv,
    dkv_slots,
    dkv_other,
    dq_own,
    dkv_own,
    spread,
    weight,
    row_weight,
    middle_ring,
    part,
    part_other,
    total,
    staged,
    grad_mid,
    gain_two_grad,
    left_t,
    right,
    gains,
    own,
    send_one,
    recv_one,
    send_two,
    recv_two,
    kept,
    recv_three,
    loads,
    load_left_sem,
    load_w,
    load_rows,
    load_ring,
    save_sem,
    send_d,
    recv_d,
    send_q,
    recv_q,
    send_x,
    recv_x,
    send_k,
    recv_k,
    send_p,
    recv_p,
    save,
    *sems,
):
    row, spot, core = place()
    low, full = jnp.bfloat16, jnp.float32
    rows, width = staged.shape
    length = 8 * rows
    runs, tiles = length // RUN, length // TILE
    per_device = rows // RUN
    halves = TILE // RUN
    share = width // 16
    quarter = 4 * share
    sibling = (row, spot, 1 - core)
    qkv_width = 16 * HEAD
    out_width = mixed_low.shape[1]
    n = grads.shape[1] // (2 * PIECE)
    near_at = right_in.shape[1] // (2 * PIECE)
    changes = (near_at, near_at + qkv_width // (2 * PIECE))
    sums = Reduce(
        n,
        changes,
        (left_t, right, gains, own, grads, save)
        + (send_one, recv_one, send_two, recv_two, kept, recv_three)
        + sems,
    )

    def stage(source):
        return pltpu.make_async_copy(source, staged, load_left_sem)

    def turn_left(index, source):
        for piece in range(4):
            turned = source[:, piece * quarter : (piece + 1) * quarter].T
            for inner in range(4):
                x, z, y = piece // 2, 2 * (piece % 2) + inner // 2, inner % 2
                left_t[index, x, y, z * share : (z + 1) * share] = turned[
                    inner * share : (inner + 1) * share
                ]

    early_loads = [
        pltpu.make_async_copy(source, target, loads.at[index])
        for index, (source, target) in enumerate(
            [
                (right_in, right),
                (q_in, q),
                (k_in, k),
                (v_in, v),
                (mixed_t_in, dq_t),
                (lse_in, lse),
                (middle, total),
            ]
        )
    ]


    def load_block(index, piece, start, wide):
        lanes = pl.ds(3 * FEED * piece + start, wide)
        levels = pl.ds(2 * lax.rem(index, 2), 2)
        return pltpu.make_async_copy(
            far.at[index // 2, levels, :, :, lanes],
            row_weight.at[piece, :, :, :, pl.ds(0, wide)],
            load_rows.at[piece],
        )

    def row_products(start, wide, landing):
        def block(index, carry):
            term = jnp.zeros((rows, quarter), full)
            for piece in range(4):
                load_block(index, piece, start, wide).wait()
                at = 3 * FEED * piece + start
                term = term + contract_cols(
                    right[:, at : at + wide],
                    row_weight[piece, :, :, :, :wide].reshape(quarter, wide),
                )

                @pl.when(index + 1 < 4)
                def _():
                    load_block(index + 1, piece, start, wide).start()

            part[:, tile_at(index, quarter)] = term.astype(low)
            pair_copy(index, landing).start()
            return carry

        lax.fori_loop(0, 4, block, 0)

    def pair_copy(index, landing):
        cut = pl.ds(pl.multiple_of(index * quarter, quarter), quarter)
        return remote(
            part.at[:, cut],
            part_other.at[landing, :, cut],
            send_p.at[index],
            recv_p.at[landing, index],
            sibling,
        )

    def second_back():
        spread[...] = spread_matrix()
        row_products(0, 2 * FEED, 0)
        for index in range(2):
            load_out_weight(index).start()

    def load_out_weight(index):
        lanes = pl.ds(qkv_width + WIDE + index * 4 * HEAD, 4 * HEAD)
        return pltpu.make_async_copy(
            near.at[:, :, :, :, lanes], weight.at[index], load_w.at[index]
        )

    d_copies = []
    for step in range(4):
        slot = lax.rem(spot + step, 4)
        chip = 4 * core + slot
        for other in range(2):
            parts = (
                d_own.at[2 * slot + other],
                d_slots.at[spot],
                send_d.at[step, other],
                recv_d.at[spot],
                (row, chip, other),
            )
            d_copies.append((parts, jnp.logical_and(chip == spot, core == other)))

    def middle_back():
        for index in range(4):
            pair_copy(index, 0).wait()
        early_loads[6].wait()
        chunk = rows // 8

        def block(index, gain_grad):
            cut = tile_at(index, chunk)
            grad = part[cut].astype(full) + part_other[0, cut].astype(full)
            values = total[cut]
            inverse = lax.rsqrt(jnp.mean(values * values, axis=-1, keepdims=True) + epsilon)
            unit = values * inverse
            scaled = grad * gains_in[1:2]
            mean = jnp.mean(scaled * unit, axis=-1, keepdims=True)
            result = staged[cut].astype(full) + inverse * (scaled - unit * mean)
            total[cut] = result
            grad_mid[cut] = result.astype(low)
            return gain_grad + jnp.sum(grad * unit, axis=0, keepdims=True)

        gain_two_grad[...] = lax.fori_loop(0, 8, block, jnp.zeros((1, width), full))
        for index in range(2):
            load_out_weight(index).wait()
            grad = dot_f32(grad_mid[...], weight[index].reshape(width, 4 * HEAD)).astype(low)
            wide = dot_f32(grad, spread[...]).astype(low)
            for head in range(4):
                value = wide[:, head * WIDE : (head + 1) * WIDE]
                d_own[4 * index + head] = value.reshape(per_device, RUN, WIDE)
        for parts, is_self in d_copies:
            move(*parts, is_self)


    def prepare():
        for copy in early_loads[1:6]:
            copy.wait()
        for index in range(tiles):
            cut = pl.ds(index * TILE, TILE)
            q_t[:, cut] = q[cut].T
            k_t[:, cut] = k[halves * index : halves * (index + 1)].reshape(TILE, WIDE).T

    def take_cotangents():
        for index in range(8):
            remote(
                d_slots.at[index], d_slots.at[index], send_d.at[0, 0], recv_d.at[index], sibling
            ).wait_recv()

        def sort_run(index, carry):
            cols = tile_at(index, RUN)
            run = d_slots[order[index, 0], order[index, 1]]
            turned = run.T
            d[index // per_device, index % per_device] = run
            d_t[:, cols] = turned
            delta[:, cols] = jnp.sum(turned.astype(full) * dq_t[:, cols], axis=0, keepdims=True)
            return carry

        lax.fori_loop(0, runs, sort_run, 0)
        dq_t[...] = jnp.zeros_like(dq_t)

    scale = HEAD ** (-0.5)

    def key_tile(block):
        cut = tile_at(block, TILE)
        both = pl.ds(block * halves, halves)
        keys, values = k[both].reshape(TILE, WIDE), v[both].reshape(TILE, WIDE)
        keys_t = k_t[:, cut]
        dk[...] = jnp.zeros_like(dk)
        dv[...] = jnp.zeros_like(dv)

        def query_tile(index, diagonal):
            cols = tile_at(index, TILE)
            scores = dot_f32(keys, q_t[:, cols]) * (scale * LOG2_E)
            if diagonal:
                scores = causal(scores)
            probs = jnp.exp2(scores - lse[:, cols])
            dv[...] += dot_f32(probs.astype(low), d[index].reshape(TILE, WIDE))
            grad_probs = dot_f32(values, d_t[:, cols])
            grad_scores = (probs * (grad_probs - delta[:, cols])).astype(low)
            dk[...] += dot_f32(grad_scores, q[cols])
            dq_t[:, cols] += dot_f32(keys_t, grad_scores)

        query_tile(block, True)

        def later(index, inner):
            query_tile(index, False)
            return inner

        lax.fori_loop(block + 1, tiles, later, 0)
        k[both] = (dk[...] * scale).astype(low).reshape(halves, RUN, WIDE)
        v[both] = dv[...].astype(low).reshape(halves, RUN, WIDE)

    def key_tiles(start, stop):
        def one(block, carry):
            key_tile(block)
            return carry

        lax.fori_loop(start, stop, one, 0)

    swap = remote(dkv_slots.at[:, :, 1 - core], dkv_other, send_x, recv_x, sibling)
    dq_copies = return_copies(d, dq_own, send_q, recv_q)
    slot, owner = lax.rem(spot, 4), spot // 4
    dkv_copies = []
    for step in range(8):
        chip = lax.rem(spot + step, 8)
        parts = (
            dkv_slots.at[:, chip, core],
            dkv_own.at[slot, :, core],
            send_k.at[step],
            recv_k.at[slot, core],
            (row, chip, owner),
        )
        dkv_copies.append((parts, (owner == core) if step == 0 else False))

    def send_back():
        def unsort_run(run, carry):
            index = ids[run]
            dkv_slots[0, run // per_device, run % per_device] = k[index]
            dkv_slots[1, run // per_device, run % per_device] = v[index]
            return carry

        lax.fori_loop(0, runs, unsort_run, 0)
        swap.start()

        def turn_run(index, carry):
            value = (dq_t[:, tile_at(index, RUN)] * scale).T
            d_slots[index // per_device, index % per_device] = value.astype(low)
            return carry

        lax.fori_loop(0, runs, turn_run, 0)

        def unsort_queries(run, carry):
            value = d_slots[order[runs + run, 0], order[runs + run, 1]]
            d[run // per_device, run % per_device] = value
            return carry

        lax.fori_loop(0, runs, unsort_queries, 0)
        start_return(dq_copies)

    def add_pairs():
        swap.wait()
        for chip in range(8):
            both = dkv_slots[:, chip, core].astype(full) + dkv_other[:, chip].astype(full)
            dkv_slots[:, chip, core] = both.astype(low)
        start_return(dkv_copies)


    def feed_forward():
        row_products(2 * FEED, FEED, 1)
        for group in range(4):
            load_group(group).start()

    save_layer = pltpu.make_async_copy(part, layer_out, save_sem)

    def finish_layer():
        for index in range(4):
            pair_copy(index, 1).wait()
        pieces = width // PIECE

        def load_piece(index):
            lanes = pl.ds(index * PIECE, PIECE)
            return pltpu.make_async_copy(
                middle.at[:, lanes], middle_ring.at[index % 2], load_ring.at[index % 2]
            )

        load_piece(0).start()
        for index in range(pieces):
            if index + 1 < pieces:
                load_piece(index + 1).start()
            load_piece(index).wait()
            cut = pl.ds(index * PIECE, PIECE)
            value = part[:, cut].astype(full) + part_other[1, :, cut].astype(full)
            part[:, cut] = (value + middle_ring[index % 2]).astype(low)
        save_layer.start()


    def load_group(group):
        lanes = pl.ds(group * 4 * HEAD, 4 * HEAD)
        return pltpu.make_async_copy(
            near.at[:, :, :, :, lanes], weight.at[group], load_w.at[group]
        )

    load_mixed = pltpu.make_async_copy(
        mixed_low, right.at[:, pl.ds(qkv_width, out_width)], loads.at[0]
    )

    def project_back():
        load_mixed.start()
        for head in range(8):
            remote(
                dq_own.at[head], dq_own.at[head], send_q.at[0], recv_q.at[head], sibling
            ).wait_recv()
        for slot_in in range(4):
            for core_in in range(2):
                target = dkv_own.at[slot_in, :, core_in]
                remote(
                    target, target, send_k.at[0], recv_k.at[slot_in, core_in], sibling
                ).wait_recv()
        for group in range(4):
            turned = []
            for head in range(4):
                if group < 2:
                    value = dq_own[4 * group + head]
                else:
                    value = dkv_own[head, group - 2]
                value = value.reshape(rows, WIDE)
                if group < 3:
                    value = value.astype(full)
                    value = value * tables[0] - pltpu.roll(value, WIDE // 2, 1) * tables[1]
                    value = value.astype(low)
                turned.append(value)
            narrow = contract_cols(jnp.concatenate(turned, axis=1), spread[...])
            right[:, group * 4 * HEAD : (group + 1) * 4 * HEAD] = narrow.astype(low)
        start = qkv_width + out_width
        right[:, start : start + PIECE] = jnp.zeros((rows, PIECE), low)
        load_mixed.wait()

    def project_normed():
        save_layer.wait()
        for group in range(4):
            load_group(group).wait()
        stage(tokens).start()

        def block(index, carry):
            term = jnp.zeros((rows, quarter), full)
            for group in range(4):
                held = weight[group, index // 2, pl.ds(2 * lax.rem(index, 2), 2)]
                term = term + contract_cols(
                    right[:, group * 4 * HEAD : (group + 1) * 4 * HEAD],
                    held.reshape(quarter, 4 * HEAD),
                )
            part[:, tile_at(index, quarter)] = term.astype(low)
            pair_copy(index, 0).start()
            return carry

        lax.fori_loop(0, 4, block, 0)

    save_input = pltpu.make_async_copy(total, input_grad, save_sem)

    def norm_back():
        stage(tokens).wait()
        for index in range(4):
            pair_copy(index, 0).wait()
        chunk = rows // 8

        def block(index, gain_grad):
            cut = tile_at(index, chunk)
            grad = part[cut].astype(full) + part_other[0, cut].astype(full)
            values = staged[cut].astype(full)
            inverse = lax.rsqrt(jnp.mean(values * values, axis=-1, keepdims=True) + epsilon)
            unit = values * inverse
            scaled = grad * gains_in[0:1]
            mean = jnp.mean(scaled * unit, axis=-1, keepdims=True)
            total[cut] = total[cut] + inverse * (scaled - unit * mean)
            return gain_grad + jnp.sum(grad * unit, axis=0, keepdims=True)

        gain_one_grad = lax.fori_loop(0, 8, block, jnp.zeros((1, width), full))
        save_input.start()
        lines = []
        for value in (gain_one_grad, gain_two_grad[...]):
            high = value.astype(low).astype(full)
            lines.append((high, value - high))
        which = lax.broadcasted_iota(jnp.int32, (WIDE, width), 0)
        table = jnp.zeros((WIDE, width), full)
        for index, line in enumerate((lines[0][0], lines[1][0], lines[0][1], lines[1][1])):
            table = jnp.where(which == index, line, table)
        columns = table.T.astype(low)
        gains[...] = jnp.zeros_like(gains)
        for x in range(2):
            for z in range(4):
                for y in range(2):
                    start = ((x * 4 + z) * 2 + y) * share
                    gains[x, y, z * share : (z + 1) * share, :WIDE] = columns[start : start + share]

    def take_normed():
        stage(normed_in).start()
        stage(normed_in).wait()
        turn_left(2, staged)

    def start_forward():
        for piece in range(4):
            load_block(0, piece, 2 * FEED, FEED).start()

    stage(second_in).start()
    for copy in early_loads:
        copy.start()
    for piece in range(4):
        load_block(0, piece, 0, 2 * FEED).start()
    greet(sequence_others() + [neighbours()[3]])
    stage(second_in).wait()
    turn_left(1, staged)
    stage(cotangent).start()
    early_loads[0].wait()
    stage(cotangent).wait()

    plan = {
        0: [second_back, lambda: turn_left(0, staged)],
        1: [middle_back],
        2: [prepare],
        3: [start_forward, take_cotangents],
        4: [lambda: key_tiles(0, 2)],
        5: [lambda: key_tiles(2, 4)],
        6: [lambda: key_tiles(4, 8), send_back],
        7: [add_pairs, feed_forward],
        8: [finish_layer, take_normed],
        10: [project_back],
        11: [project_normed],
        13: [norm_back],
        14: [lambda: turn_left(0, grad_mid)],
    }

    def run(step, carry):
        sums.turn(step)
        for when, tasks in plan.items():

            @pl.when(step == when)
            def _():
                for task in tasks:
                    task()

        return carry

    lax.fori_loop(0, n + LAST, run, 0)
    save_input.wait()
    for step in (n - 2, n - 1):
        sums.saving(step).wait()
    for copies in (d_copies, dq_copies, dkv_copies):
        for parts, is_self in copies:
            if is_self is False:
                remote(*parts).wait_send()
            else:

                @pl.when(jnp.logical_not(is_self))
                def _():
                    remote(*parts).wait_send()


def backward(order, ids, *arrays):
    dma = pltpu.SemaphoreType.DMA
    vmem = pltpu.VMEM
    low, full = jnp.bfloat16, jnp.float32
    q_sorted, k_sorted, v_sorted, mixed_t, lse, cotangent, second, normed, right = arrays[:9]
    mixed_low, middle, near, far, tokens, gains, tables = arrays[9:]
    rows, width = cotangent.shape
    length = 8 * rows
    share = width // 16
    wide = right.shape[1] + 16 * HEAD + mixed_low.shape[1] + PIECE
    quarter = 4 * share
    per_device = rows // RUN
    heads = (8, per_device, RUN, WIDE)
    tall, flat = (length, WIDE), (WIDE, length)
    by_run = (length // RUN, RUN, WIDE)
    block = (rows, width)
    smem_spec = pl.BlockSpec(memory_space=pltpu.SMEM)
    shape = jax.ShapeDtypeStruct
    return pl.pallas_call(
        backward_kernel,
        in_specs=[smem_spec] * 2 + [any_spec()] * 14 + [vmem_spec()] * 2,
        out_specs=[any_spec()] * 3,
        out_shape=[shape(block, full), shape(block, low), shape((share, wide), full)],
        scratch_shapes=[
            vmem(tall, low),
            vmem(flat, low),
            vmem(by_run, low),
            vmem(flat, low),
            vmem(by_run, low),
            vmem(heads, low),
            vmem(heads, low),
            vmem(heads, low),
            vmem(flat, low),
            vmem(flat, full),
            vmem((1, length), full),
            vmem((1, length), full),
            vmem((TILE, WIDE), full),
            vmem((TILE, WIDE), full),
            vmem((2,) + heads, low),
            vmem((2, 8, RUN, WIDE), low),
            vmem(heads, low),
            vmem((4, 2, per_device, RUN, WIDE), low),
            vmem((4 * HEAD, 4 * WIDE), low),
            vmem((4, 2, 4, 2, share, 4 * HEAD), low),
            vmem((4, 2, 2, share, 2 * FEED), low),
            vmem((2, rows, PIECE), full),
            vmem(block, low),
            vmem((2,) + block, low),
            vmem(block, full),
            vmem(block, low),
            vmem(block, low),
            vmem((1, width), full),
            vmem((3, 2, 2, quarter, rows), low),
            vmem(right.shape, low),
            vmem((2, 2, quarter, PIECE), low),
            vmem((2, share, 2 * PIECE), full),
            vmem((3, 2, 2, quarter, PIECE), low),
            vmem((4, 2, 2, quarter, PIECE), low),
            vmem((2, 2, quarter, PIECE), low),
            vmem((4, 2, quarter, PIECE), low),
            vmem((3, 2, quarter, PIECE), low),
            vmem((4, 2, 3, share, PIECE), low),
            dma((7,)),
            dma(()),
            dma((4,)),
            dma((4,)),
            dma((2,)),
            dma(()),
            dma((4, 2)),
            dma((8,)),
            dma((8,)),
            dma((8,)),
            dma(()),
            dma(()),
            dma((8,)),
            dma((4, 2)),
            dma((4,)),
            dma((2, 4)),
            dma((2,)),
            dma((3, 2)),
            dma((4, 2)),
            dma((2, 2)),
            dma((4, 2)),
            dma((3, 2, 3)),
            dma((4, 2, 3)),
        ],
        compiler_params=pltpu.CompilerParams(
            collective_id=2, has_side_effects=True, vmem_limit_bytes=62 * 1024 * 1024
        ),
        name="backward",
    )(
        order,
        ids,
        q_sorted,
        k_sorted.reshape(by_run),
        v_sorted.reshape(by_run),
        *arrays[3:],
    )


def by_heads(
    tokens,
    positions,
    gain_one,
    gain_two,
    w_query,
    w_key,
    w_value,
    w_out,
    w_gate,
    w_up,
    w_down,
    cotangent,
):
    rows, _, width = tokens.shape
    share = gain_one.shape[0]
    run_ids = positions[::RUN, 0] // RUN
    flat_in = tokens.reshape(rows, width)
    (
        near,
        far,
        normed,
        q_sorted,
        k_sorted,
        v_sorted,
        mixed_t,
        lse,
        mixed_low,
        middle,
        second,
        right,
        gains,
        tables,
        order,
        ids,
    ) = forward(
        flat_in,
        positions,
        jnp.broadcast_to(jnp.pad(run_ids, (0, WIDE - rows // RUN)), (8, WIDE)),
        gain_one.reshape(1, share),
        gain_two.reshape(1, share),
        w_query,
        w_key,
        w_value,
        w_out.T,
        w_gate,
        w_up,
        w_down.T,
        cotangent.reshape(rows, width),
    )
    input_grad, layer_out, grads = backward(
        order,
        ids,
        q_sorted,
        k_sorted,
        v_sorted,
        mixed_t,
        lse,
        cotangent.reshape(rows, width),
        second,
        normed,
        right,
        mixed_low,
        middle,
        near,
        far,
        flat_in,
        gains,
        tables,
    )
    splits, start = [], 0
    for wide in (
        w_gate.shape[1],
        w_up.shape[1],
        w_down.shape[0],
        w_query.shape[1],
        w_key.shape[1],
        w_value.shape[1],
        w_out.shape[0],
        4,
    ):
        splits.append(grads[:, start : start + wide])
        start += wide
    grad_gate, grad_up, grad_down, grad_query, grad_key, grad_value, grad_out, grad_gains = splits
    return (
        layer_out.reshape(rows, 1, width),
        input_grad.reshape(rows, 1, width),
        grad_gains[:, 0] + grad_gains[:, 2],
        grad_gains[:, 1] + grad_gains[:, 3],
        grad_query,
        grad_key,
        grad_value,
        grad_out.T,
        grad_gate,
        grad_up,
        grad_down.T,
    )


def solution(mesh):
    sizes = (mesh.shape["dp"], mesh.shape["context"], mesh.shape["tensor"])
    return jax.shard_map(
        by_heads if sizes == (2, 8, 2) else on_device,
        mesh=mesh,
        in_specs=(
            P("context", "dp", None),
            P("context", "dp"),
            P(("dp", "context")),
            P(("dp", "context")),
            P(("dp", "context"), "tensor"),
            P(("dp", "context"), "tensor"),
            P(("dp", "context"), "tensor"),
            P("tensor", ("dp", "context")),
            P(("dp", "context"), "tensor"),
            P(("dp", "context"), "tensor"),
            P("tensor", ("dp", "context")),
            P("context", "dp", None),
        ),
        out_specs=(
            P("context", "dp", None),
            P("context", "dp", None),
            P(("dp", "context")),
            P(("dp", "context")),
            P(("dp", "context"), "tensor"),
            P(("dp", "context"), "tensor"),
            P(("dp", "context"), "tensor"),
            P("tensor", ("dp", "context")),
            P(("dp", "context"), "tensor"),
            P(("dp", "context"), "tensor"),
            P("tensor", ("dp", "context")),
        ),
        check_vma=False,
    )
```

```python
import functools

import jax
import jax.numpy as jnp
from jax import lax
from jax.experimental import pallas as pl
from jax.experimental.pallas import tpu as pltpu
from jax.sharding import PartitionSpec as P

HEAD = 96


epsilon = 1e-05
theta_base = 100000.0
masked_value = -1e30


def norm_forward(values_in, gain_vec):
    inverse = lax.rsqrt(jnp.mean(values_in * values_in, axis=-1, keepdims=True) + epsilon)
    unit_vals = values_in * inverse
    return (unit_vals, inverse, (unit_vals * gain_vec.astype(jnp.float32)).astype(jnp.bfloat16))


def norm_backward(grad_in, unit_vals, inverse, gain_vec):
    scaled = grad_in * gain_vec.astype(jnp.float32)
    grad_vals = inverse * (
        scaled - unit_vals * jnp.mean(scaled * unit_vals, axis=-1, keepdims=True)
    )
    return (grad_vals, jnp.sum(grad_in * unit_vals, axis=0))


def rotate(values_in, cos_part, sin_part):
    half_size = values_in.shape[-1] // 2
    front_half = values_in[..., :half_size]
    back_half = values_in[..., half_size:]
    return jnp.concatenate(
        [
            front_half * cos_part - back_half * sin_part,
            back_half * cos_part + front_half * sin_part,
        ],
        axis=-1,
    )


def contract_rows(left_mat, right_mat):
    return lax.dot_general(
        left_mat, right_mat, (((0,), (0,)), ((), ())), preferred_element_type=jnp.float32
    )


def contract_cols(left_mat, right_mat):
    return lax.dot_general(
        left_mat, right_mat, (((1,), (1,)), ((), ())), preferred_element_type=jnp.float32
    )


def on_device(
    tokens,
    positions,
    gain_one,
    gain_two,
    w_query,
    w_key,
    w_value,
    w_out,
    w_gate,
    w_up,
    w_down,
    cotangent,
):
    slot_count, seq_count, model_width = tokens.shape
    row_count = slot_count * seq_count
    gathered = (
        lax.all_gather(gain_one, ("dp", "context"), axis=0, tiled=True),
        lax.all_gather(gain_two, ("dp", "context"), axis=0, tiled=True),
        lax.all_gather(w_query, ("dp", "context"), axis=0, tiled=True),
        lax.all_gather(w_key, ("dp", "context"), axis=0, tiled=True),
        lax.all_gather(w_value, ("dp", "context"), axis=0, tiled=True),
        lax.all_gather(w_out, ("dp", "context"), axis=1, tiled=True),
        lax.all_gather(w_gate, ("dp", "context"), axis=0, tiled=True),
        lax.all_gather(w_up, ("dp", "context"), axis=0, tiled=True),
        lax.all_gather(w_down, ("dp", "context"), axis=1, tiled=True),
    )
    full_one, full_two, query_mat, key_mat, value_mat, out_mat, gate_mat, up_mat, down_mat = (
        gathered
    )
    heads_kv = key_mat.shape[1] // HEAD
    heads_q = query_mat.shape[1] // HEAD
    group_size = heads_q // heads_kv
    score_scale = HEAD ** (-0.5)
    half_size = HEAD // 2
    inv_freqs = theta_base ** (-2.0 * jnp.arange(half_size, dtype=jnp.float32) / HEAD)
    angles = positions.astype(jnp.float32)[:, :, None] * inv_freqs
    cos_part = jnp.cos(angles)[:, :, None, :]
    sin_part = jnp.sin(angles)[:, :, None, :]
    flat_in = tokens.astype(jnp.float32).reshape(row_count, model_width)
    unit_one, inverse_one, normed = norm_forward(flat_in, full_one)
    query_proj = jnp.dot(normed, query_mat, preferred_element_type=jnp.float32).reshape(
        slot_count, seq_count, heads_q, HEAD
    )
    key_proj = jnp.dot(normed, key_mat, preferred_element_type=jnp.float32).reshape(
        slot_count, seq_count, heads_kv, HEAD
    )
    value_low = (
        jnp.dot(normed, value_mat, preferred_element_type=jnp.float32)
        .astype(jnp.bfloat16)
        .reshape(slot_count, seq_count, heads_kv * HEAD)
    )
    queries = rotate(query_proj, cos_part, sin_part).astype(jnp.bfloat16)
    keys_low = (
        rotate(key_proj, cos_part, sin_part)
        .astype(jnp.bfloat16)
        .reshape(slot_count, seq_count, heads_kv * HEAD)
    )
    query_seq = jnp.transpose(
        queries.reshape(slot_count, seq_count, heads_kv, group_size, HEAD), (1, 2, 3, 0, 4)
    )
    query_pos = positions.T
    stat_shape = (seq_count, heads_kv, group_size, slot_count)
    initial = (
        jnp.full(stat_shape, masked_value, jnp.float32),
        jnp.zeros(stat_shape, jnp.float32),
        jnp.zeros(stat_shape + (HEAD,), jnp.float32),
    )
    key_piece = lax.all_gather(keys_low, "context", axis=0, tiled=True)
    value_piece = lax.all_gather(value_low, "context", axis=0, tiled=True)
    pos_piece = lax.all_gather(positions, "context", axis=0, tiled=True)
    piece_len = key_piece.shape[0]
    key_seq = jnp.transpose(key_piece.reshape(piece_len, seq_count, heads_kv, HEAD), (1, 2, 0, 3))
    value_seq = jnp.transpose(
        value_piece.reshape(piece_len, seq_count, heads_kv, HEAD), (1, 2, 0, 3)
    )
    pos_seq = pos_piece.T

    def per_sequence(seq_items):
        peak_val, totals, accum_vals, query_one, qpos_one, key_one, value_one, kpos_one = seq_items
        raw_scores = (
            jnp.einsum("hgqd,hkd->hgqk", query_one, key_one, preferred_element_type=jnp.float32)
            * score_scale
        )
        allowed = kpos_one[None, None, None, :] <= qpos_one[None, None, :, None]
        masked = jnp.where(allowed, raw_scores, masked_value)
        new_peak = jnp.maximum(peak_val, jnp.max(masked, axis=-1))
        decay_vals = jnp.exp(peak_val - new_peak)
        weights = jnp.where(allowed, jnp.exp(masked - new_peak[..., None]), 0.0)
        totals = totals * decay_vals + jnp.sum(weights, axis=-1)
        accum_vals = accum_vals * decay_vals[..., None] + jnp.einsum(
            "hgqk,hkd->hgqd",
            weights.astype(jnp.bfloat16),
            value_one,
            preferred_element_type=jnp.float32,
        )
        return (new_peak, totals, accum_vals)

    peak_val, totals, accum_vals = lax.map(
        per_sequence,
        (initial[0], initial[1], initial[2], query_seq, query_pos, key_seq, value_seq, pos_seq),
    )
    log_total = peak_val + jnp.log(totals)
    mixed_seq = accum_vals / totals[..., None]
    mixed_low = (
        jnp.transpose(mixed_seq, (3, 0, 1, 2, 4))
        .reshape(row_count, heads_q * HEAD)
        .astype(jnp.bfloat16)
    )
    branch = lax.psum(
        jnp.dot(mixed_low, out_mat, preferred_element_type=jnp.float32).astype(jnp.bfloat16),
        "tensor",
    ).astype(jnp.float32)
    middle = flat_in + branch
    unit_two, inverse_two, second = norm_forward(middle, full_two)
    gate_vals = jnp.dot(second, gate_mat, preferred_element_type=jnp.float32)
    up_vals = jnp.dot(second, up_mat, preferred_element_type=jnp.float32)
    sigmoid_vals = jax.nn.sigmoid(gate_vals)
    silu_vals = gate_vals * sigmoid_vals
    hidden = (silu_vals * up_vals).astype(jnp.bfloat16)
    mlp_part = lax.psum(
        jnp.dot(hidden, down_mat, preferred_element_type=jnp.float32).astype(jnp.bfloat16), "tensor"
    ).astype(jnp.float32)
    layer_out = (middle + mlp_part).astype(jnp.bfloat16).reshape(slot_count, seq_count, model_width)
    regathered = (
        lax.all_gather(gain_one, ("dp", "context"), axis=0, tiled=True),
        lax.all_gather(gain_two, ("dp", "context"), axis=0, tiled=True),
        lax.all_gather(w_query, ("dp", "context"), axis=0, tiled=True),
        lax.all_gather(w_key, ("dp", "context"), axis=0, tiled=True),
        lax.all_gather(w_value, ("dp", "context"), axis=0, tiled=True),
        lax.all_gather(w_out, ("dp", "context"), axis=1, tiled=True),
        lax.all_gather(w_gate, ("dp", "context"), axis=0, tiled=True),
        lax.all_gather(w_up, ("dp", "context"), axis=0, tiled=True),
        lax.all_gather(w_down, ("dp", "context"), axis=1, tiled=True),
    )
    full_one, full_two, query_mat, key_mat, value_mat, out_mat, gate_mat, up_mat, down_mat = (
        regathered
    )
    grad_low = cotangent.reshape(row_count, model_width)
    grad_down = contract_rows(hidden, grad_low)
    grad_hidden = contract_cols(grad_low, down_mat)
    grad_gate_low = (
        grad_hidden * up_vals * sigmoid_vals * (1.0 + gate_vals * (1.0 - sigmoid_vals))
    ).astype(jnp.bfloat16)
    grad_up_low = (grad_hidden * silu_vals).astype(jnp.bfloat16)
    grad_gate = contract_rows(second, grad_gate_low)
    grad_up = contract_rows(second, grad_up_low)
    grad_second = lax.psum(
        (contract_cols(grad_gate_low, gate_mat) + contract_cols(grad_up_low, up_mat)).astype(
            jnp.bfloat16
        ),
        "tensor",
    ).astype(jnp.float32)
    grad_mid_norm, grad_gain_two = norm_backward(grad_second, unit_two, inverse_two, full_two)
    grad_middle = grad_low.astype(jnp.float32) + grad_mid_norm
    grad_mid_low = grad_middle.astype(jnp.bfloat16)
    grad_out = contract_rows(mixed_low, grad_mid_low)
    grad_mixed = contract_cols(grad_mid_low, out_mat).astype(jnp.bfloat16)
    grad_mixed_seq = jnp.transpose(
        grad_mixed.reshape(slot_count, seq_count, heads_kv, group_size, HEAD), (1, 2, 3, 0, 4)
    )
    delta_rows = jnp.sum(grad_mixed_seq.astype(jnp.float32) * mixed_seq, axis=-1)
    kv_width = heads_kv * HEAD

    def block_grads(grad_query_acc, key_blk, value_blk, pos_blk):
        block_len = key_blk.shape[0]
        key_seq = jnp.transpose(key_blk.reshape(block_len, seq_count, heads_kv, HEAD), (1, 2, 0, 3))
        value_seq = jnp.transpose(
            value_blk.reshape(block_len, seq_count, heads_kv, HEAD), (1, 2, 0, 3)
        )
        raw_scores = (
            jnp.einsum("shgqd,shkd->shgqk", query_seq, key_seq, preferred_element_type=jnp.float32)
            * score_scale
        )
        allowed = pos_blk.T[:, None, None, None, :] <= query_pos[:, None, None, :, None]
        prob_vals = jnp.where(
            allowed,
            jnp.exp(jnp.where(allowed, raw_scores - log_total[..., None], masked_value)),
            0.0,
        )
        grad_value_blk = jnp.einsum(
            "shgqk,shgqd->kshd",
            prob_vals.astype(jnp.bfloat16),
            grad_mixed_seq,
            preferred_element_type=jnp.float32,
        )
        grad_probs = jnp.einsum(
            "shgqd,shkd->shgqk", grad_mixed_seq, value_seq, preferred_element_type=jnp.float32
        )
        grad_scores = (prob_vals * (grad_probs - delta_rows[..., None])).astype(jnp.bfloat16)
        grad_query_acc = grad_query_acc + jnp.einsum(
            "shgqk,shkd->shgqd", grad_scores, key_seq, preferred_element_type=jnp.float32
        )
        grad_key_blk = jnp.einsum(
            "shgqk,shgqd->kshd", grad_scores, query_seq, preferred_element_type=jnp.float32
        )
        return (
            grad_query_acc,
            grad_key_blk.reshape(block_len, seq_count, kv_width),
            grad_value_blk.reshape(block_len, seq_count, kv_width),
        )

    zero_query = jnp.zeros(stat_shape + (HEAD,), jnp.float32)
    key_all, value_all, pos_all = (
        lax.all_gather(keys_low, "context", axis=0, tiled=True),
        lax.all_gather(value_low, "context", axis=0, tiled=True),
        lax.all_gather(positions, "context", axis=0, tiled=True),
    )
    total_len = key_all.shape[0]
    block_size = min(512, total_len)
    block_count = total_len // block_size

    def key_block(grad_query_acc, block_items):
        key_blk, value_blk, pos_blk = block_items
        grad_query_acc, grad_key_blk, grad_value_blk = block_grads(
            grad_query_acc, key_blk, value_blk, pos_blk
        )
        return (grad_query_acc, (grad_key_blk, grad_value_blk))

    grad_query_acc, (grad_keys_all, grad_values_all) = lax.scan(
        key_block,
        zero_query,
        (
            key_all.reshape(block_count, block_size, seq_count, kv_width),
            value_all.reshape(block_count, block_size, seq_count, kv_width),
            pos_all.reshape(block_count, block_size, seq_count),
        ),
    )
    grad_key_own, grad_value_own = (
        lax.psum_scatter(
            grad_keys_all.reshape(total_len, seq_count, kv_width).astype(jnp.bfloat16),
            "context",
            scatter_dimension=0,
            tiled=True,
        ).astype(jnp.float32),
        lax.psum_scatter(
            grad_values_all.reshape(total_len, seq_count, kv_width).astype(jnp.bfloat16),
            "context",
            scatter_dimension=0,
            tiled=True,
        ).astype(jnp.float32),
    )
    grad_rot_q = jnp.transpose(grad_query_acc * score_scale, (3, 0, 1, 2, 4)).reshape(
        slot_count, seq_count, heads_q, HEAD
    )
    grad_q_low = (
        rotate(grad_rot_q, cos_part, -sin_part)
        .reshape(row_count, heads_q * HEAD)
        .astype(jnp.bfloat16)
    )
    grad_rot_k = (grad_key_own * score_scale).reshape(slot_count, seq_count, heads_kv, HEAD)
    grad_k_low = (
        rotate(grad_rot_k, cos_part, -sin_part).reshape(row_count, kv_width).astype(jnp.bfloat16)
    )
    grad_v_low = grad_value_own.reshape(row_count, kv_width).astype(jnp.bfloat16)
    grad_query = contract_rows(normed, grad_q_low)
    grad_key = contract_rows(normed, grad_k_low)
    grad_value = contract_rows(normed, grad_v_low)
    grad_normed = lax.psum(
        (
            contract_cols(grad_q_low, query_mat)
            + contract_cols(grad_k_low, key_mat)
            + contract_cols(grad_v_low, value_mat)
        ).astype(jnp.bfloat16),
        "tensor",
    ).astype(jnp.float32)
    grad_in_norm, grad_gain_one = norm_backward(grad_normed, unit_one, inverse_one, full_one)
    input_grad = (grad_middle + grad_in_norm).reshape(slot_count, seq_count, model_width)
    reduced = (
        lax.psum_scatter(grad_gain_one, ("dp", "context"), scatter_dimension=0, tiled=True),
        lax.psum_scatter(grad_gain_two, ("dp", "context"), scatter_dimension=0, tiled=True),
        lax.psum_scatter(grad_query, ("dp", "context"), scatter_dimension=0, tiled=True),
        lax.psum_scatter(grad_key, ("dp", "context"), scatter_dimension=0, tiled=True),
        lax.psum_scatter(grad_value, ("dp", "context"), scatter_dimension=0, tiled=True),
        lax.psum_scatter(grad_out, ("dp", "context"), scatter_dimension=1, tiled=True),
        lax.psum_scatter(grad_gate, ("dp", "context"), scatter_dimension=0, tiled=True),
        lax.psum_scatter(grad_up, ("dp", "context"), scatter_dimension=0, tiled=True),
        lax.psum_scatter(grad_down, ("dp", "context"), scatter_dimension=1, tiled=True),
    )
    return (
        layer_out,
        input_grad,
        reduced[0],
        reduced[1],
        reduced[2],
        reduced[3],
        reduced[4],
        reduced[5],
        reduced[6],
        reduced[7],
        reduced[8],
    )


WIDE = 128
HALF = HEAD // 2
RUN = 256
TILE = 512
LOG2_E = 1.4426950408889634
MESH = pl.DeviceIdType.MESH
PIECE = 256
FEED = 512
VMEM_LIMIT = 56 * 1024 * 1024


def any_spec():
    return pl.BlockSpec(memory_space=pl.ANY)


def vmem_spec():
    return pl.BlockSpec(memory_space=pltpu.VMEM)


def place():
    return lax.axis_index("dp"), lax.axis_index("context"), lax.axis_index("tensor")


def greet(devices):
    barrier = pltpu.get_barrier_semaphore()
    for device in devices:
        pl.semaphore_signal(barrier, inc=1, device_id=device, device_id_type=MESH)
    pl.semaphore_wait(barrier, len(devices))


def sequence_others():
    row, spot, core = place()
    return [
        (row, lax.rem(spot + shift, 8), lax.rem(core + flip, 2))
        for shift in range(8)
        for flip in range(2)
        if shift or flip
    ]


def dot_f32(left, right):
    return jnp.dot(left, right, preferred_element_type=jnp.float32)


def remote(source, target, send, recv, device):
    return pltpu.make_async_remote_copy(
        src_ref=source,
        dst_ref=target,
        send_sem=send,
        recv_sem=recv,
        device_id=device,
        device_id_type=MESH,
    )


def move(source, target, send, recv, device, is_self):
    @pl.when(is_self)
    def _():
        pltpu.make_async_copy(source, target, recv).start()

    @pl.when(jnp.logical_not(is_self))
    def _():
        remote(source, target, send, recv, device).start()


def return_copies(ref, out, send, recv):
    row, spot, core = place()
    head = 2 * lax.rem(spot, 4) + core
    owner = spot // 4
    copies = []
    for step in range(8):
        chip = lax.rem(spot + step, 8)
        is_self = (owner == core) if step == 0 else False
        parts = (ref.at[chip], out.at[head], send.at[step], recv.at[head], (row, chip, owner))
        copies.append((parts, is_self))
    return copies


def start_return(copies):
    for parts, is_self in copies:
        if is_self is False:
            remote(*parts).start()
        else:
            move(*parts, is_self)


def finish_return(copies, out, send, recv):
    row, spot, core = place()
    for head in range(8):
        remote(
            out.at[head], out.at[head], send.at[0], recv.at[head], (row, spot, 1 - core)
        ).wait_recv()
    for parts, is_self in copies:
        if is_self is False:
            remote(*parts).wait_send()
        else:

            @pl.when(jnp.logical_not(is_self))
            def _():
                remote(*parts).wait_send()


def tile_at(index, size):
    return pl.ds(pl.multiple_of(index * size, size), size)


def causal(scores):
    keys = lax.broadcasted_iota(jnp.int32, scores.shape, 0)
    queries = lax.broadcasted_iota(jnp.int32, scores.shape, 1)
    return jnp.where(keys <= queries, scores, masked_value)


def neighbours():
    row, spot, core = place()
    level, column = spot // 2, lax.rem(spot, 2)
    beside_x = (1 - row, spot, core)
    beside_y = (row, 2 * level + 1 - column, core)
    along_z = [(row, 2 * lax.rem(level + k, 4) + column, core) for k in (1, 2, 3)]
    return row, level, column, beside_x, beside_y, along_z


class Gather:
    def __init__(self, own, whole, start, width, piece, sems):
        self.own, self.whole = own.at[:, pl.ds(start, width)], whole
        self.start, self.width = start, width
        names = ("send_z", "recv_z", "send_x", "recv_x", "send_y", "recv_y", "send_d", "recv_d")
        for name, sem in zip(names + ("local",), sems):
            setattr(self, name, sem.at[piece])

    def block(self, x, z, y, half=None):
        cut = self.width * 7 // 12 // WIDE * WIDE
        start, width = self.start, self.width
        if half == 0:
            width = cut
        elif half == 1:
            start, width = start + cut, width - cut
        return self.whole.at[x, z, y, :, pl.ds(start, width)]

    def arrived(self, target, recv_sem):
        device = neighbours()[3]
        remote(target, target, self.send_x.at[0], recv_sem, device).wait_recv()

    def copy_z(self, z, up):
        row, level, column, beside_x, beside_y = neighbours()[:5]
        core = place()[2]
        target = level + 1 if up else level - 1
        block = self.block(row, z, column)
        return remote(
            block,
            block,
            self.send_z.at[int(up), z],
            self.recv_z.at[z],
            (row, 2 * target + column, core),
        )

    def copies_xy(self, z):
        row, level, column, beside_x, beside_y = neighbours()[:5]
        block = self.block(row, z, column)
        return [
            remote(block, block, self.send_x.at[z], self.recv_x.at[z], beside_x),
            remote(block, block, self.send_y.at[z], self.recv_y.at[z], beside_y),
        ]

    def copies_diagonal(self, z):
        row, level, column, beside_x, beside_y = neighbours()[:5]
        by_y = self.block(1 - row, z, column, 1)
        by_x = self.block(row, z, 1 - column, 0)
        return [
            remote(by_y, by_y, self.send_d.at[0, z], self.recv_d.at[0, z], beside_y),
            remote(by_x, by_x, self.send_d.at[1, z], self.recv_d.at[1, z], beside_x),
        ]

    def own_copy(self):
        row, level, column = neighbours()[:3]
        return pltpu.make_async_copy(self.own, self.block(row, level, column), self.local)

    def each_at(self, hop, act):
        level = neighbours()[1]

        @pl.when(level >= hop)
        def _():
            act(level - hop, True)

        @pl.when(level + hop <= 3)
        def _():
            act(level + hop, False)

    def start_z(self, z, up):
        level = neighbours()[1]

        @pl.when(level < 3 if up else level > 0)
        def _():
            self.copy_z(z, up).start()

    def place_own(self):
        self.own_copy().start()

    def open(self):
        level = neighbours()[1]
        self.own_copy().wait()
        self.start_z(level, True)
        self.start_z(level, False)
        for copy in self.copies_xy(level):
            copy.start()

    def hop(self, hop):
        def act(z, up):
            row, level, column = neighbours()[:3]
            self.arrived(self.block(row, z, column), self.recv_z.at[z])
            self.start_z(z, up)
            for copy in self.copies_xy(z):
                copy.start()

        self.each_at(hop, act)

    def turn_diagonal(self, z):
        row, level, column = neighbours()[:3]
        by_y, by_x = self.copies_diagonal(z)
        self.arrived(self.block(1 - row, z, column), self.recv_x.at[z])
        by_y.start()
        self.arrived(self.block(row, z, 1 - column), self.recv_y.at[z])
        by_x.start()

    def diagonal(self, hop):
        if hop == 0:
            self.turn_diagonal(neighbours()[1])
        else:
            self.each_at(hop, lambda z, up: self.turn_diagonal(z))

    def finish(self):
        row, level, column = neighbours()[:3]
        for z in range(4):
            self.arrived(self.block(1 - row, z, 1 - column, 1), self.recv_d.at[0, z])
            self.arrived(self.block(1 - row, z, 1 - column, 0), self.recv_d.at[1, z])

    def close(self):
        level = neighbours()[1]

        def sent(z, up):
            @pl.when(level < 3 if up else level > 0)
            def _():
                self.copy_z(z, up).wait_send()

        sent(level, True)
        sent(level, False)
        for hop in range(1, 4):
            self.each_at(hop, sent)
        for z in range(4):
            for copy in self.copies_xy(z) + self.copies_diagonal(z):
                copy.wait_send()


def gather_sems(pieces):
    dma = pltpu.SemaphoreType.DMA
    shapes = [(2, 4), (4,), (4,), (4,), (4,), (4,), (2, 4), (2, 4), ()]
    return [dma((pieces,) + shape) for shape in shapes]


def forward_kernel(
    tokens,
    positions,
    freqs,
    ids_in,
    gain_one,
    gain_two,
    w_query,
    w_key,
    w_value,
    w_out_t,
    w_gate,
    w_up,
    w_down_t,
    cotangent,
    near,
    far,
    normed_out,
    q_out,
    k_out,
    v_out,
    mixed_t_out,
    lse_out,
    mixed_low_out,
    middle_out,
    second_out,
    right_out,
    gains_out,
    tables_out,
    order,
    ids_flat,
    near_own,
    far_own,
    unit,
    normed,
    tables,
    weight,
    extras,
    gain_rows,
    q_heads,
    kv_heads,
    q_slots,
    kv_slots,
    q_t,
    keys,
    v_t,
    mixed_t,
    lse,
    mixed,
    mixed_slots,
    mixed_heads,
    mixed_low,
    out_weight,
    part,
    part_other,
    second,
    cot,
    right,
    feed_weight,
    ids_all,
    ids,
    load_own,
    send_ids,
    recv_ids,
    load_ids,
    load_w,
    load_extra,
    load_out,
    load_feed,
    load_cot,
    save_right,
    saves,
    send_q,
    recv_q,
    send_kv,
    recv_kv,
    send_x,
    recv_x,
    send_m,
    recv_m,
    send_p,
    recv_p,
    *sems,
):
    row, spot, core = place()
    low, full = jnp.bfloat16, jnp.float32
    rows, width = tokens.shape
    share = near_own.shape[0]
    length = 8 * rows
    runs, tiles = length // RUN, length // TILE
    per_device = rows // RUN
    halves = TILE // RUN
    quarter = 4 * share
    sibling = (row, spot, 1 - core)
    out_width = w_out_t.shape[1]
    qkv_width = 16 * HEAD

    near_loads, far_loads, start = [], [], 0
    for ref in (w_query, w_key, w_value, w_out_t):
        if ref is w_out_t:
            start += WIDE
        target = near_own.at[:, pl.ds(start, ref.shape[1])]
        near_loads.append(pltpu.make_async_copy(ref, target, load_own.at[len(near_loads)]))
        start += ref.shape[1]
    for index, ref in enumerate((w_gate, w_up, w_down_t)):
        for piece in range(4):
            source = ref.at[:, pl.ds(piece * FEED, FEED)]
            target = far_own.at[:, pl.ds((3 * piece + index) * FEED, FEED)]
            far_loads.append(
                pltpu.make_async_copy(source, target, load_own.at[4 + 4 * index + piece])
            )
    for copy in near_loads + far_loads:
        copy.start()
    load_cotangent = pltpu.make_async_copy(cotangent, cot, load_cot)
    load_cotangent.start()
    line = lax.broadcasted_iota(jnp.int32, (WIDE, share), 0)
    gains = jnp.where(line == 0, gain_one[...].astype(full), 0.0)
    gains = jnp.where(line == 1, gain_two[...].astype(full), gains)
    near_own[:, qkv_width : qkv_width + WIDE] = gains.T.astype(low)

    first = Gather(near_own, near, 0, qkv_width + WIDE, 0, sems)
    outer = Gather(near_own, near, qkv_width + WIDE, out_width, 1, sems)
    feeds = [Gather(far_own, far, 3 * FEED * p, 3 * FEED, 2 + p, sems) for p in range(4)]
    gathers = [first, outer] + feeds
    for copy in near_loads:
        copy.wait()
    first.place_own()
    outer.place_own()
    for copy in far_loads:
        copy.wait()
    for gather in feeds:
        gather.place_own()
    greet(sequence_others() + [neighbours()[3]])
    first.open()

    for shift in range(1, 8):
        remote(
            ids_in,
            ids_all.at[spot],
            send_ids.at[shift],
            recv_ids.at[shift],
            (row, lax.rem(spot + shift, 8), core),
        ).start()
    ids_all[spot] = ids_in[...]

    values = tokens[...].astype(full)
    unit[...] = values * lax.rsqrt(jnp.mean(values * values, axis=-1, keepdims=True) + epsilon)
    angles = freqs[...] * positions[...].astype(full)
    tables[0] = jnp.cos(angles)
    tables[1] = jnp.sin(angles)

    first.hop(1)
    first.diagonal(0)
    first.hop(2)
    first.diagonal(1)
    first.hop(3)
    outer.open()
    first.diagonal(2)
    first.diagonal(3)
    outer.hop(1)
    feeds[0].open()
    for shift in range(1, 8):
        remote(
            ids_in,
            ids_all.at[lax.rem(spot + 8 - shift, 8)],
            send_ids.at[shift],
            recv_ids.at[shift],
            (row, lax.rem(spot + shift, 8), core),
        ).wait_recv()
    pltpu.make_async_copy(ids_all, ids, load_ids).start()
    first.finish()

    def load_group(group):
        lanes = pl.ds(group * 4 * HEAD, 4 * HEAD)
        return pltpu.make_async_copy(
            near.at[:, :, :, :, lanes], weight.at[group % 2], load_w.at[group % 2]
        )

    load_extras = pltpu.make_async_copy(
        near.at[:, :, :, :, pl.ds(qkv_width, WIDE)], extras, load_extra
    )
    load_out_weight = pltpu.make_async_copy(
        near.at[:, :, :, :, pl.ds(qkv_width + WIDE, out_width)], out_weight, load_out
    )
    load_extras.start()
    load_group(0).start()
    load_group(1).start()
    load_extras.wait()
    gain_rows[...] = extras[...].reshape(width, WIDE).T[0:8].astype(full)
    normed[...] = (unit[...] * gain_rows[0:1]).astype(low)
    for group in range(4):
        load_group(group).wait()
        proj = dot_f32(normed[...], weight[group % 2].reshape(width, 4 * HEAD)).T
        if group < 2:
            load_group(group + 2).start()
        for head in range(4):
            front = proj[head * HEAD : head * HEAD + HALF]
            back = proj[head * HEAD + HALF : (head + 1) * HEAD]
            if group < 3:
                front, back = (
                    front * tables[0] - back * tables[1],
                    back * tables[0] + front * tables[1],
                )
            for start, value in ((0, front.astype(low)), (HALF, back.astype(low))):
                for run in range(per_device):
                    piece = value[:, run * RUN : (run + 1) * RUN]
                    if group < 2:
                        q_heads[4 * group + head, run, start : start + HALF] = piece
                    else:
                        kv_heads[head, group - 2, run, start : start + HALF] = piece
        if group == 0:
            outer.hop(2)
            outer.diagonal(0)
        elif group == 1:
            outer.hop(3)
            outer.diagonal(1)
        elif group == 2:
            feeds[0].hop(1)
            outer.diagonal(2)

    outgoing = []
    for step in range(4):
        slot = lax.rem(spot + step, 4)
        chip = 4 * core + slot
        for other in range(2):
            is_self = jnp.logical_and(chip == spot, core == other)
            device = (row, chip, other)
            kv_parts = (
                kv_heads.at[slot, :, other],
                kv_slots.at[spot, :, other],
                send_kv.at[step, other],
                recv_kv.at[spot],
                device,
            )
            q_parts = (
                q_heads.at[2 * slot + other],
                q_slots.at[spot],
                send_q.at[step, other],
                recv_q.at[spot],
                device,
            )
            outgoing.append((kv_parts, is_self))
            outgoing.append((q_parts, is_self))
    for parts, is_self in outgoing:
        move(*parts, is_self)
    outer.diagonal(3)
    feeds[0].hop(2)
    feeds[0].diagonal(0)
    feeds[0].hop(3)
    outer.finish()
    load_out_weight.start()
    feeds[1].open()
    feeds[0].diagonal(1)
    feeds[0].diagonal(2)

    def hand_on(source):
        block = kv_slots.at[source, :, core]
        return remote(block, block, send_x.at[source], recv_x.at[source], sibling)

    for step in range(8):
        source = lax.rem(spot + step, 8)
        block = kv_slots.at[source, :, core]
        remote(block, block, send_x.at[source], recv_kv.at[source], sibling).wait_recv()
        hand_on(source).start()
    for step in range(8):
        remote(
            q_slots.at[step], q_slots.at[step], send_x.at[step], recv_q.at[step], sibling
        ).wait_recv()
        hand_on(step).wait()
    feeds[0].diagonal(3)
    feeds[1].hop(1)

    pltpu.make_async_copy(ids_all, ids, load_ids).wait()

    def find_run(index, carry):
        device, piece = 0, 0
        for run in range(runs):
            here = ids[run // per_device, 0, run % per_device] == index
            device = jnp.where(here, run // per_device, device)
            piece = jnp.where(here, run % per_device, piece)
        order[index, 0] = device
        order[index, 1] = piece
        found = ids[index // per_device, 0, index % per_device]
        order[runs + index, 0] = lax.div(found, per_device)
        order[runs + index, 1] = lax.rem(found, per_device)
        ids_flat[index] = found
        return carry

    lax.fori_loop(0, runs, find_run, 0)

    def sort_run(index, carry):
        device, piece = order[index, 0], order[index, 1]
        cols = tile_at(index, RUN)
        q_t[:, cols] = q_slots[device, piece]
        keys[index] = kv_slots[device, 0, piece].T
        v_t[:, cols] = kv_slots[device, 1, piece]
        return carry

    lax.fori_loop(0, runs, sort_run, 0)
    scale = HEAD ** (-0.5) * LOG2_E

    def query_tile(index, carry):
        cols = tile_at(index, TILE)
        queries = q_t[:, cols]

        def step(scores, block, peak, total, mix):
            high = jnp.maximum(peak, jnp.max(scores, axis=0, keepdims=True))
            decay = jnp.exp2(peak - high)
            weights = jnp.exp2(scores - high)
            total = total * decay + jnp.sum(weights, axis=0, keepdims=True)
            mix = mix * decay + dot_f32(v_t[:, tile_at(block, TILE)], weights.astype(low))
            return high, total, mix

        def scores_of(block):
            held = keys[pl.ds(block * halves, halves)].reshape(TILE, HEAD)
            return dot_f32(held, queries) * scale

        state = (
            jnp.full((1, TILE), masked_value, full),
            jnp.zeros((1, TILE), full),
            jnp.zeros((HEAD, TILE), full),
        )
        state = step(causal(scores_of(index)), index, *state)
        peak, total, mix = lax.fori_loop(
            0, index, lambda block, now: step(scores_of(block), block, *now), state
        )
        mix = mix / total
        mixed_t[:, cols] = mix
        lse[:, cols] = peak + jnp.log2(total)
        for half in range(halves):
            mixed[index * halves + half] = mix[:, half * RUN : (half + 1) * RUN].astype(low)

        hooks = {
            1: [(feeds[1].hop, 2)],
            2: [(feeds[1].hop, 3), (feeds[1].diagonal, 0)],
            4: [(feeds[1].diagonal, 1)],
            5: [(feeds[1].diagonal, 2)],
            6: [(feeds[1].diagonal, 3)],
        }
        for when, acts in hooks.items():

            @pl.when(index == when)
            def _():
                for act, hop in acts:
                    act(hop)
                if when == 2:
                    feeds[2].open()

        return carry

    lax.fori_loop(0, tiles, query_tile, 0)

    def unsort_run(run, carry):
        index = ids[run // per_device, 0, run % per_device]
        mixed_slots[run // per_device, run % per_device] = mixed[index]
        return carry

    lax.fori_loop(0, runs, unsort_run, 0)
    copies = return_copies(mixed_slots, mixed_heads, send_m, recv_m)
    start_return(copies)
    early_saves = [
        pltpu.make_async_copy(source, target, saves.at[index])
        for index, (source, target) in enumerate(
            [
                (normed, normed_out),
                (q_t, q_out),
                (keys, k_out),
                (v_t, v_out),
                (mixed_t, mixed_t_out),
                (lse, lse_out),
                (gain_rows, gains_out),
                (tables, tables_out),
            ]
        )
    ]
    for copy in early_saves:
        copy.start()
    feeds[2].hop(1)
    feeds[2].diagonal(0)
    feeds[2].hop(2)
    feeds[2].hop(3)
    feeds[3].open()
    feeds[2].diagonal(1)
    finish_return(copies, mixed_heads, send_m, recv_m)

    load_out_weight.wait()
    for run in range(per_device):
        side = mixed_heads[:, run].reshape(8 * HEAD, RUN)
        mixed_low[run * RUN : (run + 1) * RUN] = side.T

    def pair_copy(index):
        cut = pl.ds(index * quarter, quarter)
        return remote(
            part.at[:, cut], part_other.at[:, cut], send_p.at[index], recv_p.at[index], sibling
        )

    for index in range(4):
        block = out_weight[index // 2, 2 * (index % 2) : 2 * (index % 2) + 2]
        term = contract_cols(mixed_low[...], block.reshape(quarter, out_width))
        part[:, index * quarter : (index + 1) * quarter] = term.astype(low)
        pair_copy(index).start()
    feeds[2].diagonal(2)
    feeds[3].hop(1)
    load_cotangent.wait()
    for index in range(4):
        pair_copy(index).wait()
    chunk = rows // 8

    def norm_block(index, carry):
        cut = tile_at(index, chunk)
        sums = part[cut].astype(full) + part_other[cut].astype(full)
        values = tokens[cut].astype(full) + sums
        unit[cut] = values
        inverse = lax.rsqrt(jnp.mean(values * values, axis=-1, keepdims=True) + epsilon)
        second[cut] = (values * inverse * gain_rows[1:2]).astype(low)
        return carry

    lax.fori_loop(0, 8, norm_block, 0)
    late_saves = [
        pltpu.make_async_copy(source, target, saves.at[8 + index])
        for index, (source, target) in enumerate(
            [(mixed_low, mixed_low_out), (unit, middle_out), (second, second_out)]
        )
    ]
    for copy in late_saves:
        copy.start()

    def load_feed_weight(index, kind):
        piece, half = index // 2, lax.rem(index, 2)
        start = (3 * piece + kind) * FEED + half * PIECE
        lanes = pl.ds(pl.multiple_of(start, PIECE), PIECE)
        return pltpu.make_async_copy(
            far.at[:, :, :, :, lanes], feed_weight.at[half, kind], load_feed.at[half, kind]
        )

    def save_piece(piece):
        lanes = pl.ds(piece * 3 * FEED, 3 * FEED)
        return pltpu.make_async_copy(
            right.at[:, lanes], right_out.at[:, lanes], save_right.at[piece]
        )

    def feed_block(index, carry):
        piece, half = index // 2, lax.rem(index, 2)
        for when in range(4):

            @pl.when(index == 2 * when)
            def _():
                feeds[when].finish()

        @pl.when(half == 0)
        def _():
            for offset in range(2):
                for kind in range(3):
                    load_feed_weight(index + offset, kind).start()

        values = []
        for kind, left in enumerate((second, second, cot)):
            load_feed_weight(index, kind).wait()
            values.append(dot_f32(left[...], feed_weight[half, kind].reshape(width, PIECE)))
        gate, up, grad_hidden = values
        sigmoid = jax.nn.sigmoid(gate)
        silu = gate * sigmoid
        grad_gate = grad_hidden * up * sigmoid * (1.0 + gate * (1.0 - sigmoid))
        for kind, value in enumerate((grad_gate, grad_hidden * silu, silu * up)):
            start = (3 * piece + kind) * FEED + half * PIECE
            right[:, pl.ds(pl.multiple_of(start, PIECE), PIECE)] = value.astype(low)

        hooks = {
            1: [(feeds[2].diagonal, 3), (feeds[3].hop, 2), (feeds[3].diagonal, 0)],
            2: [(feeds[3].hop, 3)],
            3: [(feeds[3].diagonal, 1)],
            4: [(feeds[3].diagonal, 2)],
            5: [(feeds[3].diagonal, 3)],
        }
        for when, acts in hooks.items():

            @pl.when(index == when)
            def _():
                for act, hop in acts:
                    act(hop)

        for when in range(4):

            @pl.when(index == 2 * when + 1)
            def _():
                save_piece(when).start()

        return carry

    lax.fori_loop(0, 8, feed_block, 0)
    for gather in gathers:
        gather.close()
    for parts, is_self in outgoing:

        @pl.when(jnp.logical_not(is_self))
        def _():
            remote(*parts).wait_send()

    for shift in range(1, 8):
        remote(
            ids_in,
            ids_all.at[spot],
            send_ids.at[shift],
            recv_ids.at[shift],
            (row, lax.rem(spot + shift, 8), core),
        ).wait_send()
    for copy in early_saves + late_saves + [save_piece(piece) for piece in range(4)]:
        copy.wait()


def forward(
    tokens,
    positions,
    ids,
    gain_one,
    gain_two,
    w_query,
    w_key,
    w_value,
    w_out_t,
    w_gate,
    w_up,
    w_down_t,
    cotangent,
):
    dma = pltpu.SemaphoreType.DMA
    vmem = pltpu.VMEM
    low, full = jnp.bfloat16, jnp.float32
    rows, width = tokens.shape
    share, hidden_width = w_gate.shape
    out_width = w_out_t.shape[1]
    near_width = 16 * HEAD + out_width + WIDE
    length = 8 * rows
    per_device = rows // RUN
    heads = (8, per_device, HEAD, RUN)
    both = (2, per_device, HEAD, RUN)
    by_run = (length // RUN, RUN, HEAD)
    flat = (HEAD, length)
    smem_spec = pl.BlockSpec(memory_space=pltpu.SMEM)
    shape = jax.ShapeDtypeStruct
    return pl.pallas_call(
        forward_kernel,
        in_specs=[vmem_spec()] * 6 + [any_spec()] * 8,
        out_specs=[any_spec()] * 14 + [smem_spec] * 2,
        out_shape=[
            shape((2, 4, 2, share, near_width), low),
            shape((2, 4, 2, share, 3 * hidden_width), low),
            shape((rows, width), low),
            shape(flat, low),
            shape(by_run, low),
            shape(flat, low),
            shape(flat, full),
            shape((1, length), full),
            shape((rows, out_width), low),
            shape((rows, width), full),
            shape((rows, width), low),
            shape((rows, 3 * hidden_width), low),
            shape((8, width), full),
            shape((2, HALF, rows), full),
            shape((2 * length // RUN, 2), jnp.int32),
            shape((length // RUN,), jnp.int32),
        ],
        scratch_shapes=[
            vmem((share, near_width), low),
            vmem((share, 3 * hidden_width), low),
            vmem((rows, width), full),
            vmem((rows, width), low),
            vmem((2, HALF, rows), full),
            vmem((2, 2, 4, 2, share, 4 * HEAD), low),
            vmem((2, 4, 2, share, WIDE), low),
            vmem((8, width), full),
            vmem(heads, low),
            vmem((4,) + both, low),
            vmem(heads, low),
            vmem((8,) + both, low),
            vmem(flat, low),
            vmem(by_run, low),
            vmem(flat, low),
            vmem(flat, full),
            vmem((1, length), full),
            vmem((length // RUN, HEAD, RUN), low),
            vmem(heads, low),
            vmem(heads, low),
            vmem((rows, out_width), low),
            vmem((2, 4, 2, share, out_width), low),
            vmem((rows, width), low),
            vmem((rows, width), low),
            vmem((rows, width), low),
            vmem((rows, width), low),
            vmem((rows, 3 * hidden_width), low),
            vmem((2, 3, 2, 4, 2, share, PIECE), low),
            vmem((8, 8, WIDE), jnp.int32),
            pltpu.SMEM((8, 8, WIDE), jnp.int32),
            dma((16,)),
            dma((8,)),
            dma((8,)),
            dma(()),
            dma((2,)),
            dma(()),
            dma(()),
            dma((2, 3)),
            dma(()),
            dma((4,)),
            dma((12,)),
            dma((4, 2)),
            dma((8,)),
            dma((4, 2)),
            dma((8,)),
            dma((8,)),
            dma((8,)),
            dma((8,)),
            dma((8,)),
            dma((4,)),
            dma((4,)),
        ]
        + gather_sems(6),
        compiler_params=pltpu.CompilerParams(
            collective_id=1, has_side_effects=True, vmem_limit_bytes=VMEM_LIMIT
        ),
        name="forward",
    )(
        tokens,
        positions,
        (theta_base ** (-2.0 * jnp.arange(HALF, dtype=jnp.float32) / HEAD)).reshape(HALF, 1),
        ids,
        gain_one,
        gain_two,
        w_query,
        w_key,
        w_value,
        w_out_t,
        w_gate,
        w_up,
        w_down_t,
        cotangent,
    )


SECOND, THIRD, LAST = 2, 3, 4


class Reduce:
    def __init__(self, n, changes, refs):
        (
            self.left_t,
            self.right,
            self.gains,
            self.own,
            self.out,
            self.save,
            self.send_one,
            self.recv_one,
            self.send_two,
            self.recv_two,
            self.kept,
            self.recv_three,
            self.ss_one,
            self.rs_one,
            self.ss_two,
            self.rs_two,
            self.ss_three,
            self.rs_three,
        ) = refs
        self.n, self.changes = n, changes
        self.share = self.own.shape[1]

    def columns(self, step, kind):
        held = self.right.shape[1] // (2 * PIECE)
        start = lax.rem(step, held) * 2 * PIECE + kind * PIECE
        return pl.ds(pl.multiple_of(start, PIECE), PIECE)

    def saving(self, step):
        slot = lax.rem(step, 2)
        pieces = self.changes[0] // 3
        place = jnp.where(step < self.changes[0], lax.rem(step, 3) * pieces + step // 3, step)
        cut = pl.ds(pl.multiple_of(place * 2 * PIECE, 2 * PIECE), 2 * PIECE)
        return pltpu.make_async_copy(self.own.at[slot], self.out.at[:, cut], self.save.at[slot])

    def product(self, step, kind, x, y):
        left = jnp.where(lax.rem(step, 3) == 2, 0, 1)
        left = jnp.where(step >= self.changes[0], 2, left)
        left = jnp.where(step >= self.changes[1], 0, left)
        term = jnp.dot(
            self.left_t[left, x, y],
            self.right[:, self.columns(step, kind)],
            preferred_element_type=jnp.float32,
        )
        if kind == 1:
            term = jnp.where(step == self.n - 1, self.gains[x, y].astype(jnp.float32), term)
        return term

    def x_first(self, step, kind):
        return 1 if kind == 0 else jnp.where(lax.rem(step, 5) == 4, 1, 0)

    def beside(self, by_x):
        row, level, column = neighbours()[:3]
        core = place()[2]
        other_row = by_x * (1 - row) + (1 - by_x) * row
        other_column = by_x * column + (1 - by_x) * (1 - column)
        return (other_row, 2 * level + other_column, core)

    def first_copy(self, step, kind):
        out, into = lax.rem(step, 3), lax.rem(step, 5)
        return remote(
            self.send_one.at[out, kind],
            self.recv_one.at[into, kind],
            self.ss_one.at[out, kind],
            self.rs_one.at[into, kind],
            self.beside(self.x_first(step, kind)),
        )

    def second_copy(self, step, kind):
        out, into = lax.rem(step, 2), lax.rem(step, 5)
        return remote(
            self.send_two.at[out, kind],
            self.recv_two.at[into, kind],
            self.ss_two.at[out, kind],
            self.rs_two.at[into, kind],
            self.beside(1 - self.x_first(step, kind)),
        )

    def third_copy(self, step, kind, k):
        row, level, column, beside_x, beside_y, along_z = neighbours()
        target = lax.rem(level + k + 1, 4)
        out, into = lax.rem(step, 3), lax.rem(step, 4)
        return remote(
            self.kept.at[out, kind, pl.ds(pl.multiple_of(target * self.share, 16), self.share)],
            self.recv_three.at[into, kind, k],
            self.ss_three.at[out, kind, k],
            self.rs_three.at[into, kind, k],
            along_z[k],
        )

    def first(self, step):
        row, level, column = neighbours()[:3]
        slot = lax.rem(step, 3)
        for kind in range(2):
            by_x = self.x_first(step, kind)
            for half in range(2):
                x = by_x * (1 - row) + (1 - by_x) * half
                y = by_x * half + (1 - by_x) * (1 - column)
                self.send_one[slot, kind, half] = self.product(step, kind, x, y).astype(
                    jnp.bfloat16
                )
            self.first_copy(step, kind).start()

    def second(self, step):
        row, level, column = neighbours()[:3]
        slot, came, keep = lax.rem(step, 2), lax.rem(step, 5), lax.rem(step, 3)
        for kind in range(2):
            self.first_copy(step, kind).wait()
        for kind in range(2):
            by_x = self.x_first(step, kind)
            x = by_x * row + (1 - by_x) * (1 - row)
            y = by_x * (1 - column) + (1 - by_x) * column
            arrived = self.recv_one.at[came, kind]
            mine = by_x * column + (1 - by_x) * row
            away = self.product(step, kind, x, y) + arrived[1 - mine].astype(jnp.float32)
            self.send_two[slot, kind] = away.astype(jnp.bfloat16)
            here = self.product(step, kind, row, column) + arrived[mine].astype(jnp.float32)
            self.kept[keep, kind] = here.astype(jnp.bfloat16)
        for kind in range(2):
            self.second_copy(step, kind).start()

    def third(self, step):
        came, keep = lax.rem(step, 5), lax.rem(step, 3)
        for kind in range(2):
            self.second_copy(step, kind).wait()
            here = self.kept[keep, kind].astype(jnp.float32) + self.recv_two[came, kind].astype(
                jnp.float32
            )
            self.kept[keep, kind] = here.astype(jnp.bfloat16)
            for k in range(3):
                self.third_copy(step, kind, k).start()

    def last(self, step):
        level = neighbours()[1]
        came, keep = lax.rem(step, 4), lax.rem(step, 3)
        mine = pl.ds(pl.multiple_of(level * self.share, 16), self.share)

        @pl.when(step >= 2)
        def _():
            self.saving(step - 2).wait()

        for kind in range(2):
            total = self.kept[keep, kind, mine].astype(jnp.float32)
            for k in range(3):
                self.third_copy(step, kind, k).wait()
                total = total + self.recv_three[came, kind, k].astype(jnp.float32)
            self.own[lax.rem(step, 2), :, kind * PIECE : (kind + 1) * PIECE] = total
        self.saving(step).start()

    def turn(self, step):
        for stage, lag in (
            (self.first, 0),
            (self.second, SECOND),
            (self.third, THIRD),
            (self.last, LAST),
        ):

            @pl.when(jnp.logical_and(step >= lag, step < self.n + lag))
            def _():
                stage(step - lag)


def backward_kernel(
    order,
    ids,
    q_in,
    k_in,
    v_in,
    mixed_t_in,
    lse_in,
    cotangent,
    second_in,
    normed_in,
    right_in,
    mixed_low,
    middle,
    near,
    far,
    tokens,
    gains_in,
    tables,
    input_grad,
    layer_out,
    grads,
    q,
    q_t,
    k,
    k_t,
    v,
    d_own,
    d_slots,
    d,
    d_t,
    dq_t,
    lse,
    delta,
    dk,
    dv,
    dq_slots,
    dkv_sorted,
    dkv_slots,
    dkv_other,
    dq_own,
    dkv_own,
    weight,
    middle_ring,
    input_ring,
    part,
    part_other,
    total,
    staged,
    grad_mid,
    gain_two_grad,
    left_t,
    right,
    gains,
    own,
    send_one,
    recv_one,
    send_two,
    recv_two,
    kept,
    recv_three,
    loads,
    load_left_sem,
    load_w,
    load_ring,
    save_rows,
    save_sem,
    send_d,
    recv_d,
    send_q,
    recv_q,
    send_x,
    recv_x,
    send_k,
    recv_k,
    send_p,
    recv_p,
    save,
    *sems,
):
    row, spot, core = place()
    low, full = jnp.bfloat16, jnp.float32
    rows, width = staged.shape
    length = 8 * rows
    runs, tiles = length // RUN, length // TILE
    per_device = rows // RUN
    halves = TILE // RUN
    share = width // 16
    quarter = 4 * share
    sibling = (row, spot, 1 - core)
    qkv_width = 16 * HEAD
    out_width = mixed_low.shape[1]
    n = grads.shape[1] // (2 * PIECE)
    near_at = right_in.shape[1] // (2 * PIECE)
    changes = (near_at, near_at + qkv_width // (2 * PIECE))
    sums = Reduce(
        n,
        changes,
        (left_t, right, gains, own, grads, save)
        + (send_one, recv_one, send_two, recv_two, kept, recv_three)
        + sems,
    )

    def stage(source):
        return pltpu.make_async_copy(source, staged, load_left_sem)

    def turn_left(index, source):
        for piece in range(4):
            turned = source[:, piece * quarter : (piece + 1) * quarter].T
            for inner in range(4):
                x, z, y = piece // 2, 2 * (piece % 2) + inner // 2, inner % 2
                left_t[index, x, y, z * share : (z + 1) * share] = turned[
                    inner * share : (inner + 1) * share
                ]

    early_loads = [
        pltpu.make_async_copy(source, target, loads.at[index])
        for index, (source, target) in enumerate(
            [
                (right_in, right),
                (q_in, q_t),
                (k_in, k),
                (v_in, d_t),
                (mixed_t_in, dq_t),
                (lse_in, lse),
                (middle, total),
            ]
        )
    ]


    def load_block(index, piece, part_of, start):
        lanes = pl.ds(3 * FEED * piece + start + part_of * PIECE, PIECE)
        levels = pl.ds(2 * lax.rem(index, 2), 2)
        return pltpu.make_async_copy(
            far.at[index // 2, levels, :, :, lanes], held_block(piece, part_of), load_w.at[piece]
        )

    def held_block(piece, part_of):
        levels = pl.ds(2 * (part_of % 2), 2)
        return weight.at[piece, part_of // 2, levels, :, :, pl.ds(0, PIECE)]

    def load_blocks(index, piece, start, parts):
        for part_of in range(parts):
            load_block(index, piece, part_of, start).start()

    def row_products(start, parts, landing):
        def block(index, carry):
            term = jnp.zeros((rows, quarter), full)
            for piece in range(4):
                for part_of in range(parts):
                    load_block(index, piece, part_of, start).wait()
                for part_of in range(parts):
                    at = 3 * FEED * piece + start + part_of * PIECE
                    term = term + contract_cols(
                        right[:, at : at + PIECE],
                        held_block(piece, part_of)[...].reshape(quarter, PIECE),
                    )

                @pl.when(index + 1 < 4)
                def _():
                    load_blocks(index + 1, piece, start, parts)

            part[:, tile_at(index, quarter)] = term.astype(low)
            pair_copy(index, landing).start()
            return carry

        lax.fori_loop(0, 4, block, 0)

    def pair_copy(index, landing):
        cut = pl.ds(pl.multiple_of(index * quarter, quarter), quarter)
        return remote(
            part.at[:, cut],
            part_other.at[landing, :, cut],
            send_p.at[index],
            recv_p.at[landing, index],
            sibling,
        )

    def second_back():
        row_products(0, 4, 0)
        for index in range(2):
            load_out_weight(index).start()

    def load_out_weight(index):
        lanes = pl.ds(qkv_width + WIDE + index * 4 * HEAD, 4 * HEAD)
        return pltpu.make_async_copy(
            near.at[:, :, :, :, lanes], weight.at[index], load_w.at[index]
        )

    d_copies = []
    for step in range(4):
        slot = lax.rem(spot + step, 4)
        chip = 4 * core + slot
        for other in range(2):
            parts = (
                d_own.at[2 * slot + other],
                d_slots.at[spot],
                send_d.at[step, other],
                recv_d.at[spot],
                (row, chip, other),
            )
            d_copies.append((parts, jnp.logical_and(chip == spot, core == other)))

    def middle_back():
        for index in range(4):
            pair_copy(index, 0).wait()
        early_loads[6].wait()
        chunk = rows // 8

        def block(index, gain_grad):
            cut = tile_at(index, chunk)
            grad = part[cut].astype(full) + part_other[0, cut].astype(full)
            values = total[cut]
            inverse = lax.rsqrt(jnp.mean(values * values, axis=-1, keepdims=True) + epsilon)
            unit = values * inverse
            scaled = grad * gains_in[1:2]
            mean = jnp.mean(scaled * unit, axis=-1, keepdims=True)
            result = staged[cut].astype(full) + inverse * (scaled - unit * mean)
            total[cut] = result
            grad_mid[cut] = result.astype(low)
            return gain_grad + jnp.sum(grad * unit, axis=0, keepdims=True)

        gain_two_grad[...] = lax.fori_loop(0, 8, block, jnp.zeros((1, width), full))
        for index in range(2):
            load_out_weight(index).wait()
            grad = dot_f32(grad_mid[...], weight[index].reshape(width, 4 * HEAD)).T.astype(low)
            for head in range(4):
                for run in range(per_device):
                    d_own[4 * index + head, run] = grad[
                        head * HEAD : (head + 1) * HEAD, run * RUN : (run + 1) * RUN
                    ]
        for parts, is_self in d_copies:
            move(*parts, is_self)


    def prepare():
        for copy in early_loads[1:6]:
            copy.wait()
        for index in range(tiles):
            cut = pl.ds(index * TILE, TILE)
            q[cut] = q_t[:, cut].T
            k_t[:, cut] = k[halves * index : halves * (index + 1)].reshape(TILE, HEAD).T
            v[cut] = d_t[:, cut].T

    def take_cotangents():
        for index in range(8):
            remote(
                d_slots.at[index], d_slots.at[index], send_d.at[0, 0], recv_d.at[index], sibling
            ).wait_recv()

        def sort_run(index, carry):
            cols = tile_at(index, RUN)
            run = d_slots[order[index, 0], order[index, 1]]
            d_t[:, cols] = run
            d[cols] = run.T
            delta[:, cols] = jnp.sum(run.astype(full) * dq_t[:, cols], axis=0, keepdims=True)
            return carry

        lax.fori_loop(0, runs, sort_run, 0)
        dq_t[...] = jnp.zeros_like(dq_t)

    scale = HEAD ** (-0.5)

    def key_tile(block):
        cut = tile_at(block, TILE)
        both = pl.ds(block * halves, halves)
        keys, values = k[both].reshape(TILE, HEAD), v[cut]
        keys_t = k_t[:, cut]
        dk[...] = jnp.zeros_like(dk)
        dv[...] = jnp.zeros_like(dv)

        def query_tile(index, diagonal):
            cols = tile_at(index, TILE)
            scores = dot_f32(keys, q_t[:, cols]) * (scale * LOG2_E)
            if diagonal:
                scores = causal(scores)
            probs = jnp.exp2(scores - lse[:, cols])
            dv[...] += dot_f32(probs.astype(low), d[cols])
            grad_probs = dot_f32(values, d_t[:, cols])
            grad_scores = (probs * (grad_probs - delta[:, cols])).astype(low)
            dk[...] += dot_f32(grad_scores, q[cols])
            dq_t[:, cols] += dot_f32(keys_t, grad_scores)

        query_tile(block, True)

        def later(index, inner):
            query_tile(index, False)
            return inner

        lax.fori_loop(block + 1, tiles, later, 0)
        for kind, value in enumerate(((dk[...] * scale).T.astype(low), dv[...].T.astype(low))):
            for half in range(halves):
                dkv_sorted[block * halves + half, kind] = value[:, half * RUN : (half + 1) * RUN]

    def key_tiles(start, stop):
        def one(block, carry):
            key_tile(block)
            return carry

        lax.fori_loop(start, stop, one, 0)

    swap = remote(dkv_slots.at[:, :, 1 - core], dkv_other, send_x, recv_x, sibling)
    dq_copies = return_copies(dq_slots, dq_own, send_q, recv_q)
    slot, owner = lax.rem(spot, 4), spot // 4
    dkv_copies = []
    for step in range(8):
        chip = lax.rem(spot + step, 8)
        parts = (
            dkv_slots.at[:, chip, core],
            dkv_own.at[slot, :, core],
            send_k.at[step],
            recv_k.at[slot, core],
            (row, chip, owner),
        )
        dkv_copies.append((parts, (owner == core) if step == 0 else False))

    def send_back():
        def unsort_run(run, carry):
            index = ids[run]
            for kind in range(2):
                dkv_slots[kind, run // per_device, run % per_device] = dkv_sorted[index, kind]
            return carry

        lax.fori_loop(0, runs, unsort_run, 0)
        swap.start()

        def turn_run(index, carry):
            value = dq_t[:, tile_at(index, RUN)] * scale
            d_slots[index // per_device, index % per_device] = value.astype(low)
            return carry

        lax.fori_loop(0, runs, turn_run, 0)

        def unsort_queries(run, carry):
            value = d_slots[order[runs + run, 0], order[runs + run, 1]]
            dq_slots[run // per_device, run % per_device] = value
            return carry

        lax.fori_loop(0, runs, unsort_queries, 0)
        start_return(dq_copies)

    def add_pairs():
        swap.wait()
        for chip in range(8):
            both = dkv_slots[:, chip, core].astype(full) + dkv_other[:, chip].astype(full)
            dkv_slots[:, chip, core] = both.astype(low)
        start_return(dkv_copies)


    def feed_forward():
        row_products(2 * FEED, 2, 1)
        for group in range(4):
            load_group(group).start()

    save_layer = pltpu.make_async_copy(part, layer_out, save_sem)

    def finish_layer():
        for index in range(4):
            pair_copy(index, 1).wait()
        pieces = width // PIECE

        def load_piece(index):
            lanes = pl.ds(index * PIECE, PIECE)
            return pltpu.make_async_copy(
                middle.at[:, lanes], middle_ring.at[index % 2], load_ring.at[index % 2]
            )

        load_piece(0).start()
        for index in range(pieces):
            if index + 1 < pieces:
                load_piece(index + 1).start()
            load_piece(index).wait()
            cut = pl.ds(index * PIECE, PIECE)
            value = part[:, cut].astype(full) + part_other[1, :, cut].astype(full)
            part[:, cut] = (value + middle_ring[index % 2]).astype(low)
        save_layer.start()


    def load_group(group):
        lanes = pl.ds(group * 4 * HEAD, 4 * HEAD)
        return pltpu.make_async_copy(
            near.at[:, :, :, :, lanes], weight.at[group], load_w.at[group]
        )

    load_mixed = pltpu.make_async_copy(
        mixed_low, right.at[:, pl.ds(qkv_width, out_width)], loads.at[0]
    )

    def project_back():
        load_mixed.start()
        for head in range(8):
            remote(
                dq_own.at[head], dq_own.at[head], send_q.at[0], recv_q.at[head], sibling
            ).wait_recv()
        for slot_in in range(4):
            for core_in in range(2):
                target = dkv_own.at[slot_in, :, core_in]
                remote(
                    target, target, send_k.at[0], recv_k.at[slot_in, core_in], sibling
                ).wait_recv()
        for group in range(4):
            for run in range(per_device):
                cols = slice(run * RUN, (run + 1) * RUN)
                turned = []
                for head in range(4):
                    if group < 2:
                        value = dq_own[4 * group + head, run]
                    else:
                        value = dkv_own[head, group - 2, run]
                    if group < 3:
                        front, back = value[:HALF].astype(full), value[HALF:].astype(full)
                        cos_part, sin_part = tables[0, :, cols], tables[1, :, cols]
                        turned.append((front * cos_part + back * sin_part).astype(low))
                        turned.append((back * cos_part - front * sin_part).astype(low))
                    else:
                        turned.append(value)
                right[cols, group * 4 * HEAD : (group + 1) * 4 * HEAD] = jnp.concatenate(
                    turned, axis=0
                ).T
        start = qkv_width + out_width
        right[:, start : start + PIECE] = jnp.zeros((rows, PIECE), low)
        load_mixed.wait()

    def project_normed():
        save_layer.wait()
        for group in range(4):
            load_group(group).wait()
        stage(tokens).start()

        def block(index, carry):
            term = jnp.zeros((rows, quarter), full)
            for group in range(4):
                held = weight[group, index // 2, pl.ds(2 * lax.rem(index, 2), 2)]
                term = term + contract_cols(
                    right[:, group * 4 * HEAD : (group + 1) * 4 * HEAD],
                    held.reshape(quarter, 4 * HEAD),
                )
            part[:, tile_at(index, quarter)] = term.astype(low)
            pair_copy(index, 0).start()
            return carry

        lax.fori_loop(0, 4, block, 0)

    def save_input(index):
        cut = tile_at(index, rows // 8)
        slot = lax.rem(index, 2)
        return pltpu.make_async_copy(
            input_ring.at[slot], input_grad.at[cut], save_rows.at[slot]
        )

    def norm_back():
        stage(tokens).wait()
        for index in range(4):
            pair_copy(index, 0).wait()
        chunk = rows // 8

        def block(index, gain_grad):
            cut = tile_at(index, chunk)
            grad = part[cut].astype(full) + part_other[0, cut].astype(full)
            values = staged[cut].astype(full)
            inverse = lax.rsqrt(jnp.mean(values * values, axis=-1, keepdims=True) + epsilon)
            unit = values * inverse
            scaled = grad * gains_in[0:1]
            mean = jnp.mean(scaled * unit, axis=-1, keepdims=True)
            result = total[cut] + inverse * (scaled - unit * mean)

            @pl.when(index >= 2)
            def _():
                save_input(index - 2).wait()

            input_ring[lax.rem(index, 2)] = result.reshape(chunk, 1, width)
            save_input(index).start()
            return gain_grad + jnp.sum(grad * unit, axis=0, keepdims=True)

        gain_one_grad = lax.fori_loop(0, 8, block, jnp.zeros((1, width), full))
        lines = []
        for value in (gain_one_grad, gain_two_grad[...]):
            high = value.astype(low).astype(full)
            lines.append((high, value - high))
        which = lax.broadcasted_iota(jnp.int32, (WIDE, width), 0)
        table = jnp.zeros((WIDE, width), full)
        for index, line in enumerate((lines[0][0], lines[1][0], lines[0][1], lines[1][1])):
            table = jnp.where(which == index, line, table)
        columns = table.T.astype(low)
        gains[...] = jnp.zeros_like(gains)
        for x in range(2):
            for z in range(4):
                for y in range(2):
                    start = ((x * 4 + z) * 2 + y) * share
                    gains[x, y, z * share : (z + 1) * share, :WIDE] = columns[start : start + share]

    def take_normed():
        stage(normed_in).start()
        stage(normed_in).wait()
        turn_left(2, staged)

    def start_forward():
        for piece in range(4):
            load_blocks(0, piece, 2 * FEED, 2)

    stage(second_in).start()
    for copy in early_loads:
        copy.start()
    for piece in range(4):
        load_blocks(0, piece, 0, 4)
    greet(sequence_others() + [neighbours()[3]])
    stage(second_in).wait()
    turn_left(1, staged)
    stage(cotangent).start()
    early_loads[0].wait()
    stage(cotangent).wait()

    plan = {
        0: [second_back, lambda: turn_left(0, staged)],
        1: [middle_back],
        2: [prepare],
        3: [start_forward, take_cotangents],
        4: [lambda: key_tiles(0, 2)],
        5: [lambda: key_tiles(2, 4)],
        6: [lambda: key_tiles(4, 8), send_back],
        7: [add_pairs, feed_forward],
        8: [finish_layer, take_normed],
        10: [project_back],
        11: [project_normed],
        13: [norm_back],
        14: [lambda: turn_left(0, grad_mid)],
    }

    def run(step, carry):
        sums.turn(step)
        for when, tasks in plan.items():

            @pl.when(step == when)
            def _():
                for task in tasks:
                    task()

        return carry

    lax.fori_loop(0, n + LAST, run, 0)
    for index in (6, 7):
        save_input(index).wait()
    for step in (n - 2, n - 1):
        sums.saving(step).wait()
    for copies in (d_copies, dq_copies, dkv_copies):
        for parts, is_self in copies:
            if is_self is False:
                remote(*parts).wait_send()
            else:

                @pl.when(jnp.logical_not(is_self))
                def _():
                    remote(*parts).wait_send()


def backward(order, ids, *arrays):
    dma = pltpu.SemaphoreType.DMA
    vmem = pltpu.VMEM
    low, full = jnp.bfloat16, jnp.float32
    q_sorted, k_sorted, v_sorted, mixed_t, lse, cotangent, second, normed, right = arrays[:9]
    mixed_low, middle, near, far, tokens, gains, tables = arrays[9:]
    rows, width = cotangent.shape
    length = 8 * rows
    share = width // 16
    wide = right.shape[1] + 16 * HEAD + mixed_low.shape[1] + PIECE
    quarter = 4 * share
    per_device = rows // RUN
    heads = (8, per_device, HEAD, RUN)
    tall, flat = (length, HEAD), (HEAD, length)
    by_run = (length // RUN, RUN, HEAD)
    block = (rows, width)
    smem_spec = pl.BlockSpec(memory_space=pltpu.SMEM)
    shape = jax.ShapeDtypeStruct
    return pl.pallas_call(
        backward_kernel,
        in_specs=[smem_spec] * 2 + [any_spec()] * 14 + [vmem_spec()] * 2,
        out_specs=[any_spec()] * 3,
        out_shape=[shape((rows, 1, width), full), shape(block, low), shape((share, wide), full)],
        scratch_shapes=[
            vmem(tall, low),
            vmem(flat, low),
            vmem(by_run, low),
            vmem(flat, low),
            vmem(tall, low),
            vmem(heads, low),
            vmem(heads, low),
            vmem(tall, low),
            vmem(flat, low),
            vmem(flat, full),
            vmem((1, length), full),
            vmem((1, length), full),
            vmem((TILE, HEAD), full),
            vmem((TILE, HEAD), full),
            vmem(heads, low),
            vmem((length // RUN, 2, HEAD, RUN), low),
            vmem((2,) + heads, low),
            vmem((2, 8, HEAD, RUN), low),
            vmem(heads, low),
            vmem((4, 2, per_device, HEAD, RUN), low),
            vmem((4, 2, 4, 2, share, 4 * HEAD), low),
            vmem((2, rows, PIECE), full),
            vmem((2, rows // 8, 1, width), full),
            vmem(block, low),
            vmem((2,) + block, low),
            vmem(block, full),
            vmem(block, low),
            vmem(block, low),
            vmem((1, width), full),
            vmem((3, 2, 2, quarter, rows), low),
            vmem(right.shape, low),
            vmem((2, 2, quarter, PIECE), low),
            vmem((2, share, 2 * PIECE), full),
            vmem((3, 2, 2, quarter, PIECE), low),
            vmem((5, 2, 2, quarter, PIECE), low),
            vmem((2, 2, quarter, PIECE), low),
            vmem((5, 2, quarter, PIECE), low),
            vmem((3, 2, quarter, PIECE), low),
            vmem((4, 2, 3, share, PIECE), low),
            dma((7,)),
            dma(()),
            dma((4,)),
            dma((2,)),
            dma((2,)),
            dma(()),
            dma((4, 2)),
            dma((8,)),
            dma((8,)),
            dma((8,)),
            dma(()),
            dma(()),
            dma((8,)),
            dma((4, 2)),
            dma((4,)),
            dma((2, 4)),
            dma((2,)),
            dma((3, 2)),
            dma((5, 2)),
            dma((2, 2)),
            dma((5, 2)),
            dma((3, 2, 3)),
            dma((4, 2, 3)),
        ],
        compiler_params=pltpu.CompilerParams(
            collective_id=2, has_side_effects=True, vmem_limit_bytes=62 * 1024 * 1024
        ),
        name="backward",
    )(
        order,
        ids,
        *arrays,
    )


def by_heads(
    tokens,
    positions,
    gain_one,
    gain_two,
    w_query,
    w_key,
    w_value,
    w_out,
    w_gate,
    w_up,
    w_down,
    cotangent,
):
    rows, _, width = tokens.shape
    share = gain_one.shape[0]
    run_ids = positions[::RUN, 0] // RUN
    flat_in = tokens.reshape(rows, width)
    (
        near,
        far,
        normed,
        q_sorted,
        k_sorted,
        v_sorted,
        mixed_t,
        lse,
        mixed_low,
        middle,
        second,
        right,
        gains,
        tables,
        order,
        ids,
    ) = forward(
        flat_in,
        positions.reshape(1, rows),
        jnp.broadcast_to(jnp.pad(run_ids, (0, WIDE - rows // RUN)), (8, WIDE)),
        gain_one.reshape(1, share),
        gain_two.reshape(1, share),
        w_query,
        w_key,
        w_value,
        w_out.T,
        w_gate,
        w_up,
        w_down.T,
        cotangent.reshape(rows, width),
    )
    input_grad, layer_out, grads = backward(
        order,
        ids,
        q_sorted,
        k_sorted,
        v_sorted,
        mixed_t,
        lse,
        cotangent.reshape(rows, width),
        second,
        normed,
        right,
        mixed_low,
        middle,
        near,
        far,
        flat_in,
        gains,
        tables,
    )
    splits, start = [], 0
    for wide in (
        w_gate.shape[1],
        w_up.shape[1],
        w_down.shape[0],
        w_query.shape[1],
        w_key.shape[1],
        w_value.shape[1],
        w_out.shape[0],
        4,
    ):
        splits.append(grads[:, start : start + wide])
        start += wide
    grad_gate, grad_up, grad_down, grad_query, grad_key, grad_value, grad_out, grad_gains = splits
    return (
        layer_out.reshape(rows, 1, width),
        input_grad,
        grad_gains[:, 0] + grad_gains[:, 2],
        grad_gains[:, 1] + grad_gains[:, 3],
        grad_query,
        grad_key,
        grad_value,
        grad_out.T,
        grad_gate,
        grad_up,
        grad_down.T,
    )


def solution(mesh):
    sizes = (mesh.shape["dp"], mesh.shape["context"], mesh.shape["tensor"])
    return jax.shard_map(
        by_heads if sizes == (2, 8, 2) else on_device,
        mesh=mesh,
        in_specs=(
            P("context", "dp", None),
            P("context", "dp"),
            P(("dp", "context")),
            P(("dp", "context")),
            P(("dp", "context"), "tensor"),
            P(("dp", "context"), "tensor"),
            P(("dp", "context"), "tensor"),
            P("tensor", ("dp", "context")),
            P(("dp", "context"), "tensor"),
            P(("dp", "context"), "tensor"),
            P("tensor", ("dp", "context")),
            P("context", "dp", None),
        ),
        out_specs=(
            P("context", "dp", None),
            P("context", "dp", None),
            P(("dp", "context")),
            P(("dp", "context")),
            P(("dp", "context"), "tensor"),
            P(("dp", "context"), "tensor"),
            P(("dp", "context"), "tensor"),
            P("tensor", ("dp", "context")),
            P(("dp", "context"), "tensor"),
            P(("dp", "context"), "tensor"),
            P("tensor", ("dp", "context")),
        ),
        check_vma=False,
    )
```

```python
import functools
import types

import jax
import jax.numpy as jnp
from jax import lax
from jax.experimental import pallas as pl
from jax.experimental.pallas import tpu as pltpu
from jax.sharding import PartitionSpec as P

HEAD = 96


epsilon = 1e-05
theta_base = 100000.0
masked_value = -1e30


def norm_forward(values_in, gain_vec):
    inverse = lax.rsqrt(jnp.mean(values_in * values_in, axis=-1, keepdims=True) + epsilon)
    unit_vals = values_in * inverse
    return (unit_vals, inverse, (unit_vals * gain_vec.astype(jnp.float32)).astype(jnp.bfloat16))


def norm_backward(grad_in, unit_vals, inverse, gain_vec):
    scaled = grad_in * gain_vec.astype(jnp.float32)
    grad_vals = inverse * (
        scaled - unit_vals * jnp.mean(scaled * unit_vals, axis=-1, keepdims=True)
    )
    return (grad_vals, jnp.sum(grad_in * unit_vals, axis=0))


def rotate(values_in, cos_part, sin_part):
    half_size = values_in.shape[-1] // 2
    front_half = values_in[..., :half_size]
    back_half = values_in[..., half_size:]
    return jnp.concatenate(
        [
            front_half * cos_part - back_half * sin_part,
            back_half * cos_part + front_half * sin_part,
        ],
        axis=-1,
    )


def contract_rows(left_mat, right_mat):
    return lax.dot_general(
        left_mat, right_mat, (((0,), (0,)), ((), ())), preferred_element_type=jnp.float32
    )


def contract_cols(left_mat, right_mat):
    return lax.dot_general(
        left_mat, right_mat, (((1,), (1,)), ((), ())), preferred_element_type=jnp.float32
    )


def on_device(
    tokens,
    positions,
    gain_one,
    gain_two,
    w_query,
    w_key,
    w_value,
    w_out,
    w_gate,
    w_up,
    w_down,
    cotangent,
):
    slot_count, seq_count, model_width = tokens.shape
    row_count = slot_count * seq_count
    gathered = (
        lax.all_gather(gain_one, ("dp", "context"), axis=0, tiled=True),
        lax.all_gather(gain_two, ("dp", "context"), axis=0, tiled=True),
        lax.all_gather(w_query, ("dp", "context"), axis=0, tiled=True),
        lax.all_gather(w_key, ("dp", "context"), axis=0, tiled=True),
        lax.all_gather(w_value, ("dp", "context"), axis=0, tiled=True),
        lax.all_gather(w_out, ("dp", "context"), axis=1, tiled=True),
        lax.all_gather(w_gate, ("dp", "context"), axis=0, tiled=True),
        lax.all_gather(w_up, ("dp", "context"), axis=0, tiled=True),
        lax.all_gather(w_down, ("dp", "context"), axis=1, tiled=True),
    )
    full_one, full_two, query_mat, key_mat, value_mat, out_mat, gate_mat, up_mat, down_mat = (
        gathered
    )
    heads_kv = key_mat.shape[1] // HEAD
    heads_q = query_mat.shape[1] // HEAD
    group_size = heads_q // heads_kv
    score_scale = HEAD ** (-0.5)
    half_size = HEAD // 2
    inv_freqs = theta_base ** (-2.0 * jnp.arange(half_size, dtype=jnp.float32) / HEAD)
    angles = positions.astype(jnp.float32)[:, :, None] * inv_freqs
    cos_part = jnp.cos(angles)[:, :, None, :]
    sin_part = jnp.sin(angles)[:, :, None, :]
    flat_in = tokens.astype(jnp.float32).reshape(row_count, model_width)
    unit_one, inverse_one, normed = norm_forward(flat_in, full_one)
    query_proj = jnp.dot(normed, query_mat, preferred_element_type=jnp.float32).reshape(
        slot_count, seq_count, heads_q, HEAD
    )
    key_proj = jnp.dot(normed, key_mat, preferred_element_type=jnp.float32).reshape(
        slot_count, seq_count, heads_kv, HEAD
    )
    value_low = (
        jnp.dot(normed, value_mat, preferred_element_type=jnp.float32)
        .astype(jnp.bfloat16)
        .reshape(slot_count, seq_count, heads_kv * HEAD)
    )
    queries = rotate(query_proj, cos_part, sin_part).astype(jnp.bfloat16)
    keys_low = (
        rotate(key_proj, cos_part, sin_part)
        .astype(jnp.bfloat16)
        .reshape(slot_count, seq_count, heads_kv * HEAD)
    )
    query_seq = jnp.transpose(
        queries.reshape(slot_count, seq_count, heads_kv, group_size, HEAD), (1, 2, 3, 0, 4)
    )
    query_pos = positions.T
    stat_shape = (seq_count, heads_kv, group_size, slot_count)
    initial = (
        jnp.full(stat_shape, masked_value, jnp.float32),
        jnp.zeros(stat_shape, jnp.float32),
        jnp.zeros(stat_shape + (HEAD,), jnp.float32),
    )
    key_piece = lax.all_gather(keys_low, "context", axis=0, tiled=True)
    value_piece = lax.all_gather(value_low, "context", axis=0, tiled=True)
    pos_piece = lax.all_gather(positions, "context", axis=0, tiled=True)
    piece_len = key_piece.shape[0]
    key_seq = jnp.transpose(key_piece.reshape(piece_len, seq_count, heads_kv, HEAD), (1, 2, 0, 3))
    value_seq = jnp.transpose(
        value_piece.reshape(piece_len, seq_count, heads_kv, HEAD), (1, 2, 0, 3)
    )
    pos_seq = pos_piece.T

    def per_sequence(seq_items):
        peak_val, totals, accum_vals, query_one, qpos_one, key_one, value_one, kpos_one = seq_items
        raw_scores = (
            jnp.einsum("hgqd,hkd->hgqk", query_one, key_one, preferred_element_type=jnp.float32)
            * score_scale
        )
        allowed = kpos_one[None, None, None, :] <= qpos_one[None, None, :, None]
        masked = jnp.where(allowed, raw_scores, masked_value)
        new_peak = jnp.maximum(peak_val, jnp.max(masked, axis=-1))
        decay_vals = jnp.exp(peak_val - new_peak)
        weights = jnp.where(allowed, jnp.exp(masked - new_peak[..., None]), 0.0)
        totals = totals * decay_vals + jnp.sum(weights, axis=-1)
        accum_vals = accum_vals * decay_vals[..., None] + jnp.einsum(
            "hgqk,hkd->hgqd",
            weights.astype(jnp.bfloat16),
            value_one,
            preferred_element_type=jnp.float32,
        )
        return (new_peak, totals, accum_vals)

    peak_val, totals, accum_vals = lax.map(
        per_sequence,
        (initial[0], initial[1], initial[2], query_seq, query_pos, key_seq, value_seq, pos_seq),
    )
    log_total = peak_val + jnp.log(totals)
    mixed_seq = accum_vals / totals[..., None]
    mixed_low = (
        jnp.transpose(mixed_seq, (3, 0, 1, 2, 4))
        .reshape(row_count, heads_q * HEAD)
        .astype(jnp.bfloat16)
    )
    branch = lax.psum(
        jnp.dot(mixed_low, out_mat, preferred_element_type=jnp.float32).astype(jnp.bfloat16),
        "tensor",
    ).astype(jnp.float32)
    middle = flat_in + branch
    unit_two, inverse_two, second = norm_forward(middle, full_two)
    gate_vals = jnp.dot(second, gate_mat, preferred_element_type=jnp.float32)
    up_vals = jnp.dot(second, up_mat, preferred_element_type=jnp.float32)
    sigmoid_vals = jax.nn.sigmoid(gate_vals)
    silu_vals = gate_vals * sigmoid_vals
    hidden = (silu_vals * up_vals).astype(jnp.bfloat16)
    mlp_part = lax.psum(
        jnp.dot(hidden, down_mat, preferred_element_type=jnp.float32).astype(jnp.bfloat16), "tensor"
    ).astype(jnp.float32)
    layer_out = (middle + mlp_part).astype(jnp.bfloat16).reshape(slot_count, seq_count, model_width)
    regathered = (
        lax.all_gather(gain_one, ("dp", "context"), axis=0, tiled=True),
        lax.all_gather(gain_two, ("dp", "context"), axis=0, tiled=True),
        lax.all_gather(w_query, ("dp", "context"), axis=0, tiled=True),
        lax.all_gather(w_key, ("dp", "context"), axis=0, tiled=True),
        lax.all_gather(w_value, ("dp", "context"), axis=0, tiled=True),
        lax.all_gather(w_out, ("dp", "context"), axis=1, tiled=True),
        lax.all_gather(w_gate, ("dp", "context"), axis=0, tiled=True),
        lax.all_gather(w_up, ("dp", "context"), axis=0, tiled=True),
        lax.all_gather(w_down, ("dp", "context"), axis=1, tiled=True),
    )
    full_one, full_two, query_mat, key_mat, value_mat, out_mat, gate_mat, up_mat, down_mat = (
        regathered
    )
    grad_low = cotangent.reshape(row_count, model_width)
    grad_down = contract_rows(hidden, grad_low)
    grad_hidden = contract_cols(grad_low, down_mat)
    grad_gate_low = (
        grad_hidden * up_vals * sigmoid_vals * (1.0 + gate_vals * (1.0 - sigmoid_vals))
    ).astype(jnp.bfloat16)
    grad_up_low = (grad_hidden * silu_vals).astype(jnp.bfloat16)
    grad_gate = contract_rows(second, grad_gate_low)
    grad_up = contract_rows(second, grad_up_low)
    grad_second = lax.psum(
        (contract_cols(grad_gate_low, gate_mat) + contract_cols(grad_up_low, up_mat)).astype(
            jnp.bfloat16
        ),
        "tensor",
    ).astype(jnp.float32)
    grad_mid_norm, grad_gain_two = norm_backward(grad_second, unit_two, inverse_two, full_two)
    grad_middle = grad_low.astype(jnp.float32) + grad_mid_norm
    grad_mid_low = grad_middle.astype(jnp.bfloat16)
    grad_out = contract_rows(mixed_low, grad_mid_low)
    grad_mixed = contract_cols(grad_mid_low, out_mat).astype(jnp.bfloat16)
    grad_mixed_seq = jnp.transpose(
        grad_mixed.reshape(slot_count, seq_count, heads_kv, group_size, HEAD), (1, 2, 3, 0, 4)
    )
    delta_rows = jnp.sum(grad_mixed_seq.astype(jnp.float32) * mixed_seq, axis=-1)
    kv_width = heads_kv * HEAD

    def block_grads(grad_query_acc, key_blk, value_blk, pos_blk):
        block_len = key_blk.shape[0]
        key_seq = jnp.transpose(key_blk.reshape(block_len, seq_count, heads_kv, HEAD), (1, 2, 0, 3))
        value_seq = jnp.transpose(
            value_blk.reshape(block_len, seq_count, heads_kv, HEAD), (1, 2, 0, 3)
        )
        raw_scores = (
            jnp.einsum("shgqd,shkd->shgqk", query_seq, key_seq, preferred_element_type=jnp.float32)
            * score_scale
        )
        allowed = pos_blk.T[:, None, None, None, :] <= query_pos[:, None, None, :, None]
        prob_vals = jnp.where(
            allowed,
            jnp.exp(jnp.where(allowed, raw_scores - log_total[..., None], masked_value)),
            0.0,
        )
        grad_value_blk = jnp.einsum(
            "shgqk,shgqd->kshd",
            prob_vals.astype(jnp.bfloat16),
            grad_mixed_seq,
            preferred_element_type=jnp.float32,
        )
        grad_probs = jnp.einsum(
            "shgqd,shkd->shgqk", grad_mixed_seq, value_seq, preferred_element_type=jnp.float32
        )
        grad_scores = (prob_vals * (grad_probs - delta_rows[..., None])).astype(jnp.bfloat16)
        grad_query_acc = grad_query_acc + jnp.einsum(
            "shgqk,shkd->shgqd", grad_scores, key_seq, preferred_element_type=jnp.float32
        )
        grad_key_blk = jnp.einsum(
            "shgqk,shgqd->kshd", grad_scores, query_seq, preferred_element_type=jnp.float32
        )
        return (
            grad_query_acc,
            grad_key_blk.reshape(block_len, seq_count, kv_width),
            grad_value_blk.reshape(block_len, seq_count, kv_width),
        )

    zero_query = jnp.zeros(stat_shape + (HEAD,), jnp.float32)
    key_all, value_all, pos_all = (
        lax.all_gather(keys_low, "context", axis=0, tiled=True),
        lax.all_gather(value_low, "context", axis=0, tiled=True),
        lax.all_gather(positions, "context", axis=0, tiled=True),
    )
    total_len = key_all.shape[0]
    block_size = min(512, total_len)
    block_count = total_len // block_size

    def key_block(grad_query_acc, block_items):
        key_blk, value_blk, pos_blk = block_items
        grad_query_acc, grad_key_blk, grad_value_blk = block_grads(
            grad_query_acc, key_blk, value_blk, pos_blk
        )
        return (grad_query_acc, (grad_key_blk, grad_value_blk))

    grad_query_acc, (grad_keys_all, grad_values_all) = lax.scan(
        key_block,
        zero_query,
        (
            key_all.reshape(block_count, block_size, seq_count, kv_width),
            value_all.reshape(block_count, block_size, seq_count, kv_width),
            pos_all.reshape(block_count, block_size, seq_count),
        ),
    )
    grad_key_own, grad_value_own = (
        lax.psum_scatter(
            grad_keys_all.reshape(total_len, seq_count, kv_width).astype(jnp.bfloat16),
            "context",
            scatter_dimension=0,
            tiled=True,
        ).astype(jnp.float32),
        lax.psum_scatter(
            grad_values_all.reshape(total_len, seq_count, kv_width).astype(jnp.bfloat16),
            "context",
            scatter_dimension=0,
            tiled=True,
        ).astype(jnp.float32),
    )
    grad_rot_q = jnp.transpose(grad_query_acc * score_scale, (3, 0, 1, 2, 4)).reshape(
        slot_count, seq_count, heads_q, HEAD
    )
    grad_q_low = (
        rotate(grad_rot_q, cos_part, -sin_part)
        .reshape(row_count, heads_q * HEAD)
        .astype(jnp.bfloat16)
    )
    grad_rot_k = (grad_key_own * score_scale).reshape(slot_count, seq_count, heads_kv, HEAD)
    grad_k_low = (
        rotate(grad_rot_k, cos_part, -sin_part).reshape(row_count, kv_width).astype(jnp.bfloat16)
    )
    grad_v_low = grad_value_own.reshape(row_count, kv_width).astype(jnp.bfloat16)
    grad_query = contract_rows(normed, grad_q_low)
    grad_key = contract_rows(normed, grad_k_low)
    grad_value = contract_rows(normed, grad_v_low)
    grad_normed = lax.psum(
        (
            contract_cols(grad_q_low, query_mat)
            + contract_cols(grad_k_low, key_mat)
            + contract_cols(grad_v_low, value_mat)
        ).astype(jnp.bfloat16),
        "tensor",
    ).astype(jnp.float32)
    grad_in_norm, grad_gain_one = norm_backward(grad_normed, unit_one, inverse_one, full_one)
    input_grad = (grad_middle + grad_in_norm).reshape(slot_count, seq_count, model_width)
    reduced = (
        lax.psum_scatter(grad_gain_one, ("dp", "context"), scatter_dimension=0, tiled=True),
        lax.psum_scatter(grad_gain_two, ("dp", "context"), scatter_dimension=0, tiled=True),
        lax.psum_scatter(grad_query, ("dp", "context"), scatter_dimension=0, tiled=True),
        lax.psum_scatter(grad_key, ("dp", "context"), scatter_dimension=0, tiled=True),
        lax.psum_scatter(grad_value, ("dp", "context"), scatter_dimension=0, tiled=True),
        lax.psum_scatter(grad_out, ("dp", "context"), scatter_dimension=1, tiled=True),
        lax.psum_scatter(grad_gate, ("dp", "context"), scatter_dimension=0, tiled=True),
        lax.psum_scatter(grad_up, ("dp", "context"), scatter_dimension=0, tiled=True),
        lax.psum_scatter(grad_down, ("dp", "context"), scatter_dimension=1, tiled=True),
    )
    return (
        layer_out,
        input_grad,
        reduced[0],
        reduced[1],
        reduced[2],
        reduced[3],
        reduced[4],
        reduced[5],
        reduced[6],
        reduced[7],
        reduced[8],
    )


WIDE = 128
HALF = HEAD // 2
RUN = 256
TILE = 512
LOG2_E = 1.4426950408889634
MESH = pl.DeviceIdType.MESH
PIECE = 256
FEED = 512
VMEM_LIMIT = 56 * 1024 * 1024


def any_spec():
    return pl.BlockSpec(memory_space=pl.ANY)


def vmem_spec():
    return pl.BlockSpec(memory_space=pltpu.VMEM)


def place():
    return lax.axis_index("dp"), lax.axis_index("context"), lax.axis_index("tensor")


def greet(devices):
    barrier = pltpu.get_barrier_semaphore()
    for device in devices:
        pl.semaphore_signal(barrier, inc=1, device_id=device, device_id_type=MESH)
    pl.semaphore_wait(barrier, len(devices))


def sequence_others():
    row, spot, core = place()
    return [
        (row, lax.rem(spot + shift, 8), lax.rem(core + flip, 2))
        for shift in range(8)
        for flip in range(2)
        if shift or flip
    ]


def dot_f32(left, right):
    return jnp.dot(left, right, preferred_element_type=jnp.float32)


def remote(source, target, send, recv, device):
    return pltpu.make_async_remote_copy(
        src_ref=source,
        dst_ref=target,
        send_sem=send,
        recv_sem=recv,
        device_id=device,
        device_id_type=MESH,
    )


def move(source, target, send, recv, device, is_self):
    @pl.when(is_self)
    def _():
        pltpu.make_async_copy(source, target, recv).start()

    @pl.when(jnp.logical_not(is_self))
    def _():
        remote(source, target, send, recv, device).start()


def return_copies(ref, out, send, recv):
    row, spot, core = place()
    head = 2 * lax.rem(spot, 4) + core
    owner = spot // 4
    copies = []
    for step in range(8):
        chip = lax.rem(spot + step, 8)
        is_self = (owner == core) if step == 0 else False
        parts = (ref.at[chip], out.at[head], send.at[step], recv.at[head], (row, chip, owner))
        copies.append((parts, is_self))
    return copies


def start_return(copies):
    for parts, is_self in copies:
        if is_self is False:
            remote(*parts).start()
        else:
            move(*parts, is_self)


def finish_return(copies, out, send, recv):
    row, spot, core = place()
    for head in range(8):
        remote(
            out.at[head], out.at[head], send.at[0], recv.at[head], (row, spot, 1 - core)
        ).wait_recv()
    for parts, is_self in copies:
        if is_self is False:
            remote(*parts).wait_send()
        else:

            @pl.when(jnp.logical_not(is_self))
            def _():
                remote(*parts).wait_send()


def tile_at(index, size):
    return pl.ds(pl.multiple_of(index * size, size), size)


def causal(scores):
    keys = lax.broadcasted_iota(jnp.int32, scores.shape, 0)
    queries = lax.broadcasted_iota(jnp.int32, scores.shape, 1)
    return jnp.where(keys <= queries, scores, masked_value)


def neighbours():
    row, spot, core = place()
    level, column = spot // 2, lax.rem(spot, 2)
    beside_x = (1 - row, spot, core)
    beside_y = (row, 2 * level + 1 - column, core)
    along_z = [(row, 2 * lax.rem(level + k, 4) + column, core) for k in (1, 2, 3)]
    return row, level, column, beside_x, beside_y, along_z


class Gather:
    def __init__(self, whole, start, width, piece, sems):
        self.whole = whole
        self.start, self.width = start, width
        names = ("send_z", "recv_z", "send_x", "recv_x", "send_y", "recv_y", "send_d", "recv_d")
        for name, sem in zip(names, sems):
            setattr(self, name, sem.at[piece])

    def block(self, x, z, y, half=None):
        cut = self.width * 7 // 12 // WIDE * WIDE
        start, width = self.start, self.width
        if half == 0:
            width = cut
        elif half == 1:
            start, width = start + cut, width - cut
        return self.whole.at[x, z, y, :, pl.ds(start, width)]

    def arrived(self, target, recv_sem):
        device = neighbours()[3]
        remote(target, target, self.send_x.at[0], recv_sem, device).wait_recv()

    def copy_z(self, z, up):
        row, level, column, beside_x, beside_y = neighbours()[:5]
        core = place()[2]
        target = level + 1 if up else level - 1
        block = self.block(row, z, column)
        return remote(
            block,
            block,
            self.send_z.at[int(up), z],
            self.recv_z.at[z],
            (row, 2 * target + column, core),
        )

    def copies_xy(self, z):
        row, level, column, beside_x, beside_y = neighbours()[:5]
        block = self.block(row, z, column)
        return [
            remote(block, block, self.send_x.at[z], self.recv_x.at[z], beside_x),
            remote(block, block, self.send_y.at[z], self.recv_y.at[z], beside_y),
        ]

    def copies_diagonal(self, z):
        row, level, column, beside_x, beside_y = neighbours()[:5]
        by_y = self.block(1 - row, z, column, 1)
        by_x = self.block(row, z, 1 - column, 0)
        return [
            remote(by_y, by_y, self.send_d.at[0, z], self.recv_d.at[0, z], beside_y),
            remote(by_x, by_x, self.send_d.at[1, z], self.recv_d.at[1, z], beside_x),
        ]

    def each_at(self, hop, act):
        level = neighbours()[1]

        @pl.when(level >= hop)
        def _():
            act(level - hop, True)

        @pl.when(level + hop <= 3)
        def _():
            act(level + hop, False)

    def start_z(self, z, up):
        level = neighbours()[1]

        @pl.when(level < 3 if up else level > 0)
        def _():
            self.copy_z(z, up).start()

    def open(self):
        level = neighbours()[1]
        self.start_z(level, True)
        self.start_z(level, False)
        for copy in self.copies_xy(level):
            copy.start()

    def hop(self, hop):
        def act(z, up):
            row, level, column = neighbours()[:3]
            self.arrived(self.block(row, z, column), self.recv_z.at[z])
            self.start_z(z, up)
            for copy in self.copies_xy(z):
                copy.start()

        self.each_at(hop, act)

    def turn_diagonal(self, z):
        row, level, column = neighbours()[:3]
        by_y, by_x = self.copies_diagonal(z)
        self.arrived(self.block(1 - row, z, column), self.recv_x.at[z])
        by_y.start()
        self.arrived(self.block(row, z, 1 - column), self.recv_y.at[z])
        by_x.start()

    def diagonal(self, hop):
        if hop == 0:
            self.turn_diagonal(neighbours()[1])
        else:
            self.each_at(hop, lambda z, up: self.turn_diagonal(z))

    def finish(self):
        row, level, column = neighbours()[:3]
        for z in range(4):
            self.arrived(self.block(1 - row, z, 1 - column, 1), self.recv_d.at[0, z])
            self.arrived(self.block(1 - row, z, 1 - column, 0), self.recv_d.at[1, z])

    def close(self):
        level = neighbours()[1]

        def sent(z, up):
            @pl.when(level < 3 if up else level > 0)
            def _():
                self.copy_z(z, up).wait_send()

        sent(level, True)
        sent(level, False)
        for hop in range(1, 4):
            self.each_at(hop, sent)
        for z in range(4):
            for copy in self.copies_xy(z) + self.copies_diagonal(z):
                copy.wait_send()


def gather_sems(pieces):
    dma = pltpu.SemaphoreType.DMA
    shapes = [(2, 4), (4,), (4,), (4,), (4,), (4,), (2, 4), (2, 4)]
    return [dma((pieces,) + shape) for shape in shapes]


SECOND, THIRD, LAST = 2, 3, 4


class Reduce:
    def __init__(self, n, changes, refs):
        (
            self.left_t,
            self.right,
            self.gains,
            self.own,
            self.out,
            self.gain_out,
            self.save,
            self.send_one,
            self.recv_one,
            self.send_two,
            self.recv_two,
            self.kept,
            self.recv_three,
            self.ss_one,
            self.rs_one,
            self.ss_two,
            self.rs_two,
            self.ss_three,
            self.rs_three,
        ) = refs
        self.n, self.changes = n, changes
        self.share = self.own.shape[1]

    def columns(self, step, kind):
        held = self.right.shape[1] // (2 * PIECE)
        start = lax.rem(step, held) * 2 * PIECE + kind * PIECE
        return pl.ds(pl.multiple_of(start, PIECE), PIECE)

    def saving(self, step):
        slot = lax.rem(step, 2)
        pieces = self.changes[0] // 3
        place = jnp.where(step < self.changes[0], lax.rem(step, 3) * pieces + step // 3, step)
        cut = pl.ds(pl.multiple_of(place * 2 * PIECE, 2 * PIECE), 2 * PIECE)
        return pltpu.make_async_copy(self.own.at[slot], self.out.at[:, cut], self.save.at[slot])

    def product(self, step, kind, x, y):
        left = jnp.where(lax.rem(step, 3) == 2, 0, 1)
        left = jnp.where(step >= self.changes[0], 2, left)
        left = jnp.where(step >= self.changes[1], 0, left)
        term = jnp.dot(
            self.left_t[left, x, y],
            self.right[:, self.columns(step, kind)],
            preferred_element_type=jnp.float32,
        )
        if kind == 1:
            held = self.gains[x, y].astype(jnp.float32)
            held = jnp.concatenate([held, jnp.zeros_like(held)], axis=1)
            term = jnp.where(step == self.n - 1, held, term)
        return term

    def x_first(self, step, kind):
        return 1 if kind == 0 else jnp.where(lax.rem(step, 5) == 4, 1, 0)

    def beside(self, by_x):
        row, level, column = neighbours()[:3]
        core = place()[2]
        other_row = by_x * (1 - row) + (1 - by_x) * row
        other_column = by_x * column + (1 - by_x) * (1 - column)
        return (other_row, 2 * level + other_column, core)

    def first_copy(self, step, kind):
        out, into = lax.rem(step, 3), lax.rem(step, 5)
        return remote(
            self.send_one.at[out, kind],
            self.recv_one.at[into, kind],
            self.ss_one.at[out, kind],
            self.rs_one.at[into, kind],
            self.beside(self.x_first(step, kind)),
        )

    def second_copy(self, step, kind):
        out, into = lax.rem(step, 2), lax.rem(step, 5)
        return remote(
            self.send_two.at[out, kind],
            self.recv_two.at[into, kind],
            self.ss_two.at[out, kind],
            self.rs_two.at[into, kind],
            self.beside(1 - self.x_first(step, kind)),
        )

    def third_copy(self, step, kind, k):
        row, level, column, beside_x, beside_y, along_z = neighbours()
        target = lax.rem(level + k + 1, 4)
        out, into = lax.rem(step, 3), lax.rem(step, 4)
        return remote(
            self.kept.at[out, kind, pl.ds(pl.multiple_of(target * self.share, 16), self.share)],
            self.recv_three.at[into, kind, k],
            self.ss_three.at[out, kind, k],
            self.rs_three.at[into, kind, k],
            along_z[k],
        )

    def first(self, step):
        row, level, column = neighbours()[:3]
        slot = lax.rem(step, 3)
        for kind in range(2):
            by_x = self.x_first(step, kind)
            for half in range(2):
                x = by_x * (1 - row) + (1 - by_x) * half
                y = by_x * half + (1 - by_x) * (1 - column)
                self.send_one[slot, kind, half] = self.product(step, kind, x, y).astype(
                    jnp.bfloat16
                )
            self.first_copy(step, kind).start()

    def second(self, step):
        row, level, column = neighbours()[:3]
        slot, came, keep = lax.rem(step, 2), lax.rem(step, 5), lax.rem(step, 3)
        for kind in range(2):
            self.first_copy(step, kind).wait()
        for kind in range(2):
            by_x = self.x_first(step, kind)
            x = by_x * row + (1 - by_x) * (1 - row)
            y = by_x * (1 - column) + (1 - by_x) * column
            arrived = self.recv_one.at[came, kind]
            mine = by_x * column + (1 - by_x) * row
            away = self.product(step, kind, x, y) + arrived[1 - mine].astype(jnp.float32)
            self.send_two[slot, kind] = away.astype(jnp.bfloat16)
            here = self.product(step, kind, row, column) + arrived[mine].astype(jnp.float32)
            self.kept[keep, kind] = here.astype(jnp.bfloat16)
        for kind in range(2):
            self.second_copy(step, kind).start()

    def third(self, step):
        came, keep = lax.rem(step, 5), lax.rem(step, 3)
        for kind in range(2):
            self.second_copy(step, kind).wait()
            here = self.kept[keep, kind].astype(jnp.float32) + self.recv_two[came, kind].astype(
                jnp.float32
            )
            self.kept[keep, kind] = here.astype(jnp.bfloat16)
            for k in range(3):
                self.third_copy(step, kind, k).start()

    def last(self, step):
        level = neighbours()[1]
        came, keep = lax.rem(step, 4), lax.rem(step, 3)
        mine = pl.ds(pl.multiple_of(level * self.share, 16), self.share)

        @pl.when(step >= 2)
        def _():
            self.saving(step - 2).wait()

        for kind in range(2):
            total = self.kept[keep, kind, mine].astype(jnp.float32)
            for k in range(3):
                self.third_copy(step, kind, k).wait()
                total = total + self.recv_three[came, kind, k].astype(jnp.float32)
            self.own[lax.rem(step, 2), :, kind * PIECE : (kind + 1) * PIECE] = total
        self.saving(step).start()

        @pl.when(step == self.n - 1)
        def _():
            lines = self.own[lax.rem(step, 2), :, PIECE : PIECE + WIDE].T
            self.gain_out[0:2] = lines[0:2] + lines[2:4]

    def turn(self, step):
        for stage, lag in (
            (self.first, 0),
            (self.second, SECOND),
            (self.third, THIRD),
            (self.last, LAST),
        ):

            @pl.when(jnp.logical_and(step >= lag, step < self.n + lag))
            def _():
                stage(step - lag)


def layer_buffers(rows, width, share, out_width, hidden_width):
    dma = pltpu.SemaphoreType.DMA
    low, full = jnp.bfloat16, jnp.float32
    length = 8 * rows
    per_device = rows // RUN
    runs = length // RUN
    quarter = 4 * share
    heads = (8, per_device, HEAD, RUN)
    vmem, smem = pltpu.VMEM, pltpu.SMEM
    return dict(
        extra_own=vmem((share, WIDE), low),
        total=vmem((rows, width), full),
        feat=vmem((rows, width), low),
        cot=vmem((rows, width), low),
        part=vmem((rows, width), low),
        part_other=vmem((2, rows, width), low),
        tables=vmem((2, HALF, rows), full),
        gain_rows=vmem((8, width), full),
        gain_two_grad=vmem((1, width), full),
        weight=vmem((4, 2, 4, 2, share, 4 * HEAD), low),
        q_heads=vmem(heads, low),
        kv_heads=vmem((4, 2, per_device, HEAD, RUN), low),
        q_slots=vmem(heads, low),
        kv_slots=vmem((8, 2, per_device, HEAD, RUN), low),
        mixed_slots=vmem(heads, low),
        mixed_heads=vmem(heads, low),
        q_t=vmem((HEAD, length), low),
        q=vmem((length, HEAD), low),
        keys=vmem((length, HEAD), low),
        k_t=vmem((HEAD, length), low),
        v_t=vmem((HEAD, length), low),
        v=vmem((length, HEAD), low),
        d=vmem((length, HEAD), low),
        mixed_t=vmem((HEAD, length), full),
        lse=vmem((1, length), full),
        delta=vmem((1, length), full),
        dk=vmem((TILE, HEAD), full),
        dv=vmem((TILE, HEAD), full),
        dkv_slots=vmem((8, 2, per_device, HEAD, RUN), low),
        dkv_other=vmem((8, 2, HEAD, RUN), low),
        middle_ring=vmem((2, rows, WIDE), full),
        input_ring=vmem((2, rows // 16, 1, width), full),
        left_t=vmem((3, 2, 2, quarter, rows), low),
        right=vmem((rows, 3 * hidden_width), low),
        gains=vmem((2, 2, quarter, WIDE), low),
        own=vmem((2, share, 2 * PIECE), full),
        send_one=vmem((3, 2, 2, quarter, PIECE), low),
        recv_one=vmem((5, 2, 2, quarter, PIECE), low),
        send_two=vmem((2, 2, quarter, PIECE), low),
        recv_two=vmem((5, 2, quarter, PIECE), low),
        kept=vmem((3, 2, quarter, PIECE), low),
        recv_three=vmem((4, 2, 3, share, PIECE), low),
        ids_all=vmem((8, 8, WIDE), jnp.int32),
        ids=smem((8, 8, WIDE), jnp.int32),
        order=smem((2 * runs, 2), jnp.int32),
        load_own=dma((17,)),
        send_ids=dma((8,)),
        recv_ids=dma((8,)),
        load_ids=dma(()),
        load_w=dma((4,)),
        load_cot=dma(()),
        load_ring=dma((2,)),
        load_mixed=dma(()),
        save_rows=dma((2,)),
        save_layer=dma(()),
        save_mixed=dma(()),
        save_middle=dma(()),
        save=dma((2,)),
        send_q=dma((4, 2)),
        recv_q=dma((8,)),
        send_kv=dma((4, 2)),
        recv_kv=dma((8,)),
        send_x=dma((8,)),
        recv_x=dma((8,)),
        send_m=dma((8,)),
        recv_m=dma((8,)),
        send_p=dma((4,)),
        recv_p=dma((2, 4)),
        send_d=dma((4, 2)),
        recv_d=dma((8,)),
        send_dq=dma((8,)),
        recv_dq=dma((8,)),
        send_swap=dma(()),
        recv_swap=dma(()),
        send_dk=dma((8,)),
        recv_dk=dma((4, 2)),
        ss_one=dma((3, 2)),
        rs_one=dma((5, 2)),
        ss_two=dma((2, 2)),
        rs_two=dma((5, 2)),
        ss_three=dma((3, 2, 3)),
        rs_three=dma((4, 2, 3)),
    )


def layer_kernel(
    names,
    tokens,
    positions,
    freqs,
    ids_in,
    gain_one,
    gain_two,
    w_query,
    w_key,
    w_value,
    w_out_t,
    w_gate,
    w_up,
    w_down_t,
    cotangent,
    near,
    far,
    mixed_low,
    middle,
    input_grad,
    layer_out,
    grads,
    gain_out,
    *refs,
):
    m = types.SimpleNamespace(**dict(zip(names, refs)))
    gather_refs = refs[len(names) :]
    row, spot, core = place()
    level, column = spot // 2, lax.rem(spot, 2)
    low, full = jnp.bfloat16, jnp.float32
    rows, width = tokens.shape
    share = w_gate.shape[0]
    length = 8 * rows
    runs, tiles = length // RUN, length // TILE
    per_device = rows // RUN
    halves = TILE // RUN
    quarter = 4 * share
    sibling = (row, spot, 1 - core)
    out_width = w_out_t.shape[1]
    qkv_width = 16 * HEAD
    out_start = qkv_width + WIDE
    scale = HEAD ** (-0.5)

    first = Gather(near, 0, out_start, 0, gather_refs)
    outer = Gather(near, out_start, out_width, 1, gather_refs)
    feeds = [Gather(far, 3 * FEED * p, 3 * FEED, 2 + p, gather_refs) for p in range(4)]

    near_at = m.right.shape[1] // (2 * PIECE)
    n = grads.shape[1] // (2 * PIECE)
    sums = Reduce(
        n,
        (near_at, near_at + qkv_width // (2 * PIECE)),
        (m.left_t, m.right, m.gains, m.own, grads, gain_out, m.save)
        + (m.send_one, m.recv_one, m.send_two, m.recv_two, m.kept, m.recv_three)
        + (m.ss_one, m.rs_one, m.ss_two, m.rs_two, m.ss_three, m.rs_three),
    )

    def turn_left(index, source):
        for piece in range(4):
            turned = source[:, piece * quarter : (piece + 1) * quarter].T
            for inner in range(4):
                x, z, y = piece // 2, 2 * (piece % 2) + inner // 2, inner % 2
                m.left_t[index, x, y, z * share : (z + 1) * share] = turned[
                    inner * share : (inner + 1) * share
                ]


    own_copies, start = [], 0
    for ref in (w_query, w_key, w_value, m.extra_own, w_out_t):
        wide = ref.shape[1]
        own_copies.append((ref, near.at[row, level, column, :, pl.ds(start, wide)]))
        start += wide
    for piece in range(4):
        for index, ref in enumerate((w_gate, w_up, w_down_t)):
            target = far.at[row, level, column, :, pl.ds((3 * piece + index) * FEED, FEED)]
            own_copies.append((ref.at[:, pl.ds(piece * FEED, FEED)], target))
    own_copies = [
        pltpu.make_async_copy(source, target, m.load_own.at[index])
        for index, (source, target) in enumerate(own_copies)
    ]
    load_cotangent = pltpu.make_async_copy(cotangent, m.cot, m.load_cot)

    def ids_copy(shift, back):
        return remote(
            ids_in,
            m.ids_all.at[lax.rem(spot + 8 - shift, 8) if back else spot],
            m.send_ids.at[shift],
            m.recv_ids.at[shift],
            (row, lax.rem(spot + shift, 8), core),
        )

    def load_weight(ref, start, slot, wide=4 * HEAD):
        return pltpu.make_async_copy(
            ref.at[:, :, :, :, pl.ds(start, wide)],
            m.weight.at[slot, :, :, :, :, pl.ds(0, wide)],
            m.load_w.at[slot],
        )

    def load_group(group):
        return load_weight(near, group * 4 * HEAD, group)

    def load_out(index):
        return load_weight(near, out_start + index * 4 * HEAD, index)

    def to_heads_copies(source, target, send, recv):
        copies = []
        for step in range(4):
            slot = lax.rem(spot + step, 4)
            chip = 4 * core + slot
            for other in range(2):
                parts = (
                    source.at[2 * slot + other],
                    target.at[spot],
                    send.at[step, other],
                    recv.at[spot],
                    (row, chip, other),
                )
                copies.append((parts, jnp.logical_and(chip == spot, core == other)))
        return copies

    q_copies = to_heads_copies(m.q_heads, m.q_slots, m.send_q, m.recv_q)
    kv_copies = []
    for step in range(4):
        slot = lax.rem(spot + step, 4)
        chip = 4 * core + slot
        for other in range(2):
            parts = (
                m.kv_heads.at[slot, :, other],
                m.kv_slots.at[spot, :, other],
                m.send_kv.at[step, other],
                m.recv_kv.at[spot],
                (row, chip, other),
            )
            kv_copies.append((parts, jnp.logical_and(chip == spot, core == other)))

    def hand_on(source):
        block = m.kv_slots.at[source, :, core]
        return remote(block, block, m.send_x.at[source], m.recv_x.at[source], sibling)

    mixed_copies = return_copies(m.mixed_slots, m.mixed_heads, m.send_m, m.recv_m)
    d_own, d_slots, dq_slots, dq_own, dkv_own = (
        m.q_heads,
        m.q_slots,
        m.mixed_slots,
        m.mixed_heads,
        m.kv_heads,
    )
    mixed = dq_sorted = m.q_slots
    dkv_sorted, d_t, dq_t = m.kv_slots, m.v_t, m.mixed_t
    d_copies = to_heads_copies(d_own, d_slots, m.send_d, m.recv_d)
    dq_copies = return_copies(dq_slots, dq_own, m.send_dq, m.recv_dq)
    swap = remote(
        m.dkv_slots.at[:, :, 1 - core], m.dkv_other, m.send_swap, m.recv_swap, sibling
    )
    slot, owner = lax.rem(spot, 4), spot // 4
    dkv_copies = []
    for step in range(8):
        chip = lax.rem(spot + step, 8)
        parts = (
            m.dkv_slots.at[chip, :, core],
            dkv_own.at[slot, :, core],
            m.send_dk.at[step],
            m.recv_dk.at[slot, core],
            (row, chip, owner),
        )
        dkv_copies.append((parts, (owner == core) if step == 0 else False))

    def wait_sent(copies):
        for parts, is_self in copies:
            if is_self is False:
                remote(*parts).wait_send()
            else:

                @pl.when(jnp.logical_not(is_self))
                def _():
                    remote(*parts).wait_send()

    def wait_arrived(target, recv):
        remote(target, target, m.send_swap, recv, sibling).wait_recv()

    def pair_copy(index, landing):
        cut = pl.ds(pl.multiple_of(index * quarter, quarter), quarter)
        return remote(
            m.part.at[:, cut],
            m.part_other.at[landing, :, cut],
            m.send_p.at[index],
            m.recv_p.at[landing, index],
            sibling,
        )

    def pair_block(cut, landing):
        return m.part[cut].astype(full) + m.part_other[landing, cut].astype(full)

    save_mixed = pltpu.make_async_copy(
        m.right.at[:, pl.ds(0, out_width)], mixed_low, m.save_mixed
    )
    save_middle = pltpu.make_async_copy(m.total, middle, m.save_middle)


    def begin():
        for copy in own_copies:
            copy.start()
        load_cotangent.start()
        greet(sequence_others() + [neighbours()[3]])
        for copy in own_copies[:4]:
            copy.wait()
        first.open()
        for shift in range(1, 8):
            ids_copy(shift, False).start()
        m.ids_all[spot] = ids_in[...]
        for copy in own_copies[4:]:
            copy.wait()
        chunk = rows // 8

        def unit_block(index, carry):
            cut = tile_at(index, chunk)
            values = tokens[cut].astype(full)
            inverse = lax.rsqrt(jnp.mean(values * values, axis=-1, keepdims=True) + epsilon)
            m.total[cut] = values * inverse
            return carry

        lax.fori_loop(0, 8, unit_block, 0)
        angles = freqs[...] * positions[...].astype(full)
        m.tables[0] = jnp.cos(angles)
        m.tables[1] = jnp.sin(angles)

    def take_first():
        first.hop(1)
        first.diagonal(0)
        first.hop(2)
        first.diagonal(1)
        first.hop(3)
        outer.open()
        first.diagonal(2)
        first.diagonal(3)
        outer.hop(1)
        feeds[0].open()
        for shift in range(1, 8):
            ids_copy(shift, True).wait_recv()
        pltpu.make_async_copy(m.ids_all, m.ids, m.load_ids).start()
        first.finish()

    def project():
        load_gains = load_weight(near, qkv_width, 3, WIDE)
        load_gains.start()
        for group in range(3):
            load_group(group).start()
        load_gains.wait()
        gains = m.weight[3, :, :, :, :, :WIDE].reshape(width, WIDE).T
        m.gain_rows[...] = gains[0:8].astype(full)
        load_group(3).start()
        chunk = rows // 8

        def gain_block(index, carry):
            cut = tile_at(index, chunk)
            m.feat[cut] = (m.total[cut] * m.gain_rows[0:1]).astype(low)
            return carry

        lax.fori_loop(0, 8, gain_block, 0)
        for group in range(4):
            load_group(group).wait()
            proj = dot_f32(m.feat[...], m.weight[group].reshape(width, 4 * HEAD)).T
            for head in range(4):
                front = proj[head * HEAD : head * HEAD + HALF]
                back = proj[head * HEAD + HALF : (head + 1) * HEAD]
                if group < 3:
                    front, back = (
                        front * m.tables[0] - back * m.tables[1],
                        back * m.tables[0] + front * m.tables[1],
                    )
                for start, value in ((0, front.astype(low)), (HALF, back.astype(low))):
                    for run in range(per_device):
                        piece = value[:, run * RUN : (run + 1) * RUN]
                        if group < 2:
                            m.q_heads[4 * group + head, run, start : start + HALF] = piece
                        else:
                            m.kv_heads[head, group - 2, run, start : start + HALF] = piece
            if group == 0:
                outer.hop(2)
                outer.diagonal(0)
            elif group == 1:
                outer.hop(3)
                outer.diagonal(1)
            elif group == 2:
                feeds[0].hop(1)
                outer.diagonal(2)

    def to_heads():
        for kv_copy, q_copy in zip(kv_copies, q_copies):
            move(*kv_copy[0], kv_copy[1])
            move(*q_copy[0], q_copy[1])
        outer.diagonal(3)
        feeds[0].hop(2)
        feeds[0].diagonal(0)
        feeds[0].hop(3)
        outer.finish()
        for index in range(2):
            load_out(index).start()
        feeds[1].open()
        turn_left(2, m.feat)
        feeds[0].diagonal(1)
        feeds[0].diagonal(2)
        for step in range(8):
            source = lax.rem(spot + step, 8)
            wait_arrived(m.kv_slots.at[source, :, core], m.recv_kv.at[source])
            hand_on(source).start()
        for step in range(8):
            wait_arrived(m.q_slots.at[step], m.recv_q.at[step])
            hand_on(step).wait()
        feeds[0].diagonal(3)
        feeds[1].hop(1)


    def sort():
        pltpu.make_async_copy(m.ids_all, m.ids, m.load_ids).wait()

        def find_run(index, carry):
            device, piece = 0, 0
            for run in range(runs):
                here = m.ids[run // per_device, 0, run % per_device] == index
                device = jnp.where(here, run // per_device, device)
                piece = jnp.where(here, run % per_device, piece)
            m.order[index, 0] = device
            m.order[index, 1] = piece
            found = m.ids[index // per_device, 0, index % per_device]
            m.order[runs + index, 0] = lax.div(found, per_device)
            m.order[runs + index, 1] = lax.rem(found, per_device)
            return carry

        lax.fori_loop(0, runs, find_run, 0)

        def sort_run(index, carry):
            device, piece = m.order[index, 0], m.order[index, 1]
            cols = tile_at(index, RUN)
            m.q_t[:, cols] = m.q_slots[device, piece]
            m.keys[cols] = m.kv_slots[device, 0, piece].T
            m.v_t[:, cols] = m.kv_slots[device, 1, piece]
            return carry

        lax.fori_loop(0, runs, sort_run, 0)

    def unsort(copy_run):
        def one(run, carry):
            at, at_piece = m.order[runs + run, 0], m.order[runs + run, 1]
            copy_run(run // per_device, run % per_device, at, at_piece)
            return carry

        lax.fori_loop(0, runs, one, 0)

    def query_tile(index, carry):
        cols = tile_at(index, TILE)
        queries = m.q_t[:, cols]

        def step(scores, block, peak, total, mix):
            high = jnp.maximum(peak, jnp.max(scores, axis=0, keepdims=True))
            decay = jnp.exp2(peak - high)
            weights = jnp.exp2(scores - high)
            total = total * decay + jnp.sum(weights, axis=0, keepdims=True)
            mix = mix * decay + dot_f32(m.v_t[:, tile_at(block, TILE)], weights.astype(low))
            return high, total, mix

        def scores_of(block):
            return dot_f32(m.keys[tile_at(block, TILE)], queries) * (scale * LOG2_E)

        state = (
            jnp.full((1, TILE), masked_value, full),
            jnp.zeros((1, TILE), full),
            jnp.zeros((HEAD, TILE), full),
        )
        state = step(causal(scores_of(index)), index, *state)
        peak, total, mix = lax.fori_loop(
            0, index, lambda block, now: step(scores_of(block), block, *now), state
        )
        mix = mix / total
        m.mixed_t[:, cols] = mix
        m.lse[:, cols] = peak + jnp.log2(total)
        for half in range(halves):
            mixed[index, half] = mix[:, half * RUN : (half + 1) * RUN].astype(low)

        hooks = {
            1: [(feeds[1].hop, 2)],
            2: [(feeds[1].hop, 3), (feeds[1].diagonal, 0)],
            4: [(feeds[1].diagonal, 1)],
            5: [(feeds[1].diagonal, 2)],
            6: [(feeds[1].diagonal, 3)],
        }
        for when, acts in hooks.items():

            @pl.when(index == when)
            def _():
                for act, hop in acts:
                    act(hop)
                if when == 2:
                    feeds[2].open()

        return carry

    def return_mixed():
        def copy_run(device, piece, at, at_piece):
            m.mixed_slots[device, piece] = mixed[at, at_piece]

        unsort(copy_run)
        start_return(mixed_copies)
        feeds[2].hop(1)
        feeds[2].diagonal(0)
        feeds[2].hop(2)
        for index in range(tiles):
            cut = pl.ds(index * TILE, TILE)
            m.q[cut] = m.q_t[:, cut].T
            m.k_t[:, cut] = m.keys[cut].T
            m.v[cut] = m.v_t[:, cut].T
        feeds[2].hop(3)
        feeds[3].open()
        feeds[2].diagonal(1)
        finish_return(mixed_copies, m.mixed_heads, m.send_m, m.recv_m)

    def project_out():
        for index in range(2):
            load_out(index).wait()
        for run in range(per_device):
            side = m.mixed_heads[:, run].reshape(8 * HEAD, RUN)
            m.right[run * RUN : (run + 1) * RUN, :out_width] = side.T
        save_mixed.start()
        for index in range(4):
            term = jnp.zeros((rows, quarter), full)
            for part in range(2):
                lanes = slice(part * 4 * HEAD, (part + 1) * 4 * HEAD)
                held = m.weight[part, index // 2, 2 * (index % 2) : 2 * (index % 2) + 2]
                term = term + contract_cols(m.right[:, lanes], held.reshape(quarter, 4 * HEAD))
            m.part[:, index * quarter : (index + 1) * quarter] = term.astype(low)
            pair_copy(index, 0).start()
        feeds[2].diagonal(2)
        feeds[3].hop(1)
        for index in range(4):
            pair_copy(index, 0).wait()
        chunk = rows // 8

        def norm_block(index, carry):
            cut = tile_at(index, chunk)
            values = tokens[cut].astype(full) + pair_block(cut, 0)
            m.total[cut] = values
            inverse = lax.rsqrt(jnp.mean(values * values, axis=-1, keepdims=True) + epsilon)
            m.feat[cut] = (values * inverse * m.gain_rows[1:2]).astype(low)
            return carry

        lax.fori_loop(0, 8, norm_block, 0)
        save_middle.start()
        load_cotangent.wait()
        save_mixed.wait()


    def load_feed(piece, block):
        index = 6 * piece + block
        start = (3 * piece + block % 3) * FEED + (block // 3) * PIECE
        lanes = pl.ds(pl.multiple_of(start, PIECE), PIECE)
        at = lax.rem(index, 4)
        return pltpu.make_async_copy(
            far.at[:, :, :, :, lanes],
            m.weight.at[at, :, :, :, :, pl.ds(0, PIECE)],
            m.load_w.at[at],
        )

    def feed_piece(piece):
        for block in range(4):
            load_feed(piece, block).start()
        for half in range(2):
            values = []
            for kind, left in enumerate((m.feat, m.feat, m.cot)):
                block = 3 * half + kind
                load_feed(piece, block).wait()
                held = m.weight[lax.rem(6 * piece + block, 4), :, :, :, :, :PIECE]
                values.append(dot_f32(left[...], held.reshape(width, PIECE)))
                if block + 4 < 6:
                    load_feed(piece, block + 4).start()
            gate, up, grad_hidden = values
            sigmoid = jax.nn.sigmoid(gate)
            silu = gate * sigmoid
            grad_gate = grad_hidden * up * sigmoid * (1.0 + gate * (1.0 - sigmoid))
            for kind, value in enumerate((grad_gate, grad_hidden * silu, silu * up)):
                start = (3 * piece + kind) * FEED + half * PIECE
                m.right[:, pl.ds(pl.multiple_of(start, PIECE), PIECE)] = value.astype(low)


    def held_block(piece, part_of):
        levels = pl.ds(2 * (part_of % 2), 2)
        return m.weight.at[piece, part_of // 2, levels, :, :, pl.ds(0, PIECE)]

    def load_block(index, piece, part_of, start):
        lanes = pl.ds(3 * FEED * piece + start + part_of * PIECE, PIECE)
        levels = pl.ds(2 * lax.rem(index, 2), 2)
        return pltpu.make_async_copy(
            far.at[index // 2, levels, :, :, lanes], held_block(piece, part_of), m.load_w.at[piece]
        )

    def load_blocks(index, piece, start, parts):
        for part_of in range(parts):
            load_block(index, piece, part_of, start).start()

    def row_products(start, parts, landing):
        for piece in range(4):
            load_blocks(0, piece, start, parts)

        def block(index, carry):
            term = jnp.zeros((rows, quarter), full)
            for piece in range(4):
                for part_of in range(parts):
                    load_block(index, piece, part_of, start).wait()
                for part_of in range(parts):
                    at = 3 * FEED * piece + start + part_of * PIECE
                    term = term + contract_cols(
                        m.right[:, at : at + PIECE],
                        held_block(piece, part_of)[...].reshape(quarter, PIECE),
                    )

                @pl.when(index + 1 < 4)
                def _():
                    load_blocks(index + 1, piece, start, parts)

            m.part[:, tile_at(index, quarter)] = term.astype(low)
            pair_copy(index, landing).start()
            return carry

        lax.fori_loop(0, 4, block, 0)

    def second_back():
        row_products(0, 4, 1)
        for index in range(2):
            load_out(index).start()

    def norm_back_block(cut, grad, values, gain):
        inverse = lax.rsqrt(jnp.mean(values * values, axis=-1, keepdims=True) + epsilon)
        unit = values * inverse
        scaled = grad * gain
        mean = jnp.mean(scaled * unit, axis=-1, keepdims=True)
        return inverse * (scaled - unit * mean), jnp.sum(grad * unit, axis=0, keepdims=True)

    def middle_back():
        for index in range(4):
            pair_copy(index, 1).wait()
        save_middle.wait()
        chunk = rows // 8

        def block(index, gain_grad):
            cut = tile_at(index, chunk)
            result, more = norm_back_block(
                cut, pair_block(cut, 1), m.total[cut], m.gain_rows[1:2]
            )
            result = result + m.cot[cut].astype(full)
            m.total[cut] = result
            m.feat[cut] = result.astype(low)
            return gain_grad + more

        m.gain_two_grad[...] = lax.fori_loop(0, 8, block, jnp.zeros((1, width), full))
        wait_sent(q_copies)
        wait_sent(kv_copies)
        for index in range(2):
            load_out(index).wait()
            grad = dot_f32(m.feat[...], m.weight[index].reshape(width, 4 * HEAD)).T.astype(low)
            for head in range(4):
                for run in range(per_device):
                    d_own[4 * index + head, run] = grad[
                        head * HEAD : (head + 1) * HEAD, run * RUN : (run + 1) * RUN
                    ]
        for parts, is_self in d_copies:
            move(*parts, is_self)


    def take_cotangents():
        for index in range(8):
            wait_arrived(d_slots.at[index], m.recv_d.at[index])

        def sort_run(index, carry):
            cols = tile_at(index, RUN)
            run = d_slots[m.order[index, 0], m.order[index, 1]]
            d_t[:, cols] = run
            m.d[cols] = run.T
            m.delta[:, cols] = jnp.sum(
                run.astype(full) * m.mixed_t[:, cols], axis=0, keepdims=True
            )
            return carry

        lax.fori_loop(0, runs, sort_run, 0)
        dq_t[...] = jnp.zeros_like(dq_t)

    def key_tile(block):
        cut = tile_at(block, TILE)
        keys, keys_t, values = m.keys[cut], m.k_t[:, cut], m.v[cut]
        m.dk[...] = jnp.zeros_like(m.dk)
        m.dv[...] = jnp.zeros_like(m.dv)

        def query_tile(index, diagonal):
            cols = tile_at(index, TILE)
            scores = dot_f32(keys, m.q_t[:, cols]) * (scale * LOG2_E)
            if diagonal:
                scores = causal(scores)
            probs = jnp.exp2(scores - m.lse[:, cols])
            m.dv[...] += dot_f32(probs.astype(low), m.d[cols])
            grad_probs = dot_f32(values, d_t[:, cols])
            grad_scores = (probs * (grad_probs - m.delta[:, cols])).astype(low)
            m.dk[...] += dot_f32(grad_scores, m.q[cols])
            dq_t[:, cols] += dot_f32(keys_t, grad_scores)

        query_tile(block, True)

        def later(index, inner):
            query_tile(index, False)
            return inner

        lax.fori_loop(block + 1, tiles, later, 0)
        turned = (m.dk[...] * scale).T.astype(low), m.dv[...].T.astype(low)
        for kind, value in enumerate(turned):
            for half in range(halves):
                dkv_sorted[block, kind, half] = value[:, half * RUN : (half + 1) * RUN]

    def key_tiles(start, stop):
        def one(block, carry):
            key_tile(block)
            return carry

        lax.fori_loop(start, stop, one, 0)

    def send_back():
        def copy_keys(device, piece, at, at_piece):
            for kind in range(2):
                m.dkv_slots[device, kind, piece] = dkv_sorted[at, kind, at_piece]

        unsort(copy_keys)
        swap.start()

        def turn_run(index, carry):
            value = dq_t[:, tile_at(index, RUN)] * scale
            dq_sorted[index // per_device, index % per_device] = value.astype(low)
            return carry

        lax.fori_loop(0, runs, turn_run, 0)

        def copy_queries(device, piece, at, at_piece):
            dq_slots[device, piece] = dq_sorted[at, at_piece]

        unsort(copy_queries)
        start_return(dq_copies)

    def add_pairs():
        swap.wait()
        for chip in range(8):
            both = m.dkv_slots[chip, :, core].astype(full) + m.dkv_other[chip].astype(full)
            m.dkv_slots[chip, :, core] = both.astype(low)
        start_return(dkv_copies)


    def feed_forward():
        row_products(2 * FEED, 2, 0)
        for group in range(4):
            load_group(group).start()

    save_layer = pltpu.make_async_copy(m.part, layer_out, m.save_layer)

    def finish_layer():
        for index in range(4):
            pair_copy(index, 0).wait()
        pieces = width // WIDE

        def load_piece(index):
            return pltpu.make_async_copy(
                middle.at[:, pl.ds(index * WIDE, WIDE)],
                m.middle_ring.at[index % 2],
                m.load_ring.at[index % 2],
            )

        load_piece(0).start()
        for index in range(pieces):
            if index + 1 < pieces:
                load_piece(index + 1).start()
            load_piece(index).wait()
            cut = pl.ds(index * WIDE, WIDE)
            value = m.part[:, cut].astype(full) + m.part_other[0, :, cut].astype(full)
            m.part[:, cut] = (value + m.middle_ring[index % 2]).astype(low)
        save_layer.start()


    load_mixed = pltpu.make_async_copy(
        mixed_low, m.right.at[:, pl.ds(qkv_width, out_width)], m.load_mixed
    )

    def project_back():
        load_mixed.start()
        for head in range(8):
            wait_arrived(dq_own.at[head], m.recv_dq.at[head])
        for slot_in in range(4):
            for core_in in range(2):
                wait_arrived(dkv_own.at[slot_in, :, core_in], m.recv_dk.at[slot_in, core_in])
        for group in range(4):
            for run in range(per_device):
                cols = slice(run * RUN, (run + 1) * RUN)
                turned = []
                for head in range(4):
                    if group < 2:
                        value = dq_own[4 * group + head, run]
                    else:
                        value = dkv_own[head, group - 2, run]
                    if group < 3:
                        front, back = value[:HALF].astype(full), value[HALF:].astype(full)
                        cos_part, sin_part = m.tables[0, :, cols], m.tables[1, :, cols]
                        turned.append((front * cos_part + back * sin_part).astype(low))
                        turned.append((back * cos_part - front * sin_part).astype(low))
                    else:
                        turned.append(value)
                m.right[cols, group * 4 * HEAD : (group + 1) * 4 * HEAD] = jnp.concatenate(
                    turned, axis=0
                ).T
        start = qkv_width + out_width
        m.right[:, start : start + PIECE] = jnp.zeros((rows, PIECE), low)
        load_mixed.wait()

    def project_normed():
        save_layer.wait()
        for group in range(4):
            load_group(group).wait()

        def block(index, carry):
            term = jnp.zeros((rows, quarter), full)
            for group in range(4):
                held = m.weight[group, index // 2, pl.ds(2 * lax.rem(index, 2), 2)]
                term = term + contract_cols(
                    m.right[:, group * 4 * HEAD : (group + 1) * 4 * HEAD],
                    held.reshape(quarter, 4 * HEAD),
                )
            m.part[:, tile_at(index, quarter)] = term.astype(low)
            pair_copy(index, 1).start()
            return carry

        lax.fori_loop(0, 4, block, 0)

    input_steps = rows // m.input_ring.shape[1]

    def save_input(index):
        at = lax.rem(index, 2)
        return pltpu.make_async_copy(
            m.input_ring.at[at],
            input_grad.at[tile_at(index, rows // input_steps)],
            m.save_rows.at[at],
        )

    def norm_back():
        for index in range(4):
            pair_copy(index, 1).wait()
        chunk = rows // input_steps

        def block(index, gain_grad):
            cut = tile_at(index, chunk)
            result, more = norm_back_block(
                cut, pair_block(cut, 1), tokens[cut].astype(full), m.gain_rows[0:1]
            )

            @pl.when(index >= 2)
            def _():
                save_input(index - 2).wait()

            m.input_ring[lax.rem(index, 2)] = (m.total[cut] + result).reshape(chunk, 1, width)
            save_input(index).start()
            return gain_grad + more

        gain_one_grad = lax.fori_loop(0, input_steps, block, jnp.zeros((1, width), full))
        lines = []
        for value in (gain_one_grad, m.gain_two_grad[...]):
            high = value.astype(low).astype(full)
            lines.append((high, value - high))
        which = lax.broadcasted_iota(jnp.int32, (WIDE, quarter), 0)
        for part in range(4):
            cut = slice(part * quarter, (part + 1) * quarter)
            table = jnp.zeros((WIDE, quarter), full)
            for index, line in enumerate((lines[0][0], lines[1][0], lines[0][1], lines[1][1])):
                table = jnp.where(which == index, line[:, cut], table)
            columns = table.T.astype(low)
            for inner in range(4):
                x, z, y = part // 2, 2 * (part % 2) + inner // 2, inner % 2
                m.gains[x, y, z * share : (z + 1) * share] = columns[
                    inner * share : (inner + 1) * share
                ]


    line = lax.broadcasted_iota(jnp.int32, (WIDE, share), 0)
    gain_lines = jnp.where(line == 0, gain_one[...].astype(full), 0.0)
    gain_lines = jnp.where(line == 1, gain_two[...].astype(full), gain_lines)
    m.extra_own[...] = gain_lines.T.astype(low)
    begin()
    take_first()
    project()
    to_heads()
    sort()
    lax.fori_loop(0, tiles, query_tile, 0)
    return_mixed()
    project_out()
    turn_left(1, m.feat)
    turn_left(0, m.cot)

    before = {
        1: [(feeds[2].diagonal, 3), (feeds[3].hop, 2), (feeds[3].diagonal, 0)],
        2: [(feeds[3].hop, 3), (feeds[3].diagonal, 1)],
        3: [(feeds[3].diagonal, 2), (feeds[3].diagonal, 3)],
        12: [(lambda _: project_back(), 0)],
    }
    after = {
        3: [second_back, middle_back],
        5: [take_cotangents, lambda: key_tiles(0, 2)],
        6: [lambda: key_tiles(2, 4)],
        7: [lambda: key_tiles(4, 8), send_back],
        8: [add_pairs, feed_forward],
        9: [finish_layer],
        12: [project_normed],
        14: [norm_back, lambda: turn_left(0, m.feat)],
    }

    def run(step, carry):
        for when, acts in before.items():

            @pl.when(step == when)
            def _():
                for act, hop in acts:
                    act(hop)

        for piece in range(4):

            @pl.when(step == piece)
            def _():
                feeds[piece].finish()

        @pl.when(step < 4)
        def _():
            feed_piece(step)

        sums.turn(step)
        for when, tasks in after.items():

            @pl.when(step == when)
            def _():
                for task in tasks:
                    task()

        return carry

    lax.fori_loop(0, n + LAST, run, 0)
    for gather in [first, outer] + feeds:
        gather.close()
    for shift in range(1, 8):
        ids_copy(shift, False).wait_send()
    for index in (input_steps - 2, input_steps - 1):
        save_input(index).wait()
    for step in (n - 2, n - 1):
        sums.saving(step).wait()
    for copies in (d_copies, dq_copies, dkv_copies):
        wait_sent(copies)


def layer(tokens, positions, ids, gain_one, gain_two, *weights_and_cotangent):
    low, full = jnp.bfloat16, jnp.float32
    rows, width = tokens.shape
    out_width = weights_and_cotangent[3].shape[1]
    share, hidden_width = weights_and_cotangent[4].shape
    near_width = 16 * HEAD + WIDE + out_width
    wide = 3 * hidden_width + 16 * HEAD + out_width + PIECE
    buffers = layer_buffers(rows, width, share, out_width, hidden_width)
    shape = jax.ShapeDtypeStruct
    return pl.pallas_call(
        functools.partial(layer_kernel, tuple(buffers)),
        in_specs=[vmem_spec()] * 6 + [any_spec()] * 8,
        out_specs=[any_spec()] * 7 + [vmem_spec()],
        out_shape=[
            shape((2, 4, 2, share, near_width), low),
            shape((2, 4, 2, share, 3 * hidden_width), low),
            shape((rows, out_width), low),
            shape((rows, width), full),
            shape((rows, 1, width), full),
            shape((rows, width), low),
            shape((share, wide), full),
            shape((8, share), full),
        ],
        scratch_shapes=list(buffers.values()) + gather_sems(6),
        compiler_params=pltpu.CompilerParams(
            collective_id=1, has_side_effects=True, vmem_limit_bytes=63 * 1024 * 1024
        ),
        name="layer",
    )(
        tokens,
        positions,
        (theta_base ** (-2.0 * jnp.arange(HALF, dtype=jnp.float32) / HEAD)).reshape(HALF, 1),
        ids,
        gain_one,
        gain_two,
        *weights_and_cotangent,
    )


def by_heads(
    tokens,
    positions,
    gain_one,
    gain_two,
    w_query,
    w_key,
    w_value,
    w_out,
    w_gate,
    w_up,
    w_down,
    cotangent,
):
    rows, _, width = tokens.shape
    share = gain_one.shape[0]
    run_ids = positions[::RUN, 0] // RUN
    input_grad, layer_out, grads, gains = layer(
        tokens.reshape(rows, width),
        positions.reshape(1, rows),
        jnp.broadcast_to(jnp.pad(run_ids, (0, WIDE - rows // RUN)), (8, WIDE)),
        gain_one.reshape(1, share),
        gain_two.reshape(1, share),
        w_query,
        w_key,
        w_value,
        w_out.T,
        w_gate,
        w_up,
        w_down.T,
        cotangent.reshape(rows, width),
    )[4:]
    splits, start = [], 0
    for wide in (
        w_gate.shape[1],
        w_up.shape[1],
        w_down.shape[0],
        w_query.shape[1],
        w_key.shape[1],
        w_value.shape[1],
        w_out.shape[0],
    ):
        splits.append(grads[:, start : start + wide])
        start += wide
    grad_gate, grad_up, grad_down, grad_query, grad_key, grad_value, grad_out = splits
    return (
        layer_out.reshape(rows, 1, width),
        input_grad,
        gains[0],
        gains[1],
        grad_query,
        grad_key,
        grad_value,
        grad_out.T,
        grad_gate,
        grad_up,
        grad_down.T,
    )


def solution(mesh):
    sizes = (mesh.shape["dp"], mesh.shape["context"], mesh.shape["tensor"])
    return jax.shard_map(
        by_heads if sizes == (2, 8, 2) else on_device,
        mesh=mesh,
        in_specs=(
            P("context", "dp", None),
            P("context", "dp"),
            P(("dp", "context")),
            P(("dp", "context")),
            P(("dp", "context"), "tensor"),
            P(("dp", "context"), "tensor"),
            P(("dp", "context"), "tensor"),
            P("tensor", ("dp", "context")),
            P(("dp", "context"), "tensor"),
            P(("dp", "context"), "tensor"),
            P("tensor", ("dp", "context")),
            P("context", "dp", None),
        ),
        out_specs=(
            P("context", "dp", None),
            P("context", "dp", None),
            P(("dp", "context")),
            P(("dp", "context")),
            P(("dp", "context"), "tensor"),
            P(("dp", "context"), "tensor"),
            P(("dp", "context"), "tensor"),
            P("tensor", ("dp", "context")),
            P(("dp", "context"), "tensor"),
            P(("dp", "context"), "tensor"),
            P("tensor", ("dp", "context")),
        ),
        check_vma=False,
    )
```

```python
import functools
import types

import jax
import jax.numpy as jnp
from jax import lax
from jax.experimental import pallas as pl
from jax.experimental.pallas import tpu as pltpu
from jax.sharding import PartitionSpec as P

HEAD = 96


epsilon = 1e-05
theta_base = 100000.0
masked_value = -1e30


def norm_forward(values_in, gain_vec):
    inverse = lax.rsqrt(jnp.mean(values_in * values_in, axis=-1, keepdims=True) + epsilon)
    unit_vals = values_in * inverse
    return (unit_vals, inverse, (unit_vals * gain_vec.astype(jnp.float32)).astype(jnp.bfloat16))


def norm_backward(grad_in, unit_vals, inverse, gain_vec):
    scaled = grad_in * gain_vec.astype(jnp.float32)
    grad_vals = inverse * (
        scaled - unit_vals * jnp.mean(scaled * unit_vals, axis=-1, keepdims=True)
    )
    return (grad_vals, jnp.sum(grad_in * unit_vals, axis=0))


def rotate(values_in, cos_part, sin_part):
    half_size = values_in.shape[-1] // 2
    front_half = values_in[..., :half_size]
    back_half = values_in[..., half_size:]
    return jnp.concatenate(
        [
            front_half * cos_part - back_half * sin_part,
            back_half * cos_part + front_half * sin_part,
        ],
        axis=-1,
    )


def contract_rows(left_mat, right_mat):
    return lax.dot_general(
        left_mat, right_mat, (((0,), (0,)), ((), ())), preferred_element_type=jnp.float32
    )


def contract_cols(left_mat, right_mat):
    return lax.dot_general(
        left_mat, right_mat, (((1,), (1,)), ((), ())), preferred_element_type=jnp.float32
    )


def on_device(
    tokens,
    positions,
    gain_one,
    gain_two,
    w_query,
    w_key,
    w_value,
    w_out,
    w_gate,
    w_up,
    w_down,
    cotangent,
):
    slot_count, seq_count, model_width = tokens.shape
    row_count = slot_count * seq_count
    gathered = (
        lax.all_gather(gain_one, ("dp", "context"), axis=0, tiled=True),
        lax.all_gather(gain_two, ("dp", "context"), axis=0, tiled=True),
        lax.all_gather(w_query, ("dp", "context"), axis=0, tiled=True),
        lax.all_gather(w_key, ("dp", "context"), axis=0, tiled=True),
        lax.all_gather(w_value, ("dp", "context"), axis=0, tiled=True),
        lax.all_gather(w_out, ("dp", "context"), axis=1, tiled=True),
        lax.all_gather(w_gate, ("dp", "context"), axis=0, tiled=True),
        lax.all_gather(w_up, ("dp", "context"), axis=0, tiled=True),
        lax.all_gather(w_down, ("dp", "context"), axis=1, tiled=True),
    )
    full_one, full_two, query_mat, key_mat, value_mat, out_mat, gate_mat, up_mat, down_mat = (
        gathered
    )
    heads_kv = key_mat.shape[1] // HEAD
    heads_q = query_mat.shape[1] // HEAD
    group_size = heads_q // heads_kv
    score_scale = HEAD ** (-0.5)
    half_size = HEAD // 2
    inv_freqs = theta_base ** (-2.0 * jnp.arange(half_size, dtype=jnp.float32) / HEAD)
    angles = positions.astype(jnp.float32)[:, :, None] * inv_freqs
    cos_part = jnp.cos(angles)[:, :, None, :]
    sin_part = jnp.sin(angles)[:, :, None, :]
    flat_in = tokens.astype(jnp.float32).reshape(row_count, model_width)
    unit_one, inverse_one, normed = norm_forward(flat_in, full_one)
    query_proj = jnp.dot(normed, query_mat, preferred_element_type=jnp.float32).reshape(
        slot_count, seq_count, heads_q, HEAD
    )
    key_proj = jnp.dot(normed, key_mat, preferred_element_type=jnp.float32).reshape(
        slot_count, seq_count, heads_kv, HEAD
    )
    value_low = (
        jnp.dot(normed, value_mat, preferred_element_type=jnp.float32)
        .astype(jnp.bfloat16)
        .reshape(slot_count, seq_count, heads_kv * HEAD)
    )
    queries = rotate(query_proj, cos_part, sin_part).astype(jnp.bfloat16)
    keys_low = (
        rotate(key_proj, cos_part, sin_part)
        .astype(jnp.bfloat16)
        .reshape(slot_count, seq_count, heads_kv * HEAD)
    )
    query_seq = jnp.transpose(
        queries.reshape(slot_count, seq_count, heads_kv, group_size, HEAD), (1, 2, 3, 0, 4)
    )
    query_pos = positions.T
    stat_shape = (seq_count, heads_kv, group_size, slot_count)
    initial = (
        jnp.full(stat_shape, masked_value, jnp.float32),
        jnp.zeros(stat_shape, jnp.float32),
        jnp.zeros(stat_shape + (HEAD,), jnp.float32),
    )
    key_piece = lax.all_gather(keys_low, "context", axis=0, tiled=True)
    value_piece = lax.all_gather(value_low, "context", axis=0, tiled=True)
    pos_piece = lax.all_gather(positions, "context", axis=0, tiled=True)
    piece_len = key_piece.shape[0]
    key_seq = jnp.transpose(key_piece.reshape(piece_len, seq_count, heads_kv, HEAD), (1, 2, 0, 3))
    value_seq = jnp.transpose(
        value_piece.reshape(piece_len, seq_count, heads_kv, HEAD), (1, 2, 0, 3)
    )
    pos_seq = pos_piece.T

    def per_sequence(seq_items):
        peak_val, totals, accum_vals, query_one, qpos_one, key_one, value_one, kpos_one = seq_items
        raw_scores = (
            jnp.einsum("hgqd,hkd->hgqk", query_one, key_one, preferred_element_type=jnp.float32)
            * score_scale
        )
        allowed = kpos_one[None, None, None, :] <= qpos_one[None, None, :, None]
        masked = jnp.where(allowed, raw_scores, masked_value)
        new_peak = jnp.maximum(peak_val, jnp.max(masked, axis=-1))
        decay_vals = jnp.exp(peak_val - new_peak)
        weights = jnp.where(allowed, jnp.exp(masked - new_peak[..., None]), 0.0)
        totals = totals * decay_vals + jnp.sum(weights, axis=-1)
        accum_vals = accum_vals * decay_vals[..., None] + jnp.einsum(
            "hgqk,hkd->hgqd",
            weights.astype(jnp.bfloat16),
            value_one,
            preferred_element_type=jnp.float32,
        )
        return (new_peak, totals, accum_vals)

    peak_val, totals, accum_vals = lax.map(
        per_sequence,
        (initial[0], initial[1], initial[2], query_seq, query_pos, key_seq, value_seq, pos_seq),
    )
    log_total = peak_val + jnp.log(totals)
    mixed_seq = accum_vals / totals[..., None]
    mixed_low = (
        jnp.transpose(mixed_seq, (3, 0, 1, 2, 4))
        .reshape(row_count, heads_q * HEAD)
        .astype(jnp.bfloat16)
    )
    branch = lax.psum(
        jnp.dot(mixed_low, out_mat, preferred_element_type=jnp.float32).astype(jnp.bfloat16),
        "tensor",
    ).astype(jnp.float32)
    middle = flat_in + branch
    unit_two, inverse_two, second = norm_forward(middle, full_two)
    gate_vals = jnp.dot(second, gate_mat, preferred_element_type=jnp.float32)
    up_vals = jnp.dot(second, up_mat, preferred_element_type=jnp.float32)
    sigmoid_vals = jax.nn.sigmoid(gate_vals)
    silu_vals = gate_vals * sigmoid_vals
    hidden = (silu_vals * up_vals).astype(jnp.bfloat16)
    mlp_part = lax.psum(
        jnp.dot(hidden, down_mat, preferred_element_type=jnp.float32).astype(jnp.bfloat16), "tensor"
    ).astype(jnp.float32)
    layer_out = (middle + mlp_part).astype(jnp.bfloat16).reshape(slot_count, seq_count, model_width)
    regathered = (
        lax.all_gather(gain_one, ("dp", "context"), axis=0, tiled=True),
        lax.all_gather(gain_two, ("dp", "context"), axis=0, tiled=True),
        lax.all_gather(w_query, ("dp", "context"), axis=0, tiled=True),
        lax.all_gather(w_key, ("dp", "context"), axis=0, tiled=True),
        lax.all_gather(w_value, ("dp", "context"), axis=0, tiled=True),
        lax.all_gather(w_out, ("dp", "context"), axis=1, tiled=True),
        lax.all_gather(w_gate, ("dp", "context"), axis=0, tiled=True),
        lax.all_gather(w_up, ("dp", "context"), axis=0, tiled=True),
        lax.all_gather(w_down, ("dp", "context"), axis=1, tiled=True),
    )
    full_one, full_two, query_mat, key_mat, value_mat, out_mat, gate_mat, up_mat, down_mat = (
        regathered
    )
    grad_low = cotangent.reshape(row_count, model_width)
    grad_down = contract_rows(hidden, grad_low)
    grad_hidden = contract_cols(grad_low, down_mat)
    grad_gate_low = (
        grad_hidden * up_vals * sigmoid_vals * (1.0 + gate_vals * (1.0 - sigmoid_vals))
    ).astype(jnp.bfloat16)
    grad_up_low = (grad_hidden * silu_vals).astype(jnp.bfloat16)
    grad_gate = contract_rows(second, grad_gate_low)
    grad_up = contract_rows(second, grad_up_low)
    grad_second = lax.psum(
        (contract_cols(grad_gate_low, gate_mat) + contract_cols(grad_up_low, up_mat)).astype(
            jnp.bfloat16
        ),
        "tensor",
    ).astype(jnp.float32)
    grad_mid_norm, grad_gain_two = norm_backward(grad_second, unit_two, inverse_two, full_two)
    grad_middle = grad_low.astype(jnp.float32) + grad_mid_norm
    grad_mid_low = grad_middle.astype(jnp.bfloat16)
    grad_out = contract_rows(mixed_low, grad_mid_low)
    grad_mixed = contract_cols(grad_mid_low, out_mat).astype(jnp.bfloat16)
    grad_mixed_seq = jnp.transpose(
        grad_mixed.reshape(slot_count, seq_count, heads_kv, group_size, HEAD), (1, 2, 3, 0, 4)
    )
    delta_rows = jnp.sum(grad_mixed_seq.astype(jnp.float32) * mixed_seq, axis=-1)
    kv_width = heads_kv * HEAD

    def block_grads(grad_query_acc, key_blk, value_blk, pos_blk):
        block_len = key_blk.shape[0]
        key_seq = jnp.transpose(key_blk.reshape(block_len, seq_count, heads_kv, HEAD), (1, 2, 0, 3))
        value_seq = jnp.transpose(
            value_blk.reshape(block_len, seq_count, heads_kv, HEAD), (1, 2, 0, 3)
        )
        raw_scores = (
            jnp.einsum("shgqd,shkd->shgqk", query_seq, key_seq, preferred_element_type=jnp.float32)
            * score_scale
        )
        allowed = pos_blk.T[:, None, None, None, :] <= query_pos[:, None, None, :, None]
        prob_vals = jnp.where(
            allowed,
            jnp.exp(jnp.where(allowed, raw_scores - log_total[..., None], masked_value)),
            0.0,
        )
        grad_value_blk = jnp.einsum(
            "shgqk,shgqd->kshd",
            prob_vals.astype(jnp.bfloat16),
            grad_mixed_seq,
            preferred_element_type=jnp.float32,
        )
        grad_probs = jnp.einsum(
            "shgqd,shkd->shgqk", grad_mixed_seq, value_seq, preferred_element_type=jnp.float32
        )
        grad_scores = (prob_vals * (grad_probs - delta_rows[..., None])).astype(jnp.bfloat16)
        grad_query_acc = grad_query_acc + jnp.einsum(
            "shgqk,shkd->shgqd", grad_scores, key_seq, preferred_element_type=jnp.float32
        )
        grad_key_blk = jnp.einsum(
            "shgqk,shgqd->kshd", grad_scores, query_seq, preferred_element_type=jnp.float32
        )
        return (
            grad_query_acc,
            grad_key_blk.reshape(block_len, seq_count, kv_width),
            grad_value_blk.reshape(block_len, seq_count, kv_width),
        )

    zero_query = jnp.zeros(stat_shape + (HEAD,), jnp.float32)
    key_all, value_all, pos_all = (
        lax.all_gather(keys_low, "context", axis=0, tiled=True),
        lax.all_gather(value_low, "context", axis=0, tiled=True),
        lax.all_gather(positions, "context", axis=0, tiled=True),
    )
    total_len = key_all.shape[0]
    block_size = min(512, total_len)
    block_count = total_len // block_size

    def key_block(grad_query_acc, block_items):
        key_blk, value_blk, pos_blk = block_items
        grad_query_acc, grad_key_blk, grad_value_blk = block_grads(
            grad_query_acc, key_blk, value_blk, pos_blk
        )
        return (grad_query_acc, (grad_key_blk, grad_value_blk))

    grad_query_acc, (grad_keys_all, grad_values_all) = lax.scan(
        key_block,
        zero_query,
        (
            key_all.reshape(block_count, block_size, seq_count, kv_width),
            value_all.reshape(block_count, block_size, seq_count, kv_width),
            pos_all.reshape(block_count, block_size, seq_count),
        ),
    )
    grad_key_own, grad_value_own = (
        lax.psum_scatter(
            grad_keys_all.reshape(total_len, seq_count, kv_width).astype(jnp.bfloat16),
            "context",
            scatter_dimension=0,
            tiled=True,
        ).astype(jnp.float32),
        lax.psum_scatter(
            grad_values_all.reshape(total_len, seq_count, kv_width).astype(jnp.bfloat16),
            "context",
            scatter_dimension=0,
            tiled=True,
        ).astype(jnp.float32),
    )
    grad_rot_q = jnp.transpose(grad_query_acc * score_scale, (3, 0, 1, 2, 4)).reshape(
        slot_count, seq_count, heads_q, HEAD
    )
    grad_q_low = (
        rotate(grad_rot_q, cos_part, -sin_part)
        .reshape(row_count, heads_q * HEAD)
        .astype(jnp.bfloat16)
    )
    grad_rot_k = (grad_key_own * score_scale).reshape(slot_count, seq_count, heads_kv, HEAD)
    grad_k_low = (
        rotate(grad_rot_k, cos_part, -sin_part).reshape(row_count, kv_width).astype(jnp.bfloat16)
    )
    grad_v_low = grad_value_own.reshape(row_count, kv_width).astype(jnp.bfloat16)
    grad_query = contract_rows(normed, grad_q_low)
    grad_key = contract_rows(normed, grad_k_low)
    grad_value = contract_rows(normed, grad_v_low)
    grad_normed = lax.psum(
        (
            contract_cols(grad_q_low, query_mat)
            + contract_cols(grad_k_low, key_mat)
            + contract_cols(grad_v_low, value_mat)
        ).astype(jnp.bfloat16),
        "tensor",
    ).astype(jnp.float32)
    grad_in_norm, grad_gain_one = norm_backward(grad_normed, unit_one, inverse_one, full_one)
    input_grad = (grad_middle + grad_in_norm).reshape(slot_count, seq_count, model_width)
    reduced = (
        lax.psum_scatter(grad_gain_one, ("dp", "context"), scatter_dimension=0, tiled=True),
        lax.psum_scatter(grad_gain_two, ("dp", "context"), scatter_dimension=0, tiled=True),
        lax.psum_scatter(grad_query, ("dp", "context"), scatter_dimension=0, tiled=True),
        lax.psum_scatter(grad_key, ("dp", "context"), scatter_dimension=0, tiled=True),
        lax.psum_scatter(grad_value, ("dp", "context"), scatter_dimension=0, tiled=True),
        lax.psum_scatter(grad_out, ("dp", "context"), scatter_dimension=1, tiled=True),
        lax.psum_scatter(grad_gate, ("dp", "context"), scatter_dimension=0, tiled=True),
        lax.psum_scatter(grad_up, ("dp", "context"), scatter_dimension=0, tiled=True),
        lax.psum_scatter(grad_down, ("dp", "context"), scatter_dimension=1, tiled=True),
    )
    return (
        layer_out,
        input_grad,
        reduced[0],
        reduced[1],
        reduced[2],
        reduced[3],
        reduced[4],
        reduced[5],
        reduced[6],
        reduced[7],
        reduced[8],
    )


WIDE = 128
HALF = HEAD // 2
RUN = 256
TILE = 512
LOG2_E = 1.4426950408889634
MESH = pl.DeviceIdType.MESH
PIECE = 256
FEED = 512
VMEM_LIMIT = 56 * 1024 * 1024


def any_spec():
    return pl.BlockSpec(memory_space=pl.ANY)


def vmem_spec():
    return pl.BlockSpec(memory_space=pltpu.VMEM)


def place():
    return lax.axis_index("dp"), lax.axis_index("context"), lax.axis_index("tensor")


def greet(devices):
    barrier = pltpu.get_barrier_semaphore()
    for device in devices:
        pl.semaphore_signal(barrier, inc=1, device_id=device, device_id_type=MESH)
    pl.semaphore_wait(barrier, len(devices))


def sequence_others():
    row, spot, core = place()
    return [
        (row, lax.rem(spot + shift, 8), lax.rem(core + flip, 2))
        for shift in range(8)
        for flip in range(2)
        if shift or flip
    ]


def dot_f32(left, right):
    return jnp.dot(left, right, preferred_element_type=jnp.float32)


def remote(source, target, send, recv, device):
    return pltpu.make_async_remote_copy(
        src_ref=source,
        dst_ref=target,
        send_sem=send,
        recv_sem=recv,
        device_id=device,
        device_id_type=MESH,
    )


def move(source, target, send, recv, device, is_self):
    @pl.when(is_self)
    def _():
        pltpu.make_async_copy(source, target, recv).start()

    @pl.when(jnp.logical_not(is_self))
    def _():
        remote(source, target, send, recv, device).start()


def return_copies(ref, out, send, recv):
    row, spot, core = place()
    head = 2 * lax.rem(spot, 4) + core
    owner = spot // 4
    copies = []
    for step in range(8):
        chip = lax.rem(spot + step, 8)
        is_self = (owner == core) if step == 0 else False
        parts = (ref.at[chip], out.at[head], send.at[step], recv.at[head], (row, chip, owner))
        copies.append((parts, is_self))
    return copies


def start_return(copies):
    for parts, is_self in copies:
        if is_self is False:
            remote(*parts).start()
        else:
            move(*parts, is_self)


def finish_return(copies, out, send, recv):
    row, spot, core = place()
    for head in range(8):
        remote(
            out.at[head], out.at[head], send.at[0], recv.at[head], (row, spot, 1 - core)
        ).wait_recv()
    for parts, is_self in copies:
        if is_self is False:
            remote(*parts).wait_send()
        else:

            @pl.when(jnp.logical_not(is_self))
            def _():
                remote(*parts).wait_send()


def tile_at(index, size):
    return pl.ds(pl.multiple_of(index * size, size), size)


def causal(scores):
    keys = lax.broadcasted_iota(jnp.int32, scores.shape, 0)
    queries = lax.broadcasted_iota(jnp.int32, scores.shape, 1)
    return jnp.where(keys <= queries, scores, masked_value)


def neighbours():
    row, spot, core = place()
    level, column = spot // 2, lax.rem(spot, 2)
    beside_x = (1 - row, spot, core)
    beside_y = (row, 2 * level + 1 - column, core)
    along_z = [(row, 2 * lax.rem(level + k, 4) + column, core) for k in (1, 2, 3)]
    return row, level, column, beside_x, beside_y, along_z


class Gather:
    def __init__(self, own, whole, start, width, piece, sems):
        self.own, self.whole = own.at[:, pl.ds(start, width)], whole
        self.start, self.width = start, width
        names = ("send_z", "recv_z", "send_x", "recv_x", "send_y", "recv_y", "send_d", "recv_d")
        for name, sem in zip(names + ("local",), sems):
            setattr(self, name, sem.at[piece])

    def block(self, x, z, y, half=None):
        cut = self.width * 7 // 12 // WIDE * WIDE
        start, width = self.start, self.width
        if half == 0:
            width = cut
        elif half == 1:
            start, width = start + cut, width - cut
        return self.whole.at[x, z, y, :, pl.ds(start, width)]

    def arrived(self, target, recv_sem):
        device = neighbours()[3]
        remote(target, target, self.send_x.at[0], recv_sem, device).wait_recv()

    def copy_z(self, z, up):
        row, level, column, beside_x, beside_y = neighbours()[:5]
        core = place()[2]
        target = level + 1 if up else level - 1
        block = self.block(row, z, column)
        return remote(
            block,
            block,
            self.send_z.at[int(up), z],
            self.recv_z.at[z],
            (row, 2 * target + column, core),
        )

    def copies_xy(self, z):
        row, level, column, beside_x, beside_y = neighbours()[:5]
        block = self.block(row, z, column)
        return [
            remote(block, block, self.send_x.at[z], self.recv_x.at[z], beside_x),
            remote(block, block, self.send_y.at[z], self.recv_y.at[z], beside_y),
        ]

    def copies_diagonal(self, z):
        row, level, column, beside_x, beside_y = neighbours()[:5]
        by_y = self.block(1 - row, z, column, 1)
        by_x = self.block(row, z, 1 - column, 0)
        return [
            remote(by_y, by_y, self.send_d.at[0, z], self.recv_d.at[0, z], beside_y),
            remote(by_x, by_x, self.send_d.at[1, z], self.recv_d.at[1, z], beside_x),
        ]

    def own_copy(self):
        row, level, column = neighbours()[:3]
        return pltpu.make_async_copy(self.own, self.block(row, level, column), self.local)

    def each_at(self, hop, act):
        level = neighbours()[1]

        @pl.when(level >= hop)
        def _():
            act(level - hop, True)

        @pl.when(level + hop <= 3)
        def _():
            act(level + hop, False)

    def start_z(self, z, up):
        level = neighbours()[1]

        @pl.when(level < 3 if up else level > 0)
        def _():
            self.copy_z(z, up).start()

    def place_own(self):
        self.own_copy().start()

    def open(self):
        level = neighbours()[1]
        self.own_copy().wait()
        self.start_z(level, True)
        self.start_z(level, False)
        for copy in self.copies_xy(level):
            copy.start()

    def hop(self, hop):
        def act(z, up):
            row, level, column = neighbours()[:3]
            self.arrived(self.block(row, z, column), self.recv_z.at[z])
            self.start_z(z, up)
            for copy in self.copies_xy(z):
                copy.start()

        self.each_at(hop, act)

    def turn_diagonal(self, z):
        row, level, column = neighbours()[:3]
        by_y, by_x = self.copies_diagonal(z)
        self.arrived(self.block(1 - row, z, column), self.recv_x.at[z])
        by_y.start()
        self.arrived(self.block(row, z, 1 - column), self.recv_y.at[z])
        by_x.start()

    def diagonal(self, hop):
        if hop == 0:
            self.turn_diagonal(neighbours()[1])
        else:
            self.each_at(hop, lambda z, up: self.turn_diagonal(z))

    def finish(self):
        row, level, column = neighbours()[:3]
        for z in range(4):
            self.arrived(self.block(1 - row, z, 1 - column, 1), self.recv_d.at[0, z])
            self.arrived(self.block(1 - row, z, 1 - column, 0), self.recv_d.at[1, z])

    def close(self):
        level = neighbours()[1]

        def sent(z, up):
            @pl.when(level < 3 if up else level > 0)
            def _():
                self.copy_z(z, up).wait_send()

        sent(level, True)
        sent(level, False)
        for hop in range(1, 4):
            self.each_at(hop, sent)
        for z in range(4):
            for copy in self.copies_xy(z) + self.copies_diagonal(z):
                copy.wait_send()


def gather_sems(pieces):
    dma = pltpu.SemaphoreType.DMA
    shapes = [(2, 4), (4,), (4,), (4,), (4,), (4,), (2, 4), (2, 4), ()]
    return [dma((pieces,) + shape) for shape in shapes]


AT_BEGIN, AT_GROUP, AT_HEADS, AT_KEYS, AT_RETURN, AT_OUT, AT_NORM, AT_TILE, AT_FEED = 0, 1, 5, 6, 7, 8, 9, 10, 18
PUMPS = {
    AT_BEGIN: (4, 1, 2, 3, 5, 6, 7, 10, 11, 12, 20, 13),
    AT_GROUP + 0: (21,),
    AT_GROUP + 2: (30,),
    AT_GROUP + 3: (16, 24, 14),
    AT_HEADS: (22, 17, 15, 25, 23),
    AT_KEYS: (40,),
    AT_TILE + 0: (31,),
    AT_TILE + 1: (27,),
    AT_TILE + 2: (26,),
    AT_TILE + 3: (32,),
    AT_TILE + 5: (33,),
    AT_TILE + 6: (34, 41),
    AT_TILE + 7: (44,),
    AT_RETURN: (35, 42, 37, 36, 50, 45, 43),
    AT_OUT: (46, 51),
    AT_NORM: (54,),
    AT_FEED + 1: (47, 52, 55),
    AT_FEED + 3: (53,),
    AT_FEED + 5: (56, 57),
}


def forward_kernel(
    tokens,
    positions,
    freqs,
    ids_in,
    gain_one,
    gain_two,
    w_query,
    w_key,
    w_value,
    w_out_t,
    w_gate,
    w_up,
    w_down_t,
    cotangent,
    near,
    far,
    normed_out,
    q_out,
    k_out,
    v_out,
    mixed_t_out,
    lse_out,
    mixed_low_out,
    middle_out,
    second_out,
    right_out,
    gains_out,
    tables_out,
    order,
    ids_flat,
    near_own,
    far_own,
    unit,
    normed,
    tables,
    weight,
    extras,
    gain_rows,
    q_heads,
    kv_heads,
    q_slots,
    kv_slots,
    q_t,
    keys,
    v_t,
    mixed_t,
    lse,
    mixed,
    mixed_slots,
    mixed_heads,
    mixed_low,
    out_weight,
    part,
    part_other,
    second,
    cot,
    right,
    feed_weight,
    ids_all,
    ids,
    load_own,
    send_ids,
    recv_ids,
    load_ids,
    load_w,
    load_extra,
    load_out,
    load_feed,
    load_cot,
    save_right,
    saves,
    send_q,
    recv_q,
    send_kv,
    recv_kv,
    send_x,
    recv_x,
    send_m,
    recv_m,
    send_p,
    recv_p,
    *sems,
):
    row, spot, core = place()
    low, full = jnp.bfloat16, jnp.float32
    rows, width = tokens.shape
    share = near_own.shape[0]
    length = 8 * rows
    runs, tiles = length // RUN, length // TILE
    per_device = rows // RUN
    halves = TILE // RUN
    quarter = 4 * share
    sibling = (row, spot, 1 - core)
    out_width = w_out_t.shape[1]
    qkv_width = 16 * HEAD

    near_loads, far_loads, start = [], [], 0
    for ref in (w_query, w_key, w_value, w_out_t):
        if ref is w_out_t:
            start += WIDE
        target = near_own.at[:, pl.ds(start, ref.shape[1])]
        near_loads.append(pltpu.make_async_copy(ref, target, load_own.at[len(near_loads)]))
        start += ref.shape[1]
    for index, ref in enumerate((w_gate, w_up, w_down_t)):
        for piece in range(4):
            source = ref.at[:, pl.ds(piece * FEED, FEED)]
            target = far_own.at[:, pl.ds((3 * piece + index) * FEED, FEED)]
            far_loads.append(
                pltpu.make_async_copy(source, target, load_own.at[4 + 4 * index + piece])
            )
    for copy in near_loads + far_loads:
        copy.start()
    load_cotangent = pltpu.make_async_copy(cotangent, cot, load_cot)
    load_cotangent.start()
    line = lax.broadcasted_iota(jnp.int32, (WIDE, share), 0)
    gains = jnp.where(line == 0, gain_one[...].astype(full), 0.0)
    gains = jnp.where(line == 1, gain_two[...].astype(full), gains)
    near_own[:, qkv_width : qkv_width + WIDE] = gains.T.astype(low)

    first = Gather(near_own, near, 0, qkv_width + WIDE, 0, sems)
    outer = Gather(near_own, near, qkv_width + WIDE, out_width, 1, sems)
    feeds = [Gather(far_own, far, 3 * FEED * p, 3 * FEED, 2 + p, sems) for p in range(4)]
    gathers = [first, outer] + feeds

    def pump(place):
        for what in PUMPS.get(place, ()):
            gather, act = gathers[what // 10], what % 10
            if act == 0:
                gather.open()
            elif act < 4:
                gather.hop(act)
            else:
                gather.diagonal(act - 4)

    for copy in near_loads:
        copy.wait()
    first.place_own()
    outer.place_own()
    for copy in far_loads:
        copy.wait()
    for gather in feeds:
        gather.place_own()
    greet(sequence_others() + [neighbours()[3]])
    first.open()

    for shift in range(1, 8):
        remote(
            ids_in,
            ids_all.at[spot],
            send_ids.at[shift],
            recv_ids.at[shift],
            (row, lax.rem(spot + shift, 8), core),
        ).start()
    ids_all[spot] = ids_in[...]

    values = tokens[...].astype(full)
    unit[...] = values * lax.rsqrt(jnp.mean(values * values, axis=-1, keepdims=True) + epsilon)
    angles = freqs[...] * positions[...].astype(full)
    tables[0] = jnp.cos(angles)
    tables[1] = jnp.sin(angles)

    pump(AT_BEGIN)
    for shift in range(1, 8):
        remote(
            ids_in,
            ids_all.at[lax.rem(spot + 8 - shift, 8)],
            send_ids.at[shift],
            recv_ids.at[shift],
            (row, lax.rem(spot + shift, 8), core),
        ).wait_recv()
    pltpu.make_async_copy(ids_all, ids, load_ids).start()
    first.finish()

    def load_group(group):
        lanes = pl.ds(group * 4 * HEAD, 4 * HEAD)
        return pltpu.make_async_copy(
            near.at[:, :, :, :, lanes], weight.at[group % 2], load_w.at[group % 2]
        )

    load_extras = pltpu.make_async_copy(
        near.at[:, :, :, :, pl.ds(qkv_width, WIDE)], extras, load_extra
    )
    load_out_weight = pltpu.make_async_copy(
        near.at[:, :, :, :, pl.ds(qkv_width + WIDE, out_width)], out_weight, load_out
    )
    load_extras.start()
    load_group(0).start()
    load_group(1).start()
    load_extras.wait()
    gain_rows[...] = extras[...].reshape(width, WIDE).T[0:8].astype(full)
    normed[...] = (unit[...] * gain_rows[0:1]).astype(low)
    for group in range(4):
        load_group(group).wait()
        proj = dot_f32(normed[...], weight[group % 2].reshape(width, 4 * HEAD)).T
        if group < 2:
            load_group(group + 2).start()
        for head in range(4):
            front = proj[head * HEAD : head * HEAD + HALF]
            back = proj[head * HEAD + HALF : (head + 1) * HEAD]
            if group < 3:
                front, back = (
                    front * tables[0] - back * tables[1],
                    back * tables[0] + front * tables[1],
                )
            for start, value in ((0, front.astype(low)), (HALF, back.astype(low))):
                for run in range(per_device):
                    piece = value[:, run * RUN : (run + 1) * RUN]
                    if group < 2:
                        q_heads[4 * group + head, run, start : start + HALF] = piece
                    else:
                        kv_heads[head, group - 2, run, start : start + HALF] = piece
        pump(AT_GROUP + group)

    outgoing = []
    for step in range(4):
        slot = lax.rem(spot + step, 4)
        chip = 4 * core + slot
        for other in range(2):
            is_self = jnp.logical_and(chip == spot, core == other)
            device = (row, chip, other)
            kv_parts = (
                kv_heads.at[slot, :, other],
                kv_slots.at[spot, :, other],
                send_kv.at[step, other],
                recv_kv.at[spot],
                device,
            )
            q_parts = (
                q_heads.at[2 * slot + other],
                q_slots.at[spot],
                send_q.at[step, other],
                recv_q.at[spot],
                device,
            )
            outgoing.append((kv_parts, is_self))
            outgoing.append((q_parts, is_self))
    for parts, is_self in outgoing:
        move(*parts, is_self)
    pump(AT_HEADS)

    def hand_on(source):
        block = kv_slots.at[source, :, core]
        return remote(block, block, send_x.at[source], recv_x.at[source], sibling)

    for step in range(8):
        source = lax.rem(spot + step, 8)
        block = kv_slots.at[source, :, core]
        remote(block, block, send_x.at[source], recv_kv.at[source], sibling).wait_recv()
        hand_on(source).start()
    pump(AT_KEYS)
    for step in range(8):
        remote(
            q_slots.at[step], q_slots.at[step], send_x.at[step], recv_q.at[step], sibling
        ).wait_recv()
        hand_on(step).wait()

    pltpu.make_async_copy(ids_all, ids, load_ids).wait()

    def find_run(index, carry):
        device, piece = 0, 0
        for run in range(runs):
            here = ids[run // per_device, 0, run % per_device] == index
            device = jnp.where(here, run // per_device, device)
            piece = jnp.where(here, run % per_device, piece)
        order[index, 0] = device
        order[index, 1] = piece
        found = ids[index // per_device, 0, index % per_device]
        order[runs + index, 0] = lax.div(found, per_device)
        order[runs + index, 1] = lax.rem(found, per_device)
        ids_flat[index] = found
        return carry

    lax.fori_loop(0, runs, find_run, 0)

    def sort_run(index, carry):
        device, piece = order[index, 0], order[index, 1]
        cols = tile_at(index, RUN)
        q_t[:, cols] = q_slots[device, piece]
        keys[index] = kv_slots[device, 0, piece].T
        v_t[:, cols] = kv_slots[device, 1, piece]
        return carry

    lax.fori_loop(0, runs, sort_run, 0)
    scale = HEAD ** (-0.5) * LOG2_E

    def query_tile(index, carry):
        cols = tile_at(index, TILE)
        queries = q_t[:, cols]

        def step(scores, block, peak, total, mix):
            high = jnp.maximum(peak, jnp.max(scores, axis=0, keepdims=True))
            decay = jnp.exp2(peak - high)
            weights = jnp.exp2(scores - high)
            total = total * decay + jnp.sum(weights, axis=0, keepdims=True)
            mix = mix * decay + dot_f32(v_t[:, tile_at(block, TILE)], weights.astype(low))
            return high, total, mix

        def scores_of(block):
            held = keys[pl.ds(block * halves, halves)].reshape(TILE, HEAD)
            return dot_f32(held, queries) * scale

        state = (
            jnp.full((1, TILE), masked_value, full),
            jnp.zeros((1, TILE), full),
            jnp.zeros((HEAD, TILE), full),
        )
        state = step(causal(scores_of(index)), index, *state)
        peak, total, mix = lax.fori_loop(
            0, index, lambda block, now: step(scores_of(block), block, *now), state
        )
        mix = mix / total
        mixed_t[:, cols] = mix
        lse[:, cols] = peak + jnp.log2(total)
        for half in range(halves):
            mixed[index * halves + half] = mix[:, half * RUN : (half + 1) * RUN].astype(low)

        for tile in range(tiles):

            @pl.when(index == tile)
            def _():
                pump(AT_TILE + tile)

        return carry

    lax.fori_loop(0, tiles, query_tile, 0)

    def unsort_run(run, carry):
        index = ids[run // per_device, 0, run % per_device]
        mixed_slots[run // per_device, run % per_device] = mixed[index]
        return carry

    lax.fori_loop(0, runs, unsort_run, 0)
    copies = return_copies(mixed_slots, mixed_heads, send_m, recv_m)
    start_return(copies)
    early_saves = [
        pltpu.make_async_copy(source, target, saves.at[index])
        for index, (source, target) in enumerate(
            [
                (normed, normed_out),
                (q_t, q_out),
                (keys, k_out),
                (v_t, v_out),
                (mixed_t, mixed_t_out),
                (lse, lse_out),
                (gain_rows, gains_out),
                (tables, tables_out),
            ]
        )
    ]
    for copy in early_saves:
        copy.start()
    pump(AT_RETURN)
    outer.finish()
    load_out_weight.start()
    finish_return(copies, mixed_heads, send_m, recv_m)

    load_out_weight.wait()
    for run in range(per_device):
        side = mixed_heads[:, run].reshape(8 * HEAD, RUN)
        mixed_low[run * RUN : (run + 1) * RUN] = side.T

    def pair_copy(index):
        cut = pl.ds(index * quarter, quarter)
        return remote(
            part.at[:, cut], part_other.at[:, cut], send_p.at[index], recv_p.at[index], sibling
        )

    for index in range(4):
        block = out_weight[index // 2, 2 * (index % 2) : 2 * (index % 2) + 2]
        term = contract_cols(mixed_low[...], block.reshape(quarter, out_width))
        part[:, index * quarter : (index + 1) * quarter] = term.astype(low)
        pair_copy(index).start()
    pump(AT_OUT)
    load_cotangent.wait()
    for index in range(4):
        pair_copy(index).wait()
    chunk = rows // 8

    def norm_block(index, carry):
        cut = tile_at(index, chunk)
        sums = part[cut].astype(full) + part_other[cut].astype(full)
        values = tokens[cut].astype(full) + sums
        unit[cut] = values
        inverse = lax.rsqrt(jnp.mean(values * values, axis=-1, keepdims=True) + epsilon)
        second[cut] = (values * inverse * gain_rows[1:2]).astype(low)
        return carry

    lax.fori_loop(0, 8, norm_block, 0)
    late_saves = [
        pltpu.make_async_copy(source, target, saves.at[8 + index])
        for index, (source, target) in enumerate(
            [(mixed_low, mixed_low_out), (unit, middle_out), (second, second_out)]
        )
    ]
    for copy in late_saves:
        copy.start()
    pump(AT_NORM)

    def load_feed_weight(index, kind):
        piece, half = index // 2, lax.rem(index, 2)
        start = (3 * piece + kind) * FEED + half * PIECE
        lanes = pl.ds(pl.multiple_of(start, PIECE), PIECE)
        return pltpu.make_async_copy(
            far.at[:, :, :, :, lanes], feed_weight.at[half, kind], load_feed.at[half, kind]
        )

    def save_piece(piece):
        lanes = pl.ds(piece * 3 * FEED, 3 * FEED)
        return pltpu.make_async_copy(
            right.at[:, lanes], right_out.at[:, lanes], save_right.at[piece]
        )

    def feed_block(index, carry):
        piece, half = index // 2, lax.rem(index, 2)
        for when in range(4):

            @pl.when(index == 2 * when)
            def _():
                feeds[when].finish()

        @pl.when(half == 0)
        def _():
            for offset in range(2):
                for kind in range(3):
                    load_feed_weight(index + offset, kind).start()

        values = []
        for kind, left in enumerate((second, second, cot)):
            load_feed_weight(index, kind).wait()
            values.append(dot_f32(left[...], feed_weight[half, kind].reshape(width, PIECE)))
        gate, up, grad_hidden = values
        sigmoid = jax.nn.sigmoid(gate)
        silu = gate * sigmoid
        grad_gate = grad_hidden * up * sigmoid * (1.0 + gate * (1.0 - sigmoid))
        for kind, value in enumerate((grad_gate, grad_hidden * silu, silu * up)):
            start = (3 * piece + kind) * FEED + half * PIECE
            right[:, pl.ds(pl.multiple_of(start, PIECE), PIECE)] = value.astype(low)

        for when in range(8):

            @pl.when(index == when)
            def _():
                pump(AT_FEED + when)

        for when in range(4):

            @pl.when(index == 2 * when + 1)
            def _():
                save_piece(when).start()

        return carry

    lax.fori_loop(0, 8, feed_block, 0)
    for gather in gathers:
        gather.close()
    for parts, is_self in outgoing:

        @pl.when(jnp.logical_not(is_self))
        def _():
            remote(*parts).wait_send()

    for shift in range(1, 8):
        remote(
            ids_in,
            ids_all.at[spot],
            send_ids.at[shift],
            recv_ids.at[shift],
            (row, lax.rem(spot + shift, 8), core),
        ).wait_send()
    for copy in early_saves + late_saves + [save_piece(piece) for piece in range(4)]:
        copy.wait()


def forward(
    tokens,
    positions,
    ids,
    gain_one,
    gain_two,
    w_query,
    w_key,
    w_value,
    w_out_t,
    w_gate,
    w_up,
    w_down_t,
    cotangent,
):
    dma = pltpu.SemaphoreType.DMA
    vmem = pltpu.VMEM
    low, full = jnp.bfloat16, jnp.float32
    rows, width = tokens.shape
    share, hidden_width = w_gate.shape
    out_width = w_out_t.shape[1]
    near_width = 16 * HEAD + out_width + WIDE
    length = 8 * rows
    per_device = rows // RUN
    heads = (8, per_device, HEAD, RUN)
    both = (2, per_device, HEAD, RUN)
    by_run = (length // RUN, RUN, HEAD)
    flat = (HEAD, length)
    smem_spec = pl.BlockSpec(memory_space=pltpu.SMEM)
    shape = jax.ShapeDtypeStruct
    return pl.pallas_call(
        forward_kernel,
        in_specs=[vmem_spec()] * 6 + [any_spec()] * 8,
        out_specs=[any_spec()] * 14 + [smem_spec] * 2,
        out_shape=[
            shape((2, 4, 2, share, near_width), low),
            shape((2, 4, 2, share, 3 * hidden_width), low),
            shape((rows, width), low),
            shape(flat, low),
            shape(by_run, low),
            shape(flat, low),
            shape(flat, full),
            shape((1, length), full),
            shape((rows, out_width), low),
            shape((rows, width), full),
            shape((rows, width), low),
            shape((rows, 3 * hidden_width), low),
            shape((8, width), full),
            shape((2, HALF, rows), full),
            shape((2 * length // RUN, 2), jnp.int32),
            shape((length // RUN,), jnp.int32),
        ],
        scratch_shapes=[
            vmem((share, near_width), low),
            vmem((share, 3 * hidden_width), low),
            vmem((rows, width), full),
            vmem((rows, width), low),
            vmem((2, HALF, rows), full),
            vmem((2, 2, 4, 2, share, 4 * HEAD), low),
            vmem((2, 4, 2, share, WIDE), low),
            vmem((8, width), full),
            vmem(heads, low),
            vmem((4,) + both, low),
            vmem(heads, low),
            vmem((8,) + both, low),
            vmem(flat, low),
            vmem(by_run, low),
            vmem(flat, low),
            vmem(flat, full),
            vmem((1, length), full),
            vmem((length // RUN, HEAD, RUN), low),
            vmem(heads, low),
            vmem(heads, low),
            vmem((rows, out_width), low),
            vmem((2, 4, 2, share, out_width), low),
            vmem((rows, width), low),
            vmem((rows, width), low),
            vmem((rows, width), low),
            vmem((rows, width), low),
            vmem((rows, 3 * hidden_width), low),
            vmem((2, 3, 2, 4, 2, share, PIECE), low),
            vmem((8, 8, WIDE), jnp.int32),
            pltpu.SMEM((8, 8, WIDE), jnp.int32),
            dma((16,)),
            dma((8,)),
            dma((8,)),
            dma(()),
            dma((2,)),
            dma(()),
            dma(()),
            dma((2, 3)),
            dma(()),
            dma((4,)),
            dma((12,)),
            dma((4, 2)),
            dma((8,)),
            dma((4, 2)),
            dma((8,)),
            dma((8,)),
            dma((8,)),
            dma((8,)),
            dma((8,)),
            dma((4,)),
            dma((4,)),
        ]
        + gather_sems(6),
        compiler_params=pltpu.CompilerParams(
            collective_id=1, has_side_effects=True, vmem_limit_bytes=VMEM_LIMIT
        ),
        name="forward",
    )(
        tokens,
        positions,
        (theta_base ** (-2.0 * jnp.arange(HALF, dtype=jnp.float32) / HEAD)).reshape(HALF, 1),
        ids,
        gain_one,
        gain_two,
        w_query,
        w_key,
        w_value,
        w_out_t,
        w_gate,
        w_up,
        w_down_t,
        cotangent,
    )


SECOND, THIRD, LAST = 2, 4, 5


class Reduce:
    def __init__(self, n, changes, refs):
        (
            self.left_t,
            self.right,
            self.gains,
            self.own,
            self.out,
            self.save,
            self.send_one,
            self.recv_one,
            self.send_two,
            self.recv_two,
            self.kept,
            self.recv_three,
            self.ss_one,
            self.rs_one,
            self.ss_two,
            self.rs_two,
            self.ss_three,
            self.rs_three,
        ) = refs
        self.n, self.changes = n, changes
        self.share = self.own.shape[1]

    def columns(self, step, kind):
        held = self.right.shape[1] // (2 * PIECE)
        start = lax.rem(step, held) * 2 * PIECE + kind * PIECE
        return pl.ds(pl.multiple_of(start, PIECE), PIECE)

    def saving(self, step):
        slot = lax.rem(step, 2)
        pieces = self.changes[0] // 3
        place = jnp.where(step < self.changes[0], lax.rem(step, 3) * pieces + step // 3, step)
        cut = pl.ds(pl.multiple_of(place * 2 * PIECE, 2 * PIECE), 2 * PIECE)
        return pltpu.make_async_copy(self.own.at[slot], self.out.at[:, cut], self.save.at[slot])

    def product(self, step, kind, x, y):
        left = jnp.where(lax.rem(step, 3) == 2, 0, 1)
        left = jnp.where(step >= self.changes[0], 2, left)
        left = jnp.where(step >= self.changes[1], 0, left)
        term = jnp.dot(
            self.left_t[left, x, y],
            self.right[:, self.columns(step, kind)],
            preferred_element_type=jnp.float32,
        )
        if kind == 1:
            term = jnp.where(step == self.n - 1, self.gains[x, y].astype(jnp.float32), term)
        return term

    def x_first(self, step, kind):
        return 1 if kind == 0 else jnp.where(lax.rem(step, 5) == 4, 1, 0)

    def beside(self, by_x):
        row, level, column = neighbours()[:3]
        core = place()[2]
        other_row = by_x * (1 - row) + (1 - by_x) * row
        other_column = by_x * column + (1 - by_x) * (1 - column)
        return (other_row, 2 * level + other_column, core)

    def first_copy(self, step, kind):
        out, into = lax.rem(step, 3), lax.rem(step, 6)
        return remote(
            self.send_one.at[out, kind],
            self.recv_one.at[into, kind],
            self.ss_one.at[out, kind],
            self.rs_one.at[into, kind],
            self.beside(self.x_first(step, kind)),
        )

    def second_copy(self, step, kind):
        out, into = lax.rem(step, 3), lax.rem(step, 6)
        return remote(
            self.send_two.at[out, kind],
            self.recv_two.at[into, kind],
            self.ss_two.at[out, kind],
            self.rs_two.at[into, kind],
            self.beside(1 - self.x_first(step, kind)),
        )

    def third_copy(self, step, kind, k):
        row, level, column, beside_x, beside_y, along_z = neighbours()
        target = lax.rem(level + k + 1, 4)
        out, into = lax.rem(step, 4), lax.rem(step, 4)
        return remote(
            self.kept.at[out, kind, pl.ds(pl.multiple_of(target * self.share, 16), self.share)],
            self.recv_three.at[into, kind, k],
            self.ss_three.at[out, kind, k],
            self.rs_three.at[into, kind, k],
            along_z[k],
        )

    def first(self, step):
        row, level, column = neighbours()[:3]
        slot = lax.rem(step, 3)
        for kind in range(2):
            by_x = self.x_first(step, kind)
            for half in range(2):
                x = by_x * (1 - row) + (1 - by_x) * half
                y = by_x * half + (1 - by_x) * (1 - column)
                self.send_one[slot, kind, half] = self.product(step, kind, x, y).astype(
                    jnp.bfloat16
                )
            self.first_copy(step, kind).start()

    def second(self, step):
        row, level, column = neighbours()[:3]
        slot, came, keep = lax.rem(step, 3), lax.rem(step, 6), lax.rem(step, 4)
        for kind in range(2):
            self.first_copy(step, kind).wait()
        for kind in range(2):
            by_x = self.x_first(step, kind)
            x = by_x * row + (1 - by_x) * (1 - row)
            y = by_x * (1 - column) + (1 - by_x) * column
            arrived = self.recv_one.at[came, kind]
            mine = by_x * column + (1 - by_x) * row
            away = self.product(step, kind, x, y) + arrived[1 - mine].astype(jnp.float32)
            self.send_two[slot, kind] = away.astype(jnp.bfloat16)
            here = self.product(step, kind, row, column) + arrived[mine].astype(jnp.float32)
            self.kept[keep, kind] = here.astype(jnp.bfloat16)
        for kind in range(2):
            self.second_copy(step, kind).start()

    def third(self, step):
        came, keep = lax.rem(step, 6), lax.rem(step, 4)
        for kind in range(2):
            self.second_copy(step, kind).wait()
            here = self.kept[keep, kind].astype(jnp.float32) + self.recv_two[came, kind].astype(
                jnp.float32
            )
            self.kept[keep, kind] = here.astype(jnp.bfloat16)
            for k in range(3):
                self.third_copy(step, kind, k).start()

    def last(self, step):
        level = neighbours()[1]
        came, keep = lax.rem(step, 4), lax.rem(step, 4)
        mine = pl.ds(pl.multiple_of(level * self.share, 16), self.share)

        @pl.when(step >= 2)
        def _():
            self.saving(step - 2).wait()

        for kind in range(2):
            total = self.kept[keep, kind, mine].astype(jnp.float32)
            for k in range(3):
                self.third_copy(step, kind, k).wait()
                total = total + self.recv_three[came, kind, k].astype(jnp.float32)
            self.own[lax.rem(step, 2), :, kind * PIECE : (kind + 1) * PIECE] = total
        self.saving(step).start()

    def turn(self, step):
        for stage, lag in (
            (self.first, 0),
            (self.second, SECOND),
            (self.third, THIRD),
            (self.last, LAST),
        ):

            @pl.when(jnp.logical_and(step >= lag, step < self.n + lag))
            def _():
                stage(step - lag)


def backward_kernel(
    order,
    ids,
    q_in,
    k_in,
    v_in,
    mixed_t_in,
    lse_in,
    cotangent,
    second_in,
    normed_in,
    right_in,
    mixed_low,
    middle,
    near,
    far,
    tokens,
    gains_in,
    tables,
    input_grad,
    layer_out,
    grads,
    q,
    q_t,
    k,
    k_t,
    v,
    d_own,
    d_slots,
    d,
    d_t,
    dq_t,
    lse,
    delta,
    dk,
    dv,
    dq_slots,
    dkv_sorted,
    dkv_slots,
    dkv_other,
    dq_own,
    dkv_own,
    weight,
    middle_ring,
    input_ring,
    part,
    part_other,
    total,
    staged,
    grad_mid,
    gain_two_grad,
    left_t,
    right,
    gains,
    own,
    send_one,
    recv_one,
    send_two,
    recv_two,
    kept,
    recv_three,
    loads,
    load_left_sem,
    load_w,
    load_ring,
    save_rows,
    save_sem,
    send_d,
    recv_d,
    send_q,
    recv_q,
    send_x,
    recv_x,
    send_k,
    recv_k,
    send_p,
    recv_p,
    save,
    *sems,
):
    row, spot, core = place()
    low, full = jnp.bfloat16, jnp.float32
    rows, width = staged.shape
    length = 8 * rows
    runs, tiles = length // RUN, length // TILE
    per_device = rows // RUN
    halves = TILE // RUN
    share = width // 16
    quarter = 4 * share
    sibling = (row, spot, 1 - core)
    qkv_width = 16 * HEAD
    out_width = mixed_low.shape[1]
    n = grads.shape[1] // (2 * PIECE)
    near_at = right_in.shape[1] // (2 * PIECE)
    changes = (near_at, near_at + qkv_width // (2 * PIECE))
    sums = Reduce(
        n,
        changes,
        (left_t, right, gains, own, grads, save)
        + (send_one, recv_one, send_two, recv_two, kept, recv_three)
        + sems,
    )

    def stage(source):
        return pltpu.make_async_copy(source, staged, load_left_sem)

    def turn_left(index, source):
        for piece in range(4):
            turned = source[:, piece * quarter : (piece + 1) * quarter].T
            for inner in range(4):
                x, z, y = piece // 2, 2 * (piece % 2) + inner // 2, inner % 2
                left_t[index, x, y, z * share : (z + 1) * share] = turned[
                    inner * share : (inner + 1) * share
                ]

    early_loads = [
        pltpu.make_async_copy(source, target, loads.at[index])
        for index, (source, target) in enumerate(
            [
                (right_in, right),
                (q_in, q_t),
                (k_in, k),
                (v_in, d_t),
                (mixed_t_in, dq_t),
                (lse_in, lse),
                (middle, total),
            ]
        )
    ]


    def load_block(index, piece, part_of, start):
        lanes = pl.ds(3 * FEED * piece + start + part_of * PIECE, PIECE)
        levels = pl.ds(2 * lax.rem(index, 2), 2)
        return pltpu.make_async_copy(
            far.at[index // 2, levels, :, :, lanes], held_block(piece, part_of), load_w.at[piece]
        )

    def held_block(piece, part_of):
        levels = pl.ds(2 * (part_of % 2), 2)
        return weight.at[piece, part_of // 2, levels, :, :, pl.ds(0, PIECE)]

    def load_blocks(index, piece, start, parts):
        for part_of in range(parts):
            load_block(index, piece, part_of, start).start()

    def row_products(start, parts, landing):
        def block(index, carry):
            term = jnp.zeros((rows, quarter), full)
            for piece in range(4):
                for part_of in range(parts):
                    load_block(index, piece, part_of, start).wait()
                for part_of in range(parts):
                    at = 3 * FEED * piece + start + part_of * PIECE
                    term = term + contract_cols(
                        right[:, at : at + PIECE],
                        held_block(piece, part_of)[...].reshape(quarter, PIECE),
                    )

                @pl.when(index + 1 < 4)
                def _():
                    load_blocks(index + 1, piece, start, parts)

            part[:, tile_at(index, quarter)] = term.astype(low)
            pair_copy(index, landing).start()
            return carry

        lax.fori_loop(0, 4, block, 0)

    def pair_copy(index, landing):
        cut = pl.ds(pl.multiple_of(index * quarter, quarter), quarter)
        return remote(
            part.at[:, cut],
            part_other.at[landing, :, cut],
            send_p.at[index],
            recv_p.at[landing, index],
            sibling,
        )

    def second_back():
        row_products(0, 4, 0)
        for index in range(2):
            load_out_weight(index).start()

    def load_out_weight(index):
        lanes = pl.ds(qkv_width + WIDE + index * 4 * HEAD, 4 * HEAD)
        return pltpu.make_async_copy(
            near.at[:, :, :, :, lanes], weight.at[index], load_w.at[index]
        )

    d_copies = []
    for step in range(4):
        slot = lax.rem(spot + step, 4)
        chip = 4 * core + slot
        for other in range(2):
            parts = (
                d_own.at[2 * slot + other],
                d_slots.at[spot],
                send_d.at[step, other],
                recv_d.at[spot],
                (row, chip, other),
            )
            d_copies.append((parts, jnp.logical_and(chip == spot, core == other)))

    def middle_back():
        for index in range(4):
            pair_copy(index, 0).wait()
        early_loads[6].wait()
        chunk = rows // 8

        def block(index, gain_grad):
            cut = tile_at(index, chunk)
            grad = part[cut].astype(full) + part_other[0, cut].astype(full)
            values = total[cut]
            inverse = lax.rsqrt(jnp.mean(values * values, axis=-1, keepdims=True) + epsilon)
            unit = values * inverse
            scaled = grad * gains_in[1:2]
            mean = jnp.mean(scaled * unit, axis=-1, keepdims=True)
            result = staged[cut].astype(full) + inverse * (scaled - unit * mean)
            total[cut] = result
            grad_mid[cut] = result.astype(low)
            return gain_grad + jnp.sum(grad * unit, axis=0, keepdims=True)

        gain_two_grad[...] = lax.fori_loop(0, 8, block, jnp.zeros((1, width), full))
        for index in range(2):
            load_out_weight(index).wait()
            grad = dot_f32(grad_mid[...], weight[index].reshape(width, 4 * HEAD)).T.astype(low)
            for head in range(4):
                for run in range(per_device):
                    d_own[4 * index + head, run] = grad[
                        head * HEAD : (head + 1) * HEAD, run * RUN : (run + 1) * RUN
                    ]
        for parts, is_self in d_copies:
            move(*parts, is_self)


    def prepare():
        for copy in early_loads[1:6]:
            copy.wait()
        for index in range(tiles):
            cut = pl.ds(index * TILE, TILE)
            q[cut] = q_t[:, cut].T
            k_t[:, cut] = k[halves * index : halves * (index + 1)].reshape(TILE, HEAD).T
            v[cut] = d_t[:, cut].T

    def take_cotangents():
        for index in range(8):
            remote(
                d_slots.at[index], d_slots.at[index], send_d.at[0, 0], recv_d.at[index], sibling
            ).wait_recv()

        def sort_run(index, carry):
            cols = tile_at(index, RUN)
            run = d_slots[order[index, 0], order[index, 1]]
            d_t[:, cols] = run
            d[cols] = run.T
            delta[:, cols] = jnp.sum(run.astype(full) * dq_t[:, cols], axis=0, keepdims=True)
            return carry

        lax.fori_loop(0, runs, sort_run, 0)
        dq_t[...] = jnp.zeros_like(dq_t)

    scale = HEAD ** (-0.5)

    def key_tile(block):
        cut = tile_at(block, TILE)
        both = pl.ds(block * halves, halves)
        keys, values = k[both].reshape(TILE, HEAD), v[cut]
        keys_t = k_t[:, cut]
        dk[...] = jnp.zeros_like(dk)
        dv[...] = jnp.zeros_like(dv)

        def query_tile(index, diagonal):
            cols = tile_at(index, TILE)
            scores = dot_f32(keys, q_t[:, cols]) * (scale * LOG2_E)
            if diagonal:
                scores = causal(scores)
            probs = jnp.exp2(scores - lse[:, cols])
            dv[...] += dot_f32(probs.astype(low), d[cols])
            grad_probs = dot_f32(values, d_t[:, cols])
            grad_scores = (probs * (grad_probs - delta[:, cols])).astype(low)
            dk[...] += dot_f32(grad_scores, q[cols])
            dq_t[:, cols] += dot_f32(keys_t, grad_scores)

        query_tile(block, True)

        def later(index, inner):
            query_tile(index, False)
            return inner

        lax.fori_loop(block + 1, tiles, later, 0)
        for kind, value in enumerate(((dk[...] * scale).T.astype(low), dv[...].T.astype(low))):
            for half in range(halves):
                dkv_sorted[block * halves + half, kind] = value[:, half * RUN : (half + 1) * RUN]

    def key_tiles(start, stop):
        def one(block, carry):
            key_tile(block)
            return carry

        lax.fori_loop(start, stop, one, 0)

    swap = remote(dkv_slots.at[:, :, 1 - core], dkv_other, send_x, recv_x, sibling)
    dq_copies = return_copies(dq_slots, dq_own, send_q, recv_q)
    slot, owner = lax.rem(spot, 4), spot // 4
    dkv_copies = []
    for step in range(8):
        chip = lax.rem(spot + step, 8)
        parts = (
            dkv_slots.at[:, chip, core],
            dkv_own.at[slot, :, core],
            send_k.at[step],
            recv_k.at[slot, core],
            (row, chip, owner),
        )
        dkv_copies.append((parts, (owner == core) if step == 0 else False))

    def send_back():
        def unsort_run(run, carry):
            index = ids[run]
            for kind in range(2):
                dkv_slots[kind, run // per_device, run % per_device] = dkv_sorted[index, kind]
            return carry

        lax.fori_loop(0, runs, unsort_run, 0)
        swap.start()

        def turn_run(index, carry):
            value = dq_t[:, tile_at(index, RUN)] * scale
            d_slots[index // per_device, index % per_device] = value.astype(low)
            return carry

        lax.fori_loop(0, runs, turn_run, 0)

        def unsort_queries(run, carry):
            value = d_slots[order[runs + run, 0], order[runs + run, 1]]
            dq_slots[run // per_device, run % per_device] = value
            return carry

        lax.fori_loop(0, runs, unsort_queries, 0)
        start_return(dq_copies)

    def add_pairs():
        swap.wait()
        for chip in range(8):
            both = dkv_slots[:, chip, core].astype(full) + dkv_other[:, chip].astype(full)
            dkv_slots[:, chip, core] = both.astype(low)
        start_return(dkv_copies)


    def feed_forward():
        row_products(2 * FEED, 2, 1)
        for group in range(4):
            load_group(group).start()

    save_layer = pltpu.make_async_copy(part, layer_out, save_sem)

    def finish_layer():
        for index in range(4):
            pair_copy(index, 1).wait()
        pieces = width // PIECE

        def load_piece(index):
            lanes = pl.ds(index * PIECE, PIECE)
            return pltpu.make_async_copy(
                middle.at[:, lanes], middle_ring.at[index % 2], load_ring.at[index % 2]
            )

        load_piece(0).start()
        for index in range(pieces):
            if index + 1 < pieces:
                load_piece(index + 1).start()
            load_piece(index).wait()
            cut = pl.ds(index * PIECE, PIECE)
            value = part[:, cut].astype(full) + part_other[1, :, cut].astype(full)
            part[:, cut] = (value + middle_ring[index % 2]).astype(low)
        save_layer.start()


    def load_group(group):
        lanes = pl.ds(group * 4 * HEAD, 4 * HEAD)
        return pltpu.make_async_copy(
            near.at[:, :, :, :, lanes], weight.at[group], load_w.at[group]
        )

    load_mixed = pltpu.make_async_copy(
        mixed_low, right.at[:, pl.ds(qkv_width, out_width)], loads.at[0]
    )

    def project_back():
        load_mixed.start()
        for head in range(8):
            remote(
                dq_own.at[head], dq_own.at[head], send_q.at[0], recv_q.at[head], sibling
            ).wait_recv()
        for slot_in in range(4):
            for core_in in range(2):
                target = dkv_own.at[slot_in, :, core_in]
                remote(
                    target, target, send_k.at[0], recv_k.at[slot_in, core_in], sibling
                ).wait_recv()
        for group in range(4):
            for run in range(per_device):
                cols = slice(run * RUN, (run + 1) * RUN)
                turned = []
                for head in range(4):
                    if group < 2:
                        value = dq_own[4 * group + head, run]
                    else:
                        value = dkv_own[head, group - 2, run]
                    if group < 3:
                        front, back = value[:HALF].astype(full), value[HALF:].astype(full)
                        cos_part, sin_part = tables[0, :, cols], tables[1, :, cols]
                        turned.append((front * cos_part + back * sin_part).astype(low))
                        turned.append((back * cos_part - front * sin_part).astype(low))
                    else:
                        turned.append(value)
                right[cols, group * 4 * HEAD : (group + 1) * 4 * HEAD] = jnp.concatenate(
                    turned, axis=0
                ).T
        start = qkv_width + out_width
        right[:, start : start + PIECE] = jnp.zeros((rows, PIECE), low)
        load_mixed.wait()

    def project_normed():
        save_layer.wait()
        for group in range(4):
            load_group(group).wait()
        stage(tokens).start()

        def block(index, carry):
            term = jnp.zeros((rows, quarter), full)
            for group in range(4):
                held = weight[group, index // 2, pl.ds(2 * lax.rem(index, 2), 2)]
                term = term + contract_cols(
                    right[:, group * 4 * HEAD : (group + 1) * 4 * HEAD],
                    held.reshape(quarter, 4 * HEAD),
                )
            part[:, tile_at(index, quarter)] = term.astype(low)
            pair_copy(index, 0).start()
            return carry

        lax.fori_loop(0, 4, block, 0)

    def save_input(index):
        cut = tile_at(index, rows // 8)
        slot = lax.rem(index, 2)
        return pltpu.make_async_copy(
            input_ring.at[slot], input_grad.at[cut], save_rows.at[slot]
        )

    def norm_back():
        stage(tokens).wait()
        for index in range(4):
            pair_copy(index, 0).wait()
        chunk = rows // 8

        def block(index, gain_grad):
            cut = tile_at(index, chunk)
            grad = part[cut].astype(full) + part_other[0, cut].astype(full)
            values = staged[cut].astype(full)
            inverse = lax.rsqrt(jnp.mean(values * values, axis=-1, keepdims=True) + epsilon)
            unit = values * inverse
            scaled = grad * gains_in[0:1]
            mean = jnp.mean(scaled * unit, axis=-1, keepdims=True)
            result = total[cut] + inverse * (scaled - unit * mean)

            @pl.when(index >= 2)
            def _():
                save_input(index - 2).wait()

            input_ring[lax.rem(index, 2)] = result.reshape(chunk, 1, width)
            save_input(index).start()
            return gain_grad + jnp.sum(grad * unit, axis=0, keepdims=True)

        gain_one_grad = lax.fori_loop(0, 8, block, jnp.zeros((1, width), full))
        lines = []
        for value in (gain_one_grad, gain_two_grad[...]):
            high = value.astype(low).astype(full)
            lines.append((high, value - high))
        which = lax.broadcasted_iota(jnp.int32, (WIDE, width), 0)
        table = jnp.zeros((WIDE, width), full)
        for index, line in enumerate((lines[0][0], lines[1][0], lines[0][1], lines[1][1])):
            table = jnp.where(which == index, line, table)
        columns = table.T.astype(low)
        gains[...] = jnp.zeros_like(gains)
        for x in range(2):
            for z in range(4):
                for y in range(2):
                    start = ((x * 4 + z) * 2 + y) * share
                    gains[x, y, z * share : (z + 1) * share, :WIDE] = columns[start : start + share]

    def take_normed():
        stage(normed_in).start()
        stage(normed_in).wait()
        turn_left(2, staged)

    def start_forward():
        for piece in range(4):
            load_blocks(0, piece, 2 * FEED, 2)

    stage(second_in).start()
    for copy in early_loads:
        copy.start()
    for piece in range(4):
        load_blocks(0, piece, 0, 4)
    greet(sequence_others() + [neighbours()[3]])
    stage(second_in).wait()
    turn_left(1, staged)
    stage(cotangent).start()
    early_loads[0].wait()
    stage(cotangent).wait()

    plan = {
        2: [lambda: turn_left(0, staged), second_back],
        3: [middle_back],
        4: [prepare],
        5: [start_forward, take_cotangents],
    }
    tiles_from, tile_ranges = 5, ((0, 1), (1, 2), (2, 3), (3, 5), (5, 8))
    later = {
        9: [send_back],
        11: [add_pairs, feed_forward, finish_layer, take_normed],
        12: [project_back],
        15: [lambda: turn_left(0, grad_mid), project_normed],
        16: [norm_back],
    }

    def run(step, carry):
        for when, tasks in plan.items():

            @pl.when(step == when)
            def _():
                for task in tasks:
                    task()

        @pl.when(jnp.logical_and(step >= tiles_from, step < tiles_from + len(tile_ranges)))
        def _():
            start, stop = 0, 0
            for index, (first_tile, past_tile) in enumerate(tile_ranges):
                start = jnp.where(step == tiles_from + index, first_tile, start)
                stop = jnp.where(step == tiles_from + index, past_tile, stop)
            key_tiles(start, stop)

        for when, tasks in later.items():

            @pl.when(step == when)
            def _():
                for task in tasks:
                    task()

        sums.turn(step)
        return carry

    lax.fori_loop(0, n + LAST, run, 0)
    for index in (6, 7):
        save_input(index).wait()
    for step in (n - 2, n - 1):
        sums.saving(step).wait()
    for copies in (d_copies, dq_copies, dkv_copies):
        for parts, is_self in copies:
            if is_self is False:
                remote(*parts).wait_send()
            else:

                @pl.when(jnp.logical_not(is_self))
                def _():
                    remote(*parts).wait_send()


def backward(order, ids, *arrays):
    dma = pltpu.SemaphoreType.DMA
    vmem = pltpu.VMEM
    low, full = jnp.bfloat16, jnp.float32
    q_sorted, k_sorted, v_sorted, mixed_t, lse, cotangent, second, normed, right = arrays[:9]
    mixed_low, middle, near, far, tokens, gains, tables = arrays[9:]
    rows, width = cotangent.shape
    length = 8 * rows
    share = width // 16
    wide = right.shape[1] + 16 * HEAD + mixed_low.shape[1] + PIECE
    quarter = 4 * share
    per_device = rows // RUN
    heads = (8, per_device, HEAD, RUN)
    tall, flat = (length, HEAD), (HEAD, length)
    by_run = (length // RUN, RUN, HEAD)
    block = (rows, width)
    smem_spec = pl.BlockSpec(memory_space=pltpu.SMEM)
    shape = jax.ShapeDtypeStruct
    return pl.pallas_call(
        backward_kernel,
        in_specs=[smem_spec] * 2 + [any_spec()] * 14 + [vmem_spec()] * 2,
        out_specs=[any_spec()] * 3,
        out_shape=[shape((rows, 1, width), full), shape(block, low), shape((share, wide), full)],
        scratch_shapes=[
            vmem(tall, low),
            vmem(flat, low),
            vmem(by_run, low),
            vmem(flat, low),
            vmem(tall, low),
            vmem(heads, low),
            vmem(heads, low),
            vmem(tall, low),
            vmem(flat, low),
            vmem(flat, full),
            vmem((1, length), full),
            vmem((1, length), full),
            vmem((TILE, HEAD), full),
            vmem((TILE, HEAD), full),
            vmem(heads, low),
            vmem((length // RUN, 2, HEAD, RUN), low),
            vmem((2,) + heads, low),
            vmem((2, 8, HEAD, RUN), low),
            vmem(heads, low),
            vmem((4, 2, per_device, HEAD, RUN), low),
            vmem((4, 2, 4, 2, share, 4 * HEAD), low),
            vmem((2, rows, PIECE), full),
            vmem((2, rows // 8, 1, width), full),
            vmem(block, low),
            vmem((2,) + block, low),
            vmem(block, full),
            vmem(block, low),
            vmem(block, low),
            vmem((1, width), full),
            vmem((3, 2, 2, quarter, rows), low),
            vmem(right.shape, low),
            vmem((2, 2, quarter, PIECE), low),
            vmem((2, share, 2 * PIECE), full),
            vmem((3, 2, 2, quarter, PIECE), low),
            vmem((6, 2, 2, quarter, PIECE), low),
            vmem((3, 2, quarter, PIECE), low),
            vmem((6, 2, quarter, PIECE), low),
            vmem((4, 2, quarter, PIECE), low),
            vmem((4, 2, 3, share, PIECE), low),
            dma((7,)),
            dma(()),
            dma((4,)),
            dma((2,)),
            dma((2,)),
            dma(()),
            dma((4, 2)),
            dma((8,)),
            dma((8,)),
            dma((8,)),
            dma(()),
            dma(()),
            dma((8,)),
            dma((4, 2)),
            dma((4,)),
            dma((2, 4)),
            dma((2,)),
            dma((3, 2)),
            dma((6, 2)),
            dma((3, 2)),
            dma((6, 2)),
            dma((4, 2, 3)),
            dma((4, 2, 3)),
        ],
        compiler_params=pltpu.CompilerParams(
            collective_id=2, has_side_effects=True, vmem_limit_bytes=62 * 1024 * 1024
        ),
        name="backward",
    )(
        order,
        ids,
        *arrays,
    )


def by_heads(
    tokens,
    positions,
    gain_one,
    gain_two,
    w_query,
    w_key,
    w_value,
    w_out,
    w_gate,
    w_up,
    w_down,
    cotangent,
):
    rows, _, width = tokens.shape
    share = gain_one.shape[0]
    run_ids = positions[::RUN, 0] // RUN
    flat_in = tokens.reshape(rows, width)
    (
        near,
        far,
        normed,
        q_sorted,
        k_sorted,
        v_sorted,
        mixed_t,
        lse,
        mixed_low,
        middle,
        second,
        right,
        gains,
        tables,
        order,
        ids,
    ) = forward(
        flat_in,
        positions.reshape(1, rows),
        jnp.broadcast_to(jnp.pad(run_ids, (0, WIDE - rows // RUN)), (8, WIDE)),
        gain_one.reshape(1, share),
        gain_two.reshape(1, share),
        w_query,
        w_key,
        w_value,
        w_out.T,
        w_gate,
        w_up,
        w_down.T,
        cotangent.reshape(rows, width),
    )
    input_grad, layer_out, grads = backward(
        order,
        ids,
        q_sorted,
        k_sorted,
        v_sorted,
        mixed_t,
        lse,
        cotangent.reshape(rows, width),
        second,
        normed,
        right,
        mixed_low,
        middle,
        near,
        far,
        flat_in,
        gains,
        tables,
    )
    splits, start = [], 0
    for wide in (
        w_gate.shape[1],
        w_up.shape[1],
        w_down.shape[0],
        w_query.shape[1],
        w_key.shape[1],
        w_value.shape[1],
        w_out.shape[0],
        4,
    ):
        splits.append(grads[:, start : start + wide])
        start += wide
    grad_gate, grad_up, grad_down, grad_query, grad_key, grad_value, grad_out, grad_gains = splits
    return (
        layer_out.reshape(rows, 1, width),
        input_grad,
        grad_gains[:, 0] + grad_gains[:, 2],
        grad_gains[:, 1] + grad_gains[:, 3],
        grad_query,
        grad_key,
        grad_value,
        grad_out.T,
        grad_gate,
        grad_up,
        grad_down.T,
    )


def solution(mesh):
    sizes = (mesh.shape["dp"], mesh.shape["context"], mesh.shape["tensor"])
    return jax.shard_map(
        by_heads if sizes == (2, 8, 2) else on_device,
        mesh=mesh,
        in_specs=(
            P("context", "dp", None),
            P("context", "dp"),
            P(("dp", "context")),
            P(("dp", "context")),
            P(("dp", "context"), "tensor"),
            P(("dp", "context"), "tensor"),
            P(("dp", "context"), "tensor"),
            P("tensor", ("dp", "context")),
            P(("dp", "context"), "tensor"),
            P(("dp", "context"), "tensor"),
            P("tensor", ("dp", "context")),
            P("context", "dp", None),
        ),
        out_specs=(
            P("context", "dp", None),
            P("context", "dp", None),
            P(("dp", "context")),
            P(("dp", "context")),
            P(("dp", "context"), "tensor"),
            P(("dp", "context"), "tensor"),
            P(("dp", "context"), "tensor"),
            P("tensor", ("dp", "context")),
            P(("dp", "context"), "tensor"),
            P(("dp", "context"), "tensor"),
            P("tensor", ("dp", "context")),
        ),
        check_vma=False,
    )
```

```python
import functools
import types

import jax
import jax.numpy as jnp
from jax import lax
from jax.experimental import pallas as pl
from jax.experimental.pallas import tpu as pltpu
from jax.sharding import PartitionSpec as P

HEAD = 96


epsilon = 1e-05
theta_base = 100000.0
masked_value = -1e30


def norm_forward(values_in, gain_vec):
    inverse = lax.rsqrt(jnp.mean(values_in * values_in, axis=-1, keepdims=True) + epsilon)
    unit_vals = values_in * inverse
    return (unit_vals, inverse, (unit_vals * gain_vec.astype(jnp.float32)).astype(jnp.bfloat16))


def norm_backward(grad_in, unit_vals, inverse, gain_vec):
    scaled = grad_in * gain_vec.astype(jnp.float32)
    grad_vals = inverse * (
        scaled - unit_vals * jnp.mean(scaled * unit_vals, axis=-1, keepdims=True)
    )
    return (grad_vals, jnp.sum(grad_in * unit_vals, axis=0))


def rotate(values_in, cos_part, sin_part):
    half_size = values_in.shape[-1] // 2
    front_half = values_in[..., :half_size]
    back_half = values_in[..., half_size:]
    return jnp.concatenate(
        [
            front_half * cos_part - back_half * sin_part,
            back_half * cos_part + front_half * sin_part,
        ],
        axis=-1,
    )


def contract_rows(left_mat, right_mat):
    return lax.dot_general(
        left_mat, right_mat, (((0,), (0,)), ((), ())), preferred_element_type=jnp.float32
    )


def contract_cols(left_mat, right_mat):
    return lax.dot_general(
        left_mat, right_mat, (((1,), (1,)), ((), ())), preferred_element_type=jnp.float32
    )


def on_device(
    tokens,
    positions,
    gain_one,
    gain_two,
    w_query,
    w_key,
    w_value,
    w_out,
    w_gate,
    w_up,
    w_down,
    cotangent,
):
    slot_count, seq_count, model_width = tokens.shape
    row_count = slot_count * seq_count
    gathered = (
        lax.all_gather(gain_one, ("dp", "context"), axis=0, tiled=True),
        lax.all_gather(gain_two, ("dp", "context"), axis=0, tiled=True),
        lax.all_gather(w_query, ("dp", "context"), axis=0, tiled=True),
        lax.all_gather(w_key, ("dp", "context"), axis=0, tiled=True),
        lax.all_gather(w_value, ("dp", "context"), axis=0, tiled=True),
        lax.all_gather(w_out, ("dp", "context"), axis=1, tiled=True),
        lax.all_gather(w_gate, ("dp", "context"), axis=0, tiled=True),
        lax.all_gather(w_up, ("dp", "context"), axis=0, tiled=True),
        lax.all_gather(w_down, ("dp", "context"), axis=1, tiled=True),
    )
    full_one, full_two, query_mat, key_mat, value_mat, out_mat, gate_mat, up_mat, down_mat = (
        gathered
    )
    heads_kv = key_mat.shape[1] // HEAD
    heads_q = query_mat.shape[1] // HEAD
    group_size = heads_q // heads_kv
    score_scale = HEAD ** (-0.5)
    half_size = HEAD // 2
    inv_freqs = theta_base ** (-2.0 * jnp.arange(half_size, dtype=jnp.float32) / HEAD)
    angles = positions.astype(jnp.float32)[:, :, None] * inv_freqs
    cos_part = jnp.cos(angles)[:, :, None, :]
    sin_part = jnp.sin(angles)[:, :, None, :]
    flat_in = tokens.astype(jnp.float32).reshape(row_count, model_width)
    unit_one, inverse_one, normed = norm_forward(flat_in, full_one)
    query_proj = jnp.dot(normed, query_mat, preferred_element_type=jnp.float32).reshape(
        slot_count, seq_count, heads_q, HEAD
    )
    key_proj = jnp.dot(normed, key_mat, preferred_element_type=jnp.float32).reshape(
        slot_count, seq_count, heads_kv, HEAD
    )
    value_low = (
        jnp.dot(normed, value_mat, preferred_element_type=jnp.float32)
        .astype(jnp.bfloat16)
        .reshape(slot_count, seq_count, heads_kv * HEAD)
    )
    queries = rotate(query_proj, cos_part, sin_part).astype(jnp.bfloat16)
    keys_low = (
        rotate(key_proj, cos_part, sin_part)
        .astype(jnp.bfloat16)
        .reshape(slot_count, seq_count, heads_kv * HEAD)
    )
    query_seq = jnp.transpose(
        queries.reshape(slot_count, seq_count, heads_kv, group_size, HEAD), (1, 2, 3, 0, 4)
    )
    query_pos = positions.T
    stat_shape = (seq_count, heads_kv, group_size, slot_count)
    initial = (
        jnp.full(stat_shape, masked_value, jnp.float32),
        jnp.zeros(stat_shape, jnp.float32),
        jnp.zeros(stat_shape + (HEAD,), jnp.float32),
    )
    key_piece = lax.all_gather(keys_low, "context", axis=0, tiled=True)
    value_piece = lax.all_gather(value_low, "context", axis=0, tiled=True)
    pos_piece = lax.all_gather(positions, "context", axis=0, tiled=True)
    piece_len = key_piece.shape[0]
    key_seq = jnp.transpose(key_piece.reshape(piece_len, seq_count, heads_kv, HEAD), (1, 2, 0, 3))
    value_seq = jnp.transpose(
        value_piece.reshape(piece_len, seq_count, heads_kv, HEAD), (1, 2, 0, 3)
    )
    pos_seq = pos_piece.T

    def per_sequence(seq_items):
        peak_val, totals, accum_vals, query_one, qpos_one, key_one, value_one, kpos_one = seq_items
        raw_scores = (
            jnp.einsum("hgqd,hkd->hgqk", query_one, key_one, preferred_element_type=jnp.float32)
            * score_scale
        )
        allowed = kpos_one[None, None, None, :] <= qpos_one[None, None, :, None]
        masked = jnp.where(allowed, raw_scores, masked_value)
        new_peak = jnp.maximum(peak_val, jnp.max(masked, axis=-1))
        decay_vals = jnp.exp(peak_val - new_peak)
        weights = jnp.where(allowed, jnp.exp(masked - new_peak[..., None]), 0.0)
        totals = totals * decay_vals + jnp.sum(weights, axis=-1)
        accum_vals = accum_vals * decay_vals[..., None] + jnp.einsum(
            "hgqk,hkd->hgqd",
            weights.astype(jnp.bfloat16),
            value_one,
            preferred_element_type=jnp.float32,
        )
        return (new_peak, totals, accum_vals)

    peak_val, totals, accum_vals = lax.map(
        per_sequence,
        (initial[0], initial[1], initial[2], query_seq, query_pos, key_seq, value_seq, pos_seq),
    )
    log_total = peak_val + jnp.log(totals)
    mixed_seq = accum_vals / totals[..., None]
    mixed_low = (
        jnp.transpose(mixed_seq, (3, 0, 1, 2, 4))
        .reshape(row_count, heads_q * HEAD)
        .astype(jnp.bfloat16)
    )
    branch = lax.psum(
        jnp.dot(mixed_low, out_mat, preferred_element_type=jnp.float32).astype(jnp.bfloat16),
        "tensor",
    ).astype(jnp.float32)
    middle = flat_in + branch
    unit_two, inverse_two, second = norm_forward(middle, full_two)
    gate_vals = jnp.dot(second, gate_mat, preferred_element_type=jnp.float32)
    up_vals = jnp.dot(second, up_mat, preferred_element_type=jnp.float32)
    sigmoid_vals = jax.nn.sigmoid(gate_vals)
    silu_vals = gate_vals * sigmoid_vals
    hidden = (silu_vals * up_vals).astype(jnp.bfloat16)
    mlp_part = lax.psum(
        jnp.dot(hidden, down_mat, preferred_element_type=jnp.float32).astype(jnp.bfloat16), "tensor"
    ).astype(jnp.float32)
    layer_out = (middle + mlp_part).astype(jnp.bfloat16).reshape(slot_count, seq_count, model_width)
    regathered = (
        lax.all_gather(gain_one, ("dp", "context"), axis=0, tiled=True),
        lax.all_gather(gain_two, ("dp", "context"), axis=0, tiled=True),
        lax.all_gather(w_query, ("dp", "context"), axis=0, tiled=True),
        lax.all_gather(w_key, ("dp", "context"), axis=0, tiled=True),
        lax.all_gather(w_value, ("dp", "context"), axis=0, tiled=True),
        lax.all_gather(w_out, ("dp", "context"), axis=1, tiled=True),
        lax.all_gather(w_gate, ("dp", "context"), axis=0, tiled=True),
        lax.all_gather(w_up, ("dp", "context"), axis=0, tiled=True),
        lax.all_gather(w_down, ("dp", "context"), axis=1, tiled=True),
    )
    full_one, full_two, query_mat, key_mat, value_mat, out_mat, gate_mat, up_mat, down_mat = (
        regathered
    )
    grad_low = cotangent.reshape(row_count, model_width)
    grad_down = contract_rows(hidden, grad_low)
    grad_hidden = contract_cols(grad_low, down_mat)
    grad_gate_low = (
        grad_hidden * up_vals * sigmoid_vals * (1.0 + gate_vals * (1.0 - sigmoid_vals))
    ).astype(jnp.bfloat16)
    grad_up_low = (grad_hidden * silu_vals).astype(jnp.bfloat16)
    grad_gate = contract_rows(second, grad_gate_low)
    grad_up = contract_rows(second, grad_up_low)
    grad_second = lax.psum(
        (contract_cols(grad_gate_low, gate_mat) + contract_cols(grad_up_low, up_mat)).astype(
            jnp.bfloat16
        ),
        "tensor",
    ).astype(jnp.float32)
    grad_mid_norm, grad_gain_two = norm_backward(grad_second, unit_two, inverse_two, full_two)
    grad_middle = grad_low.astype(jnp.float32) + grad_mid_norm
    grad_mid_low = grad_middle.astype(jnp.bfloat16)
    grad_out = contract_rows(mixed_low, grad_mid_low)
    grad_mixed = contract_cols(grad_mid_low, out_mat).astype(jnp.bfloat16)
    grad_mixed_seq = jnp.transpose(
        grad_mixed.reshape(slot_count, seq_count, heads_kv, group_size, HEAD), (1, 2, 3, 0, 4)
    )
    delta_rows = jnp.sum(grad_mixed_seq.astype(jnp.float32) * mixed_seq, axis=-1)
    kv_width = heads_kv * HEAD

    def block_grads(grad_query_acc, key_blk, value_blk, pos_blk):
        block_len = key_blk.shape[0]
        key_seq = jnp.transpose(key_blk.reshape(block_len, seq_count, heads_kv, HEAD), (1, 2, 0, 3))
        value_seq = jnp.transpose(
            value_blk.reshape(block_len, seq_count, heads_kv, HEAD), (1, 2, 0, 3)
        )
        raw_scores = (
            jnp.einsum("shgqd,shkd->shgqk", query_seq, key_seq, preferred_element_type=jnp.float32)
            * score_scale
        )
        allowed = pos_blk.T[:, None, None, None, :] <= query_pos[:, None, None, :, None]
        prob_vals = jnp.where(
            allowed,
            jnp.exp(jnp.where(allowed, raw_scores - log_total[..., None], masked_value)),
            0.0,
        )
        grad_value_blk = jnp.einsum(
            "shgqk,shgqd->kshd",
            prob_vals.astype(jnp.bfloat16),
            grad_mixed_seq,
            preferred_element_type=jnp.float32,
        )
        grad_probs = jnp.einsum(
            "shgqd,shkd->shgqk", grad_mixed_seq, value_seq, preferred_element_type=jnp.float32
        )
        grad_scores = (prob_vals * (grad_probs - delta_rows[..., None])).astype(jnp.bfloat16)
        grad_query_acc = grad_query_acc + jnp.einsum(
            "shgqk,shkd->shgqd", grad_scores, key_seq, preferred_element_type=jnp.float32
        )
        grad_key_blk = jnp.einsum(
            "shgqk,shgqd->kshd", grad_scores, query_seq, preferred_element_type=jnp.float32
        )
        return (
            grad_query_acc,
            grad_key_blk.reshape(block_len, seq_count, kv_width),
            grad_value_blk.reshape(block_len, seq_count, kv_width),
        )

    zero_query = jnp.zeros(stat_shape + (HEAD,), jnp.float32)
    key_all, value_all, pos_all = (
        lax.all_gather(keys_low, "context", axis=0, tiled=True),
        lax.all_gather(value_low, "context", axis=0, tiled=True),
        lax.all_gather(positions, "context", axis=0, tiled=True),
    )
    total_len = key_all.shape[0]
    block_size = min(512, total_len)
    block_count = total_len // block_size

    def key_block(grad_query_acc, block_items):
        key_blk, value_blk, pos_blk = block_items
        grad_query_acc, grad_key_blk, grad_value_blk = block_grads(
            grad_query_acc, key_blk, value_blk, pos_blk
        )
        return (grad_query_acc, (grad_key_blk, grad_value_blk))

    grad_query_acc, (grad_keys_all, grad_values_all) = lax.scan(
        key_block,
        zero_query,
        (
            key_all.reshape(block_count, block_size, seq_count, kv_width),
            value_all.reshape(block_count, block_size, seq_count, kv_width),
            pos_all.reshape(block_count, block_size, seq_count),
        ),
    )
    grad_key_own, grad_value_own = (
        lax.psum_scatter(
            grad_keys_all.reshape(total_len, seq_count, kv_width).astype(jnp.bfloat16),
            "context",
            scatter_dimension=0,
            tiled=True,
        ).astype(jnp.float32),
        lax.psum_scatter(
            grad_values_all.reshape(total_len, seq_count, kv_width).astype(jnp.bfloat16),
            "context",
            scatter_dimension=0,
            tiled=True,
        ).astype(jnp.float32),
    )
    grad_rot_q = jnp.transpose(grad_query_acc * score_scale, (3, 0, 1, 2, 4)).reshape(
        slot_count, seq_count, heads_q, HEAD
    )
    grad_q_low = (
        rotate(grad_rot_q, cos_part, -sin_part)
        .reshape(row_count, heads_q * HEAD)
        .astype(jnp.bfloat16)
    )
    grad_rot_k = (grad_key_own * score_scale).reshape(slot_count, seq_count, heads_kv, HEAD)
    grad_k_low = (
        rotate(grad_rot_k, cos_part, -sin_part).reshape(row_count, kv_width).astype(jnp.bfloat16)
    )
    grad_v_low = grad_value_own.reshape(row_count, kv_width).astype(jnp.bfloat16)
    grad_query = contract_rows(normed, grad_q_low)
    grad_key = contract_rows(normed, grad_k_low)
    grad_value = contract_rows(normed, grad_v_low)
    grad_normed = lax.psum(
        (
            contract_cols(grad_q_low, query_mat)
            + contract_cols(grad_k_low, key_mat)
            + contract_cols(grad_v_low, value_mat)
        ).astype(jnp.bfloat16),
        "tensor",
    ).astype(jnp.float32)
    grad_in_norm, grad_gain_one = norm_backward(grad_normed, unit_one, inverse_one, full_one)
    input_grad = (grad_middle + grad_in_norm).reshape(slot_count, seq_count, model_width)
    reduced = (
        lax.psum_scatter(grad_gain_one, ("dp", "context"), scatter_dimension=0, tiled=True),
        lax.psum_scatter(grad_gain_two, ("dp", "context"), scatter_dimension=0, tiled=True),
        lax.psum_scatter(grad_query, ("dp", "context"), scatter_dimension=0, tiled=True),
        lax.psum_scatter(grad_key, ("dp", "context"), scatter_dimension=0, tiled=True),
        lax.psum_scatter(grad_value, ("dp", "context"), scatter_dimension=0, tiled=True),
        lax.psum_scatter(grad_out, ("dp", "context"), scatter_dimension=1, tiled=True),
        lax.psum_scatter(grad_gate, ("dp", "context"), scatter_dimension=0, tiled=True),
        lax.psum_scatter(grad_up, ("dp", "context"), scatter_dimension=0, tiled=True),
        lax.psum_scatter(grad_down, ("dp", "context"), scatter_dimension=1, tiled=True),
    )
    return (
        layer_out,
        input_grad,
        reduced[0],
        reduced[1],
        reduced[2],
        reduced[3],
        reduced[4],
        reduced[5],
        reduced[6],
        reduced[7],
        reduced[8],
    )


WIDE = 128
HALF = HEAD // 2
RUN = 256
TILE = 512
LOG2_E = 1.4426950408889634
MESH = pl.DeviceIdType.MESH
PIECE = 256
FEED = 512
VMEM_LIMIT = 56 * 1024 * 1024


def any_spec():
    return pl.BlockSpec(memory_space=pl.ANY)


def vmem_spec():
    return pl.BlockSpec(memory_space=pltpu.VMEM)


def place():
    return lax.axis_index("dp"), lax.axis_index("context"), lax.axis_index("tensor")


def greet(devices):
    barrier = pltpu.get_barrier_semaphore()
    for device in devices:
        pl.semaphore_signal(barrier, inc=1, device_id=device, device_id_type=MESH)
    pl.semaphore_wait(barrier, len(devices))


def sequence_others():
    row, spot, core = place()
    return [
        (row, lax.rem(spot + shift, 8), lax.rem(core + flip, 2))
        for shift in range(8)
        for flip in range(2)
        if shift or flip
    ]


def dot_f32(left, right):
    return jnp.dot(left, right, preferred_element_type=jnp.float32)


def own_shard():
    row, spot, core = place()
    return row * 8 + spot


def group_others():
    row, spot, core = place()
    return sequence_others() + [(1 - row, lax.rem(spot + shift, 8), core) for shift in range(8)]


def exchange_messages(message_to, landing, send, recv):
    row, spot, core = place()
    copies, waits = [], []

    def one(flip, shift):
        at = flip * 8 + shift
        to_row = lax.rem(row + flip, 2)
        chip, source = lax.rem(spot + shift, 8), lax.rem(spot + 8 - shift, 8)
        device = (to_row, chip, core)
        message = message_to(to_row * 8 + chip)
        copies.append(
            remote(message, landing.at[row * 8 + spot], send.at[at], recv.at[at], device)
        )
        came = landing.at[to_row * 8 + source]
        waits.append(remote(came, came, send.at[at], recv.at[at], device).wait_recv)

    for flip in range(2):
        for shift in range(8):
            if flip or shift:
                one(flip, shift)
    return copies, waits


def turn_left(left_t, index, source):
    quarter = source.shape[1] // 4
    share = quarter // 4
    for piece in range(4):
        turned = source[:, piece * quarter : (piece + 1) * quarter].T
        for inner in range(4):
            x, z, y = piece // 2, 2 * (piece % 2) + inner // 2, inner % 2
            left_t[index, x, y, z * share : (z + 1) * share] = turned[
                inner * share : (inner + 1) * share
            ]


def remote(source, target, send, recv, device):
    return pltpu.make_async_remote_copy(
        src_ref=source,
        dst_ref=target,
        send_sem=send,
        recv_sem=recv,
        device_id=device,
        device_id_type=MESH,
    )


def move(source, target, send, recv, device, is_self):
    @pl.when(is_self)
    def _():
        pltpu.make_async_copy(source, target, recv).start()

    @pl.when(jnp.logical_not(is_self))
    def _():
        remote(source, target, send, recv, device).start()


def return_copies(ref, out, send, recv):
    row, spot, core = place()
    head = 2 * lax.rem(spot, 4) + core
    owner = spot // 4
    copies = []
    for step in range(8):
        chip = lax.rem(spot + step, 8)
        is_self = (owner == core) if step == 0 else False
        parts = (ref.at[chip], out.at[head], send.at[step], recv.at[head], (row, chip, owner))
        copies.append((parts, is_self))
    return copies


def start_return(copies):
    for parts, is_self in copies:
        if is_self is False:
            remote(*parts).start()
        else:
            move(*parts, is_self)


def finish_return(copies, out, send, recv):
    row, spot, core = place()
    for head in range(8):
        remote(
            out.at[head], out.at[head], send.at[0], recv.at[head], (row, spot, 1 - core)
        ).wait_recv()
    for parts, is_self in copies:
        if is_self is False:
            remote(*parts).wait_send()
        else:

            @pl.when(jnp.logical_not(is_self))
            def _():
                remote(*parts).wait_send()


def tile_at(index, size):
    return pl.ds(pl.multiple_of(index * size, size), size)


def causal(scores):
    keys = lax.broadcasted_iota(jnp.int32, scores.shape, 0)
    queries = lax.broadcasted_iota(jnp.int32, scores.shape, 1)
    return jnp.where(keys <= queries, scores, masked_value)


def neighbours():
    row, spot, core = place()
    level, column = spot // 2, lax.rem(spot, 2)
    beside_x = (1 - row, spot, core)
    beside_y = (row, 2 * level + 1 - column, core)
    along_z = [(row, 2 * lax.rem(level + k, 4) + column, core) for k in (1, 2, 3)]
    return row, level, column, beside_x, beside_y, along_z


class Gather:
    def __init__(self, own, whole, start, width, piece, sems):
        self.own, self.whole = own.at[:, pl.ds(start, width)], whole
        self.start, self.width = start, width
        names = ("send_z", "recv_z", "send_x", "recv_x", "send_y", "recv_y", "send_d", "recv_d")
        for name, sem in zip(names + ("local",), sems):
            setattr(self, name, sem.at[piece])

    def block(self, x, z, y, half=None):
        cut = self.width * 7 // 12 // WIDE * WIDE
        start, width = self.start, self.width
        if half == 0:
            width = cut
        elif half == 1:
            start, width = start + cut, width - cut
        return self.whole.at[x, z, y, :, pl.ds(start, width)]

    def arrived(self, target, recv_sem):
        device = neighbours()[3]
        remote(target, target, self.send_x.at[0], recv_sem, device).wait_recv()

    def copy_z(self, z, up, own=False):
        row, level, column, beside_x, beside_y = neighbours()[:5]
        core = place()[2]
        target = level + 1 if up else level - 1
        block = self.block(row, z, column)
        return remote(
            self.own if own else block,
            block,
            self.send_z.at[int(up), z],
            self.recv_z.at[z],
            (row, 2 * target + column, core),
        )

    def copies_xy(self, z, own=False):
        row, level, column, beside_x, beside_y = neighbours()[:5]
        block = self.block(row, z, column)
        source = self.own if own else block
        return [
            remote(source, block, self.send_x.at[z], self.recv_x.at[z], beside_x),
            remote(source, block, self.send_y.at[z], self.recv_y.at[z], beside_y),
        ]

    def copies_diagonal(self, z):
        row, level, column, beside_x, beside_y = neighbours()[:5]
        by_y = self.block(1 - row, z, column, 1)
        by_x = self.block(row, z, 1 - column, 0)
        return [
            remote(by_y, by_y, self.send_d.at[0, z], self.recv_d.at[0, z], beside_y),
            remote(by_x, by_x, self.send_d.at[1, z], self.recv_d.at[1, z], beside_x),
        ]

    def own_copy(self):
        row, level, column = neighbours()[:3]
        return pltpu.make_async_copy(self.own, self.block(row, level, column), self.local)

    def each_at(self, hop, act):
        level = neighbours()[1]

        @pl.when(level >= hop)
        def _():
            act(level - hop, True)

        @pl.when(level + hop <= 3)
        def _():
            act(level + hop, False)

    def start_z(self, z, up, own=False):
        level = neighbours()[1]

        @pl.when(level < 3 if up else level > 0)
        def _():
            self.copy_z(z, up, own).start()

    def place_own(self):
        self.own_copy().start()

    def open(self):
        level = neighbours()[1]
        self.start_z(level, True, True)
        self.start_z(level, False, True)
        for copy in self.copies_xy(level, True):
            copy.start()

    def hop(self, hop):
        def act(z, up):
            row, level, column = neighbours()[:3]
            self.arrived(self.block(row, z, column), self.recv_z.at[z])
            self.start_z(z, up)
            for copy in self.copies_xy(z):
                copy.start()

        self.each_at(hop, act)

    def turn_diagonal(self, z):
        row, level, column = neighbours()[:3]
        by_y, by_x = self.copies_diagonal(z)
        self.arrived(self.block(1 - row, z, column), self.recv_x.at[z])
        by_y.start()
        self.arrived(self.block(row, z, 1 - column), self.recv_y.at[z])
        by_x.start()

    def diagonal(self, hop):
        if hop == 0:
            self.turn_diagonal(neighbours()[1])
        else:
            self.each_at(hop, lambda z, up: self.turn_diagonal(z))

    def finish(self):
        row, level, column = neighbours()[:3]
        self.own_copy().wait()
        for z in range(4):
            self.arrived(self.block(1 - row, z, 1 - column, 1), self.recv_d.at[0, z])
            self.arrived(self.block(1 - row, z, 1 - column, 0), self.recv_d.at[1, z])

    def close(self):
        level = neighbours()[1]

        def sent(z, up):
            @pl.when(level < 3 if up else level > 0)
            def _():
                self.copy_z(z, up).wait_send()

        sent(level, True)
        sent(level, False)
        for hop in range(1, 4):
            self.each_at(hop, sent)
        for z in range(4):
            for copy in self.copies_xy(z) + self.copies_diagonal(z):
                copy.wait_send()


def gather_sems(pieces):
    dma = pltpu.SemaphoreType.DMA
    shapes = [(2, 4), (4,), (4,), (4,), (4,), (4,), (2, 4), (2, 4), ()]
    return [dma((pieces,) + shape) for shape in shapes]


AT_BEGIN, AT_GROUP, AT_HEADS, AT_KEYS, AT_RETURN, AT_OUT, AT_NORM, AT_TILE, AT_FEED = 0, 1, 5, 6, 7, 8, 9, 10, 18
PUMPS = {
    AT_BEGIN: (4, 1, 2, 3, 5, 6, 7, 10, 11, 12, 20, 13),
    AT_GROUP + 0: (21,),
    AT_GROUP + 2: (30,),
    AT_GROUP + 3: (16, 24, 14),
    AT_HEADS: (22, 17, 15, 25, 23),
    AT_KEYS: (40,),
    AT_TILE + 0: (31,),
    AT_TILE + 1: (27,),
    AT_TILE + 2: (26,),
    AT_TILE + 3: (32,),
    AT_TILE + 5: (33,),
    AT_TILE + 6: (34, 41),
    AT_TILE + 7: (44,),
    AT_RETURN: (35, 42, 37, 36, 50, 45, 43),
    AT_OUT: (46, 51),
    AT_NORM: (54,),
    AT_FEED + 1: (47, 52, 55),
    AT_FEED + 3: (53,),
    AT_FEED + 5: (56, 57),
}


def forward_kernel(
    tokens,
    positions,
    freqs,
    ids_in,
    gain_one,
    gain_two,
    w_query,
    w_key,
    w_value,
    w_out_t,
    w_gate,
    w_up,
    w_down_t,
    cotangent,
    near,
    far,
    normed_out,
    q_out,
    k_out,
    v_out,
    mixed_t_out,
    lse_out,
    mixed_low_out,
    middle_out,
    second_out,
    right_out,
    gains_out,
    tables_out,
    left_out,
    order,
    ids_flat,
    near_own,
    far_own,
    unit,
    normed,
    tables,
    weight,
    gain_message,
    gain_all,
    gain_columns,
    gain_rows,
    left_t,
    q_heads,
    kv_heads,
    q_slots,
    kv_slots,
    q_t,
    keys,
    v_t,
    mixed_t,
    lse,
    mixed,
    mixed_slots,
    mixed_heads,
    mixed_low,
    out_weight,
    part,
    part_other,
    second,
    cot,
    right,
    feed_weight,
    ids_all,
    ids,
    load_own,
    send_ids,
    recv_ids,
    load_ids,
    send_gain,
    recv_gain,
    load_w,
    load_out,
    load_feed,
    load_cot,
    save_right,
    saves,
    send_q,
    recv_q,
    send_kv,
    recv_kv,
    send_x,
    recv_x,
    send_m,
    recv_m,
    send_p,
    recv_p,
    *sems,
):
    row, spot, core = place()
    low, full = jnp.bfloat16, jnp.float32
    rows, width = tokens.shape
    share = near_own.shape[0]
    length = 8 * rows
    runs, tiles = length // RUN, length // TILE
    per_device = rows // RUN
    halves = TILE // RUN
    quarter = 4 * share
    sibling = (row, spot, 1 - core)
    out_width = w_out_t.shape[1]
    qkv_width = 16 * HEAD

    near_loads, far_loads, start = [], [], 0
    for ref in (w_query, w_key, w_value, w_out_t):
        target = near_own.at[:, pl.ds(start, ref.shape[1])]
        near_loads.append(pltpu.make_async_copy(ref, target, load_own.at[len(near_loads)]))
        start += ref.shape[1]
    for index, ref in enumerate((w_gate, w_up, w_down_t)):
        for piece in range(4):
            source = ref.at[:, pl.ds(piece * FEED, FEED)]
            target = far_own.at[:, pl.ds((3 * piece + index) * FEED, FEED)]
            far_loads.append(
                pltpu.make_async_copy(source, target, load_own.at[4 + 4 * index + piece])
            )
    for copy in near_loads + far_loads:
        copy.start()
    load_cotangent = pltpu.make_async_copy(cotangent, cot, load_cot)
    load_cotangent.start()
    first = Gather(near_own, near, 0, qkv_width, 0, sems)
    outer = Gather(near_own, near, qkv_width, out_width, 1, sems)
    feeds = [Gather(far_own, far, 3 * FEED * p, 3 * FEED, 2 + p, sems) for p in range(4)]
    gathers = [first, outer] + feeds

    def pump(place):
        for what in PUMPS.get(place, ()):
            gather, act = gathers[what // 10], what % 10
            if act == 0:
                gather.open()
            elif act < 4:
                gather.hop(act)
            else:
                gather.diagonal(act - 4)

    gain_message[...] = jnp.zeros_like(gain_message)
    gain_message[0:1, :share] = gain_one[...].astype(full)
    gain_message[1:2, :share] = gain_two[...].astype(full)
    for copy in near_loads:
        copy.wait()
    greet(group_others())
    first.open()
    first.place_own()
    outer.place_own()

    gain_copies, gain_from = exchange_messages(
        lambda shard: gain_message, gain_all, send_gain, recv_gain
    )
    for copy in gain_copies:
        copy.start()
    gain_all[own_shard()] = gain_message[...]

    for shift in range(1, 8):
        remote(
            ids_in,
            ids_all.at[spot],
            send_ids.at[shift],
            recv_ids.at[shift],
            (row, lax.rem(spot + shift, 8), core),
        ).start()
    ids_all[spot] = ids_in[...]

    for copy in far_loads:
        copy.wait()
    for gather in feeds:
        gather.place_own()
    chunk = rows // 8

    def unit_block(index, carry):
        cut = tile_at(index, chunk)
        values = tokens[cut].astype(full)
        inverse = lax.rsqrt(jnp.mean(values * values, axis=-1, keepdims=True) + epsilon)
        unit[cut] = values * inverse
        return carry

    lax.fori_loop(0, 8, unit_block, 0)
    angles = freqs[...] * positions[...].astype(full)
    tables[0] = jnp.cos(angles)
    tables[1] = jnp.sin(angles)

    pump(AT_BEGIN)
    for shift in range(1, 8):
        remote(
            ids_in,
            ids_all.at[lax.rem(spot + 8 - shift, 8)],
            send_ids.at[shift],
            recv_ids.at[shift],
            (row, lax.rem(spot + shift, 8), core),
        ).wait_recv()
    pltpu.make_async_copy(ids_all, ids, load_ids).start()
    first.finish()

    def load_group(group):
        lanes = pl.ds(group * 4 * HEAD, 4 * HEAD)
        return pltpu.make_async_copy(
            near.at[:, :, :, :, lanes], weight.at[group % 2], load_w.at[group % 2]
        )

    load_out_weight = pltpu.make_async_copy(
        near.at[:, :, :, :, pl.ds(qkv_width, out_width)], out_weight, load_out
    )
    load_group(0).start()
    load_group(1).start()
    for wait in gain_from:
        wait()
    for shard in range(16):
        gain_columns[shard * share : (shard + 1) * share] = gain_all[shard].T[:share]
    gain_rows[...] = gain_columns[...].T
    normed[...] = (unit[...] * gain_rows[0:1]).astype(low)
    for group in range(4):
        load_group(group).wait()
        proj = dot_f32(normed[...], weight[group % 2].reshape(width, 4 * HEAD)).T
        if group < 2:
            load_group(group + 2).start()
        for head in range(4):
            front = proj[head * HEAD : head * HEAD + HALF]
            back = proj[head * HEAD + HALF : (head + 1) * HEAD]
            if group < 3:
                front, back = (
                    front * tables[0] - back * tables[1],
                    back * tables[0] + front * tables[1],
                )
            for start, value in ((0, front.astype(low)), (HALF, back.astype(low))):
                for run in range(per_device):
                    piece = value[:, run * RUN : (run + 1) * RUN]
                    if group < 2:
                        q_heads[4 * group + head, run, start : start + HALF] = piece
                    else:
                        kv_heads[head, group - 2, run, start : start + HALF] = piece
        pump(AT_GROUP + group)

    outgoing = []
    for step in range(4):
        slot = lax.rem(spot + step, 4)
        chip = 4 * core + slot
        for other in range(2):
            is_self = jnp.logical_and(chip == spot, core == other)
            device = (row, chip, other)
            kv_parts = (
                kv_heads.at[slot, :, other],
                kv_slots.at[spot, :, other],
                send_kv.at[step, other],
                recv_kv.at[spot],
                device,
            )
            q_parts = (
                q_heads.at[2 * slot + other],
                q_slots.at[spot],
                send_q.at[step, other],
                recv_q.at[spot],
                device,
            )
            outgoing.append((kv_parts, is_self))
            outgoing.append((q_parts, is_self))
    for parts, is_self in outgoing:
        move(*parts, is_self)
    pump(AT_HEADS)

    def hand_on(source):
        block = kv_slots.at[source, :, core]
        return remote(block, block, send_x.at[source], recv_x.at[source], sibling)

    for step in range(8):
        source = lax.rem(spot + step, 8)
        block = kv_slots.at[source, :, core]
        remote(block, block, send_x.at[source], recv_kv.at[source], sibling).wait_recv()
        hand_on(source).start()
    pump(AT_KEYS)
    for step in range(8):
        remote(
            q_slots.at[step], q_slots.at[step], send_x.at[step], recv_q.at[step], sibling
        ).wait_recv()
        hand_on(step).wait()

    pltpu.make_async_copy(ids_all, ids, load_ids).wait()

    def find_run(index, carry):
        device, piece = 0, 0
        for run in range(runs):
            here = ids[run // per_device, 0, run % per_device] == index
            device = jnp.where(here, run // per_device, device)
            piece = jnp.where(here, run % per_device, piece)
        order[index, 0] = device
        order[index, 1] = piece
        found = ids[index // per_device, 0, index % per_device]
        order[runs + index, 0] = lax.div(found, per_device)
        order[runs + index, 1] = lax.rem(found, per_device)
        ids_flat[index] = found
        return carry

    lax.fori_loop(0, runs, find_run, 0)

    def sort_run(index, carry):
        device, piece = order[index, 0], order[index, 1]
        cols = tile_at(index, RUN)
        q_t[:, cols] = q_slots[device, piece]
        keys[index] = kv_slots[device, 0, piece].T
        v_t[:, cols] = kv_slots[device, 1, piece]
        return carry

    lax.fori_loop(0, runs, sort_run, 0)
    scale = HEAD ** (-0.5) * LOG2_E

    def query_tile(index, carry):
        cols = tile_at(index, TILE)
        queries = q_t[:, cols]

        def step(scores, block, peak, total, mix):
            high = jnp.maximum(peak, jnp.max(scores, axis=0, keepdims=True))
            decay = jnp.exp2(peak - high)
            weights = jnp.exp2(scores - high)
            total = total * decay + jnp.sum(weights, axis=0, keepdims=True)
            mix = mix * decay + dot_f32(v_t[:, tile_at(block, TILE)], weights.astype(low))
            return high, total, mix

        def scores_of(block):
            held = keys[pl.ds(block * halves, halves)].reshape(TILE, HEAD)
            return dot_f32(held, queries) * scale

        state = (
            jnp.full((1, TILE), masked_value, full),
            jnp.zeros((1, TILE), full),
            jnp.zeros((HEAD, TILE), full),
        )
        state = step(causal(scores_of(index)), index, *state)
        peak, total, mix = lax.fori_loop(
            0, index, lambda block, now: step(scores_of(block), block, *now), state
        )
        mix = mix / total
        mixed_t[:, cols] = mix
        lse[:, cols] = peak + jnp.log2(total)
        for half in range(halves):
            mixed[index * halves + half] = mix[:, half * RUN : (half + 1) * RUN].astype(low)

        for tile in range(tiles):

            @pl.when(index == tile)
            def _():
                pump(AT_TILE + tile)

        return carry

    lax.fori_loop(0, tiles, query_tile, 0)

    def unsort_run(run, carry):
        index = ids[run // per_device, 0, run % per_device]
        mixed_slots[run // per_device, run % per_device] = mixed[index]
        return carry

    lax.fori_loop(0, runs, unsort_run, 0)
    copies = return_copies(mixed_slots, mixed_heads, send_m, recv_m)
    start_return(copies)
    early_saves = [
        pltpu.make_async_copy(source, target, saves.at[index])
        for index, (source, target) in enumerate(
            [
                (normed, normed_out),
                (q_t, q_out),
                (keys, k_out),
                (v_t, v_out),
                (mixed_t, mixed_t_out),
                (lse, lse_out),
                (gain_rows, gains_out),
                (tables, tables_out),
            ]
        )
    ]
    for copy in early_saves:
        copy.start()
    pump(AT_RETURN)
    outer.finish()
    load_out_weight.start()
    finish_return(copies, mixed_heads, send_m, recv_m)

    load_out_weight.wait()
    for run in range(per_device):
        side = mixed_heads[:, run].reshape(8 * HEAD, RUN)
        mixed_low[run * RUN : (run + 1) * RUN] = side.T

    def pair_copy(index):
        cut = pl.ds(index * quarter, quarter)
        return remote(
            part.at[:, cut], part_other.at[:, cut], send_p.at[index], recv_p.at[index], sibling
        )

    for index in range(4):
        block = out_weight[index // 2, 2 * (index % 2) : 2 * (index % 2) + 2]
        term = contract_cols(mixed_low[...], block.reshape(quarter, out_width))
        part[:, index * quarter : (index + 1) * quarter] = term.astype(low)
        pair_copy(index).start()
    pump(AT_OUT)
    load_cotangent.wait()
    for index in range(4):
        pair_copy(index).wait()
    chunk = rows // 8

    def norm_block(index, carry):
        cut = tile_at(index, chunk)
        sums = part[cut].astype(full) + part_other[cut].astype(full)
        values = tokens[cut].astype(full) + sums
        unit[cut] = values
        inverse = lax.rsqrt(jnp.mean(values * values, axis=-1, keepdims=True) + epsilon)
        second[cut] = (values * inverse * gain_rows[1:2]).astype(low)
        return carry

    lax.fori_loop(0, 8, norm_block, 0)
    late_saves = [
        pltpu.make_async_copy(source, target, saves.at[8 + index])
        for index, (source, target) in enumerate(
            [(mixed_low, mixed_low_out), (unit, middle_out), (second, second_out)]
        )
    ]
    for copy in late_saves:
        copy.start()
    pump(AT_NORM)

    def load_feed_weight(index, kind):
        piece, half = index // 2, lax.rem(index, 2)
        start = (3 * piece + kind) * FEED + half * PIECE
        lanes = pl.ds(pl.multiple_of(start, PIECE), PIECE)
        return pltpu.make_async_copy(
            far.at[:, :, :, :, lanes], feed_weight.at[half, kind], load_feed.at[half, kind]
        )

    def save_piece(piece):
        lanes = pl.ds(piece * 3 * FEED, 3 * FEED)
        return pltpu.make_async_copy(
            right.at[:, lanes], right_out.at[:, lanes], save_right.at[piece]
        )

    def feed_block(index, carry):
        piece, half = index // 2, lax.rem(index, 2)
        for when in range(4):

            @pl.when(index == 2 * when)
            def _():
                feeds[when].finish()

        @pl.when(half == 0)
        def _():
            for offset in range(2):
                for kind in range(3):
                    load_feed_weight(index + offset, kind).start()

        values = []
        for kind, left in enumerate((second, second, cot)):
            load_feed_weight(index, kind).wait()
            values.append(dot_f32(left[...], feed_weight[half, kind].reshape(width, PIECE)))
        gate, up, grad_hidden = values
        sigmoid = jax.nn.sigmoid(gate)
        silu = gate * sigmoid
        grad_gate = grad_hidden * up * sigmoid * (1.0 + gate * (1.0 - sigmoid))
        for when, source in ((1, second), (3, cot)):

            @pl.when(index == when)
            def _():
                turn_left(left_t, when % 3, source)

        for kind, value in enumerate((grad_gate, grad_hidden * silu, silu * up)):
            start = (3 * piece + kind) * FEED + half * PIECE
            right[:, pl.ds(pl.multiple_of(start, PIECE), PIECE)] = value.astype(low)

        for when in range(8):

            @pl.when(index == when)
            def _():
                pump(AT_FEED + when)

        for when in range(4):

            @pl.when(index == 2 * when + 1)
            def _():
                save_piece(when).start()

        return carry

    lax.fori_loop(0, 8, feed_block, 0)
    save_left = pltpu.make_async_copy(left_t, left_out, saves.at[11])
    save_left.start()
    for gather in gathers:
        gather.close()
    for parts, is_self in outgoing:

        @pl.when(jnp.logical_not(is_self))
        def _():
            remote(*parts).wait_send()

    for shift in range(1, 8):
        remote(
            ids_in,
            ids_all.at[spot],
            send_ids.at[shift],
            recv_ids.at[shift],
            (row, lax.rem(spot + shift, 8), core),
        ).wait_send()
    for copy in gain_copies:
        copy.wait_send()
    for copy in early_saves + late_saves + [save_left] + [save_piece(piece) for piece in range(4)]:
        copy.wait()


def forward(
    tokens,
    positions,
    ids,
    gain_one,
    gain_two,
    w_query,
    w_key,
    w_value,
    w_out_t,
    w_gate,
    w_up,
    w_down_t,
    cotangent,
):
    dma = pltpu.SemaphoreType.DMA
    vmem = pltpu.VMEM
    low, full = jnp.bfloat16, jnp.float32
    rows, width = tokens.shape
    share, hidden_width = w_gate.shape
    out_width = w_out_t.shape[1]
    near_width = 16 * HEAD + out_width
    length = 8 * rows
    per_device = rows // RUN
    heads = (8, per_device, HEAD, RUN)
    both = (2, per_device, HEAD, RUN)
    by_run = (length // RUN, RUN, HEAD)
    flat = (HEAD, length)
    smem_spec = pl.BlockSpec(memory_space=pltpu.SMEM)
    shape = jax.ShapeDtypeStruct
    return pl.pallas_call(
        forward_kernel,
        in_specs=[vmem_spec()] * 6 + [any_spec()] * 8,
        out_specs=[any_spec()] * 15 + [smem_spec] * 2,
        out_shape=[
            shape((2, 4, 2, share, near_width), low),
            shape((2, 4, 2, share, 3 * hidden_width), low),
            shape((rows, width), low),
            shape(flat, low),
            shape(by_run, low),
            shape(flat, low),
            shape(flat, full),
            shape((1, length), full),
            shape((rows, out_width), low),
            shape((rows, width), full),
            shape((rows, width), low),
            shape((rows, 3 * hidden_width), low),
            shape((8, width), full),
            shape((2, HALF, rows), full),
            shape((2, 2, 2, 4 * share, rows), low),
            shape((2 * length // RUN, 2), jnp.int32),
            shape((length // RUN,), jnp.int32),
        ],
        scratch_shapes=[
            vmem((share, near_width), low),
            vmem((share, 3 * hidden_width), low),
            vmem((rows, width), full),
            vmem((rows, width), low),
            vmem((2, HALF, rows), full),
            vmem((2, 2, 4, 2, share, 4 * HEAD), low),
            vmem((8, WIDE), full),
            vmem((16, 8, WIDE), full),
            vmem((width, 8), full),
            vmem((8, width), full),
            vmem((2, 2, 2, 4 * share, rows), low),
            vmem(heads, low),
            vmem((4,) + both, low),
            vmem(heads, low),
            vmem((8,) + both, low),
            vmem(flat, low),
            vmem(by_run, low),
            vmem(flat, low),
            vmem(flat, full),
            vmem((1, length), full),
            vmem((length // RUN, HEAD, RUN), low),
            vmem(heads, low),
            vmem(heads, low),
            vmem((rows, out_width), low),
            vmem((2, 4, 2, share, out_width), low),
            vmem((rows, width), low),
            vmem((rows, width), low),
            vmem((rows, width), low),
            vmem((rows, width), low),
            vmem((rows, 3 * hidden_width), low),
            vmem((2, 3, 2, 4, 2, share, PIECE), low),
            vmem((8, 8, WIDE), jnp.int32),
            pltpu.SMEM((8, 8, WIDE), jnp.int32),
            dma((16,)),
            dma((8,)),
            dma((8,)),
            dma(()),
            dma((16,)),
            dma((16,)),
            dma((2,)),
            dma(()),
            dma((2, 3)),
            dma(()),
            dma((4,)),
            dma((12,)),
            dma((4, 2)),
            dma((8,)),
            dma((4, 2)),
            dma((8,)),
            dma((8,)),
            dma((8,)),
            dma((8,)),
            dma((8,)),
            dma((4,)),
            dma((4,)),
        ]
        + gather_sems(6),
        compiler_params=pltpu.CompilerParams(
            collective_id=1, has_side_effects=True, vmem_limit_bytes=VMEM_LIMIT
        ),
        name="forward",
    )(
        tokens,
        positions,
        (theta_base ** (-2.0 * jnp.arange(HALF, dtype=jnp.float32) / HEAD)).reshape(HALF, 1),
        ids,
        gain_one,
        gain_two,
        w_query,
        w_key,
        w_value,
        w_out_t,
        w_gate,
        w_up,
        w_down_t,
        cotangent,
    )


SECOND, THIRD, LAST = 2, 4, 5


class Reduce:
    def __init__(self, n, changes, refs):
        (
            self.left_t,
            self.right,
            self.own,
            self.out,
            self.save,
            self.send_one,
            self.recv_one,
            self.send_two,
            self.recv_two,
            self.kept,
            self.recv_three,
            self.ss_one,
            self.rs_one,
            self.ss_two,
            self.rs_two,
            self.ss_three,
            self.rs_three,
        ) = refs
        self.n, self.changes = n, changes
        self.share = self.own.shape[1]

    def columns(self, step, kind):
        held = self.right.shape[1] // (2 * PIECE)
        start = lax.rem(step, held) * 2 * PIECE + kind * PIECE
        return pl.ds(pl.multiple_of(start, PIECE), PIECE)

    def saving(self, step):
        slot = lax.rem(step, 2)
        pieces = self.changes[0] // 3
        place = jnp.where(step < self.changes[0], lax.rem(step, 3) * pieces + step // 3, step)
        cut = pl.ds(pl.multiple_of(place * 2 * PIECE, 2 * PIECE), 2 * PIECE)
        return pltpu.make_async_copy(self.own.at[slot], self.out.at[:, cut], self.save.at[slot])

    def product(self, step, kind, x, y):
        left = jnp.where(lax.rem(step, 3) == 2, 0, 1)
        left = jnp.where(step >= self.changes[0], 2, left)
        left = jnp.where(step >= self.changes[1], 0, left)
        term = jnp.dot(
            self.left_t[left, x, y],
            self.right[:, self.columns(step, kind)],
            preferred_element_type=jnp.float32,
        )
        return term

    def x_first(self, step, kind):
        return 1 if kind == 0 else jnp.where(lax.rem(step, 5) == 4, 1, 0)

    def beside(self, by_x):
        row, level, column = neighbours()[:3]
        core = place()[2]
        other_row = by_x * (1 - row) + (1 - by_x) * row
        other_column = by_x * column + (1 - by_x) * (1 - column)
        return (other_row, 2 * level + other_column, core)

    def first_copy(self, step, kind):
        out, into = lax.rem(step, 3), lax.rem(step, 6)
        return remote(
            self.send_one.at[out, kind],
            self.recv_one.at[into, kind],
            self.ss_one.at[out, kind],
            self.rs_one.at[into, kind],
            self.beside(self.x_first(step, kind)),
        )

    def second_copy(self, step, kind):
        out, into = lax.rem(step, 3), lax.rem(step, 6)
        return remote(
            self.send_two.at[out, kind],
            self.recv_two.at[into, kind],
            self.ss_two.at[out, kind],
            self.rs_two.at[into, kind],
            self.beside(1 - self.x_first(step, kind)),
        )

    def third_copy(self, step, kind, k):
        row, level, column, beside_x, beside_y, along_z = neighbours()
        target = lax.rem(level + k + 1, 4)
        out, into = lax.rem(step, 4), lax.rem(step, 4)
        return remote(
            self.kept.at[out, kind, pl.ds(pl.multiple_of(target * self.share, 16), self.share)],
            self.recv_three.at[into, kind, k],
            self.ss_three.at[out, kind, k],
            self.rs_three.at[into, kind, k],
            along_z[k],
        )

    def pieces(self, step, act):
        act(0)

        @pl.when(step < self.n - 1)
        def _():
            act(1)

    def first(self, step):
        row, level, column = neighbours()[:3]
        slot = lax.rem(step, 3)

        def act(kind):
            by_x = self.x_first(step, kind)
            for half in range(2):
                x = by_x * (1 - row) + (1 - by_x) * half
                y = by_x * half + (1 - by_x) * (1 - column)
                self.send_one[slot, kind, half] = self.product(step, kind, x, y).astype(
                    jnp.bfloat16
                )
            self.first_copy(step, kind).start()

        self.pieces(step, act)

    def second(self, step):
        row, level, column = neighbours()[:3]
        slot, came, keep = lax.rem(step, 3), lax.rem(step, 6), lax.rem(step, 4)
        self.pieces(step, lambda kind: self.first_copy(step, kind).wait())

        def act(kind):
            by_x = self.x_first(step, kind)
            x = by_x * row + (1 - by_x) * (1 - row)
            y = by_x * (1 - column) + (1 - by_x) * column
            arrived = self.recv_one.at[came, kind]
            mine = by_x * column + (1 - by_x) * row
            away = self.product(step, kind, x, y) + arrived[1 - mine].astype(jnp.float32)
            self.send_two[slot, kind] = away.astype(jnp.bfloat16)
            here = self.product(step, kind, row, column) + arrived[mine].astype(jnp.float32)
            self.kept[keep, kind] = here.astype(jnp.bfloat16)

        self.pieces(step, act)
        self.pieces(step, lambda kind: self.second_copy(step, kind).start())

    def third(self, step):
        came, keep = lax.rem(step, 6), lax.rem(step, 4)

        def act(kind):
            self.second_copy(step, kind).wait()
            here = self.kept[keep, kind].astype(jnp.float32) + self.recv_two[came, kind].astype(
                jnp.float32
            )
            self.kept[keep, kind] = here.astype(jnp.bfloat16)
            for k in range(3):
                self.third_copy(step, kind, k).start()

        self.pieces(step, act)

    def last(self, step):
        level = neighbours()[1]
        came, keep = lax.rem(step, 4), lax.rem(step, 4)
        mine = pl.ds(pl.multiple_of(level * self.share, 16), self.share)

        @pl.when(step >= 2)
        def _():
            self.saving(step - 2).wait()

        def act(kind):
            total = self.kept[keep, kind, mine].astype(jnp.float32)
            for k in range(3):
                self.third_copy(step, kind, k).wait()
                total = total + self.recv_three[came, kind, k].astype(jnp.float32)
            self.own[lax.rem(step, 2), :, kind * PIECE : (kind + 1) * PIECE] = total

        self.pieces(step, act)
        self.saving(step).start()

    def turn(self, step):
        for stage, lag in (
            (self.first, 0),
            (self.second, SECOND),
            (self.third, THIRD),
            (self.last, LAST),
        ):

            @pl.when(jnp.logical_and(step >= lag, step < self.n + lag))
            def _():
                stage(step - lag)


def backward_kernel(
    order,
    ids,
    q_in,
    k_in,
    v_in,
    mixed_t_in,
    lse_in,
    cotangent,
    left_in,
    normed_in,
    right_in,
    mixed_low,
    middle,
    near,
    far,
    tokens,
    gains_in,
    tables,
    input_grad,
    layer_out,
    grads,
    gain_out,
    q,
    q_t,
    k,
    k_t,
    v,
    d_own,
    d_slots,
    d,
    d_t,
    dq_t,
    lse,
    delta,
    dk,
    dv,
    dq_slots,
    dkv_sorted,
    dkv_slots,
    dkv_other,
    dq_own,
    dkv_own,
    weight,
    middle_ring,
    input_ring,
    part,
    part_other,
    total,
    staged,
    grad_mid,
    gain_two_grad,
    left_t,
    right,
    gain_columns,
    gain_messages,
    gain_all,
    own,
    send_one,
    recv_one,
    send_two,
    recv_two,
    kept,
    recv_three,
    loads,
    load_first,
    send_gain,
    recv_gain,
    load_left_sem,
    load_w,
    load_ring,
    save_rows,
    save_sem,
    send_d,
    recv_d,
    send_q,
    recv_q,
    send_x,
    recv_x,
    send_k,
    recv_k,
    send_p,
    recv_p,
    save,
    *sems,
):
    row, spot, core = place()
    low, full = jnp.bfloat16, jnp.float32
    rows, width = staged.shape
    length = 8 * rows
    runs, tiles = length // RUN, length // TILE
    per_device = rows // RUN
    halves = TILE // RUN
    share = width // 16
    quarter = 4 * share
    sibling = (row, spot, 1 - core)
    qkv_width = 16 * HEAD
    out_width = mixed_low.shape[1]
    n = grads.shape[1] // (2 * PIECE)
    near_at = right_in.shape[1] // (2 * PIECE)
    changes = (near_at, near_at + qkv_width // (2 * PIECE))
    sums = Reduce(
        n,
        changes,
        (left_t, right, own, grads, save)
        + (send_one, recv_one, send_two, recv_two, kept, recv_three)
        + sems,
    )

    def stage(source):
        return pltpu.make_async_copy(source, staged, load_left_sem)

    early_loads = [
        pltpu.make_async_copy(source, target, loads.at[index])
        for index, (source, target) in enumerate(
            [
                (q_in, q_t),
                (k_in, k),
                (v_in, d_t),
                (mixed_t_in, dq_t),
                (lse_in, lse),
                (middle, total),
            ]
        )
    ]

    first_loads = [
        pltpu.make_async_copy(left_in, left_t.at[pl.ds(0, 2)], load_first.at[4])
    ] + [
        pltpu.make_async_copy(
            right_in.at[:, pl.ds(3 * FEED * piece, 3 * FEED)],
            right.at[:, pl.ds(3 * FEED * piece, 3 * FEED)],
            load_first.at[piece],
        )
        for piece in range(4)
    ]


    def load_block(index, piece, part_of, start):
        lanes = pl.ds(3 * FEED * piece + start + part_of * PIECE, PIECE)
        levels = pl.ds(2 * lax.rem(index, 2), 2)
        return pltpu.make_async_copy(
            far.at[index // 2, levels, :, :, lanes], held_block(piece, part_of), load_w.at[piece]
        )

    def held_block(piece, part_of):
        levels = pl.ds(2 * (part_of % 2), 2)
        return weight.at[piece, part_of // 2, levels, :, :, pl.ds(0, PIECE)]

    def load_blocks(index, piece, start, parts):
        for part_of in range(parts):
            load_block(index, piece, part_of, start).start()

    def row_products(start, parts, landing):
        def block(index, carry):
            term = jnp.zeros((rows, quarter), full)
            for piece in range(4):
                for part_of in range(parts):
                    load_block(index, piece, part_of, start).wait()
                for part_of in range(parts):
                    at = 3 * FEED * piece + start + part_of * PIECE
                    term = term + contract_cols(
                        right[:, at : at + PIECE],
                        held_block(piece, part_of)[...].reshape(quarter, PIECE),
                    )

                @pl.when(index + 1 < 4)
                def _():
                    load_blocks(index + 1, piece, start, parts)

            part[:, tile_at(index, quarter)] = term.astype(low)
            pair_copy(index, landing).start()
            return carry

        lax.fori_loop(0, 4, block, 0)

    def pair_copy(index, landing):
        cut = pl.ds(pl.multiple_of(index * quarter, quarter), quarter)
        return remote(
            part.at[:, cut],
            part_other.at[landing, :, cut],
            send_p.at[index],
            recv_p.at[landing, index],
            sibling,
        )

    def second_back():
        row_products(0, 4, 0)
        for index in range(2):
            load_out_weight(index).start()

    def load_out_weight(index):
        lanes = pl.ds(qkv_width + index * 4 * HEAD, 4 * HEAD)
        return pltpu.make_async_copy(
            near.at[:, :, :, :, lanes], weight.at[index], load_w.at[index]
        )

    d_copies = []
    for step in range(4):
        slot = lax.rem(spot + step, 4)
        chip = 4 * core + slot
        for other in range(2):
            parts = (
                d_own.at[2 * slot + other],
                d_slots.at[spot],
                send_d.at[step, other],
                recv_d.at[spot],
                (row, chip, other),
            )
            d_copies.append((parts, jnp.logical_and(chip == spot, core == other)))

    def middle_back():
        for index in range(4):
            pair_copy(index, 0).wait()
        early_loads[5].wait()
        stage(cotangent).wait()
        chunk = rows // 8

        def block(index, gain_grad):
            cut = tile_at(index, chunk)
            grad = part[cut].astype(full) + part_other[0, cut].astype(full)
            values = total[cut]
            inverse = lax.rsqrt(jnp.mean(values * values, axis=-1, keepdims=True) + epsilon)
            unit = values * inverse
            scaled = grad * gains_in[1:2]
            mean = jnp.mean(scaled * unit, axis=-1, keepdims=True)
            result = staged[cut].astype(full) + inverse * (scaled - unit * mean)
            total[cut] = result
            grad_mid[cut] = result.astype(low)
            return gain_grad + jnp.sum(grad * unit, axis=0, keepdims=True)

        gain_two_grad[...] = lax.fori_loop(0, 8, block, jnp.zeros((1, width), full))
        for index in range(2):
            load_out_weight(index).wait()
            grad = dot_f32(grad_mid[...], weight[index].reshape(width, 4 * HEAD)).T.astype(low)
            for head in range(4):
                for run in range(per_device):
                    d_own[4 * index + head, run] = grad[
                        head * HEAD : (head + 1) * HEAD, run * RUN : (run + 1) * RUN
                    ]
        for parts, is_self in d_copies:
            move(*parts, is_self)


    def prepare():
        for copy in early_loads[:5]:
            copy.wait()
        for index in range(tiles):
            cut = pl.ds(index * TILE, TILE)
            q[cut] = q_t[:, cut].T
            k_t[:, cut] = k[halves * index : halves * (index + 1)].reshape(TILE, HEAD).T
            v[cut] = d_t[:, cut].T

    def take_cotangents():
        for index in range(8):
            remote(
                d_slots.at[index], d_slots.at[index], send_d.at[0, 0], recv_d.at[index], sibling
            ).wait_recv()

        def sort_run(index, carry):
            cols = tile_at(index, RUN)
            run = d_slots[order[index, 0], order[index, 1]]
            d_t[:, cols] = run
            d[cols] = run.T
            delta[:, cols] = jnp.sum(run.astype(full) * dq_t[:, cols], axis=0, keepdims=True)
            return carry

        lax.fori_loop(0, runs, sort_run, 0)
        dq_t[...] = jnp.zeros_like(dq_t)

    scale = HEAD ** (-0.5)

    def key_tile(block):
        cut = tile_at(block, TILE)
        both = pl.ds(block * halves, halves)
        keys, values = k[both].reshape(TILE, HEAD), v[cut]
        keys_t = k_t[:, cut]
        dk[...] = jnp.zeros_like(dk)
        dv[...] = jnp.zeros_like(dv)

        def query_tile(index, diagonal):
            cols = tile_at(index, TILE)
            scores = dot_f32(keys, q_t[:, cols]) * (scale * LOG2_E)
            if diagonal:
                scores = causal(scores)
            probs = jnp.exp2(scores - lse[:, cols])
            dv[...] += dot_f32(probs.astype(low), d[cols])
            grad_probs = dot_f32(values, d_t[:, cols])
            grad_scores = (probs * (grad_probs - delta[:, cols])).astype(low)
            dk[...] += dot_f32(grad_scores, q[cols])
            dq_t[:, cols] += dot_f32(keys_t, grad_scores)

        query_tile(block, True)

        def later(index, inner):
            query_tile(index, False)
            return inner

        lax.fori_loop(block + 1, tiles, later, 0)
        for kind, value in enumerate(((dk[...] * scale).T.astype(low), dv[...].T.astype(low))):
            for half in range(halves):
                dkv_sorted[block * halves + half, kind] = value[:, half * RUN : (half + 1) * RUN]

    def key_tiles(start, stop):
        def one(block, carry):
            key_tile(block)
            return carry

        lax.fori_loop(start, stop, one, 0)

    swap = remote(dkv_slots.at[:, :, 1 - core], dkv_other, send_x, recv_x, sibling)
    dq_copies = return_copies(dq_slots, dq_own, send_q, recv_q)
    slot, owner = lax.rem(spot, 4), spot // 4
    dkv_copies = []
    for step in range(8):
        chip = lax.rem(spot + step, 8)
        parts = (
            dkv_slots.at[:, chip, core],
            dkv_own.at[slot, :, core],
            send_k.at[step],
            recv_k.at[slot, core],
            (row, chip, owner),
        )
        dkv_copies.append((parts, (owner == core) if step == 0 else False))

    def send_back():
        def unsort_run(run, carry):
            index = ids[run]
            for kind in range(2):
                dkv_slots[kind, run // per_device, run % per_device] = dkv_sorted[index, kind]
            return carry

        lax.fori_loop(0, runs, unsort_run, 0)
        swap.start()

        def turn_run(index, carry):
            value = dq_t[:, tile_at(index, RUN)] * scale
            d_slots[index // per_device, index % per_device] = value.astype(low)
            return carry

        lax.fori_loop(0, runs, turn_run, 0)

        def unsort_queries(run, carry):
            value = d_slots[order[runs + run, 0], order[runs + run, 1]]
            dq_slots[run // per_device, run % per_device] = value
            return carry

        lax.fori_loop(0, runs, unsort_queries, 0)
        start_return(dq_copies)

    def add_pairs():
        swap.wait()
        for chip in range(8):
            both = dkv_slots[:, chip, core].astype(full) + dkv_other[:, chip].astype(full)
            dkv_slots[:, chip, core] = both.astype(low)
        start_return(dkv_copies)


    def feed_forward():
        row_products(2 * FEED, 2, 1)
        for group in range(4):
            load_group(group).start()

    save_layer = pltpu.make_async_copy(part, layer_out, save_sem)

    def finish_layer():
        for index in range(4):
            pair_copy(index, 1).wait()
        pieces = width // PIECE

        def load_piece(index):
            lanes = pl.ds(index * PIECE, PIECE)
            return pltpu.make_async_copy(
                middle.at[:, lanes], middle_ring.at[index % 2], load_ring.at[index % 2]
            )

        load_piece(0).start()
        for index in range(pieces):
            if index + 1 < pieces:
                load_piece(index + 1).start()
            load_piece(index).wait()
            cut = pl.ds(index * PIECE, PIECE)
            value = part[:, cut].astype(full) + part_other[1, :, cut].astype(full)
            part[:, cut] = (value + middle_ring[index % 2]).astype(low)
        save_layer.start()


    def load_group(group):
        lanes = pl.ds(group * 4 * HEAD, 4 * HEAD)
        return pltpu.make_async_copy(
            near.at[:, :, :, :, lanes], weight.at[group], load_w.at[group]
        )

    load_mixed = pltpu.make_async_copy(
        mixed_low, right.at[:, pl.ds(qkv_width, out_width)], loads.at[0]
    )

    def project_back():
        load_mixed.start()
        for head in range(8):
            remote(
                dq_own.at[head], dq_own.at[head], send_q.at[0], recv_q.at[head], sibling
            ).wait_recv()
        for slot_in in range(4):
            for core_in in range(2):
                target = dkv_own.at[slot_in, :, core_in]
                remote(
                    target, target, send_k.at[0], recv_k.at[slot_in, core_in], sibling
                ).wait_recv()
        for group in range(4):
            for run in range(per_device):
                cols = slice(run * RUN, (run + 1) * RUN)
                turned = []
                for head in range(4):
                    if group < 2:
                        value = dq_own[4 * group + head, run]
                    else:
                        value = dkv_own[head, group - 2, run]
                    if group < 3:
                        front, back = value[:HALF].astype(full), value[HALF:].astype(full)
                        cos_part, sin_part = tables[0, :, cols], tables[1, :, cols]
                        turned.append((front * cos_part + back * sin_part).astype(low))
                        turned.append((back * cos_part - front * sin_part).astype(low))
                    else:
                        turned.append(value)
                right[cols, group * 4 * HEAD : (group + 1) * 4 * HEAD] = jnp.concatenate(
                    turned, axis=0
                ).T
        load_mixed.wait()

    def project_normed():
        save_layer.wait()
        for group in range(4):
            load_group(group).wait()
        stage(tokens).start()

        def block(index, carry):
            term = jnp.zeros((rows, quarter), full)
            for group in range(4):
                held = weight[group, index // 2, pl.ds(2 * lax.rem(index, 2), 2)]
                term = term + contract_cols(
                    right[:, group * 4 * HEAD : (group + 1) * 4 * HEAD],
                    held.reshape(quarter, 4 * HEAD),
                )
            part[:, tile_at(index, quarter)] = term.astype(low)
            pair_copy(index, 0).start()
            return carry

        lax.fori_loop(0, 4, block, 0)

    def save_input(index):
        cut = tile_at(index, rows // 8)
        slot = lax.rem(index, 2)
        return pltpu.make_async_copy(
            input_ring.at[slot], input_grad.at[cut], save_rows.at[slot]
        )

    def norm_back():
        stage(tokens).wait()
        for index in range(4):
            pair_copy(index, 0).wait()
        chunk = rows // 8

        def block(index, gain_grad):
            cut = tile_at(index, chunk)
            grad = part[cut].astype(full) + part_other[0, cut].astype(full)
            values = staged[cut].astype(full)
            inverse = lax.rsqrt(jnp.mean(values * values, axis=-1, keepdims=True) + epsilon)
            unit = values * inverse
            scaled = grad * gains_in[0:1]
            mean = jnp.mean(scaled * unit, axis=-1, keepdims=True)
            result = total[cut] + inverse * (scaled - unit * mean)

            @pl.when(index >= 2)
            def _():
                save_input(index - 2).wait()

            input_ring[lax.rem(index, 2)] = result.reshape(chunk, 1, width)
            save_input(index).start()
            return gain_grad + jnp.sum(grad * unit, axis=0, keepdims=True)

        gain_one_grad = lax.fori_loop(0, 8, block, jnp.zeros((1, width), full))
        lines = jnp.concatenate(
            [gain_one_grad, gain_two_grad[...], jnp.zeros((6, width), full)], axis=0
        )
        gain_columns[...] = lines.T
        for shard in range(16):
            held = gain_columns[shard * share : (shard + 1) * share]
            gain_messages[shard] = jnp.pad(held, ((0, WIDE - share), (0, 0))).T
        for copy in gain_copies:
            copy.start()
        gain_all[own_shard()] = gain_messages[own_shard()]

    gain_copies, gain_from = exchange_messages(
        lambda shard: gain_messages.at[shard], gain_all, send_gain, recv_gain
    )

    def finish_gains():
        for wait in gain_from:
            wait()
        gain_out[...] = jnp.sum(gain_all[...], axis=0)

    def take_normed():
        stage(normed_in).start()
        stage(normed_in).wait()
        turn_left(left_t, 2, staged)

    def start_forward():
        for piece in range(4):
            load_blocks(0, piece, 2 * FEED, 2)

    for copy in first_loads:
        copy.start()
    stage(cotangent).start()
    for piece in range(4):
        load_blocks(0, piece, 0, 4)
    for copy in early_loads:
        copy.start()
    greet(group_others())
    first_loads[0].wait()
    first_loads[1].wait()

    def wait_right():
        for copy in first_loads[2:]:
            copy.wait()

    plan = {
        2: [wait_right, second_back],
        3: [middle_back],
        4: [prepare],
        5: [start_forward, take_cotangents],
    }
    tiles_from, tile_ranges = 5, ((0, 1), (1, 2), (2, 3), (3, 5), (5, 8))
    later = {
        9: [send_back],
        11: [add_pairs, feed_forward, finish_layer, take_normed],
        12: [project_back],
        15: [lambda: turn_left(left_t, 0, grad_mid), project_normed],
        16: [norm_back],
        n + LAST - 1: [finish_gains],
    }

    def run(step, carry):
        for when, tasks in plan.items():

            @pl.when(step == when)
            def _():
                for task in tasks:
                    task()

        @pl.when(jnp.logical_and(step >= tiles_from, step < tiles_from + len(tile_ranges)))
        def _():
            start, stop = 0, 0
            for index, (first_tile, past_tile) in enumerate(tile_ranges):
                start = jnp.where(step == tiles_from + index, first_tile, start)
                stop = jnp.where(step == tiles_from + index, past_tile, stop)
            key_tiles(start, stop)

        for when, tasks in later.items():

            @pl.when(step == when)
            def _():
                for task in tasks:
                    task()

        sums.turn(step)
        return carry

    lax.fori_loop(0, n + LAST, run, 0)
    for index in (6, 7):
        save_input(index).wait()
    for copy in gain_copies:
        copy.wait_send()
    for step in (n - 2, n - 1):
        sums.saving(step).wait()
    for copies in (d_copies, dq_copies, dkv_copies):
        for parts, is_self in copies:
            if is_self is False:
                remote(*parts).wait_send()
            else:

                @pl.when(jnp.logical_not(is_self))
                def _():
                    remote(*parts).wait_send()


def backward(order, ids, *arrays):
    dma = pltpu.SemaphoreType.DMA
    vmem = pltpu.VMEM
    low, full = jnp.bfloat16, jnp.float32
    q_sorted, k_sorted, v_sorted, mixed_t, lse, cotangent, left, normed, right = arrays[:9]
    mixed_low, middle, near, far, tokens, gains, tables = arrays[9:]
    rows, width = cotangent.shape
    length = 8 * rows
    share = width // 16
    wide = right.shape[1] + 16 * HEAD + mixed_low.shape[1] + PIECE
    quarter = 4 * share
    per_device = rows // RUN
    heads = (8, per_device, HEAD, RUN)
    tall, flat = (length, HEAD), (HEAD, length)
    by_run = (length // RUN, RUN, HEAD)
    block = (rows, width)
    smem_spec = pl.BlockSpec(memory_space=pltpu.SMEM)
    shape = jax.ShapeDtypeStruct
    return pl.pallas_call(
        backward_kernel,
        in_specs=[smem_spec] * 2 + [any_spec()] * 14 + [vmem_spec()] * 2,
        out_specs=[any_spec()] * 3 + [vmem_spec()],
        out_shape=[
            shape((rows, 1, width), full),
            shape(block, low),
            shape((share, wide), full),
            shape((8, WIDE), full),
        ],
        scratch_shapes=[
            vmem(tall, low),
            vmem(flat, low),
            vmem(by_run, low),
            vmem(flat, low),
            vmem(tall, low),
            vmem(heads, low),
            vmem(heads, low),
            vmem(tall, low),
            vmem(flat, low),
            vmem(flat, full),
            vmem((1, length), full),
            vmem((1, length), full),
            vmem((TILE, HEAD), full),
            vmem((TILE, HEAD), full),
            vmem(heads, low),
            vmem((length // RUN, 2, HEAD, RUN), low),
            vmem((2,) + heads, low),
            vmem((2, 8, HEAD, RUN), low),
            vmem(heads, low),
            vmem((4, 2, per_device, HEAD, RUN), low),
            vmem((4, 2, 4, 2, share, 4 * HEAD), low),
            vmem((2, rows, PIECE), full),
            vmem((2, rows // 8, 1, width), full),
            vmem(block, low),
            vmem((2,) + block, low),
            vmem(block, full),
            vmem(block, low),
            vmem(block, low),
            vmem((1, width), full),
            vmem((3, 2, 2, quarter, rows), low),
            vmem(right.shape, low),
            vmem((width, 8), full),
            vmem((16, 8, WIDE), full),
            vmem((16, 8, WIDE), full),
            vmem((2, share, 2 * PIECE), full),
            vmem((3, 2, 2, quarter, PIECE), low),
            vmem((6, 2, 2, quarter, PIECE), low),
            vmem((3, 2, quarter, PIECE), low),
            vmem((6, 2, quarter, PIECE), low),
            vmem((4, 2, quarter, PIECE), low),
            vmem((4, 2, 3, share, PIECE), low),
            dma((7,)),
            dma((5,)),
            dma((16,)),
            dma((16,)),
            dma(()),
            dma((4,)),
            dma((2,)),
            dma((2,)),
            dma(()),
            dma((4, 2)),
            dma((8,)),
            dma((8,)),
            dma((8,)),
            dma(()),
            dma(()),
            dma((8,)),
            dma((4, 2)),
            dma((4,)),
            dma((2, 4)),
            dma((2,)),
            dma((3, 2)),
            dma((6, 2)),
            dma((3, 2)),
            dma((6, 2)),
            dma((4, 2, 3)),
            dma((4, 2, 3)),
        ],
        compiler_params=pltpu.CompilerParams(
            collective_id=2, has_side_effects=True, vmem_limit_bytes=62 * 1024 * 1024
        ),
        name="backward",
    )(
        order,
        ids,
        *arrays,
    )


def by_heads(
    tokens,
    positions,
    gain_one,
    gain_two,
    w_query,
    w_key,
    w_value,
    w_out,
    w_gate,
    w_up,
    w_down,
    cotangent,
):
    rows, _, width = tokens.shape
    share = gain_one.shape[0]
    run_ids = positions[::RUN, 0] // RUN
    flat_in = tokens.reshape(rows, width)
    (
        near,
        far,
        normed,
        q_sorted,
        k_sorted,
        v_sorted,
        mixed_t,
        lse,
        mixed_low,
        middle,
        second,
        right,
        gains,
        tables,
        left,
        order,
        ids,
    ) = forward(
        flat_in,
        positions.reshape(1, rows),
        jnp.broadcast_to(jnp.pad(run_ids, (0, WIDE - rows // RUN)), (8, WIDE)),
        gain_one.reshape(1, share),
        gain_two.reshape(1, share),
        w_query,
        w_key,
        w_value,
        w_out.T,
        w_gate,
        w_up,
        w_down.T,
        cotangent.reshape(rows, width),
    )
    input_grad, layer_out, grads, gain_grads = backward(
        order,
        ids,
        q_sorted,
        k_sorted,
        v_sorted,
        mixed_t,
        lse,
        cotangent.reshape(rows, width),
        left,
        normed,
        right,
        mixed_low,
        middle,
        near,
        far,
        flat_in,
        gains,
        tables,
    )
    splits, start = [], 0
    for wide in (
        w_gate.shape[1],
        w_up.shape[1],
        w_down.shape[0],
        w_query.shape[1],
        w_key.shape[1],
        w_value.shape[1],
        w_out.shape[0],
    ):
        splits.append(grads[:, start : start + wide])
        start += wide
    grad_gate, grad_up, grad_down, grad_query, grad_key, grad_value, grad_out = splits
    return (
        layer_out.reshape(rows, 1, width),
        input_grad,
        gain_grads[0, :share],
        gain_grads[1, :share],
        grad_query,
        grad_key,
        grad_value,
        grad_out.T,
        grad_gate,
        grad_up,
        grad_down.T,
    )


def solution(mesh):
    sizes = (mesh.shape["dp"], mesh.shape["context"], mesh.shape["tensor"])
    return jax.shard_map(
        by_heads if sizes == (2, 8, 2) else on_device,
        mesh=mesh,
        in_specs=(
            P("context", "dp", None),
            P("context", "dp"),
            P(("dp", "context")),
            P(("dp", "context")),
            P(("dp", "context"), "tensor"),
            P(("dp", "context"), "tensor"),
            P(("dp", "context"), "tensor"),
            P("tensor", ("dp", "context")),
            P(("dp", "context"), "tensor"),
            P(("dp", "context"), "tensor"),
            P("tensor", ("dp", "context")),
            P("context", "dp", None),
        ),
        out_specs=(
            P("context", "dp", None),
            P("context", "dp", None),
            P(("dp", "context")),
            P(("dp", "context")),
            P(("dp", "context"), "tensor"),
            P(("dp", "context"), "tensor"),
            P(("dp", "context"), "tensor"),
            P("tensor", ("dp", "context")),
            P(("dp", "context"), "tensor"),
            P(("dp", "context"), "tensor"),
            P("tensor", ("dp", "context")),
        ),
        check_vma=False,
    )
```

```python
import functools
import types

import jax
import jax.numpy as jnp
from jax import lax
from jax.experimental import pallas as pl
from jax.experimental.pallas import tpu as pltpu
from jax.sharding import PartitionSpec as P

HEAD = 96


epsilon = 1e-05
theta_base = 100000.0
masked_value = -1e30


def norm_forward(values_in, gain_vec):
    inverse = lax.rsqrt(jnp.mean(values_in * values_in, axis=-1, keepdims=True) + epsilon)
    unit_vals = values_in * inverse
    return (unit_vals, inverse, (unit_vals * gain_vec.astype(jnp.float32)).astype(jnp.bfloat16))


def norm_backward(grad_in, unit_vals, inverse, gain_vec):
    scaled = grad_in * gain_vec.astype(jnp.float32)
    grad_vals = inverse * (
        scaled - unit_vals * jnp.mean(scaled * unit_vals, axis=-1, keepdims=True)
    )
    return (grad_vals, jnp.sum(grad_in * unit_vals, axis=0))


def rotate(values_in, cos_part, sin_part):
    half_size = values_in.shape[-1] // 2
    front_half = values_in[..., :half_size]
    back_half = values_in[..., half_size:]
    return jnp.concatenate(
        [
            front_half * cos_part - back_half * sin_part,
            back_half * cos_part + front_half * sin_part,
        ],
        axis=-1,
    )


def contract_rows(left_mat, right_mat):
    return lax.dot_general(
        left_mat, right_mat, (((0,), (0,)), ((), ())), preferred_element_type=jnp.float32
    )


def contract_cols(left_mat, right_mat):
    return lax.dot_general(
        left_mat, right_mat, (((1,), (1,)), ((), ())), preferred_element_type=jnp.float32
    )


def on_device(
    tokens,
    positions,
    gain_one,
    gain_two,
    w_query,
    w_key,
    w_value,
    w_out,
    w_gate,
    w_up,
    w_down,
    cotangent,
):
    slot_count, seq_count, model_width = tokens.shape
    row_count = slot_count * seq_count
    gathered = (
        lax.all_gather(gain_one, ("dp", "context"), axis=0, tiled=True),
        lax.all_gather(gain_two, ("dp", "context"), axis=0, tiled=True),
        lax.all_gather(w_query, ("dp", "context"), axis=0, tiled=True),
        lax.all_gather(w_key, ("dp", "context"), axis=0, tiled=True),
        lax.all_gather(w_value, ("dp", "context"), axis=0, tiled=True),
        lax.all_gather(w_out, ("dp", "context"), axis=1, tiled=True),
        lax.all_gather(w_gate, ("dp", "context"), axis=0, tiled=True),
        lax.all_gather(w_up, ("dp", "context"), axis=0, tiled=True),
        lax.all_gather(w_down, ("dp", "context"), axis=1, tiled=True),
    )
    full_one, full_two, query_mat, key_mat, value_mat, out_mat, gate_mat, up_mat, down_mat = (
        gathered
    )
    heads_kv = key_mat.shape[1] // HEAD
    heads_q = query_mat.shape[1] // HEAD
    group_size = heads_q // heads_kv
    score_scale = HEAD ** (-0.5)
    half_size = HEAD // 2
    inv_freqs = theta_base ** (-2.0 * jnp.arange(half_size, dtype=jnp.float32) / HEAD)
    angles = positions.astype(jnp.float32)[:, :, None] * inv_freqs
    cos_part = jnp.cos(angles)[:, :, None, :]
    sin_part = jnp.sin(angles)[:, :, None, :]
    flat_in = tokens.astype(jnp.float32).reshape(row_count, model_width)
    unit_one, inverse_one, normed = norm_forward(flat_in, full_one)
    query_proj = jnp.dot(normed, query_mat, preferred_element_type=jnp.float32).reshape(
        slot_count, seq_count, heads_q, HEAD
    )
    key_proj = jnp.dot(normed, key_mat, preferred_element_type=jnp.float32).reshape(
        slot_count, seq_count, heads_kv, HEAD
    )
    value_low = (
        jnp.dot(normed, value_mat, preferred_element_type=jnp.float32)
        .astype(jnp.bfloat16)
        .reshape(slot_count, seq_count, heads_kv * HEAD)
    )
    queries = rotate(query_proj, cos_part, sin_part).astype(jnp.bfloat16)
    keys_low = (
        rotate(key_proj, cos_part, sin_part)
        .astype(jnp.bfloat16)
        .reshape(slot_count, seq_count, heads_kv * HEAD)
    )
    query_seq = jnp.transpose(
        queries.reshape(slot_count, seq_count, heads_kv, group_size, HEAD), (1, 2, 3, 0, 4)
    )
    query_pos = positions.T
    stat_shape = (seq_count, heads_kv, group_size, slot_count)
    initial = (
        jnp.full(stat_shape, masked_value, jnp.float32),
        jnp.zeros(stat_shape, jnp.float32),
        jnp.zeros(stat_shape + (HEAD,), jnp.float32),
    )
    key_piece = lax.all_gather(keys_low, "context", axis=0, tiled=True)
    value_piece = lax.all_gather(value_low, "context", axis=0, tiled=True)
    pos_piece = lax.all_gather(positions, "context", axis=0, tiled=True)
    piece_len = key_piece.shape[0]
    key_seq = jnp.transpose(key_piece.reshape(piece_len, seq_count, heads_kv, HEAD), (1, 2, 0, 3))
    value_seq = jnp.transpose(
        value_piece.reshape(piece_len, seq_count, heads_kv, HEAD), (1, 2, 0, 3)
    )
    pos_seq = pos_piece.T

    def per_sequence(seq_items):
        peak_val, totals, accum_vals, query_one, qpos_one, key_one, value_one, kpos_one = seq_items
        raw_scores = (
            jnp.einsum("hgqd,hkd->hgqk", query_one, key_one, preferred_element_type=jnp.float32)
            * score_scale
        )
        allowed = kpos_one[None, None, None, :] <= qpos_one[None, None, :, None]
        masked = jnp.where(allowed, raw_scores, masked_value)
        new_peak = jnp.maximum(peak_val, jnp.max(masked, axis=-1))
        decay_vals = jnp.exp(peak_val - new_peak)
        weights = jnp.where(allowed, jnp.exp(masked - new_peak[..., None]), 0.0)
        totals = totals * decay_vals + jnp.sum(weights, axis=-1)
        accum_vals = accum_vals * decay_vals[..., None] + jnp.einsum(
            "hgqk,hkd->hgqd",
            weights.astype(jnp.bfloat16),
            value_one,
            preferred_element_type=jnp.float32,
        )
        return (new_peak, totals, accum_vals)

    peak_val, totals, accum_vals = lax.map(
        per_sequence,
        (initial[0], initial[1], initial[2], query_seq, query_pos, key_seq, value_seq, pos_seq),
    )
    log_total = peak_val + jnp.log(totals)
    mixed_seq = accum_vals / totals[..., None]
    mixed_low = (
        jnp.transpose(mixed_seq, (3, 0, 1, 2, 4))
        .reshape(row_count, heads_q * HEAD)
        .astype(jnp.bfloat16)
    )
    branch = lax.psum(
        jnp.dot(mixed_low, out_mat, preferred_element_type=jnp.float32).astype(jnp.bfloat16),
        "tensor",
    ).astype(jnp.float32)
    middle = flat_in + branch
    unit_two, inverse_two, second = norm_forward(middle, full_two)
    gate_vals = jnp.dot(second, gate_mat, preferred_element_type=jnp.float32)
    up_vals = jnp.dot(second, up_mat, preferred_element_type=jnp.float32)
    sigmoid_vals = jax.nn.sigmoid(gate_vals)
    silu_vals = gate_vals * sigmoid_vals
    hidden = (silu_vals * up_vals).astype(jnp.bfloat16)
    mlp_part = lax.psum(
        jnp.dot(hidden, down_mat, preferred_element_type=jnp.float32).astype(jnp.bfloat16), "tensor"
    ).astype(jnp.float32)
    layer_out = (middle + mlp_part).astype(jnp.bfloat16).reshape(slot_count, seq_count, model_width)
    regathered = (
        lax.all_gather(gain_one, ("dp", "context"), axis=0, tiled=True),
        lax.all_gather(gain_two, ("dp", "context"), axis=0, tiled=True),
        lax.all_gather(w_query, ("dp", "context"), axis=0, tiled=True),
        lax.all_gather(w_key, ("dp", "context"), axis=0, tiled=True),
        lax.all_gather(w_value, ("dp", "context"), axis=0, tiled=True),
        lax.all_gather(w_out, ("dp", "context"), axis=1, tiled=True),
        lax.all_gather(w_gate, ("dp", "context"), axis=0, tiled=True),
        lax.all_gather(w_up, ("dp", "context"), axis=0, tiled=True),
        lax.all_gather(w_down, ("dp", "context"), axis=1, tiled=True),
    )
    full_one, full_two, query_mat, key_mat, value_mat, out_mat, gate_mat, up_mat, down_mat = (
        regathered
    )
    grad_low = cotangent.reshape(row_count, model_width)
    grad_down = contract_rows(hidden, grad_low)
    grad_hidden = contract_cols(grad_low, down_mat)
    grad_gate_low = (
        grad_hidden * up_vals * sigmoid_vals * (1.0 + gate_vals * (1.0 - sigmoid_vals))
    ).astype(jnp.bfloat16)
    grad_up_low = (grad_hidden * silu_vals).astype(jnp.bfloat16)
    grad_gate = contract_rows(second, grad_gate_low)
    grad_up = contract_rows(second, grad_up_low)
    grad_second = lax.psum(
        (contract_cols(grad_gate_low, gate_mat) + contract_cols(grad_up_low, up_mat)).astype(
            jnp.bfloat16
        ),
        "tensor",
    ).astype(jnp.float32)
    grad_mid_norm, grad_gain_two = norm_backward(grad_second, unit_two, inverse_two, full_two)
    grad_middle = grad_low.astype(jnp.float32) + grad_mid_norm
    grad_mid_low = grad_middle.astype(jnp.bfloat16)
    grad_out = contract_rows(mixed_low, grad_mid_low)
    grad_mixed = contract_cols(grad_mid_low, out_mat).astype(jnp.bfloat16)
    grad_mixed_seq = jnp.transpose(
        grad_mixed.reshape(slot_count, seq_count, heads_kv, group_size, HEAD), (1, 2, 3, 0, 4)
    )
    delta_rows = jnp.sum(grad_mixed_seq.astype(jnp.float32) * mixed_seq, axis=-1)
    kv_width = heads_kv * HEAD

    def block_grads(grad_query_acc, key_blk, value_blk, pos_blk):
        block_len = key_blk.shape[0]
        key_seq = jnp.transpose(key_blk.reshape(block_len, seq_count, heads_kv, HEAD), (1, 2, 0, 3))
        value_seq = jnp.transpose(
            value_blk.reshape(block_len, seq_count, heads_kv, HEAD), (1, 2, 0, 3)
        )
        raw_scores = (
            jnp.einsum("shgqd,shkd->shgqk", query_seq, key_seq, preferred_element_type=jnp.float32)
            * score_scale
        )
        allowed = pos_blk.T[:, None, None, None, :] <= query_pos[:, None, None, :, None]
        prob_vals = jnp.where(
            allowed,
            jnp.exp(jnp.where(allowed, raw_scores - log_total[..., None], masked_value)),
            0.0,
        )
        grad_value_blk = jnp.einsum(
            "shgqk,shgqd->kshd",
            prob_vals.astype(jnp.bfloat16),
            grad_mixed_seq,
            preferred_element_type=jnp.float32,
        )
        grad_probs = jnp.einsum(
            "shgqd,shkd->shgqk", grad_mixed_seq, value_seq, preferred_element_type=jnp.float32
        )
        grad_scores = (prob_vals * (grad_probs - delta_rows[..., None])).astype(jnp.bfloat16)
        grad_query_acc = grad_query_acc + jnp.einsum(
            "shgqk,shkd->shgqd", grad_scores, key_seq, preferred_element_type=jnp.float32
        )
        grad_key_blk = jnp.einsum(
            "shgqk,shgqd->kshd", grad_scores, query_seq, preferred_element_type=jnp.float32
        )
        return (
            grad_query_acc,
            grad_key_blk.reshape(block_len, seq_count, kv_width),
            grad_value_blk.reshape(block_len, seq_count, kv_width),
        )

    zero_query = jnp.zeros(stat_shape + (HEAD,), jnp.float32)
    key_all, value_all, pos_all = (
        lax.all_gather(keys_low, "context", axis=0, tiled=True),
        lax.all_gather(value_low, "context", axis=0, tiled=True),
        lax.all_gather(positions, "context", axis=0, tiled=True),
    )
    total_len = key_all.shape[0]
    block_size = min(512, total_len)
    block_count = total_len // block_size

    def key_block(grad_query_acc, block_items):
        key_blk, value_blk, pos_blk = block_items
        grad_query_acc, grad_key_blk, grad_value_blk = block_grads(
            grad_query_acc, key_blk, value_blk, pos_blk
        )
        return (grad_query_acc, (grad_key_blk, grad_value_blk))

    grad_query_acc, (grad_keys_all, grad_values_all) = lax.scan(
        key_block,
        zero_query,
        (
            key_all.reshape(block_count, block_size, seq_count, kv_width),
            value_all.reshape(block_count, block_size, seq_count, kv_width),
            pos_all.reshape(block_count, block_size, seq_count),
        ),
    )
    grad_key_own, grad_value_own = (
        lax.psum_scatter(
            grad_keys_all.reshape(total_len, seq_count, kv_width).astype(jnp.bfloat16),
            "context",
            scatter_dimension=0,
            tiled=True,
        ).astype(jnp.float32),
        lax.psum_scatter(
            grad_values_all.reshape(total_len, seq_count, kv_width).astype(jnp.bfloat16),
            "context",
            scatter_dimension=0,
            tiled=True,
        ).astype(jnp.float32),
    )
    grad_rot_q = jnp.transpose(grad_query_acc * score_scale, (3, 0, 1, 2, 4)).reshape(
        slot_count, seq_count, heads_q, HEAD
    )
    grad_q_low = (
        rotate(grad_rot_q, cos_part, -sin_part)
        .reshape(row_count, heads_q * HEAD)
        .astype(jnp.bfloat16)
    )
    grad_rot_k = (grad_key_own * score_scale).reshape(slot_count, seq_count, heads_kv, HEAD)
    grad_k_low = (
        rotate(grad_rot_k, cos_part, -sin_part).reshape(row_count, kv_width).astype(jnp.bfloat16)
    )
    grad_v_low = grad_value_own.reshape(row_count, kv_width).astype(jnp.bfloat16)
    grad_query = contract_rows(normed, grad_q_low)
    grad_key = contract_rows(normed, grad_k_low)
    grad_value = contract_rows(normed, grad_v_low)
    grad_normed = lax.psum(
        (
            contract_cols(grad_q_low, query_mat)
            + contract_cols(grad_k_low, key_mat)
            + contract_cols(grad_v_low, value_mat)
        ).astype(jnp.bfloat16),
        "tensor",
    ).astype(jnp.float32)
    grad_in_norm, grad_gain_one = norm_backward(grad_normed, unit_one, inverse_one, full_one)
    input_grad = (grad_middle + grad_in_norm).reshape(slot_count, seq_count, model_width)
    reduced = (
        lax.psum_scatter(grad_gain_one, ("dp", "context"), scatter_dimension=0, tiled=True),
        lax.psum_scatter(grad_gain_two, ("dp", "context"), scatter_dimension=0, tiled=True),
        lax.psum_scatter(grad_query, ("dp", "context"), scatter_dimension=0, tiled=True),
        lax.psum_scatter(grad_key, ("dp", "context"), scatter_dimension=0, tiled=True),
        lax.psum_scatter(grad_value, ("dp", "context"), scatter_dimension=0, tiled=True),
        lax.psum_scatter(grad_out, ("dp", "context"), scatter_dimension=1, tiled=True),
        lax.psum_scatter(grad_gate, ("dp", "context"), scatter_dimension=0, tiled=True),
        lax.psum_scatter(grad_up, ("dp", "context"), scatter_dimension=0, tiled=True),
        lax.psum_scatter(grad_down, ("dp", "context"), scatter_dimension=1, tiled=True),
    )
    return (
        layer_out,
        input_grad,
        reduced[0],
        reduced[1],
        reduced[2],
        reduced[3],
        reduced[4],
        reduced[5],
        reduced[6],
        reduced[7],
        reduced[8],
    )


WIDE = 128
HALF = HEAD // 2
RUN = 256
TILE = 512
LOG2_E = 1.4426950408889634
MESH = pl.DeviceIdType.MESH
PIECE = 256
FEED = 512
VMEM_LIMIT = 56 * 1024 * 1024


def any_spec():
    return pl.BlockSpec(memory_space=pl.ANY)


def vmem_spec():
    return pl.BlockSpec(memory_space=pltpu.VMEM)


def place():
    return lax.axis_index("dp"), lax.axis_index("context"), lax.axis_index("tensor")


def greet(devices):
    barrier = pltpu.get_barrier_semaphore()
    for device in devices:
        pl.semaphore_signal(barrier, inc=1, device_id=device, device_id_type=MESH)
    pl.semaphore_wait(barrier, len(devices))


def sequence_others():
    row, spot, core = place()
    return [
        (row, lax.rem(spot + shift, 8), lax.rem(core + flip, 2))
        for shift in range(8)
        for flip in range(2)
        if shift or flip
    ]


def dot_f32(left, right):
    return jnp.dot(left, right, preferred_element_type=jnp.float32)


def own_shard():
    row, spot, core = place()
    return row * 8 + spot


def group_others():
    row, spot, core = place()
    return sequence_others() + [(1 - row, lax.rem(spot + shift, 8), core) for shift in range(8)]


def exchange_messages(message_to, landing, send, recv):
    row, spot, core = place()
    copies, waits = [], []

    def one(flip, shift):
        at = flip * 8 + shift
        to_row = lax.rem(row + flip, 2)
        chip, source = lax.rem(spot + shift, 8), lax.rem(spot + 8 - shift, 8)
        device = (to_row, chip, core)
        message = message_to(to_row * 8 + chip)
        copies.append(
            remote(message, landing.at[row * 8 + spot], send.at[at], recv.at[at], device)
        )
        came = landing.at[to_row * 8 + source]
        waits.append(remote(came, came, send.at[at], recv.at[at], device).wait_recv)

    for flip in range(2):
        for shift in range(8):
            if flip or shift:
                one(flip, shift)
    return copies, waits


def turn_left(left_t, index, source):
    quarter = source.shape[1] // 4
    share = quarter // 4
    for piece in range(4):
        turned = source[:, piece * quarter : (piece + 1) * quarter].T
        for inner in range(4):
            x, z, y = piece // 2, 2 * (piece % 2) + inner // 2, inner % 2
            left_t[index, x, y, z * share : (z + 1) * share] = turned[
                inner * share : (inner + 1) * share
            ]


def remote(source, target, send, recv, device):
    return pltpu.make_async_remote_copy(
        src_ref=source,
        dst_ref=target,
        send_sem=send,
        recv_sem=recv,
        device_id=device,
        device_id_type=MESH,
    )


def move(source, target, send, recv, device, is_self):
    @pl.when(is_self)
    def _():
        pltpu.make_async_copy(source, target, recv).start()

    @pl.when(jnp.logical_not(is_self))
    def _():
        remote(source, target, send, recv, device).start()


def return_copies(ref, out, send, recv):
    row, spot, core = place()
    head = 2 * lax.rem(spot, 4) + core
    owner = spot // 4
    copies = []
    for step in range(8):
        chip = lax.rem(spot + step, 8)
        is_self = (owner == core) if step == 0 else False
        parts = (ref.at[chip], out.at[head], send.at[step], recv.at[head], (row, chip, owner))
        copies.append((parts, is_self))
    return copies


def start_return(copies):
    for parts, is_self in copies:
        if is_self is False:
            remote(*parts).start()
        else:
            move(*parts, is_self)


def finish_return(copies, out, send, recv):
    row, spot, core = place()
    for head in range(8):
        remote(
            out.at[head], out.at[head], send.at[0], recv.at[head], (row, spot, 1 - core)
        ).wait_recv()
    for parts, is_self in copies:
        if is_self is False:
            remote(*parts).wait_send()
        else:

            @pl.when(jnp.logical_not(is_self))
            def _():
                remote(*parts).wait_send()


def tile_at(index, size):
    return pl.ds(pl.multiple_of(index * size, size), size)


def causal(scores):
    keys = lax.broadcasted_iota(jnp.int32, scores.shape, 0)
    queries = lax.broadcasted_iota(jnp.int32, scores.shape, 1)
    return jnp.where(keys <= queries, scores, masked_value)


def neighbours():
    row, spot, core = place()
    level, column = spot // 2, lax.rem(spot, 2)
    beside_x = (1 - row, spot, core)
    beside_y = (row, 2 * level + 1 - column, core)
    along_z = [(row, 2 * lax.rem(level + k, 4) + column, core) for k in (1, 2, 3)]
    return row, level, column, beside_x, beside_y, along_z


class Gather:
    def __init__(self, own, whole, start, width, piece, sems):
        self.own, self.whole = own.at[:, pl.ds(start, width)], whole
        self.start, self.width = start, width
        names = ("send_z", "recv_z", "send_x", "recv_x", "send_y", "recv_y", "send_d", "recv_d")
        for name, sem in zip(names + ("local",), sems):
            setattr(self, name, sem.at[piece])

    def block(self, x, z, y, half=None):
        cut = self.width * 7 // 12 // WIDE * WIDE
        start, width = self.start, self.width
        if half == 0:
            width = cut
        elif half == 1:
            start, width = start + cut, width - cut
        return self.whole.at[x, z, y, :, pl.ds(start, width)]

    def arrived(self, target, recv_sem):
        device = neighbours()[3]
        remote(target, target, self.send_x.at[0], recv_sem, device).wait_recv()

    def copy_z(self, z, up, own=False):
        row, level, column, beside_x, beside_y = neighbours()[:5]
        core = place()[2]
        target = level + 1 if up else level - 1
        block = self.block(row, z, column)
        return remote(
            self.own if own else block,
            block,
            self.send_z.at[int(up), z],
            self.recv_z.at[z],
            (row, 2 * target + column, core),
        )

    def copies_xy(self, z, own=False):
        row, level, column, beside_x, beside_y = neighbours()[:5]
        block = self.block(row, z, column)
        source = self.own if own else block
        return [
            remote(source, block, self.send_x.at[z], self.recv_x.at[z], beside_x),
            remote(source, block, self.send_y.at[z], self.recv_y.at[z], beside_y),
        ]

    def copies_diagonal(self, z):
        row, level, column, beside_x, beside_y = neighbours()[:5]
        by_y = self.block(1 - row, z, column, 1)
        by_x = self.block(row, z, 1 - column, 0)
        return [
            remote(by_y, by_y, self.send_d.at[0, z], self.recv_d.at[0, z], beside_y),
            remote(by_x, by_x, self.send_d.at[1, z], self.recv_d.at[1, z], beside_x),
        ]

    def own_copy(self):
        row, level, column = neighbours()[:3]
        return pltpu.make_async_copy(self.own, self.block(row, level, column), self.local)

    def each_at(self, hop, act):
        level = neighbours()[1]

        @pl.when(level >= hop)
        def _():
            act(level - hop, True)

        @pl.when(level + hop <= 3)
        def _():
            act(level + hop, False)

    def start_z(self, z, up, own=False):
        level = neighbours()[1]

        @pl.when(level < 3 if up else level > 0)
        def _():
            self.copy_z(z, up, own).start()

    def place_own(self):
        self.own_copy().start()

    def open(self):
        level = neighbours()[1]
        self.start_z(level, True, True)
        self.start_z(level, False, True)
        for copy in self.copies_xy(level, True):
            copy.start()

    def hop(self, hop):
        def act(z, up):
            row, level, column = neighbours()[:3]
            self.arrived(self.block(row, z, column), self.recv_z.at[z])
            self.start_z(z, up)
            for copy in self.copies_xy(z):
                copy.start()

        self.each_at(hop, act)

    def turn_diagonal(self, z):
        row, level, column = neighbours()[:3]
        by_y, by_x = self.copies_diagonal(z)
        self.arrived(self.block(1 - row, z, column), self.recv_x.at[z])
        by_y.start()
        self.arrived(self.block(row, z, 1 - column), self.recv_y.at[z])
        by_x.start()

    def diagonal(self, hop):
        if hop == 0:
            self.turn_diagonal(neighbours()[1])
        else:
            self.each_at(hop, lambda z, up: self.turn_diagonal(z))

    def finish(self):
        row, level, column = neighbours()[:3]
        self.own_copy().wait()
        for z in range(4):
            self.arrived(self.block(1 - row, z, 1 - column, 1), self.recv_d.at[0, z])
            self.arrived(self.block(1 - row, z, 1 - column, 0), self.recv_d.at[1, z])

    def close_z(self):
        level = neighbours()[1]

        def sent(z, up):
            @pl.when(level < 3 if up else level > 0)
            def _():
                self.copy_z(z, up).wait_send()

        sent(level, True)
        sent(level, False)
        for hop in range(1, 4):
            self.each_at(hop, sent)

    def close(self):
        self.close_z()
        for z in range(4):
            for copy in self.copies_xy(z) + self.copies_diagonal(z):
                copy.wait_send()


class PlaneGather(Gather):
    def plane(self, z):
        return self.whole.at[:, z, :, :, pl.ds(self.start, self.width)]

    def copy_z(self, z, up, own=False):
        row, level, column = neighbours()[:3]
        target = level + 1 if up else level - 1
        plane = self.plane(z)
        return remote(
            plane,
            plane,
            self.send_z.at[int(up), z],
            self.recv_z.at[z],
            (row, 2 * target + column, place()[2]),
        )

    def open(self):
        for copy in self.copies_xy(neighbours()[1], True):
            copy.start()

    def spread(self):
        row, level, column = neighbours()[:3]
        self.arrived(self.block(1 - row, level, 1 - column, 1), self.recv_d.at[0, level])
        self.arrived(self.block(1 - row, level, 1 - column, 0), self.recv_d.at[1, level])
        self.own_copy().wait()
        self.start_z(level, True)
        self.start_z(level, False)

    def hop(self, hop):
        def act(z, up):
            self.arrived(self.plane(z), self.recv_z.at[z])
            self.start_z(z, up)

        self.each_at(hop, act)

    def finish(self):
        pass

    def close(self):
        level = neighbours()[1]
        self.close_z()
        for copy in self.copies_xy(level) + self.copies_diagonal(level):
            copy.wait_send()


def gather_sems(pieces):
    dma = pltpu.SemaphoreType.DMA
    shapes = [(2, 4), (4,), (4,), (4,), (4,), (4,), (2, 4), (2, 4), ()]
    return [dma((pieces,) + shape) for shape in shapes]


AT_BEGIN, AT_GAINS, AT_PAIRS, AT_QUERIES, AT_HEADS, AT_KEYS, AT_ALL, AT_SORT = 0, 1, 2, 3, 4, 5, 6, 7
AT_RETURN, AT_MIXED, AT_OUT, AT_NORM, AT_GROUP, AT_TILE, AT_FEED = 8, 9, 10, 11, 12, 16, 24
PUMPS = {
    AT_BEGIN: (1, 4, 10, 2, 5, 3, 6, 7, 11, 12, 13),
    AT_GAINS: (20,),
    AT_GROUP + 2: (14, 15, 17),
    AT_GROUP + 3: (16,),
    AT_PAIRS: (30, 70),
    AT_QUERIES: (21, 50),
    AT_GROUP + 1: (31, 22, 74, 40, 34),
    AT_HEADS: (23, 32, 75),
    AT_KEYS: (60,),
    AT_ALL: (35, 27),
    AT_SORT: (25,),
    AT_TILE + 0: (24, 33),
    AT_TILE + 2: (41, 44),
    AT_TILE + 4: (37, 71, 61, 26),
    AT_TILE + 5: (36, 42),
    AT_TILE + 6: (51,),
    AT_RETURN: (43, 52, 45, 55, 46, 54),
    AT_MIXED: (72, 47),
    AT_OUT: (53,),
    AT_NORM: (56, 62),
    AT_FEED + 1: (63, 57),
    AT_FEED + 3: (64, 67, 66, 65),
    AT_FEED + 5: (73,),
}


def forward_kernel(
    tokens,
    positions,
    freqs,
    ids_in,
    gain_one,
    gain_two,
    w_query,
    w_key,
    w_value,
    w_out_t,
    w_gate,
    w_up,
    w_down_t,
    cotangent,
    near,
    far,
    normed_out,
    q_out,
    k_out,
    v_out,
    mixed_t_out,
    lse_out,
    mixed_low_out,
    middle_out,
    second_out,
    right_out,
    gains_out,
    tables_out,
    left_out,
    order,
    ids_flat,
    near_own,
    far_own,
    unit,
    normed,
    tables,
    weight,
    gain_message,
    gain_all,
    gain_columns,
    gain_rows,
    left_t,
    q_heads,
    kv_heads,
    q_slots,
    kv_slots,
    q_t,
    keys,
    v_t,
    mixed_t,
    lse,
    mixed,
    mixed_slots,
    mixed_heads,
    mixed_low,
    out_weight,
    part,
    part_other,
    second,
    cot,
    right,
    feed_weight,
    ids_all,
    ids,
    load_own,
    send_ids,
    recv_ids,
    load_ids,
    send_gain,
    recv_gain,
    load_w,
    load_out,
    load_feed,
    load_cot,
    save_right,
    saves,
    send_q,
    recv_q,
    send_kv,
    recv_kv,
    send_x,
    recv_x,
    send_m,
    recv_m,
    send_p,
    recv_p,
    *sems,
):
    row, spot, core = place()
    low, full = jnp.bfloat16, jnp.float32
    rows, width = tokens.shape
    share = near_own.shape[0]
    length = 8 * rows
    runs, tiles = length // RUN, length // TILE
    per_device = rows // RUN
    halves = TILE // RUN
    quarter = 4 * share
    sibling = (row, spot, 1 - core)
    out_width = w_out_t.shape[1]
    qkv_width = 16 * HEAD

    near_loads, far_loads, start = [], [], 0
    for ref in (w_query, w_key, w_value, w_out_t):
        target = near_own.at[:, pl.ds(start, ref.shape[1])]
        near_loads.append(pltpu.make_async_copy(ref, target, load_own.at[len(near_loads)]))
        start += ref.shape[1]
    for index, ref in enumerate((w_gate, w_up, w_down_t)):
        for piece in range(4):
            source = ref.at[:, pl.ds(piece * FEED, FEED)]
            target = far_own.at[:, pl.ds((3 * piece + index) * FEED, FEED)]
            far_loads.append(
                pltpu.make_async_copy(source, target, load_own.at[4 + 4 * index + piece])
            )
    for copy in near_loads + far_loads:
        copy.start()
    load_cotangent = pltpu.make_async_copy(cotangent, cot, load_cot)
    load_cotangent.start()
    half = qkv_width // 2
    pairs = Gather(near_own, near, half, half, 0, sems)
    first = Gather(near_own, near, 0, half, 1, sems)
    outer = Gather(near_own, near, qkv_width, out_width, 2, sems)
    feeds = [Gather(far_own, far, 3 * FEED * p, 3 * FEED, 3 + p, sems) for p in range(3)]
    feeds.append(Gather(far_own, far, 9 * FEED, FEED, 6, sems))
    plane = PlaneGather(far_own, far, 10 * FEED, 2 * FEED, 7, sems)
    gathers = [pairs, first, outer] + feeds + [plane]

    def pump(place):
        for what in PUMPS.get(place, ()):
            gather, act = gathers[what // 10], what % 10
            if act == 0:
                gather.open()
            elif act < 4:
                gather.hop(act)
            elif gather is plane and act == 5:
                gather.spread()
            else:
                gather.diagonal(act - 4)

    gain_message[...] = jnp.zeros_like(gain_message)
    gain_message[0:1, :share] = gain_one[...].astype(full)
    gain_message[1:2, :share] = gain_two[...].astype(full)
    for copy in near_loads:
        copy.wait()
    greet(group_others())
    pairs.open()
    for gather in (pairs, first, outer):
        gather.place_own()

    gain_copies, gain_from = exchange_messages(
        lambda shard: gain_message, gain_all, send_gain, recv_gain
    )
    for copy in gain_copies:
        copy.start()
    gain_all[own_shard()] = gain_message[...]

    for shift in range(1, 8):
        remote(
            ids_in,
            ids_all.at[spot],
            send_ids.at[shift],
            recv_ids.at[shift],
            (row, lax.rem(spot + shift, 8), core),
        ).start()
    ids_all[spot] = ids_in[...]

    for copy in far_loads:
        copy.wait()
    for gather in feeds + [plane]:
        gather.place_own()
    chunk = rows // 8

    def unit_block(index, carry):
        cut = tile_at(index, chunk)
        values = tokens[cut].astype(full)
        inverse = lax.rsqrt(jnp.mean(values * values, axis=-1, keepdims=True) + epsilon)
        unit[cut] = values * inverse
        return carry

    lax.fori_loop(0, 8, unit_block, 0)
    angles = freqs[...] * positions[...].astype(full)
    tables[0] = jnp.cos(angles)
    tables[1] = jnp.sin(angles)

    pump(AT_BEGIN)
    for shift in range(1, 8):
        remote(
            ids_in,
            ids_all.at[lax.rem(spot + 8 - shift, 8)],
            send_ids.at[shift],
            recv_ids.at[shift],
            (row, lax.rem(spot + shift, 8), core),
        ).wait_recv()
    pltpu.make_async_copy(ids_all, ids, load_ids).start()
    pairs.finish()

    width = near.shape[3] * 16

    def load_group(group):
        lanes = pl.ds(group * 4 * HEAD, 4 * HEAD)
        return pltpu.make_async_copy(
            near.at[:, :, :, :, lanes], weight.at[group % 2], load_w.at[group % 2]
        )

    load_out_weight = pltpu.make_async_copy(
        near.at[:, :, :, :, pl.ds(qkv_width, out_width)], out_weight, load_out
    )
    load_group(2).start()
    load_group(3).start()
    for wait in gain_from:
        wait()
    for shard in range(16):
        gain_columns[shard * share : (shard + 1) * share] = gain_all[shard].T[:share]
    gain_rows[...] = gain_columns[...].T
    normed[...] = (unit[...] * gain_rows[0:1]).astype(low)
    pump(AT_GAINS)

    def project(group):
        load_group(group).wait()
        proj = dot_f32(normed[...], weight[group % 2].reshape(width, 4 * HEAD)).T
        for head in range(4):
            front = proj[head * HEAD : head * HEAD + HALF]
            back = proj[head * HEAD + HALF : (head + 1) * HEAD]
            if group < 3:
                front, back = (
                    front * tables[0] - back * tables[1],
                    back * tables[0] + front * tables[1],
                )
            for start, value in ((0, front.astype(low)), (HALF, back.astype(low))):
                for run in range(per_device):
                    piece = value[:, run * RUN : (run + 1) * RUN]
                    if group < 2:
                        q_heads[4 * group + head, run, start : start + HALF] = piece
                    else:
                        kv_heads[head, group - 2, run, start : start + HALF] = piece
        pump(AT_GROUP + group)

    project(2)
    project(3)

    outgoing = []
    for step in range(4):
        slot = lax.rem(spot + step, 4)
        chip = 4 * core + slot
        for other in range(2):
            is_self = jnp.logical_and(chip == spot, core == other)
            device = (row, chip, other)
            kv_parts = (
                kv_heads.at[slot, :, other],
                kv_slots.at[spot, :, other],
                send_kv.at[step, other],
                recv_kv.at[spot],
                device,
            )
            q_parts = (
                q_heads.at[2 * slot + other],
                q_slots.at[spot],
                send_q.at[step, other],
                recv_q.at[spot],
                device,
            )
            outgoing.append((kv_parts, is_self))
            outgoing.append((q_parts, is_self))
    for parts, is_self in outgoing[0::2]:
        move(*parts, is_self)
    pump(AT_PAIRS)
    first.finish()
    load_group(0).start()
    load_group(1).start()
    pump(AT_QUERIES)
    project(0)
    project(1)
    for parts, is_self in outgoing[1::2]:
        move(*parts, is_self)
    pump(AT_HEADS)

    def hand_on(source):
        block = kv_slots.at[source, :, core]
        return remote(block, block, send_x.at[source], recv_x.at[source], sibling)

    for step in range(8):
        source = lax.rem(spot + step, 8)
        block = kv_slots.at[source, :, core]
        remote(block, block, send_x.at[source], recv_kv.at[source], sibling).wait_recv()
        hand_on(source).start()
    pump(AT_KEYS)
    for step in range(8):
        remote(
            q_slots.at[step], q_slots.at[step], send_x.at[step], recv_q.at[step], sibling
        ).wait_recv()
        hand_on(step).wait()
    pump(AT_ALL)

    pltpu.make_async_copy(ids_all, ids, load_ids).wait()

    def find_run(index, carry):
        device, piece = 0, 0
        for run in range(runs):
            here = ids[run // per_device, 0, run % per_device] == index
            device = jnp.where(here, run // per_device, device)
            piece = jnp.where(here, run % per_device, piece)
        order[index, 0] = device
        order[index, 1] = piece
        found = ids[index // per_device, 0, index % per_device]
        order[runs + index, 0] = lax.div(found, per_device)
        order[runs + index, 1] = lax.rem(found, per_device)
        ids_flat[index] = found
        return carry

    lax.fori_loop(0, runs, find_run, 0)

    def sort_run(index, carry):
        device, piece = order[index, 0], order[index, 1]
        cols = tile_at(index, RUN)
        q_t[:, cols] = q_slots[device, piece]
        keys[index] = kv_slots[device, 0, piece].T
        v_t[:, cols] = kv_slots[device, 1, piece]
        return carry

    lax.fori_loop(0, runs, sort_run, 0)
    pump(AT_SORT)
    scale = HEAD ** (-0.5) * LOG2_E

    def query_tile(index, carry):
        cols = tile_at(index, TILE)
        queries = q_t[:, cols]

        def step(scores, block, peak, total, mix):
            high = jnp.maximum(peak, jnp.max(scores, axis=0, keepdims=True))
            decay = jnp.exp2(peak - high)
            weights = jnp.exp2(scores - high)
            total = total * decay + jnp.sum(weights, axis=0, keepdims=True)
            mix = mix * decay + dot_f32(v_t[:, tile_at(block, TILE)], weights.astype(low))
            return high, total, mix

        def scores_of(block):
            held = keys[pl.ds(block * halves, halves)].reshape(TILE, HEAD)
            return dot_f32(held, queries) * scale

        state = (
            jnp.full((1, TILE), masked_value, full),
            jnp.zeros((1, TILE), full),
            jnp.zeros((HEAD, TILE), full),
        )
        state = step(causal(scores_of(index)), index, *state)
        peak, total, mix = lax.fori_loop(
            0, index, lambda block, now: step(scores_of(block), block, *now), state
        )
        mix = mix / total
        mixed_t[:, cols] = mix
        lse[:, cols] = peak + jnp.log2(total)
        for half in range(halves):
            mixed[index * halves + half] = mix[:, half * RUN : (half + 1) * RUN].astype(low)

        for tile in range(tiles):

            @pl.when(index == tile)
            def _():
                pump(AT_TILE + tile)

        return carry

    lax.fori_loop(0, tiles, query_tile, 0)

    def unsort_run(run, carry):
        index = ids[run // per_device, 0, run % per_device]
        mixed_slots[run // per_device, run % per_device] = mixed[index]
        return carry

    lax.fori_loop(0, runs, unsort_run, 0)
    copies = return_copies(mixed_slots, mixed_heads, send_m, recv_m)
    start_return(copies)
    early_saves = [
        pltpu.make_async_copy(source, target, saves.at[index])
        for index, (source, target) in enumerate(
            [
                (normed, normed_out),
                (q_t, q_out),
                (keys, k_out),
                (v_t, v_out),
                (mixed_t, mixed_t_out),
                (lse, lse_out),
                (gain_rows, gains_out),
                (tables, tables_out),
            ]
        )
    ]
    for copy in early_saves:
        copy.start()
    pump(AT_RETURN)
    outer.finish()
    load_out_weight.start()
    finish_return(copies, mixed_heads, send_m, recv_m)
    pump(AT_MIXED)

    load_out_weight.wait()
    for run in range(per_device):
        side = mixed_heads[:, run].reshape(8 * HEAD, RUN)
        mixed_low[run * RUN : (run + 1) * RUN] = side.T

    def pair_copy(index):
        cut = pl.ds(index * quarter, quarter)
        return remote(
            part.at[:, cut], part_other.at[:, cut], send_p.at[index], recv_p.at[index], sibling
        )

    for index in range(4):
        block = out_weight[index // 2, 2 * (index % 2) : 2 * (index % 2) + 2]
        term = contract_cols(mixed_low[...], block.reshape(quarter, out_width))
        part[:, index * quarter : (index + 1) * quarter] = term.astype(low)
        pair_copy(index).start()
    pump(AT_OUT)
    load_cotangent.wait()
    for index in range(4):
        pair_copy(index).wait()
    chunk = rows // 8

    def norm_block(index, carry):
        cut = tile_at(index, chunk)
        sums = part[cut].astype(full) + part_other[cut].astype(full)
        values = tokens[cut].astype(full) + sums
        unit[cut] = values
        inverse = lax.rsqrt(jnp.mean(values * values, axis=-1, keepdims=True) + epsilon)
        second[cut] = (values * inverse * gain_rows[1:2]).astype(low)
        return carry

    lax.fori_loop(0, 8, norm_block, 0)
    late_saves = [
        pltpu.make_async_copy(source, target, saves.at[8 + index])
        for index, (source, target) in enumerate(
            [(mixed_low, mixed_low_out), (unit, middle_out), (second, second_out)]
        )
    ]
    for copy in late_saves:
        copy.start()
    pump(AT_NORM)

    def load_feed_weight(index, kind):
        piece, half = index // 2, lax.rem(index, 2)
        start = (3 * piece + kind) * FEED + half * PIECE
        lanes = pl.ds(pl.multiple_of(start, PIECE), PIECE)
        return pltpu.make_async_copy(
            far.at[:, :, :, :, lanes], feed_weight.at[half, kind], load_feed.at[half, kind]
        )

    def save_piece(piece):
        lanes = pl.ds(piece * 3 * FEED, 3 * FEED)
        return pltpu.make_async_copy(
            right.at[:, lanes], right_out.at[:, lanes], save_right.at[piece]
        )

    def feed_block(index, carry):
        piece, half = index // 2, lax.rem(index, 2)
        for when in range(4):

            @pl.when(index == 2 * when)
            def _():
                feeds[when].finish()

        @pl.when(half == 0)
        def _():
            for offset in range(2):
                for kind in range(3):
                    load_feed_weight(index + offset, kind).start()

        values = []
        for kind, left in enumerate((second, second, cot)):
            load_feed_weight(index, kind).wait()
            values.append(dot_f32(left[...], feed_weight[half, kind].reshape(width, PIECE)))
        gate, up, grad_hidden = values
        sigmoid = jax.nn.sigmoid(gate)
        silu = gate * sigmoid
        grad_gate = grad_hidden * up * sigmoid * (1.0 + gate * (1.0 - sigmoid))
        for when, source in ((1, second), (3, cot)):

            @pl.when(index == when)
            def _():
                turn_left(left_t, when % 3, source)

        for kind, value in enumerate((grad_gate, grad_hidden * silu, silu * up)):
            start = (3 * piece + kind) * FEED + half * PIECE
            right[:, pl.ds(pl.multiple_of(start, PIECE), PIECE)] = value.astype(low)

        for when in range(8):

            @pl.when(index == when)
            def _():
                pump(AT_FEED + when)

        for when in range(4):

            @pl.when(index == 2 * when + 1)
            def _():
                save_piece(when).start()

        return carry

    lax.fori_loop(0, 8, feed_block, 0)
    save_left = pltpu.make_async_copy(left_t, left_out, saves.at[11])
    save_left.start()
    for gather in gathers:
        gather.close()
    for parts, is_self in outgoing:

        @pl.when(jnp.logical_not(is_self))
        def _():
            remote(*parts).wait_send()

    for shift in range(1, 8):
        remote(
            ids_in,
            ids_all.at[spot],
            send_ids.at[shift],
            recv_ids.at[shift],
            (row, lax.rem(spot + shift, 8), core),
        ).wait_send()
    for copy in gain_copies:
        copy.wait_send()
    for copy in early_saves + late_saves + [save_left] + [save_piece(piece) for piece in range(4)]:
        copy.wait()


def forward(
    tokens,
    positions,
    ids,
    gain_one,
    gain_two,
    w_query,
    w_key,
    w_value,
    w_out_t,
    w_gate,
    w_up,
    w_down_t,
    cotangent,
):
    dma = pltpu.SemaphoreType.DMA
    vmem = pltpu.VMEM
    low, full = jnp.bfloat16, jnp.float32
    rows, width = tokens.shape
    share, hidden_width = w_gate.shape
    out_width = w_out_t.shape[1]
    near_width = 16 * HEAD + out_width
    length = 8 * rows
    per_device = rows // RUN
    heads = (8, per_device, HEAD, RUN)
    both = (2, per_device, HEAD, RUN)
    by_run = (length // RUN, RUN, HEAD)
    flat = (HEAD, length)
    smem_spec = pl.BlockSpec(memory_space=pltpu.SMEM)
    shape = jax.ShapeDtypeStruct
    return pl.pallas_call(
        forward_kernel,
        in_specs=[vmem_spec()] * 6 + [any_spec()] * 8,
        out_specs=[any_spec()] * 15 + [smem_spec] * 2,
        out_shape=[
            shape((2, 4, 2, share, near_width), low),
            shape((2, 4, 2, share, 3 * hidden_width), low),
            shape((rows, width), low),
            shape(flat, low),
            shape(by_run, low),
            shape(flat, low),
            shape(flat, full),
            shape((1, length), full),
            shape((rows, out_width), low),
            shape((rows, width), full),
            shape((rows, width), low),
            shape((rows, 3 * hidden_width), low),
            shape((8, width), full),
            shape((2, HALF, rows), full),
            shape((2, 2, 2, 4 * share, rows), low),
            shape((2 * length // RUN, 2), jnp.int32),
            shape((length // RUN,), jnp.int32),
        ],
        scratch_shapes=[
            vmem((share, near_width), low),
            vmem((share, 3 * hidden_width), low),
            vmem((rows, width), full),
            vmem((rows, width), low),
            vmem((2, HALF, rows), full),
            vmem((2, 2, 4, 2, share, 4 * HEAD), low),
            vmem((8, WIDE), full),
            vmem((16, 8, WIDE), full),
            vmem((width, 8), full),
            vmem((8, width), full),
            vmem((2, 2, 2, 4 * share, rows), low),
            vmem(heads, low),
            vmem((4,) + both, low),
            vmem(heads, low),
            vmem((8,) + both, low),
            vmem(flat, low),
            vmem(by_run, low),
            vmem(flat, low),
            vmem(flat, full),
            vmem((1, length), full),
            vmem((length // RUN, HEAD, RUN), low),
            vmem(heads, low),
            vmem(heads, low),
            vmem((rows, out_width), low),
            vmem((2, 4, 2, share, out_width), low),
            vmem((rows, width), low),
            vmem((rows, width), low),
            vmem((rows, width), low),
            vmem((rows, width), low),
            vmem((rows, 3 * hidden_width), low),
            vmem((2, 3, 2, 4, 2, share, PIECE), low),
            vmem((8, 8, WIDE), jnp.int32),
            pltpu.SMEM((8, 8, WIDE), jnp.int32),
            dma((16,)),
            dma((8,)),
            dma((8,)),
            dma(()),
            dma((16,)),
            dma((16,)),
            dma((2,)),
            dma(()),
            dma((2, 3)),
            dma(()),
            dma((4,)),
            dma((12,)),
            dma((4, 2)),
            dma((8,)),
            dma((4, 2)),
            dma((8,)),
            dma((8,)),
            dma((8,)),
            dma((8,)),
            dma((8,)),
            dma((4,)),
            dma((4,)),
        ]
        + gather_sems(8),
        compiler_params=pltpu.CompilerParams(
            collective_id=1, has_side_effects=True, vmem_limit_bytes=VMEM_LIMIT
        ),
        name="forward",
    )(
        tokens,
        positions,
        (theta_base ** (-2.0 * jnp.arange(HALF, dtype=jnp.float32) / HEAD)).reshape(HALF, 1),
        ids,
        gain_one,
        gain_two,
        w_query,
        w_key,
        w_value,
        w_out_t,
        w_gate,
        w_up,
        w_down_t,
        cotangent,
    )


SECOND, THIRD, LAST = 2, 4, 5


class Reduce:
    def __init__(self, n, changes, refs):
        (
            self.left_t,
            self.right,
            self.own,
            self.out,
            self.save,
            self.send_one,
            self.recv_one,
            self.send_two,
            self.recv_two,
            self.kept,
            self.recv_three,
            self.ss_one,
            self.rs_one,
            self.ss_two,
            self.rs_two,
            self.ss_three,
            self.rs_three,
        ) = refs
        self.n, self.changes = n, changes
        self.share = self.own.shape[1]

    def columns(self, step, kind):
        held = self.right.shape[1] // (2 * PIECE)
        start = lax.rem(step, held) * 2 * PIECE + kind * PIECE
        return pl.ds(pl.multiple_of(start, PIECE), PIECE)

    def saving(self, step):
        slot = lax.rem(step, 2)
        pieces = self.changes[0] // 3
        place = jnp.where(step < self.changes[0], lax.rem(step, 3) * pieces + step // 3, step)
        cut = pl.ds(pl.multiple_of(place * 2 * PIECE, 2 * PIECE), 2 * PIECE)
        return pltpu.make_async_copy(self.own.at[slot], self.out.at[:, cut], self.save.at[slot])

    def product(self, step, kind, x, y):
        left = jnp.where(lax.rem(step, 3) == 2, 0, 1)
        left = jnp.where(step >= self.changes[0], 2, left)
        left = jnp.where(step >= self.changes[1], 0, left)
        term = jnp.dot(
            self.left_t[left, x, y],
            self.right[:, self.columns(step, kind)],
            preferred_element_type=jnp.float32,
        )
        return term

    def x_first(self, step, kind):
        return 1 if kind == 0 else jnp.where(lax.rem(step, 5) == 4, 1, 0)

    def beside(self, by_x):
        row, level, column = neighbours()[:3]
        core = place()[2]
        other_row = by_x * (1 - row) + (1 - by_x) * row
        other_column = by_x * column + (1 - by_x) * (1 - column)
        return (other_row, 2 * level + other_column, core)

    def first_copy(self, step, kind):
        out, into = lax.rem(step, 3), lax.rem(step, 6)
        return remote(
            self.send_one.at[out, kind],
            self.recv_one.at[into, kind],
            self.ss_one.at[out, kind],
            self.rs_one.at[into, kind],
            self.beside(self.x_first(step, kind)),
        )

    def second_copy(self, step, kind):
        out, into = lax.rem(step, 3), lax.rem(step, 6)
        return remote(
            self.send_two.at[out, kind],
            self.recv_two.at[into, kind],
            self.ss_two.at[out, kind],
            self.rs_two.at[into, kind],
            self.beside(1 - self.x_first(step, kind)),
        )

    def third_copy(self, step, kind, k):
        row, level, column, beside_x, beside_y, along_z = neighbours()
        target = lax.rem(level + k + 1, 4)
        out, into = lax.rem(step, 4), lax.rem(step, 4)
        return remote(
            self.kept.at[out, kind, pl.ds(pl.multiple_of(target * self.share, 16), self.share)],
            self.recv_three.at[into, kind, k],
            self.ss_three.at[out, kind, k],
            self.rs_three.at[into, kind, k],
            along_z[k],
        )

    def pieces(self, step, act):
        act(0)

        @pl.when(step < self.n - 1)
        def _():
            act(1)

    def first(self, step):
        row, level, column = neighbours()[:3]
        slot = lax.rem(step, 3)

        def act(kind):
            by_x = self.x_first(step, kind)
            for half in range(2):
                x = by_x * (1 - row) + (1 - by_x) * half
                y = by_x * half + (1 - by_x) * (1 - column)
                self.send_one[slot, kind, half] = self.product(step, kind, x, y).astype(
                    jnp.bfloat16
                )
            self.first_copy(step, kind).start()

        self.pieces(step, act)

    def second(self, step):
        row, level, column = neighbours()[:3]
        slot, came, keep = lax.rem(step, 3), lax.rem(step, 6), lax.rem(step, 4)
        self.pieces(step, lambda kind: self.first_copy(step, kind).wait())

        def act(kind):
            by_x = self.x_first(step, kind)
            x = by_x * row + (1 - by_x) * (1 - row)
            y = by_x * (1 - column) + (1 - by_x) * column
            arrived = self.recv_one.at[came, kind]
            mine = by_x * column + (1 - by_x) * row
            away = self.product(step, kind, x, y) + arrived[1 - mine].astype(jnp.float32)
            self.send_two[slot, kind] = away.astype(jnp.bfloat16)
            here = self.product(step, kind, row, column) + arrived[mine].astype(jnp.float32)
            self.kept[keep, kind] = here.astype(jnp.bfloat16)

        self.pieces(step, act)
        self.pieces(step, lambda kind: self.second_copy(step, kind).start())

    def third(self, step):
        came, keep = lax.rem(step, 6), lax.rem(step, 4)

        def act(kind):
            self.second_copy(step, kind).wait()
            here = self.kept[keep, kind].astype(jnp.float32) + self.recv_two[came, kind].astype(
                jnp.float32
            )
            self.kept[keep, kind] = here.astype(jnp.bfloat16)
            for k in range(3):
                self.third_copy(step, kind, k).start()

        self.pieces(step, act)

    def last(self, step):
        level = neighbours()[1]
        came, keep = lax.rem(step, 4), lax.rem(step, 4)
        mine = pl.ds(pl.multiple_of(level * self.share, 16), self.share)

        @pl.when(step >= 2)
        def _():
            self.saving(step - 2).wait()

        def act(kind):
            total = self.kept[keep, kind, mine].astype(jnp.float32)
            for k in range(3):
                self.third_copy(step, kind, k).wait()
                total = total + self.recv_three[came, kind, k].astype(jnp.float32)
            self.own[lax.rem(step, 2), :, kind * PIECE : (kind + 1) * PIECE] = total

        self.pieces(step, act)
        self.saving(step).start()

    def turn(self, step):
        for stage, lag in (
            (self.first, 0),
            (self.second, SECOND),
            (self.third, THIRD),
            (self.last, LAST),
        ):

            @pl.when(jnp.logical_and(step >= lag, step < self.n + lag))
            def _():
                stage(step - lag)


def backward_kernel(
    order,
    ids,
    q_in,
    k_in,
    v_in,
    mixed_t_in,
    lse_in,
    cotangent,
    left_in,
    normed_in,
    right_in,
    mixed_low,
    middle,
    near,
    far,
    tokens,
    gains_in,
    tables,
    input_grad,
    layer_out,
    grads,
    gain_out,
    q,
    q_t,
    k,
    k_t,
    v,
    d_own,
    d_slots,
    d,
    d_t,
    dq_t,
    lse,
    delta,
    dk,
    dv,
    dq_slots,
    dkv_sorted,
    dkv_slots,
    dkv_other,
    dq_own,
    dkv_own,
    weight,
    middle_ring,
    input_ring,
    part,
    part_other,
    total,
    staged,
    grad_mid,
    gain_two_grad,
    left_t,
    right,
    gain_columns,
    gain_messages,
    gain_all,
    own,
    send_one,
    recv_one,
    send_two,
    recv_two,
    kept,
    recv_three,
    loads,
    load_first,
    send_gain,
    recv_gain,
    load_left_sem,
    load_w,
    load_ring,
    save_rows,
    save_sem,
    send_d,
    recv_d,
    send_q,
    recv_q,
    send_x,
    recv_x,
    send_k,
    recv_k,
    send_p,
    recv_p,
    save,
    *sems,
):
    row, spot, core = place()
    low, full = jnp.bfloat16, jnp.float32
    rows, width = staged.shape
    length = 8 * rows
    runs, tiles = length // RUN, length // TILE
    per_device = rows // RUN
    halves = TILE // RUN
    share = width // 16
    quarter = 4 * share
    sibling = (row, spot, 1 - core)
    qkv_width = 16 * HEAD
    out_width = mixed_low.shape[1]
    n = grads.shape[1] // (2 * PIECE)
    near_at = right_in.shape[1] // (2 * PIECE)
    changes = (near_at, near_at + qkv_width // (2 * PIECE))
    sums = Reduce(
        n,
        changes,
        (left_t, right, own, grads, save)
        + (send_one, recv_one, send_two, recv_two, kept, recv_three)
        + sems,
    )

    def stage(source):
        return pltpu.make_async_copy(source, staged, load_left_sem)

    early_loads = [
        pltpu.make_async_copy(source, target, loads.at[index])
        for index, (source, target) in enumerate(
            [
                (q_in, q_t),
                (k_in, k),
                (v_in, d_t),
                (mixed_t_in, dq_t),
                (lse_in, lse),
                (middle, total),
            ]
        )
    ]

    first_loads = [
        pltpu.make_async_copy(left_in, left_t.at[pl.ds(0, 2)], load_first.at[4])
    ] + [
        pltpu.make_async_copy(
            right_in.at[:, pl.ds(3 * FEED * piece, 3 * FEED)],
            right.at[:, pl.ds(3 * FEED * piece, 3 * FEED)],
            load_first.at[piece],
        )
        for piece in range(4)
    ]


    def load_block(index, piece, part_of, start):
        lanes = pl.ds(3 * FEED * piece + start + part_of * PIECE, PIECE)
        levels = pl.ds(2 * lax.rem(index, 2), 2)
        return pltpu.make_async_copy(
            far.at[index // 2, levels, :, :, lanes], held_block(piece, part_of), load_w.at[piece]
        )

    def held_block(piece, part_of):
        levels = pl.ds(2 * (part_of % 2), 2)
        return weight.at[piece, part_of // 2, levels, :, :, pl.ds(0, PIECE)]

    def load_blocks(index, piece, start, parts):
        for part_of in range(parts):
            load_block(index, piece, part_of, start).start()

    def row_products(start, parts, landing):
        def block(index, carry):
            term = jnp.zeros((rows, quarter), full)
            for piece in range(4):
                for part_of in range(parts):
                    load_block(index, piece, part_of, start).wait()
                for part_of in range(parts):
                    at = 3 * FEED * piece + start + part_of * PIECE
                    term = term + contract_cols(
                        right[:, at : at + PIECE],
                        held_block(piece, part_of)[...].reshape(quarter, PIECE),
                    )

                @pl.when(index + 1 < 4)
                def _():
                    load_blocks(index + 1, piece, start, parts)

            part[:, tile_at(index, quarter)] = term.astype(low)
            pair_copy(index, landing).start()
            return carry

        lax.fori_loop(0, 4, block, 0)

    def pair_copy(index, landing):
        cut = pl.ds(pl.multiple_of(index * quarter, quarter), quarter)
        return remote(
            part.at[:, cut],
            part_other.at[landing, :, cut],
            send_p.at[index],
            recv_p.at[landing, index],
            sibling,
        )

    def second_back():
        row_products(0, 4, 0)
        for index in range(2):
            load_out_weight(index).start()

    def load_out_weight(index):
        lanes = pl.ds(qkv_width + index * 4 * HEAD, 4 * HEAD)
        return pltpu.make_async_copy(
            near.at[:, :, :, :, lanes], weight.at[index], load_w.at[index]
        )

    d_copies = []
    for step in range(4):
        slot = lax.rem(spot + step, 4)
        chip = 4 * core + slot
        for other in range(2):
            parts = (
                d_own.at[2 * slot + other],
                d_slots.at[spot],
                send_d.at[step, other],
                recv_d.at[spot],
                (row, chip, other),
            )
            d_copies.append((parts, jnp.logical_and(chip == spot, core == other)))

    def middle_back():
        for index in range(4):
            pair_copy(index, 0).wait()
        early_loads[5].wait()
        stage(cotangent).wait()
        chunk = rows // 8

        def block(index, gain_grad):
            cut = tile_at(index, chunk)
            grad = part[cut].astype(full) + part_other[0, cut].astype(full)
            values = total[cut]
            inverse = lax.rsqrt(jnp.mean(values * values, axis=-1, keepdims=True) + epsilon)
            unit = values * inverse
            scaled = grad * gains_in[1:2]
            mean = jnp.mean(scaled * unit, axis=-1, keepdims=True)
            result = staged[cut].astype(full) + inverse * (scaled - unit * mean)
            total[cut] = result
            grad_mid[cut] = result.astype(low)
            return gain_grad + jnp.sum(grad * unit, axis=0, keepdims=True)

        gain_two_grad[...] = lax.fori_loop(0, 8, block, jnp.zeros((1, width), full))
        for index in range(2):
            load_out_weight(index).wait()
            grad = dot_f32(grad_mid[...], weight[index].reshape(width, 4 * HEAD)).T.astype(low)
            for head in range(4):
                for run in range(per_device):
                    d_own[4 * index + head, run] = grad[
                        head * HEAD : (head + 1) * HEAD, run * RUN : (run + 1) * RUN
                    ]
        for parts, is_self in d_copies:
            move(*parts, is_self)


    def prepare():
        for copy in early_loads[:5]:
            copy.wait()
        for index in range(tiles):
            cut = pl.ds(index * TILE, TILE)
            q[cut] = q_t[:, cut].T
            k_t[:, cut] = k[halves * index : halves * (index + 1)].reshape(TILE, HEAD).T
            v[cut] = d_t[:, cut].T

    def take_cotangents():
        for index in range(8):
            remote(
                d_slots.at[index], d_slots.at[index], send_d.at[0, 0], recv_d.at[index], sibling
            ).wait_recv()

        def sort_run(index, carry):
            cols = tile_at(index, RUN)
            run = d_slots[order[index, 0], order[index, 1]]
            d_t[:, cols] = run
            d[cols] = run.T
            delta[:, cols] = jnp.sum(run.astype(full) * dq_t[:, cols], axis=0, keepdims=True)
            return carry

        lax.fori_loop(0, runs, sort_run, 0)
        dq_t[...] = jnp.zeros_like(dq_t)

    scale = HEAD ** (-0.5)

    def key_tile(block):
        cut = tile_at(block, TILE)
        both = pl.ds(block * halves, halves)
        keys, values = k[both].reshape(TILE, HEAD), v[cut]
        keys_t = k_t[:, cut]
        dk[...] = jnp.zeros_like(dk)
        dv[...] = jnp.zeros_like(dv)

        def query_tile(index, diagonal):
            cols = tile_at(index, TILE)
            scores = dot_f32(keys, q_t[:, cols]) * (scale * LOG2_E)
            if diagonal:
                scores = causal(scores)
            probs = jnp.exp2(scores - lse[:, cols])
            dv[...] += dot_f32(probs.astype(low), d[cols])
            grad_probs = dot_f32(values, d_t[:, cols])
            grad_scores = (probs * (grad_probs - delta[:, cols])).astype(low)
            dk[...] += dot_f32(grad_scores, q[cols])
            dq_t[:, cols] += dot_f32(keys_t, grad_scores)

        query_tile(block, True)

        def later(index, inner):
            query_tile(index, False)
            return inner

        lax.fori_loop(block + 1, tiles, later, 0)
        for kind, value in enumerate(((dk[...] * scale).T.astype(low), dv[...].T.astype(low))):
            for half in range(halves):
                dkv_sorted[block * halves + half, kind] = value[:, half * RUN : (half + 1) * RUN]

    def key_tiles(start, stop):
        def one(block, carry):
            key_tile(block)
            return carry

        lax.fori_loop(start, stop, one, 0)

    swap = remote(dkv_slots.at[:, :, 1 - core], dkv_other, send_x, recv_x, sibling)
    dq_copies = return_copies(dq_slots, dq_own, send_q, recv_q)
    slot, owner = lax.rem(spot, 4), spot // 4
    dkv_copies = []
    for step in range(8):
        chip = lax.rem(spot + step, 8)
        parts = (
            dkv_slots.at[:, chip, core],
            dkv_own.at[slot, :, core],
            send_k.at[step],
            recv_k.at[slot, core],
            (row, chip, owner),
        )
        dkv_copies.append((parts, (owner == core) if step == 0 else False))

    def send_back():
        def unsort_run(run, carry):
            index = ids[run]
            for kind in range(2):
                dkv_slots[kind, run // per_device, run % per_device] = dkv_sorted[index, kind]
            return carry

        lax.fori_loop(0, runs, unsort_run, 0)
        swap.start()

        def turn_run(index, carry):
            value = dq_t[:, tile_at(index, RUN)] * scale
            d_slots[index // per_device, index % per_device] = value.astype(low)
            return carry

        lax.fori_loop(0, runs, turn_run, 0)

        def unsort_queries(run, carry):
            value = d_slots[order[runs + run, 0], order[runs + run, 1]]
            dq_slots[run // per_device, run % per_device] = value
            return carry

        lax.fori_loop(0, runs, unsort_queries, 0)
        start_return(dq_copies)

    def add_pairs():
        swap.wait()
        for chip in range(8):
            both = dkv_slots[:, chip, core].astype(full) + dkv_other[:, chip].astype(full)
            dkv_slots[:, chip, core] = both.astype(low)
        start_return(dkv_copies)


    def feed_forward():
        row_products(2 * FEED, 2, 1)
        for group in range(4):
            load_group(group).start()

    save_layer = pltpu.make_async_copy(part, layer_out, save_sem)

    def finish_layer():
        for index in range(4):
            pair_copy(index, 1).wait()
        pieces = width // PIECE

        def load_piece(index):
            lanes = pl.ds(index * PIECE, PIECE)
            return pltpu.make_async_copy(
                middle.at[:, lanes], middle_ring.at[index % 2], load_ring.at[index % 2]
            )

        load_piece(0).start()
        for index in range(pieces):
            if index + 1 < pieces:
                load_piece(index + 1).start()
            load_piece(index).wait()
            cut = pl.ds(index * PIECE, PIECE)
            value = part[:, cut].astype(full) + part_other[1, :, cut].astype(full)
            part[:, cut] = (value + middle_ring[index % 2]).astype(low)
        save_layer.start()


    def load_group(group):
        lanes = pl.ds(group * 4 * HEAD, 4 * HEAD)
        return pltpu.make_async_copy(
            near.at[:, :, :, :, lanes], weight.at[group], load_w.at[group]
        )

    load_mixed = pltpu.make_async_copy(
        mixed_low, right.at[:, pl.ds(qkv_width, out_width)], loads.at[0]
    )

    def project_back():
        load_mixed.start()
        for head in range(8):
            remote(
                dq_own.at[head], dq_own.at[head], send_q.at[0], recv_q.at[head], sibling
            ).wait_recv()
        for slot_in in range(4):
            for core_in in range(2):
                target = dkv_own.at[slot_in, :, core_in]
                remote(
                    target, target, send_k.at[0], recv_k.at[slot_in, core_in], sibling
                ).wait_recv()
        for group in range(4):
            for run in range(per_device):
                cols = slice(run * RUN, (run + 1) * RUN)
                turned = []
                for head in range(4):
                    if group < 2:
                        value = dq_own[4 * group + head, run]
                    else:
                        value = dkv_own[head, group - 2, run]
                    if group < 3:
                        front, back = value[:HALF].astype(full), value[HALF:].astype(full)
                        cos_part, sin_part = tables[0, :, cols], tables[1, :, cols]
                        turned.append((front * cos_part + back * sin_part).astype(low))
                        turned.append((back * cos_part - front * sin_part).astype(low))
                    else:
                        turned.append(value)
                right[cols, group * 4 * HEAD : (group + 1) * 4 * HEAD] = jnp.concatenate(
                    turned, axis=0
                ).T
        load_mixed.wait()

    def project_normed():
        save_layer.wait()
        for group in range(4):
            load_group(group).wait()
        stage(tokens).start()

        def block(index, carry):
            term = jnp.zeros((rows, quarter), full)
            for group in range(4):
                held = weight[group, index // 2, pl.ds(2 * lax.rem(index, 2), 2)]
                term = term + contract_cols(
                    right[:, group * 4 * HEAD : (group + 1) * 4 * HEAD],
                    held.reshape(quarter, 4 * HEAD),
                )
            part[:, tile_at(index, quarter)] = term.astype(low)
            pair_copy(index, 0).start()
            return carry

        lax.fori_loop(0, 4, block, 0)

    def save_input(index):
        cut = tile_at(index, rows // 8)
        slot = lax.rem(index, 2)
        return pltpu.make_async_copy(
            input_ring.at[slot], input_grad.at[cut], save_rows.at[slot]
        )

    def norm_back():
        stage(tokens).wait()
        for index in range(4):
            pair_copy(index, 0).wait()
        chunk = rows // 8

        def block(index, gain_grad):
            cut = tile_at(index, chunk)
            grad = part[cut].astype(full) + part_other[0, cut].astype(full)
            values = staged[cut].astype(full)
            inverse = lax.rsqrt(jnp.mean(values * values, axis=-1, keepdims=True) + epsilon)
            unit = values * inverse
            scaled = grad * gains_in[0:1]
            mean = jnp.mean(scaled * unit, axis=-1, keepdims=True)
            result = total[cut] + inverse * (scaled - unit * mean)

            @pl.when(index >= 2)
            def _():
                save_input(index - 2).wait()

            input_ring[lax.rem(index, 2)] = result.reshape(chunk, 1, width)
            save_input(index).start()
            return gain_grad + jnp.sum(grad * unit, axis=0, keepdims=True)

        gain_one_grad = lax.fori_loop(0, 8, block, jnp.zeros((1, width), full))
        lines = jnp.concatenate(
            [gain_one_grad, gain_two_grad[...], jnp.zeros((6, width), full)], axis=0
        )
        gain_columns[...] = lines.T
        for shard in range(16):
            held = gain_columns[shard * share : (shard + 1) * share]
            gain_messages[shard] = jnp.pad(held, ((0, WIDE - share), (0, 0))).T
        for copy in gain_copies:
            copy.start()
        gain_all[own_shard()] = gain_messages[own_shard()]

    gain_copies, gain_from = exchange_messages(
        lambda shard: gain_messages.at[shard], gain_all, send_gain, recv_gain
    )

    def finish_gains():
        for wait in gain_from:
            wait()
        gain_out[...] = jnp.sum(gain_all[...], axis=0)

    def take_normed():
        stage(normed_in).start()
        stage(normed_in).wait()
        turn_left(left_t, 2, staged)

    def start_forward():
        for piece in range(4):
            load_blocks(0, piece, 2 * FEED, 2)

    for copy in first_loads:
        copy.start()
    stage(cotangent).start()
    for piece in range(4):
        load_blocks(0, piece, 0, 4)
    for copy in early_loads:
        copy.start()
    greet(group_others())
    first_loads[0].wait()
    first_loads[1].wait()

    def wait_right():
        for copy in first_loads[2:]:
            copy.wait()

    plan = {
        2: [wait_right, second_back],
        3: [middle_back],
        4: [prepare],
        5: [start_forward, take_cotangents],
    }
    tiles_from, tile_ranges = 5, ((0, 1), (1, 2), (2, 3), (3, 5), (5, 8))
    later = {
        9: [send_back],
        11: [add_pairs, feed_forward, finish_layer, take_normed],
        12: [project_back],
        15: [lambda: turn_left(left_t, 0, grad_mid), project_normed],
        16: [norm_back],
        n + LAST - 1: [finish_gains],
    }

    def run(step, carry):
        for when, tasks in plan.items():

            @pl.when(step == when)
            def _():
                for task in tasks:
                    task()

        @pl.when(jnp.logical_and(step >= tiles_from, step < tiles_from + len(tile_ranges)))
        def _():
            start, stop = 0, 0
            for index, (first_tile, past_tile) in enumerate(tile_ranges):
                start = jnp.where(step == tiles_from + index, first_tile, start)
                stop = jnp.where(step == tiles_from + index, past_tile, stop)
            key_tiles(start, stop)

        for when, tasks in later.items():

            @pl.when(step == when)
            def _():
                for task in tasks:
                    task()

        sums.turn(step)
        return carry

    lax.fori_loop(0, n + LAST, run, 0)
    for index in (6, 7):
        save_input(index).wait()
    for copy in gain_copies:
        copy.wait_send()
    for step in (n - 2, n - 1):
        sums.saving(step).wait()
    for copies in (d_copies, dq_copies, dkv_copies):
        for parts, is_self in copies:
            if is_self is False:
                remote(*parts).wait_send()
            else:

                @pl.when(jnp.logical_not(is_self))
                def _():
                    remote(*parts).wait_send()


def backward(order, ids, *arrays):
    dma = pltpu.SemaphoreType.DMA
    vmem = pltpu.VMEM
    low, full = jnp.bfloat16, jnp.float32
    q_sorted, k_sorted, v_sorted, mixed_t, lse, cotangent, left, normed, right = arrays[:9]
    mixed_low, middle, near, far, tokens, gains, tables = arrays[9:]
    rows, width = cotangent.shape
    length = 8 * rows
    share = width // 16
    wide = right.shape[1] + 16 * HEAD + mixed_low.shape[1] + PIECE
    quarter = 4 * share
    per_device = rows // RUN
    heads = (8, per_device, HEAD, RUN)
    tall, flat = (length, HEAD), (HEAD, length)
    by_run = (length // RUN, RUN, HEAD)
    block = (rows, width)
    smem_spec = pl.BlockSpec(memory_space=pltpu.SMEM)
    shape = jax.ShapeDtypeStruct
    return pl.pallas_call(
        backward_kernel,
        in_specs=[smem_spec] * 2 + [any_spec()] * 14 + [vmem_spec()] * 2,
        out_specs=[any_spec()] * 3 + [vmem_spec()],
        out_shape=[
            shape((rows, 1, width), full),
            shape(block, low),
            shape((share, wide), full),
            shape((8, WIDE), full),
        ],
        scratch_shapes=[
            vmem(tall, low),
            vmem(flat, low),
            vmem(by_run, low),
            vmem(flat, low),
            vmem(tall, low),
            vmem(heads, low),
            vmem(heads, low),
            vmem(tall, low),
            vmem(flat, low),
            vmem(flat, full),
            vmem((1, length), full),
            vmem((1, length), full),
            vmem((TILE, HEAD), full),
            vmem((TILE, HEAD), full),
            vmem(heads, low),
            vmem((length // RUN, 2, HEAD, RUN), low),
            vmem((2,) + heads, low),
            vmem((2, 8, HEAD, RUN), low),
            vmem(heads, low),
            vmem((4, 2, per_device, HEAD, RUN), low),
            vmem((4, 2, 4, 2, share, 4 * HEAD), low),
            vmem((2, rows, PIECE), full),
            vmem((2, rows // 8, 1, width), full),
            vmem(block, low),
            vmem((2,) + block, low),
            vmem(block, full),
            vmem(block, low),
            vmem(block, low),
            vmem((1, width), full),
            vmem((3, 2, 2, quarter, rows), low),
            vmem(right.shape, low),
            vmem((width, 8), full),
            vmem((16, 8, WIDE), full),
            vmem((16, 8, WIDE), full),
            vmem((2, share, 2 * PIECE), full),
            vmem((3, 2, 2, quarter, PIECE), low),
            vmem((6, 2, 2, quarter, PIECE), low),
            vmem((3, 2, quarter, PIECE), low),
            vmem((6, 2, quarter, PIECE), low),
            vmem((4, 2, quarter, PIECE), low),
            vmem((4, 2, 3, share, PIECE), low),
            dma((7,)),
            dma((5,)),
            dma((16,)),
            dma((16,)),
            dma(()),
            dma((4,)),
            dma((2,)),
            dma((2,)),
            dma(()),
            dma((4, 2)),
            dma((8,)),
            dma((8,)),
            dma((8,)),
            dma(()),
            dma(()),
            dma((8,)),
            dma((4, 2)),
            dma((4,)),
            dma((2, 4)),
            dma((2,)),
            dma((3, 2)),
            dma((6, 2)),
            dma((3, 2)),
            dma((6, 2)),
            dma((4, 2, 3)),
            dma((4, 2, 3)),
        ],
        compiler_params=pltpu.CompilerParams(
            collective_id=2, has_side_effects=True, vmem_limit_bytes=62 * 1024 * 1024
        ),
        name="backward",
    )(
        order,
        ids,
        *arrays,
    )


def by_heads(
    tokens,
    positions,
    gain_one,
    gain_two,
    w_query,
    w_key,
    w_value,
    w_out,
    w_gate,
    w_up,
    w_down,
    cotangent,
):
    rows, _, width = tokens.shape
    share = gain_one.shape[0]
    run_ids = positions[::RUN, 0] // RUN
    flat_in = tokens.reshape(rows, width)
    (
        near,
        far,
        normed,
        q_sorted,
        k_sorted,
        v_sorted,
        mixed_t,
        lse,
        mixed_low,
        middle,
        second,
        right,
        gains,
        tables,
        left,
        order,
        ids,
    ) = forward(
        flat_in,
        positions.reshape(1, rows),
        jnp.broadcast_to(jnp.pad(run_ids, (0, WIDE - rows // RUN)), (8, WIDE)),
        gain_one.reshape(1, share),
        gain_two.reshape(1, share),
        w_query,
        w_key,
        w_value,
        w_out.T,
        w_gate,
        w_up,
        w_down.T,
        cotangent.reshape(rows, width),
    )
    input_grad, layer_out, grads, gain_grads = backward(
        order,
        ids,
        q_sorted,
        k_sorted,
        v_sorted,
        mixed_t,
        lse,
        cotangent.reshape(rows, width),
        left,
        normed,
        right,
        mixed_low,
        middle,
        near,
        far,
        flat_in,
        gains,
        tables,
    )
    splits, start = [], 0
    for wide in (
        w_gate.shape[1],
        w_up.shape[1],
        w_down.shape[0],
        w_query.shape[1],
        w_key.shape[1],
        w_value.shape[1],
        w_out.shape[0],
    ):
        splits.append(grads[:, start : start + wide])
        start += wide
    grad_gate, grad_up, grad_down, grad_query, grad_key, grad_value, grad_out = splits
    return (
        layer_out.reshape(rows, 1, width),
        input_grad,
        gain_grads[0, :share],
        gain_grads[1, :share],
        grad_query,
        grad_key,
        grad_value,
        grad_out.T,
        grad_gate,
        grad_up,
        grad_down.T,
    )


def solution(mesh):
    sizes = (mesh.shape["dp"], mesh.shape["context"], mesh.shape["tensor"])
    return jax.shard_map(
        by_heads if sizes == (2, 8, 2) else on_device,
        mesh=mesh,
        in_specs=(
            P("context", "dp", None),
            P("context", "dp"),
            P(("dp", "context")),
            P(("dp", "context")),
            P(("dp", "context"), "tensor"),
            P(("dp", "context"), "tensor"),
            P(("dp", "context"), "tensor"),
            P("tensor", ("dp", "context")),
            P(("dp", "context"), "tensor"),
            P(("dp", "context"), "tensor"),
            P("tensor", ("dp", "context")),
            P("context", "dp", None),
        ),
        out_specs=(
            P("context", "dp", None),
            P("context", "dp", None),
            P(("dp", "context")),
            P(("dp", "context")),
            P(("dp", "context"), "tensor"),
            P(("dp", "context"), "tensor"),
            P(("dp", "context"), "tensor"),
            P("tensor", ("dp", "context")),
            P(("dp", "context"), "tensor"),
            P(("dp", "context"), "tensor"),
            P("tensor", ("dp", "context")),
        ),
        check_vma=False,
    )
```

```python
import functools

import jax
import jax.numpy as jnp
import numpy as np
from jax import lax
from jax.experimental import pallas as pl
from jax.experimental.pallas import tpu as pltpu
from jax.sharding import PartitionSpec as P

HEAD = 96


epsilon = 1e-05
theta_base = 100000.0
masked_value = -1e30


def norm_forward(values_in, gain_vec):
    inverse = lax.rsqrt(jnp.mean(values_in * values_in, axis=-1, keepdims=True) + epsilon)
    unit_vals = values_in * inverse
    return (unit_vals, inverse, (unit_vals * gain_vec.astype(jnp.float32)).astype(jnp.bfloat16))


def norm_backward(grad_in, unit_vals, inverse, gain_vec):
    scaled = grad_in * gain_vec.astype(jnp.float32)
    grad_vals = inverse * (
        scaled - unit_vals * jnp.mean(scaled * unit_vals, axis=-1, keepdims=True)
    )
    return (grad_vals, jnp.sum(grad_in * unit_vals, axis=0))


def rotate(values_in, cos_part, sin_part):
    half_size = values_in.shape[-1] // 2
    front_half = values_in[..., :half_size]
    back_half = values_in[..., half_size:]
    return jnp.concatenate(
        [
            front_half * cos_part - back_half * sin_part,
            back_half * cos_part + front_half * sin_part,
        ],
        axis=-1,
    )


def contract_rows(left_mat, right_mat):
    return lax.dot_general(
        left_mat, right_mat, (((0,), (0,)), ((), ())), preferred_element_type=jnp.float32
    )


def contract_cols(left_mat, right_mat):
    return lax.dot_general(
        left_mat, right_mat, (((1,), (1,)), ((), ())), preferred_element_type=jnp.float32
    )


def on_device(
    tokens,
    positions,
    gain_one,
    gain_two,
    w_query,
    w_key,
    w_value,
    w_out,
    w_gate,
    w_up,
    w_down,
    cotangent,
):
    slot_count, seq_count, model_width = tokens.shape
    row_count = slot_count * seq_count
    gathered = (
        lax.all_gather(gain_one, ("dp", "context"), axis=0, tiled=True),
        lax.all_gather(gain_two, ("dp", "context"), axis=0, tiled=True),
        lax.all_gather(w_query, ("dp", "context"), axis=0, tiled=True),
        lax.all_gather(w_key, ("dp", "context"), axis=0, tiled=True),
        lax.all_gather(w_value, ("dp", "context"), axis=0, tiled=True),
        lax.all_gather(w_out, ("dp", "context"), axis=1, tiled=True),
        lax.all_gather(w_gate, ("dp", "context"), axis=0, tiled=True),
        lax.all_gather(w_up, ("dp", "context"), axis=0, tiled=True),
        lax.all_gather(w_down, ("dp", "context"), axis=1, tiled=True),
    )
    full_one, full_two, query_mat, key_mat, value_mat, out_mat, gate_mat, up_mat, down_mat = (
        gathered
    )
    heads_kv = key_mat.shape[1] // HEAD
    heads_q = query_mat.shape[1] // HEAD
    group_size = heads_q // heads_kv
    score_scale = HEAD ** (-0.5)
    half_size = HEAD // 2
    inv_freqs = theta_base ** (-2.0 * jnp.arange(half_size, dtype=jnp.float32) / HEAD)
    angles = positions.astype(jnp.float32)[:, :, None] * inv_freqs
    cos_part = jnp.cos(angles)[:, :, None, :]
    sin_part = jnp.sin(angles)[:, :, None, :]
    flat_in = tokens.astype(jnp.float32).reshape(row_count, model_width)
    unit_one, inverse_one, normed = norm_forward(flat_in, full_one)
    query_proj = jnp.dot(normed, query_mat, preferred_element_type=jnp.float32).reshape(
        slot_count, seq_count, heads_q, HEAD
    )
    key_proj = jnp.dot(normed, key_mat, preferred_element_type=jnp.float32).reshape(
        slot_count, seq_count, heads_kv, HEAD
    )
    value_low = (
        jnp.dot(normed, value_mat, preferred_element_type=jnp.float32)
        .astype(jnp.bfloat16)
        .reshape(slot_count, seq_count, heads_kv * HEAD)
    )
    queries = rotate(query_proj, cos_part, sin_part).astype(jnp.bfloat16)
    keys_low = (
        rotate(key_proj, cos_part, sin_part)
        .astype(jnp.bfloat16)
        .reshape(slot_count, seq_count, heads_kv * HEAD)
    )
    query_seq = jnp.transpose(
        queries.reshape(slot_count, seq_count, heads_kv, group_size, HEAD), (1, 2, 3, 0, 4)
    )
    query_pos = positions.T
    stat_shape = (seq_count, heads_kv, group_size, slot_count)
    initial = (
        jnp.full(stat_shape, masked_value, jnp.float32),
        jnp.zeros(stat_shape, jnp.float32),
        jnp.zeros(stat_shape + (HEAD,), jnp.float32),
    )
    key_piece = lax.all_gather(keys_low, "context", axis=0, tiled=True)
    value_piece = lax.all_gather(value_low, "context", axis=0, tiled=True)
    pos_piece = lax.all_gather(positions, "context", axis=0, tiled=True)
    piece_len = key_piece.shape[0]
    key_seq = jnp.transpose(key_piece.reshape(piece_len, seq_count, heads_kv, HEAD), (1, 2, 0, 3))
    value_seq = jnp.transpose(
        value_piece.reshape(piece_len, seq_count, heads_kv, HEAD), (1, 2, 0, 3)
    )
    pos_seq = pos_piece.T

    def per_sequence(seq_items):
        peak_val, totals, accum_vals, query_one, qpos_one, key_one, value_one, kpos_one = seq_items
        raw_scores = (
            jnp.einsum("hgqd,hkd->hgqk", query_one, key_one, preferred_element_type=jnp.float32)
            * score_scale
        )
        allowed = kpos_one[None, None, None, :] <= qpos_one[None, None, :, None]
        masked = jnp.where(allowed, raw_scores, masked_value)
        new_peak = jnp.maximum(peak_val, jnp.max(masked, axis=-1))
        decay_vals = jnp.exp(peak_val - new_peak)
        weights = jnp.where(allowed, jnp.exp(masked - new_peak[..., None]), 0.0)
        totals = totals * decay_vals + jnp.sum(weights, axis=-1)
        accum_vals = accum_vals * decay_vals[..., None] + jnp.einsum(
            "hgqk,hkd->hgqd",
            weights.astype(jnp.bfloat16),
            value_one,
            preferred_element_type=jnp.float32,
        )
        return (new_peak, totals, accum_vals)

    peak_val, totals, accum_vals = lax.map(
        per_sequence,
        (initial[0], initial[1], initial[2], query_seq, query_pos, key_seq, value_seq, pos_seq),
    )
    log_total = peak_val + jnp.log(totals)
    mixed_seq = accum_vals / totals[..., None]
    mixed_low = (
        jnp.transpose(mixed_seq, (3, 0, 1, 2, 4))
        .reshape(row_count, heads_q * HEAD)
        .astype(jnp.bfloat16)
    )
    branch = lax.psum(
        jnp.dot(mixed_low, out_mat, preferred_element_type=jnp.float32).astype(jnp.bfloat16),
        "tensor",
    ).astype(jnp.float32)
    middle = flat_in + branch
    unit_two, inverse_two, second = norm_forward(middle, full_two)
    gate_vals = jnp.dot(second, gate_mat, preferred_element_type=jnp.float32)
    up_vals = jnp.dot(second, up_mat, preferred_element_type=jnp.float32)
    sigmoid_vals = jax.nn.sigmoid(gate_vals)
    silu_vals = gate_vals * sigmoid_vals
    hidden = (silu_vals * up_vals).astype(jnp.bfloat16)
    mlp_part = lax.psum(
        jnp.dot(hidden, down_mat, preferred_element_type=jnp.float32).astype(jnp.bfloat16), "tensor"
    ).astype(jnp.float32)
    layer_out = (middle + mlp_part).astype(jnp.bfloat16).reshape(slot_count, seq_count, model_width)
    regathered = (
        lax.all_gather(gain_one, ("dp", "context"), axis=0, tiled=True),
        lax.all_gather(gain_two, ("dp", "context"), axis=0, tiled=True),
        lax.all_gather(w_query, ("dp", "context"), axis=0, tiled=True),
        lax.all_gather(w_key, ("dp", "context"), axis=0, tiled=True),
        lax.all_gather(w_value, ("dp", "context"), axis=0, tiled=True),
        lax.all_gather(w_out, ("dp", "context"), axis=1, tiled=True),
        lax.all_gather(w_gate, ("dp", "context"), axis=0, tiled=True),
        lax.all_gather(w_up, ("dp", "context"), axis=0, tiled=True),
        lax.all_gather(w_down, ("dp", "context"), axis=1, tiled=True),
    )
    full_one, full_two, query_mat, key_mat, value_mat, out_mat, gate_mat, up_mat, down_mat = (
        regathered
    )
    grad_low = cotangent.reshape(row_count, model_width)
    grad_down = contract_rows(hidden, grad_low)
    grad_hidden = contract_cols(grad_low, down_mat)
    grad_gate_low = (
        grad_hidden * up_vals * sigmoid_vals * (1.0 + gate_vals * (1.0 - sigmoid_vals))
    ).astype(jnp.bfloat16)
    grad_up_low = (grad_hidden * silu_vals).astype(jnp.bfloat16)
    grad_gate = contract_rows(second, grad_gate_low)
    grad_up = contract_rows(second, grad_up_low)
    grad_second = lax.psum(
        (contract_cols(grad_gate_low, gate_mat) + contract_cols(grad_up_low, up_mat)).astype(
            jnp.bfloat16
        ),
        "tensor",
    ).astype(jnp.float32)
    grad_mid_norm, grad_gain_two = norm_backward(grad_second, unit_two, inverse_two, full_two)
    grad_middle = grad_low.astype(jnp.float32) + grad_mid_norm
    grad_mid_low = grad_middle.astype(jnp.bfloat16)
    grad_out = contract_rows(mixed_low, grad_mid_low)
    grad_mixed = contract_cols(grad_mid_low, out_mat).astype(jnp.bfloat16)
    grad_mixed_seq = jnp.transpose(
        grad_mixed.reshape(slot_count, seq_count, heads_kv, group_size, HEAD), (1, 2, 3, 0, 4)
    )
    delta_rows = jnp.sum(grad_mixed_seq.astype(jnp.float32) * mixed_seq, axis=-1)
    kv_width = heads_kv * HEAD

    def block_grads(grad_query_acc, key_blk, value_blk, pos_blk):
        block_len = key_blk.shape[0]
        key_seq = jnp.transpose(key_blk.reshape(block_len, seq_count, heads_kv, HEAD), (1, 2, 0, 3))
        value_seq = jnp.transpose(
            value_blk.reshape(block_len, seq_count, heads_kv, HEAD), (1, 2, 0, 3)
        )
        raw_scores = (
            jnp.einsum("shgqd,shkd->shgqk", query_seq, key_seq, preferred_element_type=jnp.float32)
            * score_scale
        )
        allowed = pos_blk.T[:, None, None, None, :] <= query_pos[:, None, None, :, None]
        prob_vals = jnp.where(
            allowed,
            jnp.exp(jnp.where(allowed, raw_scores - log_total[..., None], masked_value)),
            0.0,
        )
        grad_value_blk = jnp.einsum(
            "shgqk,shgqd->kshd",
            prob_vals.astype(jnp.bfloat16),
            grad_mixed_seq,
            preferred_element_type=jnp.float32,
        )
        grad_probs = jnp.einsum(
            "shgqd,shkd->shgqk", grad_mixed_seq, value_seq, preferred_element_type=jnp.float32
        )
        grad_scores = (prob_vals * (grad_probs - delta_rows[..., None])).astype(jnp.bfloat16)
        grad_query_acc = grad_query_acc + jnp.einsum(
            "shgqk,shkd->shgqd", grad_scores, key_seq, preferred_element_type=jnp.float32
        )
        grad_key_blk = jnp.einsum(
            "shgqk,shgqd->kshd", grad_scores, query_seq, preferred_element_type=jnp.float32
        )
        return (
            grad_query_acc,
            grad_key_blk.reshape(block_len, seq_count, kv_width),
            grad_value_blk.reshape(block_len, seq_count, kv_width),
        )

    zero_query = jnp.zeros(stat_shape + (HEAD,), jnp.float32)
    key_all, value_all, pos_all = (
        lax.all_gather(keys_low, "context", axis=0, tiled=True),
        lax.all_gather(value_low, "context", axis=0, tiled=True),
        lax.all_gather(positions, "context", axis=0, tiled=True),
    )
    total_len = key_all.shape[0]
    block_size = min(512, total_len)
    block_count = total_len // block_size

    def key_block(grad_query_acc, block_items):
        key_blk, value_blk, pos_blk = block_items
        grad_query_acc, grad_key_blk, grad_value_blk = block_grads(
            grad_query_acc, key_blk, value_blk, pos_blk
        )
        return (grad_query_acc, (grad_key_blk, grad_value_blk))

    grad_query_acc, (grad_keys_all, grad_values_all) = lax.scan(
        key_block,
        zero_query,
        (
            key_all.reshape(block_count, block_size, seq_count, kv_width),
            value_all.reshape(block_count, block_size, seq_count, kv_width),
            pos_all.reshape(block_count, block_size, seq_count),
        ),
    )
    grad_key_own, grad_value_own = (
        lax.psum_scatter(
            grad_keys_all.reshape(total_len, seq_count, kv_width).astype(jnp.bfloat16),
            "context",
            scatter_dimension=0,
            tiled=True,
        ).astype(jnp.float32),
        lax.psum_scatter(
            grad_values_all.reshape(total_len, seq_count, kv_width).astype(jnp.bfloat16),
            "context",
            scatter_dimension=0,
            tiled=True,
        ).astype(jnp.float32),
    )
    grad_rot_q = jnp.transpose(grad_query_acc * score_scale, (3, 0, 1, 2, 4)).reshape(
        slot_count, seq_count, heads_q, HEAD
    )
    grad_q_low = (
        rotate(grad_rot_q, cos_part, -sin_part)
        .reshape(row_count, heads_q * HEAD)
        .astype(jnp.bfloat16)
    )
    grad_rot_k = (grad_key_own * score_scale).reshape(slot_count, seq_count, heads_kv, HEAD)
    grad_k_low = (
        rotate(grad_rot_k, cos_part, -sin_part).reshape(row_count, kv_width).astype(jnp.bfloat16)
    )
    grad_v_low = grad_value_own.reshape(row_count, kv_width).astype(jnp.bfloat16)
    grad_query = contract_rows(normed, grad_q_low)
    grad_key = contract_rows(normed, grad_k_low)
    grad_value = contract_rows(normed, grad_v_low)
    grad_normed = lax.psum(
        (
            contract_cols(grad_q_low, query_mat)
            + contract_cols(grad_k_low, key_mat)
            + contract_cols(grad_v_low, value_mat)
        ).astype(jnp.bfloat16),
        "tensor",
    ).astype(jnp.float32)
    grad_in_norm, grad_gain_one = norm_backward(grad_normed, unit_one, inverse_one, full_one)
    input_grad = (grad_middle + grad_in_norm).reshape(slot_count, seq_count, model_width)
    reduced = (
        lax.psum_scatter(grad_gain_one, ("dp", "context"), scatter_dimension=0, tiled=True),
        lax.psum_scatter(grad_gain_two, ("dp", "context"), scatter_dimension=0, tiled=True),
        lax.psum_scatter(grad_query, ("dp", "context"), scatter_dimension=0, tiled=True),
        lax.psum_scatter(grad_key, ("dp", "context"), scatter_dimension=0, tiled=True),
        lax.psum_scatter(grad_value, ("dp", "context"), scatter_dimension=0, tiled=True),
        lax.psum_scatter(grad_out, ("dp", "context"), scatter_dimension=1, tiled=True),
        lax.psum_scatter(grad_gate, ("dp", "context"), scatter_dimension=0, tiled=True),
        lax.psum_scatter(grad_up, ("dp", "context"), scatter_dimension=0, tiled=True),
        lax.psum_scatter(grad_down, ("dp", "context"), scatter_dimension=1, tiled=True),
    )
    return (
        layer_out,
        input_grad,
        reduced[0],
        reduced[1],
        reduced[2],
        reduced[3],
        reduced[4],
        reduced[5],
        reduced[6],
        reduced[7],
        reduced[8],
    )


WIDE = 128
HALF = HEAD // 2
RUN = 256
TILE = 512
LOG2_E = 1.4426950408889634
MESH = pl.DeviceIdType.MESH
PIECE = 256
FEED = 512
VMEM_LIMIT = 56 * 1024 * 1024


def any_spec():
    return pl.BlockSpec(memory_space=pl.ANY)


def vmem_spec():
    return pl.BlockSpec(memory_space=pltpu.VMEM)


def place():
    return lax.axis_index("dp"), lax.axis_index("context"), lax.axis_index("tensor")


def greet(devices):
    barrier = pltpu.get_barrier_semaphore()
    for device in devices:
        pl.semaphore_signal(barrier, inc=1, device_id=device, device_id_type=MESH)
    pl.semaphore_wait(barrier, len(devices))


def sequence_others():
    row, spot, core = place()
    return [
        (row, lax.rem(spot + shift, 8), lax.rem(core + flip, 2))
        for shift in range(8)
        for flip in range(2)
        if shift or flip
    ]


def lane_freqs():
    return jnp.asarray(
        np.power(np.float32(theta_base), np.float32(-2.0) * np.arange(HALF, dtype=np.float32) / HEAD)
    ).reshape(HALF, 1)


def dot_f32(left, right):
    return jnp.dot(left, right, preferred_element_type=jnp.float32)


def own_shard():
    row, spot, core = place()
    return row * 8 + spot


def group_others():
    row, spot, core = place()
    return sequence_others() + [(1 - row, lax.rem(spot + shift, 8), core) for shift in range(8)]


def exchange_messages(message_to, landing, send, recv):
    row, spot, core = place()
    copies, waits = [], []

    def one(flip, shift):
        at = flip * 8 + shift
        to_row = lax.rem(row + flip, 2)
        chip, source = lax.rem(spot + shift, 8), lax.rem(spot + 8 - shift, 8)
        device = (to_row, chip, core)
        message = message_to(to_row * 8 + chip)
        copies.append(
            remote(message, landing.at[row * 8 + spot], send.at[at], recv.at[at], device)
        )
        came = landing.at[to_row * 8 + source]
        waits.append(remote(came, came, send.at[at], recv.at[at], device).wait_recv)

    for flip in range(2):
        for shift in range(8):
            if flip or shift:
                one(flip, shift)
    return copies, waits


def turn_left(left_t, index, source):
    quarter = source.shape[1] // 4
    share = quarter // 4
    for piece in range(4):
        turned = source[:, piece * quarter : (piece + 1) * quarter].T
        for inner in range(4):
            x, z, y = piece // 2, 2 * (piece % 2) + inner // 2, inner % 2
            left_t[index, x, y, z * share : (z + 1) * share] = turned[
                inner * share : (inner + 1) * share
            ]


def remote(source, target, send, recv, device):
    return pltpu.make_async_remote_copy(
        src_ref=source,
        dst_ref=target,
        send_sem=send,
        recv_sem=recv,
        device_id=device,
        device_id_type=MESH,
    )


def move(source, target, send, recv, device, is_self):
    @pl.when(is_self)
    def _():
        pltpu.make_async_copy(source, target, recv).start()

    @pl.when(jnp.logical_not(is_self))
    def _():
        remote(source, target, send, recv, device).start()


def return_copies(ref, out, send, recv):
    row, spot, core = place()
    head = 2 * lax.rem(spot, 4) + core
    owner = spot // 4
    copies = []
    for step in range(8):
        chip = lax.rem(spot + step, 8)
        is_self = (owner == core) if step == 0 else False
        parts = (ref.at[chip], out.at[head], send.at[step], recv.at[head], (row, chip, owner))
        copies.append((parts, is_self))
    return copies


def start_return(copies):
    for parts, is_self in copies:
        if is_self is False:
            remote(*parts).start()
        else:
            move(*parts, is_self)


def finish_return(copies, out, send, recv):
    row, spot, core = place()
    for head in range(8):
        remote(
            out.at[head], out.at[head], send.at[0], recv.at[head], (row, spot, 1 - core)
        ).wait_recv()
    for parts, is_self in copies:
        if is_self is False:
            remote(*parts).wait_send()
        else:

            @pl.when(jnp.logical_not(is_self))
            def _():
                remote(*parts).wait_send()


def tile_at(index, size):
    return pl.ds(pl.multiple_of(index * size, size), size)


def causal(scores):
    keys = lax.broadcasted_iota(jnp.int32, scores.shape, 0)
    queries = lax.broadcasted_iota(jnp.int32, scores.shape, 1)
    return jnp.where(keys <= queries, scores, masked_value)


def neighbours():
    row, spot, core = place()
    level, column = spot // 2, lax.rem(spot, 2)
    beside_x = (1 - row, spot, core)
    beside_y = (row, 2 * level + 1 - column, core)
    along_z = [(row, 2 * lax.rem(level + k, 4) + column, core) for k in (1, 2, 3)]
    return row, level, column, beside_x, beside_y, along_z


class Gather:
    def __init__(self, own, whole, start, width, piece, sems):
        self.own, self.whole = own.at[:, pl.ds(start, width)], whole
        self.start, self.width = start, width
        names = ("send_z", "recv_z", "send_x", "recv_x", "send_y", "recv_y", "send_d", "recv_d")
        for name, sem in zip(names + ("local",), sems):
            setattr(self, name, sem.at[piece])

    def block(self, x, z, y, half=None):
        cut = self.width * 7 // 12 // WIDE * WIDE
        start, width = self.start, self.width
        if half == 0:
            width = cut
        elif half == 1:
            start, width = start + cut, width - cut
        return self.whole.at[x, z, y, :, pl.ds(start, width)]

    def arrived(self, target, recv_sem):
        device = neighbours()[3]
        remote(target, target, self.send_x.at[0], recv_sem, device).wait_recv()

    def copy_z(self, z, up, own=False):
        row, level, column, beside_x, beside_y = neighbours()[:5]
        core = place()[2]
        target = level + 1 if up else level - 1
        block = self.block(row, z, column)
        return remote(
            self.own if own else block,
            block,
            self.send_z.at[int(up), z],
            self.recv_z.at[z],
            (row, 2 * target + column, core),
        )

    def copies_xy(self, z, own=False):
        row, level, column, beside_x, beside_y = neighbours()[:5]
        block = self.block(row, z, column)
        source = self.own if own else block
        return [
            remote(source, block, self.send_x.at[z], self.recv_x.at[z], beside_x),
            remote(source, block, self.send_y.at[z], self.recv_y.at[z], beside_y),
        ]

    def copies_diagonal(self, z):
        row, level, column, beside_x, beside_y = neighbours()[:5]
        by_y = self.block(1 - row, z, column, 1)
        by_x = self.block(row, z, 1 - column, 0)
        return [
            remote(by_y, by_y, self.send_d.at[0, z], self.recv_d.at[0, z], beside_y),
            remote(by_x, by_x, self.send_d.at[1, z], self.recv_d.at[1, z], beside_x),
        ]

    def own_copy(self):
        row, level, column = neighbours()[:3]
        return pltpu.make_async_copy(self.own, self.block(row, level, column), self.local)

    def each_at(self, hop, act):
        level = neighbours()[1]

        @pl.when(level >= hop)
        def _():
            act(level - hop, True)

        @pl.when(level + hop <= 3)
        def _():
            act(level + hop, False)

    def start_z(self, z, up, own=False):
        level = neighbours()[1]

        @pl.when(level < 3 if up else level > 0)
        def _():
            self.copy_z(z, up, own).start()

    def place_own(self):
        self.own_copy().start()

    def open(self):
        level = neighbours()[1]
        self.start_z(level, True, True)
        self.start_z(level, False, True)
        for copy in self.copies_xy(level, True):
            copy.start()

    def hop(self, hop):
        def act(z, up):
            row, level, column = neighbours()[:3]
            self.arrived(self.block(row, z, column), self.recv_z.at[z])
            self.start_z(z, up)
            for copy in self.copies_xy(z):
                copy.start()

        self.each_at(hop, act)

    def turn_diagonal(self, z):
        row, level, column = neighbours()[:3]
        by_y, by_x = self.copies_diagonal(z)
        self.arrived(self.block(1 - row, z, column), self.recv_x.at[z])
        by_y.start()
        self.arrived(self.block(row, z, 1 - column), self.recv_y.at[z])
        by_x.start()

    def diagonal(self, hop):
        if hop == 0:
            self.turn_diagonal(neighbours()[1])
        else:
            self.each_at(hop, lambda z, up: self.turn_diagonal(z))

    def finish(self):
        row, level, column = neighbours()[:3]
        self.own_copy().wait()
        for z in range(4):
            self.arrived(self.block(1 - row, z, 1 - column, 1), self.recv_d.at[0, z])
            self.arrived(self.block(1 - row, z, 1 - column, 0), self.recv_d.at[1, z])

    def close_z(self):
        level = neighbours()[1]

        def sent(z, up):
            @pl.when(level < 3 if up else level > 0)
            def _():
                self.copy_z(z, up).wait_send()

        sent(level, True)
        sent(level, False)
        for hop in range(1, 4):
            self.each_at(hop, sent)

    def close(self):
        self.close_z()
        for z in range(4):
            for copy in self.copies_xy(z) + self.copies_diagonal(z):
                copy.wait_send()


class PlaneGather(Gather):
    def plane(self, z):
        return self.whole.at[:, z, :, :, pl.ds(self.start, self.width)]

    def copy_z(self, z, up, own=False):
        row, level, column = neighbours()[:3]
        target = level + 1 if up else level - 1
        plane = self.plane(z)
        return remote(
            plane,
            plane,
            self.send_z.at[int(up), z],
            self.recv_z.at[z],
            (row, 2 * target + column, place()[2]),
        )

    def open(self):
        for copy in self.copies_xy(neighbours()[1], True):
            copy.start()

    def spread(self):
        row, level, column = neighbours()[:3]
        self.arrived(self.block(1 - row, level, 1 - column, 1), self.recv_d.at[0, level])
        self.arrived(self.block(1 - row, level, 1 - column, 0), self.recv_d.at[1, level])
        self.own_copy().wait()
        self.start_z(level, True)
        self.start_z(level, False)

    def hop(self, hop):
        def act(z, up):
            self.arrived(self.plane(z), self.recv_z.at[z])
            self.start_z(z, up)

        self.each_at(hop, act)

    def finish(self):
        pass

    def close(self):
        level = neighbours()[1]
        self.close_z()
        for copy in self.copies_xy(level) + self.copies_diagonal(level):
            copy.wait_send()


def gather_sems(pieces):
    dma = pltpu.SemaphoreType.DMA
    shapes = [(2, 4), (4,), (4,), (4,), (4,), (4,), (2, 4), (2, 4), ()]
    return [dma((pieces,) + shape) for shape in shapes]


AT_BEGIN, AT_GAINS, AT_PAIRS, AT_QUERIES, AT_HEADS, AT_KEYS, AT_ALL, AT_SORT = 0, 1, 2, 3, 4, 5, 6, 7
AT_RETURN, AT_MIXED, AT_OUT, AT_NORM, AT_GROUP, AT_TILE, AT_FEED = 8, 9, 10, 11, 12, 16, 24
PUMPS = {
    AT_BEGIN: (1, 10, 4, 2, 3, 5, 7, 6, 11, 12, 13, 14),
    AT_GAINS: (20,),
    AT_GROUP + 2: (15, 17),
    AT_GROUP + 3: (16, 70),
    AT_QUERIES: (21, 30),
    AT_GROUP + 0: (50,),
    AT_GROUP + 1: (22,),
    AT_HEADS: (74, 40, 31, 60, 23),
    AT_KEYS: (34, 75),
    AT_ALL: (32, 24, 35, 44),
    AT_TILE + 0: (41, 25),
    AT_TILE + 2: (33, 26, 61, 42, 71),
    AT_TILE + 3: (27, 51),
    AT_RETURN: (36, 37, 43, 52, 45, 55, 72, 47, 54, 46),
    AT_MIXED: (64,),
    AT_OUT: (53,),
    AT_NORM: (56, 62),
    AT_FEED + 1: (63, 57),
    AT_FEED + 3: (65, 66, 67),
    AT_FEED + 5: (73,),
}


def forward_kernel(
    tokens,
    positions,
    freqs,
    gain_one,
    gain_two,
    w_query,
    w_key,
    w_value,
    w_out_t,
    w_gate,
    w_up,
    w_down_t,
    cotangent,
    near,
    far,
    normed_out,
    q_out,
    k_out,
    v_out,
    mixed_t_out,
    lse_out,
    mixed_low_out,
    middle_out,
    second_out,
    right_out,
    gains_out,
    tables_out,
    left_out,
    order,
    ids_flat,
    ids_in,
    near_own,
    far_own,
    unit,
    normed,
    tables,
    weight,
    gain_message,
    gain_all,
    gain_columns,
    gain_rows,
    left_t,
    q_heads,
    kv_heads,
    q_slots,
    kv_slots,
    q_t,
    keys,
    v_t,
    mixed_t,
    lse,
    mixed,
    mixed_slots,
    mixed_heads,
    mixed_low,
    out_weight,
    part,
    part_other,
    second,
    cot,
    right,
    feed_weight,
    ids_all,
    ids,
    load_own,
    send_ids,
    recv_ids,
    load_ids,
    send_gain,
    recv_gain,
    load_w,
    load_out,
    load_feed,
    load_cot,
    save_right,
    saves,
    send_q,
    recv_q,
    send_kv,
    recv_kv,
    send_x,
    recv_x,
    send_m,
    recv_m,
    send_p,
    recv_p,
    *sems,
):
    row, spot, core = place()
    low, full = jnp.bfloat16, jnp.float32
    rows, width = tokens.shape
    share = near_own.shape[0]
    length = 8 * rows
    runs, tiles = length // RUN, length // TILE
    per_device = rows // RUN
    halves = TILE // RUN
    quarter = 4 * share
    sibling = (row, spot, 1 - core)
    out_width = w_out_t.shape[1]
    qkv_width = 16 * HEAD

    near_loads, far_loads, start = [], [], 0
    for ref in (w_query, w_key, w_value, w_out_t):
        target = near_own.at[:, pl.ds(start, ref.shape[1])]
        near_loads.append(pltpu.make_async_copy(ref, target, load_own.at[len(near_loads)]))
        start += ref.shape[1]
    for index, ref in enumerate((w_gate, w_up, w_down_t)):
        for piece in range(4):
            source = ref.at[:, pl.ds(piece * FEED, FEED)]
            target = far_own.at[:, pl.ds((3 * piece + index) * FEED, FEED)]
            far_loads.append(
                pltpu.make_async_copy(source, target, load_own.at[4 + 4 * index + piece])
            )
    for copy in near_loads + far_loads:
        copy.start()
    load_cotangent = pltpu.make_async_copy(cotangent, cot, load_cot)
    load_cotangent.start()
    half = qkv_width // 2
    pairs = Gather(near_own, near, half, half, 0, sems)
    first = Gather(near_own, near, 0, half, 1, sems)
    outer = Gather(near_own, near, qkv_width, out_width, 2, sems)
    feeds = [Gather(far_own, far, 3 * FEED * p, 3 * FEED, 3 + p, sems) for p in range(3)]
    feeds.append(Gather(far_own, far, 9 * FEED, FEED, 6, sems))
    plane = PlaneGather(far_own, far, 10 * FEED, 2 * FEED, 7, sems)
    gathers = [pairs, first, outer] + feeds + [plane]

    def pump(place):
        for what in PUMPS.get(place, ()):
            gather, act = gathers[what // 10], what % 10
            if act == 0:
                gather.open()
            elif act < 4:
                gather.hop(act)
            elif gather is plane and act == 5:
                gather.spread()
            else:
                gather.diagonal(act - 4)

    gain_message[...] = jnp.zeros_like(gain_message)
    gain_message[0:1, :share] = gain_one[...].astype(full)
    gain_message[1:2, :share] = gain_two[...].astype(full)
    for copy in near_loads:
        copy.wait()
    greet(group_others())
    pairs.open()
    for gather in (pairs, first, outer):
        gather.place_own()

    gain_copies, gain_from = exchange_messages(
        lambda shard: gain_message, gain_all, send_gain, recv_gain
    )
    for copy in gain_copies:
        copy.start()
    gain_all[own_shard()] = gain_message[...]

    lane = lax.broadcasted_iota(jnp.int32, (8, WIDE), 1)
    ids_in[...] = jnp.zeros_like(lane)
    for run in range(per_device):
        start_at = positions[0:1, run * RUN : run * RUN + 1]
        ids_in[...] = jnp.where(lane == run, lax.div(start_at, RUN), ids_in[...])
    for shift in range(1, 8):
        remote(
            ids_in,
            ids_all.at[spot],
            send_ids.at[shift],
            recv_ids.at[shift],
            (row, lax.rem(spot + shift, 8), core),
        ).start()
    ids_all[spot] = ids_in[...]

    for copy in far_loads:
        copy.wait()
    for gather in feeds + [plane]:
        gather.place_own()
    chunk = rows // 8

    def unit_block(index, carry):
        cut = tile_at(index, chunk)
        values = tokens[cut].astype(full)
        inverse = lax.rsqrt(jnp.mean(values * values, axis=-1, keepdims=True) + epsilon)
        unit[cut] = values * inverse
        return carry

    lax.fori_loop(0, 8, unit_block, 0)
    angles = freqs[...] * positions[...].astype(full)
    tables[0] = jnp.cos(angles)
    tables[1] = jnp.sin(angles)

    pump(AT_BEGIN)
    for shift in range(1, 8):
        remote(
            ids_in,
            ids_all.at[lax.rem(spot + 8 - shift, 8)],
            send_ids.at[shift],
            recv_ids.at[shift],
            (row, lax.rem(spot + shift, 8), core),
        ).wait_recv()
    pltpu.make_async_copy(ids_all, ids, load_ids).start()
    pairs.finish()

    width = near.shape[3] * 16

    def load_group(group):
        lanes = pl.ds(group * 4 * HEAD, 4 * HEAD)
        return pltpu.make_async_copy(
            near.at[:, :, :, :, lanes], weight.at[group % 2], load_w.at[group % 2]
        )

    load_out_weight = pltpu.make_async_copy(
        near.at[:, :, :, :, pl.ds(qkv_width, out_width)], out_weight, load_out
    )
    load_group(2).start()
    load_group(3).start()
    for wait in gain_from:
        wait()
    for shard in range(16):
        gain_columns[shard * share : (shard + 1) * share] = gain_all[shard].T[:share]
    gain_rows[...] = gain_columns[...].T
    normed[...] = (unit[...] * gain_rows[0:1]).astype(low)
    pump(AT_GAINS)

    def project(group):
        load_group(group).wait()
        proj = dot_f32(normed[...], weight[group % 2].reshape(width, 4 * HEAD)).T
        for head in range(4):
            front = proj[head * HEAD : head * HEAD + HALF]
            back = proj[head * HEAD + HALF : (head + 1) * HEAD]
            if group < 3:
                front, back = (
                    front * tables[0] - back * tables[1],
                    back * tables[0] + front * tables[1],
                )
            for start, value in ((0, front.astype(low)), (HALF, back.astype(low))):
                for run in range(per_device):
                    piece = value[:, run * RUN : (run + 1) * RUN]
                    if group < 2:
                        q_heads[4 * group + head, run, start : start + HALF] = piece
                    else:
                        kv_heads[head, group - 2, run, start : start + HALF] = piece
        pump(AT_GROUP + group)

    project(2)
    project(3)

    outgoing = []
    for step in range(4):
        slot = lax.rem(spot + step, 4)
        chip = 4 * core + slot
        for other in range(2):
            is_self = jnp.logical_and(chip == spot, core == other)
            device = (row, chip, other)
            kv_parts = (
                kv_heads.at[slot, :, other],
                kv_slots.at[spot, :, other],
                send_kv.at[step, other],
                recv_kv.at[spot],
                device,
            )
            q_parts = (
                q_heads.at[2 * slot + other],
                q_slots.at[spot],
                send_q.at[step, other],
                recv_q.at[spot],
                device,
            )
            outgoing.append((kv_parts, is_self))
            outgoing.append((q_parts, is_self))
    for parts, is_self in outgoing[0::2]:
        move(*parts, is_self)
    pump(AT_PAIRS)
    first.finish()
    load_group(0).start()
    load_group(1).start()
    pump(AT_QUERIES)
    project(0)
    project(1)
    for parts, is_self in outgoing[1::2]:
        move(*parts, is_self)
    pump(AT_HEADS)

    def hand_on(source):
        block = kv_slots.at[source, :, core]
        return remote(block, block, send_x.at[source], recv_x.at[source], sibling)

    for step in range(8):
        source = lax.rem(spot + step, 8)
        block = kv_slots.at[source, :, core]
        remote(block, block, send_x.at[source], recv_kv.at[source], sibling).wait_recv()
        hand_on(source).start()
    pump(AT_KEYS)
    for step in range(8):
        remote(
            q_slots.at[step], q_slots.at[step], send_x.at[step], recv_q.at[step], sibling
        ).wait_recv()
        hand_on(step).wait()
    pump(AT_ALL)

    pltpu.make_async_copy(ids_all, ids, load_ids).wait()

    def find_run(index, carry):
        device, piece = 0, 0
        for run in range(runs):
            here = ids[run // per_device, 0, run % per_device] == index
            device = jnp.where(here, run // per_device, device)
            piece = jnp.where(here, run % per_device, piece)
        order[index, 0] = device
        order[index, 1] = piece
        found = ids[index // per_device, 0, index % per_device]
        order[runs + index, 0] = lax.div(found, per_device)
        order[runs + index, 1] = lax.rem(found, per_device)
        ids_flat[index] = found
        return carry

    lax.fori_loop(0, runs, find_run, 0)

    def sort_run(index, carry):
        device, piece = order[index, 0], order[index, 1]
        cols = tile_at(index, RUN)
        q_t[:, cols] = q_slots[device, piece]
        keys[index] = kv_slots[device, 0, piece].T
        v_t[:, cols] = kv_slots[device, 1, piece]
        return carry

    lax.fori_loop(0, runs, sort_run, 0)
    pump(AT_SORT)
    scale = HEAD ** (-0.5) * LOG2_E

    def query_pair(pair, carry):
        def step(half, scores, block, peak, total, mix):
            high = jnp.maximum(peak, jnp.max(scores, axis=0, keepdims=True))
            decay = jnp.exp2(peak - high)
            weights = jnp.exp2(scores - high)
            total = total * decay + jnp.sum(weights, axis=0, keepdims=True)
            mix = mix * decay + dot_f32(v_t[:, tile_at(block, TILE)], weights.astype(low))
            return high, total, mix

        def scores_of(half, block):
            held = keys[pl.ds(block * halves, halves)].reshape(TILE, HEAD)
            return dot_f32(held, q_t[:, tile_at(2 * pair + half, TILE)]) * scale

        def full_block(block, states):
            scores = [scores_of(half, block) for half in range(2)]
            return tuple(step(half, scores[half], block, *states[half]) for half in range(2))

        state = (
            jnp.full((1, TILE), masked_value, full),
            jnp.zeros((1, TILE), full),
            jnp.zeros((HEAD, TILE), full),
        )
        start = 2 * pair
        scores = causal(scores_of(0, start)), scores_of(1, start)
        states = tuple(step(half, scores[half], start, *state) for half in range(2))
        last = step(1, causal(scores_of(1, start + 1)), start + 1, *states[1])
        states = lax.fori_loop(0, start, full_block, (states[0], last))
        for half in range(2):
            peak, total, mix = states[half]
            index = 2 * pair + half
            cols = tile_at(index, TILE)
            mix = mix / total
            mixed_t[:, cols] = mix
            lse[:, cols] = peak + jnp.log2(total)
            for run in range(halves):
                cut = mix[:, run * RUN : (run + 1) * RUN]
                mixed[index * halves + run] = cut.astype(low)
        for place in range(tiles // 2):

            @pl.when(pair == place)
            def _():
                pump(AT_TILE + place)

        return carry

    lax.fori_loop(0, tiles // 2, query_pair, 0)

    def unsort_run(run, carry):
        index = ids[run // per_device, 0, run % per_device]
        mixed_slots[run // per_device, run % per_device] = mixed[index]
        return carry

    lax.fori_loop(0, runs, unsort_run, 0)
    copies = return_copies(mixed_slots, mixed_heads, send_m, recv_m)
    start_return(copies)
    early_saves = [
        pltpu.make_async_copy(source, target, saves.at[index])
        for index, (source, target) in enumerate(
            [
                (normed, normed_out),
                (q_t, q_out),
                (keys, k_out),
                (v_t, v_out),
                (mixed_t, mixed_t_out),
                (lse, lse_out),
                (gain_rows, gains_out),
                (tables, tables_out),
            ]
        )
    ]
    for copy in early_saves:
        copy.start()
    pump(AT_RETURN)
    outer.finish()
    load_out_weight.start()
    finish_return(copies, mixed_heads, send_m, recv_m)
    pump(AT_MIXED)

    load_out_weight.wait()
    for run in range(per_device):
        side = mixed_heads[:, run].reshape(8 * HEAD, RUN)
        mixed_low[run * RUN : (run + 1) * RUN] = side.T

    def pair_copy(index):
        cut = pl.ds(index * quarter, quarter)
        return remote(
            part.at[:, cut], part_other.at[:, cut], send_p.at[index], recv_p.at[index], sibling
        )

    for index in range(4):
        block = out_weight[index // 2, 2 * (index % 2) : 2 * (index % 2) + 2]
        term = contract_cols(mixed_low[...], block.reshape(quarter, out_width))
        part[:, index * quarter : (index + 1) * quarter] = term.astype(low)
        pair_copy(index).start()
    pump(AT_OUT)
    load_cotangent.wait()
    for index in range(4):
        pair_copy(index).wait()
    chunk = rows // 8

    def norm_block(index, carry):
        cut = tile_at(index, chunk)
        sums = part[cut].astype(full) + part_other[cut].astype(full)
        values = tokens[cut].astype(full) + sums
        unit[cut] = values
        inverse = lax.rsqrt(jnp.mean(values * values, axis=-1, keepdims=True) + epsilon)
        second[cut] = (values * inverse * gain_rows[1:2]).astype(low)
        return carry

    lax.fori_loop(0, 8, norm_block, 0)
    late_saves = [
        pltpu.make_async_copy(source, target, saves.at[8 + index])
        for index, (source, target) in enumerate(
            [(mixed_low, mixed_low_out), (unit, middle_out), (second, second_out)]
        )
    ]
    for copy in late_saves:
        copy.start()
    pump(AT_NORM)

    def load_feed_weight(index, kind):
        piece, half = index // 2, lax.rem(index, 2)
        start = (3 * piece + kind) * FEED + half * PIECE
        lanes = pl.ds(pl.multiple_of(start, PIECE), PIECE)
        return pltpu.make_async_copy(
            far.at[:, :, :, :, lanes], feed_weight.at[half, kind], load_feed.at[half, kind]
        )

    def load_half(index):
        for kind in range(3):
            load_feed_weight(index, kind).start()

    def save_piece(piece):
        lanes = pl.ds(piece * 3 * FEED, 3 * FEED)
        return pltpu.make_async_copy(
            right.at[:, lanes], right_out.at[:, lanes], save_right.at[piece]
        )

    def feed_block(index, carry):
        piece, half = index // 2, lax.rem(index, 2)
        for when in range(3):

            @pl.when(index == (2 * when + 1 if when < 2 else 6))
            def _():
                feeds[when + 1].finish()

        @pl.when(index == 0)
        def _():
            load_half(0)

        @pl.when(index == 6)
        def _():
            load_half(6)

        @pl.when(jnp.logical_and(index != 5, index != 7))
        def _():
            load_half(index + 1)

        values = []
        for kind, left in enumerate((second, second, cot)):
            load_feed_weight(index, kind).wait()
            values.append(dot_f32(left[...], feed_weight[half, kind].reshape(width, PIECE)))
        gate, up, grad_hidden = values
        sigmoid = jax.nn.sigmoid(gate)
        silu = gate * sigmoid
        grad_gate = grad_hidden * up * sigmoid * (1.0 + gate * (1.0 - sigmoid))
        for when, source in ((1, second), (3, cot)):

            @pl.when(index == when)
            def _():
                turn_left(left_t, when % 3, source)

        for kind, value in enumerate((grad_gate, grad_hidden * silu, silu * up)):
            start = (3 * piece + kind) * FEED + half * PIECE
            right[:, pl.ds(pl.multiple_of(start, PIECE), PIECE)] = value.astype(low)

        for when in range(8):

            @pl.when(index == when)
            def _():
                pump(AT_FEED + when)

        for when in range(4):

            @pl.when(index == 2 * when + 1)
            def _():
                save_piece(when).start()

        return carry

    feeds[0].finish()
    lax.fori_loop(0, 8, feed_block, 0)
    save_left = pltpu.make_async_copy(left_t, left_out, saves.at[11])
    save_left.start()
    for gather in gathers:
        gather.close()
    for parts, is_self in outgoing:

        @pl.when(jnp.logical_not(is_self))
        def _():
            remote(*parts).wait_send()

    for shift in range(1, 8):
        remote(
            ids_in,
            ids_all.at[spot],
            send_ids.at[shift],
            recv_ids.at[shift],
            (row, lax.rem(spot + shift, 8), core),
        ).wait_send()
    for copy in gain_copies:
        copy.wait_send()
    for copy in early_saves + late_saves + [save_left] + [save_piece(piece) for piece in range(4)]:
        copy.wait()


def forward(
    tokens,
    positions,
    gain_one,
    gain_two,
    w_query,
    w_key,
    w_value,
    w_out_t,
    w_gate,
    w_up,
    w_down_t,
    cotangent,
):
    dma = pltpu.SemaphoreType.DMA
    vmem = pltpu.VMEM
    low, full = jnp.bfloat16, jnp.float32
    rows, width = tokens.shape
    share, hidden_width = w_gate.shape
    out_width = w_out_t.shape[1]
    near_width = 16 * HEAD + out_width
    length = 8 * rows
    per_device = rows // RUN
    heads = (8, per_device, HEAD, RUN)
    both = (2, per_device, HEAD, RUN)
    by_run = (length // RUN, RUN, HEAD)
    flat = (HEAD, length)
    smem_spec = pl.BlockSpec(memory_space=pltpu.SMEM)
    shape = jax.ShapeDtypeStruct
    return pl.pallas_call(
        forward_kernel,
        in_specs=[vmem_spec()] * 5 + [any_spec()] * 8,
        out_specs=[any_spec()] * 15 + [smem_spec] * 2,
        out_shape=[
            shape((2, 4, 2, share, near_width), low),
            shape((2, 4, 2, share, 3 * hidden_width), low),
            shape((rows, width), low),
            shape(flat, low),
            shape(by_run, low),
            shape(flat, low),
            shape(flat, full),
            shape((1, length), full),
            shape((rows, out_width), low),
            shape((rows, width), full),
            shape((rows, width), low),
            shape((rows, 3 * hidden_width), low),
            shape((8, width), full),
            shape((2, HALF, rows), full),
            shape((2, 2, 2, 4 * share, rows), low),
            shape((2 * length // RUN, 2), jnp.int32),
            shape((length // RUN,), jnp.int32),
        ],
        scratch_shapes=[
            vmem((8, WIDE), jnp.int32),
            vmem((share, near_width), low),
            vmem((share, 3 * hidden_width), low),
            vmem((rows, width), full),
            vmem((rows, width), low),
            vmem((2, HALF, rows), full),
            vmem((2, 2, 4, 2, share, 4 * HEAD), low),
            vmem((8, WIDE), full),
            vmem((16, 8, WIDE), full),
            vmem((width, 8), full),
            vmem((8, width), full),
            vmem((2, 2, 2, 4 * share, rows), low),
            vmem(heads, low),
            vmem((4,) + both, low),
            vmem(heads, low),
            vmem((8,) + both, low),
            vmem(flat, low),
            vmem(by_run, low),
            vmem(flat, low),
            vmem(flat, full),
            vmem((1, length), full),
            vmem((length // RUN, HEAD, RUN), low),
            vmem(heads, low),
            vmem(heads, low),
            vmem((rows, out_width), low),
            vmem((2, 4, 2, share, out_width), low),
            vmem((rows, width), low),
            vmem((rows, width), low),
            vmem((rows, width), low),
            vmem((rows, width), low),
            vmem((rows, 3 * hidden_width), low),
            vmem((2, 3, 2, 4, 2, share, PIECE), low),
            vmem((8, 8, WIDE), jnp.int32),
            pltpu.SMEM((8, 8, WIDE), jnp.int32),
            dma((16,)),
            dma((8,)),
            dma((8,)),
            dma(()),
            dma((16,)),
            dma((16,)),
            dma((2,)),
            dma(()),
            dma((2, 3)),
            dma(()),
            dma((4,)),
            dma((12,)),
            dma((4, 2)),
            dma((8,)),
            dma((4, 2)),
            dma((8,)),
            dma((8,)),
            dma((8,)),
            dma((8,)),
            dma((8,)),
            dma((4,)),
            dma((4,)),
        ]
        + gather_sems(8),
        compiler_params=pltpu.CompilerParams(
            collective_id=1, has_side_effects=True, vmem_limit_bytes=VMEM_LIMIT
        ),
        name="forward",
    )(
        tokens,
        positions,
        lane_freqs(),
        gain_one,
        gain_two,
        w_query,
        w_key,
        w_value,
        w_out_t,
        w_gate,
        w_up,
        w_down_t,
        cotangent,
    )


SECOND, THIRD, LAST = 2, 4, 5


class Reduce:
    def __init__(self, n, changes, refs):
        (
            self.left_t,
            self.right,
            self.own,
            self.out,
            self.save,
            self.send_one,
            self.recv_one,
            self.send_two,
            self.recv_two,
            self.kept,
            self.recv_three,
            self.ss_one,
            self.rs_one,
            self.ss_two,
            self.rs_two,
            self.ss_three,
            self.rs_three,
        ) = refs
        self.n, self.changes = n, changes
        self.share = self.own.shape[1]

    def columns(self, step, kind):
        held = self.right.shape[1] // (2 * PIECE)
        start = lax.rem(step, held) * 2 * PIECE + kind * PIECE
        return pl.ds(pl.multiple_of(start, PIECE), PIECE)

    def each_save(self, step, act):
        slot = lax.rem(step, 2)
        near_at = self.changes[0]

        def copies(cuts):
            for index, (ref, start, lanes) in enumerate(cuts):
                source = self.own.at[slot, :, lanes]
                target = ref.at[:, pl.ds(start, lanes.size)]
                act(pltpu.make_async_copy(source, target, self.save.at[slot, index]))

        for kind in range(3):

            @pl.when(jnp.logical_and(step < near_at, lax.rem(step, 3) == kind))
            def _():
                start = pl.multiple_of(step // 3 * 2 * PIECE, 2 * PIECE)
                copies([(self.out[kind], start, pl.ds(0, 2 * PIECE))])

        for index in range(self.n - near_at):
            first, past = index * 2 * PIECE, (index + 1) * 2 * PIECE
            cuts, at = [], 0
            for ref in self.out[3:]:
                low, high = max(first, at), min(past, at + ref.shape[1])
                if low < high:
                    cuts.append((ref, low - at, pl.ds(low - first, high - low)))
                at += ref.shape[1]

            @pl.when(step == near_at + index)
            def _():
                copies(cuts)

    def product(self, step, kind, x, y):
        left = jnp.where(lax.rem(step, 3) == 2, 0, 1)
        left = jnp.where(step >= self.changes[0], 2, left)
        left = jnp.where(step >= self.changes[1], 0, left)
        term = jnp.dot(
            self.left_t[left, x, y],
            self.right[:, self.columns(step, kind)],
            preferred_element_type=jnp.float32,
        )
        return term

    def x_first(self, step, kind):
        return 1 if kind == 0 else jnp.where(lax.rem(step, 5) == 4, 1, 0)

    def beside(self, by_x):
        row, level, column = neighbours()[:3]
        core = place()[2]
        other_row = by_x * (1 - row) + (1 - by_x) * row
        other_column = by_x * column + (1 - by_x) * (1 - column)
        return (other_row, 2 * level + other_column, core)

    def first_copy(self, step, kind):
        out, into = lax.rem(step, 3), lax.rem(step, 6)
        return remote(
            self.send_one.at[out, kind],
            self.recv_one.at[into, kind],
            self.ss_one.at[out, kind],
            self.rs_one.at[into, kind],
            self.beside(self.x_first(step, kind)),
        )

    def second_copy(self, step, kind):
        out, into = lax.rem(step, 3), lax.rem(step, 6)
        return remote(
            self.send_two.at[out, kind],
            self.recv_two.at[into, kind],
            self.ss_two.at[out, kind],
            self.rs_two.at[into, kind],
            self.beside(1 - self.x_first(step, kind)),
        )

    def third_copy(self, step, kind, k):
        row, level, column, beside_x, beside_y, along_z = neighbours()
        target = lax.rem(level + k + 1, 4)
        out, into = lax.rem(step, 4), lax.rem(step, 4)
        return remote(
            self.kept.at[out, kind, pl.ds(pl.multiple_of(target * self.share, 16), self.share)],
            self.recv_three.at[into, kind, k],
            self.ss_three.at[out, kind, k],
            self.rs_three.at[into, kind, k],
            along_z[k],
        )

    def pieces(self, step, act):
        act(0)

        @pl.when(step < self.n - 1)
        def _():
            act(1)

    def first(self, step):
        row, level, column = neighbours()[:3]
        slot = lax.rem(step, 3)

        def act(kind):
            by_x = self.x_first(step, kind)
            for half in range(2):
                x = by_x * (1 - row) + (1 - by_x) * half
                y = by_x * half + (1 - by_x) * (1 - column)
                self.send_one[slot, kind, half] = self.product(step, kind, x, y).astype(
                    jnp.bfloat16
                )
            self.first_copy(step, kind).start()

        self.pieces(step, act)

    def second(self, step):
        row, level, column = neighbours()[:3]
        slot, came, keep = lax.rem(step, 3), lax.rem(step, 6), lax.rem(step, 4)
        self.pieces(step, lambda kind: self.first_copy(step, kind).wait())

        def act(kind):
            by_x = self.x_first(step, kind)
            x = by_x * row + (1 - by_x) * (1 - row)
            y = by_x * (1 - column) + (1 - by_x) * column
            arrived = self.recv_one.at[came, kind]
            mine = by_x * column + (1 - by_x) * row
            away = self.product(step, kind, x, y) + arrived[1 - mine].astype(jnp.float32)
            self.send_two[slot, kind] = away.astype(jnp.bfloat16)
            here = self.product(step, kind, row, column) + arrived[mine].astype(jnp.float32)
            self.kept[keep, kind] = here.astype(jnp.bfloat16)

        self.pieces(step, act)
        self.pieces(step, lambda kind: self.second_copy(step, kind).start())

    def third(self, step):
        came, keep = lax.rem(step, 6), lax.rem(step, 4)

        def act(kind):
            self.second_copy(step, kind).wait()
            here = self.kept[keep, kind].astype(jnp.float32) + self.recv_two[came, kind].astype(
                jnp.float32
            )
            self.kept[keep, kind] = here.astype(jnp.bfloat16)
            for k in range(3):
                self.third_copy(step, kind, k).start()

        self.pieces(step, act)

    def last(self, step):
        level = neighbours()[1]
        came, keep = lax.rem(step, 4), lax.rem(step, 4)
        mine = pl.ds(pl.multiple_of(level * self.share, 16), self.share)

        @pl.when(step >= 2)
        def _():
            self.each_save(step - 2, lambda copy: copy.wait())

        def act(kind):
            total = self.kept[keep, kind, mine].astype(jnp.float32)
            for k in range(3):
                self.third_copy(step, kind, k).wait()
                total = total + self.recv_three[came, kind, k].astype(jnp.float32)
            self.own[lax.rem(step, 2), :, kind * PIECE : (kind + 1) * PIECE] = total

        self.pieces(step, act)
        self.each_save(step, lambda copy: copy.start())

    def turn(self, step):
        for stage, lag in (
            (self.first, 0),
            (self.second, SECOND),
            (self.third, THIRD),
            (self.last, LAST),
        ):

            @pl.when(jnp.logical_and(step >= lag, step < self.n + lag))
            def _():
                stage(step - lag)


def backward_kernel(
    order,
    ids,
    q_in,
    k_in,
    v_in,
    mixed_t_in,
    lse_in,
    cotangent,
    left_in,
    normed_in,
    right_in,
    mixed_low,
    middle,
    near,
    far,
    tokens,
    gains_in,
    tables,
    input_grad,
    layer_out,
    gate_grad,
    up_grad,
    down_grad,
    query_grad,
    key_grad,
    value_grad,
    out_grad,
    gain_out,
    q,
    q_t,
    k,
    k_t,
    v,
    d_own,
    d_slots,
    d,
    d_t,
    dq_t,
    lse,
    delta,
    dk,
    dv,
    dq_slots,
    dkv_sorted,
    dkv_slots,
    dkv_other,
    dq_own,
    dkv_own,
    weight,
    middle_ring,
    input_ring,
    part,
    part_other,
    total,
    staged,
    grad_mid,
    gain_two_grad,
    left_t,
    right,
    gain_columns,
    gain_messages,
    gain_all,
    own,
    send_one,
    recv_one,
    send_two,
    recv_two,
    kept,
    recv_three,
    loads,
    load_first,
    send_gain,
    recv_gain,
    load_left_sem,
    load_w,
    load_ring,
    save_rows,
    save_sem,
    send_d,
    recv_d,
    send_q,
    recv_q,
    send_x,
    recv_x,
    send_k,
    recv_k,
    send_p,
    recv_p,
    save,
    *sems,
):
    row, spot, core = place()
    low, full = jnp.bfloat16, jnp.float32
    rows, width = staged.shape
    length = 8 * rows
    runs, tiles = length // RUN, length // TILE
    per_device = rows // RUN
    halves = TILE // RUN
    share = width // 16
    quarter = 4 * share
    sibling = (row, spot, 1 - core)
    qkv_width = 16 * HEAD
    out_width = mixed_low.shape[1]
    near_at = right_in.shape[1] // (2 * PIECE)
    n = near_at + (qkv_width + out_width + PIECE) // (2 * PIECE)
    grads = (gate_grad, up_grad, down_grad, query_grad, key_grad, value_grad, out_grad)
    changes = (near_at, near_at + qkv_width // (2 * PIECE))
    sums = Reduce(
        n,
        changes,
        (left_t, right, own, grads, save)
        + (send_one, recv_one, send_two, recv_two, kept, recv_three)
        + sems,
    )

    def stage(source):
        return pltpu.make_async_copy(source, staged, load_left_sem)

    early_loads = [
        pltpu.make_async_copy(source, target, loads.at[index])
        for index, (source, target) in enumerate(
            [
                (q_in, q_t),
                (k_in, k),
                (v_in, d_t),
                (mixed_t_in, dq_t),
                (lse_in, lse),
                (middle, total),
            ]
        )
    ]

    first_loads = [
        pltpu.make_async_copy(left_in, left_t.at[pl.ds(0, 2)], load_first.at[4])
    ] + [
        pltpu.make_async_copy(
            right_in.at[:, pl.ds(3 * FEED * piece, 3 * FEED)],
            right.at[:, pl.ds(3 * FEED * piece, 3 * FEED)],
            load_first.at[piece],
        )
        for piece in range(4)
    ]


    def load_block(index, piece, part_of, start):
        lanes = pl.ds(3 * FEED * piece + start + part_of * PIECE, PIECE)
        levels = pl.ds(2 * lax.rem(index, 2), 2)
        return pltpu.make_async_copy(
            far.at[index // 2, levels, :, :, lanes], held_block(piece, part_of), load_w.at[piece]
        )

    def held_block(piece, part_of):
        levels = pl.ds(2 * (part_of % 2), 2)
        return weight.at[piece, part_of // 2, levels, :, :, pl.ds(0, PIECE)]

    def load_blocks(index, piece, start, parts):
        for part_of in range(parts):
            load_block(index, piece, part_of, start).start()

    def row_products(start, parts, landing):
        def block(index, carry):
            term = jnp.zeros((rows, quarter), full)
            for piece in range(4):
                for part_of in range(parts):
                    load_block(index, piece, part_of, start).wait()
                for part_of in range(parts):
                    at = 3 * FEED * piece + start + part_of * PIECE
                    term = term + contract_cols(
                        right[:, at : at + PIECE],
                        held_block(piece, part_of)[...].reshape(quarter, PIECE),
                    )

                @pl.when(index + 1 < 4)
                def _():
                    load_blocks(index + 1, piece, start, parts)

            part[:, tile_at(index, quarter)] = term.astype(low)
            pair_copy(index, landing).start()
            return carry

        lax.fori_loop(0, 4, block, 0)

    def pair_copy(index, landing):
        cut = pl.ds(pl.multiple_of(index * quarter, quarter), quarter)
        return remote(
            part.at[:, cut],
            part_other.at[landing, :, cut],
            send_p.at[index],
            recv_p.at[landing, index],
            sibling,
        )

    def second_back():
        row_products(0, 4, 0)
        for index in range(2):
            load_out_weight(index).start()

    def load_out_weight(index):
        lanes = pl.ds(qkv_width + index * 4 * HEAD, 4 * HEAD)
        return pltpu.make_async_copy(
            near.at[:, :, :, :, lanes], weight.at[index], load_w.at[index]
        )

    d_copies = []
    for step in range(4):
        slot = lax.rem(spot + step, 4)
        chip = 4 * core + slot
        for other in range(2):
            parts = (
                d_own.at[2 * slot + other],
                d_slots.at[spot],
                send_d.at[step, other],
                recv_d.at[spot],
                (row, chip, other),
            )
            d_copies.append((parts, jnp.logical_and(chip == spot, core == other)))

    def middle_back():
        for index in range(4):
            pair_copy(index, 0).wait()
        early_loads[5].wait()
        stage(cotangent).wait()
        chunk = rows // 8

        def block(index, gain_grad):
            cut = tile_at(index, chunk)
            grad = part[cut].astype(full) + part_other[0, cut].astype(full)
            values = total[cut]
            inverse = lax.rsqrt(jnp.mean(values * values, axis=-1, keepdims=True) + epsilon)
            unit = values * inverse
            scaled = grad * gains_in[1:2]
            mean = jnp.mean(scaled * unit, axis=-1, keepdims=True)
            result = staged[cut].astype(full) + inverse * (scaled - unit * mean)
            total[cut] = result
            grad_mid[cut] = result.astype(low)
            return gain_grad + jnp.sum(grad * unit, axis=0, keepdims=True)

        gain_two_grad[...] = lax.fori_loop(0, 8, block, jnp.zeros((1, width), full))
        for index in range(2):
            load_out_weight(index).wait()
            grad = dot_f32(grad_mid[...], weight[index].reshape(width, 4 * HEAD)).T.astype(low)
            for head in range(4):
                for run in range(per_device):
                    d_own[4 * index + head, run] = grad[
                        head * HEAD : (head + 1) * HEAD, run * RUN : (run + 1) * RUN
                    ]
        for parts, is_self in d_copies:
            move(*parts, is_self)


    def prepare():
        for copy in early_loads[:5]:
            copy.wait()
        for index in range(tiles):
            cut = pl.ds(index * TILE, TILE)
            q[cut] = q_t[:, cut].T
            k_t[:, cut] = k[halves * index : halves * (index + 1)].reshape(TILE, HEAD).T
            v[cut] = d_t[:, cut].T

    def take_cotangents():
        for index in range(8):
            remote(
                d_slots.at[index], d_slots.at[index], send_d.at[0, 0], recv_d.at[index], sibling
            ).wait_recv()

        def sort_run(index, carry):
            cols = tile_at(index, RUN)
            run = d_slots[order[index, 0], order[index, 1]]
            d_t[:, cols] = run
            d[cols] = run.T
            delta[:, cols] = jnp.sum(run.astype(full) * dq_t[:, cols], axis=0, keepdims=True)
            return carry

        lax.fori_loop(0, runs, sort_run, 0)
        dq_t[...] = jnp.zeros_like(dq_t)

    scale = HEAD ** (-0.5)

    def key_tile(block):
        cut = tile_at(block, TILE)
        both = pl.ds(block * halves, halves)
        keys, values = k[both].reshape(TILE, HEAD), v[cut]
        keys_t = k_t[:, cut]
        dk[...] = jnp.zeros_like(dk)
        dv[...] = jnp.zeros_like(dv)

        def query_tile(index, diagonal):
            cols = tile_at(index, TILE)
            scores = dot_f32(keys, q_t[:, cols]) * (scale * LOG2_E)
            if diagonal:
                scores = causal(scores)
            probs = jnp.exp2(scores - lse[:, cols])
            dv[...] += dot_f32(probs.astype(low), d[cols])
            grad_probs = dot_f32(values, d_t[:, cols])
            grad_scores = (probs * (grad_probs - delta[:, cols])).astype(low)
            dk[...] += dot_f32(grad_scores, q[cols])
            dq_t[:, cols] += dot_f32(keys_t, grad_scores)

        query_tile(block, True)

        def later(index, inner):
            query_tile(index, False)
            return inner

        lax.fori_loop(block + 1, tiles, later, 0)
        for kind, value in enumerate(((dk[...] * scale).T.astype(low), dv[...].T.astype(low))):
            for half in range(halves):
                dkv_sorted[block * halves + half, kind] = value[:, half * RUN : (half + 1) * RUN]

    def key_tiles(start, stop):
        def one(block, carry):
            key_tile(block)
            return carry

        lax.fori_loop(start, stop, one, 0)

    swap = remote(dkv_slots.at[:, :, 1 - core], dkv_other, send_x, recv_x, sibling)
    dq_copies = return_copies(dq_slots, dq_own, send_q, recv_q)
    slot, owner = lax.rem(spot, 4), spot // 4
    dkv_copies = []
    for step in range(8):
        chip = lax.rem(spot + step, 8)
        parts = (
            dkv_slots.at[:, chip, core],
            dkv_own.at[slot, :, core],
            send_k.at[step],
            recv_k.at[slot, core],
            (row, chip, owner),
        )
        dkv_copies.append((parts, (owner == core) if step == 0 else False))

    def send_back():
        def unsort_run(run, carry):
            index = ids[run]
            for kind in range(2):
                dkv_slots[kind, run // per_device, run % per_device] = dkv_sorted[index, kind]
            return carry

        lax.fori_loop(0, runs, unsort_run, 0)
        swap.start()

        def turn_run(index, carry):
            value = dq_t[:, tile_at(index, RUN)] * scale
            d_slots[index // per_device, index % per_device] = value.astype(low)
            return carry

        lax.fori_loop(0, runs, turn_run, 0)

        def unsort_queries(run, carry):
            value = d_slots[order[runs + run, 0], order[runs + run, 1]]
            dq_slots[run // per_device, run % per_device] = value
            return carry

        lax.fori_loop(0, runs, unsort_queries, 0)
        start_return(dq_copies)

    def add_pairs():
        swap.wait()
        for chip in range(8):
            both = dkv_slots[:, chip, core].astype(full) + dkv_other[:, chip].astype(full)
            dkv_slots[:, chip, core] = both.astype(low)
        start_return(dkv_copies)


    def feed_forward():
        row_products(2 * FEED, 2, 1)
        for group in range(4):
            load_group(group).start()

    save_layer = pltpu.make_async_copy(part, layer_out, save_sem)

    def finish_layer():
        for index in range(4):
            pair_copy(index, 1).wait()
        pieces = width // PIECE

        def load_piece(index):
            lanes = pl.ds(index * PIECE, PIECE)
            return pltpu.make_async_copy(
                middle.at[:, lanes], middle_ring.at[index % 2], load_ring.at[index % 2]
            )

        load_piece(0).start()
        for index in range(pieces):
            if index + 1 < pieces:
                load_piece(index + 1).start()
            load_piece(index).wait()
            cut = pl.ds(index * PIECE, PIECE)
            value = part[:, cut].astype(full) + part_other[1, :, cut].astype(full)
            part[:, cut] = (value + middle_ring[index % 2]).astype(low)
        save_layer.start()


    def load_group(group):
        lanes = pl.ds(group * 4 * HEAD, 4 * HEAD)
        return pltpu.make_async_copy(
            near.at[:, :, :, :, lanes], weight.at[group], load_w.at[group]
        )

    load_mixed = pltpu.make_async_copy(
        mixed_low, right.at[:, pl.ds(qkv_width, out_width)], loads.at[0]
    )

    def project_back():
        load_mixed.start()
        for head in range(8):
            remote(
                dq_own.at[head], dq_own.at[head], send_q.at[0], recv_q.at[head], sibling
            ).wait_recv()
        for slot_in in range(4):
            for core_in in range(2):
                target = dkv_own.at[slot_in, :, core_in]
                remote(
                    target, target, send_k.at[0], recv_k.at[slot_in, core_in], sibling
                ).wait_recv()
        for group in range(4):
            for run in range(per_device):
                cols = slice(run * RUN, (run + 1) * RUN)
                turned = []
                for head in range(4):
                    if group < 2:
                        value = dq_own[4 * group + head, run]
                    else:
                        value = dkv_own[head, group - 2, run]
                    if group < 3:
                        front, back = value[:HALF].astype(full), value[HALF:].astype(full)
                        cos_part, sin_part = tables[0, :, cols], tables[1, :, cols]
                        turned.append((front * cos_part + back * sin_part).astype(low))
                        turned.append((back * cos_part - front * sin_part).astype(low))
                    else:
                        turned.append(value)
                right[cols, group * 4 * HEAD : (group + 1) * 4 * HEAD] = jnp.concatenate(
                    turned, axis=0
                ).T
        load_mixed.wait()

    def project_normed():
        save_layer.wait()
        for group in range(4):
            load_group(group).wait()
        stage(tokens).start()

        def block(index, carry):
            term = jnp.zeros((rows, quarter), full)
            for group in range(4):
                held = weight[group, index // 2, pl.ds(2 * lax.rem(index, 2), 2)]
                term = term + contract_cols(
                    right[:, group * 4 * HEAD : (group + 1) * 4 * HEAD],
                    held.reshape(quarter, 4 * HEAD),
                )
            part[:, tile_at(index, quarter)] = term.astype(low)
            pair_copy(index, 0).start()
            return carry

        lax.fori_loop(0, 4, block, 0)

    def save_input(index):
        cut = tile_at(index, rows // 8)
        slot = lax.rem(index, 2)
        return pltpu.make_async_copy(
            input_ring.at[slot], input_grad.at[cut], save_rows.at[slot]
        )

    def norm_back():
        stage(tokens).wait()
        for index in range(4):
            pair_copy(index, 0).wait()
        chunk = rows // 8

        def block(index, gain_grad):
            cut = tile_at(index, chunk)
            grad = part[cut].astype(full) + part_other[0, cut].astype(full)
            values = staged[cut].astype(full)
            inverse = lax.rsqrt(jnp.mean(values * values, axis=-1, keepdims=True) + epsilon)
            unit = values * inverse
            scaled = grad * gains_in[0:1]
            mean = jnp.mean(scaled * unit, axis=-1, keepdims=True)
            result = total[cut] + inverse * (scaled - unit * mean)

            @pl.when(index >= 2)
            def _():
                save_input(index - 2).wait()

            input_ring[lax.rem(index, 2)] = result.reshape(chunk, 1, width)
            save_input(index).start()
            return gain_grad + jnp.sum(grad * unit, axis=0, keepdims=True)

        gain_one_grad = lax.fori_loop(0, 8, block, jnp.zeros((1, width), full))
        lines = jnp.concatenate(
            [gain_one_grad, gain_two_grad[...], jnp.zeros((6, width), full)], axis=0
        )
        gain_columns[...] = lines.T
        for shard in range(16):
            held = gain_columns[shard * share : (shard + 1) * share]
            gain_messages[shard] = jnp.pad(held, ((0, WIDE - share), (0, 0))).T
        for copy in gain_copies:
            copy.start()
        gain_all[own_shard()] = gain_messages[own_shard()]

    gain_copies, gain_from = exchange_messages(
        lambda shard: gain_messages.at[shard], gain_all, send_gain, recv_gain
    )

    def finish_gains():
        for wait in gain_from:
            wait()
        gain_out[...] = jnp.sum(gain_all[...], axis=0)

    def take_normed():
        stage(normed_in).start()
        stage(normed_in).wait()
        turn_left(left_t, 2, staged)

    def start_forward():
        for piece in range(4):
            load_blocks(0, piece, 2 * FEED, 2)

    for copy in first_loads:
        copy.start()
    stage(cotangent).start()
    for piece in range(4):
        load_blocks(0, piece, 0, 4)
    for copy in early_loads:
        copy.start()
    greet(group_others())
    first_loads[0].wait()
    first_loads[1].wait()

    def wait_right():
        for copy in first_loads[2:]:
            copy.wait()

    plan = {
        2: [wait_right, second_back],
        3: [middle_back],
        4: [prepare],
        5: [start_forward, take_cotangents],
    }
    tiles_from, tile_ranges = 5, ((0, 1), (1, 2), (2, 3), (3, 5), (5, 8))
    later = {
        9: [send_back],
        11: [add_pairs, feed_forward, finish_layer, take_normed],
        12: [project_back],
        15: [lambda: turn_left(left_t, 0, grad_mid), project_normed],
        16: [norm_back],
        n + LAST - 1: [finish_gains],
    }

    def run(step, carry):
        for when, tasks in plan.items():

            @pl.when(step == when)
            def _():
                for task in tasks:
                    task()

        @pl.when(jnp.logical_and(step >= tiles_from, step < tiles_from + len(tile_ranges)))
        def _():
            start, stop = 0, 0
            for index, (first_tile, past_tile) in enumerate(tile_ranges):
                start = jnp.where(step == tiles_from + index, first_tile, start)
                stop = jnp.where(step == tiles_from + index, past_tile, stop)
            key_tiles(start, stop)

        for when, tasks in later.items():

            @pl.when(step == when)
            def _():
                for task in tasks:
                    task()

        sums.turn(step)
        return carry

    lax.fori_loop(0, n + LAST, run, 0)
    for index in (6, 7):
        save_input(index).wait()
    for copy in gain_copies:
        copy.wait_send()
    for step in (n - 2, n - 1):
        sums.each_save(step, lambda copy: copy.wait())
    for copies in (d_copies, dq_copies, dkv_copies):
        for parts, is_self in copies:
            if is_self is False:
                remote(*parts).wait_send()
            else:

                @pl.when(jnp.logical_not(is_self))
                def _():
                    remote(*parts).wait_send()


def backward(order, ids, *arrays):
    dma = pltpu.SemaphoreType.DMA
    vmem = pltpu.VMEM
    low, full = jnp.bfloat16, jnp.float32
    q_sorted, k_sorted, v_sorted, mixed_t, lse, cotangent, left, normed, right = arrays[:9]
    mixed_low, middle, near, far, tokens, gains, tables = arrays[9:]
    rows, width = cotangent.shape
    length = 8 * rows
    share = width // 16
    feed, query, out_width = right.shape[1] // 3, 8 * HEAD, mixed_low.shape[1]
    quarter = 4 * share
    per_device = rows // RUN
    heads = (8, per_device, HEAD, RUN)
    tall, flat = (length, HEAD), (HEAD, length)
    by_run = (length // RUN, RUN, HEAD)
    block = (rows, width)
    smem_spec = pl.BlockSpec(memory_space=pltpu.SMEM)
    shape = jax.ShapeDtypeStruct
    return pl.pallas_call(
        backward_kernel,
        in_specs=[smem_spec] * 2 + [any_spec()] * 14 + [vmem_spec()] * 2,
        out_specs=[any_spec()] * 9 + [vmem_spec()],
        out_shape=[
            shape((rows, 1, width), full),
            shape(block, low),
            *[
                shape((share, wide), full)
                for wide in (feed, feed, feed, query, query // 2, query // 2, out_width)
            ],
            shape((8, WIDE), full),
        ],
        scratch_shapes=[
            vmem(tall, low),
            vmem(flat, low),
            vmem(by_run, low),
            vmem(flat, low),
            vmem(tall, low),
            vmem(heads, low),
            vmem(heads, low),
            vmem(tall, low),
            vmem(flat, low),
            vmem(flat, full),
            vmem((1, length), full),
            vmem((1, length), full),
            vmem((TILE, HEAD), full),
            vmem((TILE, HEAD), full),
            vmem(heads, low),
            vmem((length // RUN, 2, HEAD, RUN), low),
            vmem((2,) + heads, low),
            vmem((2, 8, HEAD, RUN), low),
            vmem(heads, low),
            vmem((4, 2, per_device, HEAD, RUN), low),
            vmem((4, 2, 4, 2, share, 4 * HEAD), low),
            vmem((2, rows, PIECE), full),
            vmem((2, rows // 8, 1, width), full),
            vmem(block, low),
            vmem((2,) + block, low),
            vmem(block, full),
            vmem(block, low),
            vmem(block, low),
            vmem((1, width), full),
            vmem((3, 2, 2, quarter, rows), low),
            vmem(right.shape, low),
            vmem((width, 8), full),
            vmem((16, 8, WIDE), full),
            vmem((16, 8, WIDE), full),
            vmem((2, share, 2 * PIECE), full),
            vmem((3, 2, 2, quarter, PIECE), low),
            vmem((6, 2, 2, quarter, PIECE), low),
            vmem((3, 2, quarter, PIECE), low),
            vmem((6, 2, quarter, PIECE), low),
            vmem((4, 2, quarter, PIECE), low),
            vmem((4, 2, 3, share, PIECE), low),
            dma((7,)),
            dma((5,)),
            dma((16,)),
            dma((16,)),
            dma(()),
            dma((4,)),
            dma((2,)),
            dma((2,)),
            dma(()),
            dma((4, 2)),
            dma((8,)),
            dma((8,)),
            dma((8,)),
            dma(()),
            dma(()),
            dma((8,)),
            dma((4, 2)),
            dma((4,)),
            dma((2, 4)),
            dma((2, 3)),
            dma((3, 2)),
            dma((6, 2)),
            dma((3, 2)),
            dma((6, 2)),
            dma((4, 2, 3)),
            dma((4, 2, 3)),
        ],
        compiler_params=pltpu.CompilerParams(
            collective_id=2, has_side_effects=True, vmem_limit_bytes=62 * 1024 * 1024
        ),
        name="backward",
    )(
        order,
        ids,
        *arrays,
    )


def by_heads(
    tokens,
    positions,
    gain_one,
    gain_two,
    w_query,
    w_key,
    w_value,
    w_out,
    w_gate,
    w_up,
    w_down,
    cotangent,
):
    rows, _, width = tokens.shape
    share = gain_one.shape[0]
    flat_in = tokens.reshape(rows, width)
    (
        near,
        far,
        normed,
        q_sorted,
        k_sorted,
        v_sorted,
        mixed_t,
        lse,
        mixed_low,
        middle,
        second,
        right,
        gains,
        tables,
        left,
        order,
        ids,
    ) = forward(
        flat_in,
        positions.reshape(1, rows),
        gain_one.reshape(1, share),
        gain_two.reshape(1, share),
        w_query,
        w_key,
        w_value,
        w_out.T,
        w_gate,
        w_up,
        w_down.T,
        cotangent.reshape(rows, width),
    )
    input_grad, layer_out, *grads, gain_grads = backward(
        order,
        ids,
        q_sorted,
        k_sorted,
        v_sorted,
        mixed_t,
        lse,
        cotangent.reshape(rows, width),
        left,
        normed,
        right,
        mixed_low,
        middle,
        near,
        far,
        flat_in,
        gains,
        tables,
    )
    grad_gate, grad_up, grad_down, grad_query, grad_key, grad_value, grad_out = grads
    return (
        layer_out.reshape(rows, 1, width),
        input_grad,
        gain_grads[0, :share],
        gain_grads[1, :share],
        grad_query,
        grad_key,
        grad_value,
        grad_out.T,
        grad_gate,
        grad_up,
        grad_down.T,
    )


def solution(mesh):
    sizes = (mesh.shape["dp"], mesh.shape["context"], mesh.shape["tensor"])
    return jax.shard_map(
        by_heads if sizes == (2, 8, 2) else on_device,
        mesh=mesh,
        in_specs=(
            P("context", "dp", None),
            P("context", "dp"),
            P(("dp", "context")),
            P(("dp", "context")),
            P(("dp", "context"), "tensor"),
            P(("dp", "context"), "tensor"),
            P(("dp", "context"), "tensor"),
            P("tensor", ("dp", "context")),
            P(("dp", "context"), "tensor"),
            P(("dp", "context"), "tensor"),
            P("tensor", ("dp", "context")),
            P("context", "dp", None),
        ),
        out_specs=(
            P("context", "dp", None),
            P("context", "dp", None),
            P(("dp", "context")),
            P(("dp", "context")),
            P(("dp", "context"), "tensor"),
            P(("dp", "context"), "tensor"),
            P(("dp", "context"), "tensor"),
            P("tensor", ("dp", "context")),
            P(("dp", "context"), "tensor"),
            P(("dp", "context"), "tensor"),
            P("tensor", ("dp", "context")),
        ),
        check_vma=False,
    )
```

```python
import functools

import jax
import jax.numpy as jnp
import numpy as np
from jax import lax
from jax.experimental import pallas as pl
from jax.experimental.pallas import tpu as pltpu
from jax.sharding import PartitionSpec as P

HEAD = 96


epsilon = 1e-05
theta_base = 100000.0
masked_value = -1e30


def norm_forward(values_in, gain_vec):
    inverse = lax.rsqrt(jnp.mean(values_in * values_in, axis=-1, keepdims=True) + epsilon)
    unit_vals = values_in * inverse
    return (unit_vals, inverse, (unit_vals * gain_vec.astype(jnp.float32)).astype(jnp.bfloat16))


def norm_backward(grad_in, unit_vals, inverse, gain_vec):
    scaled = grad_in * gain_vec.astype(jnp.float32)
    grad_vals = inverse * (
        scaled - unit_vals * jnp.mean(scaled * unit_vals, axis=-1, keepdims=True)
    )
    return (grad_vals, jnp.sum(grad_in * unit_vals, axis=0))


def rotate(values_in, cos_part, sin_part):
    half_size = values_in.shape[-1] // 2
    front_half = values_in[..., :half_size]
    back_half = values_in[..., half_size:]
    return jnp.concatenate(
        [
            front_half * cos_part - back_half * sin_part,
            back_half * cos_part + front_half * sin_part,
        ],
        axis=-1,
    )


def contract_rows(left_mat, right_mat):
    return lax.dot_general(
        left_mat, right_mat, (((0,), (0,)), ((), ())), preferred_element_type=jnp.float32
    )


def contract_cols(left_mat, right_mat):
    return lax.dot_general(
        left_mat, right_mat, (((1,), (1,)), ((), ())), preferred_element_type=jnp.float32
    )


def on_device(
    tokens,
    positions,
    gain_one,
    gain_two,
    w_query,
    w_key,
    w_value,
    w_out,
    w_gate,
    w_up,
    w_down,
    cotangent,
):
    slot_count, seq_count, model_width = tokens.shape
    row_count = slot_count * seq_count
    gathered = (
        lax.all_gather(gain_one, ("dp", "context"), axis=0, tiled=True),
        lax.all_gather(gain_two, ("dp", "context"), axis=0, tiled=True),
        lax.all_gather(w_query, ("dp", "context"), axis=0, tiled=True),
        lax.all_gather(w_key, ("dp", "context"), axis=0, tiled=True),
        lax.all_gather(w_value, ("dp", "context"), axis=0, tiled=True),
        lax.all_gather(w_out, ("dp", "context"), axis=1, tiled=True),
        lax.all_gather(w_gate, ("dp", "context"), axis=0, tiled=True),
        lax.all_gather(w_up, ("dp", "context"), axis=0, tiled=True),
        lax.all_gather(w_down, ("dp", "context"), axis=1, tiled=True),
    )
    full_one, full_two, query_mat, key_mat, value_mat, out_mat, gate_mat, up_mat, down_mat = (
        gathered
    )
    heads_kv = key_mat.shape[1] // HEAD
    heads_q = query_mat.shape[1] // HEAD
    group_size = heads_q // heads_kv
    score_scale = HEAD ** (-0.5)
    half_size = HEAD // 2
    inv_freqs = theta_base ** (-2.0 * jnp.arange(half_size, dtype=jnp.float32) / HEAD)
    angles = positions.astype(jnp.float32)[:, :, None] * inv_freqs
    cos_part = jnp.cos(angles)[:, :, None, :]
    sin_part = jnp.sin(angles)[:, :, None, :]
    flat_in = tokens.astype(jnp.float32).reshape(row_count, model_width)
    unit_one, inverse_one, normed = norm_forward(flat_in, full_one)
    query_proj = jnp.dot(normed, query_mat, preferred_element_type=jnp.float32).reshape(
        slot_count, seq_count, heads_q, HEAD
    )
    key_proj = jnp.dot(normed, key_mat, preferred_element_type=jnp.float32).reshape(
        slot_count, seq_count, heads_kv, HEAD
    )
    value_low = (
        jnp.dot(normed, value_mat, preferred_element_type=jnp.float32)
        .astype(jnp.bfloat16)
        .reshape(slot_count, seq_count, heads_kv * HEAD)
    )
    queries = rotate(query_proj, cos_part, sin_part).astype(jnp.bfloat16)
    keys_low = (
        rotate(key_proj, cos_part, sin_part)
        .astype(jnp.bfloat16)
        .reshape(slot_count, seq_count, heads_kv * HEAD)
    )
    query_seq = jnp.transpose(
        queries.reshape(slot_count, seq_count, heads_kv, group_size, HEAD), (1, 2, 3, 0, 4)
    )
    query_pos = positions.T
    stat_shape = (seq_count, heads_kv, group_size, slot_count)
    initial = (
        jnp.full(stat_shape, masked_value, jnp.float32),
        jnp.zeros(stat_shape, jnp.float32),
        jnp.zeros(stat_shape + (HEAD,), jnp.float32),
    )
    key_piece = lax.all_gather(keys_low, "context", axis=0, tiled=True)
    value_piece = lax.all_gather(value_low, "context", axis=0, tiled=True)
    pos_piece = lax.all_gather(positions, "context", axis=0, tiled=True)
    piece_len = key_piece.shape[0]
    key_seq = jnp.transpose(key_piece.reshape(piece_len, seq_count, heads_kv, HEAD), (1, 2, 0, 3))
    value_seq = jnp.transpose(
        value_piece.reshape(piece_len, seq_count, heads_kv, HEAD), (1, 2, 0, 3)
    )
    pos_seq = pos_piece.T

    def per_sequence(seq_items):
        peak_val, totals, accum_vals, query_one, qpos_one, key_one, value_one, kpos_one = seq_items
        raw_scores = (
            jnp.einsum("hgqd,hkd->hgqk", query_one, key_one, preferred_element_type=jnp.float32)
            * score_scale
        )
        allowed = kpos_one[None, None, None, :] <= qpos_one[None, None, :, None]
        masked = jnp.where(allowed, raw_scores, masked_value)
        new_peak = jnp.maximum(peak_val, jnp.max(masked, axis=-1))
        decay_vals = jnp.exp(peak_val - new_peak)
        weights = jnp.where(allowed, jnp.exp(masked - new_peak[..., None]), 0.0)
        totals = totals * decay_vals + jnp.sum(weights, axis=-1)
        accum_vals = accum_vals * decay_vals[..., None] + jnp.einsum(
            "hgqk,hkd->hgqd",
            weights.astype(jnp.bfloat16),
            value_one,
            preferred_element_type=jnp.float32,
        )
        return (new_peak, totals, accum_vals)

    peak_val, totals, accum_vals = lax.map(
        per_sequence,
        (initial[0], initial[1], initial[2], query_seq, query_pos, key_seq, value_seq, pos_seq),
    )
    log_total = peak_val + jnp.log(totals)
    mixed_seq = accum_vals / totals[..., None]
    mixed_low = (
        jnp.transpose(mixed_seq, (3, 0, 1, 2, 4))
        .reshape(row_count, heads_q * HEAD)
        .astype(jnp.bfloat16)
    )
    branch = lax.psum(
        jnp.dot(mixed_low, out_mat, preferred_element_type=jnp.float32).astype(jnp.bfloat16),
        "tensor",
    ).astype(jnp.float32)
    middle = flat_in + branch
    unit_two, inverse_two, second = norm_forward(middle, full_two)
    gate_vals = jnp.dot(second, gate_mat, preferred_element_type=jnp.float32)
    up_vals = jnp.dot(second, up_mat, preferred_element_type=jnp.float32)
    sigmoid_vals = jax.nn.sigmoid(gate_vals)
    silu_vals = gate_vals * sigmoid_vals
    hidden = (silu_vals * up_vals).astype(jnp.bfloat16)
    mlp_part = lax.psum(
        jnp.dot(hidden, down_mat, preferred_element_type=jnp.float32).astype(jnp.bfloat16), "tensor"
    ).astype(jnp.float32)
    layer_out = (middle + mlp_part).astype(jnp.bfloat16).reshape(slot_count, seq_count, model_width)
    regathered = (
        lax.all_gather(gain_one, ("dp", "context"), axis=0, tiled=True),
        lax.all_gather(gain_two, ("dp", "context"), axis=0, tiled=True),
        lax.all_gather(w_query, ("dp", "context"), axis=0, tiled=True),
        lax.all_gather(w_key, ("dp", "context"), axis=0, tiled=True),
        lax.all_gather(w_value, ("dp", "context"), axis=0, tiled=True),
        lax.all_gather(w_out, ("dp", "context"), axis=1, tiled=True),
        lax.all_gather(w_gate, ("dp", "context"), axis=0, tiled=True),
        lax.all_gather(w_up, ("dp", "context"), axis=0, tiled=True),
        lax.all_gather(w_down, ("dp", "context"), axis=1, tiled=True),
    )
    full_one, full_two, query_mat, key_mat, value_mat, out_mat, gate_mat, up_mat, down_mat = (
        regathered
    )
    grad_low = cotangent.reshape(row_count, model_width)
    grad_down = contract_rows(hidden, grad_low)
    grad_hidden = contract_cols(grad_low, down_mat)
    grad_gate_low = (
        grad_hidden * up_vals * sigmoid_vals * (1.0 + gate_vals * (1.0 - sigmoid_vals))
    ).astype(jnp.bfloat16)
    grad_up_low = (grad_hidden * silu_vals).astype(jnp.bfloat16)
    grad_gate = contract_rows(second, grad_gate_low)
    grad_up = contract_rows(second, grad_up_low)
    grad_second = lax.psum(
        (contract_cols(grad_gate_low, gate_mat) + contract_cols(grad_up_low, up_mat)).astype(
            jnp.bfloat16
        ),
        "tensor",
    ).astype(jnp.float32)
    grad_mid_norm, grad_gain_two = norm_backward(grad_second, unit_two, inverse_two, full_two)
    grad_middle = grad_low.astype(jnp.float32) + grad_mid_norm
    grad_mid_low = grad_middle.astype(jnp.bfloat16)
    grad_out = contract_rows(mixed_low, grad_mid_low)
    grad_mixed = contract_cols(grad_mid_low, out_mat).astype(jnp.bfloat16)
    grad_mixed_seq = jnp.transpose(
        grad_mixed.reshape(slot_count, seq_count, heads_kv, group_size, HEAD), (1, 2, 3, 0, 4)
    )
    delta_rows = jnp.sum(grad_mixed_seq.astype(jnp.float32) * mixed_seq, axis=-1)
    kv_width = heads_kv * HEAD

    def block_grads(grad_query_acc, key_blk, value_blk, pos_blk):
        block_len = key_blk.shape[0]
        key_seq = jnp.transpose(key_blk.reshape(block_len, seq_count, heads_kv, HEAD), (1, 2, 0, 3))
        value_seq = jnp.transpose(
            value_blk.reshape(block_len, seq_count, heads_kv, HEAD), (1, 2, 0, 3)
        )
        raw_scores = (
            jnp.einsum("shgqd,shkd->shgqk", query_seq, key_seq, preferred_element_type=jnp.float32)
            * score_scale
        )
        allowed = pos_blk.T[:, None, None, None, :] <= query_pos[:, None, None, :, None]
        prob_vals = jnp.where(
            allowed,
            jnp.exp(jnp.where(allowed, raw_scores - log_total[..., None], masked_value)),
            0.0,
        )
        grad_value_blk = jnp.einsum(
            "shgqk,shgqd->kshd",
            prob_vals.astype(jnp.bfloat16),
            grad_mixed_seq,
            preferred_element_type=jnp.float32,
        )
        grad_probs = jnp.einsum(
            "shgqd,shkd->shgqk", grad_mixed_seq, value_seq, preferred_element_type=jnp.float32
        )
        grad_scores = (prob_vals * (grad_probs - delta_rows[..., None])).astype(jnp.bfloat16)
        grad_query_acc = grad_query_acc + jnp.einsum(
            "shgqk,shkd->shgqd", grad_scores, key_seq, preferred_element_type=jnp.float32
        )
        grad_key_blk = jnp.einsum(
            "shgqk,shgqd->kshd", grad_scores, query_seq, preferred_element_type=jnp.float32
        )
        return (
            grad_query_acc,
            grad_key_blk.reshape(block_len, seq_count, kv_width),
            grad_value_blk.reshape(block_len, seq_count, kv_width),
        )

    zero_query = jnp.zeros(stat_shape + (HEAD,), jnp.float32)
    key_all, value_all, pos_all = (
        lax.all_gather(keys_low, "context", axis=0, tiled=True),
        lax.all_gather(value_low, "context", axis=0, tiled=True),
        lax.all_gather(positions, "context", axis=0, tiled=True),
    )
    total_len = key_all.shape[0]
    block_size = min(512, total_len)
    block_count = total_len // block_size

    def key_block(grad_query_acc, block_items):
        key_blk, value_blk, pos_blk = block_items
        grad_query_acc, grad_key_blk, grad_value_blk = block_grads(
            grad_query_acc, key_blk, value_blk, pos_blk
        )
        return (grad_query_acc, (grad_key_blk, grad_value_blk))

    grad_query_acc, (grad_keys_all, grad_values_all) = lax.scan(
        key_block,
        zero_query,
        (
            key_all.reshape(block_count, block_size, seq_count, kv_width),
            value_all.reshape(block_count, block_size, seq_count, kv_width),
            pos_all.reshape(block_count, block_size, seq_count),
        ),
    )
    grad_key_own, grad_value_own = (
        lax.psum_scatter(
            grad_keys_all.reshape(total_len, seq_count, kv_width).astype(jnp.bfloat16),
            "context",
            scatter_dimension=0,
            tiled=True,
        ).astype(jnp.float32),
        lax.psum_scatter(
            grad_values_all.reshape(total_len, seq_count, kv_width).astype(jnp.bfloat16),
            "context",
            scatter_dimension=0,
            tiled=True,
        ).astype(jnp.float32),
    )
    grad_rot_q = jnp.transpose(grad_query_acc * score_scale, (3, 0, 1, 2, 4)).reshape(
        slot_count, seq_count, heads_q, HEAD
    )
    grad_q_low = (
        rotate(grad_rot_q, cos_part, -sin_part)
        .reshape(row_count, heads_q * HEAD)
        .astype(jnp.bfloat16)
    )
    grad_rot_k = (grad_key_own * score_scale).reshape(slot_count, seq_count, heads_kv, HEAD)
    grad_k_low = (
        rotate(grad_rot_k, cos_part, -sin_part).reshape(row_count, kv_width).astype(jnp.bfloat16)
    )
    grad_v_low = grad_value_own.reshape(row_count, kv_width).astype(jnp.bfloat16)
    grad_query = contract_rows(normed, grad_q_low)
    grad_key = contract_rows(normed, grad_k_low)
    grad_value = contract_rows(normed, grad_v_low)
    grad_normed = lax.psum(
        (
            contract_cols(grad_q_low, query_mat)
            + contract_cols(grad_k_low, key_mat)
            + contract_cols(grad_v_low, value_mat)
        ).astype(jnp.bfloat16),
        "tensor",
    ).astype(jnp.float32)
    grad_in_norm, grad_gain_one = norm_backward(grad_normed, unit_one, inverse_one, full_one)
    input_grad = (grad_middle + grad_in_norm).reshape(slot_count, seq_count, model_width)
    reduced = (
        lax.psum_scatter(grad_gain_one, ("dp", "context"), scatter_dimension=0, tiled=True),
        lax.psum_scatter(grad_gain_two, ("dp", "context"), scatter_dimension=0, tiled=True),
        lax.psum_scatter(grad_query, ("dp", "context"), scatter_dimension=0, tiled=True),
        lax.psum_scatter(grad_key, ("dp", "context"), scatter_dimension=0, tiled=True),
        lax.psum_scatter(grad_value, ("dp", "context"), scatter_dimension=0, tiled=True),
        lax.psum_scatter(grad_out, ("dp", "context"), scatter_dimension=1, tiled=True),
        lax.psum_scatter(grad_gate, ("dp", "context"), scatter_dimension=0, tiled=True),
        lax.psum_scatter(grad_up, ("dp", "context"), scatter_dimension=0, tiled=True),
        lax.psum_scatter(grad_down, ("dp", "context"), scatter_dimension=1, tiled=True),
    )
    return (
        layer_out,
        input_grad,
        reduced[0],
        reduced[1],
        reduced[2],
        reduced[3],
        reduced[4],
        reduced[5],
        reduced[6],
        reduced[7],
        reduced[8],
    )


WIDE = 128
HALF = HEAD // 2
RUN = 256
TILE = 512
LOG2_E = 1.4426950408889634
MESH = pl.DeviceIdType.MESH
PIECE = 256
FEED = 512
VMEM_LIMIT = 56 * 1024 * 1024


def any_spec():
    return pl.BlockSpec(memory_space=pl.ANY)


def vmem_spec():
    return pl.BlockSpec(memory_space=pltpu.VMEM)


def place():
    return lax.axis_index("dp"), lax.axis_index("context"), lax.axis_index("tensor")


def greet(devices):
    barrier = pltpu.get_barrier_semaphore()
    for device in devices:
        pl.semaphore_signal(barrier, inc=1, device_id=device, device_id_type=MESH)
    pl.semaphore_wait(barrier, len(devices))


def sequence_others():
    row, spot, core = place()
    return [
        (row, lax.rem(spot + shift, 8), lax.rem(core + flip, 2))
        for shift in range(8)
        for flip in range(2)
        if shift or flip
    ]


def lane_freqs():
    return jnp.asarray(
        np.power(np.float32(theta_base), np.float32(-2.0) * np.arange(HALF, dtype=np.float32) / HEAD)
    ).reshape(HALF, 1)


def dot_f32(left, right):
    return jnp.dot(left, right, preferred_element_type=jnp.float32)


def own_shard():
    row, spot, core = place()
    return row * 8 + spot


def group_others():
    row, spot, core = place()
    return sequence_others() + [(1 - row, lax.rem(spot + shift, 8), core) for shift in range(8)]


def exchange_messages(message_to, landing, send, recv):
    row, spot, core = place()
    copies, waits = [], []

    def one(flip, shift):
        at = flip * 8 + shift
        to_row = lax.rem(row + flip, 2)
        chip, source = lax.rem(spot + shift, 8), lax.rem(spot + 8 - shift, 8)
        device = (to_row, chip, core)
        message = message_to(to_row * 8 + chip)
        copies.append(
            remote(message, landing.at[row * 8 + spot], send.at[at], recv.at[at], device)
        )
        came = landing.at[to_row * 8 + source]
        waits.append(remote(came, came, send.at[at], recv.at[at], device).wait_recv)

    for flip in range(2):
        for shift in range(8):
            if flip or shift:
                one(flip, shift)
    return copies, waits


def turn_left(left_t, index, source):
    quarter = source.shape[1] // 4
    share = quarter // 4
    for piece in range(4):
        turned = source[:, piece * quarter : (piece + 1) * quarter].T
        for inner in range(4):
            x, z, y = piece // 2, 2 * (piece % 2) + inner // 2, inner % 2
            left_t[index, x, y, z * share : (z + 1) * share] = turned[
                inner * share : (inner + 1) * share
            ]


def remote(source, target, send, recv, device):
    return pltpu.make_async_remote_copy(
        src_ref=source,
        dst_ref=target,
        send_sem=send,
        recv_sem=recv,
        device_id=device,
        device_id_type=MESH,
    )


def move(source, target, send, recv, device, is_self):
    @pl.when(is_self)
    def _():
        pltpu.make_async_copy(source, target, recv).start()

    @pl.when(jnp.logical_not(is_self))
    def _():
        remote(source, target, send, recv, device).start()


def return_copies(ref, out, send, recv):
    row, spot, core = place()
    head = 2 * lax.rem(spot, 4) + core
    owner = spot // 4
    copies = []
    for step in range(8):
        chip = lax.rem(spot + step, 8)
        is_self = (owner == core) if step == 0 else False
        parts = (ref.at[chip], out.at[head], send.at[step], recv.at[head], (row, chip, owner))
        copies.append((parts, is_self))
    return copies


def start_return(copies):
    for parts, is_self in copies:
        if is_self is False:
            remote(*parts).start()
        else:
            move(*parts, is_self)


def finish_return(copies, out, send, recv):
    row, spot, core = place()
    for head in range(8):
        remote(
            out.at[head], out.at[head], send.at[0], recv.at[head], (row, spot, 1 - core)
        ).wait_recv()
    for parts, is_self in copies:
        if is_self is False:
            remote(*parts).wait_send()
        else:

            @pl.when(jnp.logical_not(is_self))
            def _():
                remote(*parts).wait_send()


def tile_at(index, size):
    return pl.ds(pl.multiple_of(index * size, size), size)


def causal(scores):
    keys = lax.broadcasted_iota(jnp.int32, scores.shape, 0)
    queries = lax.broadcasted_iota(jnp.int32, scores.shape, 1)
    return jnp.where(keys <= queries, scores, masked_value)


def neighbours():
    row, spot, core = place()
    level, column = spot // 2, lax.rem(spot, 2)
    beside_x = (1 - row, spot, core)
    beside_y = (row, 2 * level + 1 - column, core)
    along_z = [(row, 2 * lax.rem(level + k, 4) + column, core) for k in (1, 2, 3)]
    return row, level, column, beside_x, beside_y, along_z


class Gather:
    def __init__(self, own, whole, start, width, piece, sems):
        self.own, self.whole = own.at[:, pl.ds(start, width)], whole
        self.start, self.width = start, width
        names = ("send_z", "recv_z", "send_x", "recv_x", "send_y", "recv_y", "send_d", "recv_d")
        for name, sem in zip(names + ("local",), sems):
            setattr(self, name, sem.at[piece])

    def block(self, x, z, y, half=None):
        cut = self.width * 7 // 12 // WIDE * WIDE
        start, width = self.start, self.width
        if half == 0:
            width = cut
        elif half == 1:
            start, width = start + cut, width - cut
        return self.whole.at[x, z, y, :, pl.ds(start, width)]

    def arrived(self, target, recv_sem):
        device = neighbours()[3]
        remote(target, target, self.send_x.at[0], recv_sem, device).wait_recv()

    def copy_z(self, z, up, own=False):
        row, level, column, beside_x, beside_y = neighbours()[:5]
        core = place()[2]
        target = level + 1 if up else level - 1
        block = self.block(row, z, column)
        return remote(
            self.own if own else block,
            block,
            self.send_z.at[int(up), z],
            self.recv_z.at[z],
            (row, 2 * target + column, core),
        )

    def copies_xy(self, z, own=False):
        row, level, column, beside_x, beside_y = neighbours()[:5]
        block = self.block(row, z, column)
        source = self.own if own else block
        return [
            remote(source, block, self.send_x.at[z], self.recv_x.at[z], beside_x),
            remote(source, block, self.send_y.at[z], self.recv_y.at[z], beside_y),
        ]

    def copies_diagonal(self, z):
        row, level, column, beside_x, beside_y = neighbours()[:5]
        by_y = self.block(1 - row, z, column, 1)
        by_x = self.block(row, z, 1 - column, 0)
        return [
            remote(by_y, by_y, self.send_d.at[0, z], self.recv_d.at[0, z], beside_y),
            remote(by_x, by_x, self.send_d.at[1, z], self.recv_d.at[1, z], beside_x),
        ]

    def own_copy(self):
        row, level, column = neighbours()[:3]
        return pltpu.make_async_copy(self.own, self.block(row, level, column), self.local)

    def each_at(self, hop, act):
        level = neighbours()[1]

        @pl.when(level >= hop)
        def _():
            act(level - hop, True)

        @pl.when(level + hop <= 3)
        def _():
            act(level + hop, False)

    def start_z(self, z, up, own=False):
        level = neighbours()[1]

        @pl.when(level < 3 if up else level > 0)
        def _():
            self.copy_z(z, up, own).start()

    def place_own(self):
        self.own_copy().start()

    def open(self):
        level = neighbours()[1]
        self.start_z(level, True, True)
        self.start_z(level, False, True)
        for copy in self.copies_xy(level, True):
            copy.start()

    def hop(self, hop):
        def act(z, up):
            row, level, column = neighbours()[:3]
            self.arrived(self.block(row, z, column), self.recv_z.at[z])
            self.start_z(z, up)
            for copy in self.copies_xy(z):
                copy.start()

        self.each_at(hop, act)

    def turn_diagonal(self, z):
        row, level, column = neighbours()[:3]
        by_y, by_x = self.copies_diagonal(z)
        self.arrived(self.block(1 - row, z, column), self.recv_x.at[z])
        by_y.start()
        self.arrived(self.block(row, z, 1 - column), self.recv_y.at[z])
        by_x.start()

    def diagonal(self, hop):
        if hop == 0:
            self.turn_diagonal(neighbours()[1])
        else:
            self.each_at(hop, lambda z, up: self.turn_diagonal(z))

    def finish(self):
        row, level, column = neighbours()[:3]
        self.own_copy().wait()
        for z in range(4):
            self.arrived(self.block(1 - row, z, 1 - column, 1), self.recv_d.at[0, z])
            self.arrived(self.block(1 - row, z, 1 - column, 0), self.recv_d.at[1, z])

    def close_z(self):
        level = neighbours()[1]

        def sent(z, up):
            @pl.when(level < 3 if up else level > 0)
            def _():
                self.copy_z(z, up).wait_send()

        sent(level, True)
        sent(level, False)
        for hop in range(1, 4):
            self.each_at(hop, sent)

    def close(self):
        self.close_z()
        for z in range(4):
            for copy in self.copies_xy(z) + self.copies_diagonal(z):
                copy.wait_send()


class PlaneGather(Gather):
    def plane(self, z):
        return self.whole.at[:, z, :, :, pl.ds(self.start, self.width)]

    def copy_z(self, z, up, own=False):
        row, level, column = neighbours()[:3]
        target = level + 1 if up else level - 1
        plane = self.plane(z)
        return remote(
            plane,
            plane,
            self.send_z.at[int(up), z],
            self.recv_z.at[z],
            (row, 2 * target + column, place()[2]),
        )

    def open(self):
        for copy in self.copies_xy(neighbours()[1], True):
            copy.start()

    def spread(self):
        row, level, column = neighbours()[:3]
        self.arrived(self.block(1 - row, level, 1 - column, 1), self.recv_d.at[0, level])
        self.arrived(self.block(1 - row, level, 1 - column, 0), self.recv_d.at[1, level])
        self.own_copy().wait()
        self.start_z(level, True)
        self.start_z(level, False)

    def hop(self, hop):
        def act(z, up):
            self.arrived(self.plane(z), self.recv_z.at[z])
            self.start_z(z, up)

        self.each_at(hop, act)

    def finish(self):
        pass

    def close(self):
        level = neighbours()[1]
        self.close_z()
        for copy in self.copies_xy(level) + self.copies_diagonal(level):
            copy.wait_send()


def gather_sems(pieces):
    dma = pltpu.SemaphoreType.DMA
    shapes = [(2, 4), (4,), (4,), (4,), (4,), (4,), (2, 4), (2, 4), ()]
    return [dma((pieces,) + shape) for shape in shapes]


AT_BEGIN, AT_GAINS, AT_PAIRS, AT_QUERIES, AT_HEADS, AT_KEYS, AT_ALL, AT_SORT = 0, 1, 2, 3, 4, 5, 6, 7
AT_RETURN, AT_MIXED, AT_OUT, AT_NORM, AT_GROUP, AT_TILE, AT_FEED = 8, 9, 10, 11, 12, 16, 24
PUMPS = {
    AT_BEGIN: (1, 10, 4, 2, 3, 5, 7, 6, 11, 12, 13, 14),
    AT_GAINS: (20,),
    AT_GROUP + 2: (15, 17),
    AT_GROUP + 3: (16, 70),
    AT_QUERIES: (21, 30),
    AT_GROUP + 0: (50,),
    AT_GROUP + 1: (22,),
    AT_HEADS: (74, 40, 31, 60, 23),
    AT_KEYS: (34, 75),
    AT_ALL: (32, 24, 35, 44),
    AT_TILE + 0: (41, 25),
    AT_TILE + 2: (33, 26, 61, 42, 71),
    AT_TILE + 3: (27, 51),
    AT_RETURN: (36, 37, 43, 52, 45, 55, 72, 47, 54, 46),
    AT_MIXED: (64,),
    AT_OUT: (53,),
    AT_NORM: (56, 62),
    AT_FEED + 1: (63, 57),
    AT_FEED + 3: (65, 66, 67),
    AT_FEED + 5: (73,),
}


def forward_kernel(
    tokens,
    positions,
    freqs,
    gain_one,
    gain_two,
    w_query,
    w_key,
    w_value,
    w_out_t,
    w_gate,
    w_up,
    w_down_t,
    cotangent,
    near,
    far,
    normed_out,
    q_out,
    k_out,
    v_out,
    mixed_t_out,
    lse_out,
    mixed_low_out,
    middle_out,
    second_out,
    right_out,
    gains_out,
    tables_out,
    left_out,
    order,
    ids_flat,
    ids_in,
    near_own,
    far_own,
    unit,
    normed,
    tables,
    weight,
    gain_message,
    gain_all,
    gain_columns,
    gain_rows,
    left_t,
    q_heads,
    kv_heads,
    q_slots,
    kv_slots,
    q_t,
    keys,
    v_t,
    mixed_t,
    lse,
    mixed,
    mixed_slots,
    mixed_heads,
    mixed_low,
    out_weight,
    part,
    part_other,
    second,
    cot,
    right,
    feed_weight,
    grad_hiddens,
    ids_all,
    ids,
    load_own,
    send_ids,
    recv_ids,
    load_ids,
    send_gain,
    recv_gain,
    load_w,
    load_out,
    load_feed,
    load_cot,
    save_right,
    saves,
    send_q,
    recv_q,
    send_kv,
    recv_kv,
    send_x,
    recv_x,
    send_m,
    recv_m,
    send_p,
    recv_p,
    *sems,
):
    row, spot, core = place()
    low, full = jnp.bfloat16, jnp.float32
    rows, width = tokens.shape
    share = near_own.shape[0]
    length = 8 * rows
    runs, tiles = length // RUN, length // TILE
    per_device = rows // RUN
    halves = TILE // RUN
    quarter = 4 * share
    sibling = (row, spot, 1 - core)
    out_width = w_out_t.shape[1]
    qkv_width = 16 * HEAD

    near_loads, far_loads, start = [], [], 0
    for ref in (w_query, w_key, w_value, w_out_t):
        target = near_own.at[:, pl.ds(start, ref.shape[1])]
        near_loads.append(pltpu.make_async_copy(ref, target, load_own.at[len(near_loads)]))
        start += ref.shape[1]
    for index, ref in enumerate((w_gate, w_up, w_down_t)):
        for piece in range(4):
            source = ref.at[:, pl.ds(piece * FEED, FEED)]
            target = far_own.at[:, pl.ds((3 * piece + index) * FEED, FEED)]
            far_loads.append(
                pltpu.make_async_copy(source, target, load_own.at[4 + 4 * index + piece])
            )
    for copy in near_loads + far_loads:
        copy.start()
    load_cotangent = pltpu.make_async_copy(cotangent, cot, load_cot)
    load_cotangent.start()
    half = qkv_width // 2
    pairs = Gather(near_own, near, half, half, 0, sems)
    first = Gather(near_own, near, 0, half, 1, sems)
    outer = Gather(near_own, near, qkv_width, out_width, 2, sems)
    feeds = [Gather(far_own, far, 3 * FEED * p, 3 * FEED, 3 + p, sems) for p in range(3)]
    feeds.append(Gather(far_own, far, 9 * FEED, FEED, 6, sems))
    plane = PlaneGather(far_own, far, 10 * FEED, 2 * FEED, 7, sems)
    gathers = [pairs, first, outer] + feeds + [plane]

    def pump(place):
        for what in PUMPS.get(place, ()):
            gather, act = gathers[what // 10], what % 10
            if act == 0:
                gather.open()
            elif act < 4:
                gather.hop(act)
            elif gather is plane and act == 5:
                gather.spread()
            else:
                gather.diagonal(act - 4)

    gain_message[...] = jnp.zeros_like(gain_message)
    gain_message[0:1, :share] = gain_one[...].astype(full)
    gain_message[1:2, :share] = gain_two[...].astype(full)
    for copy in near_loads:
        copy.wait()
    greet(group_others())
    pairs.open()
    for gather in (pairs, first, outer):
        gather.place_own()

    gain_copies, gain_from = exchange_messages(
        lambda shard: gain_message, gain_all, send_gain, recv_gain
    )
    for copy in gain_copies:
        copy.start()
    gain_all[own_shard()] = gain_message[...]

    lane = lax.broadcasted_iota(jnp.int32, (8, WIDE), 1)
    ids_in[...] = jnp.zeros_like(lane)
    for run in range(per_device):
        start_at = positions[0:1, run * RUN : run * RUN + 1]
        ids_in[...] = jnp.where(lane == run, lax.div(start_at, RUN), ids_in[...])
    for shift in range(1, 8):
        remote(
            ids_in,
            ids_all.at[spot],
            send_ids.at[shift],
            recv_ids.at[shift],
            (row, lax.rem(spot + shift, 8), core),
        ).start()
    ids_all[spot] = ids_in[...]

    for copy in far_loads:
        copy.wait()
    for gather in feeds + [plane]:
        gather.place_own()
    chunk = rows // 8

    def unit_block(index, carry):
        cut = tile_at(index, chunk)
        values = tokens[cut].astype(full)
        inverse = lax.rsqrt(jnp.mean(values * values, axis=-1, keepdims=True) + epsilon)
        unit[cut] = values * inverse
        return carry

    lax.fori_loop(0, 8, unit_block, 0)
    angles = freqs[...] * positions[...].astype(full)
    tables[0] = jnp.cos(angles)
    tables[1] = jnp.sin(angles)

    pump(AT_BEGIN)
    for shift in range(1, 8):
        remote(
            ids_in,
            ids_all.at[lax.rem(spot + 8 - shift, 8)],
            send_ids.at[shift],
            recv_ids.at[shift],
            (row, lax.rem(spot + shift, 8), core),
        ).wait_recv()
    pltpu.make_async_copy(ids_all, ids, load_ids).start()
    pairs.finish()

    width = near.shape[3] * 16

    def load_group(group):
        lanes = pl.ds(group * 4 * HEAD, 4 * HEAD)
        return pltpu.make_async_copy(
            near.at[:, :, :, :, lanes], weight.at[group % 2], load_w.at[group % 2]
        )

    load_out_weight = pltpu.make_async_copy(
        near.at[:, :, :, :, pl.ds(qkv_width, out_width)], out_weight, load_out
    )
    load_group(2).start()
    load_group(3).start()
    for wait in gain_from:
        wait()
    for shard in range(16):
        gain_columns[shard * share : (shard + 1) * share] = gain_all[shard].T[:share]
    gain_rows[...] = gain_columns[...].T
    normed[...] = (unit[...] * gain_rows[0:1]).astype(low)
    pump(AT_GAINS)

    def project(group):
        load_group(group).wait()
        proj = dot_f32(normed[...], weight[group % 2].reshape(width, 4 * HEAD)).T
        for head in range(4):
            front = proj[head * HEAD : head * HEAD + HALF]
            back = proj[head * HEAD + HALF : (head + 1) * HEAD]
            if group < 3:
                front, back = (
                    front * tables[0] - back * tables[1],
                    back * tables[0] + front * tables[1],
                )
            for start, value in ((0, front.astype(low)), (HALF, back.astype(low))):
                for run in range(per_device):
                    piece = value[:, run * RUN : (run + 1) * RUN]
                    if group < 2:
                        q_heads[4 * group + head, run, start : start + HALF] = piece
                    else:
                        kv_heads[head, group - 2, run, start : start + HALF] = piece
        pump(AT_GROUP + group)

    project(2)
    project(3)

    outgoing = []
    for step in range(4):
        slot = lax.rem(spot + step, 4)
        chip = 4 * core + slot
        for other in range(2):
            is_self = jnp.logical_and(chip == spot, core == other)
            device = (row, chip, other)
            kv_parts = (
                kv_heads.at[slot, :, other],
                kv_slots.at[spot, :, other],
                send_kv.at[step, other],
                recv_kv.at[spot],
                device,
            )
            q_parts = (
                q_heads.at[2 * slot + other],
                q_slots.at[spot],
                send_q.at[step, other],
                recv_q.at[spot],
                device,
            )
            outgoing.append((kv_parts, is_self))
            outgoing.append((q_parts, is_self))
    for parts, is_self in outgoing[0::2]:
        move(*parts, is_self)
    pump(AT_PAIRS)
    first.finish()
    load_group(0).start()
    load_group(1).start()
    pump(AT_QUERIES)
    project(0)
    project(1)
    for parts, is_self in outgoing[1::2]:
        move(*parts, is_self)
    pump(AT_HEADS)

    def hand_on(source):
        block = kv_slots.at[source, :, core]
        return remote(block, block, send_x.at[source], recv_x.at[source], sibling)

    for step in range(8):
        source = lax.rem(spot + step, 8)
        block = kv_slots.at[source, :, core]
        remote(block, block, send_x.at[source], recv_kv.at[source], sibling).wait_recv()
        hand_on(source).start()
    pump(AT_KEYS)
    for step in range(8):
        remote(
            q_slots.at[step], q_slots.at[step], send_x.at[step], recv_q.at[step], sibling
        ).wait_recv()
        hand_on(step).wait()
    pump(AT_ALL)

    pltpu.make_async_copy(ids_all, ids, load_ids).wait()

    def find_run(index, carry):
        device, piece = 0, 0
        for run in range(runs):
            here = ids[run // per_device, 0, run % per_device] == index
            device = jnp.where(here, run // per_device, device)
            piece = jnp.where(here, run % per_device, piece)
        order[index, 0] = device
        order[index, 1] = piece
        found = ids[index // per_device, 0, index % per_device]
        order[runs + index, 0] = lax.div(found, per_device)
        order[runs + index, 1] = lax.rem(found, per_device)
        ids_flat[index] = found
        return carry

    lax.fori_loop(0, runs, find_run, 0)

    def sort_run(index, carry):
        device, piece = order[index, 0], order[index, 1]
        cols = tile_at(index, RUN)
        q_t[:, cols] = q_slots[device, piece]
        keys[index] = kv_slots[device, 0, piece].T
        v_t[:, cols] = kv_slots[device, 1, piece]
        return carry

    lax.fori_loop(0, runs, sort_run, 0)
    pump(AT_SORT)
    scale = HEAD ** (-0.5) * LOG2_E

    def query_pair(pair, carry):
        def step(half, scores, block, peak, total, mix):
            high = jnp.maximum(peak, jnp.max(scores, axis=0, keepdims=True))
            decay = jnp.exp2(peak - high)
            weights = jnp.exp2(scores - high)
            total = total * decay + jnp.sum(weights, axis=0, keepdims=True)
            mix = mix * decay + dot_f32(v_t[:, tile_at(block, TILE)], weights.astype(low))
            return high, total, mix

        def scores_of(half, block):
            held = keys[pl.ds(block * halves, halves)].reshape(TILE, HEAD)
            return dot_f32(held, q_t[:, tile_at(2 * pair + half, TILE)]) * scale

        def full_block(block, states):
            scores = [scores_of(half, block) for half in range(2)]
            return tuple(step(half, scores[half], block, *states[half]) for half in range(2))

        state = (
            jnp.full((1, TILE), masked_value, full),
            jnp.zeros((1, TILE), full),
            jnp.zeros((HEAD, TILE), full),
        )
        start = 2 * pair
        scores = causal(scores_of(0, start)), scores_of(1, start)
        states = tuple(step(half, scores[half], start, *state) for half in range(2))
        last = step(1, causal(scores_of(1, start + 1)), start + 1, *states[1])
        states = lax.fori_loop(0, start, full_block, (states[0], last))
        for half in range(2):
            peak, total, mix = states[half]
            index = 2 * pair + half
            cols = tile_at(index, TILE)
            mix = mix / total
            mixed_t[:, cols] = mix
            lse[:, cols] = peak + jnp.log2(total)
            for run in range(halves):
                cut = mix[:, run * RUN : (run + 1) * RUN]
                mixed[index * halves + run] = cut.astype(low)
        for place in range(tiles // 2):

            @pl.when(pair == place)
            def _():
                pump(AT_TILE + place)

        return carry

    lax.fori_loop(0, tiles // 2, query_pair, 0)

    def load_feed_weight(index, kind):
        piece, half = index // 2, lax.rem(index, 2)
        start = (3 * piece + kind) * FEED + half * PIECE
        lanes = pl.ds(pl.multiple_of(start, PIECE), PIECE)
        return pltpu.make_async_copy(
            far.at[:, :, :, :, lanes], feed_weight.at[half, kind], load_feed.at[half, kind]
        )

    def unsort_run(run, carry):
        index = ids[run // per_device, 0, run % per_device]
        mixed_slots[run // per_device, run % per_device] = mixed[index]
        return carry

    lax.fori_loop(0, runs, unsort_run, 0)
    copies = return_copies(mixed_slots, mixed_heads, send_m, recv_m)
    start_return(copies)
    early_saves = [
        pltpu.make_async_copy(source, target, saves.at[index])
        for index, (source, target) in enumerate(
            [
                (normed, normed_out),
                (q_t, q_out),
                (keys, k_out),
                (v_t, v_out),
                (mixed_t, mixed_t_out),
                (lse, lse_out),
                (gain_rows, gains_out),
                (tables, tables_out),
            ]
        )
    ]
    for copy in early_saves:
        copy.start()
    pump(AT_RETURN)
    outer.finish()
    load_out_weight.start()
    load_cotangent.wait()
    for piece in range(2):
        feeds[piece].finish()
    early = [load_feed_weight(index, 2) for index in range(4)]
    for index in range(2):
        early[index].start()
    for index in range(4):
        early[index].wait()
        held = feed_weight[index % 2, 2].reshape(width, PIECE)
        grad_hiddens[index] = dot_f32(cot[...], held)
        if index < 2:
            early[index + 2].start()
    finish_return(copies, mixed_heads, send_m, recv_m)
    pump(AT_MIXED)

    load_out_weight.wait()
    for run in range(per_device):
        side = mixed_heads[:, run].reshape(8 * HEAD, RUN)
        mixed_low[run * RUN : (run + 1) * RUN] = side.T

    def pair_copy(index):
        cut = pl.ds(index * quarter, quarter)
        return remote(
            part.at[:, cut], part_other.at[:, cut], send_p.at[index], recv_p.at[index], sibling
        )

    for index in range(4):
        block = out_weight[index // 2, 2 * (index % 2) : 2 * (index % 2) + 2]
        term = contract_cols(mixed_low[...], block.reshape(quarter, out_width))
        part[:, index * quarter : (index + 1) * quarter] = term.astype(low)
        pair_copy(index).start()
    pump(AT_OUT)
    for index in range(4):
        pair_copy(index).wait()
    chunk = rows // 8

    def norm_block(index, carry):
        cut = tile_at(index, chunk)
        sums = part[cut].astype(full) + part_other[cut].astype(full)
        values = tokens[cut].astype(full) + sums
        unit[cut] = values
        inverse = lax.rsqrt(jnp.mean(values * values, axis=-1, keepdims=True) + epsilon)
        second[cut] = (values * inverse * gain_rows[1:2]).astype(low)
        return carry

    lax.fori_loop(0, 8, norm_block, 0)
    late_saves = [
        pltpu.make_async_copy(source, target, saves.at[8 + index])
        for index, (source, target) in enumerate(
            [(mixed_low, mixed_low_out), (unit, middle_out), (second, second_out)]
        )
    ]
    for copy in late_saves:
        copy.start()
    pump(AT_NORM)

    def load_half(index):
        for kind in range(2):
            load_feed_weight(index, kind).start()

        @pl.when(index >= 4)
        def _():
            load_feed_weight(index, 2).start()

    def save_piece(piece):
        lanes = pl.ds(piece * 3 * FEED, 3 * FEED)
        return pltpu.make_async_copy(
            right.at[:, lanes], right_out.at[:, lanes], save_right.at[piece]
        )

    def feed_block(index, carry):
        piece, half = index // 2, lax.rem(index, 2)
        for when, which in ((3, 2), (6, 3)):

            @pl.when(index == when)
            def _():
                feeds[which].finish()

        @pl.when(index == 0)
        def _():
            load_half(0)

        @pl.when(index == 6)
        def _():
            load_half(6)

        @pl.when(jnp.logical_and(index != 5, index != 7))
        def _():
            load_half(index + 1)

        @pl.when(index >= 4)
        def _():
            load_feed_weight(index, 2).wait()
            held = feed_weight[half, 2].reshape(width, PIECE)
            grad_hiddens[index - 4] = dot_f32(cot[...], held)

        values = []
        for kind in range(2):
            load_feed_weight(index, kind).wait()
            values.append(dot_f32(second[...], feed_weight[half, kind].reshape(width, PIECE)))
        gate, up = values
        grad_hidden = grad_hiddens[lax.rem(index, 4)]
        sigmoid = jax.nn.sigmoid(gate)
        silu = gate * sigmoid
        grad_gate = grad_hidden * up * sigmoid * (1.0 + gate * (1.0 - sigmoid))
        for when, source in ((1, second), (3, cot)):

            @pl.when(index == when)
            def _():
                turn_left(left_t, when % 3, source)

        for kind, value in enumerate((grad_gate, grad_hidden * silu, silu * up)):
            start = (3 * piece + kind) * FEED + half * PIECE
            right[:, pl.ds(pl.multiple_of(start, PIECE), PIECE)] = value.astype(low)

        for when in range(8):

            @pl.when(index == when)
            def _():
                pump(AT_FEED + when)

        for when in range(4):

            @pl.when(index == 2 * when + 1)
            def _():
                save_piece(when).start()

        return carry

    lax.fori_loop(0, 8, feed_block, 0)
    save_left = pltpu.make_async_copy(left_t, left_out, saves.at[11])
    save_left.start()
    for gather in gathers:
        gather.close()
    for parts, is_self in outgoing:

        @pl.when(jnp.logical_not(is_self))
        def _():
            remote(*parts).wait_send()

    for shift in range(1, 8):
        remote(
            ids_in,
            ids_all.at[spot],
            send_ids.at[shift],
            recv_ids.at[shift],
            (row, lax.rem(spot + shift, 8), core),
        ).wait_send()
    for copy in gain_copies:
        copy.wait_send()
    for copy in early_saves + late_saves + [save_left] + [save_piece(piece) for piece in range(4)]:
        copy.wait()


def forward(
    tokens,
    positions,
    gain_one,
    gain_two,
    w_query,
    w_key,
    w_value,
    w_out_t,
    w_gate,
    w_up,
    w_down_t,
    cotangent,
):
    dma = pltpu.SemaphoreType.DMA
    vmem = pltpu.VMEM
    low, full = jnp.bfloat16, jnp.float32
    rows, width = tokens.shape
    share, hidden_width = w_gate.shape
    out_width = w_out_t.shape[1]
    near_width = 16 * HEAD + out_width
    length = 8 * rows
    per_device = rows // RUN
    heads = (8, per_device, HEAD, RUN)
    both = (2, per_device, HEAD, RUN)
    by_run = (length // RUN, RUN, HEAD)
    flat = (HEAD, length)
    smem_spec = pl.BlockSpec(memory_space=pltpu.SMEM)
    shape = jax.ShapeDtypeStruct
    return pl.pallas_call(
        forward_kernel,
        in_specs=[vmem_spec()] * 5 + [any_spec()] * 8,
        out_specs=[any_spec()] * 15 + [smem_spec] * 2,
        out_shape=[
            shape((2, 4, 2, share, near_width), low),
            shape((2, 4, 2, share, 3 * hidden_width), low),
            shape((rows, width), low),
            shape(flat, low),
            shape(by_run, low),
            shape(flat, low),
            shape(flat, full),
            shape((1, length), full),
            shape((rows, out_width), low),
            shape((rows, width), full),
            shape((rows, width), low),
            shape((rows, 3 * hidden_width), low),
            shape((8, width), full),
            shape((2, HALF, rows), full),
            shape((2, 2, 2, 4 * share, rows), low),
            shape((2 * length // RUN, 2), jnp.int32),
            shape((length // RUN,), jnp.int32),
        ],
        scratch_shapes=[
            vmem((8, WIDE), jnp.int32),
            vmem((share, near_width), low),
            vmem((share, 3 * hidden_width), low),
            vmem((rows, width), full),
            vmem((rows, width), low),
            vmem((2, HALF, rows), full),
            vmem((2, 2, 4, 2, share, 4 * HEAD), low),
            vmem((8, WIDE), full),
            vmem((16, 8, WIDE), full),
            vmem((width, 8), full),
            vmem((8, width), full),
            vmem((2, 2, 2, 4 * share, rows), low),
            vmem(heads, low),
            vmem((4,) + both, low),
            vmem(heads, low),
            vmem((8,) + both, low),
            vmem(flat, low),
            vmem(by_run, low),
            vmem(flat, low),
            vmem(flat, full),
            vmem((1, length), full),
            vmem((length // RUN, HEAD, RUN), low),
            vmem(heads, low),
            vmem(heads, low),
            vmem((rows, out_width), low),
            vmem((2, 4, 2, share, out_width), low),
            vmem((rows, width), low),
            vmem((rows, width), low),
            vmem((rows, width), low),
            vmem((rows, width), low),
            vmem((rows, 3 * hidden_width), low),
            vmem((2, 3, 2, 4, 2, share, PIECE), low),
            vmem((4, rows, PIECE), full),
            vmem((8, 8, WIDE), jnp.int32),
            pltpu.SMEM((8, 8, WIDE), jnp.int32),
            dma((16,)),
            dma((8,)),
            dma((8,)),
            dma(()),
            dma((16,)),
            dma((16,)),
            dma((2,)),
            dma(()),
            dma((2, 3)),
            dma(()),
            dma((4,)),
            dma((12,)),
            dma((4, 2)),
            dma((8,)),
            dma((4, 2)),
            dma((8,)),
            dma((8,)),
            dma((8,)),
            dma((8,)),
            dma((8,)),
            dma((4,)),
            dma((4,)),
        ]
        + gather_sems(8),
        compiler_params=pltpu.CompilerParams(
            collective_id=1, has_side_effects=True, vmem_limit_bytes=VMEM_LIMIT
        ),
        name="forward",
    )(
        tokens,
        positions,
        lane_freqs(),
        gain_one,
        gain_two,
        w_query,
        w_key,
        w_value,
        w_out_t,
        w_gate,
        w_up,
        w_down_t,
        cotangent,
    )


SECOND, THIRD, LAST = 2, 4, 5


class Reduce:
    def __init__(self, n, changes, refs):
        (
            self.left_t,
            self.right,
            self.own,
            self.out,
            self.save,
            self.send_one,
            self.recv_one,
            self.send_two,
            self.recv_two,
            self.kept,
            self.recv_three,
            self.ss_one,
            self.rs_one,
            self.ss_two,
            self.rs_two,
            self.ss_three,
            self.rs_three,
        ) = refs
        self.n, self.changes = n, changes
        self.share = self.own.shape[1]

    def columns(self, step, kind):
        held = self.right.shape[1] // (2 * PIECE)
        start = lax.rem(step, held) * 2 * PIECE + kind * PIECE
        return pl.ds(pl.multiple_of(start, PIECE), PIECE)

    def each_save(self, step, act):
        slot = lax.rem(step, 2)
        near_at = self.changes[0]

        def copies(cuts):
            for index, (ref, start, lanes) in enumerate(cuts):
                source = self.own.at[slot, :, lanes]
                target = ref.at[:, pl.ds(start, lanes.size)]
                act(pltpu.make_async_copy(source, target, self.save.at[slot, index]))

        for kind in range(3):

            @pl.when(jnp.logical_and(step < near_at, lax.rem(step, 3) == kind))
            def _():
                start = pl.multiple_of(step // 3 * 2 * PIECE, 2 * PIECE)
                copies([(self.out[kind], start, pl.ds(0, 2 * PIECE))])

        for index in range(self.n - near_at):
            first, past = index * 2 * PIECE, (index + 1) * 2 * PIECE
            cuts, at = [], 0
            for ref in self.out[3:]:
                low, high = max(first, at), min(past, at + ref.shape[1])
                if low < high:
                    cuts.append((ref, low - at, pl.ds(low - first, high - low)))
                at += ref.shape[1]

            @pl.when(step == near_at + index)
            def _():
                copies(cuts)

    def product(self, step, kind, x, y):
        left = jnp.where(lax.rem(step, 3) == 2, 0, 1)
        left = jnp.where(step >= self.changes[0], 2, left)
        left = jnp.where(step >= self.changes[1], 0, left)
        term = jnp.dot(
            self.left_t[left, x, y],
            self.right[:, self.columns(step, kind)],
            preferred_element_type=jnp.float32,
        )
        return term

    def x_first(self, step, kind):
        return 1 if kind == 0 else jnp.where(lax.rem(step, 5) == 4, 1, 0)

    def beside(self, by_x):
        row, level, column = neighbours()[:3]
        core = place()[2]
        other_row = by_x * (1 - row) + (1 - by_x) * row
        other_column = by_x * column + (1 - by_x) * (1 - column)
        return (other_row, 2 * level + other_column, core)

    def first_copy(self, step, kind):
        out, into = lax.rem(step, 3), lax.rem(step, 6)
        return remote(
            self.send_one.at[out, kind],
            self.recv_one.at[into, kind],
            self.ss_one.at[out, kind],
            self.rs_one.at[into, kind],
            self.beside(self.x_first(step, kind)),
        )

    def second_copy(self, step, kind):
        out, into = lax.rem(step, 3), lax.rem(step, 6)
        return remote(
            self.send_two.at[out, kind],
            self.recv_two.at[into, kind],
            self.ss_two.at[out, kind],
            self.rs_two.at[into, kind],
            self.beside(1 - self.x_first(step, kind)),
        )

    def third_copy(self, step, kind, k):
        row, level, column, beside_x, beside_y, along_z = neighbours()
        target = lax.rem(level + k + 1, 4)
        out, into = lax.rem(step, 4), lax.rem(step, 4)
        return remote(
            self.kept.at[out, kind, pl.ds(pl.multiple_of(target * self.share, 16), self.share)],
            self.recv_three.at[into, kind, k],
            self.ss_three.at[out, kind, k],
            self.rs_three.at[into, kind, k],
            along_z[k],
        )

    def pieces(self, step, act):
        act(0)

        @pl.when(step < self.n - 1)
        def _():
            act(1)

    def first(self, step):
        row, level, column = neighbours()[:3]
        slot = lax.rem(step, 3)

        def act(kind):
            by_x = self.x_first(step, kind)
            for half in range(2):
                x = by_x * (1 - row) + (1 - by_x) * half
                y = by_x * half + (1 - by_x) * (1 - column)
                self.send_one[slot, kind, half] = self.product(step, kind, x, y).astype(
                    jnp.bfloat16
                )
            self.first_copy(step, kind).start()

        self.pieces(step, act)

    def second(self, step):
        row, level, column = neighbours()[:3]
        slot, came, keep = lax.rem(step, 3), lax.rem(step, 6), lax.rem(step, 4)
        self.pieces(step, lambda kind: self.first_copy(step, kind).wait())

        def act(kind):
            by_x = self.x_first(step, kind)
            x = by_x * row + (1 - by_x) * (1 - row)
            y = by_x * (1 - column) + (1 - by_x) * column
            arrived = self.recv_one.at[came, kind]
            mine = by_x * column + (1 - by_x) * row
            away = self.product(step, kind, x, y) + arrived[1 - mine].astype(jnp.float32)
            self.send_two[slot, kind] = away.astype(jnp.bfloat16)
            here = self.product(step, kind, row, column) + arrived[mine].astype(jnp.float32)
            self.kept[keep, kind] = here.astype(jnp.bfloat16)

        self.pieces(step, act)
        self.pieces(step, lambda kind: self.second_copy(step, kind).start())

    def third(self, step):
        came, keep = lax.rem(step, 6), lax.rem(step, 4)

        def act(kind):
            self.second_copy(step, kind).wait()
            here = self.kept[keep, kind].astype(jnp.float32) + self.recv_two[came, kind].astype(
                jnp.float32
            )
            self.kept[keep, kind] = here.astype(jnp.bfloat16)
            for k in range(3):
                self.third_copy(step, kind, k).start()

        self.pieces(step, act)

    def last(self, step):
        level = neighbours()[1]
        came, keep = lax.rem(step, 4), lax.rem(step, 4)
        mine = pl.ds(pl.multiple_of(level * self.share, 16), self.share)

        @pl.when(step >= 2)
        def _():
            self.each_save(step - 2, lambda copy: copy.wait())

        def act(kind):
            total = self.kept[keep, kind, mine].astype(jnp.float32)
            for k in range(3):
                self.third_copy(step, kind, k).wait()
                total = total + self.recv_three[came, kind, k].astype(jnp.float32)
            self.own[lax.rem(step, 2), :, kind * PIECE : (kind + 1) * PIECE] = total

        self.pieces(step, act)
        self.each_save(step, lambda copy: copy.start())

    def turn(self, step):
        for stage, lag in (
            (self.first, 0),
            (self.second, SECOND),
            (self.third, THIRD),
            (self.last, LAST),
        ):

            @pl.when(jnp.logical_and(step >= lag, step < self.n + lag))
            def _():
                stage(step - lag)


def backward_kernel(
    order,
    ids,
    q_in,
    k_in,
    v_in,
    mixed_t_in,
    lse_in,
    cotangent,
    left_in,
    normed_in,
    right_in,
    mixed_low,
    middle,
    near,
    far,
    tokens,
    gains_in,
    tables,
    input_grad,
    layer_out,
    gate_grad,
    up_grad,
    down_grad,
    query_grad,
    key_grad,
    value_grad,
    out_grad,
    gain_out,
    q,
    q_t,
    k,
    k_t,
    v,
    d_own,
    d_slots,
    d,
    d_t,
    dq_t,
    lse,
    delta,
    dk,
    dv,
    dq_slots,
    dkv_sorted,
    dkv_slots,
    dkv_other,
    dq_own,
    dkv_own,
    weight,
    middle_ring,
    input_ring,
    part,
    part_other,
    total,
    staged,
    grad_mid,
    gain_two_grad,
    left_t,
    right,
    gain_columns,
    gain_messages,
    gain_all,
    own,
    send_one,
    recv_one,
    send_two,
    recv_two,
    kept,
    recv_three,
    loads,
    load_first,
    send_gain,
    recv_gain,
    load_left_sem,
    load_w,
    load_ring,
    save_rows,
    save_sem,
    send_d,
    recv_d,
    send_q,
    recv_q,
    send_x,
    recv_x,
    send_k,
    recv_k,
    send_p,
    recv_p,
    save,
    *sems,
):
    row, spot, core = place()
    low, full = jnp.bfloat16, jnp.float32
    rows, width = staged.shape
    length = 8 * rows
    runs, tiles = length // RUN, length // TILE
    per_device = rows // RUN
    halves = TILE // RUN
    share = width // 16
    quarter = 4 * share
    sibling = (row, spot, 1 - core)
    qkv_width = 16 * HEAD
    out_width = mixed_low.shape[1]
    near_at = right_in.shape[1] // (2 * PIECE)
    n = near_at + (qkv_width + out_width + PIECE) // (2 * PIECE)
    grads = (gate_grad, up_grad, down_grad, query_grad, key_grad, value_grad, out_grad)
    changes = (near_at, near_at + qkv_width // (2 * PIECE))
    sums = Reduce(
        n,
        changes,
        (left_t, right, own, grads, save)
        + (send_one, recv_one, send_two, recv_two, kept, recv_three)
        + sems,
    )

    def stage(source):
        return pltpu.make_async_copy(source, staged, load_left_sem)

    early_loads = [
        pltpu.make_async_copy(source, target, loads.at[index])
        for index, (source, target) in enumerate(
            [
                (q_in, q_t),
                (k_in, k),
                (v_in, d_t),
                (mixed_t_in, dq_t),
                (lse_in, lse),
                (middle, total),
            ]
        )
    ]

    first_loads = [
        pltpu.make_async_copy(left_in, left_t.at[pl.ds(0, 2)], load_first.at[4])
    ] + [
        pltpu.make_async_copy(
            right_in.at[:, pl.ds(3 * FEED * piece, 3 * FEED)],
            right.at[:, pl.ds(3 * FEED * piece, 3 * FEED)],
            load_first.at[piece],
        )
        for piece in range(4)
    ]


    def load_block(index, piece, part_of, start):
        lanes = pl.ds(3 * FEED * piece + start + part_of * PIECE, PIECE)
        levels = pl.ds(2 * lax.rem(index, 2), 2)
        return pltpu.make_async_copy(
            far.at[index // 2, levels, :, :, lanes], held_block(piece, part_of), load_w.at[piece]
        )

    def held_block(piece, part_of):
        levels = pl.ds(2 * (part_of % 2), 2)
        return weight.at[piece, part_of // 2, levels, :, :, pl.ds(0, PIECE)]

    def load_blocks(index, piece, start, parts):
        for part_of in range(parts):
            load_block(index, piece, part_of, start).start()

    def row_products(start, parts, landing):
        def block(index, carry):
            term = jnp.zeros((rows, quarter), full)
            for piece in range(4):
                for part_of in range(parts):
                    load_block(index, piece, part_of, start).wait()
                for part_of in range(parts):
                    at = 3 * FEED * piece + start + part_of * PIECE
                    term = term + contract_cols(
                        right[:, at : at + PIECE],
                        held_block(piece, part_of)[...].reshape(quarter, PIECE),
                    )

                @pl.when(index + 1 < 4)
                def _():
                    load_blocks(index + 1, piece, start, parts)

            part[:, tile_at(index, quarter)] = term.astype(low)
            pair_copy(index, landing).start()
            return carry

        lax.fori_loop(0, 4, block, 0)

    def pair_copy(index, landing):
        cut = pl.ds(pl.multiple_of(index * quarter, quarter), quarter)
        return remote(
            part.at[:, cut],
            part_other.at[landing, :, cut],
            send_p.at[index],
            recv_p.at[landing, index],
            sibling,
        )

    def second_back():
        row_products(0, 4, 0)
        for index in range(2):
            load_out_weight(index).start()

    def load_out_weight(index):
        lanes = pl.ds(qkv_width + index * 4 * HEAD, 4 * HEAD)
        return pltpu.make_async_copy(
            near.at[:, :, :, :, lanes], weight.at[index], load_w.at[index]
        )

    d_copies = []
    for step in range(4):
        slot = lax.rem(spot + step, 4)
        chip = 4 * core + slot
        for other in range(2):
            parts = (
                d_own.at[2 * slot + other],
                d_slots.at[spot],
                send_d.at[step, other],
                recv_d.at[spot],
                (row, chip, other),
            )
            d_copies.append((parts, jnp.logical_and(chip == spot, core == other)))

    def middle_back():
        for index in range(4):
            pair_copy(index, 0).wait()
        early_loads[5].wait()
        stage(cotangent).wait()
        chunk = rows // 8

        def block(index, gain_grad):
            cut = tile_at(index, chunk)
            grad = part[cut].astype(full) + part_other[0, cut].astype(full)
            values = total[cut]
            inverse = lax.rsqrt(jnp.mean(values * values, axis=-1, keepdims=True) + epsilon)
            unit = values * inverse
            scaled = grad * gains_in[1:2]
            mean = jnp.mean(scaled * unit, axis=-1, keepdims=True)
            result = staged[cut].astype(full) + inverse * (scaled - unit * mean)
            total[cut] = result
            grad_mid[cut] = result.astype(low)
            return gain_grad + jnp.sum(grad * unit, axis=0, keepdims=True)

        gain_two_grad[...] = lax.fori_loop(0, 8, block, jnp.zeros((1, width), full))
        for index in range(2):
            load_out_weight(index).wait()
            grad = dot_f32(grad_mid[...], weight[index].reshape(width, 4 * HEAD)).T.astype(low)
            for head in range(4):
                for run in range(per_device):
                    d_own[4 * index + head, run] = grad[
                        head * HEAD : (head + 1) * HEAD, run * RUN : (run + 1) * RUN
                    ]
        for parts, is_self in d_copies:
            move(*parts, is_self)


    def prepare():
        for copy in early_loads[:5]:
            copy.wait()
        for index in range(tiles):
            cut = pl.ds(index * TILE, TILE)
            q[cut] = q_t[:, cut].T
            k_t[:, cut] = k[halves * index : halves * (index + 1)].reshape(TILE, HEAD).T
            v[cut] = d_t[:, cut].T

    def take_cotangents():
        for index in range(8):
            remote(
                d_slots.at[index], d_slots.at[index], send_d.at[0, 0], recv_d.at[index], sibling
            ).wait_recv()

        def sort_run(index, carry):
            cols = tile_at(index, RUN)
            run = d_slots[order[index, 0], order[index, 1]]
            d_t[:, cols] = run
            d[cols] = run.T
            delta[:, cols] = jnp.sum(run.astype(full) * dq_t[:, cols], axis=0, keepdims=True)
            return carry

        lax.fori_loop(0, runs, sort_run, 0)
        dq_t[...] = jnp.zeros_like(dq_t)

    scale = HEAD ** (-0.5)

    def key_tile(block):
        cut = tile_at(block, TILE)
        both = pl.ds(block * halves, halves)
        keys, values = k[both].reshape(TILE, HEAD), v[cut]
        keys_t = k_t[:, cut]
        dk[...] = jnp.zeros_like(dk)
        dv[...] = jnp.zeros_like(dv)

        def query_tile(index, diagonal):
            cols = tile_at(index, TILE)
            scores = dot_f32(keys, q_t[:, cols]) * (scale * LOG2_E)
            if diagonal:
                scores = causal(scores)
            probs = jnp.exp2(scores - lse[:, cols])
            dv[...] += dot_f32(probs.astype(low), d[cols])
            grad_probs = dot_f32(values, d_t[:, cols])
            grad_scores = (probs * (grad_probs - delta[:, cols])).astype(low)
            dk[...] += dot_f32(grad_scores, q[cols])
            dq_t[:, cols] += dot_f32(keys_t, grad_scores)

        query_tile(block, True)

        def later(index, inner):
            query_tile(index, False)
            return inner

        lax.fori_loop(block + 1, tiles, later, 0)
        for kind, value in enumerate(((dk[...] * scale).T.astype(low), dv[...].T.astype(low))):
            for half in range(halves):
                dkv_sorted[block * halves + half, kind] = value[:, half * RUN : (half + 1) * RUN]

    def key_tiles(start, stop):
        def one(block, carry):
            key_tile(block)
            return carry

        lax.fori_loop(start, stop, one, 0)

    swap = remote(dkv_slots.at[:, :, 1 - core], dkv_other, send_x, recv_x, sibling)
    dq_copies = return_copies(dq_slots, dq_own, send_q, recv_q)
    slot, owner = lax.rem(spot, 4), spot // 4
    dkv_copies = []
    for step in range(8):
        chip = lax.rem(spot + step, 8)
        parts = (
            dkv_slots.at[:, chip, core],
            dkv_own.at[slot, :, core],
            send_k.at[step],
            recv_k.at[slot, core],
            (row, chip, owner),
        )
        dkv_copies.append((parts, (owner == core) if step == 0 else False))

    def send_back():
        def unsort_run(run, carry):
            index = ids[run]
            for kind in range(2):
                dkv_slots[kind, run // per_device, run % per_device] = dkv_sorted[index, kind]
            return carry

        lax.fori_loop(0, runs, unsort_run, 0)
        swap.start()

        def turn_run(index, carry):
            value = dq_t[:, tile_at(index, RUN)] * scale
            d_slots[index // per_device, index % per_device] = value.astype(low)
            return carry

        lax.fori_loop(0, runs, turn_run, 0)

        def unsort_queries(run, carry):
            value = d_slots[order[runs + run, 0], order[runs + run, 1]]
            dq_slots[run // per_device, run % per_device] = value
            return carry

        lax.fori_loop(0, runs, unsort_queries, 0)
        start_return(dq_copies)

    def add_pairs():
        swap.wait()
        for chip in range(8):
            both = dkv_slots[:, chip, core].astype(full) + dkv_other[:, chip].astype(full)
            dkv_slots[:, chip, core] = both.astype(low)
        start_return(dkv_copies)


    def feed_forward():
        row_products(2 * FEED, 2, 1)
        for group in range(4):
            load_group(group).start()

    save_layer = pltpu.make_async_copy(part, layer_out, save_sem)

    def finish_layer():
        for index in range(4):
            pair_copy(index, 1).wait()
        pieces = width // PIECE

        def load_piece(index):
            lanes = pl.ds(index * PIECE, PIECE)
            return pltpu.make_async_copy(
                middle.at[:, lanes], middle_ring.at[index % 2], load_ring.at[index % 2]
            )

        load_piece(0).start()
        for index in range(pieces):
            if index + 1 < pieces:
                load_piece(index + 1).start()
            load_piece(index).wait()
            cut = pl.ds(index * PIECE, PIECE)
            value = part[:, cut].astype(full) + part_other[1, :, cut].astype(full)
            part[:, cut] = (value + middle_ring[index % 2]).astype(low)
        save_layer.start()


    def load_group(group):
        lanes = pl.ds(group * 4 * HEAD, 4 * HEAD)
        return pltpu.make_async_copy(
            near.at[:, :, :, :, lanes], weight.at[group], load_w.at[group]
        )

    load_mixed = pltpu.make_async_copy(
        mixed_low, right.at[:, pl.ds(qkv_width, out_width)], loads.at[0]
    )

    def project_back():
        load_mixed.start()
        for head in range(8):
            remote(
                dq_own.at[head], dq_own.at[head], send_q.at[0], recv_q.at[head], sibling
            ).wait_recv()
        for slot_in in range(4):
            for core_in in range(2):
                target = dkv_own.at[slot_in, :, core_in]
                remote(
                    target, target, send_k.at[0], recv_k.at[slot_in, core_in], sibling
                ).wait_recv()
        for group in range(4):
            for run in range(per_device):
                cols = slice(run * RUN, (run + 1) * RUN)
                turned = []
                for head in range(4):
                    if group < 2:
                        value = dq_own[4 * group + head, run]
                    else:
                        value = dkv_own[head, group - 2, run]
                    if group < 3:
                        front, back = value[:HALF].astype(full), value[HALF:].astype(full)
                        cos_part, sin_part = tables[0, :, cols], tables[1, :, cols]
                        turned.append((front * cos_part + back * sin_part).astype(low))
                        turned.append((back * cos_part - front * sin_part).astype(low))
                    else:
                        turned.append(value)
                right[cols, group * 4 * HEAD : (group + 1) * 4 * HEAD] = jnp.concatenate(
                    turned, axis=0
                ).T
        load_mixed.wait()

    def project_normed():
        save_layer.wait()
        for group in range(4):
            load_group(group).wait()
        stage(tokens).start()

        def block(index, carry):
            term = jnp.zeros((rows, quarter), full)
            for group in range(4):
                held = weight[group, index // 2, pl.ds(2 * lax.rem(index, 2), 2)]
                term = term + contract_cols(
                    right[:, group * 4 * HEAD : (group + 1) * 4 * HEAD],
                    held.reshape(quarter, 4 * HEAD),
                )
            part[:, tile_at(index, quarter)] = term.astype(low)
            pair_copy(index, 0).start()
            return carry

        lax.fori_loop(0, 4, block, 0)

    def save_input(index):
        cut = tile_at(index, rows // 8)
        slot = lax.rem(index, 2)
        return pltpu.make_async_copy(
            input_ring.at[slot], input_grad.at[cut], save_rows.at[slot]
        )

    def norm_back():
        stage(tokens).wait()
        for index in range(4):
            pair_copy(index, 0).wait()
        chunk = rows // 8

        def block(index, gain_grad):
            cut = tile_at(index, chunk)
            grad = part[cut].astype(full) + part_other[0, cut].astype(full)
            values = staged[cut].astype(full)
            inverse = lax.rsqrt(jnp.mean(values * values, axis=-1, keepdims=True) + epsilon)
            unit = values * inverse
            scaled = grad * gains_in[0:1]
            mean = jnp.mean(scaled * unit, axis=-1, keepdims=True)
            result = total[cut] + inverse * (scaled - unit * mean)

            @pl.when(index >= 2)
            def _():
                save_input(index - 2).wait()

            input_ring[lax.rem(index, 2)] = result.reshape(chunk, 1, width)
            save_input(index).start()
            return gain_grad + jnp.sum(grad * unit, axis=0, keepdims=True)

        gain_one_grad = lax.fori_loop(0, 8, block, jnp.zeros((1, width), full))
        lines = jnp.concatenate(
            [gain_one_grad, gain_two_grad[...], jnp.zeros((6, width), full)], axis=0
        )
        gain_columns[...] = lines.T
        for shard in range(16):
            held = gain_columns[shard * share : (shard + 1) * share]
            gain_messages[shard] = jnp.pad(held, ((0, WIDE - share), (0, 0))).T
        for copy in gain_copies:
            copy.start()
        gain_all[own_shard()] = gain_messages[own_shard()]

    gain_copies, gain_from = exchange_messages(
        lambda shard: gain_messages.at[shard], gain_all, send_gain, recv_gain
    )

    def finish_gains():
        for wait in gain_from:
            wait()
        gain_out[...] = jnp.sum(gain_all[...], axis=0)

    def take_normed():
        stage(normed_in).start()
        stage(normed_in).wait()
        turn_left(left_t, 2, staged)

    def start_forward():
        for piece in range(4):
            load_blocks(0, piece, 2 * FEED, 2)

    for copy in first_loads:
        copy.start()
    stage(cotangent).start()
    for piece in range(4):
        load_blocks(0, piece, 0, 4)
    for copy in early_loads:
        copy.start()
    greet(group_others())
    first_loads[0].wait()
    first_loads[1].wait()

    def wait_right():
        for copy in first_loads[2:]:
            copy.wait()

    plan = {
        2: [wait_right, second_back],
        3: [middle_back],
        4: [prepare],
        5: [start_forward, take_cotangents],
    }
    tiles_from, tile_ranges = 5, ((0, 1), (1, 2), (2, 3), (3, 5), (5, 8))
    later = {
        9: [send_back],
        11: [add_pairs, feed_forward, finish_layer, take_normed],
        12: [project_back],
        15: [lambda: turn_left(left_t, 0, grad_mid), project_normed],
        16: [norm_back],
        n + LAST - 1: [finish_gains],
    }

    def run(step, carry):
        for when, tasks in plan.items():

            @pl.when(step == when)
            def _():
                for task in tasks:
                    task()

        @pl.when(jnp.logical_and(step >= tiles_from, step < tiles_from + len(tile_ranges)))
        def _():
            start, stop = 0, 0
            for index, (first_tile, past_tile) in enumerate(tile_ranges):
                start = jnp.where(step == tiles_from + index, first_tile, start)
                stop = jnp.where(step == tiles_from + index, past_tile, stop)
            key_tiles(start, stop)

        for when, tasks in later.items():

            @pl.when(step == when)
            def _():
                for task in tasks:
                    task()

        sums.turn(step)
        return carry

    lax.fori_loop(0, n + LAST, run, 0)
    for index in (6, 7):
        save_input(index).wait()
    for copy in gain_copies:
        copy.wait_send()
    for step in (n - 2, n - 1):
        sums.each_save(step, lambda copy: copy.wait())
    for copies in (d_copies, dq_copies, dkv_copies):
        for parts, is_self in copies:
            if is_self is False:
                remote(*parts).wait_send()
            else:

                @pl.when(jnp.logical_not(is_self))
                def _():
                    remote(*parts).wait_send()


def backward(order, ids, *arrays):
    dma = pltpu.SemaphoreType.DMA
    vmem = pltpu.VMEM
    low, full = jnp.bfloat16, jnp.float32
    q_sorted, k_sorted, v_sorted, mixed_t, lse, cotangent, left, normed, right = arrays[:9]
    mixed_low, middle, near, far, tokens, gains, tables = arrays[9:]
    rows, width = cotangent.shape
    length = 8 * rows
    share = width // 16
    feed, query, out_width = right.shape[1] // 3, 8 * HEAD, mixed_low.shape[1]
    quarter = 4 * share
    per_device = rows // RUN
    heads = (8, per_device, HEAD, RUN)
    tall, flat = (length, HEAD), (HEAD, length)
    by_run = (length // RUN, RUN, HEAD)
    block = (rows, width)
    smem_spec = pl.BlockSpec(memory_space=pltpu.SMEM)
    shape = jax.ShapeDtypeStruct
    return pl.pallas_call(
        backward_kernel,
        in_specs=[smem_spec] * 2 + [any_spec()] * 14 + [vmem_spec()] * 2,
        out_specs=[any_spec()] * 9 + [vmem_spec()],
        out_shape=[
            shape((rows, 1, width), full),
            shape(block, low),
            *[
                shape((share, wide), full)
                for wide in (feed, feed, feed, query, query // 2, query // 2, out_width)
            ],
            shape((8, WIDE), full),
        ],
        scratch_shapes=[
            vmem(tall, low),
            vmem(flat, low),
            vmem(by_run, low),
            vmem(flat, low),
            vmem(tall, low),
            vmem(heads, low),
            vmem(heads, low),
            vmem(tall, low),
            vmem(flat, low),
            vmem(flat, full),
            vmem((1, length), full),
            vmem((1, length), full),
            vmem((TILE, HEAD), full),
            vmem((TILE, HEAD), full),
            vmem(heads, low),
            vmem((length // RUN, 2, HEAD, RUN), low),
            vmem((2,) + heads, low),
            vmem((2, 8, HEAD, RUN), low),
            vmem(heads, low),
            vmem((4, 2, per_device, HEAD, RUN), low),
            vmem((4, 2, 4, 2, share, 4 * HEAD), low),
            vmem((2, rows, PIECE), full),
            vmem((2, rows // 8, 1, width), full),
            vmem(block, low),
            vmem((2,) + block, low),
            vmem(block, full),
            vmem(block, low),
            vmem(block, low),
            vmem((1, width), full),
            vmem((3, 2, 2, quarter, rows), low),
            vmem(right.shape, low),
            vmem((width, 8), full),
            vmem((16, 8, WIDE), full),
            vmem((16, 8, WIDE), full),
            vmem((2, share, 2 * PIECE), full),
            vmem((3, 2, 2, quarter, PIECE), low),
            vmem((6, 2, 2, quarter, PIECE), low),
            vmem((3, 2, quarter, PIECE), low),
            vmem((6, 2, quarter, PIECE), low),
            vmem((4, 2, quarter, PIECE), low),
            vmem((4, 2, 3, share, PIECE), low),
            dma((7,)),
            dma((5,)),
            dma((16,)),
            dma((16,)),
            dma(()),
            dma((4,)),
            dma((2,)),
            dma((2,)),
            dma(()),
            dma((4, 2)),
            dma((8,)),
            dma((8,)),
            dma((8,)),
            dma(()),
            dma(()),
            dma((8,)),
            dma((4, 2)),
            dma((4,)),
            dma((2, 4)),
            dma((2, 3)),
            dma((3, 2)),
            dma((6, 2)),
            dma((3, 2)),
            dma((6, 2)),
            dma((4, 2, 3)),
            dma((4, 2, 3)),
        ],
        compiler_params=pltpu.CompilerParams(
            collective_id=2, has_side_effects=True, vmem_limit_bytes=62 * 1024 * 1024
        ),
        name="backward",
    )(
        order,
        ids,
        *arrays,
    )


def deliver_kernel(count, *refs):
    arrays, gain_grads = refs[:count], refs[count]
    results, gain_one, gain_two, sems = refs[count + 1 : -3], refs[-3], refs[-2], refs[-1]
    copies = [
        pltpu.make_async_copy(source, target, sems.at[index])
        for index, (source, target) in enumerate(zip(arrays, results))
    ]
    for copy in copies:
        copy.start()
    share = gain_one.shape[1]
    gain_one[...] = gain_grads[0:1, :share]
    gain_two[...] = gain_grads[1:2, :share]
    for copy in copies:
        copy.wait()


def deliver(arrays, gain_grads, share):
    count = len(arrays)
    shape = jax.ShapeDtypeStruct
    return pl.pallas_call(
        functools.partial(deliver_kernel, count),
        in_specs=[any_spec()] * count + [vmem_spec()],
        out_specs=[any_spec()] * count + [vmem_spec()] * 2,
        out_shape=[shape(array.shape, array.dtype) for array in arrays]
        + [shape((1, share), jnp.float32)] * 2,
        scratch_shapes=[pltpu.SemaphoreType.DMA((count,))],
        compiler_params=pltpu.CompilerParams(vmem_limit_bytes=VMEM_LIMIT),
        name="deliver",
    )(*arrays, gain_grads)


def by_heads(
    tokens,
    positions,
    gain_one,
    gain_two,
    w_query,
    w_key,
    w_value,
    w_out,
    w_gate,
    w_up,
    w_down,
    cotangent,
):
    rows, _, width = tokens.shape
    share = gain_one.shape[0]
    flat_in = tokens.reshape(rows, width)
    (
        near,
        far,
        normed,
        q_sorted,
        k_sorted,
        v_sorted,
        mixed_t,
        lse,
        mixed_low,
        middle,
        second,
        right,
        gains,
        tables,
        left,
        order,
        ids,
    ) = forward(
        flat_in,
        positions.reshape(1, rows),
        gain_one.reshape(1, share),
        gain_two.reshape(1, share),
        w_query,
        w_key,
        w_value,
        w_out.T,
        w_gate,
        w_up,
        w_down.T,
        cotangent.reshape(rows, width),
    )
    input_grad, layer_out, *grads, gain_grads = backward(
        order,
        ids,
        q_sorted,
        k_sorted,
        v_sorted,
        mixed_t,
        lse,
        cotangent.reshape(rows, width),
        left,
        normed,
        right,
        mixed_low,
        middle,
        near,
        far,
        flat_in,
        gains,
        tables,
    )
    input_grad, layer_out, *grads, grad_one, grad_two = deliver(
        [input_grad, layer_out, *grads], gain_grads, share
    )
    grad_gate, grad_up, grad_down, grad_query, grad_key, grad_value, grad_out = grads
    return (
        layer_out.reshape(rows, 1, width),
        input_grad,
        grad_one.reshape(share),
        grad_two.reshape(share),
        grad_query,
        grad_key,
        grad_value,
        grad_out.T,
        grad_gate,
        grad_up,
        grad_down.T,
    )


def solution(mesh):
    sizes = (mesh.shape["dp"], mesh.shape["context"], mesh.shape["tensor"])
    return jax.shard_map(
        by_heads if sizes == (2, 8, 2) else on_device,
        mesh=mesh,
        in_specs=(
            P("context", "dp", None),
            P("context", "dp"),
            P(("dp", "context")),
            P(("dp", "context")),
            P(("dp", "context"), "tensor"),
            P(("dp", "context"), "tensor"),
            P(("dp", "context"), "tensor"),
            P("tensor", ("dp", "context")),
            P(("dp", "context"), "tensor"),
            P(("dp", "context"), "tensor"),
            P("tensor", ("dp", "context")),
            P("context", "dp", None),
        ),
        out_specs=(
            P("context", "dp", None),
            P("context", "dp", None),
            P(("dp", "context")),
            P(("dp", "context")),
            P(("dp", "context"), "tensor"),
            P(("dp", "context"), "tensor"),
            P(("dp", "context"), "tensor"),
            P("tensor", ("dp", "context")),
            P(("dp", "context"), "tensor"),
            P(("dp", "context"), "tensor"),
            P("tensor", ("dp", "context")),
        ),
        check_vma=False,
    )
```

```python
import functools

import jax
import jax.numpy as jnp
import numpy as np
from jax import lax
from jax.experimental import pallas as pl
from jax.experimental.pallas import tpu as pltpu
from jax.sharding import PartitionSpec as P

HEAD = 96


epsilon = 1e-05
theta_base = 100000.0
masked_value = -1e30


def norm_forward(values_in, gain_vec):
    inverse = lax.rsqrt(jnp.mean(values_in * values_in, axis=-1, keepdims=True) + epsilon)
    unit_vals = values_in * inverse
    return (unit_vals, inverse, (unit_vals * gain_vec.astype(jnp.float32)).astype(jnp.bfloat16))


def norm_backward(grad_in, unit_vals, inverse, gain_vec):
    scaled = grad_in * gain_vec.astype(jnp.float32)
    grad_vals = inverse * (
        scaled - unit_vals * jnp.mean(scaled * unit_vals, axis=-1, keepdims=True)
    )
    return (grad_vals, jnp.sum(grad_in * unit_vals, axis=0))


def rotate(values_in, cos_part, sin_part):
    half_size = values_in.shape[-1] // 2
    front_half = values_in[..., :half_size]
    back_half = values_in[..., half_size:]
    return jnp.concatenate(
        [
            front_half * cos_part - back_half * sin_part,
            back_half * cos_part + front_half * sin_part,
        ],
        axis=-1,
    )


def contract_rows(left_mat, right_mat):
    return lax.dot_general(
        left_mat, right_mat, (((0,), (0,)), ((), ())), preferred_element_type=jnp.float32
    )


def contract_cols(left_mat, right_mat):
    return lax.dot_general(
        left_mat, right_mat, (((1,), (1,)), ((), ())), preferred_element_type=jnp.float32
    )


def on_device(
    tokens,
    positions,
    gain_one,
    gain_two,
    w_query,
    w_key,
    w_value,
    w_out,
    w_gate,
    w_up,
    w_down,
    cotangent,
):
    slot_count, seq_count, model_width = tokens.shape
    row_count = slot_count * seq_count
    gathered = (
        lax.all_gather(gain_one, ("dp", "context"), axis=0, tiled=True),
        lax.all_gather(gain_two, ("dp", "context"), axis=0, tiled=True),
        lax.all_gather(w_query, ("dp", "context"), axis=0, tiled=True),
        lax.all_gather(w_key, ("dp", "context"), axis=0, tiled=True),
        lax.all_gather(w_value, ("dp", "context"), axis=0, tiled=True),
        lax.all_gather(w_out, ("dp", "context"), axis=1, tiled=True),
        lax.all_gather(w_gate, ("dp", "context"), axis=0, tiled=True),
        lax.all_gather(w_up, ("dp", "context"), axis=0, tiled=True),
        lax.all_gather(w_down, ("dp", "context"), axis=1, tiled=True),
    )
    full_one, full_two, query_mat, key_mat, value_mat, out_mat, gate_mat, up_mat, down_mat = (
        gathered
    )
    heads_kv = key_mat.shape[1] // HEAD
    heads_q = query_mat.shape[1] // HEAD
    group_size = heads_q // heads_kv
    score_scale = HEAD ** (-0.5)
    half_size = HEAD // 2
    inv_freqs = theta_base ** (-2.0 * jnp.arange(half_size, dtype=jnp.float32) / HEAD)
    angles = positions.astype(jnp.float32)[:, :, None] * inv_freqs
    cos_part = jnp.cos(angles)[:, :, None, :]
    sin_part = jnp.sin(angles)[:, :, None, :]
    flat_in = tokens.astype(jnp.float32).reshape(row_count, model_width)
    unit_one, inverse_one, normed = norm_forward(flat_in, full_one)
    query_proj = jnp.dot(normed, query_mat, preferred_element_type=jnp.float32).reshape(
        slot_count, seq_count, heads_q, HEAD
    )
    key_proj = jnp.dot(normed, key_mat, preferred_element_type=jnp.float32).reshape(
        slot_count, seq_count, heads_kv, HEAD
    )
    value_low = (
        jnp.dot(normed, value_mat, preferred_element_type=jnp.float32)
        .astype(jnp.bfloat16)
        .reshape(slot_count, seq_count, heads_kv * HEAD)
    )
    queries = rotate(query_proj, cos_part, sin_part).astype(jnp.bfloat16)
    keys_low = (
        rotate(key_proj, cos_part, sin_part)
        .astype(jnp.bfloat16)
        .reshape(slot_count, seq_count, heads_kv * HEAD)
    )
    query_seq = jnp.transpose(
        queries.reshape(slot_count, seq_count, heads_kv, group_size, HEAD), (1, 2, 3, 0, 4)
    )
    query_pos = positions.T
    stat_shape = (seq_count, heads_kv, group_size, slot_count)
    initial = (
        jnp.full(stat_shape, masked_value, jnp.float32),
        jnp.zeros(stat_shape, jnp.float32),
        jnp.zeros(stat_shape + (HEAD,), jnp.float32),
    )
    key_piece = lax.all_gather(keys_low, "context", axis=0, tiled=True)
    value_piece = lax.all_gather(value_low, "context", axis=0, tiled=True)
    pos_piece = lax.all_gather(positions, "context", axis=0, tiled=True)
    piece_len = key_piece.shape[0]
    key_seq = jnp.transpose(key_piece.reshape(piece_len, seq_count, heads_kv, HEAD), (1, 2, 0, 3))
    value_seq = jnp.transpose(
        value_piece.reshape(piece_len, seq_count, heads_kv, HEAD), (1, 2, 0, 3)
    )
    pos_seq = pos_piece.T

    def per_sequence(seq_items):
        peak_val, totals, accum_vals, query_one, qpos_one, key_one, value_one, kpos_one = seq_items
        raw_scores = (
            jnp.einsum("hgqd,hkd->hgqk", query_one, key_one, preferred_element_type=jnp.float32)
            * score_scale
        )
        allowed = kpos_one[None, None, None, :] <= qpos_one[None, None, :, None]
        masked = jnp.where(allowed, raw_scores, masked_value)
        new_peak = jnp.maximum(peak_val, jnp.max(masked, axis=-1))
        decay_vals = jnp.exp(peak_val - new_peak)
        weights = jnp.where(allowed, jnp.exp(masked - new_peak[..., None]), 0.0)
        totals = totals * decay_vals + jnp.sum(weights, axis=-1)
        accum_vals = accum_vals * decay_vals[..., None] + jnp.einsum(
            "hgqk,hkd->hgqd",
            weights.astype(jnp.bfloat16),
            value_one,
            preferred_element_type=jnp.float32,
        )
        return (new_peak, totals, accum_vals)

    peak_val, totals, accum_vals = lax.map(
        per_sequence,
        (initial[0], initial[1], initial[2], query_seq, query_pos, key_seq, value_seq, pos_seq),
    )
    log_total = peak_val + jnp.log(totals)
    mixed_seq = accum_vals / totals[..., None]
    mixed_low = (
        jnp.transpose(mixed_seq, (3, 0, 1, 2, 4))
        .reshape(row_count, heads_q * HEAD)
        .astype(jnp.bfloat16)
    )
    branch = lax.psum(
        jnp.dot(mixed_low, out_mat, preferred_element_type=jnp.float32).astype(jnp.bfloat16),
        "tensor",
    ).astype(jnp.float32)
    middle = flat_in + branch
    unit_two, inverse_two, second = norm_forward(middle, full_two)
    gate_vals = jnp.dot(second, gate_mat, preferred_element_type=jnp.float32)
    up_vals = jnp.dot(second, up_mat, preferred_element_type=jnp.float32)
    sigmoid_vals = jax.nn.sigmoid(gate_vals)
    silu_vals = gate_vals * sigmoid_vals
    hidden = (silu_vals * up_vals).astype(jnp.bfloat16)
    mlp_part = lax.psum(
        jnp.dot(hidden, down_mat, preferred_element_type=jnp.float32).astype(jnp.bfloat16), "tensor"
    ).astype(jnp.float32)
    layer_out = (middle + mlp_part).astype(jnp.bfloat16).reshape(slot_count, seq_count, model_width)
    regathered = (
        lax.all_gather(gain_one, ("dp", "context"), axis=0, tiled=True),
        lax.all_gather(gain_two, ("dp", "context"), axis=0, tiled=True),
        lax.all_gather(w_query, ("dp", "context"), axis=0, tiled=True),
        lax.all_gather(w_key, ("dp", "context"), axis=0, tiled=True),
        lax.all_gather(w_value, ("dp", "context"), axis=0, tiled=True),
        lax.all_gather(w_out, ("dp", "context"), axis=1, tiled=True),
        lax.all_gather(w_gate, ("dp", "context"), axis=0, tiled=True),
        lax.all_gather(w_up, ("dp", "context"), axis=0, tiled=True),
        lax.all_gather(w_down, ("dp", "context"), axis=1, tiled=True),
    )
    full_one, full_two, query_mat, key_mat, value_mat, out_mat, gate_mat, up_mat, down_mat = (
        regathered
    )
    grad_low = cotangent.reshape(row_count, model_width)
    grad_down = contract_rows(hidden, grad_low)
    grad_hidden = contract_cols(grad_low, down_mat)
    grad_gate_low = (
        grad_hidden * up_vals * sigmoid_vals * (1.0 + gate_vals * (1.0 - sigmoid_vals))
    ).astype(jnp.bfloat16)
    grad_up_low = (grad_hidden * silu_vals).astype(jnp.bfloat16)
    grad_gate = contract_rows(second, grad_gate_low)
    grad_up = contract_rows(second, grad_up_low)
    grad_second = lax.psum(
        (contract_cols(grad_gate_low, gate_mat) + contract_cols(grad_up_low, up_mat)).astype(
            jnp.bfloat16
        ),
        "tensor",
    ).astype(jnp.float32)
    grad_mid_norm, grad_gain_two = norm_backward(grad_second, unit_two, inverse_two, full_two)
    grad_middle = grad_low.astype(jnp.float32) + grad_mid_norm
    grad_mid_low = grad_middle.astype(jnp.bfloat16)
    grad_out = contract_rows(mixed_low, grad_mid_low)
    grad_mixed = contract_cols(grad_mid_low, out_mat).astype(jnp.bfloat16)
    grad_mixed_seq = jnp.transpose(
        grad_mixed.reshape(slot_count, seq_count, heads_kv, group_size, HEAD), (1, 2, 3, 0, 4)
    )
    delta_rows = jnp.sum(grad_mixed_seq.astype(jnp.float32) * mixed_seq, axis=-1)
    kv_width = heads_kv * HEAD

    def block_grads(grad_query_acc, key_blk, value_blk, pos_blk):
        block_len = key_blk.shape[0]
        key_seq = jnp.transpose(key_blk.reshape(block_len, seq_count, heads_kv, HEAD), (1, 2, 0, 3))
        value_seq = jnp.transpose(
            value_blk.reshape(block_len, seq_count, heads_kv, HEAD), (1, 2, 0, 3)
        )
        raw_scores = (
            jnp.einsum("shgqd,shkd->shgqk", query_seq, key_seq, preferred_element_type=jnp.float32)
            * score_scale
        )
        allowed = pos_blk.T[:, None, None, None, :] <= query_pos[:, None, None, :, None]
        prob_vals = jnp.where(
            allowed,
            jnp.exp(jnp.where(allowed, raw_scores - log_total[..., None], masked_value)),
            0.0,
        )
        grad_value_blk = jnp.einsum(
            "shgqk,shgqd->kshd",
            prob_vals.astype(jnp.bfloat16),
            grad_mixed_seq,
            preferred_element_type=jnp.float32,
        )
        grad_probs = jnp.einsum(
            "shgqd,shkd->shgqk", grad_mixed_seq, value_seq, preferred_element_type=jnp.float32
        )
        grad_scores = (prob_vals * (grad_probs - delta_rows[..., None])).astype(jnp.bfloat16)
        grad_query_acc = grad_query_acc + jnp.einsum(
            "shgqk,shkd->shgqd", grad_scores, key_seq, preferred_element_type=jnp.float32
        )
        grad_key_blk = jnp.einsum(
            "shgqk,shgqd->kshd", grad_scores, query_seq, preferred_element_type=jnp.float32
        )
        return (
            grad_query_acc,
            grad_key_blk.reshape(block_len, seq_count, kv_width),
            grad_value_blk.reshape(block_len, seq_count, kv_width),
        )

    zero_query = jnp.zeros(stat_shape + (HEAD,), jnp.float32)
    key_all, value_all, pos_all = (
        lax.all_gather(keys_low, "context", axis=0, tiled=True),
        lax.all_gather(value_low, "context", axis=0, tiled=True),
        lax.all_gather(positions, "context", axis=0, tiled=True),
    )
    total_len = key_all.shape[0]
    block_size = min(512, total_len)
    block_count = total_len // block_size

    def key_block(grad_query_acc, block_items):
        key_blk, value_blk, pos_blk = block_items
        grad_query_acc, grad_key_blk, grad_value_blk = block_grads(
            grad_query_acc, key_blk, value_blk, pos_blk
        )
        return (grad_query_acc, (grad_key_blk, grad_value_blk))

    grad_query_acc, (grad_keys_all, grad_values_all) = lax.scan(
        key_block,
        zero_query,
        (
            key_all.reshape(block_count, block_size, seq_count, kv_width),
            value_all.reshape(block_count, block_size, seq_count, kv_width),
            pos_all.reshape(block_count, block_size, seq_count),
        ),
    )
    grad_key_own, grad_value_own = (
        lax.psum_scatter(
            grad_keys_all.reshape(total_len, seq_count, kv_width).astype(jnp.bfloat16),
            "context",
            scatter_dimension=0,
            tiled=True,
        ).astype(jnp.float32),
        lax.psum_scatter(
            grad_values_all.reshape(total_len, seq_count, kv_width).astype(jnp.bfloat16),
            "context",
            scatter_dimension=0,
            tiled=True,
        ).astype(jnp.float32),
    )
    grad_rot_q = jnp.transpose(grad_query_acc * score_scale, (3, 0, 1, 2, 4)).reshape(
        slot_count, seq_count, heads_q, HEAD
    )
    grad_q_low = (
        rotate(grad_rot_q, cos_part, -sin_part)
        .reshape(row_count, heads_q * HEAD)
        .astype(jnp.bfloat16)
    )
    grad_rot_k = (grad_key_own * score_scale).reshape(slot_count, seq_count, heads_kv, HEAD)
    grad_k_low = (
        rotate(grad_rot_k, cos_part, -sin_part).reshape(row_count, kv_width).astype(jnp.bfloat16)
    )
    grad_v_low = grad_value_own.reshape(row_count, kv_width).astype(jnp.bfloat16)
    grad_query = contract_rows(normed, grad_q_low)
    grad_key = contract_rows(normed, grad_k_low)
    grad_value = contract_rows(normed, grad_v_low)
    grad_normed = lax.psum(
        (
            contract_cols(grad_q_low, query_mat)
            + contract_cols(grad_k_low, key_mat)
            + contract_cols(grad_v_low, value_mat)
        ).astype(jnp.bfloat16),
        "tensor",
    ).astype(jnp.float32)
    grad_in_norm, grad_gain_one = norm_backward(grad_normed, unit_one, inverse_one, full_one)
    input_grad = (grad_middle + grad_in_norm).reshape(slot_count, seq_count, model_width)
    reduced = (
        lax.psum_scatter(grad_gain_one, ("dp", "context"), scatter_dimension=0, tiled=True),
        lax.psum_scatter(grad_gain_two, ("dp", "context"), scatter_dimension=0, tiled=True),
        lax.psum_scatter(grad_query, ("dp", "context"), scatter_dimension=0, tiled=True),
        lax.psum_scatter(grad_key, ("dp", "context"), scatter_dimension=0, tiled=True),
        lax.psum_scatter(grad_value, ("dp", "context"), scatter_dimension=0, tiled=True),
        lax.psum_scatter(grad_out, ("dp", "context"), scatter_dimension=1, tiled=True),
        lax.psum_scatter(grad_gate, ("dp", "context"), scatter_dimension=0, tiled=True),
        lax.psum_scatter(grad_up, ("dp", "context"), scatter_dimension=0, tiled=True),
        lax.psum_scatter(grad_down, ("dp", "context"), scatter_dimension=1, tiled=True),
    )
    return (
        layer_out,
        input_grad,
        reduced[0],
        reduced[1],
        reduced[2],
        reduced[3],
        reduced[4],
        reduced[5],
        reduced[6],
        reduced[7],
        reduced[8],
    )


WIDE = 128
HALF = HEAD // 2
RUN = 256
TILE = 512
LOG2_E = 1.4426950408889634
MESH = pl.DeviceIdType.MESH
PIECE = 256
FEED = 512
VMEM_LIMIT = 56 * 1024 * 1024


def any_spec():
    return pl.BlockSpec(memory_space=pl.ANY)


def vmem_spec():
    return pl.BlockSpec(memory_space=pltpu.VMEM)


def place():
    return lax.axis_index("dp"), lax.axis_index("context"), lax.axis_index("tensor")


def greet(devices):
    barrier = pltpu.get_barrier_semaphore()
    for device in devices:
        pl.semaphore_signal(barrier, inc=1, device_id=device, device_id_type=MESH)
    pl.semaphore_wait(barrier, len(devices))


def sequence_others():
    row, spot, core = place()
    return [
        (row, lax.rem(spot + shift, 8), lax.rem(core + flip, 2))
        for shift in range(8)
        for flip in range(2)
        if shift or flip
    ]


def lane_freqs():
    return jnp.asarray(
        np.power(np.float32(theta_base), np.float32(-2.0) * np.arange(HALF, dtype=np.float32) / HEAD)
    ).reshape(HALF, 1)


def dot_f32(left, right):
    return jnp.dot(left, right, preferred_element_type=jnp.float32)


def own_shard():
    row, spot, core = place()
    return row * 8 + spot


def group_others():
    row, spot, core = place()
    return sequence_others() + [(1 - row, lax.rem(spot + shift, 8), core) for shift in range(8)]


def exchange_messages(message_to, landing, send, recv):
    row, spot, core = place()
    copies, waits = [], []

    def one(flip, shift):
        at = flip * 8 + shift
        to_row = lax.rem(row + flip, 2)
        chip, source = lax.rem(spot + shift, 8), lax.rem(spot + 8 - shift, 8)
        device = (to_row, chip, core)
        message = message_to(to_row * 8 + chip)
        copies.append(
            remote(message, landing.at[row * 8 + spot], send.at[at], recv.at[at], device)
        )
        came = landing.at[to_row * 8 + source]
        waits.append(remote(came, came, send.at[at], recv.at[at], device).wait_recv)

    for flip in range(2):
        for shift in range(8):
            if flip or shift:
                one(flip, shift)
    return copies, waits


def turn_left(left_t, index, source):
    quarter = source.shape[1] // 4
    share = quarter // 4
    for piece in range(4):
        turned = source[:, piece * quarter : (piece + 1) * quarter].T
        for inner in range(4):
            x, z, y = piece // 2, 2 * (piece % 2) + inner // 2, inner % 2
            left_t[index, x, y, z * share : (z + 1) * share] = turned[
                inner * share : (inner + 1) * share
            ]


def remote(source, target, send, recv, device):
    return pltpu.make_async_remote_copy(
        src_ref=source,
        dst_ref=target,
        send_sem=send,
        recv_sem=recv,
        device_id=device,
        device_id_type=MESH,
    )


def move(source, target, send, recv, device, is_self):
    @pl.when(is_self)
    def _():
        pltpu.make_async_copy(source, target, recv).start()

    @pl.when(jnp.logical_not(is_self))
    def _():
        remote(source, target, send, recv, device).start()


def return_copies(ref, out, send, recv):
    row, spot, core = place()
    head = 2 * lax.rem(spot, 4) + core
    owner = spot // 4
    copies = []
    for step in range(8):
        chip = lax.rem(spot + step, 8)
        is_self = (owner == core) if step == 0 else False
        parts = (ref.at[chip], out.at[head], send.at[step], recv.at[head], (row, chip, owner))
        copies.append((parts, is_self))
    return copies


def start_return(copies):
    for parts, is_self in copies:
        if is_self is False:
            remote(*parts).start()
        else:
            move(*parts, is_self)


def finish_return(copies, out, send, recv):
    row, spot, core = place()
    for head in range(8):
        remote(
            out.at[head], out.at[head], send.at[0], recv.at[head], (row, spot, 1 - core)
        ).wait_recv()
    for parts, is_self in copies:
        if is_self is False:
            remote(*parts).wait_send()
        else:

            @pl.when(jnp.logical_not(is_self))
            def _():
                remote(*parts).wait_send()


def tile_at(index, size):
    return pl.ds(pl.multiple_of(index * size, size), size)


def causal(scores):
    keys = lax.broadcasted_iota(jnp.int32, scores.shape, 0)
    queries = lax.broadcasted_iota(jnp.int32, scores.shape, 1)
    return jnp.where(keys <= queries, scores, masked_value)


def neighbours():
    row, spot, core = place()
    level, column = spot // 2, lax.rem(spot, 2)
    beside_x = (1 - row, spot, core)
    beside_y = (row, 2 * level + 1 - column, core)
    along_z = [(row, 2 * lax.rem(level + k, 4) + column, core) for k in (1, 2, 3)]
    return row, level, column, beside_x, beside_y, along_z


class Gather:
    def __init__(self, own, whole, start, width, piece, sems):
        self.own, self.whole = own.at[:, pl.ds(start, width)], whole
        self.start, self.width = start, width
        names = ("send_z", "recv_z", "send_x", "recv_x", "send_y", "recv_y", "send_d", "recv_d")
        for name, sem in zip(names + ("local",), sems):
            setattr(self, name, sem.at[piece])

    def block(self, x, z, y, half=None):
        cut = self.width * 7 // 12 // WIDE * WIDE
        start, width = self.start, self.width
        if half == 0:
            width = cut
        elif half == 1:
            start, width = start + cut, width - cut
        return self.whole.at[x, z, y, :, pl.ds(start, width)]

    def arrived(self, target, recv_sem):
        device = neighbours()[3]
        remote(target, target, self.send_x.at[0], recv_sem, device).wait_recv()

    def copy_z(self, z, up, own=False):
        row, level, column, beside_x, beside_y = neighbours()[:5]
        core = place()[2]
        target = level + 1 if up else level - 1
        block = self.block(row, z, column)
        return remote(
            self.own if own else block,
            block,
            self.send_z.at[int(up), z],
            self.recv_z.at[z],
            (row, 2 * target + column, core),
        )

    def copies_xy(self, z, own=False):
        row, level, column, beside_x, beside_y = neighbours()[:5]
        block = self.block(row, z, column)
        source = self.own if own else block
        return [
            remote(source, block, self.send_x.at[z], self.recv_x.at[z], beside_x),
            remote(source, block, self.send_y.at[z], self.recv_y.at[z], beside_y),
        ]

    def copies_diagonal(self, z):
        row, level, column, beside_x, beside_y = neighbours()[:5]
        by_y = self.block(1 - row, z, column, 1)
        by_x = self.block(row, z, 1 - column, 0)
        return [
            remote(by_y, by_y, self.send_d.at[0, z], self.recv_d.at[0, z], beside_y),
            remote(by_x, by_x, self.send_d.at[1, z], self.recv_d.at[1, z], beside_x),
        ]

    def own_copy(self):
        row, level, column = neighbours()[:3]
        return pltpu.make_async_copy(self.own, self.block(row, level, column), self.local)

    def each_at(self, hop, act):
        level = neighbours()[1]

        @pl.when(level >= hop)
        def _():
            act(level - hop, True)

        @pl.when(level + hop <= 3)
        def _():
            act(level + hop, False)

    def start_z(self, z, up, own=False):
        level = neighbours()[1]

        @pl.when(level < 3 if up else level > 0)
        def _():
            self.copy_z(z, up, own).start()

    def place_own(self):
        self.own_copy().start()

    def open(self):
        level = neighbours()[1]
        self.start_z(level, True, True)
        self.start_z(level, False, True)
        for copy in self.copies_xy(level, True):
            copy.start()

    def hop(self, hop):
        def act(z, up):
            row, level, column = neighbours()[:3]
            self.arrived(self.block(row, z, column), self.recv_z.at[z])
            self.start_z(z, up)
            for copy in self.copies_xy(z):
                copy.start()

        self.each_at(hop, act)

    def turn_diagonal(self, z):
        row, level, column = neighbours()[:3]
        by_y, by_x = self.copies_diagonal(z)
        self.arrived(self.block(1 - row, z, column), self.recv_x.at[z])
        by_y.start()
        self.arrived(self.block(row, z, 1 - column), self.recv_y.at[z])
        by_x.start()

    def diagonal(self, hop):
        if hop == 0:
            self.turn_diagonal(neighbours()[1])
        else:
            self.each_at(hop, lambda z, up: self.turn_diagonal(z))

    def finish(self):
        row, level, column = neighbours()[:3]
        self.own_copy().wait()
        for z in range(4):
            self.arrived(self.block(1 - row, z, 1 - column, 1), self.recv_d.at[0, z])
            self.arrived(self.block(1 - row, z, 1 - column, 0), self.recv_d.at[1, z])

    def close_z(self):
        level = neighbours()[1]

        def sent(z, up):
            @pl.when(level < 3 if up else level > 0)
            def _():
                self.copy_z(z, up).wait_send()

        sent(level, True)
        sent(level, False)
        for hop in range(1, 4):
            self.each_at(hop, sent)

    def close(self):
        self.close_z()
        for z in range(4):
            for copy in self.copies_xy(z) + self.copies_diagonal(z):
                copy.wait_send()


class PlaneGather(Gather):
    def plane(self, z):
        return self.whole.at[:, z, :, :, pl.ds(self.start, self.width)]

    def copy_z(self, z, up, own=False):
        row, level, column = neighbours()[:3]
        target = level + 1 if up else level - 1
        plane = self.plane(z)
        return remote(
            plane,
            plane,
            self.send_z.at[int(up), z],
            self.recv_z.at[z],
            (row, 2 * target + column, place()[2]),
        )

    def open(self):
        for copy in self.copies_xy(neighbours()[1], True):
            copy.start()

    def spread(self):
        row, level, column = neighbours()[:3]
        self.arrived(self.block(1 - row, level, 1 - column, 1), self.recv_d.at[0, level])
        self.arrived(self.block(1 - row, level, 1 - column, 0), self.recv_d.at[1, level])
        self.own_copy().wait()
        self.start_z(level, True)
        self.start_z(level, False)

    def hop(self, hop):
        def act(z, up):
            self.arrived(self.plane(z), self.recv_z.at[z])
            self.start_z(z, up)

        self.each_at(hop, act)

    def finish(self):
        pass

    def close(self):
        level = neighbours()[1]
        self.close_z()
        for copy in self.copies_xy(level) + self.copies_diagonal(level):
            copy.wait_send()


def gather_sems(pieces):
    dma = pltpu.SemaphoreType.DMA
    shapes = [(2, 4), (4,), (4,), (4,), (4,), (4,), (2, 4), (2, 4), ()]
    return [dma((pieces,) + shape) for shape in shapes]


AT_BEGIN, AT_GAINS, AT_PAIRS, AT_QUERIES, AT_HEADS, AT_KEYS, AT_ALL, AT_SORT = 0, 1, 2, 3, 4, 5, 6, 7
AT_RETURN, AT_MIXED, AT_OUT, AT_NORM, AT_GROUP, AT_TILE, AT_FEED = 8, 9, 10, 11, 12, 16, 24
PUMPS = {
    AT_BEGIN: (1, 10, 4, 2, 3, 5, 7, 6, 11, 12, 13, 14),
    AT_GAINS: (20,),
    AT_GROUP + 2: (15, 17),
    AT_GROUP + 3: (16, 70),
    AT_QUERIES: (21, 30),
    AT_GROUP + 0: (50,),
    AT_GROUP + 1: (22,),
    AT_HEADS: (74, 40, 31, 60, 23),
    AT_KEYS: (34, 75),
    AT_ALL: (32, 24, 35, 44),
    AT_TILE + 0: (41, 25),
    AT_TILE + 2: (33, 26, 61, 42, 71),
    AT_TILE + 3: (27, 51),
    AT_RETURN: (36, 37, 43, 52, 45, 55, 72, 47, 54, 46),
    AT_MIXED: (64,),
    AT_OUT: (53,),
    AT_NORM: (56, 62),
    AT_FEED + 1: (63, 57),
    AT_FEED + 3: (65, 66, 67),
    AT_FEED + 5: (73,),
}


def forward_kernel(
    tokens,
    positions,
    freqs,
    gain_one,
    gain_two,
    w_query,
    w_key,
    w_value,
    w_out_t,
    w_gate,
    w_up,
    w_down_t,
    cotangent,
    near,
    far,
    normed_out,
    q_out,
    k_out,
    v_out,
    mixed_t_out,
    lse_out,
    mixed_low_out,
    middle_out,
    second_out,
    right_out,
    gains_out,
    tables_out,
    left_out,
    order,
    ids_flat,
    ids_in,
    near_own,
    far_own,
    unit,
    normed,
    tables,
    weight,
    gain_message,
    gain_all,
    gain_columns,
    gain_rows,
    left_t,
    q_heads,
    kv_heads,
    q_slots,
    kv_slots,
    q_t,
    keys,
    v_t,
    mixed_t,
    lse,
    mixed,
    mixed_slots,
    mixed_heads,
    mixed_low,
    out_weight,
    part,
    part_other,
    second,
    cot,
    right,
    feed_weight,
    ids_all,
    ids,
    load_own,
    send_ids,
    recv_ids,
    load_ids,
    send_gain,
    recv_gain,
    load_w,
    load_out,
    load_feed,
    load_cot,
    save_right,
    saves,
    send_q,
    recv_q,
    send_kv,
    recv_kv,
    send_x,
    recv_x,
    send_m,
    recv_m,
    send_p,
    recv_p,
    *sems,
):
    row, spot, core = place()
    low, full = jnp.bfloat16, jnp.float32
    rows, width = tokens.shape
    share = near_own.shape[0]
    length = 8 * rows
    runs, tiles = length // RUN, length // TILE
    per_device = rows // RUN
    halves = TILE // RUN
    quarter = 4 * share
    sibling = (row, spot, 1 - core)
    out_width = w_out_t.shape[1]
    qkv_width = 16 * HEAD

    near_loads, far_loads, start = [], [], 0
    for ref in (w_query, w_key, w_value, w_out_t):
        target = near_own.at[:, pl.ds(start, ref.shape[1])]
        near_loads.append(pltpu.make_async_copy(ref, target, load_own.at[len(near_loads)]))
        start += ref.shape[1]
    for index, ref in enumerate((w_gate, w_up, w_down_t)):
        for piece in range(4):
            source = ref.at[:, pl.ds(piece * FEED, FEED)]
            target = far_own.at[:, pl.ds((3 * piece + index) * FEED, FEED)]
            far_loads.append(
                pltpu.make_async_copy(source, target, load_own.at[4 + 4 * index + piece])
            )
    for copy in near_loads + far_loads:
        copy.start()
    load_cotangent = pltpu.make_async_copy(cotangent, cot, load_cot)
    load_cotangent.start()
    half = qkv_width // 2
    pairs = Gather(near_own, near, half, half, 0, sems)
    first = Gather(near_own, near, 0, half, 1, sems)
    outer = Gather(near_own, near, qkv_width, out_width, 2, sems)
    feeds = [Gather(far_own, far, 3 * FEED * p, 3 * FEED, 3 + p, sems) for p in range(3)]
    feeds.append(Gather(far_own, far, 9 * FEED, FEED, 6, sems))
    plane = PlaneGather(far_own, far, 10 * FEED, 2 * FEED, 7, sems)
    gathers = [pairs, first, outer] + feeds + [plane]

    def pump(place):
        for what in PUMPS.get(place, ()):
            gather, act = gathers[what // 10], what % 10
            if act == 0:
                gather.open()
            elif act < 4:
                gather.hop(act)
            elif gather is plane and act == 5:
                gather.spread()
            else:
                gather.diagonal(act - 4)

    gain_message[...] = jnp.zeros_like(gain_message)
    gain_message[0:1, :share] = gain_one[...].astype(full)
    gain_message[1:2, :share] = gain_two[...].astype(full)
    for copy in near_loads:
        copy.wait()
    greet(group_others())
    pairs.open()
    for gather in (pairs, first, outer):
        gather.place_own()

    gain_copies, gain_from = exchange_messages(
        lambda shard: gain_message, gain_all, send_gain, recv_gain
    )
    for copy in gain_copies:
        copy.start()
    gain_all[own_shard()] = gain_message[...]

    lane = lax.broadcasted_iota(jnp.int32, (8, WIDE), 1)
    ids_in[...] = jnp.zeros_like(lane)
    for run in range(per_device):
        start_at = positions[0:1, run * RUN : run * RUN + 1]
        ids_in[...] = jnp.where(lane == run, lax.div(start_at, RUN), ids_in[...])
    for shift in range(1, 8):
        remote(
            ids_in,
            ids_all.at[spot],
            send_ids.at[shift],
            recv_ids.at[shift],
            (row, lax.rem(spot + shift, 8), core),
        ).start()
    ids_all[spot] = ids_in[...]

    for copy in far_loads:
        copy.wait()
    for gather in feeds + [plane]:
        gather.place_own()
    chunk = rows // 8

    def unit_block(index, carry):
        cut = tile_at(index, chunk)
        values = tokens[cut].astype(full)
        inverse = lax.rsqrt(jnp.mean(values * values, axis=-1, keepdims=True) + epsilon)
        unit[cut] = values * inverse
        return carry

    lax.fori_loop(0, 8, unit_block, 0)
    angles = freqs[...] * positions[...].astype(full)
    tables[0] = jnp.cos(angles)
    tables[1] = jnp.sin(angles)

    pump(AT_BEGIN)
    for shift in range(1, 8):
        remote(
            ids_in,
            ids_all.at[lax.rem(spot + 8 - shift, 8)],
            send_ids.at[shift],
            recv_ids.at[shift],
            (row, lax.rem(spot + shift, 8), core),
        ).wait_recv()
    pltpu.make_async_copy(ids_all, ids, load_ids).start()
    pairs.finish()

    width = near.shape[3] * 16

    def load_group(group):
        lanes = pl.ds(group * 4 * HEAD, 4 * HEAD)
        return pltpu.make_async_copy(
            near.at[:, :, :, :, lanes], weight.at[group % 2], load_w.at[group % 2]
        )

    load_out_weight = pltpu.make_async_copy(
        near.at[:, :, :, :, pl.ds(qkv_width, out_width)], out_weight, load_out
    )
    load_group(2).start()
    load_group(3).start()
    for wait in gain_from:
        wait()
    for shard in range(16):
        gain_columns[shard * share : (shard + 1) * share] = gain_all[shard].T[:share]
    gain_rows[...] = gain_columns[...].T
    normed[...] = (unit[...] * gain_rows[0:1]).astype(low)
    pump(AT_GAINS)

    def project(group):
        load_group(group).wait()
        proj = dot_f32(normed[...], weight[group % 2].reshape(width, 4 * HEAD)).T
        for head in range(4):
            front = proj[head * HEAD : head * HEAD + HALF]
            back = proj[head * HEAD + HALF : (head + 1) * HEAD]
            if group < 3:
                front, back = (
                    front * tables[0] - back * tables[1],
                    back * tables[0] + front * tables[1],
                )
            for start, value in ((0, front.astype(low)), (HALF, back.astype(low))):
                for run in range(per_device):
                    piece = value[:, run * RUN : (run + 1) * RUN]
                    if group < 2:
                        q_heads[4 * group + head, run, start : start + HALF] = piece
                    else:
                        kv_heads[head, group - 2, run, start : start + HALF] = piece
        pump(AT_GROUP + group)

    project(2)
    project(3)

    outgoing = []
    for step in range(4):
        slot = lax.rem(spot + step, 4)
        chip = 4 * core + slot
        for other in range(2):
            is_self = jnp.logical_and(chip == spot, core == other)
            device = (row, chip, other)
            kv_parts = (
                kv_heads.at[slot, :, other],
                kv_slots.at[spot, :, other],
                send_kv.at[step, other],
                recv_kv.at[spot],
                device,
            )
            q_parts = (
                q_heads.at[2 * slot + other],
                q_slots.at[spot],
                send_q.at[step, other],
                recv_q.at[spot],
                device,
            )
            outgoing.append((kv_parts, is_self))
            outgoing.append((q_parts, is_self))
    for parts, is_self in outgoing[0::2]:
        move(*parts, is_self)
    pump(AT_PAIRS)
    first.finish()
    load_group(0).start()
    load_group(1).start()
    pump(AT_QUERIES)
    project(0)
    project(1)
    for parts, is_self in outgoing[1::2]:
        move(*parts, is_self)
    pump(AT_HEADS)

    def hand_on(source):
        block = kv_slots.at[source, :, core]
        return remote(block, block, send_x.at[source], recv_x.at[source], sibling)

    for step in range(8):
        source = lax.rem(spot + step, 8)
        block = kv_slots.at[source, :, core]
        remote(block, block, send_x.at[source], recv_kv.at[source], sibling).wait_recv()
        hand_on(source).start()
    pump(AT_KEYS)
    for step in range(8):
        remote(
            q_slots.at[step], q_slots.at[step], send_x.at[step], recv_q.at[step], sibling
        ).wait_recv()
        hand_on(step).wait()
    pump(AT_ALL)

    pltpu.make_async_copy(ids_all, ids, load_ids).wait()

    def find_run(index, carry):
        device, piece = 0, 0
        for run in range(runs):
            here = ids[run // per_device, 0, run % per_device] == index
            device = jnp.where(here, run // per_device, device)
            piece = jnp.where(here, run % per_device, piece)
        order[index, 0] = device
        order[index, 1] = piece
        found = ids[index // per_device, 0, index % per_device]
        order[runs + index, 0] = lax.div(found, per_device)
        order[runs + index, 1] = lax.rem(found, per_device)
        ids_flat[index] = found
        return carry

    lax.fori_loop(0, runs, find_run, 0)

    def sort_run(index, carry):
        device, piece = order[index, 0], order[index, 1]
        cols = tile_at(index, RUN)
        q_t[:, cols] = q_slots[device, piece]
        keys[index] = kv_slots[device, 0, piece].T
        v_t[:, cols] = kv_slots[device, 1, piece]
        return carry

    lax.fori_loop(0, runs, sort_run, 0)
    pump(AT_SORT)
    scale = HEAD ** (-0.5) * LOG2_E

    def query_pair(pair, carry):
        def step(half, scores, block, peak, total, mix):
            high = jnp.maximum(peak, jnp.max(scores, axis=0, keepdims=True))
            decay = jnp.exp2(peak - high)
            weights = jnp.exp2(scores - high)
            total = total * decay + jnp.sum(weights, axis=0, keepdims=True)
            mix = mix * decay + dot_f32(v_t[:, tile_at(block, TILE)], weights.astype(low))
            return high, total, mix

        def scores_of(half, block):
            held = keys[pl.ds(block * halves, halves)].reshape(TILE, HEAD)
            return dot_f32(held, q_t[:, tile_at(2 * pair + half, TILE)]) * scale

        def full_block(block, states):
            scores = [scores_of(half, block) for half in range(2)]
            return tuple(step(half, scores[half], block, *states[half]) for half in range(2))

        state = (
            jnp.full((1, TILE), masked_value, full),
            jnp.zeros((1, TILE), full),
            jnp.zeros((HEAD, TILE), full),
        )
        start = 2 * pair
        scores = causal(scores_of(0, start)), scores_of(1, start)
        states = tuple(step(half, scores[half], start, *state) for half in range(2))
        last = step(1, causal(scores_of(1, start + 1)), start + 1, *states[1])
        states = lax.fori_loop(0, start, full_block, (states[0], last))
        for half in range(2):
            peak, total, mix = states[half]
            index = 2 * pair + half
            cols = tile_at(index, TILE)
            mix = mix / total
            mixed_t[:, cols] = mix
            lse[:, cols] = peak + jnp.log2(total)
            for run in range(halves):
                cut = mix[:, run * RUN : (run + 1) * RUN]
                mixed[index * halves + run] = cut.astype(low)
        for place in range(tiles // 2):

            @pl.when(pair == place)
            def _():
                pump(AT_TILE + place)

        return carry

    lax.fori_loop(0, tiles // 2, query_pair, 0)

    def unsort_run(run, carry):
        index = ids[run // per_device, 0, run % per_device]
        mixed_slots[run // per_device, run % per_device] = mixed[index]
        return carry

    lax.fori_loop(0, runs, unsort_run, 0)
    copies = return_copies(mixed_slots, mixed_heads, send_m, recv_m)
    start_return(copies)
    early_saves = [
        pltpu.make_async_copy(source, target, saves.at[index])
        for index, (source, target) in enumerate(
            [
                (normed, normed_out),
                (q_t, q_out),
                (keys, k_out),
                (v_t, v_out),
                (mixed_t, mixed_t_out),
                (lse, lse_out),
                (gain_rows, gains_out),
                (tables, tables_out),
            ]
        )
    ]
    for copy in early_saves:
        copy.start()
    pump(AT_RETURN)
    outer.finish()
    load_out_weight.start()
    finish_return(copies, mixed_heads, send_m, recv_m)
    pump(AT_MIXED)

    load_out_weight.wait()
    for run in range(per_device):
        side = mixed_heads[:, run].reshape(8 * HEAD, RUN)
        mixed_low[run * RUN : (run + 1) * RUN] = side.T

    def pair_copy(index):
        cut = pl.ds(index * quarter, quarter)
        return remote(
            part.at[:, cut], part_other.at[:, cut], send_p.at[index], recv_p.at[index], sibling
        )

    for index in range(4):
        block = out_weight[index // 2, 2 * (index % 2) : 2 * (index % 2) + 2]
        term = contract_cols(mixed_low[...], block.reshape(quarter, out_width))
        part[:, index * quarter : (index + 1) * quarter] = term.astype(low)
        pair_copy(index).start()
    pump(AT_OUT)
    load_cotangent.wait()
    for index in range(4):
        pair_copy(index).wait()
    chunk = rows // 8

    def norm_block(index, carry):
        cut = tile_at(index, chunk)
        sums = part[cut].astype(full) + part_other[cut].astype(full)
        values = tokens[cut].astype(full) + sums
        unit[cut] = values
        inverse = lax.rsqrt(jnp.mean(values * values, axis=-1, keepdims=True) + epsilon)
        second[cut] = (values * inverse * gain_rows[1:2]).astype(low)
        return carry

    lax.fori_loop(0, 8, norm_block, 0)
    late_saves = [
        pltpu.make_async_copy(source, target, saves.at[8 + index])
        for index, (source, target) in enumerate(
            [(mixed_low, mixed_low_out), (unit, middle_out), (second, second_out)]
        )
    ]
    for copy in late_saves:
        copy.start()
    pump(AT_NORM)

    def load_feed_weight(index, kind):
        piece, half = index // 2, lax.rem(index, 2)
        start = (3 * piece + kind) * FEED + half * PIECE
        lanes = pl.ds(pl.multiple_of(start, PIECE), PIECE)
        return pltpu.make_async_copy(
            far.at[:, :, :, :, lanes], feed_weight.at[half, kind], load_feed.at[half, kind]
        )

    def load_half(index):
        for kind in range(3):
            load_feed_weight(index, kind).start()

    def save_piece(piece):
        lanes = pl.ds(piece * 3 * FEED, 3 * FEED)
        return pltpu.make_async_copy(
            right.at[:, lanes], right_out.at[:, lanes], save_right.at[piece]
        )

    def feed_block(index, carry):
        piece, half = index // 2, lax.rem(index, 2)
        for when in range(3):

            @pl.when(index == (2 * when + 1 if when < 2 else 6))
            def _():
                feeds[when + 1].finish()

        @pl.when(index == 0)
        def _():
            load_half(0)

        @pl.when(index == 6)
        def _():
            load_half(6)

        @pl.when(jnp.logical_and(index != 5, index != 7))
        def _():
            load_half(index + 1)

        values = []
        for kind, left in enumerate((second, second, cot)):
            load_feed_weight(index, kind).wait()
            values.append(dot_f32(left[...], feed_weight[half, kind].reshape(width, PIECE)))
        gate, up, grad_hidden = values
        sigmoid = jax.nn.sigmoid(gate)
        silu = gate * sigmoid
        grad_gate = grad_hidden * up * sigmoid * (1.0 + gate * (1.0 - sigmoid))
        for when, source in ((1, second), (3, cot)):

            @pl.when(index == when)
            def _():
                turn_left(left_t, when % 3, source)

        for kind, value in enumerate((grad_gate, grad_hidden * silu, silu * up)):
            start = (3 * piece + kind) * FEED + half * PIECE
            right[:, pl.ds(pl.multiple_of(start, PIECE), PIECE)] = value.astype(low)

        for when in range(8):

            @pl.when(index == when)
            def _():
                pump(AT_FEED + when)

        for when in range(4):

            @pl.when(index == 2 * when + 1)
            def _():
                save_piece(when).start()

        return carry

    feeds[0].finish()
    lax.fori_loop(0, 8, feed_block, 0)
    save_left = pltpu.make_async_copy(left_t, left_out, saves.at[11])
    save_left.start()
    for gather in gathers:
        gather.close()
    for parts, is_self in outgoing:

        @pl.when(jnp.logical_not(is_self))
        def _():
            remote(*parts).wait_send()

    for shift in range(1, 8):
        remote(
            ids_in,
            ids_all.at[spot],
            send_ids.at[shift],
            recv_ids.at[shift],
            (row, lax.rem(spot + shift, 8), core),
        ).wait_send()
    for copy in gain_copies:
        copy.wait_send()
    for copy in early_saves + late_saves + [save_left] + [save_piece(piece) for piece in range(4)]:
        copy.wait()


def forward(
    tokens,
    positions,
    gain_one,
    gain_two,
    w_query,
    w_key,
    w_value,
    w_out_t,
    w_gate,
    w_up,
    w_down_t,
    cotangent,
):
    dma = pltpu.SemaphoreType.DMA
    vmem = pltpu.VMEM
    low, full = jnp.bfloat16, jnp.float32
    rows, width = tokens.shape
    share, hidden_width = w_gate.shape
    out_width = w_out_t.shape[1]
    near_width = 16 * HEAD + out_width
    length = 8 * rows
    per_device = rows // RUN
    heads = (8, per_device, HEAD, RUN)
    both = (2, per_device, HEAD, RUN)
    by_run = (length // RUN, RUN, HEAD)
    flat = (HEAD, length)
    smem_spec = pl.BlockSpec(memory_space=pltpu.SMEM)
    shape = jax.ShapeDtypeStruct
    return pl.pallas_call(
        forward_kernel,
        in_specs=[vmem_spec()] * 5 + [any_spec()] * 8,
        out_specs=[any_spec()] * 15 + [smem_spec] * 2,
        out_shape=[
            shape((2, 4, 2, share, near_width), low),
            shape((2, 4, 2, share, 3 * hidden_width), low),
            shape((rows, width), low),
            shape(flat, low),
            shape(by_run, low),
            shape(flat, low),
            shape(flat, full),
            shape((1, length), full),
            shape((rows, out_width), low),
            shape((rows, width), full),
            shape((rows, width), low),
            shape((rows, 3 * hidden_width), low),
            shape((8, width), full),
            shape((2, HALF, rows), full),
            shape((2, 2, 2, 4 * share, rows), low),
            shape((2 * length // RUN, 2), jnp.int32),
            shape((length // RUN,), jnp.int32),
        ],
        scratch_shapes=[
            vmem((8, WIDE), jnp.int32),
            vmem((share, near_width), low),
            vmem((share, 3 * hidden_width), low),
            vmem((rows, width), full),
            vmem((rows, width), low),
            vmem((2, HALF, rows), full),
            vmem((2, 2, 4, 2, share, 4 * HEAD), low),
            vmem((8, WIDE), full),
            vmem((16, 8, WIDE), full),
            vmem((width, 8), full),
            vmem((8, width), full),
            vmem((2, 2, 2, 4 * share, rows), low),
            vmem(heads, low),
            vmem((4,) + both, low),
            vmem(heads, low),
            vmem((8,) + both, low),
            vmem(flat, low),
            vmem(by_run, low),
            vmem(flat, low),
            vmem(flat, full),
            vmem((1, length), full),
            vmem((length // RUN, HEAD, RUN), low),
            vmem(heads, low),
            vmem(heads, low),
            vmem((rows, out_width), low),
            vmem((2, 4, 2, share, out_width), low),
            vmem((rows, width), low),
            vmem((rows, width), low),
            vmem((rows, width), low),
            vmem((rows, width), low),
            vmem((rows, 3 * hidden_width), low),
            vmem((2, 3, 2, 4, 2, share, PIECE), low),
            vmem((8, 8, WIDE), jnp.int32),
            pltpu.SMEM((8, 8, WIDE), jnp.int32),
            dma((16,)),
            dma((8,)),
            dma((8,)),
            dma(()),
            dma((16,)),
            dma((16,)),
            dma((2,)),
            dma(()),
            dma((2, 3)),
            dma(()),
            dma((4,)),
            dma((12,)),
            dma((4, 2)),
            dma((8,)),
            dma((4, 2)),
            dma((8,)),
            dma((8,)),
            dma((8,)),
            dma((8,)),
            dma((8,)),
            dma((4,)),
            dma((4,)),
        ]
        + gather_sems(8),
        compiler_params=pltpu.CompilerParams(
            collective_id=1, has_side_effects=True, vmem_limit_bytes=VMEM_LIMIT
        ),
        name="forward",
    )(
        tokens,
        positions,
        lane_freqs(),
        gain_one,
        gain_two,
        w_query,
        w_key,
        w_value,
        w_out_t,
        w_gate,
        w_up,
        w_down_t,
        cotangent,
    )


SECOND, THIRD, LAST = 2, 4, 5


class Reduce:
    def __init__(self, n, changes, refs):
        (
            self.left_t,
            self.right,
            self.own,
            self.out,
            self.save,
            self.send_one,
            self.recv_one,
            self.send_two,
            self.recv_two,
            self.kept,
            self.recv_three,
            self.ss_one,
            self.rs_one,
            self.ss_two,
            self.rs_two,
            self.ss_three,
            self.rs_three,
        ) = refs
        self.n, self.changes = n, changes
        self.share = self.own.shape[1]

    def columns(self, step, kind):
        held = self.right.shape[1] // (2 * PIECE)
        start = lax.rem(step, held) * 2 * PIECE + kind * PIECE
        return pl.ds(pl.multiple_of(start, PIECE), PIECE)

    def each_save(self, step, act):
        slot = lax.rem(step, 2)
        near_at = self.changes[0]

        def copies(cuts):
            for index, (ref, start, lanes) in enumerate(cuts):
                source = self.own.at[slot, :, lanes]
                target = ref.at[:, pl.ds(start, lanes.size)]
                act(pltpu.make_async_copy(source, target, self.save.at[slot, index]))

        for kind in range(3):

            @pl.when(jnp.logical_and(step < near_at, lax.rem(step, 3) == kind))
            def _():
                start = pl.multiple_of(step // 3 * 2 * PIECE, 2 * PIECE)
                copies([(self.out[kind], start, pl.ds(0, 2 * PIECE))])

        for index in range(self.n - near_at):
            first, past = index * 2 * PIECE, (index + 1) * 2 * PIECE
            cuts, at = [], 0
            for ref in self.out[3:]:
                low, high = max(first, at), min(past, at + ref.shape[1])
                if low < high:
                    cuts.append((ref, low - at, pl.ds(low - first, high - low)))
                at += ref.shape[1]

            @pl.when(step == near_at + index)
            def _():
                copies(cuts)

    def product(self, step, kind, x, y):
        left = jnp.where(lax.rem(step, 3) == 2, 0, 1)
        left = jnp.where(step >= self.changes[0], 2, left)
        left = jnp.where(step >= self.changes[1], 0, left)
        term = jnp.dot(
            self.left_t[left, x, y],
            self.right[:, self.columns(step, kind)],
            preferred_element_type=jnp.float32,
        )
        return term

    def x_first(self, step, kind):
        return 1 if kind == 0 else jnp.where(lax.rem(step, 5) == 4, 1, 0)

    def beside(self, by_x):
        row, level, column = neighbours()[:3]
        core = place()[2]
        other_row = by_x * (1 - row) + (1 - by_x) * row
        other_column = by_x * column + (1 - by_x) * (1 - column)
        return (other_row, 2 * level + other_column, core)

    def first_copy(self, step, kind):
        out, into = lax.rem(step, 3), lax.rem(step, 6)
        return remote(
            self.send_one.at[out, kind],
            self.recv_one.at[into, kind],
            self.ss_one.at[out, kind],
            self.rs_one.at[into, kind],
            self.beside(self.x_first(step, kind)),
        )

    def second_copy(self, step, kind):
        out, into = lax.rem(step, 3), lax.rem(step, 6)
        return remote(
            self.send_two.at[out, kind],
            self.recv_two.at[into, kind],
            self.ss_two.at[out, kind],
            self.rs_two.at[into, kind],
            self.beside(1 - self.x_first(step, kind)),
        )

    def third_copy(self, step, kind, k):
        row, level, column, beside_x, beside_y, along_z = neighbours()
        target = lax.rem(level + k + 1, 4)
        out, into = lax.rem(step, 4), lax.rem(step, 4)
        return remote(
            self.kept.at[out, kind, pl.ds(pl.multiple_of(target * self.share, 16), self.share)],
            self.recv_three.at[into, kind, k],
            self.ss_three.at[out, kind, k],
            self.rs_three.at[into, kind, k],
            along_z[k],
        )

    def pieces(self, step, act):
        act(0)

        @pl.when(step < self.n - 1)
        def _():
            act(1)

    def first(self, step):
        row, level, column = neighbours()[:3]
        slot = lax.rem(step, 3)

        def act(kind):
            by_x = self.x_first(step, kind)
            for half in range(2):
                x = by_x * (1 - row) + (1 - by_x) * half
                y = by_x * half + (1 - by_x) * (1 - column)
                self.send_one[slot, kind, half] = self.product(step, kind, x, y).astype(
                    jnp.bfloat16
                )
            self.first_copy(step, kind).start()

        self.pieces(step, act)

    def second(self, step):
        row, level, column = neighbours()[:3]
        slot, came, keep = lax.rem(step, 3), lax.rem(step, 6), lax.rem(step, 4)
        self.pieces(step, lambda kind: self.first_copy(step, kind).wait())

        def act(kind):
            by_x = self.x_first(step, kind)
            x = by_x * row + (1 - by_x) * (1 - row)
            y = by_x * (1 - column) + (1 - by_x) * column
            arrived = self.recv_one.at[came, kind]
            mine = by_x * column + (1 - by_x) * row
            away = self.product(step, kind, x, y) + arrived[1 - mine].astype(jnp.float32)
            self.send_two[slot, kind] = away.astype(jnp.bfloat16)
            here = self.product(step, kind, row, column) + arrived[mine].astype(jnp.float32)
            self.kept[keep, kind] = here.astype(jnp.bfloat16)

        self.pieces(step, act)
        self.pieces(step, lambda kind: self.second_copy(step, kind).start())

    def third(self, step):
        came, keep = lax.rem(step, 6), lax.rem(step, 4)

        def act(kind):
            self.second_copy(step, kind).wait()
            here = self.kept[keep, kind].astype(jnp.float32) + self.recv_two[came, kind].astype(
                jnp.float32
            )
            self.kept[keep, kind] = here.astype(jnp.bfloat16)
            for k in range(3):
                self.third_copy(step, kind, k).start()

        self.pieces(step, act)

    def last(self, step):
        level = neighbours()[1]
        came, keep = lax.rem(step, 4), lax.rem(step, 4)
        mine = pl.ds(pl.multiple_of(level * self.share, 16), self.share)

        @pl.when(step >= 2)
        def _():
            self.each_save(step - 2, lambda copy: copy.wait())

        def act(kind):
            total = self.kept[keep, kind, mine].astype(jnp.float32)
            for k in range(3):
                self.third_copy(step, kind, k).wait()
                total = total + self.recv_three[came, kind, k].astype(jnp.float32)
            self.own[lax.rem(step, 2), :, kind * PIECE : (kind + 1) * PIECE] = total

        self.pieces(step, act)
        self.each_save(step, lambda copy: copy.start())

    def turn(self, step):
        for stage, lag in (
            (self.first, 0),
            (self.second, SECOND),
            (self.third, THIRD),
            (self.last, LAST),
        ):

            @pl.when(jnp.logical_and(step >= lag, step < self.n + lag))
            def _():
                stage(step - lag)


def backward_kernel(
    order,
    ids,
    q_in,
    k_in,
    v_in,
    mixed_t_in,
    lse_in,
    cotangent,
    left_in,
    normed_in,
    right_in,
    mixed_low,
    middle,
    near,
    far,
    tokens,
    gains_in,
    tables,
    input_grad,
    layer_out,
    gate_grad,
    up_grad,
    down_grad,
    query_grad,
    key_grad,
    value_grad,
    out_grad,
    gain_out,
    q,
    q_t,
    k,
    k_t,
    v,
    d_own,
    d_slots,
    d,
    d_t,
    dq_t,
    lse,
    delta,
    dk,
    dv,
    dq_slots,
    dkv_sorted,
    dkv_slots,
    dkv_other,
    dq_own,
    dkv_own,
    weight,
    middle_ring,
    input_ring,
    part,
    part_other,
    total,
    staged,
    grad_mid,
    gain_two_grad,
    left_t,
    right,
    gain_columns,
    gain_messages,
    gain_all,
    own,
    send_one,
    recv_one,
    send_two,
    recv_two,
    kept,
    recv_three,
    loads,
    load_first,
    send_gain,
    recv_gain,
    load_left_sem,
    load_w,
    load_ring,
    save_rows,
    save_sem,
    send_d,
    recv_d,
    send_q,
    recv_q,
    send_x,
    recv_x,
    send_k,
    recv_k,
    send_p,
    recv_p,
    save,
    *sems,
):
    row, spot, core = place()
    low, full = jnp.bfloat16, jnp.float32
    rows, width = staged.shape
    length = 8 * rows
    runs, tiles = length // RUN, length // TILE
    per_device = rows // RUN
    halves = TILE // RUN
    share = width // 16
    quarter = 4 * share
    sibling = (row, spot, 1 - core)
    qkv_width = 16 * HEAD
    out_width = mixed_low.shape[1]
    near_at = right_in.shape[1] // (2 * PIECE)
    n = near_at + (qkv_width + out_width + PIECE) // (2 * PIECE)
    grads = (gate_grad, up_grad, down_grad, query_grad, key_grad, value_grad, out_grad)
    changes = (near_at, near_at + qkv_width // (2 * PIECE))
    sums = Reduce(
        n,
        changes,
        (left_t, right, own, grads, save)
        + (send_one, recv_one, send_two, recv_two, kept, recv_three)
        + sems,
    )

    def stage(source):
        return pltpu.make_async_copy(source, staged, load_left_sem)

    early_loads = [
        pltpu.make_async_copy(source, target, loads.at[index])
        for index, (source, target) in enumerate(
            [
                (q_in, q_t),
                (k_in, k),
                (v_in, d_t),
                (mixed_t_in, dq_t),
                (lse_in, lse),
                (middle, total),
            ]
        )
    ]

    first_loads = [
        pltpu.make_async_copy(left_in, left_t.at[pl.ds(0, 2)], load_first.at[4])
    ] + [
        pltpu.make_async_copy(
            right_in.at[:, pl.ds(3 * FEED * piece, 3 * FEED)],
            right.at[:, pl.ds(3 * FEED * piece, 3 * FEED)],
            load_first.at[piece],
        )
        for piece in range(4)
    ]


    def load_block(index, piece, part_of, start):
        lanes = pl.ds(3 * FEED * piece + start + part_of * PIECE, PIECE)
        levels = pl.ds(2 * lax.rem(index, 2), 2)
        return pltpu.make_async_copy(
            far.at[index // 2, levels, :, :, lanes], held_block(piece, part_of), load_w.at[piece]
        )

    def held_block(piece, part_of):
        levels = pl.ds(2 * (part_of % 2), 2)
        return weight.at[piece, part_of // 2, levels, :, :, pl.ds(0, PIECE)]

    def load_blocks(index, piece, start, parts):
        for part_of in range(parts):
            load_block(index, piece, part_of, start).start()

    def row_products(start, parts, landing):
        def block(index, carry):
            term = jnp.zeros((rows, quarter), full)
            for piece in range(4):
                for part_of in range(parts):
                    load_block(index, piece, part_of, start).wait()
                for part_of in range(parts):
                    at = 3 * FEED * piece + start + part_of * PIECE
                    term = term + contract_cols(
                        right[:, at : at + PIECE],
                        held_block(piece, part_of)[...].reshape(quarter, PIECE),
                    )

                @pl.when(index + 1 < 4)
                def _():
                    load_blocks(index + 1, piece, start, parts)

            part[:, tile_at(index, quarter)] = term.astype(low)
            pair_copy(index, landing).start()
            return carry

        lax.fori_loop(0, 4, block, 0)

    def pair_copy(index, landing):
        cut = pl.ds(pl.multiple_of(index * quarter, quarter), quarter)
        return remote(
            part.at[:, cut],
            part_other.at[landing, :, cut],
            send_p.at[index],
            recv_p.at[landing, index],
            sibling,
        )

    def second_back():
        row_products(0, 4, 0)
        for index in range(2):
            load_out_weight(index).start()

    def load_out_weight(index):
        lanes = pl.ds(qkv_width + index * 4 * HEAD, 4 * HEAD)
        return pltpu.make_async_copy(
            near.at[:, :, :, :, lanes], weight.at[index], load_w.at[index]
        )

    d_copies = []
    for step in range(4):
        slot = lax.rem(spot + step, 4)
        chip = 4 * core + slot
        for other in range(2):
            parts = (
                d_own.at[2 * slot + other],
                d_slots.at[spot],
                send_d.at[step, other],
                recv_d.at[spot],
                (row, chip, other),
            )
            d_copies.append((parts, jnp.logical_and(chip == spot, core == other)))

    def middle_back():
        for index in range(4):
            pair_copy(index, 0).wait()
        early_loads[5].wait()
        stage(cotangent).wait()
        chunk = rows // 8

        def block(index, gain_grad):
            cut = tile_at(index, chunk)
            grad = part[cut].astype(full) + part_other[0, cut].astype(full)
            values = total[cut]
            inverse = lax.rsqrt(jnp.mean(values * values, axis=-1, keepdims=True) + epsilon)
            unit = values * inverse
            scaled = grad * gains_in[1:2]
            mean = jnp.mean(scaled * unit, axis=-1, keepdims=True)
            result = staged[cut].astype(full) + inverse * (scaled - unit * mean)
            total[cut] = result
            grad_mid[cut] = result.astype(low)
            return gain_grad + jnp.sum(grad * unit, axis=0, keepdims=True)

        gain_two_grad[...] = lax.fori_loop(0, 8, block, jnp.zeros((1, width), full))
        for index in range(2):
            load_out_weight(index).wait()
            grad = dot_f32(grad_mid[...], weight[index].reshape(width, 4 * HEAD)).T.astype(low)
            for head in range(4):
                for run in range(per_device):
                    d_own[4 * index + head, run] = grad[
                        head * HEAD : (head + 1) * HEAD, run * RUN : (run + 1) * RUN
                    ]
        for parts, is_self in d_copies:
            move(*parts, is_self)


    def prepare():
        for copy in early_loads[:5]:
            copy.wait()
        for index in range(tiles):
            cut = pl.ds(index * TILE, TILE)
            q[cut] = q_t[:, cut].T
            k_t[:, cut] = k[halves * index : halves * (index + 1)].reshape(TILE, HEAD).T
            v[cut] = d_t[:, cut].T

    def take_cotangents():
        for index in range(8):
            remote(
                d_slots.at[index], d_slots.at[index], send_d.at[0, 0], recv_d.at[index], sibling
            ).wait_recv()

        def sort_run(index, carry):
            cols = tile_at(index, RUN)
            run = d_slots[order[index, 0], order[index, 1]]
            d_t[:, cols] = run
            d[cols] = run.T
            delta[:, cols] = jnp.sum(run.astype(full) * dq_t[:, cols], axis=0, keepdims=True)
            return carry

        lax.fori_loop(0, runs, sort_run, 0)
        dq_t[...] = jnp.zeros_like(dq_t)

    scale = HEAD ** (-0.5)

    def key_tile(block):
        cut = tile_at(block, TILE)
        both = pl.ds(block * halves, halves)
        keys, values = k[both].reshape(TILE, HEAD), v[cut]
        keys_t = k_t[:, cut]
        dk[...] = jnp.zeros_like(dk)
        dv[...] = jnp.zeros_like(dv)

        def query_tile(index, diagonal):
            cols = tile_at(index, TILE)
            scores = dot_f32(keys, q_t[:, cols]) * (scale * LOG2_E)
            if diagonal:
                scores = causal(scores)
            probs = jnp.exp2(scores - lse[:, cols])
            dv[...] += dot_f32(probs.astype(low), d[cols])
            grad_probs = dot_f32(values, d_t[:, cols])
            grad_scores = (probs * (grad_probs - delta[:, cols])).astype(low)
            dk[...] += dot_f32(grad_scores, q[cols])
            dq_t[:, cols] += dot_f32(keys_t, grad_scores)

        query_tile(block, True)

        def later(index, inner):
            query_tile(index, False)
            return inner

        lax.fori_loop(block + 1, tiles, later, 0)
        for kind, value in enumerate(((dk[...] * scale).T.astype(low), dv[...].T.astype(low))):
            for half in range(halves):
                dkv_sorted[block * halves + half, kind] = value[:, half * RUN : (half + 1) * RUN]

    def key_tiles(start, stop):
        def one(block, carry):
            key_tile(block)
            return carry

        lax.fori_loop(start, stop, one, 0)

    swap = remote(dkv_slots.at[:, :, 1 - core], dkv_other, send_x, recv_x, sibling)
    dq_copies = return_copies(dq_slots, dq_own, send_q, recv_q)
    slot, owner = lax.rem(spot, 4), spot // 4
    dkv_copies = []
    for step in range(8):
        chip = lax.rem(spot + step, 8)
        parts = (
            dkv_slots.at[:, chip, core],
            dkv_own.at[slot, :, core],
            send_k.at[step],
            recv_k.at[slot, core],
            (row, chip, owner),
        )
        dkv_copies.append((parts, (owner == core) if step == 0 else False))

    def send_back():
        def unsort_run(run, carry):
            index = ids[run]
            for kind in range(2):
                dkv_slots[kind, run // per_device, run % per_device] = dkv_sorted[index, kind]
            return carry

        lax.fori_loop(0, runs, unsort_run, 0)
        swap.start()

        def turn_run(index, carry):
            value = dq_t[:, tile_at(index, RUN)] * scale
            d_slots[index // per_device, index % per_device] = value.astype(low)
            return carry

        lax.fori_loop(0, runs, turn_run, 0)

        def unsort_queries(run, carry):
            value = d_slots[order[runs + run, 0], order[runs + run, 1]]
            dq_slots[run // per_device, run % per_device] = value
            return carry

        lax.fori_loop(0, runs, unsort_queries, 0)
        start_return(dq_copies)

    def add_pairs():
        swap.wait()
        for chip in range(8):
            both = dkv_slots[:, chip, core].astype(full) + dkv_other[:, chip].astype(full)
            dkv_slots[:, chip, core] = both.astype(low)
        start_return(dkv_copies)


    def feed_forward():
        row_products(2 * FEED, 2, 1)
        for group in range(4):
            load_group(group).start()

    save_layer = pltpu.make_async_copy(part, layer_out, save_sem)

    def finish_layer():
        for index in range(4):
            pair_copy(index, 1).wait()
        pieces = width // PIECE

        def load_piece(index):
            lanes = pl.ds(index * PIECE, PIECE)
            return pltpu.make_async_copy(
                middle.at[:, lanes], middle_ring.at[index % 2], load_ring.at[index % 2]
            )

        load_piece(0).start()
        for index in range(pieces):
            if index + 1 < pieces:
                load_piece(index + 1).start()
            load_piece(index).wait()
            cut = pl.ds(index * PIECE, PIECE)
            value = part[:, cut].astype(full) + part_other[1, :, cut].astype(full)
            part[:, cut] = (value + middle_ring[index % 2]).astype(low)
        save_layer.start()


    def load_group(group):
        lanes = pl.ds(group * 4 * HEAD, 4 * HEAD)
        return pltpu.make_async_copy(
            near.at[:, :, :, :, lanes], weight.at[group], load_w.at[group]
        )

    load_mixed = pltpu.make_async_copy(
        mixed_low, right.at[:, pl.ds(qkv_width, out_width)], loads.at[0]
    )

    def project_back():
        load_mixed.start()
        for head in range(8):
            remote(
                dq_own.at[head], dq_own.at[head], send_q.at[0], recv_q.at[head], sibling
            ).wait_recv()
        for slot_in in range(4):
            for core_in in range(2):
                target = dkv_own.at[slot_in, :, core_in]
                remote(
                    target, target, send_k.at[0], recv_k.at[slot_in, core_in], sibling
                ).wait_recv()
        for group in range(4):
            for run in range(per_device):
                cols = slice(run * RUN, (run + 1) * RUN)
                turned = []
                for head in range(4):
                    if group < 2:
                        value = dq_own[4 * group + head, run]
                    else:
                        value = dkv_own[head, group - 2, run]
                    if group < 3:
                        front, back = value[:HALF].astype(full), value[HALF:].astype(full)
                        cos_part, sin_part = tables[0, :, cols], tables[1, :, cols]
                        turned.append((front * cos_part + back * sin_part).astype(low))
                        turned.append((back * cos_part - front * sin_part).astype(low))
                    else:
                        turned.append(value)
                right[cols, group * 4 * HEAD : (group + 1) * 4 * HEAD] = jnp.concatenate(
                    turned, axis=0
                ).T
        load_mixed.wait()

    def project_normed():
        save_layer.wait()
        for group in range(4):
            load_group(group).wait()
        stage(tokens).start()

        def block(index, carry):
            term = jnp.zeros((rows, quarter), full)
            for group in range(4):
                held = weight[group, index // 2, pl.ds(2 * lax.rem(index, 2), 2)]
                term = term + contract_cols(
                    right[:, group * 4 * HEAD : (group + 1) * 4 * HEAD],
                    held.reshape(quarter, 4 * HEAD),
                )
            part[:, tile_at(index, quarter)] = term.astype(low)
            pair_copy(index, 0).start()
            return carry

        lax.fori_loop(0, 4, block, 0)

    def save_input(index):
        cut = tile_at(index, rows // 8)
        slot = lax.rem(index, 2)
        return pltpu.make_async_copy(
            input_ring.at[slot], input_grad.at[cut], save_rows.at[slot]
        )

    def norm_back():
        stage(tokens).wait()
        for index in range(4):
            pair_copy(index, 0).wait()
        chunk = rows // 8

        def block(index, gain_grad):
            cut = tile_at(index, chunk)
            grad = part[cut].astype(full) + part_other[0, cut].astype(full)
            values = staged[cut].astype(full)
            inverse = lax.rsqrt(jnp.mean(values * values, axis=-1, keepdims=True) + epsilon)
            unit = values * inverse
            scaled = grad * gains_in[0:1]
            mean = jnp.mean(scaled * unit, axis=-1, keepdims=True)
            result = total[cut] + inverse * (scaled - unit * mean)

            @pl.when(index >= 2)
            def _():
                save_input(index - 2).wait()

            input_ring[lax.rem(index, 2)] = result.reshape(chunk, 1, width)
            save_input(index).start()
            return gain_grad + jnp.sum(grad * unit, axis=0, keepdims=True)

        gain_one_grad = lax.fori_loop(0, 8, block, jnp.zeros((1, width), full))
        lines = jnp.concatenate(
            [gain_one_grad, gain_two_grad[...], jnp.zeros((6, width), full)], axis=0
        )
        gain_columns[...] = lines.T
        for shard in range(16):
            held = gain_columns[shard * share : (shard + 1) * share]
            gain_messages[shard] = jnp.pad(held, ((0, WIDE - share), (0, 0))).T
        for copy in gain_copies:
            copy.start()
        gain_all[own_shard()] = gain_messages[own_shard()]

    gain_copies, gain_from = exchange_messages(
        lambda shard: gain_messages.at[shard], gain_all, send_gain, recv_gain
    )

    def finish_gains():
        for wait in gain_from:
            wait()
        gain_out[...] = jnp.sum(gain_all[...], axis=0)

    def take_normed():
        stage(normed_in).start()
        stage(normed_in).wait()
        turn_left(left_t, 2, staged)

    def start_forward():
        for piece in range(4):
            load_blocks(0, piece, 2 * FEED, 2)

    for copy in first_loads:
        copy.start()
    stage(cotangent).start()
    for piece in range(4):
        load_blocks(0, piece, 0, 4)
    for copy in early_loads:
        copy.start()
    greet(group_others())
    first_loads[0].wait()
    first_loads[1].wait()

    def wait_right():
        for copy in first_loads[2:]:
            copy.wait()

    plan = {
        2: [wait_right, second_back],
        3: [middle_back],
        4: [prepare],
        5: [start_forward, take_cotangents],
    }
    tiles_from, tile_ranges = 5, ((0, 1), (1, 2), (2, 3), (3, 5), (5, 8))
    later = {
        9: [send_back],
        11: [add_pairs, feed_forward, finish_layer, take_normed],
        12: [project_back],
        15: [lambda: turn_left(left_t, 0, grad_mid), project_normed],
        16: [norm_back],
        n + LAST - 1: [finish_gains],
    }

    def run(step, carry):
        for when, tasks in plan.items():

            @pl.when(step == when)
            def _():
                for task in tasks:
                    task()

        @pl.when(jnp.logical_and(step >= tiles_from, step < tiles_from + len(tile_ranges)))
        def _():
            start, stop = 0, 0
            for index, (first_tile, past_tile) in enumerate(tile_ranges):
                start = jnp.where(step == tiles_from + index, first_tile, start)
                stop = jnp.where(step == tiles_from + index, past_tile, stop)
            key_tiles(start, stop)

        for when, tasks in later.items():

            @pl.when(step == when)
            def _():
                for task in tasks:
                    task()

        sums.turn(step)
        return carry

    lax.fori_loop(0, n + LAST, run, 0)
    for index in (6, 7):
        save_input(index).wait()
    for copy in gain_copies:
        copy.wait_send()
    for step in (n - 2, n - 1):
        sums.each_save(step, lambda copy: copy.wait())
    for copies in (d_copies, dq_copies, dkv_copies):
        for parts, is_self in copies:
            if is_self is False:
                remote(*parts).wait_send()
            else:

                @pl.when(jnp.logical_not(is_self))
                def _():
                    remote(*parts).wait_send()


def backward(order, ids, *arrays):
    dma = pltpu.SemaphoreType.DMA
    vmem = pltpu.VMEM
    low, full = jnp.bfloat16, jnp.float32
    q_sorted, k_sorted, v_sorted, mixed_t, lse, cotangent, left, normed, right = arrays[:9]
    mixed_low, middle, near, far, tokens, gains, tables = arrays[9:]
    rows, width = cotangent.shape
    length = 8 * rows
    share = width // 16
    feed, query, out_width = right.shape[1] // 3, 8 * HEAD, mixed_low.shape[1]
    quarter = 4 * share
    per_device = rows // RUN
    heads = (8, per_device, HEAD, RUN)
    tall, flat = (length, HEAD), (HEAD, length)
    by_run = (length // RUN, RUN, HEAD)
    block = (rows, width)
    smem_spec = pl.BlockSpec(memory_space=pltpu.SMEM)
    shape = jax.ShapeDtypeStruct
    return pl.pallas_call(
        backward_kernel,
        in_specs=[smem_spec] * 2 + [any_spec()] * 14 + [vmem_spec()] * 2,
        out_specs=[any_spec()] * 9 + [vmem_spec()],
        out_shape=[
            shape((rows, 1, width), full),
            shape(block, low),
            *[
                shape((share, wide), full)
                for wide in (feed, feed, feed, query, query // 2, query // 2, out_width)
            ],
            shape((8, WIDE), full),
        ],
        scratch_shapes=[
            vmem(tall, low),
            vmem(flat, low),
            vmem(by_run, low),
            vmem(flat, low),
            vmem(tall, low),
            vmem(heads, low),
            vmem(heads, low),
            vmem(tall, low),
            vmem(flat, low),
            vmem(flat, full),
            vmem((1, length), full),
            vmem((1, length), full),
            vmem((TILE, HEAD), full),
            vmem((TILE, HEAD), full),
            vmem(heads, low),
            vmem((length // RUN, 2, HEAD, RUN), low),
            vmem((2,) + heads, low),
            vmem((2, 8, HEAD, RUN), low),
            vmem(heads, low),
            vmem((4, 2, per_device, HEAD, RUN), low),
            vmem((4, 2, 4, 2, share, 4 * HEAD), low),
            vmem((2, rows, PIECE), full),
            vmem((2, rows // 8, 1, width), full),
            vmem(block, low),
            vmem((2,) + block, low),
            vmem(block, full),
            vmem(block, low),
            vmem(block, low),
            vmem((1, width), full),
            vmem((3, 2, 2, quarter, rows), low),
            vmem(right.shape, low),
            vmem((width, 8), full),
            vmem((16, 8, WIDE), full),
            vmem((16, 8, WIDE), full),
            vmem((2, share, 2 * PIECE), full),
            vmem((3, 2, 2, quarter, PIECE), low),
            vmem((6, 2, 2, quarter, PIECE), low),
            vmem((3, 2, quarter, PIECE), low),
            vmem((6, 2, quarter, PIECE), low),
            vmem((4, 2, quarter, PIECE), low),
            vmem((4, 2, 3, share, PIECE), low),
            dma((7,)),
            dma((5,)),
            dma((16,)),
            dma((16,)),
            dma(()),
            dma((4,)),
            dma((2,)),
            dma((2,)),
            dma(()),
            dma((4, 2)),
            dma((8,)),
            dma((8,)),
            dma((8,)),
            dma(()),
            dma(()),
            dma((8,)),
            dma((4, 2)),
            dma((4,)),
            dma((2, 4)),
            dma((2, 3)),
            dma((3, 2)),
            dma((6, 2)),
            dma((3, 2)),
            dma((6, 2)),
            dma((4, 2, 3)),
            dma((4, 2, 3)),
        ],
        compiler_params=pltpu.CompilerParams(
            collective_id=2, has_side_effects=True, vmem_limit_bytes=62 * 1024 * 1024
        ),
        name="backward",
    )(
        order,
        ids,
        *arrays,
    )


def deliver_kernel(count, *refs):
    arrays, gain_grads = refs[:count], refs[count]
    results, gain_one, gain_two = refs[count + 1 : 2 * count + 1], refs[2 * count + 1], refs[2 * count + 2]
    held, loads, saves = refs[2 * count + 3 : 3 * count + 3], refs[-2], refs[-1]
    into, out = [], []
    for index in range(count):
        rows = arrays[index].shape[0]
        pieces = rows // 128 if rows % 128 == 0 else 1
        for piece in range(pieces):
            cut = pl.ds(piece * (rows // pieces), rows // pieces)
            place = index, piece
            into.append(
                pltpu.make_async_copy(
                    arrays[index].at[cut], held[index].at[cut], loads.at[place]
                )
            )
            out.append(
                pltpu.make_async_copy(
                    held[index].at[cut], results[index].at[cut], saves.at[place]
                )
            )
    for copy in into:
        copy.start()
    share = gain_one.shape[1]
    gain_one[...] = gain_grads[0:1, :share]
    gain_two[...] = gain_grads[1:2, :share]
    for came, goes in zip(into, out):
        came.wait()
        goes.start()
    for goes in out:
        goes.wait()


def deliver(arrays, gain_grads, share):
    count = len(arrays)
    shape = jax.ShapeDtypeStruct
    dma = pltpu.SemaphoreType.DMA
    return pl.pallas_call(
        functools.partial(deliver_kernel, count),
        in_specs=[any_spec()] * count + [vmem_spec()],
        out_specs=[any_spec()] * count + [vmem_spec()] * 2,
        out_shape=[shape(array.shape, array.dtype) for array in arrays]
        + [shape((1, share), jnp.float32)] * 2,
        scratch_shapes=[pltpu.VMEM(array.shape, array.dtype) for array in arrays]
        + [dma((count, 4)), dma((count, 4))],
        compiler_params=pltpu.CompilerParams(vmem_limit_bytes=VMEM_LIMIT),
        name="deliver",
    )(*arrays, gain_grads)


def by_heads(
    tokens,
    positions,
    gain_one,
    gain_two,
    w_query,
    w_key,
    w_value,
    w_out,
    w_gate,
    w_up,
    w_down,
    cotangent,
):
    rows, _, width = tokens.shape
    share = gain_one.shape[0]
    flat_in = tokens.reshape(rows, width)
    (
        near,
        far,
        normed,
        q_sorted,
        k_sorted,
        v_sorted,
        mixed_t,
        lse,
        mixed_low,
        middle,
        second,
        right,
        gains,
        tables,
        left,
        order,
        ids,
    ) = forward(
        flat_in,
        positions.reshape(1, rows),
        gain_one.reshape(1, share),
        gain_two.reshape(1, share),
        w_query,
        w_key,
        w_value,
        w_out.T,
        w_gate,
        w_up,
        w_down.T,
        cotangent.reshape(rows, width),
    )
    input_grad, layer_out, *grads, gain_grads = backward(
        order,
        ids,
        q_sorted,
        k_sorted,
        v_sorted,
        mixed_t,
        lse,
        cotangent.reshape(rows, width),
        left,
        normed,
        right,
        mixed_low,
        middle,
        near,
        far,
        flat_in,
        gains,
        tables,
    )
    input_grad, layer_out, *grads, grad_one, grad_two = deliver(
        [input_grad, layer_out, *grads], gain_grads, share
    )
    grad_gate, grad_up, grad_down, grad_query, grad_key, grad_value, grad_out = grads
    return (
        layer_out.reshape(rows, 1, width),
        input_grad,
        grad_one.reshape(share),
        grad_two.reshape(share),
        grad_query,
        grad_key,
        grad_value,
        grad_out.T,
        grad_gate,
        grad_up,
        grad_down.T,
    )


def solution(mesh):
    sizes = (mesh.shape["dp"], mesh.shape["context"], mesh.shape["tensor"])
    return jax.shard_map(
        by_heads if sizes == (2, 8, 2) else on_device,
        mesh=mesh,
        in_specs=(
            P("context", "dp", None),
            P("context", "dp"),
            P(("dp", "context")),
            P(("dp", "context")),
            P(("dp", "context"), "tensor"),
            P(("dp", "context"), "tensor"),
            P(("dp", "context"), "tensor"),
            P("tensor", ("dp", "context")),
            P(("dp", "context"), "tensor"),
            P(("dp", "context"), "tensor"),
            P("tensor", ("dp", "context")),
            P("context", "dp", None),
        ),
        out_specs=(
            P("context", "dp", None),
            P("context", "dp", None),
            P(("dp", "context")),
            P(("dp", "context")),
            P(("dp", "context"), "tensor"),
            P(("dp", "context"), "tensor"),
            P(("dp", "context"), "tensor"),
            P("tensor", ("dp", "context")),
            P(("dp", "context"), "tensor"),
            P(("dp", "context"), "tensor"),
            P("tensor", ("dp", "context")),
        ),
        check_vma=False,
    )
```

```python
import functools

import jax
import jax.numpy as jnp
import numpy as np
from jax import lax
from jax.experimental import pallas as pl
from jax.experimental.pallas import tpu as pltpu
from jax.sharding import PartitionSpec as P

HEAD = 96


epsilon = 1e-05
theta_base = 100000.0
masked_value = -1e30


def norm_forward(values_in, gain_vec):
    inverse = lax.rsqrt(jnp.mean(values_in * values_in, axis=-1, keepdims=True) + epsilon)
    unit_vals = values_in * inverse
    return (unit_vals, inverse, (unit_vals * gain_vec.astype(jnp.float32)).astype(jnp.bfloat16))


def norm_backward(grad_in, unit_vals, inverse, gain_vec):
    scaled = grad_in * gain_vec.astype(jnp.float32)
    grad_vals = inverse * (
        scaled - unit_vals * jnp.mean(scaled * unit_vals, axis=-1, keepdims=True)
    )
    return (grad_vals, jnp.sum(grad_in * unit_vals, axis=0))


def rotate(values_in, cos_part, sin_part):
    half_size = values_in.shape[-1] // 2
    front_half = values_in[..., :half_size]
    back_half = values_in[..., half_size:]
    return jnp.concatenate(
        [
            front_half * cos_part - back_half * sin_part,
            back_half * cos_part + front_half * sin_part,
        ],
        axis=-1,
    )


def contract_rows(left_mat, right_mat):
    return lax.dot_general(
        left_mat, right_mat, (((0,), (0,)), ((), ())), preferred_element_type=jnp.float32
    )


def contract_cols(left_mat, right_mat):
    return lax.dot_general(
        left_mat, right_mat, (((1,), (1,)), ((), ())), preferred_element_type=jnp.float32
    )


def on_device(
    tokens,
    positions,
    gain_one,
    gain_two,
    w_query,
    w_key,
    w_value,
    w_out,
    w_gate,
    w_up,
    w_down,
    cotangent,
):
    slot_count, seq_count, model_width = tokens.shape
    row_count = slot_count * seq_count
    gathered = (
        lax.all_gather(gain_one, ("dp", "context"), axis=0, tiled=True),
        lax.all_gather(gain_two, ("dp", "context"), axis=0, tiled=True),
        lax.all_gather(w_query, ("dp", "context"), axis=0, tiled=True),
        lax.all_gather(w_key, ("dp", "context"), axis=0, tiled=True),
        lax.all_gather(w_value, ("dp", "context"), axis=0, tiled=True),
        lax.all_gather(w_out, ("dp", "context"), axis=1, tiled=True),
        lax.all_gather(w_gate, ("dp", "context"), axis=0, tiled=True),
        lax.all_gather(w_up, ("dp", "context"), axis=0, tiled=True),
        lax.all_gather(w_down, ("dp", "context"), axis=1, tiled=True),
    )
    full_one, full_two, query_mat, key_mat, value_mat, out_mat, gate_mat, up_mat, down_mat = (
        gathered
    )
    heads_kv = key_mat.shape[1] // HEAD
    heads_q = query_mat.shape[1] // HEAD
    group_size = heads_q // heads_kv
    score_scale = HEAD ** (-0.5)
    half_size = HEAD // 2
    inv_freqs = theta_base ** (-2.0 * jnp.arange(half_size, dtype=jnp.float32) / HEAD)
    angles = positions.astype(jnp.float32)[:, :, None] * inv_freqs
    cos_part = jnp.cos(angles)[:, :, None, :]
    sin_part = jnp.sin(angles)[:, :, None, :]
    flat_in = tokens.astype(jnp.float32).reshape(row_count, model_width)
    unit_one, inverse_one, normed = norm_forward(flat_in, full_one)
    query_proj = jnp.dot(normed, query_mat, preferred_element_type=jnp.float32).reshape(
        slot_count, seq_count, heads_q, HEAD
    )
    key_proj = jnp.dot(normed, key_mat, preferred_element_type=jnp.float32).reshape(
        slot_count, seq_count, heads_kv, HEAD
    )
    value_low = (
        jnp.dot(normed, value_mat, preferred_element_type=jnp.float32)
        .astype(jnp.bfloat16)
        .reshape(slot_count, seq_count, heads_kv * HEAD)
    )
    queries = rotate(query_proj, cos_part, sin_part).astype(jnp.bfloat16)
    keys_low = (
        rotate(key_proj, cos_part, sin_part)
        .astype(jnp.bfloat16)
        .reshape(slot_count, seq_count, heads_kv * HEAD)
    )
    query_seq = jnp.transpose(
        queries.reshape(slot_count, seq_count, heads_kv, group_size, HEAD), (1, 2, 3, 0, 4)
    )
    query_pos = positions.T
    stat_shape = (seq_count, heads_kv, group_size, slot_count)
    initial = (
        jnp.full(stat_shape, masked_value, jnp.float32),
        jnp.zeros(stat_shape, jnp.float32),
        jnp.zeros(stat_shape + (HEAD,), jnp.float32),
    )
    key_piece = lax.all_gather(keys_low, "context", axis=0, tiled=True)
    value_piece = lax.all_gather(value_low, "context", axis=0, tiled=True)
    pos_piece = lax.all_gather(positions, "context", axis=0, tiled=True)
    piece_len = key_piece.shape[0]
    key_seq = jnp.transpose(key_piece.reshape(piece_len, seq_count, heads_kv, HEAD), (1, 2, 0, 3))
    value_seq = jnp.transpose(
        value_piece.reshape(piece_len, seq_count, heads_kv, HEAD), (1, 2, 0, 3)
    )
    pos_seq = pos_piece.T

    def per_sequence(seq_items):
        peak_val, totals, accum_vals, query_one, qpos_one, key_one, value_one, kpos_one = seq_items
        raw_scores = (
            jnp.einsum("hgqd,hkd->hgqk", query_one, key_one, preferred_element_type=jnp.float32)
            * score_scale
        )
        allowed = kpos_one[None, None, None, :] <= qpos_one[None, None, :, None]
        masked = jnp.where(allowed, raw_scores, masked_value)
        new_peak = jnp.maximum(peak_val, jnp.max(masked, axis=-1))
        decay_vals = jnp.exp(peak_val - new_peak)
        weights = jnp.where(allowed, jnp.exp(masked - new_peak[..., None]), 0.0)
        totals = totals * decay_vals + jnp.sum(weights, axis=-1)
        accum_vals = accum_vals * decay_vals[..., None] + jnp.einsum(
            "hgqk,hkd->hgqd",
            weights.astype(jnp.bfloat16),
            value_one,
            preferred_element_type=jnp.float32,
        )
        return (new_peak, totals, accum_vals)

    peak_val, totals, accum_vals = lax.map(
        per_sequence,
        (initial[0], initial[1], initial[2], query_seq, query_pos, key_seq, value_seq, pos_seq),
    )
    log_total = peak_val + jnp.log(totals)
    mixed_seq = accum_vals / totals[..., None]
    mixed_low = (
        jnp.transpose(mixed_seq, (3, 0, 1, 2, 4))
        .reshape(row_count, heads_q * HEAD)
        .astype(jnp.bfloat16)
    )
    branch = lax.psum(
        jnp.dot(mixed_low, out_mat, preferred_element_type=jnp.float32).astype(jnp.bfloat16),
        "tensor",
    ).astype(jnp.float32)
    middle = flat_in + branch
    unit_two, inverse_two, second = norm_forward(middle, full_two)
    gate_vals = jnp.dot(second, gate_mat, preferred_element_type=jnp.float32)
    up_vals = jnp.dot(second, up_mat, preferred_element_type=jnp.float32)
    sigmoid_vals = jax.nn.sigmoid(gate_vals)
    silu_vals = gate_vals * sigmoid_vals
    hidden = (silu_vals * up_vals).astype(jnp.bfloat16)
    mlp_part = lax.psum(
        jnp.dot(hidden, down_mat, preferred_element_type=jnp.float32).astype(jnp.bfloat16), "tensor"
    ).astype(jnp.float32)
    layer_out = (middle + mlp_part).astype(jnp.bfloat16).reshape(slot_count, seq_count, model_width)
    regathered = (
        lax.all_gather(gain_one, ("dp", "context"), axis=0, tiled=True),
        lax.all_gather(gain_two, ("dp", "context"), axis=0, tiled=True),
        lax.all_gather(w_query, ("dp", "context"), axis=0, tiled=True),
        lax.all_gather(w_key, ("dp", "context"), axis=0, tiled=True),
        lax.all_gather(w_value, ("dp", "context"), axis=0, tiled=True),
        lax.all_gather(w_out, ("dp", "context"), axis=1, tiled=True),
        lax.all_gather(w_gate, ("dp", "context"), axis=0, tiled=True),
        lax.all_gather(w_up, ("dp", "context"), axis=0, tiled=True),
        lax.all_gather(w_down, ("dp", "context"), axis=1, tiled=True),
    )
    full_one, full_two, query_mat, key_mat, value_mat, out_mat, gate_mat, up_mat, down_mat = (
        regathered
    )
    grad_low = cotangent.reshape(row_count, model_width)
    grad_down = contract_rows(hidden, grad_low)
    grad_hidden = contract_cols(grad_low, down_mat)
    grad_gate_low = (
        grad_hidden * up_vals * sigmoid_vals * (1.0 + gate_vals * (1.0 - sigmoid_vals))
    ).astype(jnp.bfloat16)
    grad_up_low = (grad_hidden * silu_vals).astype(jnp.bfloat16)
    grad_gate = contract_rows(second, grad_gate_low)
    grad_up = contract_rows(second, grad_up_low)
    grad_second = lax.psum(
        (contract_cols(grad_gate_low, gate_mat) + contract_cols(grad_up_low, up_mat)).astype(
            jnp.bfloat16
        ),
        "tensor",
    ).astype(jnp.float32)
    grad_mid_norm, grad_gain_two = norm_backward(grad_second, unit_two, inverse_two, full_two)
    grad_middle = grad_low.astype(jnp.float32) + grad_mid_norm
    grad_mid_low = grad_middle.astype(jnp.bfloat16)
    grad_out = contract_rows(mixed_low, grad_mid_low)
    grad_mixed = contract_cols(grad_mid_low, out_mat).astype(jnp.bfloat16)
    grad_mixed_seq = jnp.transpose(
        grad_mixed.reshape(slot_count, seq_count, heads_kv, group_size, HEAD), (1, 2, 3, 0, 4)
    )
    delta_rows = jnp.sum(grad_mixed_seq.astype(jnp.float32) * mixed_seq, axis=-1)
    kv_width = heads_kv * HEAD

    def block_grads(grad_query_acc, key_blk, value_blk, pos_blk):
        block_len = key_blk.shape[0]
        key_seq = jnp.transpose(key_blk.reshape(block_len, seq_count, heads_kv, HEAD), (1, 2, 0, 3))
        value_seq = jnp.transpose(
            value_blk.reshape(block_len, seq_count, heads_kv, HEAD), (1, 2, 0, 3)
        )
        raw_scores = (
            jnp.einsum("shgqd,shkd->shgqk", query_seq, key_seq, preferred_element_type=jnp.float32)
            * score_scale
        )
        allowed = pos_blk.T[:, None, None, None, :] <= query_pos[:, None, None, :, None]
        prob_vals = jnp.where(
            allowed,
            jnp.exp(jnp.where(allowed, raw_scores - log_total[..., None], masked_value)),
            0.0,
        )
        grad_value_blk = jnp.einsum(
            "shgqk,shgqd->kshd",
            prob_vals.astype(jnp.bfloat16),
            grad_mixed_seq,
            preferred_element_type=jnp.float32,
        )
        grad_probs = jnp.einsum(
            "shgqd,shkd->shgqk", grad_mixed_seq, value_seq, preferred_element_type=jnp.float32
        )
        grad_scores = (prob_vals * (grad_probs - delta_rows[..., None])).astype(jnp.bfloat16)
        grad_query_acc = grad_query_acc + jnp.einsum(
            "shgqk,shkd->shgqd", grad_scores, key_seq, preferred_element_type=jnp.float32
        )
        grad_key_blk = jnp.einsum(
            "shgqk,shgqd->kshd", grad_scores, query_seq, preferred_element_type=jnp.float32
        )
        return (
            grad_query_acc,
            grad_key_blk.reshape(block_len, seq_count, kv_width),
            grad_value_blk.reshape(block_len, seq_count, kv_width),
        )

    zero_query = jnp.zeros(stat_shape + (HEAD,), jnp.float32)
    key_all, value_all, pos_all = (
        lax.all_gather(keys_low, "context", axis=0, tiled=True),
        lax.all_gather(value_low, "context", axis=0, tiled=True),
        lax.all_gather(positions, "context", axis=0, tiled=True),
    )
    total_len = key_all.shape[0]
    block_size = min(512, total_len)
    block_count = total_len // block_size

    def key_block(grad_query_acc, block_items):
        key_blk, value_blk, pos_blk = block_items
        grad_query_acc, grad_key_blk, grad_value_blk = block_grads(
            grad_query_acc, key_blk, value_blk, pos_blk
        )
        return (grad_query_acc, (grad_key_blk, grad_value_blk))

    grad_query_acc, (grad_keys_all, grad_values_all) = lax.scan(
        key_block,
        zero_query,
        (
            key_all.reshape(block_count, block_size, seq_count, kv_width),
            value_all.reshape(block_count, block_size, seq_count, kv_width),
            pos_all.reshape(block_count, block_size, seq_count),
        ),
    )
    grad_key_own, grad_value_own = (
        lax.psum_scatter(
            grad_keys_all.reshape(total_len, seq_count, kv_width).astype(jnp.bfloat16),
            "context",
            scatter_dimension=0,
            tiled=True,
        ).astype(jnp.float32),
        lax.psum_scatter(
            grad_values_all.reshape(total_len, seq_count, kv_width).astype(jnp.bfloat16),
            "context",
            scatter_dimension=0,
            tiled=True,
        ).astype(jnp.float32),
    )
    grad_rot_q = jnp.transpose(grad_query_acc * score_scale, (3, 0, 1, 2, 4)).reshape(
        slot_count, seq_count, heads_q, HEAD
    )
    grad_q_low = (
        rotate(grad_rot_q, cos_part, -sin_part)
        .reshape(row_count, heads_q * HEAD)
        .astype(jnp.bfloat16)
    )
    grad_rot_k = (grad_key_own * score_scale).reshape(slot_count, seq_count, heads_kv, HEAD)
    grad_k_low = (
        rotate(grad_rot_k, cos_part, -sin_part).reshape(row_count, kv_width).astype(jnp.bfloat16)
    )
    grad_v_low = grad_value_own.reshape(row_count, kv_width).astype(jnp.bfloat16)
    grad_query = contract_rows(normed, grad_q_low)
    grad_key = contract_rows(normed, grad_k_low)
    grad_value = contract_rows(normed, grad_v_low)
    grad_normed = lax.psum(
        (
            contract_cols(grad_q_low, query_mat)
            + contract_cols(grad_k_low, key_mat)
            + contract_cols(grad_v_low, value_mat)
        ).astype(jnp.bfloat16),
        "tensor",
    ).astype(jnp.float32)
    grad_in_norm, grad_gain_one = norm_backward(grad_normed, unit_one, inverse_one, full_one)
    input_grad = (grad_middle + grad_in_norm).reshape(slot_count, seq_count, model_width)
    reduced = (
        lax.psum_scatter(grad_gain_one, ("dp", "context"), scatter_dimension=0, tiled=True),
        lax.psum_scatter(grad_gain_two, ("dp", "context"), scatter_dimension=0, tiled=True),
        lax.psum_scatter(grad_query, ("dp", "context"), scatter_dimension=0, tiled=True),
        lax.psum_scatter(grad_key, ("dp", "context"), scatter_dimension=0, tiled=True),
        lax.psum_scatter(grad_value, ("dp", "context"), scatter_dimension=0, tiled=True),
        lax.psum_scatter(grad_out, ("dp", "context"), scatter_dimension=1, tiled=True),
        lax.psum_scatter(grad_gate, ("dp", "context"), scatter_dimension=0, tiled=True),
        lax.psum_scatter(grad_up, ("dp", "context"), scatter_dimension=0, tiled=True),
        lax.psum_scatter(grad_down, ("dp", "context"), scatter_dimension=1, tiled=True),
    )
    return (
        layer_out,
        input_grad,
        reduced[0],
        reduced[1],
        reduced[2],
        reduced[3],
        reduced[4],
        reduced[5],
        reduced[6],
        reduced[7],
        reduced[8],
    )


WIDE = 128
HALF = HEAD // 2
RUN = 256
TILE = 512
LOG2_E = 1.4426950408889634
MESH = pl.DeviceIdType.MESH
PIECE = 256
FEED = 512
VMEM_LIMIT = 56 * 1024 * 1024


def any_spec():
    return pl.BlockSpec(memory_space=pl.ANY)


def vmem_spec():
    return pl.BlockSpec(memory_space=pltpu.VMEM)


def place():
    return lax.axis_index("dp"), lax.axis_index("context"), lax.axis_index("tensor")


def greet(devices):
    barrier = pltpu.get_barrier_semaphore()
    for device in devices:
        pl.semaphore_signal(barrier, inc=1, device_id=device, device_id_type=MESH)
    pl.semaphore_wait(barrier, len(devices))


def sequence_others():
    row, spot, core = place()
    return [
        (row, lax.rem(spot + shift, 8), lax.rem(core + flip, 2))
        for shift in range(8)
        for flip in range(2)
        if shift or flip
    ]


def lane_freqs():
    return jnp.asarray(
        np.power(np.float32(theta_base), np.float32(-2.0) * np.arange(HALF, dtype=np.float32) / HEAD)
    ).reshape(HALF, 1)


def dot_f32(left, right):
    return jnp.dot(left, right, preferred_element_type=jnp.float32)


def own_shard():
    row, spot, core = place()
    return row * 8 + spot


def group_others():
    row, spot, core = place()
    return sequence_others() + [(1 - row, lax.rem(spot + shift, 8), core) for shift in range(8)]


def exchange_messages(message_to, landing, send, recv):
    row, spot, core = place()
    copies, waits = [], []

    def one(flip, shift):
        at = flip * 8 + shift
        to_row = lax.rem(row + flip, 2)
        chip, source = lax.rem(spot + shift, 8), lax.rem(spot + 8 - shift, 8)
        device = (to_row, chip, core)
        message = message_to(to_row * 8 + chip)
        copies.append(
            remote(message, landing.at[row * 8 + spot], send.at[at], recv.at[at], device)
        )
        came = landing.at[to_row * 8 + source]
        waits.append(remote(came, came, send.at[at], recv.at[at], device).wait_recv)

    for flip in range(2):
        for shift in range(8):
            if flip or shift:
                one(flip, shift)
    return copies, waits


def turn_left(left_t, index, source):
    quarter = source.shape[1] // 4
    share = quarter // 4
    for piece in range(4):
        turned = source[:, piece * quarter : (piece + 1) * quarter].T
        for inner in range(4):
            x, z, y = piece // 2, 2 * (piece % 2) + inner // 2, inner % 2
            left_t[index, x, y, z * share : (z + 1) * share] = turned[
                inner * share : (inner + 1) * share
            ]


def remote(source, target, send, recv, device):
    return pltpu.make_async_remote_copy(
        src_ref=source,
        dst_ref=target,
        send_sem=send,
        recv_sem=recv,
        device_id=device,
        device_id_type=MESH,
    )


def move(source, target, send, recv, device, is_self):
    @pl.when(is_self)
    def _():
        pltpu.make_async_copy(source, target, recv).start()

    @pl.when(jnp.logical_not(is_self))
    def _():
        remote(source, target, send, recv, device).start()


def return_copies(ref, out, send, recv):
    row, spot, core = place()
    head = 2 * lax.rem(spot, 4) + core
    owner = spot // 4
    copies = []
    for step in range(8):
        chip = lax.rem(spot + step, 8)
        is_self = (owner == core) if step == 0 else False
        parts = (ref.at[chip], out.at[head], send.at[step], recv.at[head], (row, chip, owner))
        copies.append((parts, is_self))
    return copies


def start_return(copies):
    for parts, is_self in copies:
        if is_self is False:
            remote(*parts).start()
        else:
            move(*parts, is_self)


def finish_return(copies, out, send, recv):
    row, spot, core = place()
    for head in range(8):
        remote(
            out.at[head], out.at[head], send.at[0], recv.at[head], (row, spot, 1 - core)
        ).wait_recv()
    for parts, is_self in copies:
        if is_self is False:
            remote(*parts).wait_send()
        else:

            @pl.when(jnp.logical_not(is_self))
            def _():
                remote(*parts).wait_send()


def tile_at(index, size):
    return pl.ds(pl.multiple_of(index * size, size), size)


def causal(scores):
    keys = lax.broadcasted_iota(jnp.int32, scores.shape, 0)
    queries = lax.broadcasted_iota(jnp.int32, scores.shape, 1)
    return jnp.where(keys <= queries, scores, masked_value)


def neighbours():
    row, spot, core = place()
    level, column = spot // 2, lax.rem(spot, 2)
    beside_x = (1 - row, spot, core)
    beside_y = (row, 2 * level + 1 - column, core)
    along_z = [(row, 2 * lax.rem(level + k, 4) + column, core) for k in (1, 2, 3)]
    return row, level, column, beside_x, beside_y, along_z


class Gather:
    def __init__(self, own, whole, start, width, piece, sems):
        self.own, self.whole = own.at[:, pl.ds(start, width)], whole
        self.start, self.width = start, width
        names = ("send_z", "recv_z", "send_x", "recv_x", "send_y", "recv_y", "send_d", "recv_d")
        for name, sem in zip(names + ("local",), sems):
            setattr(self, name, sem.at[piece])

    def block(self, x, z, y, half=None):
        cut = self.width * 7 // 12 // WIDE * WIDE
        start, width = self.start, self.width
        if half == 0:
            width = cut
        elif half == 1:
            start, width = start + cut, width - cut
        return self.whole.at[x, z, y, :, pl.ds(start, width)]

    def arrived(self, target, recv_sem):
        device = neighbours()[3]
        remote(target, target, self.send_x.at[0], recv_sem, device).wait_recv()

    def copy_z(self, z, up, own=False):
        row, level, column, beside_x, beside_y = neighbours()[:5]
        core = place()[2]
        target = level + 1 if up else level - 1
        block = self.block(row, z, column)
        return remote(
            self.own if own else block,
            block,
            self.send_z.at[int(up), z],
            self.recv_z.at[z],
            (row, 2 * target + column, core),
        )

    def copies_xy(self, z, own=False):
        row, level, column, beside_x, beside_y = neighbours()[:5]
        block = self.block(row, z, column)
        source = self.own if own else block
        return [
            remote(source, block, self.send_x.at[z], self.recv_x.at[z], beside_x),
            remote(source, block, self.send_y.at[z], self.recv_y.at[z], beside_y),
        ]

    def copies_diagonal(self, z):
        row, level, column, beside_x, beside_y = neighbours()[:5]
        by_y = self.block(1 - row, z, column, 1)
        by_x = self.block(row, z, 1 - column, 0)
        return [
            remote(by_y, by_y, self.send_d.at[0, z], self.recv_d.at[0, z], beside_y),
            remote(by_x, by_x, self.send_d.at[1, z], self.recv_d.at[1, z], beside_x),
        ]

    def own_copy(self):
        row, level, column = neighbours()[:3]
        return pltpu.make_async_copy(self.own, self.block(row, level, column), self.local)

    def each_at(self, hop, act):
        level = neighbours()[1]

        @pl.when(level >= hop)
        def _():
            act(level - hop, True)

        @pl.when(level + hop <= 3)
        def _():
            act(level + hop, False)

    def start_z(self, z, up, own=False):
        level = neighbours()[1]

        @pl.when(level < 3 if up else level > 0)
        def _():
            self.copy_z(z, up, own).start()

    def place_own(self):
        self.own_copy().start()

    def open(self):
        level = neighbours()[1]
        self.start_z(level, True, True)
        self.start_z(level, False, True)
        for copy in self.copies_xy(level, True):
            copy.start()

    def hop(self, hop):
        def act(z, up):
            row, level, column = neighbours()[:3]
            self.arrived(self.block(row, z, column), self.recv_z.at[z])
            self.start_z(z, up)
            for copy in self.copies_xy(z):
                copy.start()

        self.each_at(hop, act)

    def turn_diagonal(self, z):
        row, level, column = neighbours()[:3]
        by_y, by_x = self.copies_diagonal(z)
        self.arrived(self.block(1 - row, z, column), self.recv_x.at[z])
        by_y.start()
        self.arrived(self.block(row, z, 1 - column), self.recv_y.at[z])
        by_x.start()

    def diagonal(self, hop):
        if hop == 0:
            self.turn_diagonal(neighbours()[1])
        else:
            self.each_at(hop, lambda z, up: self.turn_diagonal(z))

    def finish(self):
        row, level, column = neighbours()[:3]
        self.own_copy().wait()
        for z in range(4):
            self.arrived(self.block(1 - row, z, 1 - column, 1), self.recv_d.at[0, z])
            self.arrived(self.block(1 - row, z, 1 - column, 0), self.recv_d.at[1, z])

    def close_z(self):
        level = neighbours()[1]

        def sent(z, up):
            @pl.when(level < 3 if up else level > 0)
            def _():
                self.copy_z(z, up).wait_send()

        sent(level, True)
        sent(level, False)
        for hop in range(1, 4):
            self.each_at(hop, sent)

    def close(self):
        self.close_z()
        for z in range(4):
            for copy in self.copies_xy(z) + self.copies_diagonal(z):
                copy.wait_send()


class PlaneGather(Gather):
    def plane(self, z):
        return self.whole.at[:, z, :, :, pl.ds(self.start, self.width)]

    def copy_z(self, z, up, own=False):
        row, level, column = neighbours()[:3]
        target = level + 1 if up else level - 1
        plane = self.plane(z)
        return remote(
            plane,
            plane,
            self.send_z.at[int(up), z],
            self.recv_z.at[z],
            (row, 2 * target + column, place()[2]),
        )

    def open(self):
        for copy in self.copies_xy(neighbours()[1], True):
            copy.start()

    def spread(self):
        row, level, column = neighbours()[:3]
        self.arrived(self.block(1 - row, level, 1 - column, 1), self.recv_d.at[0, level])
        self.arrived(self.block(1 - row, level, 1 - column, 0), self.recv_d.at[1, level])
        self.own_copy().wait()
        self.start_z(level, True)
        self.start_z(level, False)

    def hop(self, hop):
        def act(z, up):
            self.arrived(self.plane(z), self.recv_z.at[z])
            self.start_z(z, up)

        self.each_at(hop, act)

    def finish(self):
        pass

    def close(self):
        level = neighbours()[1]
        self.close_z()
        for copy in self.copies_xy(level) + self.copies_diagonal(level):
            copy.wait_send()


def gather_sems(pieces):
    dma = pltpu.SemaphoreType.DMA
    shapes = [(2, 4), (4,), (4,), (4,), (4,), (4,), (2, 4), (2, 4), ()]
    return [dma((pieces,) + shape) for shape in shapes]


AT_BEGIN, AT_GAINS, AT_PAIRS, AT_QUERIES, AT_HEADS, AT_KEYS, AT_ALL, AT_SORT = 0, 1, 2, 3, 4, 5, 6, 7
AT_RETURN, AT_MIXED, AT_OUT, AT_NORM, AT_GROUP, AT_TILE, AT_FEED = 8, 9, 10, 11, 12, 16, 24
PUMPS = {
    AT_BEGIN: (1, 10, 4, 2, 3, 5, 7, 6, 11, 12, 13, 14),
    AT_GAINS: (20,),
    AT_GROUP + 2: (15, 17),
    AT_GROUP + 3: (16, 70),
    AT_QUERIES: (21, 30),
    AT_GROUP + 0: (50,),
    AT_GROUP + 1: (22,),
    AT_HEADS: (74, 40, 31, 60, 23),
    AT_KEYS: (34, 75),
    AT_ALL: (32, 24, 35, 44),
    AT_TILE + 0: (41, 25),
    AT_TILE + 2: (33, 26, 61, 42, 71),
    AT_TILE + 3: (27, 51),
    AT_RETURN: (36, 37, 43, 52, 45, 55, 72, 47, 54, 46),
    AT_MIXED: (64,),
    AT_OUT: (53,),
    AT_NORM: (56, 62),
    AT_FEED + 1: (63, 57),
    AT_FEED + 3: (65, 66, 67),
    AT_FEED + 5: (73,),
}


def forward_kernel(
    tokens,
    positions,
    freqs,
    gain_one,
    gain_two,
    w_query,
    w_key,
    w_value,
    w_out_t,
    w_gate,
    w_up,
    w_down_t,
    cotangent,
    near,
    far,
    normed_out,
    q_out,
    k_out,
    v_out,
    mixed_t_out,
    lse_out,
    mixed_low_out,
    middle_out,
    second_out,
    right_out,
    gains_out,
    tables_out,
    left_out,
    order,
    ids_flat,
    ids_in,
    near_own,
    far_own,
    unit,
    normed,
    tables,
    weight,
    gain_message,
    gain_all,
    gain_columns,
    gain_rows,
    left_t,
    q_heads,
    kv_heads,
    q_slots,
    kv_slots,
    q_t,
    keys,
    v_t,
    mixed_t,
    lse,
    mixed,
    mixed_slots,
    mixed_heads,
    mixed_low,
    out_weight,
    part,
    part_other,
    second,
    cot,
    right,
    feed_weight,
    ids_all,
    ids,
    load_own,
    send_ids,
    recv_ids,
    load_ids,
    send_gain,
    recv_gain,
    load_w,
    load_out,
    load_feed,
    load_cot,
    save_right,
    saves,
    send_q,
    recv_q,
    send_kv,
    recv_kv,
    send_x,
    recv_x,
    send_m,
    recv_m,
    send_p,
    recv_p,
    *sems,
):
    row, spot, core = place()
    low, full = jnp.bfloat16, jnp.float32
    rows, width = tokens.shape
    share = near_own.shape[0]
    length = 8 * rows
    runs, tiles = length // RUN, length // TILE
    per_device = rows // RUN
    halves = TILE // RUN
    quarter = 4 * share
    sibling = (row, spot, 1 - core)
    out_width = w_out_t.shape[1]
    qkv_width = 16 * HEAD

    near_loads, far_loads, start = [], [], 0
    for ref in (w_query, w_key, w_value, w_out_t):
        target = near_own.at[:, pl.ds(start, ref.shape[1])]
        near_loads.append(pltpu.make_async_copy(ref, target, load_own.at[len(near_loads)]))
        start += ref.shape[1]
    for index, ref in enumerate((w_gate, w_up, w_down_t)):
        for piece in range(4):
            source = ref.at[:, pl.ds(piece * FEED, FEED)]
            target = far_own.at[:, pl.ds((3 * piece + index) * FEED, FEED)]
            far_loads.append(
                pltpu.make_async_copy(source, target, load_own.at[4 + 4 * index + piece])
            )
    for copy in near_loads + far_loads:
        copy.start()
    load_cotangent = pltpu.make_async_copy(cotangent, cot, load_cot)
    load_cotangent.start()
    half = qkv_width // 2
    pairs = Gather(near_own, near, half, half, 0, sems)
    first = Gather(near_own, near, 0, half, 1, sems)
    outer = Gather(near_own, near, qkv_width, out_width, 2, sems)
    feeds = [Gather(far_own, far, 3 * FEED * p, 3 * FEED, 3 + p, sems) for p in range(3)]
    feeds.append(Gather(far_own, far, 9 * FEED, FEED, 6, sems))
    plane = PlaneGather(far_own, far, 10 * FEED, 2 * FEED, 7, sems)
    gathers = [pairs, first, outer] + feeds + [plane]

    def pump(place):
        for what in PUMPS.get(place, ()):
            gather, act = gathers[what // 10], what % 10
            if act == 0:
                gather.open()
            elif act < 4:
                gather.hop(act)
            elif gather is plane and act == 5:
                gather.spread()
            else:
                gather.diagonal(act - 4)

    gain_message[...] = jnp.zeros_like(gain_message)
    gain_message[0:1, :share] = gain_one[...].astype(full)
    gain_message[1:2, :share] = gain_two[...].astype(full)
    for copy in near_loads:
        copy.wait()
    greet(group_others())
    pairs.open()
    for gather in (pairs, first, outer):
        gather.place_own()

    gain_copies, gain_from = exchange_messages(
        lambda shard: gain_message, gain_all, send_gain, recv_gain
    )
    for copy in gain_copies:
        copy.start()
    gain_all[own_shard()] = gain_message[...]

    lane = lax.broadcasted_iota(jnp.int32, (8, WIDE), 1)
    ids_in[...] = jnp.zeros_like(lane)
    for run in range(per_device):
        start_at = positions[0:1, run * RUN : run * RUN + 1]
        ids_in[...] = jnp.where(lane == run, lax.div(start_at, RUN), ids_in[...])
    for shift in range(1, 8):
        remote(
            ids_in,
            ids_all.at[spot],
            send_ids.at[shift],
            recv_ids.at[shift],
            (row, lax.rem(spot + shift, 8), core),
        ).start()
    ids_all[spot] = ids_in[...]

    for copy in far_loads:
        copy.wait()
    for gather in feeds + [plane]:
        gather.place_own()
    chunk = rows // 8

    def unit_block(index, carry):
        cut = tile_at(index, chunk)
        values = tokens[cut].astype(full)
        inverse = lax.rsqrt(jnp.mean(values * values, axis=-1, keepdims=True) + epsilon)
        unit[cut] = values * inverse
        return carry

    lax.fori_loop(0, 8, unit_block, 0)
    angles = freqs[...] * positions[...].astype(full)
    tables[0] = jnp.cos(angles)
    tables[1] = jnp.sin(angles)
    for wait in gain_from:
        wait()
    for shard in range(16):
        gain_columns[shard * share : (shard + 1) * share] = gain_all[shard].T[:share]
    gain_rows[...] = gain_columns[...].T

    def gain_block(index, carry):
        cut = tile_at(index, chunk)
        normed[cut] = (unit[cut] * gain_rows[0:1]).astype(low)
        return carry

    lax.fori_loop(0, 8, gain_block, 0)

    pump(AT_BEGIN)
    for shift in range(1, 8):
        remote(
            ids_in,
            ids_all.at[lax.rem(spot + 8 - shift, 8)],
            send_ids.at[shift],
            recv_ids.at[shift],
            (row, lax.rem(spot + shift, 8), core),
        ).wait_recv()
    pltpu.make_async_copy(ids_all, ids, load_ids).start()
    pairs.finish()

    width = near.shape[3] * 16

    def load_group(group):
        lanes = pl.ds(group * 4 * HEAD, 4 * HEAD)
        return pltpu.make_async_copy(
            near.at[:, :, :, :, lanes], weight.at[group % 2], load_w.at[group % 2]
        )

    load_out_weight = pltpu.make_async_copy(
        near.at[:, :, :, :, pl.ds(qkv_width, out_width)], out_weight, load_out
    )
    load_group(2).start()
    load_group(3).start()
    pump(AT_GAINS)

    def project(group):
        load_group(group).wait()
        proj = dot_f32(normed[...], weight[group % 2].reshape(width, 4 * HEAD)).T
        for head in range(4):
            front = proj[head * HEAD : head * HEAD + HALF]
            back = proj[head * HEAD + HALF : (head + 1) * HEAD]
            if group < 3:
                front, back = (
                    front * tables[0] - back * tables[1],
                    back * tables[0] + front * tables[1],
                )
            for start, value in ((0, front.astype(low)), (HALF, back.astype(low))):
                for run in range(per_device):
                    piece = value[:, run * RUN : (run + 1) * RUN]
                    if group < 2:
                        q_heads[4 * group + head, run, start : start + HALF] = piece
                    else:
                        kv_heads[head, group - 2, run, start : start + HALF] = piece
        pump(AT_GROUP + group)

    project(2)
    project(3)

    outgoing = []
    for step in range(4):
        slot = lax.rem(spot + step, 4)
        chip = 4 * core + slot
        for other in range(2):
            is_self = jnp.logical_and(chip == spot, core == other)
            device = (row, chip, other)
            kv_parts = (
                kv_heads.at[slot, :, other],
                kv_slots.at[spot, :, other],
                send_kv.at[step, other],
                recv_kv.at[spot],
                device,
            )
            q_parts = (
                q_heads.at[2 * slot + other],
                q_slots.at[spot],
                send_q.at[step, other],
                recv_q.at[spot],
                device,
            )
            outgoing.append((kv_parts, is_self))
            outgoing.append((q_parts, is_self))
    for parts, is_self in outgoing[0::2]:
        move(*parts, is_self)
    pump(AT_PAIRS)
    first.finish()
    load_group(0).start()
    load_group(1).start()
    pump(AT_QUERIES)
    project(0)
    project(1)
    for parts, is_self in outgoing[1::2]:
        move(*parts, is_self)
    pump(AT_HEADS)

    pltpu.make_async_copy(ids_all, ids, load_ids).wait()

    def find_run(index, carry):
        device, piece = 0, 0
        for run in range(runs):
            here = ids[run // per_device, 0, run % per_device] == index
            device = jnp.where(here, run // per_device, device)
            piece = jnp.where(here, run % per_device, piece)
        order[index, 0] = device
        order[index, 1] = piece
        found = ids[index // per_device, 0, index % per_device]
        order[runs + index, 0] = lax.div(found, per_device)
        order[runs + index, 1] = lax.rem(found, per_device)
        ids_flat[index] = found
        return carry

    lax.fori_loop(0, runs, find_run, 0)

    def hand_on(source):
        block = kv_slots.at[source, :, core]
        return remote(block, block, send_x.at[source], recv_x.at[source], sibling)

    for step in range(8):
        source = lax.rem(spot + step, 8)
        block = kv_slots.at[source, :, core]
        remote(block, block, send_x.at[source], recv_kv.at[source], sibling).wait_recv()
        hand_on(source).start()
    pump(AT_KEYS)
    for step in range(8):
        remote(
            q_slots.at[step], q_slots.at[step], send_x.at[step], recv_q.at[step], sibling
        ).wait_recv()
        hand_on(step).wait()
    pump(AT_ALL)

    def sort_run(index, carry):
        device, piece = order[index, 0], order[index, 1]
        cols = tile_at(index, RUN)
        q_t[:, cols] = q_slots[device, piece]
        keys[index] = kv_slots[device, 0, piece].T
        v_t[:, cols] = kv_slots[device, 1, piece]
        return carry

    lax.fori_loop(0, runs, sort_run, 0)
    pump(AT_SORT)
    scale = HEAD ** (-0.5) * LOG2_E

    def query_pair(pair, carry):
        def step(half, scores, block, peak, total, mix):
            high = jnp.maximum(peak, jnp.max(scores, axis=0, keepdims=True))
            decay = jnp.exp2(peak - high)
            weights = jnp.exp2(scores - high)
            total = total * decay + jnp.sum(weights, axis=0, keepdims=True)
            mix = mix * decay + dot_f32(v_t[:, tile_at(block, TILE)], weights.astype(low))
            return high, total, mix

        def scores_of(half, block):
            held = keys[pl.ds(block * halves, halves)].reshape(TILE, HEAD)
            return dot_f32(held, q_t[:, tile_at(2 * pair + half, TILE)]) * scale

        def full_block(block, states):
            scores = [scores_of(half, block) for half in range(2)]
            return tuple(step(half, scores[half], block, *states[half]) for half in range(2))

        state = (
            jnp.full((1, TILE), masked_value, full),
            jnp.zeros((1, TILE), full),
            jnp.zeros((HEAD, TILE), full),
        )
        start = 2 * pair
        scores = causal(scores_of(0, start)), scores_of(1, start)
        states = tuple(step(half, scores[half], start, *state) for half in range(2))
        last = step(1, causal(scores_of(1, start + 1)), start + 1, *states[1])
        states = lax.fori_loop(0, start, full_block, (states[0], last))
        for half in range(2):
            peak, total, mix = states[half]
            index = 2 * pair + half
            cols = tile_at(index, TILE)
            mix = mix / total
            mixed_t[:, cols] = mix
            lse[:, cols] = peak + jnp.log2(total)
            for run in range(halves):
                cut = mix[:, run * RUN : (run + 1) * RUN]
                mixed[index * halves + run] = cut.astype(low)
        for place in range(tiles // 2):

            @pl.when(pair == place)
            def _():
                pump(AT_TILE + place)

        return carry

    lax.fori_loop(0, tiles // 2, query_pair, 0)

    def unsort_run(run, carry):
        index = ids[run // per_device, 0, run % per_device]
        mixed_slots[run // per_device, run % per_device] = mixed[index]
        return carry

    lax.fori_loop(0, runs, unsort_run, 0)
    copies = return_copies(mixed_slots, mixed_heads, send_m, recv_m)
    start_return(copies)
    early_saves = [
        pltpu.make_async_copy(source, target, saves.at[index])
        for index, (source, target) in enumerate(
            [
                (normed, normed_out),
                (q_t, q_out),
                (keys, k_out),
                (v_t, v_out),
                (mixed_t, mixed_t_out),
                (lse, lse_out),
                (gain_rows, gains_out),
                (tables, tables_out),
            ]
        )
    ]
    for copy in early_saves:
        copy.start()
    pump(AT_RETURN)
    outer.finish()
    load_out_weight.start()
    finish_return(copies, mixed_heads, send_m, recv_m)
    pump(AT_MIXED)

    def load_feed_weight(index, kind):
        piece, half = index // 2, lax.rem(index, 2)
        start = (3 * piece + kind) * FEED + half * PIECE
        lanes = pl.ds(pl.multiple_of(start, PIECE), PIECE)
        return pltpu.make_async_copy(
            far.at[:, :, :, :, lanes], feed_weight.at[half, kind], load_feed.at[half, kind]
        )

    def load_half(index):
        for kind in range(3):
            load_feed_weight(index, kind).start()

    feeds[0].finish()
    load_half(0)

    load_out_weight.wait()
    for run in range(per_device):
        side = mixed_heads[:, run].reshape(8 * HEAD, RUN)
        mixed_low[run * RUN : (run + 1) * RUN] = side.T

    def pair_copy(index):
        cut = pl.ds(index * quarter, quarter)
        return remote(
            part.at[:, cut], part_other.at[:, cut], send_p.at[index], recv_p.at[index], sibling
        )

    for index in range(4):
        block = out_weight[index // 2, 2 * (index % 2) : 2 * (index % 2) + 2]
        term = contract_cols(mixed_low[...], block.reshape(quarter, out_width))
        part[:, index * quarter : (index + 1) * quarter] = term.astype(low)
        pair_copy(index).start()
    pump(AT_OUT)
    load_cotangent.wait()
    for index in range(4):
        pair_copy(index).wait()
    chunk = rows // 8

    def norm_block(index, carry):
        cut = tile_at(index, chunk)
        sums = part[cut].astype(full) + part_other[cut].astype(full)
        values = tokens[cut].astype(full) + sums
        unit[cut] = values
        inverse = lax.rsqrt(jnp.mean(values * values, axis=-1, keepdims=True) + epsilon)
        second[cut] = (values * inverse * gain_rows[1:2]).astype(low)
        return carry

    lax.fori_loop(0, 8, norm_block, 0)
    late_saves = [
        pltpu.make_async_copy(source, target, saves.at[8 + index])
        for index, (source, target) in enumerate(
            [(mixed_low, mixed_low_out), (unit, middle_out), (second, second_out)]
        )
    ]
    for copy in late_saves:
        copy.start()
    pump(AT_NORM)

    def save_piece(piece):
        lanes = pl.ds(piece * 3 * FEED, 3 * FEED)
        return pltpu.make_async_copy(
            right.at[:, lanes], right_out.at[:, lanes], save_right.at[piece]
        )

    def feed_block(index, carry):
        piece, half = index // 2, lax.rem(index, 2)
        for when in range(3):

            @pl.when(index == (2 * when + 1 if when < 2 else 6))
            def _():
                feeds[when + 1].finish()

        @pl.when(index == 6)
        def _():
            load_half(6)

        @pl.when(jnp.logical_and(index != 5, index != 7))
        def _():
            load_half(index + 1)

        values = []
        for kind, left in enumerate((second, second, cot)):
            load_feed_weight(index, kind).wait()
            values.append(dot_f32(left[...], feed_weight[half, kind].reshape(width, PIECE)))
        gate, up, grad_hidden = values
        sigmoid = jax.nn.sigmoid(gate)
        silu = gate * sigmoid
        grad_gate = grad_hidden * up * sigmoid * (1.0 + gate * (1.0 - sigmoid))
        for when, source in ((1, second), (3, cot)):

            @pl.when(index == when)
            def _():
                turn_left(left_t, when % 3, source)

        for kind, value in enumerate((grad_gate, grad_hidden * silu, silu * up)):
            start = (3 * piece + kind) * FEED + half * PIECE
            right[:, pl.ds(pl.multiple_of(start, PIECE), PIECE)] = value.astype(low)

        for when in range(8):

            @pl.when(index == when)
            def _():
                pump(AT_FEED + when)

        for when in range(4):

            @pl.when(index == 2 * when + 1)
            def _():
                save_piece(when).start()

        return carry

    lax.fori_loop(0, 8, feed_block, 0)
    save_left = pltpu.make_async_copy(left_t, left_out, saves.at[11])
    save_left.start()
    for gather in gathers:
        gather.close()
    for parts, is_self in outgoing:

        @pl.when(jnp.logical_not(is_self))
        def _():
            remote(*parts).wait_send()

    for shift in range(1, 8):
        remote(
            ids_in,
            ids_all.at[spot],
            send_ids.at[shift],
            recv_ids.at[shift],
            (row, lax.rem(spot + shift, 8), core),
        ).wait_send()
    for copy in gain_copies:
        copy.wait_send()
    for copy in early_saves + late_saves + [save_left] + [save_piece(piece) for piece in range(4)]:
        copy.wait()


def forward(
    tokens,
    positions,
    gain_one,
    gain_two,
    w_query,
    w_key,
    w_value,
    w_out_t,
    w_gate,
    w_up,
    w_down_t,
    cotangent,
):
    dma = pltpu.SemaphoreType.DMA
    vmem = pltpu.VMEM
    low, full = jnp.bfloat16, jnp.float32
    rows, width = tokens.shape
    share, hidden_width = w_gate.shape
    out_width = w_out_t.shape[1]
    near_width = 16 * HEAD + out_width
    length = 8 * rows
    per_device = rows // RUN
    heads = (8, per_device, HEAD, RUN)
    both = (2, per_device, HEAD, RUN)
    by_run = (length // RUN, RUN, HEAD)
    flat = (HEAD, length)
    smem_spec = pl.BlockSpec(memory_space=pltpu.SMEM)
    shape = jax.ShapeDtypeStruct
    return pl.pallas_call(
        forward_kernel,
        in_specs=[vmem_spec()] * 5 + [any_spec()] * 8,
        out_specs=[any_spec()] * 15 + [smem_spec] * 2,
        out_shape=[
            shape((2, 4, 2, share, near_width), low),
            shape((2, 4, 2, share, 3 * hidden_width), low),
            shape((rows, width), low),
            shape(flat, low),
            shape(by_run, low),
            shape(flat, low),
            shape(flat, full),
            shape((1, length), full),
            shape((rows, out_width), low),
            shape((rows, width), full),
            shape((rows, width), low),
            shape((rows, 3 * hidden_width), low),
            shape((8, width), full),
            shape((2, HALF, rows), full),
            shape((2, 2, 2, 4 * share, rows), low),
            shape((2 * length // RUN, 2), jnp.int32),
            shape((length // RUN,), jnp.int32),
        ],
        scratch_shapes=[
            vmem((8, WIDE), jnp.int32),
            vmem((share, near_width), low),
            vmem((share, 3 * hidden_width), low),
            vmem((rows, width), full),
            vmem((rows, width), low),
            vmem((2, HALF, rows), full),
            vmem((2, 2, 4, 2, share, 4 * HEAD), low),
            vmem((8, WIDE), full),
            vmem((16, 8, WIDE), full),
            vmem((width, 8), full),
            vmem((8, width), full),
            vmem((2, 2, 2, 4 * share, rows), low),
            vmem(heads, low),
            vmem((4,) + both, low),
            vmem(heads, low),
            vmem((8,) + both, low),
            vmem(flat, low),
            vmem(by_run, low),
            vmem(flat, low),
            vmem(flat, full),
            vmem((1, length), full),
            vmem((length // RUN, HEAD, RUN), low),
            vmem(heads, low),
            vmem(heads, low),
            vmem((rows, out_width), low),
            vmem((2, 4, 2, share, out_width), low),
            vmem((rows, width), low),
            vmem((rows, width), low),
            vmem((rows, width), low),
            vmem((rows, width), low),
            vmem((rows, 3 * hidden_width), low),
            vmem((2, 3, 2, 4, 2, share, PIECE), low),
            vmem((8, 8, WIDE), jnp.int32),
            pltpu.SMEM((8, 8, WIDE), jnp.int32),
            dma((16,)),
            dma((8,)),
            dma((8,)),
            dma(()),
            dma((16,)),
            dma((16,)),
            dma((2,)),
            dma(()),
            dma((2, 3)),
            dma(()),
            dma((4,)),
            dma((12,)),
            dma((4, 2)),
            dma((8,)),
            dma((4, 2)),
            dma((8,)),
            dma((8,)),
            dma((8,)),
            dma((8,)),
            dma((8,)),
            dma((4,)),
            dma((4,)),
        ]
        + gather_sems(8),
        compiler_params=pltpu.CompilerParams(
            collective_id=1, has_side_effects=True, vmem_limit_bytes=VMEM_LIMIT
        ),
        name="forward",
    )(
        tokens,
        positions,
        lane_freqs(),
        gain_one,
        gain_two,
        w_query,
        w_key,
        w_value,
        w_out_t,
        w_gate,
        w_up,
        w_down_t,
        cotangent,
    )


SECOND, THIRD, LAST = 2, 4, 5


class Reduce:
    def __init__(self, n, changes, refs):
        (
            self.left_t,
            self.right,
            self.own,
            self.out,
            self.save,
            self.send_one,
            self.recv_one,
            self.send_two,
            self.recv_two,
            self.kept,
            self.recv_three,
            self.ss_one,
            self.rs_one,
            self.ss_two,
            self.rs_two,
            self.ss_three,
            self.rs_three,
        ) = refs
        self.n, self.changes = n, changes
        self.share = self.own.shape[1]

    def columns(self, step, kind):
        held = self.right.shape[1] // (2 * PIECE)
        start = lax.rem(step, held) * 2 * PIECE + kind * PIECE
        return pl.ds(pl.multiple_of(start, PIECE), PIECE)

    def each_save(self, step, act):
        slot = lax.rem(step, 2)
        near_at = self.changes[0]

        def copies(cuts):
            for index, (ref, start, lanes) in enumerate(cuts):
                source = self.own.at[slot, :, lanes]
                target = ref.at[:, pl.ds(start, lanes.size)]
                act(pltpu.make_async_copy(source, target, self.save.at[slot, index]))

        for kind in range(3):

            @pl.when(jnp.logical_and(step < near_at, lax.rem(step, 3) == kind))
            def _():
                start = pl.multiple_of(step // 3 * 2 * PIECE, 2 * PIECE)
                copies([(self.out[kind], start, pl.ds(0, 2 * PIECE))])

        for index in range(self.n - near_at):
            first, past = index * 2 * PIECE, (index + 1) * 2 * PIECE
            cuts, at = [], 0
            for ref in self.out[3:]:
                low, high = max(first, at), min(past, at + ref.shape[1])
                if low < high:
                    cuts.append((ref, low - at, pl.ds(low - first, high - low)))
                at += ref.shape[1]

            @pl.when(step == near_at + index)
            def _():
                copies(cuts)

    def product(self, step, kind, x, y):
        left = jnp.where(lax.rem(step, 3) == 2, 0, 1)
        left = jnp.where(step >= self.changes[0], 2, left)
        left = jnp.where(step >= self.changes[1], 0, left)
        term = jnp.dot(
            self.left_t[left, x, y],
            self.right[:, self.columns(step, kind)],
            preferred_element_type=jnp.float32,
        )
        return term

    def x_first(self, step, kind):
        return 1 if kind == 0 else jnp.where(lax.rem(step, 5) == 4, 1, 0)

    def beside(self, by_x):
        row, level, column = neighbours()[:3]
        core = place()[2]
        other_row = by_x * (1 - row) + (1 - by_x) * row
        other_column = by_x * column + (1 - by_x) * (1 - column)
        return (other_row, 2 * level + other_column, core)

    def first_copy(self, step, kind):
        out, into = lax.rem(step, 3), lax.rem(step, 6)
        return remote(
            self.send_one.at[out, kind],
            self.recv_one.at[into, kind],
            self.ss_one.at[out, kind],
            self.rs_one.at[into, kind],
            self.beside(self.x_first(step, kind)),
        )

    def second_copy(self, step, kind):
        out, into = lax.rem(step, 3), lax.rem(step, 6)
        return remote(
            self.send_two.at[out, kind],
            self.recv_two.at[into, kind],
            self.ss_two.at[out, kind],
            self.rs_two.at[into, kind],
            self.beside(1 - self.x_first(step, kind)),
        )

    def third_copy(self, step, kind, k):
        row, level, column, beside_x, beside_y, along_z = neighbours()
        target = lax.rem(level + k + 1, 4)
        out, into = lax.rem(step, 4), lax.rem(step, 4)
        return remote(
            self.kept.at[out, kind, pl.ds(pl.multiple_of(target * self.share, 16), self.share)],
            self.recv_three.at[into, kind, k],
            self.ss_three.at[out, kind, k],
            self.rs_three.at[into, kind, k],
            along_z[k],
        )

    def pieces(self, step, act):
        act(0)

        @pl.when(step < self.n - 1)
        def _():
            act(1)

    def first(self, step):
        row, level, column = neighbours()[:3]
        slot = lax.rem(step, 3)

        def act(kind):
            by_x = self.x_first(step, kind)
            for half in range(2):
                x = by_x * (1 - row) + (1 - by_x) * half
                y = by_x * half + (1 - by_x) * (1 - column)
                self.send_one[slot, kind, half] = self.product(step, kind, x, y).astype(
                    jnp.bfloat16
                )
            self.first_copy(step, kind).start()

        self.pieces(step, act)

    def second(self, step):
        row, level, column = neighbours()[:3]
        slot, came, keep = lax.rem(step, 3), lax.rem(step, 6), lax.rem(step, 4)
        self.pieces(step, lambda kind: self.first_copy(step, kind).wait())

        def act(kind):
            by_x = self.x_first(step, kind)
            x = by_x * row + (1 - by_x) * (1 - row)
            y = by_x * (1 - column) + (1 - by_x) * column
            arrived = self.recv_one.at[came, kind]
            mine = by_x * column + (1 - by_x) * row
            away = self.product(step, kind, x, y) + arrived[1 - mine].astype(jnp.float32)
            self.send_two[slot, kind] = away.astype(jnp.bfloat16)
            here = self.product(step, kind, row, column) + arrived[mine].astype(jnp.float32)
            self.kept[keep, kind] = here.astype(jnp.bfloat16)

        self.pieces(step, act)
        self.pieces(step, lambda kind: self.second_copy(step, kind).start())

    def third(self, step):
        came, keep = lax.rem(step, 6), lax.rem(step, 4)

        def act(kind):
            self.second_copy(step, kind).wait()
            here = self.kept[keep, kind].astype(jnp.float32) + self.recv_two[came, kind].astype(
                jnp.float32
            )
            self.kept[keep, kind] = here.astype(jnp.bfloat16)
            for k in range(3):
                self.third_copy(step, kind, k).start()

        self.pieces(step, act)

    def last(self, step):
        level = neighbours()[1]
        came, keep = lax.rem(step, 4), lax.rem(step, 4)
        mine = pl.ds(pl.multiple_of(level * self.share, 16), self.share)

        @pl.when(step >= 2)
        def _():
            self.each_save(step - 2, lambda copy: copy.wait())

        def act(kind):
            total = self.kept[keep, kind, mine].astype(jnp.float32)
            for k in range(3):
                self.third_copy(step, kind, k).wait()
                total = total + self.recv_three[came, kind, k].astype(jnp.float32)
            self.own[lax.rem(step, 2), :, kind * PIECE : (kind + 1) * PIECE] = total

        self.pieces(step, act)
        self.each_save(step, lambda copy: copy.start())

    def turn(self, step):
        for stage, lag in (
            (self.first, 0),
            (self.second, SECOND),
            (self.third, THIRD),
            (self.last, LAST),
        ):

            @pl.when(jnp.logical_and(step >= lag, step < self.n + lag))
            def _():
                stage(step - lag)


def backward_kernel(
    order,
    ids,
    q_in,
    k_in,
    v_in,
    mixed_t_in,
    lse_in,
    cotangent,
    left_in,
    normed_in,
    right_in,
    mixed_low,
    middle,
    near,
    far,
    tokens,
    gains_in,
    tables,
    input_grad,
    layer_out,
    gate_grad,
    up_grad,
    down_grad,
    query_grad,
    key_grad,
    value_grad,
    out_grad,
    gain_out,
    q,
    q_t,
    k,
    k_t,
    v,
    d_own,
    d_slots,
    d,
    d_t,
    dq_t,
    lse,
    delta,
    dk,
    dv,
    dq_slots,
    dkv_sorted,
    dkv_slots,
    dkv_other,
    dq_own,
    dkv_own,
    weight,
    middle_ring,
    input_ring,
    part,
    part_other,
    total,
    staged,
    grad_mid,
    gain_two_grad,
    left_t,
    right,
    gain_columns,
    gain_messages,
    gain_all,
    own,
    send_one,
    recv_one,
    send_two,
    recv_two,
    kept,
    recv_three,
    loads,
    load_first,
    send_gain,
    recv_gain,
    load_left_sem,
    load_w,
    load_ring,
    save_rows,
    save_sem,
    send_d,
    recv_d,
    send_q,
    recv_q,
    send_x,
    recv_x,
    send_k,
    recv_k,
    send_p,
    recv_p,
    save,
    *sems,
):
    row, spot, core = place()
    low, full = jnp.bfloat16, jnp.float32
    rows, width = staged.shape
    length = 8 * rows
    runs, tiles = length // RUN, length // TILE
    per_device = rows // RUN
    halves = TILE // RUN
    share = width // 16
    quarter = 4 * share
    sibling = (row, spot, 1 - core)
    qkv_width = 16 * HEAD
    out_width = mixed_low.shape[1]
    near_at = right_in.shape[1] // (2 * PIECE)
    n = near_at + (qkv_width + out_width + PIECE) // (2 * PIECE)
    grads = (gate_grad, up_grad, down_grad, query_grad, key_grad, value_grad, out_grad)
    changes = (near_at, near_at + qkv_width // (2 * PIECE))
    sums = Reduce(
        n,
        changes,
        (left_t, right, own, grads, save)
        + (send_one, recv_one, send_two, recv_two, kept, recv_three)
        + sems,
    )

    def stage(source):
        return pltpu.make_async_copy(source, staged, load_left_sem)

    early_loads = [
        pltpu.make_async_copy(source, target, loads.at[index])
        for index, (source, target) in enumerate(
            [
                (q_in, q_t),
                (k_in, k),
                (v_in, d_t),
                (mixed_t_in, dq_t),
                (lse_in, lse),
                (middle, total),
            ]
        )
    ]

    first_loads = [
        pltpu.make_async_copy(left_in, left_t.at[pl.ds(0, 2)], load_first.at[4])
    ] + [
        pltpu.make_async_copy(
            right_in.at[:, pl.ds(3 * FEED * piece, 3 * FEED)],
            right.at[:, pl.ds(3 * FEED * piece, 3 * FEED)],
            load_first.at[piece],
        )
        for piece in range(4)
    ]


    def load_block(index, piece, part_of, start):
        lanes = pl.ds(3 * FEED * piece + start + part_of * PIECE, PIECE)
        levels = pl.ds(2 * lax.rem(index, 2), 2)
        return pltpu.make_async_copy(
            far.at[index // 2, levels, :, :, lanes], held_block(piece, part_of), load_w.at[piece]
        )

    def held_block(piece, part_of):
        levels = pl.ds(2 * (part_of % 2), 2)
        return weight.at[piece, part_of // 2, levels, :, :, pl.ds(0, PIECE)]

    def load_blocks(index, piece, start, parts):
        for part_of in range(parts):
            load_block(index, piece, part_of, start).start()

    def row_products(start, parts, landing):
        def block(index, carry):
            term = jnp.zeros((rows, quarter), full)
            for piece in range(4):
                for part_of in range(parts):
                    load_block(index, piece, part_of, start).wait()
                for part_of in range(parts):
                    at = 3 * FEED * piece + start + part_of * PIECE
                    term = term + contract_cols(
                        right[:, at : at + PIECE],
                        held_block(piece, part_of)[...].reshape(quarter, PIECE),
                    )

                @pl.when(index + 1 < 4)
                def _():
                    load_blocks(index + 1, piece, start, parts)

            part[:, tile_at(index, quarter)] = term.astype(low)
            pair_copy(index, landing).start()
            return carry

        lax.fori_loop(0, 4, block, 0)

    def pair_copy(index, landing):
        cut = pl.ds(pl.multiple_of(index * quarter, quarter), quarter)
        return remote(
            part.at[:, cut],
            part_other.at[landing, :, cut],
            send_p.at[index],
            recv_p.at[landing, index],
            sibling,
        )

    def second_back():
        row_products(0, 4, 0)
        for index in range(2):
            load_out_weight(index).start()

    def load_out_weight(index):
        lanes = pl.ds(qkv_width + index * 4 * HEAD, 4 * HEAD)
        return pltpu.make_async_copy(
            near.at[:, :, :, :, lanes], weight.at[index], load_w.at[index]
        )

    d_copies = []
    for step in range(4):
        slot = lax.rem(spot + step, 4)
        chip = 4 * core + slot
        for other in range(2):
            parts = (
                d_own.at[2 * slot + other],
                d_slots.at[spot],
                send_d.at[step, other],
                recv_d.at[spot],
                (row, chip, other),
            )
            d_copies.append((parts, jnp.logical_and(chip == spot, core == other)))

    def middle_back():
        for index in range(4):
            pair_copy(index, 0).wait()
        early_loads[5].wait()
        stage(cotangent).wait()
        chunk = rows // 8

        def block(index, gain_grad):
            cut = tile_at(index, chunk)
            grad = part[cut].astype(full) + part_other[0, cut].astype(full)
            values = total[cut]
            inverse = lax.rsqrt(jnp.mean(values * values, axis=-1, keepdims=True) + epsilon)
            unit = values * inverse
            scaled = grad * gains_in[1:2]
            mean = jnp.mean(scaled * unit, axis=-1, keepdims=True)
            result = staged[cut].astype(full) + inverse * (scaled - unit * mean)
            total[cut] = result
            grad_mid[cut] = result.astype(low)
            return gain_grad + jnp.sum(grad * unit, axis=0, keepdims=True)

        gain_two_grad[...] = lax.fori_loop(0, 8, block, jnp.zeros((1, width), full))
        for index in range(2):
            load_out_weight(index).wait()
            grad = dot_f32(grad_mid[...], weight[index].reshape(width, 4 * HEAD)).T.astype(low)
            for head in range(4):
                for run in range(per_device):
                    d_own[4 * index + head, run] = grad[
                        head * HEAD : (head + 1) * HEAD, run * RUN : (run + 1) * RUN
                    ]
        for parts, is_self in d_copies:
            move(*parts, is_self)


    def prepare():
        for copy in early_loads[:5]:
            copy.wait()
        for index in range(tiles):
            cut = pl.ds(index * TILE, TILE)
            q[cut] = q_t[:, cut].T
            k_t[:, cut] = k[halves * index : halves * (index + 1)].reshape(TILE, HEAD).T
            v[cut] = d_t[:, cut].T

    def take_cotangents():
        for index in range(8):
            remote(
                d_slots.at[index], d_slots.at[index], send_d.at[0, 0], recv_d.at[index], sibling
            ).wait_recv()

        def sort_run(index, carry):
            cols = tile_at(index, RUN)
            run = d_slots[order[index, 0], order[index, 1]]
            d_t[:, cols] = run
            d[cols] = run.T
            delta[:, cols] = jnp.sum(run.astype(full) * dq_t[:, cols], axis=0, keepdims=True)
            return carry

        lax.fori_loop(0, runs, sort_run, 0)
        dq_t[...] = jnp.zeros_like(dq_t)

    scale = HEAD ** (-0.5)

    def key_tile(block):
        cut = tile_at(block, TILE)
        both = pl.ds(block * halves, halves)
        keys, values = k[both].reshape(TILE, HEAD), v[cut]
        keys_t = k_t[:, cut]
        dk[...] = jnp.zeros_like(dk)
        dv[...] = jnp.zeros_like(dv)

        def query_tile(index, diagonal):
            cols = tile_at(index, TILE)
            scores = dot_f32(keys, q_t[:, cols]) * (scale * LOG2_E)
            if diagonal:
                scores = causal(scores)
            probs = jnp.exp2(scores - lse[:, cols])
            dv[...] += dot_f32(probs.astype(low), d[cols])
            grad_probs = dot_f32(values, d_t[:, cols])
            grad_scores = (probs * (grad_probs - delta[:, cols])).astype(low)
            dk[...] += dot_f32(grad_scores, q[cols])
            dq_t[:, cols] += dot_f32(keys_t, grad_scores)

        query_tile(block, True)

        def later(index, inner):
            query_tile(index, False)
            return inner

        lax.fori_loop(block + 1, tiles, later, 0)
        for kind, value in enumerate(((dk[...] * scale).T.astype(low), dv[...].T.astype(low))):
            for half in range(halves):
                dkv_sorted[block * halves + half, kind] = value[:, half * RUN : (half + 1) * RUN]

    def key_tiles(start, stop):
        def one(block, carry):
            key_tile(block)
            return carry

        lax.fori_loop(start, stop, one, 0)

    swap = remote(dkv_slots.at[:, :, 1 - core], dkv_other, send_x, recv_x, sibling)
    dq_copies = return_copies(dq_slots, dq_own, send_q, recv_q)
    slot, owner = lax.rem(spot, 4), spot // 4
    dkv_copies = []
    for step in range(8):
        chip = lax.rem(spot + step, 8)
        parts = (
            dkv_slots.at[:, chip, core],
            dkv_own.at[slot, :, core],
            send_k.at[step],
            recv_k.at[slot, core],
            (row, chip, owner),
        )
        dkv_copies.append((parts, (owner == core) if step == 0 else False))

    def send_back():
        def unsort_run(run, carry):
            index = ids[run]
            for kind in range(2):
                dkv_slots[kind, run // per_device, run % per_device] = dkv_sorted[index, kind]
            return carry

        lax.fori_loop(0, runs, unsort_run, 0)
        swap.start()

        def turn_run(index, carry):
            value = dq_t[:, tile_at(index, RUN)] * scale
            d_slots[index // per_device, index % per_device] = value.astype(low)
            return carry

        lax.fori_loop(0, runs, turn_run, 0)

        def unsort_queries(run, carry):
            value = d_slots[order[runs + run, 0], order[runs + run, 1]]
            dq_slots[run // per_device, run % per_device] = value
            return carry

        lax.fori_loop(0, runs, unsort_queries, 0)
        start_return(dq_copies)

    def add_pairs():
        swap.wait()
        for chip in range(8):
            both = dkv_slots[:, chip, core].astype(full) + dkv_other[:, chip].astype(full)
            dkv_slots[:, chip, core] = both.astype(low)
        start_return(dkv_copies)


    def feed_forward():
        row_products(2 * FEED, 2, 1)
        for group in range(4):
            load_group(group).start()

    save_layer = pltpu.make_async_copy(part, layer_out, save_sem)

    def finish_layer():
        for index in range(4):
            pair_copy(index, 1).wait()
        pieces = width // PIECE

        def load_piece(index):
            lanes = pl.ds(index * PIECE, PIECE)
            return pltpu.make_async_copy(
                middle.at[:, lanes], middle_ring.at[index % 2], load_ring.at[index % 2]
            )

        load_piece(0).start()
        for index in range(pieces):
            if index + 1 < pieces:
                load_piece(index + 1).start()
            load_piece(index).wait()
            cut = pl.ds(index * PIECE, PIECE)
            value = part[:, cut].astype(full) + part_other[1, :, cut].astype(full)
            part[:, cut] = (value + middle_ring[index % 2]).astype(low)
        save_layer.start()


    def load_group(group):
        lanes = pl.ds(group * 4 * HEAD, 4 * HEAD)
        return pltpu.make_async_copy(
            near.at[:, :, :, :, lanes], weight.at[group], load_w.at[group]
        )

    load_mixed = pltpu.make_async_copy(
        mixed_low, right.at[:, pl.ds(qkv_width, out_width)], loads.at[0]
    )

    def project_back():
        load_mixed.start()
        for head in range(8):
            remote(
                dq_own.at[head], dq_own.at[head], send_q.at[0], recv_q.at[head], sibling
            ).wait_recv()
        for slot_in in range(4):
            for core_in in range(2):
                target = dkv_own.at[slot_in, :, core_in]
                remote(
                    target, target, send_k.at[0], recv_k.at[slot_in, core_in], sibling
                ).wait_recv()
        for group in range(4):
            for run in range(per_device):
                cols = slice(run * RUN, (run + 1) * RUN)
                turned = []
                for head in range(4):
                    if group < 2:
                        value = dq_own[4 * group + head, run]
                    else:
                        value = dkv_own[head, group - 2, run]
                    if group < 3:
                        front, back = value[:HALF].astype(full), value[HALF:].astype(full)
                        cos_part, sin_part = tables[0, :, cols], tables[1, :, cols]
                        turned.append((front * cos_part + back * sin_part).astype(low))
                        turned.append((back * cos_part - front * sin_part).astype(low))
                    else:
                        turned.append(value)
                right[cols, group * 4 * HEAD : (group + 1) * 4 * HEAD] = jnp.concatenate(
                    turned, axis=0
                ).T
        load_mixed.wait()

    def project_normed():
        save_layer.wait()
        for group in range(4):
            load_group(group).wait()
        stage(tokens).start()

        def block(index, carry):
            term = jnp.zeros((rows, quarter), full)
            for group in range(4):
                held = weight[group, index // 2, pl.ds(2 * lax.rem(index, 2), 2)]
                term = term + contract_cols(
                    right[:, group * 4 * HEAD : (group + 1) * 4 * HEAD],
                    held.reshape(quarter, 4 * HEAD),
                )
            part[:, tile_at(index, quarter)] = term.astype(low)
            pair_copy(index, 0).start()
            return carry

        lax.fori_loop(0, 4, block, 0)

    def save_input(index):
        cut = tile_at(index, rows // 8)
        slot = lax.rem(index, 2)
        return pltpu.make_async_copy(
            input_ring.at[slot], input_grad.at[cut], save_rows.at[slot]
        )

    def norm_back():
        stage(tokens).wait()
        for index in range(4):
            pair_copy(index, 0).wait()
        chunk = rows // 8

        def block(index, gain_grad):
            cut = tile_at(index, chunk)
            grad = part[cut].astype(full) + part_other[0, cut].astype(full)
            values = staged[cut].astype(full)
            inverse = lax.rsqrt(jnp.mean(values * values, axis=-1, keepdims=True) + epsilon)
            unit = values * inverse
            scaled = grad * gains_in[0:1]
            mean = jnp.mean(scaled * unit, axis=-1, keepdims=True)
            result = total[cut] + inverse * (scaled - unit * mean)

            @pl.when(index >= 2)
            def _():
                save_input(index - 2).wait()

            input_ring[lax.rem(index, 2)] = result.reshape(chunk, 1, width)
            save_input(index).start()
            return gain_grad + jnp.sum(grad * unit, axis=0, keepdims=True)

        gain_one_grad = lax.fori_loop(0, 8, block, jnp.zeros((1, width), full))
        lines = jnp.concatenate(
            [gain_one_grad, gain_two_grad[...], jnp.zeros((6, width), full)], axis=0
        )
        gain_columns[...] = lines.T
        for shard in range(16):
            held = gain_columns[shard * share : (shard + 1) * share]
            gain_messages[shard] = jnp.pad(held, ((0, WIDE - share), (0, 0))).T
        for copy in gain_copies:
            copy.start()
        gain_all[own_shard()] = gain_messages[own_shard()]

    gain_copies, gain_from = exchange_messages(
        lambda shard: gain_messages.at[shard], gain_all, send_gain, recv_gain
    )

    def finish_gains():
        for wait in gain_from:
            wait()
        gain_out[...] = jnp.sum(gain_all[...], axis=0)

    def take_normed():
        stage(normed_in).start()
        stage(normed_in).wait()
        turn_left(left_t, 2, staged)

    def start_forward():
        for piece in range(4):
            load_blocks(0, piece, 2 * FEED, 2)

    for copy in first_loads:
        copy.start()
    stage(cotangent).start()
    for piece in range(4):
        load_blocks(0, piece, 0, 4)
    for copy in early_loads:
        copy.start()
    greet(group_others())
    first_loads[0].wait()
    first_loads[1].wait()

    def wait_right():
        for copy in first_loads[2:]:
            copy.wait()

    plan = {
        2: [wait_right, second_back],
        3: [middle_back],
        4: [prepare],
        5: [start_forward, take_cotangents],
    }
    tiles_from, tile_ranges = 5, ((0, 1), (1, 2), (2, 3), (3, 5), (5, 8))
    later = {
        9: [send_back],
        11: [add_pairs, feed_forward, finish_layer, take_normed],
        12: [project_back],
        15: [lambda: turn_left(left_t, 0, grad_mid), project_normed],
        16: [norm_back],
        n + LAST - 1: [finish_gains],
    }

    def run(step, carry):
        for when, tasks in plan.items():

            @pl.when(step == when)
            def _():
                for task in tasks:
                    task()

        @pl.when(jnp.logical_and(step >= tiles_from, step < tiles_from + len(tile_ranges)))
        def _():
            start, stop = 0, 0
            for index, (first_tile, past_tile) in enumerate(tile_ranges):
                start = jnp.where(step == tiles_from + index, first_tile, start)
                stop = jnp.where(step == tiles_from + index, past_tile, stop)
            key_tiles(start, stop)

        for when, tasks in later.items():

            @pl.when(step == when)
            def _():
                for task in tasks:
                    task()

        sums.turn(step)
        return carry

    lax.fori_loop(0, n + LAST, run, 0)
    for index in (6, 7):
        save_input(index).wait()
    for copy in gain_copies:
        copy.wait_send()
    for step in (n - 2, n - 1):
        sums.each_save(step, lambda copy: copy.wait())
    for copies in (d_copies, dq_copies, dkv_copies):
        for parts, is_self in copies:
            if is_self is False:
                remote(*parts).wait_send()
            else:

                @pl.when(jnp.logical_not(is_self))
                def _():
                    remote(*parts).wait_send()


def backward(order, ids, *arrays):
    dma = pltpu.SemaphoreType.DMA
    vmem = pltpu.VMEM
    low, full = jnp.bfloat16, jnp.float32
    q_sorted, k_sorted, v_sorted, mixed_t, lse, cotangent, left, normed, right = arrays[:9]
    mixed_low, middle, near, far, tokens, gains, tables = arrays[9:]
    rows, width = cotangent.shape
    length = 8 * rows
    share = width // 16
    feed, query, out_width = right.shape[1] // 3, 8 * HEAD, mixed_low.shape[1]
    quarter = 4 * share
    per_device = rows // RUN
    heads = (8, per_device, HEAD, RUN)
    tall, flat = (length, HEAD), (HEAD, length)
    by_run = (length // RUN, RUN, HEAD)
    block = (rows, width)
    smem_spec = pl.BlockSpec(memory_space=pltpu.SMEM)
    shape = jax.ShapeDtypeStruct
    return pl.pallas_call(
        backward_kernel,
        in_specs=[smem_spec] * 2 + [any_spec()] * 14 + [vmem_spec()] * 2,
        out_specs=[any_spec()] * 9 + [vmem_spec()],
        out_shape=[
            shape((rows, 1, width), full),
            shape(block, low),
            *[
                shape((share, wide), full)
                for wide in (feed, feed, feed, query, query // 2, query // 2, out_width)
            ],
            shape((8, WIDE), full),
        ],
        scratch_shapes=[
            vmem(tall, low),
            vmem(flat, low),
            vmem(by_run, low),
            vmem(flat, low),
            vmem(tall, low),
            vmem(heads, low),
            vmem(heads, low),
            vmem(tall, low),
            vmem(flat, low),
            vmem(flat, full),
            vmem((1, length), full),
            vmem((1, length), full),
            vmem((TILE, HEAD), full),
            vmem((TILE, HEAD), full),
            vmem(heads, low),
            vmem((length // RUN, 2, HEAD, RUN), low),
            vmem((2,) + heads, low),
            vmem((2, 8, HEAD, RUN), low),
            vmem(heads, low),
            vmem((4, 2, per_device, HEAD, RUN), low),
            vmem((4, 2, 4, 2, share, 4 * HEAD), low),
            vmem((2, rows, PIECE), full),
            vmem((2, rows // 8, 1, width), full),
            vmem(block, low),
            vmem((2,) + block, low),
            vmem(block, full),
            vmem(block, low),
            vmem(block, low),
            vmem((1, width), full),
            vmem((3, 2, 2, quarter, rows), low),
            vmem(right.shape, low),
            vmem((width, 8), full),
            vmem((16, 8, WIDE), full),
            vmem((16, 8, WIDE), full),
            vmem((2, share, 2 * PIECE), full),
            vmem((3, 2, 2, quarter, PIECE), low),
            vmem((6, 2, 2, quarter, PIECE), low),
            vmem((3, 2, quarter, PIECE), low),
            vmem((6, 2, quarter, PIECE), low),
            vmem((4, 2, quarter, PIECE), low),
            vmem((4, 2, 3, share, PIECE), low),
            dma((7,)),
            dma((5,)),
            dma((16,)),
            dma((16,)),
            dma(()),
            dma((4,)),
            dma((2,)),
            dma((2,)),
            dma(()),
            dma((4, 2)),
            dma((8,)),
            dma((8,)),
            dma((8,)),
            dma(()),
            dma(()),
            dma((8,)),
            dma((4, 2)),
            dma((4,)),
            dma((2, 4)),
            dma((2, 3)),
            dma((3, 2)),
            dma((6, 2)),
            dma((3, 2)),
            dma((6, 2)),
            dma((4, 2, 3)),
            dma((4, 2, 3)),
        ],
        compiler_params=pltpu.CompilerParams(
            collective_id=2, has_side_effects=True, vmem_limit_bytes=62 * 1024 * 1024
        ),
        name="backward",
    )(
        order,
        ids,
        *arrays,
    )


def deliver_kernel(count, *refs):
    arrays, gain_grads = refs[:count], refs[count]
    results, gain_one, gain_two = refs[count + 1 : 2 * count + 1], refs[2 * count + 1], refs[2 * count + 2]
    held, loads, saves = refs[2 * count + 3 : 3 * count + 3], refs[-2], refs[-1]
    into, out = [], []
    for index in range(count):
        rows = arrays[index].shape[0]
        pieces = rows // 128 if rows % 128 == 0 else 1
        for piece in range(pieces):
            cut = pl.ds(piece * (rows // pieces), rows // pieces)
            place = index, piece
            into.append(
                pltpu.make_async_copy(
                    arrays[index].at[cut], held[index].at[cut], loads.at[place]
                )
            )
            out.append(
                pltpu.make_async_copy(
                    held[index].at[cut], results[index].at[cut], saves.at[place]
                )
            )
    for copy in into:
        copy.start()
    share = gain_one.shape[1]
    gain_one[...] = gain_grads[0:1, :share]
    gain_two[...] = gain_grads[1:2, :share]
    for came, goes in zip(into, out):
        came.wait()
        goes.start()
    for goes in out:
        goes.wait()


def deliver(arrays, gain_grads, share):
    count = len(arrays)
    shape = jax.ShapeDtypeStruct
    dma = pltpu.SemaphoreType.DMA
    return pl.pallas_call(
        functools.partial(deliver_kernel, count),
        in_specs=[any_spec()] * count + [vmem_spec()],
        out_specs=[any_spec()] * count + [vmem_spec()] * 2,
        out_shape=[shape(array.shape, array.dtype) for array in arrays]
        + [shape((1, share), jnp.float32)] * 2,
        scratch_shapes=[pltpu.VMEM(array.shape, array.dtype) for array in arrays]
        + [dma((count, 4)), dma((count, 4))],
        compiler_params=pltpu.CompilerParams(vmem_limit_bytes=VMEM_LIMIT),
        name="deliver",
    )(*arrays, gain_grads)


def by_heads(
    tokens,
    positions,
    gain_one,
    gain_two,
    w_query,
    w_key,
    w_value,
    w_out,
    w_gate,
    w_up,
    w_down,
    cotangent,
):
    rows, _, width = tokens.shape
    share = gain_one.shape[0]
    flat_in = tokens.reshape(rows, width)
    (
        near,
        far,
        normed,
        q_sorted,
        k_sorted,
        v_sorted,
        mixed_t,
        lse,
        mixed_low,
        middle,
        second,
        right,
        gains,
        tables,
        left,
        order,
        ids,
    ) = forward(
        flat_in,
        positions.reshape(1, rows),
        gain_one.reshape(1, share),
        gain_two.reshape(1, share),
        w_query,
        w_key,
        w_value,
        w_out.T,
        w_gate,
        w_up,
        w_down.T,
        cotangent.reshape(rows, width),
    )
    input_grad, layer_out, *grads, gain_grads = backward(
        order,
        ids,
        q_sorted,
        k_sorted,
        v_sorted,
        mixed_t,
        lse,
        cotangent.reshape(rows, width),
        left,
        normed,
        right,
        mixed_low,
        middle,
        near,
        far,
        flat_in,
        gains,
        tables,
    )
    input_grad, layer_out, *grads, grad_one, grad_two = deliver(
        [input_grad, layer_out, *grads], gain_grads, share
    )
    grad_gate, grad_up, grad_down, grad_query, grad_key, grad_value, grad_out = grads
    return (
        layer_out.reshape(rows, 1, width),
        input_grad,
        grad_one.reshape(share),
        grad_two.reshape(share),
        grad_query,
        grad_key,
        grad_value,
        grad_out.T,
        grad_gate,
        grad_up,
        grad_down.T,
    )


def solution(mesh):
    sizes = (mesh.shape["dp"], mesh.shape["context"], mesh.shape["tensor"])
    return jax.shard_map(
        by_heads if sizes == (2, 8, 2) else on_device,
        mesh=mesh,
        in_specs=(
            P("context", "dp", None),
            P("context", "dp"),
            P(("dp", "context")),
            P(("dp", "context")),
            P(("dp", "context"), "tensor"),
            P(("dp", "context"), "tensor"),
            P(("dp", "context"), "tensor"),
            P("tensor", ("dp", "context")),
            P(("dp", "context"), "tensor"),
            P(("dp", "context"), "tensor"),
            P("tensor", ("dp", "context")),
            P("context", "dp", None),
        ),
        out_specs=(
            P("context", "dp", None),
            P("context", "dp", None),
            P(("dp", "context")),
            P(("dp", "context")),
            P(("dp", "context"), "tensor"),
            P(("dp", "context"), "tensor"),
            P(("dp", "context"), "tensor"),
            P("tensor", ("dp", "context")),
            P(("dp", "context"), "tensor"),
            P(("dp", "context"), "tensor"),
            P("tensor", ("dp", "context")),
        ),
        check_vma=False,
    )
```

```python
import functools

import jax
import jax.numpy as jnp
import numpy as np
from jax import lax
from jax.experimental import pallas as pl
from jax.experimental.pallas import tpu as pltpu
from jax.sharding import PartitionSpec as P

HEAD = 96


epsilon = 1e-05
theta_base = 100000.0
masked_value = -1e30


def norm_forward(values_in, gain_vec):
    inverse = lax.rsqrt(jnp.mean(values_in * values_in, axis=-1, keepdims=True) + epsilon)
    unit_vals = values_in * inverse
    return (unit_vals, inverse, (unit_vals * gain_vec.astype(jnp.float32)).astype(jnp.bfloat16))


def norm_backward(grad_in, unit_vals, inverse, gain_vec):
    scaled = grad_in * gain_vec.astype(jnp.float32)
    grad_vals = inverse * (
        scaled - unit_vals * jnp.mean(scaled * unit_vals, axis=-1, keepdims=True)
    )
    return (grad_vals, jnp.sum(grad_in * unit_vals, axis=0))


def rotate(values_in, cos_part, sin_part):
    half_size = values_in.shape[-1] // 2
    front_half = values_in[..., :half_size]
    back_half = values_in[..., half_size:]
    return jnp.concatenate(
        [
            front_half * cos_part - back_half * sin_part,
            back_half * cos_part + front_half * sin_part,
        ],
        axis=-1,
    )


def contract_rows(left_mat, right_mat):
    return lax.dot_general(
        left_mat, right_mat, (((0,), (0,)), ((), ())), preferred_element_type=jnp.float32
    )


def contract_cols(left_mat, right_mat):
    return lax.dot_general(
        left_mat, right_mat, (((1,), (1,)), ((), ())), preferred_element_type=jnp.float32
    )


def on_device(
    tokens,
    positions,
    gain_one,
    gain_two,
    w_query,
    w_key,
    w_value,
    w_out,
    w_gate,
    w_up,
    w_down,
    cotangent,
):
    slot_count, seq_count, model_width = tokens.shape
    row_count = slot_count * seq_count
    gathered = (
        lax.all_gather(gain_one, ("dp", "context"), axis=0, tiled=True),
        lax.all_gather(gain_two, ("dp", "context"), axis=0, tiled=True),
        lax.all_gather(w_query, ("dp", "context"), axis=0, tiled=True),
        lax.all_gather(w_key, ("dp", "context"), axis=0, tiled=True),
        lax.all_gather(w_value, ("dp", "context"), axis=0, tiled=True),
        lax.all_gather(w_out, ("dp", "context"), axis=1, tiled=True),
        lax.all_gather(w_gate, ("dp", "context"), axis=0, tiled=True),
        lax.all_gather(w_up, ("dp", "context"), axis=0, tiled=True),
        lax.all_gather(w_down, ("dp", "context"), axis=1, tiled=True),
    )
    full_one, full_two, query_mat, key_mat, value_mat, out_mat, gate_mat, up_mat, down_mat = (
        gathered
    )
    heads_kv = key_mat.shape[1] // HEAD
    heads_q = query_mat.shape[1] // HEAD
    group_size = heads_q // heads_kv
    score_scale = HEAD ** (-0.5)
    half_size = HEAD // 2
    inv_freqs = theta_base ** (-2.0 * jnp.arange(half_size, dtype=jnp.float32) / HEAD)
    angles = positions.astype(jnp.float32)[:, :, None] * inv_freqs
    cos_part = jnp.cos(angles)[:, :, None, :]
    sin_part = jnp.sin(angles)[:, :, None, :]
    flat_in = tokens.astype(jnp.float32).reshape(row_count, model_width)
    unit_one, inverse_one, normed = norm_forward(flat_in, full_one)
    query_proj = jnp.dot(normed, query_mat, preferred_element_type=jnp.float32).reshape(
        slot_count, seq_count, heads_q, HEAD
    )
    key_proj = jnp.dot(normed, key_mat, preferred_element_type=jnp.float32).reshape(
        slot_count, seq_count, heads_kv, HEAD
    )
    value_low = (
        jnp.dot(normed, value_mat, preferred_element_type=jnp.float32)
        .astype(jnp.bfloat16)
        .reshape(slot_count, seq_count, heads_kv * HEAD)
    )
    queries = rotate(query_proj, cos_part, sin_part).astype(jnp.bfloat16)
    keys_low = (
        rotate(key_proj, cos_part, sin_part)
        .astype(jnp.bfloat16)
        .reshape(slot_count, seq_count, heads_kv * HEAD)
    )
    query_seq = jnp.transpose(
        queries.reshape(slot_count, seq_count, heads_kv, group_size, HEAD), (1, 2, 3, 0, 4)
    )
    query_pos = positions.T
    stat_shape = (seq_count, heads_kv, group_size, slot_count)
    initial = (
        jnp.full(stat_shape, masked_value, jnp.float32),
        jnp.zeros(stat_shape, jnp.float32),
        jnp.zeros(stat_shape + (HEAD,), jnp.float32),
    )
    key_piece = lax.all_gather(keys_low, "context", axis=0, tiled=True)
    value_piece = lax.all_gather(value_low, "context", axis=0, tiled=True)
    pos_piece = lax.all_gather(positions, "context", axis=0, tiled=True)
    piece_len = key_piece.shape[0]
    key_seq = jnp.transpose(key_piece.reshape(piece_len, seq_count, heads_kv, HEAD), (1, 2, 0, 3))
    value_seq = jnp.transpose(
        value_piece.reshape(piece_len, seq_count, heads_kv, HEAD), (1, 2, 0, 3)
    )
    pos_seq = pos_piece.T

    def per_sequence(seq_items):
        peak_val, totals, accum_vals, query_one, qpos_one, key_one, value_one, kpos_one = seq_items
        raw_scores = (
            jnp.einsum("hgqd,hkd->hgqk", query_one, key_one, preferred_element_type=jnp.float32)
            * score_scale
        )
        allowed = kpos_one[None, None, None, :] <= qpos_one[None, None, :, None]
        masked = jnp.where(allowed, raw_scores, masked_value)
        new_peak = jnp.maximum(peak_val, jnp.max(masked, axis=-1))
        decay_vals = jnp.exp(peak_val - new_peak)
        weights = jnp.where(allowed, jnp.exp(masked - new_peak[..., None]), 0.0)
        totals = totals * decay_vals + jnp.sum(weights, axis=-1)
        accum_vals = accum_vals * decay_vals[..., None] + jnp.einsum(
            "hgqk,hkd->hgqd",
            weights.astype(jnp.bfloat16),
            value_one,
            preferred_element_type=jnp.float32,
        )
        return (new_peak, totals, accum_vals)

    peak_val, totals, accum_vals = lax.map(
        per_sequence,
        (initial[0], initial[1], initial[2], query_seq, query_pos, key_seq, value_seq, pos_seq),
    )
    log_total = peak_val + jnp.log(totals)
    mixed_seq = accum_vals / totals[..., None]
    mixed_low = (
        jnp.transpose(mixed_seq, (3, 0, 1, 2, 4))
        .reshape(row_count, heads_q * HEAD)
        .astype(jnp.bfloat16)
    )
    branch = lax.psum(
        jnp.dot(mixed_low, out_mat, preferred_element_type=jnp.float32).astype(jnp.bfloat16),
        "tensor",
    ).astype(jnp.float32)
    middle = flat_in + branch
    unit_two, inverse_two, second = norm_forward(middle, full_two)
    gate_vals = jnp.dot(second, gate_mat, preferred_element_type=jnp.float32)
    up_vals = jnp.dot(second, up_mat, preferred_element_type=jnp.float32)
    sigmoid_vals = jax.nn.sigmoid(gate_vals)
    silu_vals = gate_vals * sigmoid_vals
    hidden = (silu_vals * up_vals).astype(jnp.bfloat16)
    mlp_part = lax.psum(
        jnp.dot(hidden, down_mat, preferred_element_type=jnp.float32).astype(jnp.bfloat16), "tensor"
    ).astype(jnp.float32)
    layer_out = (middle + mlp_part).astype(jnp.bfloat16).reshape(slot_count, seq_count, model_width)
    regathered = (
        lax.all_gather(gain_one, ("dp", "context"), axis=0, tiled=True),
        lax.all_gather(gain_two, ("dp", "context"), axis=0, tiled=True),
        lax.all_gather(w_query, ("dp", "context"), axis=0, tiled=True),
        lax.all_gather(w_key, ("dp", "context"), axis=0, tiled=True),
        lax.all_gather(w_value, ("dp", "context"), axis=0, tiled=True),
        lax.all_gather(w_out, ("dp", "context"), axis=1, tiled=True),
        lax.all_gather(w_gate, ("dp", "context"), axis=0, tiled=True),
        lax.all_gather(w_up, ("dp", "context"), axis=0, tiled=True),
        lax.all_gather(w_down, ("dp", "context"), axis=1, tiled=True),
    )
    full_one, full_two, query_mat, key_mat, value_mat, out_mat, gate_mat, up_mat, down_mat = (
        regathered
    )
    grad_low = cotangent.reshape(row_count, model_width)
    grad_down = contract_rows(hidden, grad_low)
    grad_hidden = contract_cols(grad_low, down_mat)
    grad_gate_low = (
        grad_hidden * up_vals * sigmoid_vals * (1.0 + gate_vals * (1.0 - sigmoid_vals))
    ).astype(jnp.bfloat16)
    grad_up_low = (grad_hidden * silu_vals).astype(jnp.bfloat16)
    grad_gate = contract_rows(second, grad_gate_low)
    grad_up = contract_rows(second, grad_up_low)
    grad_second = lax.psum(
        (contract_cols(grad_gate_low, gate_mat) + contract_cols(grad_up_low, up_mat)).astype(
            jnp.bfloat16
        ),
        "tensor",
    ).astype(jnp.float32)
    grad_mid_norm, grad_gain_two = norm_backward(grad_second, unit_two, inverse_two, full_two)
    grad_middle = grad_low.astype(jnp.float32) + grad_mid_norm
    grad_mid_low = grad_middle.astype(jnp.bfloat16)
    grad_out = contract_rows(mixed_low, grad_mid_low)
    grad_mixed = contract_cols(grad_mid_low, out_mat).astype(jnp.bfloat16)
    grad_mixed_seq = jnp.transpose(
        grad_mixed.reshape(slot_count, seq_count, heads_kv, group_size, HEAD), (1, 2, 3, 0, 4)
    )
    delta_rows = jnp.sum(grad_mixed_seq.astype(jnp.float32) * mixed_seq, axis=-1)
    kv_width = heads_kv * HEAD

    def block_grads(grad_query_acc, key_blk, value_blk, pos_blk):
        block_len = key_blk.shape[0]
        key_seq = jnp.transpose(key_blk.reshape(block_len, seq_count, heads_kv, HEAD), (1, 2, 0, 3))
        value_seq = jnp.transpose(
            value_blk.reshape(block_len, seq_count, heads_kv, HEAD), (1, 2, 0, 3)
        )
        raw_scores = (
            jnp.einsum("shgqd,shkd->shgqk", query_seq, key_seq, preferred_element_type=jnp.float32)
            * score_scale
        )
        allowed = pos_blk.T[:, None, None, None, :] <= query_pos[:, None, None, :, None]
        prob_vals = jnp.where(
            allowed,
            jnp.exp(jnp.where(allowed, raw_scores - log_total[..., None], masked_value)),
            0.0,
        )
        grad_value_blk = jnp.einsum(
            "shgqk,shgqd->kshd",
            prob_vals.astype(jnp.bfloat16),
            grad_mixed_seq,
            preferred_element_type=jnp.float32,
        )
        grad_probs = jnp.einsum(
            "shgqd,shkd->shgqk", grad_mixed_seq, value_seq, preferred_element_type=jnp.float32
        )
        grad_scores = (prob_vals * (grad_probs - delta_rows[..., None])).astype(jnp.bfloat16)
        grad_query_acc = grad_query_acc + jnp.einsum(
            "shgqk,shkd->shgqd", grad_scores, key_seq, preferred_element_type=jnp.float32
        )
        grad_key_blk = jnp.einsum(
            "shgqk,shgqd->kshd", grad_scores, query_seq, preferred_element_type=jnp.float32
        )
        return (
            grad_query_acc,
            grad_key_blk.reshape(block_len, seq_count, kv_width),
            grad_value_blk.reshape(block_len, seq_count, kv_width),
        )

    zero_query = jnp.zeros(stat_shape + (HEAD,), jnp.float32)
    key_all, value_all, pos_all = (
        lax.all_gather(keys_low, "context", axis=0, tiled=True),
        lax.all_gather(value_low, "context", axis=0, tiled=True),
        lax.all_gather(positions, "context", axis=0, tiled=True),
    )
    total_len = key_all.shape[0]
    block_size = min(512, total_len)
    block_count = total_len // block_size

    def key_block(grad_query_acc, block_items):
        key_blk, value_blk, pos_blk = block_items
        grad_query_acc, grad_key_blk, grad_value_blk = block_grads(
            grad_query_acc, key_blk, value_blk, pos_blk
        )
        return (grad_query_acc, (grad_key_blk, grad_value_blk))

    grad_query_acc, (grad_keys_all, grad_values_all) = lax.scan(
        key_block,
        zero_query,
        (
            key_all.reshape(block_count, block_size, seq_count, kv_width),
            value_all.reshape(block_count, block_size, seq_count, kv_width),
            pos_all.reshape(block_count, block_size, seq_count),
        ),
    )
    grad_key_own, grad_value_own = (
        lax.psum_scatter(
            grad_keys_all.reshape(total_len, seq_count, kv_width).astype(jnp.bfloat16),
            "context",
            scatter_dimension=0,
            tiled=True,
        ).astype(jnp.float32),
        lax.psum_scatter(
            grad_values_all.reshape(total_len, seq_count, kv_width).astype(jnp.bfloat16),
            "context",
            scatter_dimension=0,
            tiled=True,
        ).astype(jnp.float32),
    )
    grad_rot_q = jnp.transpose(grad_query_acc * score_scale, (3, 0, 1, 2, 4)).reshape(
        slot_count, seq_count, heads_q, HEAD
    )
    grad_q_low = (
        rotate(grad_rot_q, cos_part, -sin_part)
        .reshape(row_count, heads_q * HEAD)
        .astype(jnp.bfloat16)
    )
    grad_rot_k = (grad_key_own * score_scale).reshape(slot_count, seq_count, heads_kv, HEAD)
    grad_k_low = (
        rotate(grad_rot_k, cos_part, -sin_part).reshape(row_count, kv_width).astype(jnp.bfloat16)
    )
    grad_v_low = grad_value_own.reshape(row_count, kv_width).astype(jnp.bfloat16)
    grad_query = contract_rows(normed, grad_q_low)
    grad_key = contract_rows(normed, grad_k_low)
    grad_value = contract_rows(normed, grad_v_low)
    grad_normed = lax.psum(
        (
            contract_cols(grad_q_low, query_mat)
            + contract_cols(grad_k_low, key_mat)
            + contract_cols(grad_v_low, value_mat)
        ).astype(jnp.bfloat16),
        "tensor",
    ).astype(jnp.float32)
    grad_in_norm, grad_gain_one = norm_backward(grad_normed, unit_one, inverse_one, full_one)
    input_grad = (grad_middle + grad_in_norm).reshape(slot_count, seq_count, model_width)
    reduced = (
        lax.psum_scatter(grad_gain_one, ("dp", "context"), scatter_dimension=0, tiled=True),
        lax.psum_scatter(grad_gain_two, ("dp", "context"), scatter_dimension=0, tiled=True),
        lax.psum_scatter(grad_query, ("dp", "context"), scatter_dimension=0, tiled=True),
        lax.psum_scatter(grad_key, ("dp", "context"), scatter_dimension=0, tiled=True),
        lax.psum_scatter(grad_value, ("dp", "context"), scatter_dimension=0, tiled=True),
        lax.psum_scatter(grad_out, ("dp", "context"), scatter_dimension=1, tiled=True),
        lax.psum_scatter(grad_gate, ("dp", "context"), scatter_dimension=0, tiled=True),
        lax.psum_scatter(grad_up, ("dp", "context"), scatter_dimension=0, tiled=True),
        lax.psum_scatter(grad_down, ("dp", "context"), scatter_dimension=1, tiled=True),
    )
    return (
        layer_out,
        input_grad,
        reduced[0],
        reduced[1],
        reduced[2],
        reduced[3],
        reduced[4],
        reduced[5],
        reduced[6],
        reduced[7],
        reduced[8],
    )


WIDE = 128
HALF = HEAD // 2
RUN = 256
TILE = 512
LOG2_E = 1.4426950408889634
MESH = pl.DeviceIdType.MESH
PIECE = 256
FEED = 512
VMEM_LIMIT = 56 * 1024 * 1024


def any_spec():
    return pl.BlockSpec(memory_space=pl.ANY)


def vmem_spec():
    return pl.BlockSpec(memory_space=pltpu.VMEM)


def place():
    return lax.axis_index("dp"), lax.axis_index("context"), lax.axis_index("tensor")


def greet(devices):
    barrier = pltpu.get_barrier_semaphore()
    for device in devices:
        pl.semaphore_signal(barrier, inc=1, device_id=device, device_id_type=MESH)
    pl.semaphore_wait(barrier, len(devices))


def sequence_others():
    row, spot, core = place()
    return [
        (row, lax.rem(spot + shift, 8), lax.rem(core + flip, 2))
        for shift in range(8)
        for flip in range(2)
        if shift or flip
    ]


def lane_freqs():
    return jnp.asarray(
        np.power(np.float32(theta_base), np.float32(-2.0) * np.arange(HALF, dtype=np.float32) / HEAD)
    ).reshape(HALF, 1)


def dot_f32(left, right):
    return jnp.dot(left, right, preferred_element_type=jnp.float32)


def own_shard():
    row, spot, core = place()
    return row * 8 + spot


def group_others():
    row, spot, core = place()
    return sequence_others() + [(1 - row, lax.rem(spot + shift, 8), core) for shift in range(8)]


def exchange_messages(message_to, landing, send, recv):
    row, spot, core = place()
    copies, waits = [], []

    def one(flip, shift):
        at = flip * 8 + shift
        to_row = lax.rem(row + flip, 2)
        chip, source = lax.rem(spot + shift, 8), lax.rem(spot + 8 - shift, 8)
        device = (to_row, chip, core)
        message = message_to(to_row * 8 + chip)
        copies.append(
            remote(message, landing.at[row * 8 + spot], send.at[at], recv.at[at], device)
        )
        came = landing.at[to_row * 8 + source]
        waits.append(remote(came, came, send.at[at], recv.at[at], device).wait_recv)

    for flip in range(2):
        for shift in range(8):
            if flip or shift:
                one(flip, shift)
    return copies, waits


def turn_left(left_t, index, source):
    quarter = source.shape[1] // 4
    share = quarter // 4
    for piece in range(4):
        turned = source[:, piece * quarter : (piece + 1) * quarter].T
        for inner in range(4):
            x, z, y = piece // 2, 2 * (piece % 2) + inner // 2, inner % 2
            left_t[index, x, y, z * share : (z + 1) * share] = turned[
                inner * share : (inner + 1) * share
            ]


def remote(source, target, send, recv, device):
    return pltpu.make_async_remote_copy(
        src_ref=source,
        dst_ref=target,
        send_sem=send,
        recv_sem=recv,
        device_id=device,
        device_id_type=MESH,
    )


def move(source, target, send, recv, device, is_self):
    @pl.when(is_self)
    def _():
        pltpu.make_async_copy(source, target, recv).start()

    @pl.when(jnp.logical_not(is_self))
    def _():
        remote(source, target, send, recv, device).start()


def return_copies(ref, out, send, recv):
    row, spot, core = place()
    head = 2 * lax.rem(spot, 4) + core
    owner = spot // 4
    copies = []
    for step in range(8):
        chip = lax.rem(spot + step, 8)
        is_self = (owner == core) if step == 0 else False
        parts = (ref.at[chip], out.at[head], send.at[step], recv.at[head], (row, chip, owner))
        copies.append((parts, is_self))
    return copies


def start_return(copies):
    for parts, is_self in copies:
        if is_self is False:
            remote(*parts).start()
        else:
            move(*parts, is_self)


def finish_return(copies, out, send, recv):
    row, spot, core = place()
    for head in range(8):
        remote(
            out.at[head], out.at[head], send.at[0], recv.at[head], (row, spot, 1 - core)
        ).wait_recv()
    for parts, is_self in copies:
        if is_self is False:
            remote(*parts).wait_send()
        else:

            @pl.when(jnp.logical_not(is_self))
            def _():
                remote(*parts).wait_send()


def tile_at(index, size):
    return pl.ds(pl.multiple_of(index * size, size), size)


def causal(scores):
    keys = lax.broadcasted_iota(jnp.int32, scores.shape, 0)
    queries = lax.broadcasted_iota(jnp.int32, scores.shape, 1)
    return jnp.where(keys <= queries, scores, masked_value)


def neighbours():
    row, spot, core = place()
    level, column = spot // 2, lax.rem(spot, 2)
    beside_x = (1 - row, spot, core)
    beside_y = (row, 2 * level + 1 - column, core)
    along_z = [(row, 2 * lax.rem(level + k, 4) + column, core) for k in (1, 2, 3)]
    return row, level, column, beside_x, beside_y, along_z


class Gather:
    def __init__(self, own, whole, start, width, piece, sems):
        self.own, self.whole = own.at[:, pl.ds(start, width)], whole
        self.start, self.width = start, width
        names = ("send_z", "recv_z", "send_x", "recv_x", "send_y", "recv_y", "send_d", "recv_d")
        for name, sem in zip(names + ("local",), sems):
            setattr(self, name, sem.at[piece])

    def block(self, x, z, y, half=None):
        cut = self.width * 7 // 12 // WIDE * WIDE
        start, width = self.start, self.width
        if half == 0:
            width = cut
        elif half == 1:
            start, width = start + cut, width - cut
        return self.whole.at[x, z, y, :, pl.ds(start, width)]

    def arrived(self, target, recv_sem):
        device = neighbours()[3]
        remote(target, target, self.send_x.at[0], recv_sem, device).wait_recv()

    def copy_z(self, z, up, own=False):
        row, level, column, beside_x, beside_y = neighbours()[:5]
        core = place()[2]
        target = level + 1 if up else level - 1
        block = self.block(row, z, column)
        return remote(
            self.own if own else block,
            block,
            self.send_z.at[int(up), z],
            self.recv_z.at[z],
            (row, 2 * target + column, core),
        )

    def copies_xy(self, z, own=False):
        row, level, column, beside_x, beside_y = neighbours()[:5]
        block = self.block(row, z, column)
        source = self.own if own else block
        return [
            remote(source, block, self.send_x.at[z], self.recv_x.at[z], beside_x),
            remote(source, block, self.send_y.at[z], self.recv_y.at[z], beside_y),
        ]

    def copies_diagonal(self, z):
        row, level, column, beside_x, beside_y = neighbours()[:5]
        by_y = self.block(1 - row, z, column, 1)
        by_x = self.block(row, z, 1 - column, 0)
        return [
            remote(by_y, by_y, self.send_d.at[0, z], self.recv_d.at[0, z], beside_y),
            remote(by_x, by_x, self.send_d.at[1, z], self.recv_d.at[1, z], beside_x),
        ]

    def own_copy(self):
        row, level, column = neighbours()[:3]
        return pltpu.make_async_copy(self.own, self.block(row, level, column), self.local)

    def each_at(self, hop, act):
        level = neighbours()[1]

        @pl.when(level >= hop)
        def _():
            act(level - hop, True)

        @pl.when(level + hop <= 3)
        def _():
            act(level + hop, False)

    def start_z(self, z, up, own=False):
        level = neighbours()[1]

        @pl.when(level < 3 if up else level > 0)
        def _():
            self.copy_z(z, up, own).start()

    def place_own(self):
        self.own_copy().start()

    def open(self):
        level = neighbours()[1]
        self.start_z(level, True, True)
        self.start_z(level, False, True)
        for copy in self.copies_xy(level, True):
            copy.start()

    def hop(self, hop):
        def act(z, up):
            row, level, column = neighbours()[:3]
            self.arrived(self.block(row, z, column), self.recv_z.at[z])
            self.start_z(z, up)
            for copy in self.copies_xy(z):
                copy.start()

        self.each_at(hop, act)

    def turn_diagonal(self, z):
        row, level, column = neighbours()[:3]
        by_y, by_x = self.copies_diagonal(z)
        self.arrived(self.block(1 - row, z, column), self.recv_x.at[z])
        by_y.start()
        self.arrived(self.block(row, z, 1 - column), self.recv_y.at[z])
        by_x.start()

    def diagonal(self, hop):
        if hop == 0:
            self.turn_diagonal(neighbours()[1])
        else:
            self.each_at(hop, lambda z, up: self.turn_diagonal(z))

    def finish(self):
        row, level, column = neighbours()[:3]
        self.own_copy().wait()
        for z in range(4):
            self.arrived(self.block(1 - row, z, 1 - column, 1), self.recv_d.at[0, z])
            self.arrived(self.block(1 - row, z, 1 - column, 0), self.recv_d.at[1, z])

    def close_z(self):
        level = neighbours()[1]

        def sent(z, up):
            @pl.when(level < 3 if up else level > 0)
            def _():
                self.copy_z(z, up).wait_send()

        sent(level, True)
        sent(level, False)
        for hop in range(1, 4):
            self.each_at(hop, sent)

    def close(self):
        self.close_z()
        for z in range(4):
            for copy in self.copies_xy(z) + self.copies_diagonal(z):
                copy.wait_send()


class PlaneGather(Gather):
    def plane(self, z):
        return self.whole.at[:, z, :, :, pl.ds(self.start, self.width)]

    def copy_z(self, z, up, own=False):
        row, level, column = neighbours()[:3]
        target = level + 1 if up else level - 1
        plane = self.plane(z)
        return remote(
            plane,
            plane,
            self.send_z.at[int(up), z],
            self.recv_z.at[z],
            (row, 2 * target + column, place()[2]),
        )

    def open(self):
        for copy in self.copies_xy(neighbours()[1], True):
            copy.start()

    def spread(self):
        row, level, column = neighbours()[:3]
        self.arrived(self.block(1 - row, level, 1 - column, 1), self.recv_d.at[0, level])
        self.arrived(self.block(1 - row, level, 1 - column, 0), self.recv_d.at[1, level])
        self.own_copy().wait()
        self.start_z(level, True)
        self.start_z(level, False)

    def hop(self, hop):
        def act(z, up):
            self.arrived(self.plane(z), self.recv_z.at[z])
            self.start_z(z, up)

        self.each_at(hop, act)

    def finish(self):
        pass

    def close(self):
        level = neighbours()[1]
        self.close_z()
        for copy in self.copies_xy(level) + self.copies_diagonal(level):
            copy.wait_send()


def gather_sems(pieces):
    dma = pltpu.SemaphoreType.DMA
    shapes = [(2, 4), (4,), (4,), (4,), (4,), (4,), (2, 4), (2, 4), ()]
    return [dma((pieces,) + shape) for shape in shapes]


AT_BEGIN, AT_GAINS, AT_PAIRS, AT_QUERIES, AT_HEADS, AT_KEYS, AT_ALL, AT_SORT = 0, 1, 2, 3, 4, 5, 6, 7
AT_RETURN, AT_MIXED, AT_OUT, AT_NORM, AT_GROUP, AT_TILE, AT_FEED = 8, 9, 10, 11, 12, 16, 24
PUMPS = {
    AT_BEGIN: (1, 10, 4, 2, 3, 5, 7, 6, 11, 12, 13, 14),
    AT_GAINS: (20,),
    AT_GROUP + 2: (15, 17),
    AT_GROUP + 3: (16, 70),
    AT_QUERIES: (21, 30),
    AT_GROUP + 0: (50,),
    AT_GROUP + 1: (22,),
    AT_HEADS: (74, 40, 31, 60, 23),
    AT_KEYS: (34, 75),
    AT_ALL: (32, 24, 35, 44),
    AT_TILE + 0: (41, 25),
    AT_TILE + 2: (33, 26, 61, 42, 71),
    AT_TILE + 3: (27, 51),
    AT_RETURN: (36, 37, 43, 52, 45, 55, 72, 47, 54, 46),
    AT_MIXED: (64,),
    AT_OUT: (53,),
    AT_NORM: (56, 62),
    AT_FEED + 1: (63, 57),
    AT_FEED + 3: (65, 66, 67),
    AT_FEED + 5: (73,),
}


def forward_kernel(
    tokens,
    positions,
    freqs,
    gain_one,
    gain_two,
    w_query,
    w_key,
    w_value,
    w_out_t,
    w_gate,
    w_up,
    w_down_t,
    cotangent,
    near,
    far,
    normed_out,
    q_out,
    k_out,
    v_out,
    mixed_t_out,
    lse_out,
    mixed_low_out,
    middle_out,
    second_out,
    right_out,
    gains_out,
    tables_out,
    left_out,
    order,
    ids_flat,
    ids_in,
    near_own,
    far_own,
    unit,
    normed,
    tables,
    weight,
    gain_message,
    gain_all,
    gain_columns,
    gain_rows,
    left_t,
    q_heads,
    kv_heads,
    q_slots,
    kv_slots,
    q_t,
    keys,
    v_t,
    mixed_t,
    lse,
    mixed,
    mixed_slots,
    mixed_heads,
    mixed_low,
    out_weight,
    part,
    part_other,
    second,
    cot,
    right,
    feed_weight,
    ids_all,
    ids,
    load_own,
    send_ids,
    recv_ids,
    load_ids,
    send_gain,
    recv_gain,
    load_w,
    load_out,
    load_feed,
    load_cot,
    save_right,
    saves,
    send_q,
    recv_q,
    send_kv,
    recv_kv,
    send_x,
    recv_x,
    send_m,
    recv_m,
    send_p,
    recv_p,
    *sems,
):
    row, spot, core = place()
    low, full = jnp.bfloat16, jnp.float32
    rows, width = tokens.shape
    share = near_own.shape[0]
    length = 8 * rows
    runs, tiles = length // RUN, length // TILE
    per_device = rows // RUN
    halves = TILE // RUN
    quarter = 4 * share
    sibling = (row, spot, 1 - core)
    out_width = w_out_t.shape[1]
    qkv_width = 16 * HEAD

    near_loads, far_loads, start = [], [], 0
    for ref in (w_query, w_key, w_value, w_out_t):
        target = near_own.at[:, pl.ds(start, ref.shape[1])]
        near_loads.append(pltpu.make_async_copy(ref, target, load_own.at[len(near_loads)]))
        start += ref.shape[1]
    for index, ref in enumerate((w_gate, w_up, w_down_t)):
        for piece in range(4):
            source = ref.at[:, pl.ds(piece * FEED, FEED)]
            target = far_own.at[:, pl.ds((3 * piece + index) * FEED, FEED)]
            far_loads.append(
                pltpu.make_async_copy(source, target, load_own.at[4 + 4 * index + piece])
            )
    for copy in near_loads + far_loads:
        copy.start()
    load_cotangent = pltpu.make_async_copy(cotangent, cot, load_cot)
    load_cotangent.start()
    half = qkv_width // 2
    pairs = Gather(near_own, near, half, half, 0, sems)
    first = Gather(near_own, near, 0, half, 1, sems)
    outer = Gather(near_own, near, qkv_width, out_width, 2, sems)
    feeds = [Gather(far_own, far, 3 * FEED * p, 3 * FEED, 3 + p, sems) for p in range(3)]
    feeds.append(Gather(far_own, far, 9 * FEED, FEED, 6, sems))
    plane = PlaneGather(far_own, far, 10 * FEED, 2 * FEED, 7, sems)
    gathers = [pairs, first, outer] + feeds + [plane]

    def pump(place):
        for what in PUMPS.get(place, ()):
            gather, act = gathers[what // 10], what % 10
            if act == 0:
                gather.open()
            elif act < 4:
                gather.hop(act)
            elif gather is plane and act == 5:
                gather.spread()
            else:
                gather.diagonal(act - 4)

    gain_message[...] = jnp.zeros_like(gain_message)
    gain_message[0:1, :share] = gain_one[...].astype(full)
    gain_message[1:2, :share] = gain_two[...].astype(full)
    for copy in near_loads:
        copy.wait()
    greet(group_others())
    pairs.open()
    for gather in (pairs, first, outer):
        gather.place_own()

    gain_copies, gain_from = exchange_messages(
        lambda shard: gain_message, gain_all, send_gain, recv_gain
    )
    for copy in gain_copies:
        copy.start()
    gain_all[own_shard()] = gain_message[...]

    lane = lax.broadcasted_iota(jnp.int32, (8, WIDE), 1)
    ids_in[...] = jnp.zeros_like(lane)
    for run in range(per_device):
        start_at = positions[0:1, run * RUN : run * RUN + 1]
        ids_in[...] = jnp.where(lane == run, lax.div(start_at, RUN), ids_in[...])
    for shift in range(1, 8):
        remote(
            ids_in,
            ids_all.at[spot],
            send_ids.at[shift],
            recv_ids.at[shift],
            (row, lax.rem(spot + shift, 8), core),
        ).start()
    ids_all[spot] = ids_in[...]

    for copy in far_loads:
        copy.wait()
    for gather in feeds + [plane]:
        gather.place_own()
    chunk = rows // 8

    def unit_block(index, carry):
        cut = tile_at(index, chunk)
        values = tokens[cut].astype(full)
        inverse = lax.rsqrt(jnp.mean(values * values, axis=-1, keepdims=True) + epsilon)
        unit[cut] = values * inverse
        return carry

    lax.fori_loop(0, 8, unit_block, 0)
    angles = freqs[...] * positions[...].astype(full)
    tables[0] = jnp.cos(angles)
    tables[1] = jnp.sin(angles)

    pump(AT_BEGIN)
    for shift in range(1, 8):
        remote(
            ids_in,
            ids_all.at[lax.rem(spot + 8 - shift, 8)],
            send_ids.at[shift],
            recv_ids.at[shift],
            (row, lax.rem(spot + shift, 8), core),
        ).wait_recv()
    pltpu.make_async_copy(ids_all, ids, load_ids).start()
    pairs.finish()

    width = near.shape[3] * 16

    def load_group(group):
        lanes = pl.ds(group * 4 * HEAD, 4 * HEAD)
        return pltpu.make_async_copy(
            near.at[:, :, :, :, lanes], weight.at[group % 2], load_w.at[group % 2]
        )

    load_out_weight = pltpu.make_async_copy(
        near.at[:, :, :, :, pl.ds(qkv_width, out_width)], out_weight, load_out
    )
    load_group(2).start()
    load_group(3).start()
    for wait in gain_from:
        wait()
    for shard in range(16):
        gain_columns[shard * share : (shard + 1) * share] = gain_all[shard].T[:share]
    gain_rows[...] = gain_columns[...].T
    normed[...] = (unit[...] * gain_rows[0:1]).astype(low)
    pump(AT_GAINS)

    def project(group):
        load_group(group).wait()
        proj = dot_f32(normed[...], weight[group % 2].reshape(width, 4 * HEAD)).T
        for head in range(4):
            front = proj[head * HEAD : head * HEAD + HALF]
            back = proj[head * HEAD + HALF : (head + 1) * HEAD]
            if group < 3:
                front, back = (
                    front * tables[0] - back * tables[1],
                    back * tables[0] + front * tables[1],
                )
            for start, value in ((0, front.astype(low)), (HALF, back.astype(low))):
                for run in range(per_device):
                    piece = value[:, run * RUN : (run + 1) * RUN]
                    if group < 2:
                        q_heads[4 * group + head, run, start : start + HALF] = piece
                    else:
                        kv_heads[head, group - 2, run, start : start + HALF] = piece
        pump(AT_GROUP + group)

    project(2)
    project(3)

    outgoing = []
    for step in range(4):
        slot = lax.rem(spot + step, 4)
        chip = 4 * core + slot
        for other in range(2):
            is_self = jnp.logical_and(chip == spot, core == other)
            device = (row, chip, other)
            kv_parts = (
                kv_heads.at[slot, :, other],
                kv_slots.at[spot, :, other],
                send_kv.at[step, other],
                recv_kv.at[spot],
                device,
            )
            q_parts = (
                q_heads.at[2 * slot + other],
                q_slots.at[spot],
                send_q.at[step, other],
                recv_q.at[spot],
                device,
            )
            outgoing.append((kv_parts, is_self))
            outgoing.append((q_parts, is_self))
    for parts, is_self in outgoing[0::2]:
        move(*parts, is_self)
    pump(AT_PAIRS)
    first.finish()
    load_group(0).start()
    load_group(1).start()
    pump(AT_QUERIES)
    project(0)
    project(1)
    for parts, is_self in outgoing[1::2]:
        move(*parts, is_self)
    pump(AT_HEADS)

    def hand_on(source):
        block = kv_slots.at[source, :, core]
        return remote(block, block, send_x.at[source], recv_x.at[source], sibling)

    for step in range(8):
        source = lax.rem(spot + step, 8)
        block = kv_slots.at[source, :, core]
        remote(block, block, send_x.at[source], recv_kv.at[source], sibling).wait_recv()
        hand_on(source).start()
    pump(AT_KEYS)
    for step in range(8):
        remote(
            q_slots.at[step], q_slots.at[step], send_x.at[step], recv_q.at[step], sibling
        ).wait_recv()
        hand_on(step).wait()
    pump(AT_ALL)

    pltpu.make_async_copy(ids_all, ids, load_ids).wait()

    def find_run(index, carry):
        device, piece = 0, 0
        for run in range(runs):
            here = ids[run // per_device, 0, run % per_device] == index
            device = jnp.where(here, run // per_device, device)
            piece = jnp.where(here, run % per_device, piece)
        order[index, 0] = device
        order[index, 1] = piece
        found = ids[index // per_device, 0, index % per_device]
        order[runs + index, 0] = lax.div(found, per_device)
        order[runs + index, 1] = lax.rem(found, per_device)
        ids_flat[index] = found
        return carry

    lax.fori_loop(0, runs, find_run, 0)

    def sort_run(index, carry):
        device, piece = order[index, 0], order[index, 1]
        cols = tile_at(index, RUN)
        q_t[:, cols] = q_slots[device, piece]
        keys[index] = kv_slots[device, 0, piece].T
        v_t[:, cols] = kv_slots[device, 1, piece]
        return carry

    lax.fori_loop(0, runs, sort_run, 0)
    pump(AT_SORT)
    scale = HEAD ** (-0.5) * LOG2_E

    def query_pair(pair, carry):
        def step(half, scores, block, peak, total, mix):
            high = jnp.maximum(peak, jnp.max(scores, axis=0, keepdims=True))
            decay = jnp.exp2(peak - high)
            weights = jnp.exp2(scores - high)
            total = total * decay + jnp.sum(weights, axis=0, keepdims=True)
            mix = mix * decay + dot_f32(v_t[:, tile_at(block, TILE)], weights.astype(low))
            return high, total, mix

        def scores_of(half, block):
            held = keys[pl.ds(block * halves, halves)].reshape(TILE, HEAD)
            return dot_f32(held, q_t[:, tile_at(2 * pair + half, TILE)]) * scale

        def full_block(block, states):
            scores = [scores_of(half, block) for half in range(2)]
            return tuple(step(half, scores[half], block, *states[half]) for half in range(2))

        state = (
            jnp.full((1, TILE), masked_value, full),
            jnp.zeros((1, TILE), full),
            jnp.zeros((HEAD, TILE), full),
        )
        start = 2 * pair
        scores = causal(scores_of(0, start)), scores_of(1, start)
        states = tuple(step(half, scores[half], start, *state) for half in range(2))
        last = step(1, causal(scores_of(1, start + 1)), start + 1, *states[1])
        states = lax.fori_loop(0, start, full_block, (states[0], last))
        for half in range(2):
            peak, total, mix = states[half]
            index = 2 * pair + half
            cols = tile_at(index, TILE)
            mix = mix / total
            mixed_t[:, cols] = mix
            lse[:, cols] = peak + jnp.log2(total)
            for run in range(halves):
                cut = mix[:, run * RUN : (run + 1) * RUN]
                mixed[index * halves + run] = cut.astype(low)
        for place in range(tiles // 2):

            @pl.when(pair == place)
            def _():
                pump(AT_TILE + place)

        return carry

    lax.fori_loop(0, tiles // 2, query_pair, 0)

    def unsort_run(run, carry):
        index = ids[run // per_device, 0, run % per_device]
        mixed_slots[run // per_device, run % per_device] = mixed[index]
        return carry

    lax.fori_loop(0, runs, unsort_run, 0)
    copies = return_copies(mixed_slots, mixed_heads, send_m, recv_m)
    start_return(copies)
    early_saves = [
        pltpu.make_async_copy(source, target, saves.at[index])
        for index, (source, target) in enumerate(
            [
                (normed, normed_out),
                (q_t, q_out),
                (keys, k_out),
                (v_t, v_out),
                (mixed_t, mixed_t_out),
                (lse, lse_out),
                (gain_rows, gains_out),
                (tables, tables_out),
            ]
        )
    ]
    for copy in early_saves:
        copy.start()
    pump(AT_RETURN)
    outer.finish()
    load_out_weight.start()
    finish_return(copies, mixed_heads, send_m, recv_m)
    pump(AT_MIXED)

    load_out_weight.wait()
    for run in range(per_device):
        side = mixed_heads[:, run].reshape(8 * HEAD, RUN)
        mixed_low[run * RUN : (run + 1) * RUN] = side.T

    def pair_copy(index):
        cut = pl.ds(index * quarter, quarter)
        return remote(
            part.at[:, cut], part_other.at[:, cut], send_p.at[index], recv_p.at[index], sibling
        )

    for index in range(4):
        block = out_weight[index // 2, 2 * (index % 2) : 2 * (index % 2) + 2]
        term = contract_cols(mixed_low[...], block.reshape(quarter, out_width))
        part[:, index * quarter : (index + 1) * quarter] = term.astype(low)
        pair_copy(index).start()
    pump(AT_OUT)
    load_cotangent.wait()
    for index in range(4):
        pair_copy(index).wait()
    chunk = rows // 8

    def norm_block(index, carry):
        cut = tile_at(index, chunk)
        sums = part[cut].astype(full) + part_other[cut].astype(full)
        values = tokens[cut].astype(full) + sums
        unit[cut] = values
        inverse = lax.rsqrt(jnp.mean(values * values, axis=-1, keepdims=True) + epsilon)
        second[cut] = (values * inverse * gain_rows[1:2]).astype(low)
        return carry

    lax.fori_loop(0, 8, norm_block, 0)
    late_saves = [
        pltpu.make_async_copy(source, target, saves.at[8 + index])
        for index, (source, target) in enumerate(
            [(mixed_low, mixed_low_out), (unit, middle_out), (second, second_out)]
        )
    ]
    for copy in late_saves:
        copy.start()
    pump(AT_NORM)

    def load_feed_weight(index, kind):
        piece, half = index // 2, lax.rem(index, 2)
        start = (3 * piece + kind) * FEED + half * PIECE
        lanes = pl.ds(pl.multiple_of(start, PIECE), PIECE)
        return pltpu.make_async_copy(
            far.at[:, :, :, :, lanes], feed_weight.at[half, kind], load_feed.at[half, kind]
        )

    def load_half(index):
        for kind in range(3):
            load_feed_weight(index, kind).start()

    def save_piece(piece):
        lanes = pl.ds(piece * 3 * FEED, 3 * FEED)
        return pltpu.make_async_copy(
            right.at[:, lanes], right_out.at[:, lanes], save_right.at[piece]
        )

    def feed_block(index, carry):
        piece, half = index // 2, lax.rem(index, 2)
        for when in range(3):

            @pl.when(index == (2 * when + 1 if when < 2 else 6))
            def _():
                feeds[when + 1].finish()

        @pl.when(index == 0)
        def _():
            load_half(0)

        @pl.when(index == 6)
        def _():
            load_half(6)

        @pl.when(jnp.logical_and(index != 5, index != 7))
        def _():
            load_half(index + 1)

        values = []
        for kind, left in enumerate((second, second, cot)):
            load_feed_weight(index, kind).wait()
            values.append(dot_f32(left[...], feed_weight[half, kind].reshape(width, PIECE)))
        gate, up, grad_hidden = values
        sigmoid = jax.nn.sigmoid(gate)
        silu = gate * sigmoid
        grad_gate = grad_hidden * up * sigmoid * (1.0 + gate * (1.0 - sigmoid))
        for when, source in ((1, second), (3, cot)):

            @pl.when(index == when)
            def _():
                turn_left(left_t, when % 3, source)

        for kind, value in enumerate((grad_gate, grad_hidden * silu, silu * up)):
            start = (3 * piece + kind) * FEED + half * PIECE
            right[:, pl.ds(pl.multiple_of(start, PIECE), PIECE)] = value.astype(low)

        for when in range(8):

            @pl.when(index == when)
            def _():
                pump(AT_FEED + when)

        for when in range(4):

            @pl.when(index == 2 * when + 1)
            def _():
                save_piece(when).start()

        return carry

    feeds[0].finish()
    lax.fori_loop(0, 8, feed_block, 0)
    save_left = pltpu.make_async_copy(left_t, left_out, saves.at[11])
    save_left.start()
    for gather in gathers:
        gather.close()
    for parts, is_self in outgoing:

        @pl.when(jnp.logical_not(is_self))
        def _():
            remote(*parts).wait_send()

    for shift in range(1, 8):
        remote(
            ids_in,
            ids_all.at[spot],
            send_ids.at[shift],
            recv_ids.at[shift],
            (row, lax.rem(spot + shift, 8), core),
        ).wait_send()
    for copy in gain_copies:
        copy.wait_send()
    for copy in early_saves + late_saves + [save_left] + [save_piece(piece) for piece in range(4)]:
        copy.wait()


def forward(
    tokens,
    positions,
    gain_one,
    gain_two,
    w_query,
    w_key,
    w_value,
    w_out_t,
    w_gate,
    w_up,
    w_down_t,
    cotangent,
):
    dma = pltpu.SemaphoreType.DMA
    vmem = pltpu.VMEM
    low, full = jnp.bfloat16, jnp.float32
    rows, width = tokens.shape
    share, hidden_width = w_gate.shape
    out_width = w_out_t.shape[1]
    near_width = 16 * HEAD + out_width
    length = 8 * rows
    per_device = rows // RUN
    heads = (8, per_device, HEAD, RUN)
    both = (2, per_device, HEAD, RUN)
    by_run = (length // RUN, RUN, HEAD)
    flat = (HEAD, length)
    smem_spec = pl.BlockSpec(memory_space=pltpu.SMEM)
    shape = jax.ShapeDtypeStruct
    return pl.pallas_call(
        forward_kernel,
        in_specs=[vmem_spec()] * 5 + [any_spec()] * 8,
        out_specs=[any_spec()] * 15 + [smem_spec] * 2,
        out_shape=[
            shape((2, 4, 2, share, near_width), low),
            shape((2, 4, 2, share, 3 * hidden_width), low),
            shape((rows, width), low),
            shape(flat, low),
            shape(by_run, low),
            shape(flat, low),
            shape(flat, full),
            shape((1, length), full),
            shape((rows, out_width), low),
            shape((rows, width), full),
            shape((rows, width), low),
            shape((rows, 3 * hidden_width), low),
            shape((8, width), full),
            shape((2, HALF, rows), full),
            shape((2, 2, 2, 4 * share, rows), low),
            shape((2 * length // RUN, 2), jnp.int32),
            shape((length // RUN,), jnp.int32),
        ],
        scratch_shapes=[
            vmem((8, WIDE), jnp.int32),
            vmem((share, near_width), low),
            vmem((share, 3 * hidden_width), low),
            vmem((rows, width), full),
            vmem((rows, width), low),
            vmem((2, HALF, rows), full),
            vmem((2, 2, 4, 2, share, 4 * HEAD), low),
            vmem((8, WIDE), full),
            vmem((16, 8, WIDE), full),
            vmem((width, 8), full),
            vmem((8, width), full),
            vmem((2, 2, 2, 4 * share, rows), low),
            vmem(heads, low),
            vmem((4,) + both, low),
            vmem(heads, low),
            vmem((8,) + both, low),
            vmem(flat, low),
            vmem(by_run, low),
            vmem(flat, low),
            vmem(flat, full),
            vmem((1, length), full),
            vmem((length // RUN, HEAD, RUN), low),
            vmem(heads, low),
            vmem(heads, low),
            vmem((rows, out_width), low),
            vmem((2, 4, 2, share, out_width), low),
            vmem((rows, width), low),
            vmem((rows, width), low),
            vmem((rows, width), low),
            vmem((rows, width), low),
            vmem((rows, 3 * hidden_width), low),
            vmem((2, 3, 2, 4, 2, share, PIECE), low),
            vmem((8, 8, WIDE), jnp.int32),
            pltpu.SMEM((8, 8, WIDE), jnp.int32),
            dma((16,)),
            dma((8,)),
            dma((8,)),
            dma(()),
            dma((16,)),
            dma((16,)),
            dma((2,)),
            dma(()),
            dma((2, 3)),
            dma(()),
            dma((4,)),
            dma((12,)),
            dma((4, 2)),
            dma((8,)),
            dma((4, 2)),
            dma((8,)),
            dma((8,)),
            dma((8,)),
            dma((8,)),
            dma((8,)),
            dma((4,)),
            dma((4,)),
        ]
        + gather_sems(8),
        compiler_params=pltpu.CompilerParams(
            collective_id=1, has_side_effects=True, vmem_limit_bytes=VMEM_LIMIT
        ),
        name="forward",
    )(
        tokens,
        positions,
        lane_freqs(),
        gain_one,
        gain_two,
        w_query,
        w_key,
        w_value,
        w_out_t,
        w_gate,
        w_up,
        w_down_t,
        cotangent,
    )


SECOND, THIRD, LAST = 2, 4, 5


class Reduce:
    def __init__(self, n, changes, refs):
        (
            self.left_t,
            self.right,
            self.own,
            self.out,
            self.save,
            self.send_one,
            self.recv_one,
            self.send_two,
            self.recv_two,
            self.kept,
            self.recv_three,
            self.ss_one,
            self.rs_one,
            self.ss_two,
            self.rs_two,
            self.ss_three,
            self.rs_three,
        ) = refs
        self.n, self.changes = n, changes
        self.share = self.own.shape[1]

    def columns(self, step, kind):
        held = self.right.shape[1] // (2 * PIECE)
        start = lax.rem(step, held) * 2 * PIECE + kind * PIECE
        return pl.ds(pl.multiple_of(start, PIECE), PIECE)

    def each_save(self, step, act):
        slot = lax.rem(step, 2)
        near_at = self.changes[0]

        def copies(cuts):
            for index, (ref, start, lanes) in enumerate(cuts):
                source = self.own.at[slot, :, lanes]
                target = ref.at[:, pl.ds(start, lanes.size)]
                act(pltpu.make_async_copy(source, target, self.save.at[slot, index]))

        for kind in range(3):

            @pl.when(jnp.logical_and(step < near_at, lax.rem(step, 3) == kind))
            def _():
                start = pl.multiple_of(step // 3 * 2 * PIECE, 2 * PIECE)
                copies([(self.out[kind], start, pl.ds(0, 2 * PIECE))])

        for index in range(self.n - near_at):
            first, past = index * 2 * PIECE, (index + 1) * 2 * PIECE
            cuts, at = [], 0
            for ref in self.out[3:]:
                low, high = max(first, at), min(past, at + ref.shape[1])
                if low < high:
                    cuts.append((ref, low - at, pl.ds(low - first, high - low)))
                at += ref.shape[1]

            @pl.when(step == near_at + index)
            def _():
                copies(cuts)

    def product(self, step, kind, x, y):
        left = jnp.where(lax.rem(step, 3) == 2, 0, 1)
        left = jnp.where(step >= self.changes[0], 2, left)
        left = jnp.where(step >= self.changes[1], 0, left)
        term = jnp.dot(
            self.left_t[left, x, y],
            self.right[:, self.columns(step, kind)],
            preferred_element_type=jnp.float32,
        )
        return term

    def x_first(self, step, kind):
        return 1 if kind == 0 else jnp.where(lax.rem(step, 5) == 4, 1, 0)

    def beside(self, by_x):
        row, level, column = neighbours()[:3]
        core = place()[2]
        other_row = by_x * (1 - row) + (1 - by_x) * row
        other_column = by_x * column + (1 - by_x) * (1 - column)
        return (other_row, 2 * level + other_column, core)

    def first_copy(self, step, kind):
        out, into = lax.rem(step, 3), lax.rem(step, 6)
        return remote(
            self.send_one.at[out, kind],
            self.recv_one.at[into, kind],
            self.ss_one.at[out, kind],
            self.rs_one.at[into, kind],
            self.beside(self.x_first(step, kind)),
        )

    def second_copy(self, step, kind):
        out, into = lax.rem(step, 3), lax.rem(step, 6)
        return remote(
            self.send_two.at[out, kind],
            self.recv_two.at[into, kind],
            self.ss_two.at[out, kind],
            self.rs_two.at[into, kind],
            self.beside(1 - self.x_first(step, kind)),
        )

    def third_copy(self, step, kind, k):
        row, level, column, beside_x, beside_y, along_z = neighbours()
        target = lax.rem(level + k + 1, 4)
        out, into = lax.rem(step, 4), lax.rem(step, 5)
        return remote(
            self.kept.at[out, kind, pl.ds(pl.multiple_of(target * self.share, 16), self.share)],
            self.recv_three.at[into, kind, k],
            self.ss_three.at[out, kind, k],
            self.rs_three.at[into, kind, k],
            along_z[k],
        )

    def pieces(self, step, act):
        act(0)

        @pl.when(step < self.n - 1)
        def _():
            act(1)

    def first(self, step):
        row, level, column = neighbours()[:3]
        slot = lax.rem(step, 3)

        def act(kind):
            by_x = self.x_first(step, kind)
            for half in range(2):
                x = by_x * (1 - row) + (1 - by_x) * half
                y = by_x * half + (1 - by_x) * (1 - column)
                self.send_one[slot, kind, half] = self.product(step, kind, x, y).astype(
                    jnp.bfloat16
                )
            self.first_copy(step, kind).start()

        self.pieces(step, act)

    def second(self, step):
        row, level, column = neighbours()[:3]
        slot, came, keep = lax.rem(step, 3), lax.rem(step, 6), lax.rem(step, 4)
        self.pieces(step, lambda kind: self.first_copy(step, kind).wait())

        def act(kind):
            by_x = self.x_first(step, kind)
            x = by_x * row + (1 - by_x) * (1 - row)
            y = by_x * (1 - column) + (1 - by_x) * column
            arrived = self.recv_one.at[came, kind]
            mine = by_x * column + (1 - by_x) * row
            away = self.product(step, kind, x, y) + arrived[1 - mine].astype(jnp.float32)
            self.send_two[slot, kind] = away.astype(jnp.bfloat16)
            here = self.product(step, kind, row, column) + arrived[mine].astype(jnp.float32)
            self.kept[keep, kind] = here.astype(jnp.bfloat16)

        self.pieces(step, act)
        self.pieces(step, lambda kind: self.second_copy(step, kind).start())

    def third(self, step):
        came, keep = lax.rem(step, 6), lax.rem(step, 4)

        def act(kind):
            self.second_copy(step, kind).wait()
            here = self.kept[keep, kind].astype(jnp.float32) + self.recv_two[came, kind].astype(
                jnp.float32
            )
            self.kept[keep, kind] = here.astype(jnp.bfloat16)
            for k in range(3):
                self.third_copy(step, kind, k).start()

        self.pieces(step, act)

    def last(self, step):
        level = neighbours()[1]
        came, keep = lax.rem(step, 5), lax.rem(step, 4)
        mine = pl.ds(pl.multiple_of(level * self.share, 16), self.share)

        @pl.when(step >= 2)
        def _():
            self.each_save(step - 2, lambda copy: copy.wait())

        def act(kind):
            total = self.kept[keep, kind, mine].astype(jnp.float32)
            for k in range(3):
                self.third_copy(step, kind, k).wait()
                total = total + self.recv_three[came, kind, k].astype(jnp.float32)
            self.own[lax.rem(step, 2), :, kind * PIECE : (kind + 1) * PIECE] = total

        self.pieces(step, act)
        self.each_save(step, lambda copy: copy.start())

    def turn(self, step):
        n, hurry = self.n, self.n - 1
        for stage, lag, begin, end in (
            (self.first, 0, 0, n),
            (self.second, SECOND, SECOND, n + SECOND),
            (self.third, THIRD, THIRD, hurry + 1),
            (self.third, THIRD - 1, hurry, n + THIRD - 1),
            (self.last, LAST, LAST, hurry + 2),
            (self.last, LAST - 1, hurry + 1, n + LAST - 1),
        ):

            @pl.when(jnp.logical_and(step >= begin, step < end))
            def _():
                stage(step - lag)


def backward_kernel(
    order,
    ids,
    q_in,
    k_in,
    v_in,
    mixed_t_in,
    lse_in,
    cotangent,
    left_in,
    normed_in,
    right_in,
    mixed_low,
    middle,
    near,
    far,
    tokens,
    gains_in,
    tables,
    input_grad,
    layer_out,
    gate_grad,
    up_grad,
    down_grad,
    query_grad,
    key_grad,
    value_grad,
    out_grad,
    gain_out,
    q,
    q_t,
    k,
    k_t,
    v,
    d_own,
    d_slots,
    d,
    d_t,
    dq_t,
    lse,
    delta,
    dk,
    dv,
    dq_slots,
    dkv_sorted,
    dkv_slots,
    dkv_other,
    dq_own,
    dkv_own,
    weight,
    middle_ring,
    input_ring,
    part,
    part_other,
    total,
    staged,
    grad_mid,
    gain_two_grad,
    left_t,
    right,
    gain_columns,
    gain_messages,
    gain_all,
    own,
    send_one,
    recv_one,
    send_two,
    recv_two,
    kept,
    recv_three,
    loads,
    load_first,
    send_gain,
    recv_gain,
    load_left_sem,
    load_w,
    load_ring,
    save_rows,
    save_sem,
    send_d,
    recv_d,
    send_q,
    recv_q,
    send_x,
    recv_x,
    send_k,
    recv_k,
    send_p,
    recv_p,
    save,
    *sems,
):
    row, spot, core = place()
    low, full = jnp.bfloat16, jnp.float32
    rows, width = staged.shape
    length = 8 * rows
    runs, tiles = length // RUN, length // TILE
    per_device = rows // RUN
    halves = TILE // RUN
    share = width // 16
    quarter = 4 * share
    sibling = (row, spot, 1 - core)
    qkv_width = 16 * HEAD
    out_width = mixed_low.shape[1]
    near_at = right_in.shape[1] // (2 * PIECE)
    n = near_at + (qkv_width + out_width + PIECE) // (2 * PIECE)
    grads = (gate_grad, up_grad, down_grad, query_grad, key_grad, value_grad, out_grad)
    changes = (near_at, near_at + qkv_width // (2 * PIECE))
    sums = Reduce(
        n,
        changes,
        (left_t, right, own, grads, save)
        + (send_one, recv_one, send_two, recv_two, kept, recv_three)
        + sems,
    )

    def stage(source):
        return pltpu.make_async_copy(source, staged, load_left_sem)

    early_loads = [
        pltpu.make_async_copy(source, target, loads.at[index])
        for index, (source, target) in enumerate(
            [
                (q_in, q_t),
                (k_in, k),
                (v_in, d_t),
                (mixed_t_in, dq_t),
                (lse_in, lse),
                (middle, total),
            ]
        )
    ]

    first_loads = [
        pltpu.make_async_copy(left_in, left_t.at[pl.ds(0, 2)], load_first.at[4])
    ] + [
        pltpu.make_async_copy(
            right_in.at[:, pl.ds(3 * FEED * piece, 3 * FEED)],
            right.at[:, pl.ds(3 * FEED * piece, 3 * FEED)],
            load_first.at[piece],
        )
        for piece in range(4)
    ]


    def load_block(index, piece, part_of, start):
        lanes = pl.ds(3 * FEED * piece + start + part_of * PIECE, PIECE)
        levels = pl.ds(2 * lax.rem(index, 2), 2)
        return pltpu.make_async_copy(
            far.at[index // 2, levels, :, :, lanes], held_block(piece, part_of), load_w.at[piece]
        )

    def held_block(piece, part_of):
        levels = pl.ds(2 * (part_of % 2), 2)
        return weight.at[piece, part_of // 2, levels, :, :, pl.ds(0, PIECE)]

    def load_blocks(index, piece, start, parts):
        for part_of in range(parts):
            load_block(index, piece, part_of, start).start()

    def row_products(start, parts, landing):
        def block(index, carry):
            term = jnp.zeros((rows, quarter), full)
            for piece in range(4):
                for part_of in range(parts):
                    load_block(index, piece, part_of, start).wait()
                for part_of in range(parts):
                    at = 3 * FEED * piece + start + part_of * PIECE
                    term = term + contract_cols(
                        right[:, at : at + PIECE],
                        held_block(piece, part_of)[...].reshape(quarter, PIECE),
                    )

                @pl.when(index + 1 < 4)
                def _():
                    load_blocks(index + 1, piece, start, parts)

            part[:, tile_at(index, quarter)] = term.astype(low)
            pair_copy(index, landing).start()
            return carry

        lax.fori_loop(0, 4, block, 0)

    def pair_copy(index, landing):
        cut = pl.ds(pl.multiple_of(index * quarter, quarter), quarter)
        return remote(
            part.at[:, cut],
            part_other.at[landing, :, cut],
            send_p.at[index],
            recv_p.at[landing, index],
            sibling,
        )

    def second_back():
        row_products(0, 4, 0)
        for index in range(2):
            load_out_weight(index).start()

    def load_out_weight(index):
        lanes = pl.ds(qkv_width + index * 4 * HEAD, 4 * HEAD)
        return pltpu.make_async_copy(
            near.at[:, :, :, :, lanes], weight.at[index], load_w.at[index]
        )

    d_copies = []
    for step in range(4):
        slot = lax.rem(spot + step, 4)
        chip = 4 * core + slot
        for other in range(2):
            parts = (
                d_own.at[2 * slot + other],
                d_slots.at[spot],
                send_d.at[step, other],
                recv_d.at[spot],
                (row, chip, other),
            )
            d_copies.append((parts, jnp.logical_and(chip == spot, core == other)))

    def middle_back():
        for index in range(4):
            pair_copy(index, 0).wait()
        early_loads[5].wait()
        stage(cotangent).wait()
        chunk = rows // 8

        def block(index, gain_grad):
            cut = tile_at(index, chunk)
            grad = part[cut].astype(full) + part_other[0, cut].astype(full)
            values = total[cut]
            inverse = lax.rsqrt(jnp.mean(values * values, axis=-1, keepdims=True) + epsilon)
            unit = values * inverse
            scaled = grad * gains_in[1:2]
            mean = jnp.mean(scaled * unit, axis=-1, keepdims=True)
            result = staged[cut].astype(full) + inverse * (scaled - unit * mean)
            total[cut] = result
            grad_mid[cut] = result.astype(low)
            return gain_grad + jnp.sum(grad * unit, axis=0, keepdims=True)

        gain_two_grad[...] = lax.fori_loop(0, 8, block, jnp.zeros((1, width), full))
        for index in range(2):
            load_out_weight(index).wait()
            grad = dot_f32(grad_mid[...], weight[index].reshape(width, 4 * HEAD)).T.astype(low)
            for head in range(4):
                for run in range(per_device):
                    d_own[4 * index + head, run] = grad[
                        head * HEAD : (head + 1) * HEAD, run * RUN : (run + 1) * RUN
                    ]
        for parts, is_self in d_copies:
            move(*parts, is_self)


    def prepare():
        for copy in early_loads[:5]:
            copy.wait()
        for index in range(tiles):
            cut = pl.ds(index * TILE, TILE)
            q[cut] = q_t[:, cut].T
            k_t[:, cut] = k[halves * index : halves * (index + 1)].reshape(TILE, HEAD).T
            v[cut] = d_t[:, cut].T

    def take_cotangents():
        for index in range(8):
            remote(
                d_slots.at[index], d_slots.at[index], send_d.at[0, 0], recv_d.at[index], sibling
            ).wait_recv()

        def sort_run(index, carry):
            cols = tile_at(index, RUN)
            run = d_slots[order[index, 0], order[index, 1]]
            d_t[:, cols] = run
            d[cols] = run.T
            delta[:, cols] = jnp.sum(run.astype(full) * dq_t[:, cols], axis=0, keepdims=True)
            return carry

        lax.fori_loop(0, runs, sort_run, 0)
        dq_t[...] = jnp.zeros_like(dq_t)

    scale = HEAD ** (-0.5)

    def key_tile(block):
        cut = tile_at(block, TILE)
        both = pl.ds(block * halves, halves)
        keys, values = k[both].reshape(TILE, HEAD), v[cut]
        keys_t = k_t[:, cut]
        dk[...] = jnp.zeros_like(dk)
        dv[...] = jnp.zeros_like(dv)

        def query_tile(index, diagonal):
            cols = tile_at(index, TILE)
            scores = dot_f32(keys, q_t[:, cols]) * (scale * LOG2_E)
            if diagonal:
                scores = causal(scores)
            probs = jnp.exp2(scores - lse[:, cols])
            dv[...] += dot_f32(probs.astype(low), d[cols])
            grad_probs = dot_f32(values, d_t[:, cols])
            grad_scores = (probs * (grad_probs - delta[:, cols])).astype(low)
            dk[...] += dot_f32(grad_scores, q[cols])
            dq_t[:, cols] += dot_f32(keys_t, grad_scores)

        query_tile(block, True)

        def later(index, inner):
            query_tile(index, False)
            return inner

        lax.fori_loop(block + 1, tiles, later, 0)
        for kind, value in enumerate(((dk[...] * scale).T.astype(low), dv[...].T.astype(low))):
            for half in range(halves):
                dkv_sorted[block * halves + half, kind] = value[:, half * RUN : (half + 1) * RUN]

    def key_tiles(start, stop):
        def one(block, carry):
            key_tile(block)
            return carry

        lax.fori_loop(start, stop, one, 0)

    swap = remote(dkv_slots.at[:, :, 1 - core], dkv_other, send_x, recv_x, sibling)
    dq_copies = return_copies(dq_slots, dq_own, send_q, recv_q)
    slot, owner = lax.rem(spot, 4), spot // 4
    dkv_copies = []
    for step in range(8):
        chip = lax.rem(spot + step, 8)
        parts = (
            dkv_slots.at[:, chip, core],
            dkv_own.at[slot, :, core],
            send_k.at[step],
            recv_k.at[slot, core],
            (row, chip, owner),
        )
        dkv_copies.append((parts, (owner == core) if step == 0 else False))

    def send_back():
        def unsort_run(run, carry):
            index = ids[run]
            for kind in range(2):
                dkv_slots[kind, run // per_device, run % per_device] = dkv_sorted[index, kind]
            return carry

        lax.fori_loop(0, runs, unsort_run, 0)
        swap.start()

        def turn_run(index, carry):
            value = dq_t[:, tile_at(index, RUN)] * scale
            d_slots[index // per_device, index % per_device] = value.astype(low)
            return carry

        lax.fori_loop(0, runs, turn_run, 0)

        def unsort_queries(run, carry):
            value = d_slots[order[runs + run, 0], order[runs + run, 1]]
            dq_slots[run // per_device, run % per_device] = value
            return carry

        lax.fori_loop(0, runs, unsort_queries, 0)
        start_return(dq_copies)

    def add_pairs():
        swap.wait()
        for chip in range(8):
            both = dkv_slots[:, chip, core].astype(full) + dkv_other[:, chip].astype(full)
            dkv_slots[:, chip, core] = both.astype(low)
        start_return(dkv_copies)


    def feed_forward():
        row_products(2 * FEED, 2, 1)
        for group in range(4):
            load_group(group).start()

    save_layer = pltpu.make_async_copy(part, layer_out, save_sem)

    def finish_layer():
        for index in range(4):
            pair_copy(index, 1).wait()
        pieces = width // PIECE

        def load_piece(index):
            lanes = pl.ds(index * PIECE, PIECE)
            return pltpu.make_async_copy(
                middle.at[:, lanes], middle_ring.at[index % 2], load_ring.at[index % 2]
            )

        load_piece(0).start()
        for index in range(pieces):
            if index + 1 < pieces:
                load_piece(index + 1).start()
            load_piece(index).wait()
            cut = pl.ds(index * PIECE, PIECE)
            value = part[:, cut].astype(full) + part_other[1, :, cut].astype(full)
            part[:, cut] = (value + middle_ring[index % 2]).astype(low)
        save_layer.start()


    def load_group(group):
        lanes = pl.ds(group * 4 * HEAD, 4 * HEAD)
        return pltpu.make_async_copy(
            near.at[:, :, :, :, lanes], weight.at[group], load_w.at[group]
        )

    load_mixed = pltpu.make_async_copy(
        mixed_low, right.at[:, pl.ds(qkv_width, out_width)], loads.at[0]
    )

    def project_back():
        load_mixed.start()
        for head in range(8):
            remote(
                dq_own.at[head], dq_own.at[head], send_q.at[0], recv_q.at[head], sibling
            ).wait_recv()
        for slot_in in range(4):
            for core_in in range(2):
                target = dkv_own.at[slot_in, :, core_in]
                remote(
                    target, target, send_k.at[0], recv_k.at[slot_in, core_in], sibling
                ).wait_recv()
        for group in range(4):
            for run in range(per_device):
                cols = slice(run * RUN, (run + 1) * RUN)
                turned = []
                for head in range(4):
                    if group < 2:
                        value = dq_own[4 * group + head, run]
                    else:
                        value = dkv_own[head, group - 2, run]
                    if group < 3:
                        front, back = value[:HALF].astype(full), value[HALF:].astype(full)
                        cos_part, sin_part = tables[0, :, cols], tables[1, :, cols]
                        turned.append((front * cos_part + back * sin_part).astype(low))
                        turned.append((back * cos_part - front * sin_part).astype(low))
                    else:
                        turned.append(value)
                right[cols, group * 4 * HEAD : (group + 1) * 4 * HEAD] = jnp.concatenate(
                    turned, axis=0
                ).T
        load_mixed.wait()

    def project_normed():
        save_layer.wait()
        for group in range(4):
            load_group(group).wait()
        stage(tokens).start()

        def block(index, carry):
            term = jnp.zeros((rows, quarter), full)
            for group in range(4):
                held = weight[group, index // 2, pl.ds(2 * lax.rem(index, 2), 2)]
                term = term + contract_cols(
                    right[:, group * 4 * HEAD : (group + 1) * 4 * HEAD],
                    held.reshape(quarter, 4 * HEAD),
                )
            part[:, tile_at(index, quarter)] = term.astype(low)
            pair_copy(index, 0).start()
            return carry

        lax.fori_loop(0, 4, block, 0)

    def save_input(index):
        cut = tile_at(index, rows // 8)
        slot = lax.rem(index, 2)
        return pltpu.make_async_copy(
            input_ring.at[slot], input_grad.at[cut], save_rows.at[slot]
        )

    def norm_back():
        stage(tokens).wait()
        for index in range(4):
            pair_copy(index, 0).wait()
        chunk = rows // 8

        def block(index, gain_grad):
            cut = tile_at(index, chunk)
            grad = part[cut].astype(full) + part_other[0, cut].astype(full)
            values = staged[cut].astype(full)
            inverse = lax.rsqrt(jnp.mean(values * values, axis=-1, keepdims=True) + epsilon)
            unit = values * inverse
            scaled = grad * gains_in[0:1]
            mean = jnp.mean(scaled * unit, axis=-1, keepdims=True)
            result = total[cut] + inverse * (scaled - unit * mean)

            @pl.when(index >= 2)
            def _():
                save_input(index - 2).wait()

            input_ring[lax.rem(index, 2)] = result.reshape(chunk, 1, width)
            save_input(index).start()
            return gain_grad + jnp.sum(grad * unit, axis=0, keepdims=True)

        gain_one_grad = lax.fori_loop(0, 8, block, jnp.zeros((1, width), full))
        lines = jnp.concatenate(
            [gain_one_grad, gain_two_grad[...], jnp.zeros((6, width), full)], axis=0
        )
        gain_columns[...] = lines.T
        for shard in range(16):
            held = gain_columns[shard * share : (shard + 1) * share]
            gain_messages[shard] = jnp.pad(held, ((0, WIDE - share), (0, 0))).T
        for copy in gain_copies:
            copy.start()
        gain_all[own_shard()] = gain_messages[own_shard()]

    gain_copies, gain_from = exchange_messages(
        lambda shard: gain_messages.at[shard], gain_all, send_gain, recv_gain
    )

    def finish_gains():
        for wait in gain_from:
            wait()
        gain_out[...] = jnp.sum(gain_all[...], axis=0)

    def take_normed():
        stage(normed_in).start()
        stage(normed_in).wait()
        turn_left(left_t, 2, staged)

    def start_forward():
        for piece in range(4):
            load_blocks(0, piece, 2 * FEED, 2)

    for copy in first_loads:
        copy.start()
    stage(cotangent).start()
    for piece in range(4):
        load_blocks(0, piece, 0, 4)
    for copy in early_loads:
        copy.start()
    greet(group_others())
    first_loads[0].wait()
    first_loads[1].wait()

    def wait_right():
        for copy in first_loads[2:]:
            copy.wait()

    plan = {
        2: [wait_right, second_back],
        3: [middle_back],
        4: [prepare],
        5: [start_forward, take_cotangents],
    }
    tiles_from, tile_ranges = 5, ((0, 1), (1, 2), (2, 3), (3, 5), (5, 8))
    later = {
        9: [send_back],
        11: [add_pairs, feed_forward, finish_layer, take_normed],
        12: [project_back],
        15: [lambda: turn_left(left_t, 0, grad_mid), project_normed],
        16: [norm_back],
        n + LAST - 2: [finish_gains],
    }

    def run(step, carry):
        for when, tasks in plan.items():

            @pl.when(step == when)
            def _():
                for task in tasks:
                    task()

        @pl.when(jnp.logical_and(step >= tiles_from, step < tiles_from + len(tile_ranges)))
        def _():
            start, stop = 0, 0
            for index, (first_tile, past_tile) in enumerate(tile_ranges):
                start = jnp.where(step == tiles_from + index, first_tile, start)
                stop = jnp.where(step == tiles_from + index, past_tile, stop)
            key_tiles(start, stop)

        for when, tasks in later.items():

            @pl.when(step == when)
            def _():
                for task in tasks:
                    task()

        sums.turn(step)
        return carry

    lax.fori_loop(0, n + LAST - 1, run, 0)
    for index in (6, 7):
        save_input(index).wait()
    for copy in gain_copies:
        copy.wait_send()
    for step in (n - 2, n - 1):
        sums.each_save(step, lambda copy: copy.wait())
    for copies in (d_copies, dq_copies, dkv_copies):
        for parts, is_self in copies:
            if is_self is False:
                remote(*parts).wait_send()
            else:

                @pl.when(jnp.logical_not(is_self))
                def _():
                    remote(*parts).wait_send()


def backward(order, ids, *arrays):
    dma = pltpu.SemaphoreType.DMA
    vmem = pltpu.VMEM
    low, full = jnp.bfloat16, jnp.float32
    q_sorted, k_sorted, v_sorted, mixed_t, lse, cotangent, left, normed, right = arrays[:9]
    mixed_low, middle, near, far, tokens, gains, tables = arrays[9:]
    rows, width = cotangent.shape
    length = 8 * rows
    share = width // 16
    feed, query, out_width = right.shape[1] // 3, 8 * HEAD, mixed_low.shape[1]
    quarter = 4 * share
    per_device = rows // RUN
    heads = (8, per_device, HEAD, RUN)
    tall, flat = (length, HEAD), (HEAD, length)
    by_run = (length // RUN, RUN, HEAD)
    block = (rows, width)
    smem_spec = pl.BlockSpec(memory_space=pltpu.SMEM)
    shape = jax.ShapeDtypeStruct
    return pl.pallas_call(
        backward_kernel,
        in_specs=[smem_spec] * 2 + [any_spec()] * 14 + [vmem_spec()] * 2,
        out_specs=[any_spec()] * 9 + [vmem_spec()],
        out_shape=[
            shape((rows, 1, width), full),
            shape(block, low),
            *[
                shape((share, wide), full)
                for wide in (feed, feed, feed, query, query // 2, query // 2, out_width)
            ],
            shape((8, WIDE), full),
        ],
        scratch_shapes=[
            vmem(tall, low),
            vmem(flat, low),
            vmem(by_run, low),
            vmem(flat, low),
            vmem(tall, low),
            vmem(heads, low),
            vmem(heads, low),
            vmem(tall, low),
            vmem(flat, low),
            vmem(flat, full),
            vmem((1, length), full),
            vmem((1, length), full),
            vmem((TILE, HEAD), full),
            vmem((TILE, HEAD), full),
            vmem(heads, low),
            vmem((length // RUN, 2, HEAD, RUN), low),
            vmem((2,) + heads, low),
            vmem((2, 8, HEAD, RUN), low),
            vmem(heads, low),
            vmem((4, 2, per_device, HEAD, RUN), low),
            vmem((4, 2, 4, 2, share, 4 * HEAD), low),
            vmem((2, rows, PIECE), full),
            vmem((2, rows // 8, 1, width), full),
            vmem(block, low),
            vmem((2,) + block, low),
            vmem(block, full),
            vmem(block, low),
            vmem(block, low),
            vmem((1, width), full),
            vmem((3, 2, 2, quarter, rows), low),
            vmem(right.shape, low),
            vmem((width, 8), full),
            vmem((16, 8, WIDE), full),
            vmem((16, 8, WIDE), full),
            vmem((2, share, 2 * PIECE), full),
            vmem((3, 2, 2, quarter, PIECE), low),
            vmem((6, 2, 2, quarter, PIECE), low),
            vmem((3, 2, quarter, PIECE), low),
            vmem((6, 2, quarter, PIECE), low),
            vmem((4, 2, quarter, PIECE), low),
            vmem((5, 2, 3, share, PIECE), low),
            dma((7,)),
            dma((5,)),
            dma((16,)),
            dma((16,)),
            dma(()),
            dma((4,)),
            dma((2,)),
            dma((2,)),
            dma(()),
            dma((4, 2)),
            dma((8,)),
            dma((8,)),
            dma((8,)),
            dma(()),
            dma(()),
            dma((8,)),
            dma((4, 2)),
            dma((4,)),
            dma((2, 4)),
            dma((2, 3)),
            dma((3, 2)),
            dma((6, 2)),
            dma((3, 2)),
            dma((6, 2)),
            dma((4, 2, 3)),
            dma((5, 2, 3)),
        ],
        compiler_params=pltpu.CompilerParams(
            collective_id=2, has_side_effects=True, vmem_limit_bytes=62 * 1024 * 1024
        ),
        name="backward",
    )(
        order,
        ids,
        *arrays,
    )


def deliver_kernel(count, *refs):
    arrays, gain_grads = refs[:count], refs[count]
    results, gain_one, gain_two = refs[count + 1 : 2 * count + 1], refs[2 * count + 1], refs[2 * count + 2]
    held, loads, saves = refs[2 * count + 3 : 3 * count + 3], refs[-2], refs[-1]
    into, out = [], []
    for index in range(count):
        rows = arrays[index].shape[0]
        pieces = rows // 128 if rows % 128 == 0 else 1
        for piece in range(pieces):
            cut = pl.ds(piece * (rows // pieces), rows // pieces)
            place = index, piece
            into.append(
                pltpu.make_async_copy(
                    arrays[index].at[cut], held[index].at[cut], loads.at[place]
                )
            )
            out.append(
                pltpu.make_async_copy(
                    held[index].at[cut], results[index].at[cut], saves.at[place]
                )
            )
    for copy in into:
        copy.start()
    share = gain_one.shape[1]
    gain_one[...] = gain_grads[0:1, :share]
    gain_two[...] = gain_grads[1:2, :share]
    for came, goes in zip(into, out):
        came.wait()
        goes.start()
    for goes in out:
        goes.wait()


def deliver(arrays, gain_grads, share):
    count = len(arrays)
    shape = jax.ShapeDtypeStruct
    dma = pltpu.SemaphoreType.DMA
    return pl.pallas_call(
        functools.partial(deliver_kernel, count),
        in_specs=[any_spec()] * count + [vmem_spec()],
        out_specs=[any_spec()] * count + [vmem_spec()] * 2,
        out_shape=[shape(array.shape, array.dtype) for array in arrays]
        + [shape((1, share), jnp.float32)] * 2,
        scratch_shapes=[pltpu.VMEM(array.shape, array.dtype) for array in arrays]
        + [dma((count, 4)), dma((count, 4))],
        compiler_params=pltpu.CompilerParams(vmem_limit_bytes=VMEM_LIMIT),
        name="deliver",
    )(*arrays, gain_grads)


def by_heads(
    tokens,
    positions,
    gain_one,
    gain_two,
    w_query,
    w_key,
    w_value,
    w_out,
    w_gate,
    w_up,
    w_down,
    cotangent,
):
    rows, _, width = tokens.shape
    share = gain_one.shape[0]
    flat_in = tokens.reshape(rows, width)
    (
        near,
        far,
        normed,
        q_sorted,
        k_sorted,
        v_sorted,
        mixed_t,
        lse,
        mixed_low,
        middle,
        second,
        right,
        gains,
        tables,
        left,
        order,
        ids,
    ) = forward(
        flat_in,
        positions.reshape(1, rows),
        gain_one.reshape(1, share),
        gain_two.reshape(1, share),
        w_query,
        w_key,
        w_value,
        w_out.T,
        w_gate,
        w_up,
        w_down.T,
        cotangent.reshape(rows, width),
    )
    input_grad, layer_out, *grads, gain_grads = backward(
        order,
        ids,
        q_sorted,
        k_sorted,
        v_sorted,
        mixed_t,
        lse,
        cotangent.reshape(rows, width),
        left,
        normed,
        right,
        mixed_low,
        middle,
        near,
        far,
        flat_in,
        gains,
        tables,
    )
    input_grad, layer_out, *grads, grad_one, grad_two = deliver(
        [input_grad, layer_out, *grads], gain_grads, share
    )
    grad_gate, grad_up, grad_down, grad_query, grad_key, grad_value, grad_out = grads
    return (
        layer_out.reshape(rows, 1, width),
        input_grad,
        grad_one.reshape(share),
        grad_two.reshape(share),
        grad_query,
        grad_key,
        grad_value,
        grad_out.T,
        grad_gate,
        grad_up,
        grad_down.T,
    )


def solution(mesh):
    sizes = (mesh.shape["dp"], mesh.shape["context"], mesh.shape["tensor"])
    return jax.shard_map(
        by_heads if sizes == (2, 8, 2) else on_device,
        mesh=mesh,
        in_specs=(
            P("context", "dp", None),
            P("context", "dp"),
            P(("dp", "context")),
            P(("dp", "context")),
            P(("dp", "context"), "tensor"),
            P(("dp", "context"), "tensor"),
            P(("dp", "context"), "tensor"),
            P("tensor", ("dp", "context")),
            P(("dp", "context"), "tensor"),
            P(("dp", "context"), "tensor"),
            P("tensor", ("dp", "context")),
            P("context", "dp", None),
        ),
        out_specs=(
            P("context", "dp", None),
            P("context", "dp", None),
            P(("dp", "context")),
            P(("dp", "context")),
            P(("dp", "context"), "tensor"),
            P(("dp", "context"), "tensor"),
            P(("dp", "context"), "tensor"),
            P("tensor", ("dp", "context")),
            P(("dp", "context"), "tensor"),
            P(("dp", "context"), "tensor"),
            P("tensor", ("dp", "context")),
        ),
        check_vma=False,
    )
```
